32 devices in a mesh: dp: 8 (over z, y), head: 4 (over x, core).
Axes of the slice: x: 2, y: 2, z: 4, core: 2. Of those that a mesh axis runs over, the one named last changes fastest.
Arguments:
- images: bfloat16 [16, 32, 32, 384], P('dp', 'head'), may hold values from -16 to 16
- noise_field: bfloat16 [16, 32, 32, 384], P('dp', 'head'), may hold values from -6 to 6
- time_steps: int32 [16], P('dp'), may hold values from 0 to 3999
- embedding: bfloat16 [16, 768], P('dp'), may hold values from -5 to 5
- first_kernel: bfloat16 [3, 3, 384, 384], P(None, None, 'dp', 'head'), may hold values from -0.109375 to 0.109375
- second_kernel: bfloat16 [3, 3, 384, 384], P(None, None, 'dp', 'head'), may hold values from -0.109375 to 0.109375
- film_weight: bfloat16 [768, 768], P('dp', 'head'), may hold values from -0.21875 to 0.21875
- attend_weight: bfloat16 [384, 1152], P('dp', 'head'), may hold values from -0.3125 to 0.3125
- output_weight: bfloat16 [384, 384], P('dp', 'head'), may hold values from -1.25 to 1.25
- norm_gains: float32 [3, 384], replicated, may hold values from 0.1 to 1.9
- biases: float32 [10, 384], replicated, may hold values from -3 to 3
- cotangent: bfloat16 [16, 32, 32, 384], P('dp', 'head'), may hold values from -6 to 6
Outputs:
- result: float32 [16, 32, 32, 384], P('dp', 'head')
- image_grad: float32 [16, 32, 32, 384], P('dp', 'head')
- embed_grad: float32 [16, 768], P('dp')
- first_grad: float32 [3, 3, 384, 384], P(None, None, 'dp', 'head')
- second_grad: float32 [3, 3, 384, 384], P(None, None, 'dp', 'head')
- film_grad: float32 [768, 768], P('dp', 'head')
- attend_grad: float32 [384, 1152], P('dp', 'head')
- output_grad: float32 [384, 384], P('dp', 'head')
- gains_grad: float32 [3, 384], replicated
- biases_grad: float32 [10, 384], replicated
The draws below stay inside these ranges and needn't reach their ends.
All inputs are finite; a program needn't handle non-finite values.
Results may differ from the reference program's by a relative error of at most 0.015.
Values may be sent and summed in bfloat16 or wider, within the bound.
A program may use at most 128 MiB of HBM per device.

```python
import math
import jax
import jax.numpy as jnp
from jax import lax

WIDTH = 384
EMBED = 768
HEADS = 4
HEAD_DIM = 96
GROUPS = 32
SIDE = 32
PIXELS = 1024
STEPS = 4000
MAPS = 16


def draw_images(key, part):
    key = jax.random.fold_in(key, 11)
    key_list = jax.random.split(key, 4)
    full_shape = (MAPS, SIDE, SIDE, WIDTH)
    basic_draw = jax.random.truncated_normal(key_list[0], -2.5, 2.5, full_shape, jnp.float32)
    map_factor = jax.random.uniform(key_list[1], (MAPS, 1, 1, 1), jnp.float32, 0.7, 1.3)
    row_place = jnp.arange(SIDE, dtype=jnp.float32) / (SIDE - 1)
    row_factor = (0.5 * jnp.exp(1.6 * row_place)).reshape(1, SIDE, 1, 1)
    channel_factor = jnp.exp(jax.random.uniform(key_list[2], (1, 1, 1, WIDTH), jnp.float32, math.log(0.6), math.log(1.6)))
    offsets = 0.3 * jax.random.truncated_normal(key_list[3], -3.0, 3.0, (MAPS, 1, 1, WIDTH), jnp.float32)
    return (basic_draw * row_factor * map_factor * channel_factor + offsets).astype(jnp.bfloat16)


def plant(drawn, rng, least, top_value):
    place = [jax.random.randint(jax.random.fold_in(rng, axis), (), 0, length) for axis, length in enumerate(drawn.shape)]
    widest = drawn.shape.index(max(drawn.shape))
    next_to = place[:widest] + [(place[widest] + 1) % drawn.shape[widest]] + place[widest + 1:]
    return drawn.at[tuple(place)].set(least).at[tuple(next_to)].set(top_value)


def shard_levels(stream_key, extent, shards, low, top_value):
    def one(axis_at, blocks):
        draws = jax.random.uniform(jax.random.fold_in(jax.random.fold_in(stream_key, 6), axis_at), (blocks,), jnp.float32, low / len(shards), top_value / len(shards))
        return jnp.repeat(jnp.exp(draws), extent[axis_at] // blocks).reshape((-1,) + (1,) * (len(extent) - axis_at - 1))

    factor_of = one(*shards[0])
    for cut in shards[1:]:
        factor_of = factor_of * one(*cut)
    return factor_of


def noise(rng, dims, spread, reach, cuts=(), held_as=jnp.bfloat16):
    values = spread * jax.random.normal(rng, dims, jnp.float32)
    if cuts:
        values = values * shard_levels(rng, dims, cuts, -0.22, 0.18)
    return jnp.clip(values, -reach, reach).astype(held_as)


def setup_inputs(seed: int = 0) -> dict:
    arg_keys = jax.random.split(jax.random.key(seed), 13)
    images = draw_images(jax.random.fold_in(arg_keys[12], 71), 0)
    noise_field = noise(arg_keys[1], (MAPS, SIDE, SIDE, WIDTH), 1.0, 6.0, ((0, 8), (1, 4)))
    time_steps = plant(jax.random.randint(arg_keys[2], (MAPS,), 0, STEPS), jax.random.fold_in(arg_keys[2], 1), 0, STEPS - 1).astype(jnp.int32)
    embedding = noise(arg_keys[3], (MAPS, EMBED), 1.0, 5.0, ((0, 8),))
    first_kernel = noise(arg_keys[4], (3, 3, WIDTH, WIDTH), (9 * WIDTH) ** -0.5, 0.109375, ((2, 8), (3, 4)))
    second_kernel = noise(arg_keys[5], (3, 3, WIDTH, WIDTH), (9 * WIDTH) ** -0.5, 0.109375, ((2, 8), (3, 4)))
    film_weight = noise(arg_keys[6], (EMBED, 2 * WIDTH), EMBED ** -0.5, 0.21875, ((0, 8), (1, 4)))
    attend_weight = noise(arg_keys[7], (WIDTH, 3 * WIDTH), WIDTH ** -0.5, 0.3125, ((0, 8), (1, 4)))
    output_weight = noise(arg_keys[8], (WIDTH, WIDTH), (WIDTH // 16) ** -0.5, 1.25, ((0, 8), (1, 4)))
    norm_gains = jnp.clip(1.0 + 0.18 * jax.random.normal(arg_keys[9], (3, WIDTH), jnp.float32), 0.1, 1.9)
    biases = noise(arg_keys[10], (10, WIDTH), 0.5, 3.0, (), jnp.float32)
    cotangent = noise(arg_keys[11], (MAPS, SIDE, SIDE, WIDTH), 1.0, 6.0, ((0, 8), (1, 4)))
    return dict(images=images, noise_field=noise_field, time_steps=time_steps, embedding=embedding, first_kernel=first_kernel, second_kernel=second_kernel, film_weight=film_weight, attend_weight=attend_weight, output_weight=output_weight, norm_gains=norm_gains, biases=biases, cotangent=cotangent)


@jax.custom_vjp
def low(v):
    return lax.optimization_barrier(v.astype(jnp.bfloat16)).astype(jnp.float32)

@jax.custom_vjp
def low_back(v):
    return v

def low_keep(v):
    return (low(v), None)

def low_pass(kept, grad):
    return (grad,)

def back_keep(v):
    return (v, None)

def back_low(kept, grad):
    return (low(grad),)
low.defvjp(low_keep, low_pass)
low_back.defvjp(back_keep, back_low)
EPS = 1e-05
OFFSET = 0.008
HIGH = lax.Precision.HIGHEST

def plan(time_steps):
    fraction = (time_steps.astype(jnp.float32) + 1.0) / STEPS
    start = jnp.square(jnp.cos(jnp.float32(OFFSET / (1.0 + OFFSET) * (math.pi / 2))))
    curve = jnp.square(jnp.cos((fraction + OFFSET) / (1.0 + OFFSET) * (math.pi / 2))) / start
    return (jnp.sqrt(curve), jnp.sqrt(1.0 - curve))

def group_norm(field, gain, shift):
    batch_size = field.shape[0]
    grouped = field.reshape(batch_size, PIXELS, GROUPS, WIDTH // GROUPS)
    center = lax.optimization_barrier(jnp.mean(grouped, axis=(1, 3), keepdims=True))
    variance = lax.optimization_barrier(jnp.mean(jnp.square(grouped - center), axis=(1, 3), keepdims=True))
    normed = (grouped - center) * lax.rsqrt(variance + EPS)
    return normed.reshape(field.shape) * gain + shift

def convolve(field, kernel, bias):
    convolved = lax.conv_general_dilated(field, kernel, (1, 1), 'SAME', dimension_numbers=('NHWC', 'HWIO', 'NHWC'), precision=HIGH)
    return convolved + bias

def attention(query, keys, values):
    batch_size = query.shape[0]
    block = min(512, PIXELS)
    blocks = PIXELS // block
    factor = 1.0 / math.sqrt(HEAD_DIM)
    query_blocks = jnp.moveaxis(query.reshape(batch_size, blocks, block, HEADS, HEAD_DIM), 1, 0)

    def one_block(query_part):
        scores = low_back(jnp.einsum('bqhd,bkhd->bhqk', query_part, keys, precision=HIGH) * factor)
        weights = low(jax.nn.softmax(scores, axis=3))
        return jnp.einsum('bhqk,bkhd->bqhd', weights, values, precision=HIGH)
    attended = lax.map(jax.checkpoint(one_block), query_blocks)
    return jnp.moveaxis(attended, 0, 1).reshape(batch_size, PIXELS, WIDTH)

def forward(images, embedding, first_kernel, second_kernel, film_weight, attend_weight, output_weight, norm_gains, biases, noise_field, keep_coef, noise_coef):
    batch_size = images.shape[0]
    mixed = keep_coef[:, None, None, None] * images + noise_coef[:, None, None, None] * noise_field
    first_act = low(jax.nn.silu(group_norm(mixed, norm_gains[0], biases[0])))
    first_conv = low_back(convolve(first_act, first_kernel, biases[3]))
    film = jnp.dot(low(jax.nn.silu(embedding)), film_weight, precision=HIGH) + jnp.concatenate([biases[5], biases[6]])
    film_scale = film[:, :WIDTH][:, None, None, :]
    film_shift = film[:, WIDTH:][:, None, None, :]
    second_pre = group_norm(first_conv, norm_gains[1], biases[1]) * (1.0 + film_scale) + film_shift
    second_act = low(jax.nn.silu(second_pre))
    second_conv = low_back(convolve(second_act, second_kernel, biases[4]))
    residual = mixed + second_conv
    attend_in = low(group_norm(residual, norm_gains[2], biases[2])).reshape(batch_size, PIXELS, WIDTH)
    projected = jnp.einsum('bpc,ce->bpe', attend_in, attend_weight, precision=HIGH)
    projected = projected + jnp.concatenate([biases[7], jnp.zeros_like(biases[7]), biases[8]])
    projected = low(low_back(projected)).reshape(batch_size, PIXELS, 3, HEADS, HEAD_DIM)
    attended = attention(projected[:, :, 0], projected[:, :, 1], projected[:, :, 2])
    attended = low(low_back(attended))
    branch = low_back(jnp.einsum('bpc,cd->bpd', attended, output_weight, precision=HIGH) + biases[9])
    return residual + branch.reshape(residual.shape)

def reference(images, noise_field, time_steps, embedding, first_kernel, second_kernel, film_weight, attend_weight, output_weight, norm_gains, biases, cotangent):
    keep_coef, noise_coef = plan(time_steps)
    weight_list = tuple((array.astype(jnp.float32) for array in (first_kernel, second_kernel, film_weight, attend_weight, output_weight, norm_gains, biases)))
    group_size = 4
    group_count = MAPS // group_size

    def regroup(array):
        return array.reshape((group_count, group_size) + array.shape[1:])
    batches = (regroup(images.astype(jnp.float32)), regroup(noise_field.astype(jnp.float32)), regroup(embedding.astype(jnp.float32)), regroup(keep_coef), regroup(noise_coef), regroup(cotangent.astype(jnp.float32)))

    def one_group(totals, batch_part):
        image_part, noise_part, embed_part, keep_part, spread_part, cot_part = batch_part

        def closed(image_in, embed_in, *weights):
            return forward(image_in, embed_in, *weights, noise_part, keep_part, spread_part)
        output_part, pullback = jax.vjp(closed, image_part, embed_part, *weight_list)
        gradients = pullback(cot_part)
        totals = tuple((total + grad for total, grad in zip(totals, gradients[2:])))
        return (totals, (output_part, gradients[0], gradients[1]))
    zero_totals = tuple((jnp.zeros_like(array) for array in weight_list))
    totals, (outputs, image_grads, embed_grads) = lax.scan(one_group, zero_totals, batches)
    full_shape = (MAPS, SIDE, SIDE, WIDTH)
    return (outputs.reshape(full_shape), image_grads.reshape(full_shape), embed_grads.reshape(MAPS, EMBED), totals[0], totals[1], totals[2], totals[3], totals[4], totals[5], totals[6])
```

```python
import math

import jax
import jax.numpy as jnp
import numpy as np
from jax import lax
from jax.experimental import pallas as pl
from jax.experimental.pallas import tpu as pltpu
from jax.sharding import PartitionSpec as P

HEAD_DIM = 96
GROUPS = 32
STEPS = 4000
EPS = 1e-05
OFFSET = 0.008
MESH = pl.DeviceIdType.MESH
F32 = jnp.float32
BF16 = jnp.bfloat16

PX = 1024
ROW = 32
CHUNK = 256
BLK = 96
HALF = 256
NHEAD = 4


def plan(time_steps):
    fraction = (time_steps.astype(F32) + 1.0) / STEPS
    start = jnp.square(jnp.cos(jnp.float32(OFFSET / (1.0 + OFFSET) * (math.pi / 2))))
    curve = jnp.square(jnp.cos((fraction + OFFSET) / (1.0 + OFFSET) * (math.pi / 2))) / start
    return (jnp.sqrt(curve), jnp.sqrt(1.0 - curve))


def channel_lanes():
    sel = np.zeros((2, 384, HALF), np.float32)
    for block in range(4):
        for j in range(BLK):
            sel[block % 2, block * BLK + j, (block // 2) * 128 + j] = 1.0
    return sel


def block_lanes(count):
    sel = np.zeros((count * BLK, count * 128), np.float32)
    for block in range(count):
        for j in range(BLK):
            sel[block * BLK + j, block * 128 + j] = 1.0
    return sel


def group_mask():
    lane = np.arange(HALF)
    ok = lane % 128 < BLK
    group = (lane // 128) * 100 + (lane % 128) // 12
    return ((group[:, None] == group[None, :]) & ok[:, None] & ok[None, :]).astype(np.float32)


def dot(a, b):
    return lax.dot_general(a, b, (((1,), (0,)), ((), ())), preferred_element_type=F32)


def dot_nt(a, b):
    return lax.dot_general(a, b, (((1,), (1,)), ((), ())), preferred_element_type=F32)


def dot_nt_high(a, b):
    return lax.dot_general(
        a, b, (((1,), (1,)), ((), ())), preferred_element_type=F32, precision=lax.Precision.HIGHEST
    )


def dot_tn_high(a, b):
    return lax.dot_general(
        a, b, (((0,), (0,)), ((), ())), preferred_element_type=F32, precision=lax.Precision.HIGHEST
    )


def exact_dot(values, ones):
    high = values.astype(BF16).astype(F32)
    rest = values - high
    middle = rest.astype(BF16).astype(F32)
    low = rest - middle
    rows = values.shape[0]
    out = dot(jnp.concatenate([high, middle, low], axis=0).astype(BF16), ones)
    return out[:rows] + out[rows : 2 * rows] + out[2 * rows :]


def sigmoid(v):
    return 1.0 / (1.0 + jnp.exp(-v))


def silu(v):
    return v / (1.0 + jnp.exp(-v))


def silu_slope(v):
    s = sigmoid(v)
    return s * (1.0 + v * (1.0 - s))


INPUTS = (
    "coef",
    "images",
    "noise",
    "cot",
    "emb",
    "k1",
    "k2",
    "wf",
    "wa",
    "wo",
    "gains",
    "biases",
    "sel",
    "gmask",
    "selp",
)
OUTPUTS = (
    "result",
    "image_grad",
    "embed_grad",
    "first",
    "second",
    "film",
    "attend",
    "output",
    "gains_out",
    "biases_out",
)


class Names:
    def __init__(self, names, refs):
        for name, ref in zip(names, refs):
            setattr(self, name, ref)


def scratch_list(n, inside):
    dma = pltpu.SemaphoreType.DMA
    items = []

    def vm(name, shape, dtype):
        items.append((name, pltpu.VMEM(shape, dtype)))

    def sem(name, count):
        items.append((name + "_s", dma((count,))))
        items.append((name + "_r", dma((count,))))

    for name in ("mx", "cx", "ro", "io"):
        vm(name + "_src", (4, CHUNK, HALF), BF16)
        vm(name + "_dst", (4, CHUNK, HALF), BF16)
        sem(name, 4)
    for name in ("act1", "act2"):
        vm(name, (2, PX + 2 * ROW, HALF), BF16)
        vm(name + "_t", (2, HALF, PX), BF16)
        sem(name, 4)
    vm("ai", (2, PX, HALF), BF16)
    vm("ai_t", (2, HALF, PX), BF16)
    sem("ai", 4)
    vm("att", (4, PX, 128), BF16)
    vm("att_t", (4, 128, PX), BF16)
    sem("att", 4)
    for name in ("do", "n3", "d2", "d1"):
        vm(name + "_src", (PX, HALF), BF16)
        vm(name + "_dst", (PX, HALF), BF16)
        sem(name, 4)
    vm("v2", (PX, HALF), F32)
    vm("v3", (PX, HALF), F32)
    vm("gres", (PX, HALF), F32)
    vm("gtmp", (PX, HALF), F32)
    vm("qkv", (6, PX, 128), BF16)
    vm("kvt", (4, 128, PX), BF16)
    vm("dout", (2, PX, 128), BF16)
    vm("dacc", (4, PX, 128), F32)
    vm("dproj", (6, PX, 128), BF16)
    vm("gr2", (3, PX + 2 * ROW, HALF), BF16)
    vm("gr1", (3, PX + 2 * ROW, HALF), BF16)
    vm("par", (16, 384), F32)
    vm("parown", (16, HALF), F32)
    vm("stat", (16, HALF), F32)
    vm("sums", (16, HALF), F32)
    if inside:
        vm("g1", (4, 4, 432, 128), BF16)
        vm("g2", (4, 4, 432, 128), BF16)
        vm("g3", (4, 4, 192, 128), BF16)
        for name in ("g1", "g2", "g3"):
            sem(name + "z", 4)
            sem(name + "v", 4)
            sem(name + "w", 8)
        vm("sw_src", (48, 128), BF16)
        vm("sw_dst", (48, 128), BF16)
        sem("sw", 1)
        vm("sb_src", (48, 128), F32)
        vm("sb_dst", (48, 128), F32)
        sem("sb", 1)
        for name, nc, rows in (("r1", 3, 144), ("r2", 3, 144), ("r3", 1, 192)):
            vm(name + "_acc", (nc, 4, 4, rows, 128), F32)
            vm(name + "w_src", (nc, 2, 4, rows, 128), BF16)
            vm(name + "w_dst", (nc, 2, 4, rows, 128), BF16)
            vm(name + "v_src", (nc, 4, rows, 128), BF16)
            vm(name + "v_dst", (nc, 4, rows, 128), BF16)
            vm(name + "z_src", (nc, 4, rows, 128), BF16)
            vm(name + "z_dst", (nc, 4, rows, 128), BF16)
            sem(name + "w", nc)
            sem(name + "v", nc)
            sem(name + "z", nc * 4)
    vm("el", (n, 2, 768), F32)
    sem("el", n)
    vm("em", (2 * n, 768), F32)
    vm("wfp", (128, HALF), BF16)
    vm("esel", (2 * n, 128), F32)
    vm("fp", (n, 2, HALF), F32)
    vm("fr", (n, 2, HALF), F32)
    sem("fr", n)
    vm("fx", (4, 1, 128), F32)
    vm("fh", (4, 1, 128), F32)
    sem("fh", 4)
    vm("ft", (4, 1, 128), F32)
    vm("th", (4, 1, 128), F32)
    sem("th", 4)
    vm("fa", (n, 2, HALF), F32)
    sem("fa", n)
    vm("fta", (2 * n, HALF), F32)
    vm("ep", (n, 2, 128), F32)
    vm("er", (n, 2, 128), F32)
    sem("er", n)
    vm("eh", (4, n, 2, 128), F32)
    sem("eh", 4)
    vm("ad", (n, 16, HALF), F32)
    sem("ad", n)
    vm("hb", (4, 16, HALF), F32)
    sem("hb", 4)
    return items


def make_kernel(n, inside, names):
    film_rows = 768 // n

    def kernel(*refs):
        r = Names(names, refs)
        d = lax.axis_index("dp")
        h = lax.axis_index("head")
        x = h // 2
        c = h - 2 * x
        z = d // 2
        y = d - 2 * z
        sib = (d, h + 1 - 2 * c)
        xdev = (d, h + 2 - 4 * x)
        v = x + c * (y - x)
        w = y + c * (x - y)
        vdev = (d + c * (1 - 2 * y), h + (1 - c) * (2 - 4 * x))
        wdev = (d + (1 - c) * (1 - 2 * y), h + c * (2 - 4 * x))

        def slot(xx, yy):
            if inside:
                return (yy + c * (xx - yy)) * 2 + xx + c * (yy - xx)
            return yy * 2 + xx

        def rc(src, dst, send, recv, dev):
            return pltpu.make_async_remote_copy(
                src_ref=src, dst_ref=dst, send_sem=send, recv_sem=recv, device_id=dev, device_id_type=MESH
            )

        def loop(count, body):
            def step(i, carry):
                body(i)
                return carry

            lax.fori_loop(0, count, step, 0)

        def rows(i, size=CHUNK, base=0):
            return pl.ds(pl.multiple_of(base + i * size, 32), size)

        def dp_start(src_of, dst, send, recv):
            def step(k, carry):
                peer = lax.rem(d + k, n)
                rc(src_of(peer), dst.at[d], send.at[k], recv.at[d], (peer, h)).start()
                return carry

            lax.fori_loop(1, n, step, 0)

        def dp_wait(src_of, dst, send, recv):
            def step(k, carry):
                peer = lax.rem(d + k, n)
                copy = rc(src_of(peer), dst.at[peer], send.at[k], recv.at[peer], (peer, h))
                copy.wait_recv()
                copy.wait_send()
                return carry

            lax.fori_loop(1, n, step, 0)

        def head_start(src_of, dst, send, recv):
            for k in range(1, 4):
                peer = lax.rem(h + k, 4)
                rc(src_of(peer), dst.at[h], send.at[k], recv.at[h], (d, peer)).start()

        def head_wait(src_of, dst, send, recv):
            for k in range(1, 4):
                peer = lax.rem(h + k, 4)
                copy = rc(src_of(peer), dst.at[peer], send.at[k], recv.at[peer], (d, peer))
                copy.wait_recv()
                copy.wait_send()

        class Halves:
            def __init__(self, name, base):
                self.buf, self.base = getattr(r, name), base
                self.send, self.recv = getattr(r, name + "_s"), getattr(r, name + "_r")

            def at(self, core, i):
                return self.buf.at[core, rows(i, CHUNK, self.base)]

            def start(self, i):
                ref = self.at(c, i)
                rc(ref, ref, self.send.at[i], self.recv.at[i], sib).start()

            def wait(self):
                for i in range(4):
                    ref = self.at(1 - c, i)
                    copy = rc(ref, ref, self.send.at[i], self.recv.at[i], sib)
                    copy.wait_recv()
                    copy.wait_send()

        class Parts:
            def __init__(self, name):
                self.src, self.dst = getattr(r, name + "_src"), getattr(r, name + "_dst")
                self.send, self.recv = getattr(r, name + "_s"), getattr(r, name + "_r")

            def start(self, i):
                rc(self.src.at[rows(i)], self.dst.at[rows(i)], self.send.at[i], self.recv.at[i], sib).start()

            def wait(self, i):
                copy = rc(self.src.at[rows(i)], self.dst.at[rows(i)], self.send.at[i], self.recv.at[i], sib)
                copy.wait_recv()
                copy.wait_send()

        class Gather:
            def __init__(self, name):
                self.g = getattr(r, name)
                self.zs, self.zr = getattr(r, name + "z_s"), getattr(r, name + "z_r")
                self.vs, self.vr = getattr(r, name + "v_s"), getattr(r, name + "v_r")
                self.ws, self.wr = getattr(r, name + "w_s"), getattr(r, name + "w_r")

            def zcopy(self, k, zslot):
                ref = self.g.at[w * 2 + v, zslot]
                return rc(ref, ref, self.zs.at[k], self.zr.at[zslot], (lax.rem(z + k, 4) * 2 + y, h))

            def vcopy(self, vv, zz):
                ref = self.g.at[w * 2 + vv, zz]
                return rc(ref, ref, self.vs.at[zz], self.vr.at[zz], vdev)

            def wcopy(self, ww, vv, zz):
                ref = self.g.at[ww * 2 + vv, zz]
                return rc(ref, ref, self.ws.at[vv * 4 + zz], self.wr.at[vv * 4 + zz], wdev)

            def own(self):
                for k in range(1, 4):
                    self.zcopy(k, z).start()
                self.vcopy(v, z).start()
                self.wcopy(w, v, z).start()

            def pass_z(self):
                self.vcopy(1 - v, z).wait_recv()
                self.wcopy(w, 1 - v, z).start()

                def step(k, carry):
                    zz = lax.rem(z + k, 4)
                    self.zcopy(k, zz).wait_recv()
                    self.vcopy(v, zz).start()
                    self.wcopy(w, v, zz).start()
                    return carry

                lax.fori_loop(1, 4, step, 0)

            def pass_v(self):
                def step(k, carry):
                    zz = lax.rem(z + k, 4)
                    self.vcopy(1 - v, zz).wait_recv()
                    self.wcopy(w, 1 - v, zz).start()
                    return carry

                lax.fori_loop(1, 4, step, 0)

            def done(self):
                def zstep(k, carry):
                    self.zcopy(k, z).wait_send()
                    return carry

                lax.fori_loop(1, 4, zstep, 0)

                def step(zz, carry):
                    self.vcopy(v, zz).wait_send()
                    for vv in range(2):
                        self.wcopy(1 - w, vv, zz).wait_recv()
                        self.wcopy(w, vv, zz).wait_send()
                    return carry

                lax.fori_loop(0, 4, step, 0)

        class Reduce:
            def __init__(self, name, count):
                get = lambda tail: getattr(r, name + tail)
                self.acc, self.count = get("_acc"), count
                self.wsrc, self.wdst, self.ws, self.wr = get("w_src"), get("w_dst"), get("w_s"), get("w_r")
                self.vsrc, self.vdst, self.vs, self.vr = get("v_src"), get("v_dst"), get("v_s"), get("v_r")
                self.zsrc, self.zdst, self.zs, self.zr = get("z_src"), get("z_dst"), get("z_s"), get("z_r")

            def wcopy(self, a):
                return rc(self.wsrc.at[a], self.wdst.at[a], self.ws.at[a], self.wr.at[a], wdev)

            def vcopy(self, a):
                return rc(self.vsrc.at[a], self.vdst.at[a], self.vs.at[a], self.vr.at[a], vdev)

            def zcopy(self, a, k, dst):
                peer = lax.rem(z + k, 4)
                return rc(
                    self.zsrc.at[a, peer],
                    self.zdst.at[a, dst],
                    self.zs.at[a * 4 + k],
                    self.zr.at[a * 4 + dst],
                    (peer * 2 + y, h),
                )

            def start(self, a):
                def step(i, carry):
                    vv, zz = i // 4, lax.rem(i, 4)
                    self.wsrc[a, vv, zz] = self.acc[a, (1 - w) * 2 + vv, zz].astype(BF16)
                    return carry

                lax.fori_loop(0, 8, step, 0)
                self.wcopy(a).start()

            def second(self, a):
                self.wcopy(a).wait_recv()

                def step(zz, carry):
                    self.vsrc[a, zz] = (
                        self.acc[a, w * 2 + 1 - v, zz] + self.wdst[a, 1 - v, zz].astype(F32)
                    ).astype(BF16)
                    self.acc[a, w * 2 + v, zz] = self.acc[a, w * 2 + v, zz] + self.wdst[a, v, zz].astype(F32)
                    return carry

                lax.fori_loop(0, 4, step, 0)
                self.vcopy(a).start()

            def third(self, a):
                self.vcopy(a).wait_recv()

                def step(zz, carry):
                    total = self.acc[a, w * 2 + v, zz] + self.vdst[a, zz].astype(F32)
                    self.acc[a, w * 2 + v, zz] = total
                    self.zsrc[a, zz] = total.astype(BF16)
                    return carry

                lax.fori_loop(0, 4, step, 0)
                for k in range(1, 4):
                    self.zcopy(a, k, z).start()

            def last(self, a):
                total = self.acc[a, w * 2 + v, z]
                for k in range(1, 4):
                    peer = lax.rem(z + k, 4)
                    copy = self.zcopy(a, k, peer)
                    copy.wait_recv()
                    copy.wait_send()
                    total = total + self.zdst[a, peer].astype(F32)
                self.wcopy(a).wait_send()
                self.vcopy(a).wait_send()
                return total

        def wtile(g, tap, zc, xx):
            return jnp.concatenate(
                [
                    g[slot(xx, 0), zc, pl.ds(tap * 48, 48), :],
                    g[slot(xx, 1), zc, pl.ds(tap * 48, 48), :],
                    jnp.zeros((32, 128), BF16),
                ],
                axis=0,
            )

        def wtap(g, tap, zcs):
            return jnp.concatenate(
                [jnp.concatenate([wtile(g, tap, zc, xx) for xx in range(2)], axis=1) for zc in zcs], axis=0
            )

        ALL = (0, 2, 1, 3)

        def half_of(core):
            return (core, core + 2)

        def wproj(zcs):
            return jnp.concatenate(
                [
                    jnp.concatenate([wtile(r.g3, j, zc, xx) for xx in range(2) for j in range(3)], axis=1)
                    for zc in zcs
                ],
                axis=0,
            )

        def flat(buf, base, i, size):
            return jnp.concatenate([buf[0, rows(i, size, base), :], buf[1, rows(i, size, base), :]], axis=1)

        barrier = pltpu.get_barrier_semaphore()

        def greet(k, carry):
            pl.semaphore_signal(barrier, inc=1, device_id=(lax.rem(d + k, n), h), device_id_type=MESH)
            return carry

        lax.fori_loop(1, n, greet, 0)
        for k in range(1, 4):
            pl.semaphore_signal(barrier, inc=1, device_id=(d, lax.rem(h + k, 4)), device_id_type=MESH)
        if inside:
            pad = jnp.zeros((48, 32), BF16)
            for tap in range(9):
                r.g1[w * 2 + v, z, pl.ds(tap * 48, 48), :] = jnp.concatenate([r.k1[tap], pad], axis=1)
        pl.semaphore_wait(barrier, n - 1 + 3)
        if inside:
            ga, gb, gc = Gather("g1"), Gather("g2"), Gather("g3")
            ga.own()

        def mix(m, carry):
            field = r.coef[0, m] * r.images[m].astype(F32) + r.coef[1, m] * r.noise[m].astype(F32)
            low = field.astype(BF16)
            for core in range(2):
                r.mx_src[m * 2 + core] = dot(low, r.sel[core]).astype(BF16)
            return carry

        lax.fori_loop(0, 2, mix, 0)
        head_start(lambda p: r.mx_src.at[p], r.mx_dst, r.mx_s, r.mx_r)
        r.mx_dst[h] = r.mx_src[h]

        emb = r.emb[...].astype(F32)
        r.el[d] = silu(emb).astype(BF16).astype(F32)
        dp_start(lambda p: r.el.at[d], r.el, r.el_s, r.el_r)

        if inside:
            blocks = dot(r.wa[...], r.selp[: 3 * BLK, : 3 * 128]).astype(BF16)
            r.sw_src[...] = blocks[:, 128:256]
            swap = rc(r.sw_src, r.sw_dst, r.sw_s.at[0], r.sw_r.at[0], sib)
            swap.start()
            for tap in range(9):
                r.g2[w * 2 + v, z, pl.ds(tap * 48, 48), :] = jnp.concatenate([r.k2[tap], pad], axis=1)
            me3 = r.g3.at[w * 2 + v, z]
            me3[pl.ds(pl.multiple_of(c * 48, 16), 48), :] = blocks[:, :128]
            me3[pl.ds(pl.multiple_of(48 + c * 48, 16), 48), :] = blocks[:, 256:]
            me3[pl.ds(144, 48), :] = jnp.concatenate([r.wo[...], pad], axis=1)
        r.par[0:3, :] = r.gains[...]
        r.par[3:13, :] = r.biases[...]
        r.par[13:16, :] = jnp.zeros((3, 384), F32)
        r.parown[...] = exact_dot(r.par[...], r.sel[c])

        def prow(i):
            return r.parown[pl.ds(i, 1), :]

        for buf in (r.act1, r.act2):
            for core in range(2):
                buf[core, pl.ds(0, ROW), :] = jnp.zeros((ROW, HALF), BF16)
                buf[core, pl.ds(PX + ROW, ROW), :] = jnp.zeros((ROW, HALF), BF16)
        for buf in (r.gr1, r.gr2):
            for b in range(3):
                buf[b, pl.ds(0, ROW), :] = jnp.zeros((ROW, HALF), BF16)
                buf[b, pl.ds(PX + ROW, ROW), :] = jnp.zeros((ROW, HALF), BF16)
        r.wfp[...] = jnp.zeros((128, HALF), BF16)
        r.wfp[pl.ds(0, film_rows), :] = dot(r.wf[...], r.selp[: 2 * BLK, :HALF]).astype(BF16)
        if inside:
            ga.pass_z()
            gb.own()

        count = float(PX * 12)

        def fold(vals):
            return jnp.sum(vals.reshape(CHUNK // 8, 8, HALF), axis=0)

        def sums_of(fn, k):
            def step(i, carry):
                return tuple(a + fold(b) for a, b in zip(carry, fn(i)))

            zero = jnp.zeros((8, HALF), F32)
            return lax.fori_loop(0, 4, step, (zero,) * k)

        def group_mean(part):
            return jnp.sum(exact_dot(part, r.gmask[...]), axis=0, keepdims=True) / count

        def norm(load, which):
            (total,) = sums_of(lambda i: (load(i),), 1)
            mean = group_mean(total)
            (square,) = sums_of(lambda i: (jnp.square(load(i) - mean),), 1)
            inv = lax.rsqrt(group_mean(square) + EPS)
            r.stat[pl.ds(2 * which, 1), :] = mean
            r.stat[pl.ds(2 * which + 1, 1), :] = inv
            return mean, inv

        def norm_back(load_grad, load_hat, coef, inv, sum_row):
            plain, cross = sums_of(lambda i: (load_grad(i), load_grad(i) * load_hat(i)), 2)
            plain_mean, cross_mean = group_mean(coef * plain), group_mean(coef * cross)

            def chunk(i):
                return inv * (coef * load_grad(i) - plain_mean - load_hat(i) * cross_mean)

            return (
                jnp.sum(plain, axis=0, keepdims=True),
                jnp.sum(cross, axis=0, keepdims=True),
                chunk,
            )

        head_wait(lambda p: r.mx_src.at[p], r.mx_dst, r.mx_s, r.mx_r)

        def mixed(i):
            return r.mx_dst[i].astype(F32)

        mean1, inv1 = norm(mixed, 0)
        gain1, shift1 = prow(0), prow(3)
        act1 = Halves("act1", ROW)

        def pre1(i):
            return (mixed(i) - mean1) * inv1 * gain1 + shift1

        def first_act(i):
            r.act1[c, rows(i, CHUNK, ROW), :] = silu(pre1(i)).astype(BF16)
            act1.start(i)

        loop(4, first_act)
        if inside:
            ga.pass_v()

        dp_wait(lambda p: r.el.at[d], r.el, r.el_s, r.el_r)
        for j in range(n):
            r.em[pl.ds(2 * j, 2), :] = r.el[j]
        place = lax.broadcasted_iota(jnp.int32, (768, 128), 0) - film_rows * d
        lane = lax.broadcasted_iota(jnp.int32, (768, 128), 1)
        pick = jnp.where((place == lane) & (lane < film_rows), 1.0, 0.0).astype(BF16)
        r.esel[...] = dot(r.em[...].astype(BF16), pick)
        film_part = dot(r.esel[...].astype(BF16), r.wfp[...])
        for j in range(n):
            r.fp[j] = film_part[2 * j : 2 * j + 2]
        dp_start(lambda p: r.fp.at[p], r.fr, r.fr_s, r.fr_r)
        r.fr[d] = r.fp[d]
        if inside:
            swap.wait()
            me3[pl.ds(pl.multiple_of(96 - c * 96, 16), 48), :] = r.sw_dst[...]
            gb.pass_z()
            gc.own()
        dp_wait(lambda p: r.fp.at[p], r.fr, r.fr_s, r.fr_r)
        film_sum = r.fr[0]
        for j in range(1, n):
            film_sum = film_sum + r.fr[j]
        for m in range(2):
            for core in range(2):
                r.fx[m * 2 + core] = film_sum[m : m + 1, core * 128 : core * 128 + 128]
        head_start(lambda p: r.fx.at[p], r.fh, r.fh_s, r.fh_r)
        r.fh[h] = r.fx[h]

        def split_cot(m, carry):
            for core in range(2):
                r.cx_src[m * 2 + core] = dot(r.cot[m], r.sel[core]).astype(BF16)
            return carry

        lax.fori_loop(0, 2, split_cot, 0)
        head_start(lambda p: r.cx_src.at[p], r.cx_dst, r.cx_s, r.cx_r)
        r.cx_dst[h] = r.cx_src[h]

        column = lax.broadcasted_iota(jnp.int32, (CHUNK, HALF), 0) % ROW
        not_first = column > 0
        not_last = column < ROW - 1

        def from_left(vals):
            return jnp.where(not_first, pltpu.roll(vals, 1, 0), 0.0)

        def from_right(vals):
            return jnp.where(not_last, pltpu.roll(vals, CHUNK - 1, 0), 0.0)

        def conv(buf, g, store):
            weights = lambda: jnp.concatenate(
                [jnp.concatenate([wtap(g, 3 * a + b, ALL) for b in range(3)], axis=1) for a in range(3)], axis=0
            )

            def step(i):
                left = jnp.concatenate([flat(buf, ROW * a, i, CHUNK) for a in range(3)], axis=1)
                out = dot(left, weights())
                store(
                    i,
                    out[:, HALF : 2 * HALF] + from_left(out[:, :HALF]) + from_right(out[:, 2 * HALF :]),
                )

            loop(4, step)

        act1.wait()
        if inside:
            ga.done()

        def store_v2(i, vals):
            r.v2[rows(i), :] = vals + prow(6)

        conv(r.act1, r.g1, store_v2)
        if inside:
            gb.pass_v()
        head_wait(lambda p: r.fx.at[p], r.fh, r.fh_s, r.fh_r)
        scale = 1.0 + (jnp.concatenate([r.fh[0], r.fh[1]], axis=1) + prow(8))
        shift = jnp.concatenate([r.fh[2], r.fh[3]], axis=1) + prow(9)
        mean2, inv2 = norm(lambda i: r.v2[rows(i), :], 1)
        gain2, shift2 = prow(1), prow(4)
        act2 = Halves("act2", ROW)

        def hat2(i):
            return (r.v2[rows(i), :] - mean2) * inv2

        def pre2(i):
            return (hat2(i) * gain2 + shift2) * scale + shift

        def second_act(i):
            r.act2[c, rows(i, CHUNK, ROW), :] = silu(pre2(i)).astype(BF16)
            act2.start(i)

        loop(4, second_act)
        if inside:
            gc.pass_z()

        act2.wait()
        if inside:
            gb.done()

        def store_v3(i, vals):
            r.v3[rows(i), :] = mixed(i) + (vals + prow(7))

        conv(r.act2, r.g2, store_v3)
        if inside:
            gc.pass_v()
        mean3, inv3 = norm(lambda i: r.v3[rows(i), :], 2)
        gain3, shift3 = prow(2), prow(5)
        ai = Halves("ai", 0)

        def hat3(i):
            return (r.v3[rows(i), :] - mean3) * inv3

        def attend_in(i):
            r.ai[c, rows(i), :] = (hat3(i) * gain3 + shift3).astype(BF16)
            ai.start(i)

        loop(4, attend_in)

        if inside:
            gc.done()
        head_wait(lambda p: r.cx_src.at[p], r.cx_dst, r.cx_s, r.cx_r)
        dop = Parts("do")

        def do_other(i):
            r.do_src[rows(i), :] = dot_nt(r.cx_dst[i], wtap(r.g3, 3, half_of(1 - c))).astype(BF16)
            dop.start(i)

        loop(4, do_other)

        ai.wait()
        bias_proj = [prow(10)[:, :128], prow(10)[:, 128:], None, None, prow(11)[:, :128], prow(11)[:, 128:]]

        def project(i):
            out = dot(flat(r.ai, 0, i, CHUNK), wproj(ALL))
            for k in range(6):
                part = out[:, k * 128 : k * 128 + 128]
                if bias_proj[k] is not None:
                    part = part + bias_proj[k]
                r.qkv[k, rows(i), :] = part.astype(BF16)

        loop(4, project)

        def do_own(i):
            own = dot_nt(r.cx_dst[i], wtap(r.g3, 3, half_of(c)))
            dop.wait(i)
            full = (own + r.do_dst[rows(i), :].astype(F32)).astype(BF16)
            for k in range(2):
                r.dout[k, rows(i), :] = full[:, k * 128 : k * 128 + 128]

        loop(4, do_own)

        factor = 1.0 / math.sqrt(HEAD_DIM)
        factor2 = factor * math.log2(math.e)
        att = []

        def transposes(k):
            r.kvt[k] = jnp.transpose(r.qkv[k + 2])

        loop(4, transposes)

        def att_ref(core, k):
            return r.att.at[core * 2 + k]

        def one_head(k):
            r.dacc[k] = jnp.zeros((PX, 128), F32)
            r.dacc[2 + k] = jnp.zeros((PX, 128), F32)

            def one_block(b):
                query = r.qkv[k, rows(b), :]
                grad = r.dout[k, rows(b), :]
                scores = dot_nt(r.qkv[2 + k], query)
                peak = jnp.max(scores, axis=0, keepdims=True)
                expo = jnp.exp2((scores - peak) * factor2)
                probs = expo * (1.0 / jnp.sum(expo, axis=0, keepdims=True))
                low = probs.astype(BF16)
                got = dot(r.kvt[2 + k], low)
                r.att[2 * c + k, rows(b), :] = jnp.transpose(got).astype(BF16)
                r.dacc[2 + k] = r.dacc[2 + k] + dot(low, grad)
                probs_grad = dot_nt(r.qkv[4 + k], grad)
                spread = jnp.sum(probs * probs_grad, axis=0, keepdims=True)
                scores_grad = (probs * (probs_grad - spread)).astype(BF16)
                back = dot(r.kvt[k], scores_grad)
                r.dproj[k, rows(b), :] = (jnp.transpose(back) * factor).astype(BF16)
                r.dacc[k] = r.dacc[k] + dot(scores_grad, query)

            loop(4, one_block)
            r.dproj[2 + k] = (r.dacc[k] * factor).astype(BF16)
            r.dproj[4 + k] = r.dacc[2 + k].astype(BF16)
            ref = att_ref(c, k)
            rc(ref, ref, r.att_s.at[k], r.att_r.at[k], sib).start()

        loop(2, one_head)

        n3 = Parts("n3")

        def proj_rows(i):
            return jnp.concatenate([r.dproj[k, rows(i), :] for k in range(6)], axis=1)

        def n3_other(i):
            r.n3_src[rows(i), :] = dot_nt(proj_rows(i), wproj(half_of(1 - c))).astype(BF16)
            n3.start(i)

        loop(4, n3_other)

        def n3_own(i):
            own = dot_nt(proj_rows(i), wproj(half_of(c)))
            n3.wait(i)
            r.gtmp[rows(i), :] = own + r.n3_dst[rows(i), :].astype(F32)

        loop(4, n3_own)
        plain3, cross3, back3 = norm_back(lambda i: r.gtmp[rows(i), :], hat3, gain3, inv3, 0)
        r.sums[pl.ds(2, 1), :] = cross3
        r.sums[pl.ds(3 + 2, 1), :] = plain3

        def shifted(buf, i, vals):
            buf[0, rows(i, CHUNK, ROW), :] = from_right(vals).astype(BF16)
            buf[1, rows(i, CHUNK, ROW), :] = vals.astype(BF16)
            buf[2, rows(i, CHUNK, ROW), :] = from_left(vals).astype(BF16)

        def residual_back(i, carry):
            vals = r.cx_dst[i].astype(F32) + back3(i)
            r.gres[rows(i), :] = vals
            shifted(r.gr2, i, vals)
            return carry + fold(vals.astype(BF16).astype(F32))

        bias_two = lax.fori_loop(0, 4, residual_back, jnp.zeros((8, HALF), F32))
        r.sums[pl.ds(3 + 4, 1), :] = jnp.sum(bias_two, axis=0, keepdims=True)

        def act_back(buf, g, core, i, size):
            left = jnp.concatenate(
                [buf[b, rows(i, size, 2 * ROW - ROW * a), :] for a in range(3) for b in range(3)], axis=1
            )
            right = jnp.concatenate(
                [wtap(g, 3 * a + b, half_of(core)) for a in range(3) for b in range(3)], axis=1
            )
            return dot_nt(left, right)

        def conv_back(parts, buf, g, name):
            def other(i):
                getattr(r, name + "_src")[rows(i), :] = act_back(buf, g, 1 - c, i, CHUNK).astype(BF16)
                parts.start(i)

            loop(4, other)

        def conv_back_own(parts, buf, g, name, store):
            def own(i):
                vals = act_back(buf, g, c, i, CHUNK)
                parts.wait(i)
                store(i, vals + getattr(r, name + "_dst")[rows(i), :].astype(F32))

            loop(4, own)

        def transpose_act(buf, base, out):
            for core in range(2):
                for q in range(4):
                    out[core, :, pl.ds(q * CHUNK, CHUNK)] = jnp.transpose(
                        buf[core, pl.ds(base + q * CHUNK, CHUNK), :]
                    )

        def slots(acc, a, zc, xx, yy, row, value):
            acc[a, slot(xx, yy), zc, pl.ds(row * 48, 48), :] = value

        def kernel_grad(act_t, buf, acc, after):
            def step(a, carry):
                right = jnp.concatenate(
                    [buf[b, pl.ds(pl.multiple_of(2 * ROW - ROW * a, 32), PX), :] for b in range(3)], axis=1
                )
                for core in range(2):
                    out = dot(act_t[core], right)
                    for k in range(2):
                        for yy in range(2):
                            for b in range(3):
                                for xx in range(2):
                                    low_row = k * 128 + yy * 48
                                    lane0 = b * HALF + xx * 128
                                    slots(
                                        acc,
                                        a,
                                        core + 2 * k,
                                        xx,
                                        yy,
                                        b,
                                        out[low_row : low_row + 48, lane0 : lane0 + 128],
                                    )
                after(a)
                return carry

            lax.fori_loop(0, 3, step, 0)

        d2 = Parts("d2")
        conv_back(d2, r.gr2, r.g2, "d2")
        if inside:
            red1, red2, red3 = Reduce("r1", 3), Reduce("r2", 3), Reduce("r3", 1)
            acc1, acc2, acc3 = r.r1_acc, r.r2_acc, r.r3_acc
        else:
            acc1, acc2, acc3 = r.first, r.second, r.attend

        transpose_act(r.act2, ROW, r.act2_t)
        kernel_grad(r.act2_t, r.gr2, acc2, red2.start if inside else lambda a: None)

        def store_pre2(i, vals):
            r.gtmp[rows(i), :] = vals * silu_slope(pre2(i))

        conv_back_own(d2, r.gr2, r.g2, "d2", store_pre2)

        plain2, cross2, back2 = norm_back(lambda i: r.gtmp[rows(i), :], hat2, gain2 * scale, inv2, 1)
        r.sums[pl.ds(1, 1), :] = scale * cross2
        r.sums[pl.ds(3 + 1, 1), :] = scale * plain2
        film_scale_term = gain2 * cross2 + shift2 * plain2
        r.sums[pl.ds(3 + 5, 1), :] = film_scale_term
        r.sums[pl.ds(3 + 6, 1), :] = plain2
        for j in range(2):
            r.ft[j] = film_scale_term[:, j * 128 : j * 128 + 128]
            r.ft[2 + j] = plain2[:, j * 128 : j * 128 + 128]
        head_start(lambda p: r.ft.at[p], r.th, r.th_s, r.th_r)
        r.th[h] = r.ft[h]

        def first_back(i, carry):
            vals = back2(i)
            shifted(r.gr1, i, vals)
            return carry + fold(vals.astype(BF16).astype(F32))

        bias_one = lax.fori_loop(0, 4, first_back, jnp.zeros((8, HALF), F32))
        r.sums[pl.ds(3 + 3, 1), :] = jnp.sum(bias_one, axis=0, keepdims=True)

        d1 = Parts("d1")
        conv_back(d1, r.gr1, r.g1, "d1")
        transpose_act(r.act1, ROW, r.act1_t)
        kernel_grad(r.act1_t, r.gr1, acc1, red1.start if inside else lambda a: None)

        if inside:
            for a in range(3):
                red2.second(a)

        for k in range(2):
            ref = att_ref(1 - c, k)
            copy = rc(ref, ref, r.att_s.at[k], r.att_r.at[k], sib)
            copy.wait_recv()
            copy.wait_send()

        def result(i):
            left = jnp.concatenate([r.att[p, rows(i), :] for p in range(4)], axis=1)
            branch = dot(left, wtap(r.g3, 3, ALL)) + prow(12)
            r.ro_src[i] = (r.v3[rows(i), :] + branch).astype(BF16)

        loop(4, result)
        head_start(lambda p: r.ro_src.at[p], r.ro_dst, r.ro_s, r.ro_r)
        r.ro_dst[h] = r.ro_src[h]

        def transpose_att(p):
            r.att_t[p] = jnp.transpose(r.att[p])

        loop(4, transpose_att)
        transpose_act(r.ai, 0, r.ai_t)
        right = jnp.concatenate([r.dproj[k] for k in range(6)], axis=1)
        for core in range(2):
            out = dot(r.ai_t[core], right)
            for k in range(2):
                for yy in range(2):
                    for xx in range(2):
                        for j in range(3):
                            low_row = k * 128 + yy * 48
                            lane0 = (xx * 3 + j) * 128
                            slots(
                                acc3, 0, core + 2 * k, xx, yy, j, out[low_row : low_row + 48, lane0 : lane0 + 128]
                            )
        cot_rows = jnp.concatenate([r.cx_dst[i] for i in range(4)], axis=0)
        for p in range(4):
            out = dot(r.att_t[p], cot_rows)
            for yy in range(2):
                for xx in range(2):
                    slots(
                        acc3,
                        0,
                        p // 2 + 2 * (p % 2),
                        xx,
                        yy,
                        3,
                        out[yy * 48 : yy * 48 + 48, xx * 128 : xx * 128 + 128],
                    )
        if inside:
            red3.start(0)

        def proj_sums(i, carry):
            q = jnp.concatenate([r.dproj[0, rows(i), :], r.dproj[1, rows(i), :]], axis=1).astype(F32)
            val = jnp.concatenate([r.dproj[4, rows(i), :], r.dproj[5, rows(i), :]], axis=1).astype(F32)
            return (carry[0] + fold(q), carry[1] + fold(val), carry[2] + fold(r.cx_dst[i].astype(F32)))

        zero8 = jnp.zeros((8, HALF), F32)
        qsum, vsum, csum = lax.fori_loop(0, 4, proj_sums, (zero8, zero8, zero8))
        r.sums[pl.ds(3 + 7, 1), :] = jnp.sum(qsum, axis=0, keepdims=True)
        r.sums[pl.ds(3 + 8, 1), :] = jnp.sum(vsum, axis=0, keepdims=True)
        r.sums[pl.ds(3 + 9, 1), :] = jnp.sum(csum, axis=0, keepdims=True)
        r.sums[pl.ds(13, 3), :] = jnp.zeros((3, HALF), F32)

        head_wait(lambda p: r.ft.at[p], r.th, r.th_s, r.th_r)
        for m in range(2):
            r.fa[d, pl.ds(m, 1), :] = jnp.concatenate([r.th[2 * m], r.th[2 * m + 1]], axis=1)
        dp_start(lambda p: r.fa.at[d], r.fa, r.fa_s, r.fa_r)

        def store_pre1(i, vals):
            r.gtmp[rows(i), :] = vals * silu_slope(pre1(i))

        conv_back_own(d1, r.gr1, r.g1, "d1", store_pre1)

        def hat1(i):
            return (mixed(i) - mean1) * inv1

        plain1, cross1, back1 = norm_back(lambda i: r.gtmp[rows(i), :], hat1, gain1, inv1, 0)
        r.sums[pl.ds(0, 1), :] = cross1
        r.sums[pl.ds(3, 1), :] = plain1
        r.ad[d] = r.sums[...]
        dp_start(lambda p: r.ad.at[d], r.ad, r.ad_s, r.ad_r)

        keep = r.coef[0, x]

        def image_back(i):
            r.io_src[i] = (keep * (r.gres[rows(i), :] + back1(i))).astype(BF16)

        loop(4, image_back)
        head_start(lambda p: r.io_src.at[p], r.io_dst, r.io_s, r.io_r)
        r.io_dst[h] = r.io_src[h]
        if inside:
            for a in range(3):
                red1.second(a)
            red3.second(0)
            for a in range(3):
                red2.third(a)

        dp_wait(lambda p: r.fa.at[d], r.fa, r.fa_s, r.fa_r)
        for j in range(n):
            r.fta[pl.ds(2 * j, 2), :] = r.fa[j]
        film_block = dot_tn_high(r.esel[...], r.fta[...])
        r.film[...] = jnp.concatenate([film_block[:film_rows, :BLK], film_block[:film_rows, 128 : 128 + BLK]], axis=1)
        embed_part = dot_nt_high(r.fta[...], r.wfp[...].astype(F32))
        for j in range(n):
            r.ep[j] = embed_part[2 * j : 2 * j + 2]
        dp_start(lambda p: r.ep.at[p], r.er, r.er_s, r.er_r)
        r.er[d] = r.ep[d]

        dp_wait(lambda p: r.ad.at[d], r.ad, r.ad_s, r.ad_r)
        total = r.ad[0]
        for j in range(1, n):
            total = total + r.ad[j]
        r.hb[h] = total
        head_start(lambda p: r.hb.at[h], r.hb, r.hb_s, r.hb_r)
        if inside:
            for a in range(3):
                red1.third(a)
            red3.third(0)

        head_wait(lambda p: r.ro_src.at[p], r.ro_dst, r.ro_s, r.ro_r)

        def unpack(buf, m):
            return dot_nt(buf[2 * m], r.sel[0]) + dot_nt(buf[2 * m + 1], r.sel[1])

        def out_result(m):
            r.result[m] = unpack(r.ro_dst, m)

        loop(2, out_result)

        dp_wait(lambda p: r.ep.at[p], r.er, r.er_s, r.er_r)
        r.eh[h] = r.er[...]
        head_start(lambda p: r.eh.at[h], r.eh, r.eh_s, r.eh_r)

        if inside:
            for a in range(3):
                total = red2.last(a)
                for b in range(3):
                    r.second[3 * a + b] = total[b * 48 : b * 48 + 48, :BLK]

        head_wait(lambda p: r.hb.at[h], r.hb, r.hb_s, r.hb_r)
        even = r.hb[0] + r.hb[2]
        odd = r.hb[1] + r.hb[3]
        wide = jnp.concatenate(
            [even[:, :BLK], odd[:, :BLK], even[:, 128 : 128 + BLK], odd[:, 128 : 128 + BLK]], axis=1
        )
        r.gains_out[...] = wide[0:3]
        r.biases_out[...] = wide[3:13]

        head_wait(lambda p: r.eh.at[h], r.eh, r.eh_s, r.eh_r)
        pieces = []
        for j in range(n):
            piece = (r.eh[0, j] + r.eh[1, j]) + (r.eh[2, j] + r.eh[3, j])
            pieces.append(piece[:, :film_rows])
        r.embed_grad[...] = jnp.concatenate(pieces, axis=1) * silu_slope(r.emb[...].astype(F32))

        head_wait(lambda p: r.io_src.at[p], r.io_dst, r.io_s, r.io_r)

        def out_image(m):
            r.image_grad[m] = unpack(r.io_dst, m)

        loop(2, out_image)

        if inside:
            total = red3.last(0)
            r.sb_src[...] = jnp.where(c == 0, total[96:144], total[0:48])
            back = rc(r.sb_src, r.sb_dst, r.sb_s.at[0], r.sb_r.at[0], sib)
            back.start()
            r.output[...] = total[144:192, :BLK]
            for a in range(3):
                block = red1.last(a)
                for b in range(3):
                    r.first[3 * a + b] = block[b * 48 : b * 48 + 48, :BLK]
            back.wait()
            r.attend[...] = jnp.concatenate(
                [
                    jnp.where(c == 0, total[0:48], total[48:96])[:, :BLK],
                    r.sb_dst[:, :BLK],
                    jnp.where(c == 0, total[48:96], total[96:144])[:, :BLK],
                ],
                axis=1,
            )

    return kernel


def per_device(n, *args):
    (
        images,
        noise_field,
        time_steps,
        embedding,
        first_kernel,
        second_kernel,
        film_weight,
        attend_weight,
        output_weight,
        norm_gains,
        biases,
        cotangent,
    ) = args
    inside = n == 8
    keep, noise = plan(time_steps)
    coef = jnp.stack([keep, noise])
    maps, height, width, channels = images.shape
    flat_shape = (maps, height * width, channels)
    film_rows = film_weight.shape[0]
    inputs = dict(
        coef=coef,
        images=images.reshape(flat_shape),
        noise=noise_field.reshape(flat_shape),
        cot=cotangent.reshape(flat_shape),
        emb=embedding,
        k1=first_kernel.reshape((9,) + first_kernel.shape[2:]),
        k2=second_kernel.reshape((9,) + second_kernel.shape[2:]),
        wf=film_weight,
        wa=attend_weight,
        wo=output_weight,
        gains=norm_gains,
        biases=biases,
        sel=jnp.asarray(channel_lanes(), BF16),
        gmask=jnp.asarray(group_mask(), BF16),
        selp=jnp.asarray(block_lanes(3), BF16),
    )
    shapes = dict(
        result=flat_shape,
        image_grad=flat_shape,
        embed_grad=embedding.shape,
        first=(9, 48, BLK),
        second=(9, 48, BLK),
        film=film_weight.shape,
        attend=attend_weight.shape,
        output=output_weight.shape,
        gains_out=norm_gains.shape,
        biases_out=biases.shape,
    )
    names_in, names_out = list(INPUTS), list(OUTPUTS)
    core = lax.axis_index("head") % 2
    if not inside:
        def whole(array, row_axis):
            array = lax.all_gather(array, "dp", axis=row_axis, tiled=True)
            return lax.all_gather(array, "head", axis=array.ndim - 1, tiled=True)

        def spread(array, count):
            taps = array.shape[0]
            array = array.reshape(taps, 4, 2, 48, 2, 2, BLK)
            array = lax.dynamic_index_in_dim(array, core, 5, keepdims=False)
            array = jnp.transpose(array, (2, 4, 1, 0, 3, 5))
            array = jnp.pad(array, ((0, 0),) * 5 + ((0, 32),))
            return array.reshape(4, 4, taps * 48, 128)

        full_a = whole(attend_weight, 0).reshape(384, 2, 3, 2, BLK)
        full_a = jnp.transpose(full_a, (2, 0, 1, 3, 4)).reshape(3, 384, 384)
        full_o = whole(output_weight, 0)[None]
        inputs["g1"] = spread(whole(first_kernel, 2).reshape(9, 384, 384), 9)
        inputs["g2"] = spread(whole(second_kernel, 2).reshape(9, 384, 384), 9)
        inputs["g3"] = spread(jnp.concatenate([full_a, full_o], axis=0), 4)
        names_in += ["g1", "g2", "g3"]
        shapes["first"] = shapes["second"] = (3, 4, 4, 144, 128)
        shapes["attend"] = (1, 4, 4, 192, 128)
        del shapes["output"]
        names_out.remove("output")
    items = scratch_list(n, inside)
    smem = pl.BlockSpec(memory_space=pltpu.SMEM)
    vmem = pl.BlockSpec(memory_space=pltpu.VMEM)
    outs = pl.pallas_call(
        make_kernel(n, inside, names_in + names_out + [name for name, _ in items]),
        out_shape=[jax.ShapeDtypeStruct(shapes[name], F32) for name in names_out],
        in_specs=[smem if name == "coef" else vmem for name in names_in],
        out_specs=[vmem] * len(names_out),
        scratch_shapes=[item for _, item in items],
        compiler_params=pltpu.CompilerParams(
            collective_id=0, has_side_effects=True, vmem_limit_bytes=63 * 1024 * 1024
        ),
        name="blocks",
    )(*[inputs[name] for name in names_in])
    out = dict(zip(names_out, outs))
    if not inside:

        def gathered(array):
            taps = array.shape[0] * array.shape[3] // 48
            array = array.reshape(array.shape[0], 2, 2, 4, -1, 48, 128)[..., :BLK]
            array = jnp.transpose(array, (0, 4, 3, 1, 5, 2, 6)).reshape(taps, 384, 2, 1, BLK)
            both = jnp.concatenate([array, jnp.zeros_like(array)], axis=3)
            return jnp.where(core == 0, both, both[:, :, :, ::-1]).reshape(taps, 384, 384)

        def shared(array, axis):
            array = lax.psum_scatter(array, "head", scatter_dimension=array.ndim - 1, tiled=True)
            return lax.psum_scatter(array, "dp", scatter_dimension=axis, tiled=True)

        out["first"] = shared(gathered(out["first"]), 1)
        out["second"] = shared(gathered(out["second"]), 1)
        both = gathered(out["attend"])
        joined = both[:3].reshape(3, 384, 2, 2, BLK)
        joined = jnp.transpose(joined, (1, 2, 0, 3, 4)).reshape(384, 1152)
        out["attend"] = shared(joined, 0)
        out["output"] = shared(both[3], 0)
    return (
        out["result"].reshape(images.shape),
        out["image_grad"].reshape(images.shape),
        out["embed_grad"],
        out["first"].reshape(first_kernel.shape),
        out["second"].reshape(second_kernel.shape),
        out["film"],
        out["attend"],
        out["output"],
        out["gains_out"],
        out["biases_out"],
    )


def solution(mesh):
    n = mesh.shape["dp"]
    field = P("dp", "head", None, None)
    taps = P(None, None, "dp", "head")
    both = P("dp", "head")
    return jax.shard_map(
        lambda *args: per_device(n, *args),
        mesh=mesh,
        in_specs=(field, field, P("dp"), P("dp", None), taps, taps, both, both, both, P(), P(), field),
        out_specs=(field, field, P("dp", None), taps, taps, both, both, both, P(), P()),
        check_vma=False,
    )
```

```python
import math

import jax
import jax.numpy as jnp
import numpy as np
from jax import lax
from jax.experimental import pallas as pl
from jax.experimental.pallas import tpu as pltpu
from jax.sharding import PartitionSpec as P

HEAD_DIM = 96
GROUPS = 32
STEPS = 4000
EPS = 1e-05
OFFSET = 0.008
MESH = pl.DeviceIdType.MESH
F32 = jnp.float32
BF16 = jnp.bfloat16

PX = 1024
ROW = 32
CHUNK = 256
BLK = 96
HALF = 256
NHEAD = 4


def plan(time_steps):
    fraction = (time_steps.astype(F32) + 1.0) / STEPS
    start = jnp.square(jnp.cos(jnp.float32(OFFSET / (1.0 + OFFSET) * (math.pi / 2))))
    curve = jnp.square(jnp.cos((fraction + OFFSET) / (1.0 + OFFSET) * (math.pi / 2))) / start
    return (jnp.sqrt(curve), jnp.sqrt(1.0 - curve))


def channel_lanes():
    sel = np.zeros((2, 384, HALF), np.float32)
    for block in range(4):
        for j in range(BLK):
            sel[block % 2, block * BLK + j, (block // 2) * 128 + j] = 1.0
    return sel


def block_lanes(count):
    sel = np.zeros((count * BLK, count * 128), np.float32)
    for block in range(count):
        for j in range(BLK):
            sel[block * BLK + j, block * 128 + j] = 1.0
    return sel


def group_mask():
    lane = np.arange(HALF)
    ok = lane % 128 < BLK
    group = (lane // 128) * 100 + (lane % 128) // 12
    return ((group[:, None] == group[None, :]) & ok[:, None] & ok[None, :]).astype(np.float32)


def dot(a, b):
    return lax.dot_general(a, b, (((1,), (0,)), ((), ())), preferred_element_type=F32)


def dot_nt(a, b):
    return lax.dot_general(a, b, (((1,), (1,)), ((), ())), preferred_element_type=F32)


def dot_nt_high(a, b):
    return lax.dot_general(
        a, b, (((1,), (1,)), ((), ())), preferred_element_type=F32, precision=lax.Precision.HIGHEST
    )


def dot_tn_high(a, b):
    return lax.dot_general(
        a, b, (((0,), (0,)), ((), ())), preferred_element_type=F32, precision=lax.Precision.HIGHEST
    )


def exact_dot(values, ones):
    high = values.astype(BF16).astype(F32)
    rest = values - high
    middle = rest.astype(BF16).astype(F32)
    low = rest - middle
    rows = values.shape[0]
    out = dot(jnp.concatenate([high, middle, low], axis=0).astype(BF16), ones)
    return out[:rows] + out[rows : 2 * rows] + out[2 * rows :]


def sigmoid(v):
    return 1.0 / (1.0 + jnp.exp(-v))


def silu(v):
    return v / (1.0 + jnp.exp(-v))


def silu_slope(v):
    s = sigmoid(v)
    return s * (1.0 + v * (1.0 - s))


def pack_taps(t0, t1, t2):
    t0, t1, t2 = t0[:, :BLK], t1[:, :BLK], t2[:, :BLK]
    join = lambda a, b: jnp.concatenate([a, b], axis=1)
    return jnp.concatenate(
        [
            join(t0[:32], t2[:32, :32]),
            join(t0[32:], t2[:16, 32:64]),
            join(t1[:16], t2[16:32, 32:64]),
            join(t1[16:], t2[:32, 64:]),
            join(t2[32:], jnp.zeros((16, 32), t2.dtype)),
        ],
        axis=0,
    )


def last_tap(packed):
    lanes = [packed[:32, BLK:], packed[32:64, BLK:], packed[64:96, BLK:], jnp.zeros((32, 32), packed.dtype)]
    return jnp.concatenate([jnp.concatenate(lanes, axis=1), packed[96:112]], axis=0)


def pack_four(b0, b1, b2, b3):
    return jnp.concatenate(
        [jnp.concatenate([b[:, :BLK], b3[:, 32 * k : 32 * k + 32]], axis=1) for k, b in enumerate((b0, b1, b2))],
        axis=0,
    )


def unpack_four(packed):
    size = packed.shape[0] // 3
    parts = [packed[k * size : k * size + size] for k in range(3)]
    zero = jnp.zeros((size, 32), packed.dtype)
    fourth = jnp.concatenate([p[:, BLK:] for p in parts] + [zero], axis=1)
    return [jnp.concatenate([p[:, :BLK], zero], axis=1) for p in parts] + [fourth]


def pack_pixels(full):
    half = CHUNK // 2
    return pack_four(full[:half, :128], full[half:, :128], full[:half, 128:], full[half:, 128:])


def unpack_pixels(packed):
    b0, b1, b2, b3 = unpack_four(packed)
    return jnp.concatenate([jnp.concatenate([b0, b2], axis=1), jnp.concatenate([b1, b3], axis=1)], axis=0)


INPUTS = (
    "coef",
    "images",
    "noise",
    "cot",
    "emb",
    "k1",
    "k2",
    "wf",
    "wa",
    "wo",
    "gains",
    "biases",
    "sel",
    "gmask",
    "selp",
)
OUTPUTS = (
    "ro_dst",
    "io_dst",
    "embed_grad",
    "first",
    "second",
    "film",
    "attend",
    "output",
    "gains_out",
    "biases_out",
)


class Names:
    def __init__(self, names, refs):
        for name, ref in zip(names, refs):
            setattr(self, name, ref)


def scratch_list(n, inside):
    dma = pltpu.SemaphoreType.DMA
    items = []

    def vm(name, shape, dtype):
        items.append((name, pltpu.VMEM(shape, dtype)))

    def sem(name, count):
        items.append((name + "_s", dma((count,))))
        items.append((name + "_r", dma((count,))))

    for name in ("mx", "cx", "ro", "io"):
        vm(name + "_src", (4, 384, 128), BF16)
        if name in ("mx", "cx"):
            vm(name + "_dst", (4, 384, 128), BF16)
            vm(name, (4, CHUNK, HALF), BF16)
        sem(name, 4)
    for name in ("act1", "act2"):
        vm(name, (2, PX + 2 * ROW, HALF), BF16)
        vm(name + "_t", (2, HALF, PX), BF16)
        sem(name, 4)
    vm("ai", (2, PX, HALF), BF16)
    vm("ai_t", (2, HALF, PX), BF16)
    sem("ai", 4)
    vm("att", (4, PX, 128), BF16)
    vm("att_t", (2, HALF, PX), BF16)
    sem("att", 4)
    for name in ("do", "n3", "d2", "d1"):
        vm(name + "_src", (PX, HALF), BF16)
        vm(name + "_dst", (PX, HALF), BF16)
        sem(name, 4)
    vm("v2", (PX, HALF), F32)
    vm("v3", (PX, HALF), F32)
    vm("gres", (PX, HALF), F32)
    vm("gtmp", (PX, HALF), F32)
    vm("qkv", (6, PX, 128), BF16)
    vm("kvt", (4, 128, PX), BF16)
    vm("dout", (2, PX, 128), BF16)
    vm("dacc", (4, PX, 128), F32)
    vm("dproj", (6, PX, 128), BF16)
    vm("gr2", (3, PX + 2 * ROW, HALF), BF16)
    vm("gr1", (3, PX + 2 * ROW, HALF), BF16)
    vm("par", (16, 384), F32)
    vm("parown", (16, HALF), F32)
    vm("stat", (16, HALF), F32)
    vm("sums", (16, HALF), F32)
    if inside:
        vm("g1", (4, 4, 336, 128), BF16)
        vm("g2", (4, 4, 336, 128), BF16)
        vm("t1", (4, 4, 144, 128), BF16)
        vm("t2", (4, 4, 144, 128), BF16)
        vm("p3", (4, 4, 144, 128), BF16)
        vm("g3", (4, 4, 192, 128), BF16)
        for name in ("g1", "g2", "p3"):
            sem(name + "z", 4)
            sem(name + "v", 4)
            sem(name + "w", 8)
        vm("sw_src", (48, 128), BF16)
        vm("sw_dst", (48, 128), BF16)
        sem("sw", 1)
        vm("sb_src", (48, 128), F32)
        vm("sb_dst", (48, 128), F32)
        sem("sb", 1)
        for name, nc, rows in (("r1", 3, 112), ("r2", 3, 112), ("r3", 1, 144)):
            vm(name + "_acc", (nc, 4, 4, rows, 128), F32)
            vm(name + "w_src", (nc, 2, 4, rows, 128), BF16)
            vm(name + "w_dst", (nc, 2, 4, rows, 128), BF16)
            vm(name + "v_src", (nc, 4, rows, 128), BF16)
            vm(name + "v_dst", (nc, 4, rows, 128), BF16)
            vm(name + "z_src", (nc, 4, rows, 128), BF16)
            vm(name + "z_dst", (nc, 4, rows, 128), BF16)
            sem(name + "w", nc)
            sem(name + "v", nc)
            sem(name + "z", nc * 4)
    vm("el", (n, 2, 768), F32)
    sem("el", n)
    vm("em", (2 * n, 768), F32)
    vm("wfp", (128, HALF), BF16)
    vm("esel", (2 * n, 128), F32)
    vm("fp", (n, 2, HALF), F32)
    vm("fr", (n, 2, HALF), F32)
    sem("fr", n)
    vm("fx", (4, 1, 128), F32)
    vm("fh", (4, 1, 128), F32)
    sem("fh", 4)
    vm("ft", (4, 1, 128), F32)
    vm("th", (4, 1, 128), F32)
    sem("th", 4)
    vm("fa", (n, 2, HALF), F32)
    sem("fa", n)
    vm("fta", (2 * n, HALF), F32)
    vm("ep", (n, 2, 128), F32)
    vm("er", (n, 2, 128), F32)
    sem("er", n)
    vm("eh", (4, n, 2, 128), F32)
    sem("eh", 4)
    vm("ad", (n, 16, HALF), F32)
    sem("ad", n)
    vm("hb", (4, 16, HALF), F32)
    sem("hb", 4)
    return items


def make_kernel(n, inside, names):
    film_rows = 768 // n

    def kernel(*refs):
        r = Names(names, refs)
        d = lax.axis_index("dp")
        h = lax.axis_index("head")
        x = h // 2
        c = h - 2 * x
        z = d // 2
        y = d - 2 * z
        sib = (d, h + 1 - 2 * c)
        xdev = (d, h + 2 - 4 * x)
        v = x + c * (y - x)
        w = y + c * (x - y)
        vdev = (d + c * (1 - 2 * y), h + (1 - c) * (2 - 4 * x))
        wdev = (d + (1 - c) * (1 - 2 * y), h + c * (2 - 4 * x))

        def slot(xx, yy):
            if inside:
                return (yy + c * (xx - yy)) * 2 + xx + c * (yy - xx)
            return yy * 2 + xx

        def rc(src, dst, send, recv, dev):
            return pltpu.make_async_remote_copy(
                src_ref=src, dst_ref=dst, send_sem=send, recv_sem=recv, device_id=dev, device_id_type=MESH
            )

        def loop(count, body):
            def step(i, carry):
                body(i)
                return carry

            lax.fori_loop(0, count, step, 0)

        def rows(i, size=CHUNK, base=0):
            return pl.ds(pl.multiple_of(base + i * size, 32), size)

        def dp_start(src_of, dst, send, recv):
            def step(k, carry):
                peer = lax.rem(d + k, n)
                rc(src_of(peer), dst.at[d], send.at[k], recv.at[d], (peer, h)).start()
                return carry

            lax.fori_loop(1, n, step, 0)

        def dp_wait(src_of, dst, send, recv):
            def step(k, carry):
                peer = lax.rem(d + k, n)
                copy = rc(src_of(peer), dst.at[peer], send.at[k], recv.at[peer], (peer, h))
                copy.wait_recv()
                copy.wait_send()
                return carry

            lax.fori_loop(1, n, step, 0)

        def head_start(src_of, dst, send, recv):
            for k in range(1, 4):
                peer = lax.rem(h + k, 4)
                rc(src_of(peer), dst.at[h], send.at[k], recv.at[h], (d, peer)).start()

        def head_wait(src_of, dst, send, recv):
            for k in range(1, 4):
                peer = lax.rem(h + k, 4)
                copy = rc(src_of(peer), dst.at[peer], send.at[k], recv.at[peer], (d, peer))
                copy.wait_recv()
                copy.wait_send()

        class Halves:
            def __init__(self, name, base):
                self.buf, self.base = getattr(r, name), base
                self.send, self.recv = getattr(r, name + "_s"), getattr(r, name + "_r")

            def at(self, core, i):
                return self.buf.at[core, rows(i, CHUNK, self.base)]

            def start(self, i):
                ref = self.at(c, i)
                rc(ref, ref, self.send.at[i], self.recv.at[i], sib).start()

            def wait(self):
                for i in range(4):
                    ref = self.at(1 - c, i)
                    copy = rc(ref, ref, self.send.at[i], self.recv.at[i], sib)
                    copy.wait_recv()
                    copy.wait_send()

        class Parts:
            def __init__(self, name):
                self.src, self.dst = getattr(r, name + "_src"), getattr(r, name + "_dst")
                self.send, self.recv = getattr(r, name + "_s"), getattr(r, name + "_r")

            def start(self, i):
                rc(self.src.at[rows(i)], self.dst.at[rows(i)], self.send.at[i], self.recv.at[i], sib).start()

            def wait(self, i):
                copy = rc(self.src.at[rows(i)], self.dst.at[rows(i)], self.send.at[i], self.recv.at[i], sib)
                copy.wait_recv()
                copy.wait_send()

        class Gather:
            def __init__(self, name):
                self.g = getattr(r, name)
                self.zs, self.zr = getattr(r, name + "z_s"), getattr(r, name + "z_r")
                self.vs, self.vr = getattr(r, name + "v_s"), getattr(r, name + "v_r")
                self.ws, self.wr = getattr(r, name + "w_s"), getattr(r, name + "w_r")

            def zcopy(self, k, zslot):
                ref = self.g.at[w * 2 + v, zslot]
                return rc(ref, ref, self.zs.at[k], self.zr.at[zslot], (lax.rem(z + k, 4) * 2 + y, h))

            def vcopy(self, vv, zz):
                ref = self.g.at[w * 2 + vv, zz]
                return rc(ref, ref, self.vs.at[zz], self.vr.at[zz], vdev)

            def wcopy(self, ww, vv, zz):
                ref = self.g.at[ww * 2 + vv, zz]
                return rc(ref, ref, self.ws.at[vv * 4 + zz], self.wr.at[vv * 4 + zz], wdev)

            def own(self):
                for k in range(1, 4):
                    self.zcopy(k, z).start()
                self.vcopy(v, z).start()
                self.wcopy(w, v, z).start()

            def pass_z(self):
                self.vcopy(1 - v, z).wait_recv()
                self.wcopy(w, 1 - v, z).start()

                def step(k, carry):
                    zz = lax.rem(z + k, 4)
                    self.zcopy(k, zz).wait_recv()
                    self.vcopy(v, zz).start()
                    self.wcopy(w, v, zz).start()
                    return carry

                lax.fori_loop(1, 4, step, 0)

            def pass_v(self):
                def step(k, carry):
                    zz = lax.rem(z + k, 4)
                    self.vcopy(1 - v, zz).wait_recv()
                    self.wcopy(w, 1 - v, zz).start()
                    return carry

                lax.fori_loop(1, 4, step, 0)

            def done(self):
                def zstep(k, carry):
                    self.zcopy(k, z).wait_send()
                    return carry

                lax.fori_loop(1, 4, zstep, 0)

                def step(zz, carry):
                    self.vcopy(v, zz).wait_send()
                    for vv in range(2):
                        self.wcopy(1 - w, vv, zz).wait_recv()
                        self.wcopy(w, vv, zz).wait_send()
                    return carry

                lax.fori_loop(0, 4, step, 0)

        class Reduce:
            def __init__(self, name, count):
                get = lambda tail: getattr(r, name + tail)
                self.acc, self.count = get("_acc"), count
                self.wsrc, self.wdst, self.ws, self.wr = get("w_src"), get("w_dst"), get("w_s"), get("w_r")
                self.vsrc, self.vdst, self.vs, self.vr = get("v_src"), get("v_dst"), get("v_s"), get("v_r")
                self.zsrc, self.zdst, self.zs, self.zr = get("z_src"), get("z_dst"), get("z_s"), get("z_r")

            def wcopy(self, a):
                return rc(self.wsrc.at[a], self.wdst.at[a], self.ws.at[a], self.wr.at[a], wdev)

            def vcopy(self, a):
                return rc(self.vsrc.at[a], self.vdst.at[a], self.vs.at[a], self.vr.at[a], vdev)

            def zcopy(self, a, k, dst):
                peer = lax.rem(z + k, 4)
                return rc(
                    self.zsrc.at[a, peer],
                    self.zdst.at[a, dst],
                    self.zs.at[a * 4 + k],
                    self.zr.at[a * 4 + dst],
                    (peer * 2 + y, h),
                )

            def start(self, a):
                def step(i, carry):
                    vv, zz = i // 4, lax.rem(i, 4)
                    self.wsrc[a, vv, zz] = self.acc[a, (1 - w) * 2 + vv, zz].astype(BF16)
                    return carry

                lax.fori_loop(0, 8, step, 0)
                self.wcopy(a).start()

            def second(self, a):
                self.wcopy(a).wait_recv()

                def step(zz, carry):
                    self.vsrc[a, zz] = (
                        self.acc[a, w * 2 + 1 - v, zz] + self.wdst[a, 1 - v, zz].astype(F32)
                    ).astype(BF16)
                    self.acc[a, w * 2 + v, zz] = self.acc[a, w * 2 + v, zz] + self.wdst[a, v, zz].astype(F32)
                    return carry

                lax.fori_loop(0, 4, step, 0)
                self.vcopy(a).start()

            def third(self, a):
                self.vcopy(a).wait_recv()

                def step(zz, carry):
                    total = self.acc[a, w * 2 + v, zz] + self.vdst[a, zz].astype(F32)
                    self.acc[a, w * 2 + v, zz] = total
                    self.zsrc[a, zz] = total.astype(BF16)
                    return carry

                lax.fori_loop(0, 4, step, 0)
                for k in range(1, 4):
                    self.zcopy(a, k, z).start()

            def last(self, a):
                total = self.acc[a, w * 2 + v, z]
                for k in range(1, 4):
                    peer = lax.rem(z + k, 4)
                    copy = self.zcopy(a, k, peer)
                    copy.wait_recv()
                    copy.wait_send()
                    total = total + self.zdst[a, peer].astype(F32)
                self.wcopy(a).wait_send()
                self.vcopy(a).wait_send()
                return total

        class Taps:
            def __init__(self, packed, last):
                self.packed, self.last = packed, last

            def block(self, tap, zc, xx, yy):
                a, b = tap // 3, tap % 3
                if b < 2:
                    return self.packed[slot(xx, yy), zc, pl.ds(a * 112 + b * 48, 48), :]
                return self.last[slot(xx, yy), zc, pl.ds(a * 48, 48), :]

            def unpack(self):
                def step(i, carry):
                    q, zz = i // 4, lax.rem(i, 4)
                    for a in range(3):
                        self.last[q, zz, pl.ds(a * 48, 48), :] = last_tap(
                            self.packed[q, zz, pl.ds(a * 112, 112), :]
                        )
                    return carry

                lax.fori_loop(0, 16, step, 0)

        class Plain:
            def __init__(self, blocks):
                self.blocks = blocks

            def block(self, tap, zc, xx, yy):
                return self.blocks[slot(xx, yy), zc, pl.ds(tap * 48, 48), :]

            def unpack(self):
                def step(i, carry):
                    q, zz = i // 4, lax.rem(i, 4)
                    self.blocks[q, zz] = jnp.concatenate(unpack_four(r.p3[q, zz]), axis=0)
                    return carry

                lax.fori_loop(0, 16, step, 0)

        k1, k2, k3 = Taps(r.g1, r.t1), Taps(r.g2, r.t2), Plain(r.g3)

        def wtile(g, tap, zc, xx):
            return jnp.concatenate(
                [g.block(tap, zc, xx, 0), g.block(tap, zc, xx, 1), jnp.zeros((32, 128), BF16)], axis=0
            )

        def wtap(g, tap, zcs):
            return jnp.concatenate(
                [jnp.concatenate([wtile(g, tap, zc, xx) for xx in range(2)], axis=1) for zc in zcs], axis=0
            )

        ALL = (0, 2, 1, 3)

        def half_of(core):
            return (core, core + 2)

        def wproj(zcs):
            return jnp.concatenate(
                [
                    jnp.concatenate([wtile(k3, j, zc, xx) for xx in range(2) for j in range(3)], axis=1)
                    for zc in zcs
                ],
                axis=0,
            )

        def flat(buf, base, i, size):
            return jnp.concatenate([buf[0, rows(i, size, base), :], buf[1, rows(i, size, base), :]], axis=1)

        barrier = pltpu.get_barrier_semaphore()

        def greet(k, carry):
            pl.semaphore_signal(barrier, inc=1, device_id=(lax.rem(d + k, n), h), device_id_type=MESH)
            return carry

        lax.fori_loop(1, n, greet, 0)
        for k in range(1, 4):
            pl.semaphore_signal(barrier, inc=1, device_id=(d, lax.rem(h + k, 4)), device_id_type=MESH)
        if inside:
            for a in range(3):
                r.g1[w * 2 + v, z, pl.ds(a * 112, 112), :] = pack_taps(*[r.k1[3 * a + b] for b in range(3)])
        pl.semaphore_wait(barrier, n - 1 + 3)
        if inside:
            ga, gb, gc = Gather("g1"), Gather("g2"), Gather("p3")
            ga.own()

        def mix(m, carry):
            field = r.coef[0, m] * r.images[m].astype(F32) + r.coef[1, m] * r.noise[m].astype(F32)
            low = field.astype(BF16)
            for core in range(2):
                r.mx_src[m * 2 + core] = pack_pixels(dot(low, r.sel[core])).astype(BF16)
            return carry

        lax.fori_loop(0, 2, mix, 0)
        head_start(lambda p: r.mx_src.at[p], r.mx_dst, r.mx_s, r.mx_r)
        r.mx_dst[h] = r.mx_src[h]

        emb = r.emb[...].astype(F32)
        r.el[d] = silu(emb).astype(BF16).astype(F32)
        dp_start(lambda p: r.el.at[d], r.el, r.el_s, r.el_r)

        if inside:
            blocks = dot(r.wa[...], r.selp[: 3 * BLK, : 3 * 128]).astype(BF16)
            r.sw_src[...] = blocks[:, 128:256]
            swap = rc(r.sw_src, r.sw_dst, r.sw_s.at[0], r.sw_r.at[0], sib)
            swap.start()
            for a in range(3):
                r.g2[w * 2 + v, z, pl.ds(a * 112, 112), :] = pack_taps(*[r.k2[3 * a + b] for b in range(3)])
        r.par[0:3, :] = r.gains[...]
        r.par[3:13, :] = r.biases[...]
        r.par[13:16, :] = jnp.zeros((3, 384), F32)
        r.parown[...] = exact_dot(r.par[...], r.sel[c])

        def prow(i):
            return r.parown[pl.ds(i, 1), :]

        for buf in (r.act1, r.act2):
            for core in range(2):
                buf[core, pl.ds(0, ROW), :] = jnp.zeros((ROW, HALF), BF16)
                buf[core, pl.ds(PX + ROW, ROW), :] = jnp.zeros((ROW, HALF), BF16)
        for buf in (r.gr1, r.gr2):
            for b in range(3):
                buf[b, pl.ds(0, ROW), :] = jnp.zeros((ROW, HALF), BF16)
                buf[b, pl.ds(PX + ROW, ROW), :] = jnp.zeros((ROW, HALF), BF16)
        r.wfp[...] = jnp.zeros((128, HALF), BF16)
        r.wfp[pl.ds(0, film_rows), :] = dot(r.wf[...], r.selp[: 2 * BLK, :HALF]).astype(BF16)
        if inside:
            ga.pass_z()
            gb.own()

        count = float(PX * 12)

        def fold(vals):
            return jnp.sum(vals.reshape(CHUNK // 8, 8, HALF), axis=0)

        def sums_of(fn, k):
            def step(i, carry):
                return tuple(a + fold(b) for a, b in zip(carry, fn(i)))

            zero = jnp.zeros((8, HALF), F32)
            return lax.fori_loop(0, 4, step, (zero,) * k)

        def group_mean(part):
            return jnp.sum(exact_dot(part, r.gmask[...]), axis=0, keepdims=True) / count

        def norm(load, which):
            (total,) = sums_of(lambda i: (load(i),), 1)
            mean = group_mean(total)
            (square,) = sums_of(lambda i: (jnp.square(load(i) - mean),), 1)
            inv = lax.rsqrt(group_mean(square) + EPS)
            r.stat[pl.ds(2 * which, 1), :] = mean
            r.stat[pl.ds(2 * which + 1, 1), :] = inv
            return mean, inv

        def norm_back(load_grad, load_hat, coef, inv, sum_row):
            plain, cross = sums_of(lambda i: (load_grad(i), load_grad(i) * load_hat(i)), 2)
            plain_mean, cross_mean = group_mean(coef * plain), group_mean(coef * cross)

            def chunk(i):
                return inv * (coef * load_grad(i) - plain_mean - load_hat(i) * cross_mean)

            return (
                jnp.sum(plain, axis=0, keepdims=True),
                jnp.sum(cross, axis=0, keepdims=True),
                chunk,
            )

        head_wait(lambda p: r.mx_src.at[p], r.mx_dst, r.mx_s, r.mx_r)

        def unpack_mixed(i):
            r.mx[i] = unpack_pixels(r.mx_dst[i])

        loop(4, unpack_mixed)

        def mixed(i):
            return r.mx[i].astype(F32)

        mean1, inv1 = norm(mixed, 0)
        gain1, shift1 = prow(0), prow(3)
        act1 = Halves("act1", ROW)

        def pre1(i):
            return (mixed(i) - mean1) * inv1 * gain1 + shift1

        def first_act(i):
            r.act1[c, rows(i, CHUNK, ROW), :] = silu(pre1(i)).astype(BF16)
            act1.start(i)

        loop(4, first_act)
        if inside:
            ga.pass_v()

        dp_wait(lambda p: r.el.at[d], r.el, r.el_s, r.el_r)
        for j in range(n):
            r.em[pl.ds(2 * j, 2), :] = r.el[j]
        place = lax.broadcasted_iota(jnp.int32, (768, 128), 0) - film_rows * d
        lane = lax.broadcasted_iota(jnp.int32, (768, 128), 1)
        pick = jnp.where((place == lane) & (lane < film_rows), 1.0, 0.0).astype(BF16)
        r.esel[...] = dot(r.em[...].astype(BF16), pick)
        film_part = dot(r.esel[...].astype(BF16), r.wfp[...])
        for j in range(n):
            r.fp[j] = film_part[2 * j : 2 * j + 2]
        dp_start(lambda p: r.fp.at[p], r.fr, r.fr_s, r.fr_r)
        r.fr[d] = r.fp[d]
        if inside:
            swap.wait()
            got = r.sw_dst[...]
            keep0, keep2 = blocks[:, :128], blocks[:, 256:]
            r.p3[w * 2 + v, z] = pack_four(
                jnp.where(c == 0, keep0, got),
                jnp.where(c == 0, keep2, keep0),
                jnp.where(c == 0, got, keep2),
                r.wo[...],
            )
            gb.pass_z()
            gc.own()
        dp_wait(lambda p: r.fp.at[p], r.fr, r.fr_s, r.fr_r)
        film_sum = r.fr[0]
        for j in range(1, n):
            film_sum = film_sum + r.fr[j]
        for m in range(2):
            for core in range(2):
                r.fx[m * 2 + core] = film_sum[m : m + 1, core * 128 : core * 128 + 128]
        head_start(lambda p: r.fx.at[p], r.fh, r.fh_s, r.fh_r)
        r.fh[h] = r.fx[h]

        def split_cot(m, carry):
            for core in range(2):
                r.cx_src[m * 2 + core] = pack_pixels(dot(r.cot[m], r.sel[core])).astype(BF16)
            return carry

        lax.fori_loop(0, 2, split_cot, 0)
        head_start(lambda p: r.cx_src.at[p], r.cx_dst, r.cx_s, r.cx_r)
        r.cx_dst[h] = r.cx_src[h]

        column = lax.broadcasted_iota(jnp.int32, (CHUNK, HALF), 0) % ROW
        not_first = column > 0
        not_last = column < ROW - 1

        def from_left(vals):
            return jnp.where(not_first, pltpu.roll(vals, 1, 0), 0.0)

        def from_right(vals):
            return jnp.where(not_last, pltpu.roll(vals, CHUNK - 1, 0), 0.0)

        def conv(buf, g, store):
            weights = lambda: jnp.concatenate(
                [jnp.concatenate([wtap(g, 3 * a + b, ALL) for b in range(3)], axis=1) for a in range(3)], axis=0
            )

            def step(i):
                left = jnp.concatenate([flat(buf, ROW * a, i, 2 * CHUNK) for a in range(3)], axis=1)
                out = dot(left, weights())
                for j in range(2):
                    part = out[j * CHUNK : j * CHUNK + CHUNK]
                    store(
                        2 * i + j,
                        part[:, HALF : 2 * HALF] + from_left(part[:, :HALF]) + from_right(part[:, 2 * HALF :]),
                    )

            loop(2, step)

        act1.wait()
        if inside:
            ga.done()
            k1.unpack()

        def store_v2(i, vals):
            r.v2[rows(i), :] = vals + prow(6)

        conv(r.act1, k1, store_v2)
        if inside:
            gb.pass_v()
        head_wait(lambda p: r.fx.at[p], r.fh, r.fh_s, r.fh_r)
        scale = 1.0 + (jnp.concatenate([r.fh[0], r.fh[1]], axis=1) + prow(8))
        shift = jnp.concatenate([r.fh[2], r.fh[3]], axis=1) + prow(9)
        mean2, inv2 = norm(lambda i: r.v2[rows(i), :], 1)
        gain2, shift2 = prow(1), prow(4)
        act2 = Halves("act2", ROW)

        def hat2(i):
            return (r.v2[rows(i), :] - mean2) * inv2

        def pre2(i):
            return (hat2(i) * gain2 + shift2) * scale + shift

        def second_act(i):
            r.act2[c, rows(i, CHUNK, ROW), :] = silu(pre2(i)).astype(BF16)
            act2.start(i)

        loop(4, second_act)
        if inside:
            gc.pass_z()

        act2.wait()
        if inside:
            gb.done()
            k2.unpack()

        def store_v3(i, vals):
            r.v3[rows(i), :] = mixed(i) + (vals + prow(7))

        conv(r.act2, k2, store_v3)
        if inside:
            gc.pass_v()
        mean3, inv3 = norm(lambda i: r.v3[rows(i), :], 2)
        gain3, shift3 = prow(2), prow(5)
        ai = Halves("ai", 0)

        def hat3(i):
            return (r.v3[rows(i), :] - mean3) * inv3

        def attend_in(i):
            r.ai[c, rows(i), :] = (hat3(i) * gain3 + shift3).astype(BF16)
            ai.start(i)

        loop(4, attend_in)

        if inside:
            gc.done()
            k3.unpack()
        head_wait(lambda p: r.cx_src.at[p], r.cx_dst, r.cx_s, r.cx_r)

        def unpack_cot(i):
            r.cx[i] = unpack_pixels(r.cx_dst[i])

        loop(4, unpack_cot)
        dop = Parts("do")

        def do_other(i):
            r.do_src[rows(i), :] = dot_nt(r.cx[i], wtap(k3, 3, half_of(1 - c))).astype(BF16)
            dop.start(i)

        loop(4, do_other)

        ai.wait()
        bias_proj = [prow(10)[:, :128], prow(10)[:, 128:], None, None, prow(11)[:, :128], prow(11)[:, 128:]]

        def project(i):
            out = dot(flat(r.ai, 0, i, CHUNK), wproj(ALL))
            for k in range(6):
                part = out[:, k * 128 : k * 128 + 128]
                if bias_proj[k] is not None:
                    part = part + bias_proj[k]
                r.qkv[k, rows(i), :] = part.astype(BF16)

        loop(4, project)

        def do_own(i):
            own = dot_nt(r.cx[i], wtap(k3, 3, half_of(c)))
            dop.wait(i)
            full = (own + r.do_dst[rows(i), :].astype(F32)).astype(BF16)
            for k in range(2):
                r.dout[k, rows(i), :] = full[:, k * 128 : k * 128 + 128]

        loop(4, do_own)

        factor = 1.0 / math.sqrt(HEAD_DIM)
        factor2 = factor * math.log2(math.e)
        att = []

        def transposes(k):
            r.kvt[k] = jnp.transpose(r.qkv[k + 2])

        loop(4, transposes)

        def att_ref(core, k):
            return r.att.at[core * 2 + k]

        def one_head(k):
            r.dacc[k] = jnp.zeros((PX, 128), F32)
            r.dacc[2 + k] = jnp.zeros((PX, 128), F32)

            def one_block(b):
                query = r.qkv[k, rows(b), :]
                grad = r.dout[k, rows(b), :]
                scores = dot_nt(r.qkv[2 + k], query)
                peak = jnp.max(scores, axis=0, keepdims=True)
                expo = jnp.exp2((scores - peak) * factor2)
                probs = expo * (1.0 / jnp.sum(expo, axis=0, keepdims=True))
                low = probs.astype(BF16)
                got = dot(r.kvt[2 + k], low)
                r.att[2 * c + k, rows(b), :] = jnp.transpose(got).astype(BF16)
                r.dacc[2 + k] = r.dacc[2 + k] + dot(low, grad)
                probs_grad = dot_nt(r.qkv[4 + k], grad)
                spread = jnp.sum(probs * probs_grad, axis=0, keepdims=True)
                scores_grad = (probs * (probs_grad - spread)).astype(BF16)
                back = dot(r.kvt[k], scores_grad)
                r.dproj[k, rows(b), :] = (jnp.transpose(back) * factor).astype(BF16)
                r.dacc[k] = r.dacc[k] + dot(scores_grad, query)

            loop(4, one_block)
            r.dproj[2 + k] = (r.dacc[k] * factor).astype(BF16)
            r.dproj[4 + k] = r.dacc[2 + k].astype(BF16)
            ref = att_ref(c, k)
            rc(ref, ref, r.att_s.at[k], r.att_r.at[k], sib).start()

        loop(2, one_head)

        n3 = Parts("n3")

        def proj_rows(i):
            return jnp.concatenate([r.dproj[k, rows(i), :] for k in range(6)], axis=1)

        def n3_other(i):
            r.n3_src[rows(i), :] = dot_nt(proj_rows(i), wproj(half_of(1 - c))).astype(BF16)
            n3.start(i)

        loop(4, n3_other)

        for k in range(2):
            ref = att_ref(1 - c, k)
            copy = rc(ref, ref, r.att_s.at[k], r.att_r.at[k], sib)
            copy.wait_recv()
            copy.wait_send()

        def result(i):
            left = jnp.concatenate([r.att[p, rows(i), :] for p in range(4)], axis=1)
            branch = dot(left, wtap(k3, 3, ALL)) + prow(12)
            r.ro_src[i] = pack_pixels(r.v3[rows(i), :] + branch).astype(BF16)

        loop(4, result)
        head_start(lambda p: r.ro_src.at[p], r.ro_dst, r.ro_s, r.ro_r)
        r.ro_dst[h] = r.ro_src[h]

        def transpose_act(buf, base, out):
            for core in range(2):
                for q in range(4):
                    out[core, :, pl.ds(q * CHUNK, CHUNK)] = jnp.transpose(
                        buf[core, pl.ds(base + q * CHUNK, CHUNK), :]
                    )

        if inside:
            red1, red2, red3 = Reduce("r1", 3), Reduce("r2", 3), Reduce("r3", 1)
            acc1, acc2, acc3 = r.r1_acc, r.r2_acc, r.r3_acc
        else:
            acc1, acc2, acc3 = r.first, r.second, r.attend

        def transpose_att(p):
            r.att_t[p // 2, pl.ds(pl.multiple_of(lax.rem(p, 2) * 128, 128), 128), :] = jnp.transpose(r.att[p])

        loop(4, transpose_att)
        transpose_act(r.ai, 0, r.ai_t)
        right = jnp.concatenate([r.dproj[k] for k in range(6)], axis=1)
        cot_rows = jnp.concatenate([r.cx[i] for i in range(4)], axis=0)
        for core in range(2):
            attend_out = dot(r.ai_t[core], right)
            output_out = dot(r.att_t[core], cot_rows)
            for k in range(2):
                for yy in range(2):
                    for xx in range(2):
                        row = k * 128 + yy * 48
                        tiles = [
                            attend_out[row : row + 48, (xx * 3 + j) * 128 : (xx * 3 + j) * 128 + 128] for j in range(3)
                        ]
                        acc3[0, slot(xx, yy), core + 2 * k] = pack_four(
                            *tiles, output_out[row : row + 48, xx * 128 : xx * 128 + 128]
                        )
        if inside:
            red3.start(0)

        def proj_sums(i, carry):
            q = jnp.concatenate([r.dproj[0, rows(i), :], r.dproj[1, rows(i), :]], axis=1).astype(F32)
            val = jnp.concatenate([r.dproj[4, rows(i), :], r.dproj[5, rows(i), :]], axis=1).astype(F32)
            return (carry[0] + fold(q), carry[1] + fold(val), carry[2] + fold(r.cx[i].astype(F32)))

        zero8 = jnp.zeros((8, HALF), F32)
        qsum, vsum, csum = lax.fori_loop(0, 4, proj_sums, (zero8, zero8, zero8))
        r.sums[pl.ds(3 + 7, 1), :] = jnp.sum(qsum, axis=0, keepdims=True)
        r.sums[pl.ds(3 + 8, 1), :] = jnp.sum(vsum, axis=0, keepdims=True)
        r.sums[pl.ds(3 + 9, 1), :] = jnp.sum(csum, axis=0, keepdims=True)
        r.sums[pl.ds(13, 3), :] = jnp.zeros((3, HALF), F32)

        def n3_own(i):
            own = dot_nt(proj_rows(i), wproj(half_of(c)))
            n3.wait(i)
            r.gtmp[rows(i), :] = own + r.n3_dst[rows(i), :].astype(F32)

        loop(4, n3_own)
        plain3, cross3, back3 = norm_back(lambda i: r.gtmp[rows(i), :], hat3, gain3, inv3, 0)
        r.sums[pl.ds(2, 1), :] = cross3
        r.sums[pl.ds(3 + 2, 1), :] = plain3

        def shifted(buf, i, vals):
            buf[0, rows(i, CHUNK, ROW), :] = from_right(vals).astype(BF16)
            buf[1, rows(i, CHUNK, ROW), :] = vals.astype(BF16)
            buf[2, rows(i, CHUNK, ROW), :] = from_left(vals).astype(BF16)

        def residual_back(i, carry):
            vals = r.cx[i].astype(F32) + back3(i)
            r.gres[rows(i), :] = vals
            shifted(r.gr2, i, vals)
            return carry + fold(vals.astype(BF16).astype(F32))

        bias_two = lax.fori_loop(0, 4, residual_back, jnp.zeros((8, HALF), F32))
        r.sums[pl.ds(3 + 4, 1), :] = jnp.sum(bias_two, axis=0, keepdims=True)

        def act_back(buf, g, core, i, size):
            left = jnp.concatenate(
                [buf[b, rows(i, size, 2 * ROW - ROW * a), :] for a in range(3) for b in range(3)], axis=1
            )
            right = jnp.concatenate(
                [wtap(g, 3 * a + b, half_of(core)) for a in range(3) for b in range(3)], axis=1
            )
            return dot_nt(left, right)

        def conv_back(parts, buf, g, name):
            def other(i):
                vals = act_back(buf, g, 1 - c, i, 2 * CHUNK).astype(BF16)
                getattr(r, name + "_src")[rows(i, 2 * CHUNK), :] = vals
                parts.start(2 * i)
                parts.start(2 * i + 1)

            loop(2, other)

        def conv_back_own(parts, buf, g, name, store):
            def own(i):
                vals = act_back(buf, g, c, i, 2 * CHUNK)
                for j in range(2):
                    at = 2 * i + j
                    parts.wait(at)
                    got = getattr(r, name + "_dst")[rows(at), :].astype(F32)
                    store(at, vals[j * CHUNK : j * CHUNK + CHUNK] + got)

            loop(2, own)

        def kernel_grad(act_t, buf, acc, after):
            def step(a, carry):
                right = jnp.concatenate(
                    [buf[b, pl.ds(pl.multiple_of(2 * ROW - ROW * a, 32), PX), :] for b in range(3)], axis=1
                )
                out = dot(jnp.concatenate([act_t[0], act_t[1]], axis=0), right)
                for p, zc in enumerate(ALL):
                    for yy in range(2):
                        for xx in range(2):
                            row = p * 128 + yy * 48
                            tiles = [
                                out[row : row + 48, b * HALF + xx * 128 : b * HALF + xx * 128 + 128] for b in range(3)
                            ]
                            acc[a, slot(xx, yy), zc] = pack_taps(*tiles)
                after(a)
                return carry

            lax.fori_loop(0, 3, step, 0)

        d2 = Parts("d2")
        conv_back(d2, r.gr2, k2, "d2")
        transpose_act(r.act2, ROW, r.act2_t)
        kernel_grad(r.act2_t, r.gr2, acc2, red2.start if inside else lambda a: None)

        def store_pre2(i, vals):
            r.gtmp[rows(i), :] = vals * silu_slope(pre2(i))

        conv_back_own(d2, r.gr2, k2, "d2", store_pre2)
        if inside:
            red3.second(0)

        plain2, cross2, back2 = norm_back(lambda i: r.gtmp[rows(i), :], hat2, gain2 * scale, inv2, 1)
        r.sums[pl.ds(1, 1), :] = scale * cross2
        r.sums[pl.ds(3 + 1, 1), :] = scale * plain2
        film_scale_term = gain2 * cross2 + shift2 * plain2
        r.sums[pl.ds(3 + 5, 1), :] = film_scale_term
        r.sums[pl.ds(3 + 6, 1), :] = plain2
        for j in range(2):
            r.ft[j] = film_scale_term[:, j * 128 : j * 128 + 128]
            r.ft[2 + j] = plain2[:, j * 128 : j * 128 + 128]
        head_start(lambda p: r.ft.at[p], r.th, r.th_s, r.th_r)
        r.th[h] = r.ft[h]

        def first_back(i, carry):
            vals = back2(i)
            shifted(r.gr1, i, vals)
            return carry + fold(vals.astype(BF16).astype(F32))

        bias_one = lax.fori_loop(0, 4, first_back, jnp.zeros((8, HALF), F32))
        r.sums[pl.ds(3 + 3, 1), :] = jnp.sum(bias_one, axis=0, keepdims=True)

        d1 = Parts("d1")
        transpose_act(r.act1, ROW, r.act1_t)
        kernel_grad(r.act1_t, r.gr1, acc1, red1.start if inside else lambda a: None)
        if inside:
            for a in range(3):
                red2.second(a)
            red3.third(0)
        conv_back(d1, r.gr1, k1, "d1")

        head_wait(lambda p: r.ft.at[p], r.th, r.th_s, r.th_r)
        for m in range(2):
            r.fa[d, pl.ds(m, 1), :] = jnp.concatenate([r.th[2 * m], r.th[2 * m + 1]], axis=1)
        dp_start(lambda p: r.fa.at[d], r.fa, r.fa_s, r.fa_r)

        def store_pre1(i, vals):
            r.gtmp[rows(i), :] = vals * silu_slope(pre1(i))

        if inside:
            red1.second(0)
            red1.second(1)
            for a in range(3):
                red2.third(a)
        conv_back_own(d1, r.gr1, k1, "d1", store_pre1)
        if inside:
            red1.second(2)
            red1.third(0)
            red1.third(1)

        def hat1(i):
            return (mixed(i) - mean1) * inv1

        plain1, cross1, back1 = norm_back(lambda i: r.gtmp[rows(i), :], hat1, gain1, inv1, 0)
        r.sums[pl.ds(0, 1), :] = cross1
        r.sums[pl.ds(3, 1), :] = plain1
        r.ad[d] = r.sums[...]
        dp_start(lambda p: r.ad.at[d], r.ad, r.ad_s, r.ad_r)

        keep = r.coef[0, x]

        def image_back(i):
            r.io_src[i] = pack_pixels(keep * (r.gres[rows(i), :] + back1(i))).astype(BF16)

        loop(4, image_back)
        head_start(lambda p: r.io_src.at[p], r.io_dst, r.io_s, r.io_r)
        r.io_dst[h] = r.io_src[h]
        if inside:
            red1.third(2)

        dp_wait(lambda p: r.fa.at[d], r.fa, r.fa_s, r.fa_r)
        for j in range(n):
            r.fta[pl.ds(2 * j, 2), :] = r.fa[j]
        film_block = dot_tn_high(r.esel[...], r.fta[...])
        r.film[...] = jnp.concatenate([film_block[:film_rows, :BLK], film_block[:film_rows, 128 : 128 + BLK]], axis=1)
        embed_part = dot_nt_high(r.fta[...], r.wfp[...].astype(F32))
        for j in range(n):
            r.ep[j] = embed_part[2 * j : 2 * j + 2]
        dp_start(lambda p: r.ep.at[p], r.er, r.er_s, r.er_r)
        r.er[d] = r.ep[d]

        dp_wait(lambda p: r.ad.at[d], r.ad, r.ad_s, r.ad_r)
        total = r.ad[0]
        for j in range(1, n):
            total = total + r.ad[j]
        r.hb[h] = total
        head_start(lambda p: r.hb.at[h], r.hb, r.hb_s, r.hb_r)
        head_wait(lambda p: r.ro_src.at[p], r.ro_dst, r.ro_s, r.ro_r)

        dp_wait(lambda p: r.ep.at[p], r.er, r.er_s, r.er_r)
        r.eh[h] = r.er[...]
        head_start(lambda p: r.eh.at[h], r.eh, r.eh_s, r.eh_r)

        if inside:
            for a in range(3):
                r.second[a] = red2.last(a)

        head_wait(lambda p: r.hb.at[h], r.hb, r.hb_s, r.hb_r)
        even = r.hb[0] + r.hb[2]
        odd = r.hb[1] + r.hb[3]
        wide = jnp.concatenate(
            [even[:, :BLK], odd[:, :BLK], even[:, 128 : 128 + BLK], odd[:, 128 : 128 + BLK]], axis=1
        )
        r.gains_out[...] = wide[0:3]
        r.biases_out[...] = wide[3:13]

        head_wait(lambda p: r.eh.at[h], r.eh, r.eh_s, r.eh_r)
        pieces = []
        for j in range(n):
            piece = (r.eh[0, j] + r.eh[1, j]) + (r.eh[2, j] + r.eh[3, j])
            pieces.append(piece[:, :film_rows])
        r.embed_grad[...] = jnp.concatenate(pieces, axis=1) * silu_slope(r.emb[...].astype(F32))

        head_wait(lambda p: r.io_src.at[p], r.io_dst, r.io_s, r.io_r)

        if inside:
            tiles = unpack_four(red3.last(0))
            r.sb_src[...] = jnp.where(c == 0, tiles[2], tiles[0])
            back = rc(r.sb_src, r.sb_dst, r.sb_s.at[0], r.sb_r.at[0], sib)
            back.start()
            r.output[...] = tiles[3]
            for a in range(3):
                r.first[a] = red1.last(a)
            back.wait()
            r.attend[:, 0:128] = jnp.where(c == 0, tiles[0], tiles[1])
            r.attend[:, 128:256] = r.sb_dst[...]
            r.attend[:, 256:384] = jnp.where(c == 0, tiles[1], tiles[2])

    return kernel


def make_writer(names_in, names_out):
    def kernel(*refs):
        count = len(names_in)
        src, dst = Names(names_in, refs[:count]), Names(names_out, refs[count:])
        for name, packed in (("result", src.ro_dst), ("image_grad", src.io_dst)):
            for m in range(2):
                getattr(dst, name)[m] = dot_nt(unpack_pixels(packed[2 * m]), src.sel[0]) + dot_nt(
                    unpack_pixels(packed[2 * m + 1]), src.sel[1]
                )
        for name in ("first", "second"):
            if name in names_out:
                for a in range(3):
                    block = getattr(src, name)[a]
                    getattr(dst, name)[3 * a] = block[:48, :BLK]
                    getattr(dst, name)[3 * a + 1] = block[48:96, :BLK]
                    getattr(dst, name)[3 * a + 2] = last_tap(block)[:, :BLK]
        if "attend" in names_out:
            dst.attend[...] = jnp.concatenate([src.attend[:, j * 128 : j * 128 + BLK] for j in range(3)], axis=1)
            dst.output[...] = src.output[:, :BLK]
        for name in ("embed_grad", "film", "gains_out", "biases_out"):
            getattr(dst, name)[...] = getattr(src, name)[...]

    return kernel


def per_device(n, *args):
    (
        images,
        noise_field,
        time_steps,
        embedding,
        first_kernel,
        second_kernel,
        film_weight,
        attend_weight,
        output_weight,
        norm_gains,
        biases,
        cotangent,
    ) = args
    inside = n == 8
    keep, noise = plan(time_steps)
    coef = jnp.stack([keep, noise])
    maps, height, width, channels = images.shape
    flat_shape = (maps, height * width, channels)
    film_rows = film_weight.shape[0]
    inputs = dict(
        coef=coef,
        images=images.reshape(flat_shape),
        noise=noise_field.reshape(flat_shape),
        cot=cotangent.reshape(flat_shape),
        emb=embedding,
        k1=first_kernel.reshape((9,) + first_kernel.shape[2:]),
        k2=second_kernel.reshape((9,) + second_kernel.shape[2:]),
        wf=film_weight,
        wa=attend_weight,
        wo=output_weight,
        gains=norm_gains,
        biases=biases,
        sel=jnp.asarray(channel_lanes(), BF16),
        gmask=jnp.asarray(group_mask(), BF16),
        selp=jnp.asarray(block_lanes(3), BF16),
    )
    shapes = dict(
        ro_dst=(4, 384, 128),
        io_dst=(4, 384, 128),
        embed_grad=embedding.shape,
        first=(3, 112, 128),
        second=(3, 112, 128),
        film=film_weight.shape,
        attend=(48, 384),
        output=(48, 128),
        gains_out=norm_gains.shape,
        biases_out=biases.shape,
    )
    names_in, names_out = list(INPUTS), list(OUTPUTS)
    core = lax.axis_index("head") % 2
    if not inside:
        def whole(array, row_axis):
            array = lax.all_gather(array, "dp", axis=row_axis, tiled=True)
            return lax.all_gather(array, "head", axis=array.ndim - 1, tiled=True)

        def spread(array, count):
            taps = array.shape[0]
            array = array.reshape(taps, 4, 2, 48, 2, 2, BLK)
            array = lax.dynamic_index_in_dim(array, core, 5, keepdims=False)
            array = jnp.transpose(array, (2, 4, 1, 0, 3, 5))
            array = jnp.pad(array, ((0, 0),) * 5 + ((0, 32),))
            return array.reshape(4, 4, taps * 48, 128)

        full_a = whole(attend_weight, 0).reshape(384, 2, 3, 2, BLK)
        full_a = jnp.transpose(full_a, (2, 0, 1, 3, 4)).reshape(3, 384, 384)
        full_o = whole(output_weight, 0)[None]
        for name, last, array in (("g1", "t1", first_kernel), ("g2", "t2", second_kernel)):
            blocks = spread(whole(array, 2).reshape(9, 384, 384), 9).reshape(4, 4, 3, 3, 48, 128)
            two = blocks[:, :, :, :2].reshape(4, 4, 3, 96, 128)
            inputs[name] = jnp.pad(two, ((0, 0),) * 3 + ((0, 16), (0, 0))).reshape(4, 4, 336, 128)
            inputs[last] = blocks[:, :, :, 2].reshape(4, 4, 144, 128)
        inputs["g3"] = spread(jnp.concatenate([full_a, full_o], axis=0), 4)
        names_in += ["g1", "g2", "t1", "t2", "g3"]
        shapes["first"] = shapes["second"] = (3, 4, 4, 112, 128)
        shapes["attend"] = (1, 4, 4, 144, 128)
        del shapes["output"]
        names_out.remove("output")
    items = scratch_list(n, inside)
    smem = pl.BlockSpec(memory_space=pltpu.SMEM)
    vmem = pl.BlockSpec(memory_space=pltpu.VMEM)
    outs = pl.pallas_call(
        make_kernel(n, inside, names_in + names_out + [name for name, _ in items]),
        out_shape=[
            jax.ShapeDtypeStruct(shapes[name], BF16 if name in ("ro_dst", "io_dst") else F32) for name in names_out
        ],
        in_specs=[smem if name == "coef" else vmem for name in names_in],
        out_specs=[vmem] * len(names_out),
        scratch_shapes=[item for _, item in items],
        compiler_params=pltpu.CompilerParams(
            collective_id=0, has_side_effects=True, vmem_limit_bytes=63 * 1024 * 1024
        ),
        name="blocks",
    )(*[inputs[name] for name in names_in])
    raw = dict(zip(names_out, outs))
    final = dict(
        result=flat_shape,
        image_grad=flat_shape,
        embed_grad=embedding.shape,
        film=film_weight.shape,
        gains_out=norm_gains.shape,
        biases_out=biases.shape,
    )
    if inside:
        final.update(first=(9, 48, BLK), second=(9, 48, BLK), attend=attend_weight.shape, output=output_weight.shape)
    names_last = [name for name in names_out if inside or name not in ("first", "second", "attend")] + ["sel"]
    names_final = list(final)
    outs = pl.pallas_call(
        make_writer(names_last, names_final),
        out_shape=[jax.ShapeDtypeStruct(final[name], F32) for name in names_final],
        in_specs=[vmem] * len(names_last),
        out_specs=[vmem] * len(names_final),
        compiler_params=pltpu.CompilerParams(vmem_limit_bytes=32 * 1024 * 1024),
        name="outputs",
    )(*[inputs["sel"] if name == "sel" else raw[name] for name in names_last])
    out = dict(zip(names_final, outs))
    if not inside:

        def blocks_of(array, size):
            parts = [array[..., k * 48 : k * 48 + 48, :BLK] for k in range(size)]
            if size == 2:
                lanes = [array[..., k * 32 : k * 32 + 32, BLK:] for k in range(3)]
                lanes = jnp.concatenate(lanes, axis=-1)
                parts.append(jnp.concatenate([lanes, array[..., 96:112, :BLK]], axis=-2))
            else:
                lanes = [array[..., k * 48 : k * 48 + 48, BLK:] for k in range(3)]
                parts.append(jnp.concatenate(lanes, axis=-1))
            array = jnp.stack(parts, axis=1)
            array = array.reshape(array.shape[:2] + (2, 2, 4, 48, BLK))
            taps = array.shape[0] * array.shape[1]
            array = jnp.transpose(array, (0, 1, 4, 2, 5, 3, 6)).reshape(taps, 384, 2, 1, BLK)
            both = jnp.concatenate([array, jnp.zeros_like(array)], axis=3)
            return jnp.where(core == 0, both, both[:, :, :, ::-1]).reshape(taps, 384, 384)

        def shared(array, axis):
            array = lax.psum_scatter(array, "head", scatter_dimension=array.ndim - 1, tiled=True)
            return lax.psum_scatter(array, "dp", scatter_dimension=axis, tiled=True)

        out["first"] = shared(blocks_of(raw["first"], 2), 1)
        out["second"] = shared(blocks_of(raw["second"], 2), 1)
        both = blocks_of(raw["attend"], 3)
        joined = both[:3].reshape(3, 384, 2, 2, BLK)
        joined = jnp.transpose(joined, (1, 2, 0, 3, 4)).reshape(384, 1152)
        out["attend"] = shared(joined, 0)
        out["output"] = shared(both[3], 0)
    return (
        out["result"].reshape(images.shape),
        out["image_grad"].reshape(images.shape),
        out["embed_grad"],
        out["first"].reshape(first_kernel.shape),
        out["second"].reshape(second_kernel.shape),
        out["film"],
        out["attend"],
        out["output"],
        out["gains_out"],
        out["biases_out"],
    )


def solution(mesh):
    n = mesh.shape["dp"]
    field = P("dp", "head", None, None)
    taps = P(None, None, "dp", "head")
    both = P("dp", "head")
    return jax.shard_map(
        lambda *args: per_device(n, *args),
        mesh=mesh,
        in_specs=(field, field, P("dp"), P("dp", None), taps, taps, both, both, both, P(), P(), field),
        out_specs=(field, field, P("dp", None), taps, taps, both, both, both, P(), P()),
        check_vma=False,
    )
```

```python
import math

import jax
import jax.numpy as jnp
import numpy as np
from jax import lax
from jax.experimental import pallas as pl
from jax.experimental.pallas import tpu as pltpu
from jax.sharding import PartitionSpec as P

HEAD_DIM = 96
GROUPS = 32
STEPS = 4000
EPS = 1e-05
OFFSET = 0.008
MESH = pl.DeviceIdType.MESH
F32 = jnp.float32
BF16 = jnp.bfloat16

PX = 1024
ROW = 32
CHUNK = 256
BLK = 96
HALF = 256
NHEAD = 4


def plan(time_steps):
    fraction = (time_steps.astype(F32) + 1.0) / STEPS
    start = jnp.square(jnp.cos(jnp.float32(OFFSET / (1.0 + OFFSET) * (math.pi / 2))))
    curve = jnp.square(jnp.cos((fraction + OFFSET) / (1.0 + OFFSET) * (math.pi / 2))) / start
    return (jnp.sqrt(curve), jnp.sqrt(1.0 - curve))


def channel_lanes():
    sel = np.zeros((2, 384, HALF), np.float32)
    for block in range(4):
        for j in range(BLK):
            sel[block % 2, block * BLK + j, (block // 2) * 128 + j] = 1.0
    return sel


def block_lanes(count):
    sel = np.zeros((count * BLK, count * 128), np.float32)
    for block in range(count):
        for j in range(BLK):
            sel[block * BLK + j, block * 128 + j] = 1.0
    return sel


def group_mask():
    lane = np.arange(HALF)
    ok = lane % 128 < BLK
    group = (lane // 128) * 100 + (lane % 128) // 12
    return ((group[:, None] == group[None, :]) & ok[:, None] & ok[None, :]).astype(np.float32)


def dot(a, b):
    return lax.dot_general(a, b, (((1,), (0,)), ((), ())), preferred_element_type=F32)


def dot_nt(a, b):
    return lax.dot_general(a, b, (((1,), (1,)), ((), ())), preferred_element_type=F32)


def dot_nt_high(a, b):
    return lax.dot_general(
        a, b, (((1,), (1,)), ((), ())), preferred_element_type=F32, precision=lax.Precision.HIGHEST
    )


def dot_tn_high(a, b):
    return lax.dot_general(
        a, b, (((0,), (0,)), ((), ())), preferred_element_type=F32, precision=lax.Precision.HIGHEST
    )


def exact_dot(values, ones):
    high = values.astype(BF16).astype(F32)
    rest = values - high
    middle = rest.astype(BF16).astype(F32)
    low = rest - middle
    rows = values.shape[0]
    out = dot(jnp.concatenate([high, middle, low], axis=0).astype(BF16), ones)
    return out[:rows] + out[rows : 2 * rows] + out[2 * rows :]


def sigmoid(v):
    return 1.0 / (1.0 + jnp.exp(-v))


def silu(v):
    return v / (1.0 + jnp.exp(-v))


def silu_slope(v):
    s = sigmoid(v)
    return s * (1.0 + v * (1.0 - s))


def pack_taps(t0, t1, t2):
    t0, t1, t2 = t0[:, :BLK], t1[:, :BLK], t2[:, :BLK]
    join = lambda a, b: jnp.concatenate([a, b], axis=1)
    return jnp.concatenate(
        [
            join(t0[:32], t2[:32, :32]),
            join(t0[32:], t2[:16, 32:64]),
            join(t1[:16], t2[16:32, 32:64]),
            join(t1[16:], t2[:32, 64:]),
            join(t2[32:], jnp.zeros((16, 32), t2.dtype)),
        ],
        axis=0,
    )


def last_tap(packed):
    lanes = [packed[:32, BLK:], packed[32:64, BLK:], packed[64:96, BLK:], jnp.zeros((32, 32), packed.dtype)]
    return jnp.concatenate([jnp.concatenate(lanes, axis=1), packed[96:112]], axis=0)


def pack_four(b0, b1, b2, b3):
    return jnp.concatenate(
        [jnp.concatenate([b[:, :BLK], b3[:, 32 * k : 32 * k + 32]], axis=1) for k, b in enumerate((b0, b1, b2))],
        axis=0,
    )


def unpack_four(packed):
    size = packed.shape[0] // 3
    parts = [packed[k * size : k * size + size] for k in range(3)]
    zero = jnp.zeros((size, 32), packed.dtype)
    fourth = jnp.concatenate([p[:, BLK:] for p in parts] + [zero], axis=1)
    return [jnp.concatenate([p[:, :BLK], zero], axis=1) for p in parts] + [fourth]


def pack_pixels(full):
    half = CHUNK // 2
    return pack_four(full[:half, :128], full[half:, :128], full[:half, 128:], full[half:, 128:])


def unpack_pixels(packed):
    b0, b1, b2, b3 = unpack_four(packed)
    return jnp.concatenate([jnp.concatenate([b0, b2], axis=1), jnp.concatenate([b1, b3], axis=1)], axis=0)


INPUTS = (
    "coef",
    "images",
    "noise",
    "cot",
    "emb",
    "k1",
    "k2",
    "wf",
    "wa",
    "wo",
    "gains",
    "biases",
    "sel",
    "gmask",
    "selp",
)
OUTPUTS = (
    "ro_dst",
    "io_dst",
    "embed_grad",
    "first",
    "second",
    "film",
    "attend",
    "output",
    "gains_out",
    "biases_out",
)


class Names:
    def __init__(self, names, refs):
        for name, ref in zip(names, refs):
            setattr(self, name, ref)


def scratch_list(n, inside):
    dma = pltpu.SemaphoreType.DMA
    items = []

    def vm(name, shape, dtype):
        items.append((name, pltpu.VMEM(shape, dtype)))

    def sem(name, count):
        items.append((name + "_s", dma((count,))))
        items.append((name + "_r", dma((count,))))

    for name in ("mx", "cx", "ro", "io"):
        vm(name + "_src", (4, 384, 128), BF16)
        if name in ("mx", "cx"):
            vm(name + "_dst", (4, 384, 128), BF16)
            vm(name, (4, CHUNK, HALF), BF16)
        sem(name, 4)
    for name in ("act1", "act2"):
        vm(name, (2, PX + 2 * ROW, HALF), BF16)
        vm(name + "_t", (2, HALF, PX), BF16)
        sem(name, 4)
    vm("ai", (2, PX, HALF), BF16)
    vm("ai_t", (2, HALF, PX), BF16)
    sem("ai", 4)
    vm("att", (4, PX, 128), BF16)
    vm("att_t", (2, HALF, PX), BF16)
    sem("att", 4)
    for name in ("do", "n3", "d2", "d1"):
        vm(name + "_src", (PX, HALF), BF16)
        vm(name + "_dst", (PX, HALF), BF16)
        sem(name, 4)
    vm("v2", (PX, HALF), F32)
    vm("v3", (PX, HALF), F32)
    vm("gres", (PX, HALF), F32)
    vm("gtmp", (PX, HALF), F32)
    vm("qkv", (6, PX, 128), BF16)
    vm("kvt", (4, 128, PX), BF16)
    vm("dout", (2, PX, 128), BF16)
    vm("dproj", (6, PX, 128), BF16)
    vm("gr2", (3, PX + 2 * ROW, HALF), BF16)
    vm("gr1", (3, PX + 2 * ROW, HALF), BF16)
    vm("par", (16, 384), F32)
    vm("parown", (16, HALF), F32)
    vm("stat", (16, HALF), F32)
    vm("sums", (16, HALF), F32)
    if inside:
        vm("g1", (4, 4, 336, 128), BF16)
        vm("g2", (4, 4, 336, 128), BF16)
        vm("t1", (4, 4, 144, 128), BF16)
        vm("t2", (4, 4, 144, 128), BF16)
        vm("p3", (4, 4, 144, 128), BF16)
        vm("g3", (4, 4, 192, 128), BF16)
        for name in ("g1", "g2", "p3"):
            sem(name + "z", 4)
            sem(name + "v", 4)
            sem(name + "w", 8)
        vm("sw_src", (48, 128), BF16)
        vm("sw_dst", (48, 128), BF16)
        sem("sw", 1)
        vm("sb_src", (48, 128), F32)
        vm("sb_dst", (48, 128), F32)
        sem("sb", 1)
        for name, nc, rows in (("r1", 3, 112), ("r2", 3, 112), ("r3", 1, 144)):
            vm(name + "_acc", (nc, 4, 4, rows, 128), F32)
            vm(name + "w_src", (nc, 2, 4, rows, 128), BF16)
            vm(name + "w_dst", (nc, 2, 4, rows, 128), BF16)
            vm(name + "v_src", (nc, 4, rows, 128), BF16)
            vm(name + "v_dst", (nc, 4, rows, 128), BF16)
            vm(name + "z_src", (nc, 4, rows, 128), BF16)
            vm(name + "z_dst", (nc, 4, rows, 128), BF16)
            sem(name + "w", nc)
            sem(name + "v", nc)
            sem(name + "z", nc * 4)
    vm("el", (n, 2, 768), F32)
    sem("el", n)
    vm("em", (2 * n, 768), F32)
    vm("wfp", (128, HALF), BF16)
    vm("esel", (2 * n, 128), F32)
    vm("fp", (n, 2, HALF), F32)
    vm("fr", (n, 2, HALF), F32)
    sem("fr", n)
    vm("fx", (4, 1, 128), F32)
    vm("fh", (4, 1, 128), F32)
    sem("fh", 4)
    vm("ft", (4, 1, 128), F32)
    vm("th", (4, 1, 128), F32)
    sem("th", 4)
    vm("fa", (n, 2, HALF), F32)
    sem("fa", n)
    vm("fta", (2 * n, HALF), F32)
    vm("ep", (n, 2, 128), F32)
    vm("er", (n, 2, 128), F32)
    sem("er", n)
    vm("eh", (4, n, 2, 128), F32)
    sem("eh", 4)
    vm("ad", (n, 16, HALF), F32)
    sem("ad", n)
    vm("hb", (4, 16, HALF), F32)
    sem("hb", 4)
    return items


def make_kernel(n, inside, names):
    film_rows = 768 // n

    def kernel(*refs):
        r = Names(names, refs)
        d = lax.axis_index("dp")
        h = lax.axis_index("head")
        x = h // 2
        c = h - 2 * x
        z = d // 2
        y = d - 2 * z
        sib = (d, h + 1 - 2 * c)
        xdev = (d, h + 2 - 4 * x)
        v = x + c * (y - x)
        w = y + c * (x - y)
        vdev = (d + c * (1 - 2 * y), h + (1 - c) * (2 - 4 * x))
        wdev = (d + (1 - c) * (1 - 2 * y), h + c * (2 - 4 * x))

        def slot(xx, yy):
            if inside:
                return (yy + c * (xx - yy)) * 2 + xx + c * (yy - xx)
            return yy * 2 + xx

        def rc(src, dst, send, recv, dev):
            return pltpu.make_async_remote_copy(
                src_ref=src, dst_ref=dst, send_sem=send, recv_sem=recv, device_id=dev, device_id_type=MESH
            )

        def loop(count, body):
            def step(i, carry):
                body(i)
                return carry

            lax.fori_loop(0, count, step, 0)

        def rows(i, size=CHUNK, base=0):
            return pl.ds(pl.multiple_of(base + i * size, 32), size)

        def dp_start(src_of, dst, send, recv):
            def step(k, carry):
                peer = lax.rem(d + k, n)
                rc(src_of(peer), dst.at[d], send.at[k], recv.at[d], (peer, h)).start()
                return carry

            lax.fori_loop(1, n, step, 0)

        def dp_wait(src_of, dst, send, recv):
            def step(k, carry):
                peer = lax.rem(d + k, n)
                copy = rc(src_of(peer), dst.at[peer], send.at[k], recv.at[peer], (peer, h))
                copy.wait_recv()
                copy.wait_send()
                return carry

            lax.fori_loop(1, n, step, 0)

        def head_start(src_of, dst, send, recv):
            for k in range(1, 4):
                peer = lax.rem(h + k, 4)
                rc(src_of(peer), dst.at[h], send.at[k], recv.at[h], (d, peer)).start()

        def head_wait(src_of, dst, send, recv):
            for k in range(1, 4):
                peer = lax.rem(h + k, 4)
                copy = rc(src_of(peer), dst.at[peer], send.at[k], recv.at[peer], (d, peer))
                copy.wait_recv()
                copy.wait_send()

        class Halves:
            def __init__(self, name, base):
                self.buf, self.base = getattr(r, name), base
                self.send, self.recv = getattr(r, name + "_s"), getattr(r, name + "_r")

            def at(self, core, i):
                return self.buf.at[core, rows(i, CHUNK, self.base)]

            def start(self, i):
                ref = self.at(c, i)
                rc(ref, ref, self.send.at[i], self.recv.at[i], sib).start()

            def wait(self):
                for i in range(4):
                    ref = self.at(1 - c, i)
                    copy = rc(ref, ref, self.send.at[i], self.recv.at[i], sib)
                    copy.wait_recv()
                    copy.wait_send()

        class Parts:
            def __init__(self, name):
                self.src, self.dst = getattr(r, name + "_src"), getattr(r, name + "_dst")
                self.send, self.recv = getattr(r, name + "_s"), getattr(r, name + "_r")

            def start(self, i):
                rc(self.src.at[rows(i)], self.dst.at[rows(i)], self.send.at[i], self.recv.at[i], sib).start()

            def wait(self, i):
                copy = rc(self.src.at[rows(i)], self.dst.at[rows(i)], self.send.at[i], self.recv.at[i], sib)
                copy.wait_recv()
                copy.wait_send()

        class Gather:
            def __init__(self, name):
                self.g = getattr(r, name)
                self.zs, self.zr = getattr(r, name + "z_s"), getattr(r, name + "z_r")
                self.vs, self.vr = getattr(r, name + "v_s"), getattr(r, name + "v_r")
                self.ws, self.wr = getattr(r, name + "w_s"), getattr(r, name + "w_r")

            def zcopy(self, k, zslot):
                ref = self.g.at[w * 2 + v, zslot]
                return rc(ref, ref, self.zs.at[k], self.zr.at[zslot], (lax.rem(z + k, 4) * 2 + y, h))

            def vcopy(self, vv, zz):
                ref = self.g.at[w * 2 + vv, zz]
                return rc(ref, ref, self.vs.at[zz], self.vr.at[zz], vdev)

            def wcopy(self, ww, vv, zz):
                ref = self.g.at[ww * 2 + vv, zz]
                return rc(ref, ref, self.ws.at[vv * 4 + zz], self.wr.at[vv * 4 + zz], wdev)

            def own(self):
                for k in range(1, 4):
                    self.zcopy(k, z).start()
                self.vcopy(v, z).start()
                self.wcopy(w, v, z).start()

            def pass_z(self):
                self.vcopy(1 - v, z).wait_recv()
                self.wcopy(w, 1 - v, z).start()

                def step(k, carry):
                    zz = lax.rem(z + k, 4)
                    self.zcopy(k, zz).wait_recv()
                    self.vcopy(v, zz).start()
                    self.wcopy(w, v, zz).start()
                    return carry

                lax.fori_loop(1, 4, step, 0)

            def pass_v(self):
                def step(k, carry):
                    zz = lax.rem(z + k, 4)
                    self.vcopy(1 - v, zz).wait_recv()
                    self.wcopy(w, 1 - v, zz).start()
                    return carry

                lax.fori_loop(1, 4, step, 0)

            def done(self):
                def zstep(k, carry):
                    self.zcopy(k, z).wait_send()
                    return carry

                lax.fori_loop(1, 4, zstep, 0)

                def step(zz, carry):
                    self.vcopy(v, zz).wait_send()
                    for vv in range(2):
                        self.wcopy(1 - w, vv, zz).wait_recv()
                        self.wcopy(w, vv, zz).wait_send()
                    return carry

                lax.fori_loop(0, 4, step, 0)

        class Reduce:
            def __init__(self, name, count):
                get = lambda tail: getattr(r, name + tail)
                self.acc, self.count = get("_acc"), count
                self.wsrc, self.wdst, self.ws, self.wr = get("w_src"), get("w_dst"), get("w_s"), get("w_r")
                self.vsrc, self.vdst, self.vs, self.vr = get("v_src"), get("v_dst"), get("v_s"), get("v_r")
                self.zsrc, self.zdst, self.zs, self.zr = get("z_src"), get("z_dst"), get("z_s"), get("z_r")

            def wcopy(self, a):
                return rc(self.wsrc.at[a], self.wdst.at[a], self.ws.at[a], self.wr.at[a], wdev)

            def vcopy(self, a):
                return rc(self.vsrc.at[a], self.vdst.at[a], self.vs.at[a], self.vr.at[a], vdev)

            def zcopy(self, a, k, dst):
                peer = lax.rem(z + k, 4)
                return rc(
                    self.zsrc.at[a, peer],
                    self.zdst.at[a, dst],
                    self.zs.at[a * 4 + k],
                    self.zr.at[a * 4 + dst],
                    (peer * 2 + y, h),
                )

            def start(self, a):
                def step(i, carry):
                    vv, zz = i // 4, lax.rem(i, 4)
                    self.wsrc[a, vv, zz] = self.acc[a, (1 - w) * 2 + vv, zz].astype(BF16)
                    return carry

                lax.fori_loop(0, 8, step, 0)
                self.wcopy(a).start()

            def second(self, a):
                self.wcopy(a).wait_recv()

                def step(zz, carry):
                    self.vsrc[a, zz] = (
                        self.acc[a, w * 2 + 1 - v, zz] + self.wdst[a, 1 - v, zz].astype(F32)
                    ).astype(BF16)
                    self.acc[a, w * 2 + v, zz] = self.acc[a, w * 2 + v, zz] + self.wdst[a, v, zz].astype(F32)
                    return carry

                lax.fori_loop(0, 4, step, 0)
                self.vcopy(a).start()

            def third(self, a):
                self.vcopy(a).wait_recv()

                def step(zz, carry):
                    total = self.acc[a, w * 2 + v, zz] + self.vdst[a, zz].astype(F32)
                    self.acc[a, w * 2 + v, zz] = total
                    self.zsrc[a, zz] = total.astype(BF16)
                    return carry

                lax.fori_loop(0, 4, step, 0)
                for k in range(1, 4):
                    self.zcopy(a, k, z).start()

            def last(self, a):
                total = self.acc[a, w * 2 + v, z]
                for k in range(1, 4):
                    peer = lax.rem(z + k, 4)
                    copy = self.zcopy(a, k, peer)
                    copy.wait_recv()
                    copy.wait_send()
                    total = total + self.zdst[a, peer].astype(F32)
                self.wcopy(a).wait_send()
                self.vcopy(a).wait_send()
                return total

        class Taps:
            def __init__(self, packed, last):
                self.packed, self.last = packed, last

            def block(self, tap, zc, xx, yy):
                a, b = tap // 3, tap % 3
                if b < 2:
                    return self.packed[slot(xx, yy), zc, pl.ds(a * 112 + b * 48, 48), :]
                return self.last[slot(xx, yy), zc, pl.ds(a * 48, 48), :]

            def unpack(self):
                def step(i, carry):
                    q, zz = i // 4, lax.rem(i, 4)
                    for a in range(3):
                        self.last[q, zz, pl.ds(a * 48, 48), :] = last_tap(
                            self.packed[q, zz, pl.ds(a * 112, 112), :]
                        )
                    return carry

                lax.fori_loop(0, 16, step, 0)

        class Plain:
            def __init__(self, blocks):
                self.blocks = blocks

            def block(self, tap, zc, xx, yy):
                return self.blocks[slot(xx, yy), zc, pl.ds(tap * 48, 48), :]

            def unpack(self):
                def step(i, carry):
                    q, zz = i // 4, lax.rem(i, 4)
                    self.blocks[q, zz] = jnp.concatenate(unpack_four(r.p3[q, zz]), axis=0)
                    return carry

                lax.fori_loop(0, 16, step, 0)

        k1, k2, k3 = Taps(r.g1, r.t1), Taps(r.g2, r.t2), Plain(r.g3)

        def wtile(g, tap, zc, xx):
            return jnp.concatenate(
                [g.block(tap, zc, xx, 0), g.block(tap, zc, xx, 1), jnp.zeros((32, 128), BF16)], axis=0
            )

        def wtap(g, tap, zcs):
            return jnp.concatenate(
                [jnp.concatenate([wtile(g, tap, zc, xx) for xx in range(2)], axis=1) for zc in zcs], axis=0
            )

        ALL = (0, 2, 1, 3)

        def half_of(core):
            return (core, core + 2)

        def wproj(zcs):
            return jnp.concatenate(
                [
                    jnp.concatenate([wtile(k3, j, zc, xx) for xx in range(2) for j in range(3)], axis=1)
                    for zc in zcs
                ],
                axis=0,
            )

        def flat(buf, base, i, size):
            return jnp.concatenate([buf[0, rows(i, size, base), :], buf[1, rows(i, size, base), :]], axis=1)

        barrier = pltpu.get_barrier_semaphore()

        def greet(k, carry):
            pl.semaphore_signal(barrier, inc=1, device_id=(lax.rem(d + k, n), h), device_id_type=MESH)
            return carry

        lax.fori_loop(1, n, greet, 0)
        for k in range(1, 4):
            pl.semaphore_signal(barrier, inc=1, device_id=(d, lax.rem(h + k, 4)), device_id_type=MESH)
        if inside:
            for a in range(3):
                r.g1[w * 2 + v, z, pl.ds(a * 112, 112), :] = pack_taps(*[r.k1[3 * a + b] for b in range(3)])
        pl.semaphore_wait(barrier, n - 1 + 3)
        if inside:
            ga, gb, gc = Gather("g1"), Gather("g2"), Gather("p3")
            ga.own()

        def mix(m, carry):
            field = r.coef[0, m] * r.images[m].astype(F32) + r.coef[1, m] * r.noise[m].astype(F32)
            low = field.astype(BF16)
            for core in range(2):
                r.mx_src[m * 2 + core] = pack_pixels(dot(low, r.sel[core])).astype(BF16)
            return carry

        lax.fori_loop(0, 2, mix, 0)
        head_start(lambda p: r.mx_src.at[p], r.mx_dst, r.mx_s, r.mx_r)
        r.mx_dst[h] = r.mx_src[h]

        emb = r.emb[...].astype(F32)
        r.el[d] = silu(emb).astype(BF16).astype(F32)
        dp_start(lambda p: r.el.at[d], r.el, r.el_s, r.el_r)

        if inside:
            blocks = dot(r.wa[...], r.selp[: 3 * BLK, : 3 * 128]).astype(BF16)
            r.sw_src[...] = blocks[:, 128:256]
            swap = rc(r.sw_src, r.sw_dst, r.sw_s.at[0], r.sw_r.at[0], sib)
            swap.start()
            for a in range(3):
                r.g2[w * 2 + v, z, pl.ds(a * 112, 112), :] = pack_taps(*[r.k2[3 * a + b] for b in range(3)])
        r.par[0:3, :] = r.gains[...]
        r.par[3:13, :] = r.biases[...]
        r.par[13:16, :] = jnp.zeros((3, 384), F32)
        r.parown[...] = exact_dot(r.par[...], r.sel[c])

        def prow(i):
            return r.parown[pl.ds(i, 1), :]

        for buf in (r.act1, r.act2):
            for core in range(2):
                buf[core, pl.ds(0, ROW), :] = jnp.zeros((ROW, HALF), BF16)
                buf[core, pl.ds(PX + ROW, ROW), :] = jnp.zeros((ROW, HALF), BF16)
        for buf in (r.gr1, r.gr2):
            for b in range(3):
                buf[b, pl.ds(0, ROW), :] = jnp.zeros((ROW, HALF), BF16)
                buf[b, pl.ds(PX + ROW, ROW), :] = jnp.zeros((ROW, HALF), BF16)
        r.wfp[...] = jnp.zeros((128, HALF), BF16)
        r.wfp[pl.ds(0, film_rows), :] = dot(r.wf[...], r.selp[: 2 * BLK, :HALF]).astype(BF16)
        if inside:
            ga.pass_z()
            gb.own()

        count = float(PX * 12)

        def fold(vals):
            return jnp.sum(vals.reshape(CHUNK // 8, 8, HALF), axis=0)

        def sums_of(fn, k):
            def step(i, carry):
                return tuple(a + fold(b) for a, b in zip(carry, fn(i)))

            zero = jnp.zeros((8, HALF), F32)
            return lax.fori_loop(0, 4, step, (zero,) * k)

        def group_mean(part):
            return jnp.sum(exact_dot(part, r.gmask[...]), axis=0, keepdims=True) / count

        def norm(load, which, total):
            mean = group_mean(total)
            (square,) = sums_of(lambda i: (jnp.square(load(i) - mean),), 1)
            inv = lax.rsqrt(group_mean(square) + EPS)
            r.stat[pl.ds(2 * which, 1), :] = mean
            r.stat[pl.ds(2 * which + 1, 1), :] = inv
            return mean, inv

        zero8 = jnp.zeros((8, HALF), F32)

        def norm_back(sums, load_grad, load_hat, coef, inv):
            plain, cross = sums
            plain_mean, cross_mean = group_mean(coef * plain), group_mean(coef * cross)

            def chunk(i):
                return inv * (coef * load_grad(i) - plain_mean - load_hat(i) * cross_mean)

            return (
                jnp.sum(plain, axis=0, keepdims=True),
                jnp.sum(cross, axis=0, keepdims=True),
                chunk,
            )

        head_wait(lambda p: r.mx_src.at[p], r.mx_dst, r.mx_s, r.mx_r)

        def unpack_mixed(i, carry):
            vals = unpack_pixels(r.mx_dst[i])
            r.mx[i] = vals
            return carry + fold(vals.astype(F32))

        mixed_sum = lax.fori_loop(0, 4, unpack_mixed, zero8)

        def mixed(i):
            return r.mx[i].astype(F32)

        mean1, inv1 = norm(mixed, 0, mixed_sum)
        gain1, shift1 = prow(0), prow(3)
        act1 = Halves("act1", ROW)

        def pre1(i):
            return (mixed(i) - mean1) * inv1 * gain1 + shift1

        def first_act(i):
            r.act1[c, rows(i, CHUNK, ROW), :] = silu(pre1(i)).astype(BF16)
            act1.start(i)

        loop(4, first_act)
        if inside:
            ga.pass_v()

        dp_wait(lambda p: r.el.at[d], r.el, r.el_s, r.el_r)
        for j in range(n):
            r.em[pl.ds(2 * j, 2), :] = r.el[j]
        place = lax.broadcasted_iota(jnp.int32, (768, 128), 0) - film_rows * d
        lane = lax.broadcasted_iota(jnp.int32, (768, 128), 1)
        pick = jnp.where((place == lane) & (lane < film_rows), 1.0, 0.0).astype(BF16)
        r.esel[...] = dot(r.em[...].astype(BF16), pick)
        film_part = dot(r.esel[...].astype(BF16), r.wfp[...])
        for j in range(n):
            r.fp[j] = film_part[2 * j : 2 * j + 2]
        dp_start(lambda p: r.fp.at[p], r.fr, r.fr_s, r.fr_r)
        r.fr[d] = r.fp[d]
        if inside:
            swap.wait()
            got = r.sw_dst[...]
            keep0, keep2 = blocks[:, :128], blocks[:, 256:]
            r.p3[w * 2 + v, z] = pack_four(
                jnp.where(c == 0, keep0, got),
                jnp.where(c == 0, keep2, keep0),
                jnp.where(c == 0, got, keep2),
                r.wo[...],
            )
            gb.pass_z()
            gc.own()
        dp_wait(lambda p: r.fp.at[p], r.fr, r.fr_s, r.fr_r)
        film_sum = r.fr[0]
        for j in range(1, n):
            film_sum = film_sum + r.fr[j]
        for m in range(2):
            for core in range(2):
                r.fx[m * 2 + core] = film_sum[m : m + 1, core * 128 : core * 128 + 128]
        head_start(lambda p: r.fx.at[p], r.fh, r.fh_s, r.fh_r)
        r.fh[h] = r.fx[h]

        def split_cot(m, carry):
            for core in range(2):
                r.cx_src[m * 2 + core] = pack_pixels(dot(r.cot[m], r.sel[core])).astype(BF16)
            return carry

        lax.fori_loop(0, 2, split_cot, 0)
        head_start(lambda p: r.cx_src.at[p], r.cx_dst, r.cx_s, r.cx_r)
        r.cx_dst[h] = r.cx_src[h]

        column = lax.broadcasted_iota(jnp.int32, (CHUNK, HALF), 0) % ROW
        not_first = column > 0
        not_last = column < ROW - 1

        def from_left(vals):
            return jnp.where(not_first, pltpu.roll(vals, 1, 0), 0.0)

        def from_right(vals):
            return jnp.where(not_last, pltpu.roll(vals, CHUNK - 1, 0), 0.0)

        def transpose_act(buf, base, out):
            for core in range(2):
                for q in range(4):
                    out[core, :, pl.ds(q * CHUNK, CHUNK)] = jnp.transpose(
                        buf[core, pl.ds(base + q * CHUNK, CHUNK), :]
                    )

        def conv(buf, g, store, between):
            weights = lambda: jnp.concatenate(
                [jnp.concatenate([wtap(g, 3 * a + b, ALL) for b in range(3)], axis=1) for a in range(3)], axis=0
            )

            total = zero8
            for i in range(2):
                left = jnp.concatenate([flat(buf, ROW * a, i, 2 * CHUNK) for a in range(3)], axis=1)
                out = dot(left, weights())
                for j in range(2):
                    part = out[j * CHUNK : j * CHUNK + CHUNK]
                    part = part[:, HALF : 2 * HALF] + from_left(part[:, :HALF]) + from_right(part[:, 2 * HALF :])
                    total = total + fold(store(2 * i + j, part))
                if i == 0:
                    between()
            return total

        act1.wait()
        transpose_act(r.act1, ROW, r.act1_t)
        if inside:
            ga.done()
            k1.unpack()

        def store_v2(i, vals):
            vals = vals + prow(6)
            r.v2[rows(i), :] = vals
            return vals

        v2_sum = conv(r.act1, k1, store_v2, gb.pass_v if inside else lambda: None)
        head_wait(lambda p: r.fx.at[p], r.fh, r.fh_s, r.fh_r)
        scale = 1.0 + (jnp.concatenate([r.fh[0], r.fh[1]], axis=1) + prow(8))
        shift = jnp.concatenate([r.fh[2], r.fh[3]], axis=1) + prow(9)
        mean2, inv2 = norm(lambda i: r.v2[rows(i), :], 1, v2_sum)
        gain2, shift2 = prow(1), prow(4)
        act2 = Halves("act2", ROW)

        def hat2(i):
            return (r.v2[rows(i), :] - mean2) * inv2

        def pre2(i):
            return (hat2(i) * gain2 + shift2) * scale + shift

        def second_act(i):
            r.act2[c, rows(i, CHUNK, ROW), :] = silu(pre2(i)).astype(BF16)
            act2.start(i)

        loop(4, second_act)
        if inside:
            gc.pass_z()

        act2.wait()
        transpose_act(r.act2, ROW, r.act2_t)
        if inside:
            gb.done()
            k2.unpack()

        def store_v3(i, vals):
            vals = mixed(i) + (vals + prow(7))
            r.v3[rows(i), :] = vals
            return vals

        v3_sum = conv(r.act2, k2, store_v3, gc.pass_v if inside else lambda: None)
        mean3, inv3 = norm(lambda i: r.v3[rows(i), :], 2, v3_sum)
        gain3, shift3 = prow(2), prow(5)
        ai = Halves("ai", 0)

        def hat3(i):
            return (r.v3[rows(i), :] - mean3) * inv3

        def attend_in(i):
            r.ai[c, rows(i), :] = (hat3(i) * gain3 + shift3).astype(BF16)
            ai.start(i)

        loop(4, attend_in)

        if inside:
            gc.done()
            k3.unpack()
        head_wait(lambda p: r.cx_src.at[p], r.cx_dst, r.cx_s, r.cx_r)

        def unpack_cot(i):
            r.cx[i] = unpack_pixels(r.cx_dst[i])

        loop(4, unpack_cot)
        dop = Parts("do")

        def do_other(i):
            r.do_src[rows(i), :] = dot_nt(r.cx[i], wtap(k3, 3, half_of(1 - c))).astype(BF16)
            dop.start(i)

        loop(4, do_other)

        ai.wait()
        bias_proj = [prow(10)[:, :128], prow(10)[:, 128:], None, None, prow(11)[:, :128], prow(11)[:, 128:]]

        def project(i):
            out = dot(flat(r.ai, 0, i, CHUNK), wproj(ALL))
            for k in range(6):
                part = out[:, k * 128 : k * 128 + 128]
                if bias_proj[k] is not None:
                    part = part + bias_proj[k]
                r.qkv[k, rows(i), :] = part.astype(BF16)

        loop(4, project)

        def do_own(i):
            own = dot_nt(r.cx[i], wtap(k3, 3, half_of(c)))
            dop.wait(i)
            full = (own + r.do_dst[rows(i), :].astype(F32)).astype(BF16)
            for k in range(2):
                r.dout[k, rows(i), :] = full[:, k * 128 : k * 128 + 128]

        loop(4, do_own)

        factor = 1.0 / math.sqrt(HEAD_DIM)
        factor2 = factor * math.log2(math.e)
        att = []

        def transposes(k):
            r.kvt[k] = jnp.transpose(r.qkv[k + 2])

        loop(4, transposes)

        def att_ref(core, k):
            return r.att.at[core * 2 + k]

        def one_head(k):
            lows, grads = [], []
            for b in range(2):
                at = pl.ds(b * 2 * CHUNK, 2 * CHUNK)
                query = r.qkv[k, at, :]
                grad = r.dout[k, at, :]
                scores = dot_nt(r.qkv[2 + k], query)
                peak = jnp.max(scores, axis=0, keepdims=True)
                expo = jnp.exp2((scores - peak) * factor2)
                inverse = 1.0 / jnp.sum(expo, axis=0, keepdims=True)
                low = (expo * inverse).astype(BF16)
                got = dot(r.kvt[2 + k], low)
                r.att[2 * c + k, at, :] = jnp.transpose(got).astype(BF16)
                spread = jnp.sum(got * jnp.transpose(grad).astype(F32), axis=0, keepdims=True)
                probs_grad = dot_nt(r.qkv[4 + k], grad)
                scores_grad = ((probs_grad - spread) * inverse * expo).astype(BF16)
                back = dot(r.kvt[k], scores_grad)
                r.dproj[k, at, :] = (jnp.transpose(back) * factor).astype(BF16)
                lows.append(low)
                grads.append(scores_grad)
            ref = att_ref(c, k)
            rc(ref, ref, r.att_s.at[k], r.att_r.at[k], sib).start()
            r.dproj[4 + k] = dot(jnp.concatenate(lows, axis=1), r.dout[k]).astype(BF16)
            r.dproj[2 + k] = (dot(jnp.concatenate(grads, axis=1), r.qkv[k]) * factor).astype(BF16)

        loop(2, one_head)

        n3 = Parts("n3")

        def proj_rows(i):
            return jnp.concatenate([r.dproj[k, rows(i), :] for k in range(6)], axis=1)

        def n3_other(i):
            r.n3_src[rows(i), :] = dot_nt(proj_rows(i), wproj(half_of(1 - c))).astype(BF16)
            n3.start(i)

        loop(4, n3_other)

        for k in range(2):
            ref = att_ref(1 - c, k)
            copy = rc(ref, ref, r.att_s.at[k], r.att_r.at[k], sib)
            copy.wait_recv()
            copy.wait_send()

        def result(i):
            left = jnp.concatenate([r.att[p, rows(i), :] for p in range(4)], axis=1)
            branch = dot(left, wtap(k3, 3, ALL)) + prow(12)
            r.ro_src[i] = pack_pixels(r.v3[rows(i), :] + branch).astype(BF16)

        loop(4, result)
        head_start(lambda p: r.ro_src.at[p], r.ro_dst, r.ro_s, r.ro_r)
        r.ro_dst[h] = r.ro_src[h]

        if inside:
            red1, red2, red3 = Reduce("r1", 3), Reduce("r2", 3), Reduce("r3", 1)
            acc1, acc2, acc3 = r.r1_acc, r.r2_acc, r.r3_acc
        else:
            acc1, acc2, acc3 = r.first, r.second, r.attend

        def transpose_att(p):
            r.att_t[p // 2, pl.ds(pl.multiple_of(lax.rem(p, 2) * 128, 128), 128), :] = jnp.transpose(r.att[p])

        loop(4, transpose_att)
        transpose_act(r.ai, 0, r.ai_t)
        right = jnp.concatenate([r.dproj[k] for k in range(6)], axis=1)
        cot_rows = jnp.concatenate([r.cx[i] for i in range(4)], axis=0)
        for core in range(2):
            attend_out = dot(r.ai_t[core], right)
            output_out = dot(r.att_t[core], cot_rows)
            for k in range(2):
                for yy in range(2):
                    for xx in range(2):
                        row = k * 128 + yy * 48
                        tiles = [
                            attend_out[row : row + 48, (xx * 3 + j) * 128 : (xx * 3 + j) * 128 + 128] for j in range(3)
                        ]
                        acc3[0, slot(xx, yy), core + 2 * k] = pack_four(
                            *tiles, output_out[row : row + 48, xx * 128 : xx * 128 + 128]
                        )
        if inside:
            red3.start(0)

        def proj_sums(i, carry):
            q = jnp.concatenate([r.dproj[0, rows(i), :], r.dproj[1, rows(i), :]], axis=1).astype(F32)
            val = jnp.concatenate([r.dproj[4, rows(i), :], r.dproj[5, rows(i), :]], axis=1).astype(F32)
            return (carry[0] + fold(q), carry[1] + fold(val), carry[2] + fold(r.cx[i].astype(F32)))

        qsum, vsum, csum = lax.fori_loop(0, 4, proj_sums, (zero8, zero8, zero8))
        r.sums[pl.ds(3 + 7, 1), :] = jnp.sum(qsum, axis=0, keepdims=True)
        r.sums[pl.ds(3 + 8, 1), :] = jnp.sum(vsum, axis=0, keepdims=True)
        r.sums[pl.ds(3 + 9, 1), :] = jnp.sum(csum, axis=0, keepdims=True)
        r.sums[pl.ds(13, 3), :] = jnp.zeros((3, HALF), F32)

        def n3_own(i, carry):
            own = dot_nt(proj_rows(i), wproj(half_of(c)))
            n3.wait(i)
            vals = own + r.n3_dst[rows(i), :].astype(F32)
            r.gtmp[rows(i), :] = vals
            return carry[0] + fold(vals), carry[1] + fold(vals * hat3(i))

        sums3 = lax.fori_loop(0, 4, n3_own, (zero8, zero8))
        plain3, cross3, back3 = norm_back(sums3, lambda i: r.gtmp[rows(i), :], hat3, gain3, inv3)
        r.sums[pl.ds(2, 1), :] = cross3
        r.sums[pl.ds(3 + 2, 1), :] = plain3

        def shifted(buf, i, vals):
            buf[0, rows(i, CHUNK, ROW), :] = from_right(vals).astype(BF16)
            buf[1, rows(i, CHUNK, ROW), :] = vals.astype(BF16)
            buf[2, rows(i, CHUNK, ROW), :] = from_left(vals).astype(BF16)

        def residual_back(i, carry):
            vals = r.cx[i].astype(F32) + back3(i)
            r.gres[rows(i), :] = vals
            shifted(r.gr2, i, vals)
            return carry + fold(vals.astype(BF16).astype(F32))

        bias_two = lax.fori_loop(0, 4, residual_back, jnp.zeros((8, HALF), F32))
        r.sums[pl.ds(3 + 4, 1), :] = jnp.sum(bias_two, axis=0, keepdims=True)

        def act_back(buf, g, core, i, size):
            left = jnp.concatenate(
                [buf[b, rows(i, size, 2 * ROW - ROW * a), :] for a in range(3) for b in range(3)], axis=1
            )
            right = jnp.concatenate(
                [wtap(g, 3 * a + b, half_of(core)) for a in range(3) for b in range(3)], axis=1
            )
            return dot_nt(left, right)

        def conv_back(parts, buf, g, name):
            def other(i):
                vals = act_back(buf, g, 1 - c, i, 2 * CHUNK).astype(BF16)
                getattr(r, name + "_src")[rows(i, 2 * CHUNK), :] = vals
                parts.start(2 * i)
                parts.start(2 * i + 1)

            loop(2, other)

        def conv_back_own(parts, buf, g, name, outer, hat):
            def own(i, carry):
                vals = act_back(buf, g, c, i, 2 * CHUNK)
                for j in range(2):
                    at = 2 * i + j
                    parts.wait(at)
                    got = getattr(r, name + "_dst")[rows(at), :].astype(F32)
                    grad = (vals[j * CHUNK : j * CHUNK + CHUNK] + got) * outer(at)
                    r.gtmp[rows(at), :] = grad
                    carry = carry[0] + fold(grad), carry[1] + fold(grad * hat(at))
                return carry

            return lax.fori_loop(0, 2, own, (zero8, zero8))

        def kernel_grad(act_t, buf, acc, after):
            def step(a, carry):
                right = jnp.concatenate(
                    [buf[b, pl.ds(pl.multiple_of(2 * ROW - ROW * a, 32), PX), :] for b in range(3)], axis=1
                )
                out = dot(jnp.concatenate([act_t[0], act_t[1]], axis=0), right)
                for p, zc in enumerate(ALL):
                    for yy in range(2):
                        for xx in range(2):
                            row = p * 128 + yy * 48
                            tiles = [
                                out[row : row + 48, b * HALF + xx * 128 : b * HALF + xx * 128 + 128] for b in range(3)
                            ]
                            acc[a, slot(xx, yy), zc] = pack_taps(*tiles)
                after(a)
                return carry

            lax.fori_loop(0, 3, step, 0)

        d2 = Parts("d2")
        conv_back(d2, r.gr2, k2, "d2")
        kernel_grad(r.act2_t, r.gr2, acc2, red2.start if inside else lambda a: None)

        sums2 = conv_back_own(d2, r.gr2, k2, "d2", lambda i: silu_slope(pre2(i)), hat2)
        if inside:
            red3.second(0)

        plain2, cross2, back2 = norm_back(sums2, lambda i: r.gtmp[rows(i), :], hat2, gain2 * scale, inv2)
        r.sums[pl.ds(1, 1), :] = scale * cross2
        r.sums[pl.ds(3 + 1, 1), :] = scale * plain2
        film_scale_term = gain2 * cross2 + shift2 * plain2
        r.sums[pl.ds(3 + 5, 1), :] = film_scale_term
        r.sums[pl.ds(3 + 6, 1), :] = plain2
        for j in range(2):
            r.ft[j] = film_scale_term[:, j * 128 : j * 128 + 128]
            r.ft[2 + j] = plain2[:, j * 128 : j * 128 + 128]
        head_start(lambda p: r.ft.at[p], r.th, r.th_s, r.th_r)
        r.th[h] = r.ft[h]

        def first_back(i, carry):
            vals = back2(i)
            shifted(r.gr1, i, vals)
            return carry + fold(vals.astype(BF16).astype(F32))

        bias_one = lax.fori_loop(0, 4, first_back, jnp.zeros((8, HALF), F32))
        r.sums[pl.ds(3 + 3, 1), :] = jnp.sum(bias_one, axis=0, keepdims=True)

        d1 = Parts("d1")
        kernel_grad(r.act1_t, r.gr1, acc1, red1.start if inside else lambda a: None)
        if inside:
            for a in range(3):
                red2.second(a)
            red3.third(0)
        conv_back(d1, r.gr1, k1, "d1")

        head_wait(lambda p: r.ft.at[p], r.th, r.th_s, r.th_r)
        for m in range(2):
            r.fa[d, pl.ds(m, 1), :] = jnp.concatenate([r.th[2 * m], r.th[2 * m + 1]], axis=1)
        dp_start(lambda p: r.fa.at[d], r.fa, r.fa_s, r.fa_r)

        def hat1(i):
            return (mixed(i) - mean1) * inv1

        if inside:
            red1.second(0)
            red1.second(1)
            for a in range(3):
                red2.third(a)
        sums1 = conv_back_own(d1, r.gr1, k1, "d1", lambda i: silu_slope(pre1(i)), hat1)
        if inside:
            red1.second(2)
            red1.third(0)
            red1.third(1)

        plain1, cross1, back1 = norm_back(sums1, lambda i: r.gtmp[rows(i), :], hat1, gain1, inv1)
        r.sums[pl.ds(0, 1), :] = cross1
        r.sums[pl.ds(3, 1), :] = plain1
        r.ad[d] = r.sums[...]
        dp_start(lambda p: r.ad.at[d], r.ad, r.ad_s, r.ad_r)

        keep = r.coef[0, x]

        def image_back(i):
            r.io_src[i] = pack_pixels(keep * (r.gres[rows(i), :] + back1(i))).astype(BF16)

        loop(4, image_back)
        head_start(lambda p: r.io_src.at[p], r.io_dst, r.io_s, r.io_r)
        r.io_dst[h] = r.io_src[h]
        if inside:
            red1.third(2)

        dp_wait(lambda p: r.fa.at[d], r.fa, r.fa_s, r.fa_r)
        for j in range(n):
            r.fta[pl.ds(2 * j, 2), :] = r.fa[j]
        film_block = dot_tn_high(r.esel[...], r.fta[...])
        r.film[...] = jnp.concatenate([film_block[:film_rows, :BLK], film_block[:film_rows, 128 : 128 + BLK]], axis=1)
        embed_part = dot_nt_high(r.fta[...], r.wfp[...].astype(F32))
        for j in range(n):
            r.ep[j] = embed_part[2 * j : 2 * j + 2]
        dp_start(lambda p: r.ep.at[p], r.er, r.er_s, r.er_r)
        r.er[d] = r.ep[d]

        dp_wait(lambda p: r.ad.at[d], r.ad, r.ad_s, r.ad_r)
        total = r.ad[0]
        for j in range(1, n):
            total = total + r.ad[j]
        r.hb[h] = total
        head_start(lambda p: r.hb.at[h], r.hb, r.hb_s, r.hb_r)
        head_wait(lambda p: r.ro_src.at[p], r.ro_dst, r.ro_s, r.ro_r)

        dp_wait(lambda p: r.ep.at[p], r.er, r.er_s, r.er_r)
        r.eh[h] = r.er[...]
        head_start(lambda p: r.eh.at[h], r.eh, r.eh_s, r.eh_r)

        if inside:
            for a in range(3):
                r.second[a] = red2.last(a)

        head_wait(lambda p: r.hb.at[h], r.hb, r.hb_s, r.hb_r)
        even = r.hb[0] + r.hb[2]
        odd = r.hb[1] + r.hb[3]
        wide = jnp.concatenate(
            [even[:, :BLK], odd[:, :BLK], even[:, 128 : 128 + BLK], odd[:, 128 : 128 + BLK]], axis=1
        )
        r.gains_out[...] = wide[0:3]
        r.biases_out[...] = wide[3:13]

        head_wait(lambda p: r.eh.at[h], r.eh, r.eh_s, r.eh_r)
        pieces = []
        for j in range(n):
            piece = (r.eh[0, j] + r.eh[1, j]) + (r.eh[2, j] + r.eh[3, j])
            pieces.append(piece[:, :film_rows])
        r.embed_grad[...] = jnp.concatenate(pieces, axis=1) * silu_slope(r.emb[...].astype(F32))

        head_wait(lambda p: r.io_src.at[p], r.io_dst, r.io_s, r.io_r)

        if inside:
            tiles = unpack_four(red3.last(0))
            r.sb_src[...] = jnp.where(c == 0, tiles[2], tiles[0])
            back = rc(r.sb_src, r.sb_dst, r.sb_s.at[0], r.sb_r.at[0], sib)
            back.start()
            r.output[...] = tiles[3]
            for a in range(3):
                r.first[a] = red1.last(a)
            back.wait()
            r.attend[:, 0:128] = jnp.where(c == 0, tiles[0], tiles[1])
            r.attend[:, 128:256] = r.sb_dst[...]
            r.attend[:, 256:384] = jnp.where(c == 0, tiles[1], tiles[2])

    return kernel


def make_writer(names_in, names_out):
    def kernel(*refs):
        count = len(names_in)
        src, dst = Names(names_in, refs[:count]), Names(names_out, refs[count:])
        for name, packed in (("result", src.ro_dst), ("image_grad", src.io_dst)):
            for m in range(2):
                getattr(dst, name)[m] = dot_nt(unpack_pixels(packed[2 * m]), src.sel[0]) + dot_nt(
                    unpack_pixels(packed[2 * m + 1]), src.sel[1]
                )
        for name in ("first", "second"):
            if name in names_out:
                for a in range(3):
                    block = getattr(src, name)[a]
                    getattr(dst, name)[3 * a] = block[:48, :BLK]
                    getattr(dst, name)[3 * a + 1] = block[48:96, :BLK]
                    getattr(dst, name)[3 * a + 2] = last_tap(block)[:, :BLK]
        if "attend" in names_out:
            dst.attend[...] = jnp.concatenate([src.attend[:, j * 128 : j * 128 + BLK] for j in range(3)], axis=1)
            dst.output[...] = src.output[:, :BLK]
        for name in ("embed_grad", "film", "gains_out", "biases_out"):
            getattr(dst, name)[...] = getattr(src, name)[...]

    return kernel


def per_device(n, *args):
    (
        images,
        noise_field,
        time_steps,
        embedding,
        first_kernel,
        second_kernel,
        film_weight,
        attend_weight,
        output_weight,
        norm_gains,
        biases,
        cotangent,
    ) = args
    inside = n == 8
    keep, noise = plan(time_steps)
    coef = jnp.stack([keep, noise])
    maps, height, width, channels = images.shape
    flat_shape = (maps, height * width, channels)
    film_rows = film_weight.shape[0]
    inputs = dict(
        coef=coef,
        images=images.reshape(flat_shape),
        noise=noise_field.reshape(flat_shape),
        cot=cotangent.reshape(flat_shape),
        emb=embedding,
        k1=first_kernel.reshape((9,) + first_kernel.shape[2:]),
        k2=second_kernel.reshape((9,) + second_kernel.shape[2:]),
        wf=film_weight,
        wa=attend_weight,
        wo=output_weight,
        gains=norm_gains,
        biases=biases,
        sel=jnp.asarray(channel_lanes(), BF16),
        gmask=jnp.asarray(group_mask(), BF16),
        selp=jnp.asarray(block_lanes(3), BF16),
    )
    shapes = dict(
        ro_dst=(4, 384, 128),
        io_dst=(4, 384, 128),
        embed_grad=embedding.shape,
        first=(3, 112, 128),
        second=(3, 112, 128),
        film=film_weight.shape,
        attend=(48, 384),
        output=(48, 128),
        gains_out=norm_gains.shape,
        biases_out=biases.shape,
    )
    names_in, names_out = list(INPUTS), list(OUTPUTS)
    core = lax.axis_index("head") % 2
    if not inside:
        def whole(array, row_axis):
            array = lax.all_gather(array, "dp", axis=row_axis, tiled=True)
            return lax.all_gather(array, "head", axis=array.ndim - 1, tiled=True)

        def spread(array, count):
            taps = array.shape[0]
            array = array.reshape(taps, 4, 2, 48, 2, 2, BLK)
            array = lax.dynamic_index_in_dim(array, core, 5, keepdims=False)
            array = jnp.transpose(array, (2, 4, 1, 0, 3, 5))
            array = jnp.pad(array, ((0, 0),) * 5 + ((0, 32),))
            return array.reshape(4, 4, taps * 48, 128)

        full_a = whole(attend_weight, 0).reshape(384, 2, 3, 2, BLK)
        full_a = jnp.transpose(full_a, (2, 0, 1, 3, 4)).reshape(3, 384, 384)
        full_o = whole(output_weight, 0)[None]
        for name, last, array in (("g1", "t1", first_kernel), ("g2", "t2", second_kernel)):
            blocks = spread(whole(array, 2).reshape(9, 384, 384), 9).reshape(4, 4, 3, 3, 48, 128)
            two = blocks[:, :, :, :2].reshape(4, 4, 3, 96, 128)
            inputs[name] = jnp.pad(two, ((0, 0),) * 3 + ((0, 16), (0, 0))).reshape(4, 4, 336, 128)
            inputs[last] = blocks[:, :, :, 2].reshape(4, 4, 144, 128)
        inputs["g3"] = spread(jnp.concatenate([full_a, full_o], axis=0), 4)
        names_in += ["g1", "g2", "t1", "t2", "g3"]
        shapes["first"] = shapes["second"] = (3, 4, 4, 112, 128)
        shapes["attend"] = (1, 4, 4, 144, 128)
        del shapes["output"]
        names_out.remove("output")
    items = scratch_list(n, inside)
    smem = pl.BlockSpec(memory_space=pltpu.SMEM)
    vmem = pl.BlockSpec(memory_space=pltpu.VMEM)
    outs = pl.pallas_call(
        make_kernel(n, inside, names_in + names_out + [name for name, _ in items]),
        out_shape=[
            jax.ShapeDtypeStruct(shapes[name], BF16 if name in ("ro_dst", "io_dst") else F32) for name in names_out
        ],
        in_specs=[smem if name == "coef" else vmem for name in names_in],
        out_specs=[vmem] * len(names_out),
        scratch_shapes=[item for _, item in items],
        compiler_params=pltpu.CompilerParams(
            collective_id=0, has_side_effects=True, vmem_limit_bytes=63 * 1024 * 1024
        ),
        name="blocks",
    )(*[inputs[name] for name in names_in])
    raw = dict(zip(names_out, outs))
    final = dict(
        result=flat_shape,
        image_grad=flat_shape,
        embed_grad=embedding.shape,
        film=film_weight.shape,
        gains_out=norm_gains.shape,
        biases_out=biases.shape,
    )
    if inside:
        final.update(first=(9, 48, BLK), second=(9, 48, BLK), attend=attend_weight.shape, output=output_weight.shape)
    names_last = [name for name in names_out if inside or name not in ("first", "second", "attend")] + ["sel"]
    names_final = list(final)
    outs = pl.pallas_call(
        make_writer(names_last, names_final),
        out_shape=[jax.ShapeDtypeStruct(final[name], F32) for name in names_final],
        in_specs=[vmem] * len(names_last),
        out_specs=[vmem] * len(names_final),
        compiler_params=pltpu.CompilerParams(vmem_limit_bytes=63 * 1024 * 1024),
        name="outputs",
    )(*[inputs["sel"] if name == "sel" else raw[name] for name in names_last])
    out = dict(zip(names_final, outs))
    if not inside:

        def blocks_of(array, size):
            parts = [array[..., k * 48 : k * 48 + 48, :BLK] for k in range(size)]
            if size == 2:
                lanes = [array[..., k * 32 : k * 32 + 32, BLK:] for k in range(3)]
                lanes = jnp.concatenate(lanes, axis=-1)
                parts.append(jnp.concatenate([lanes, array[..., 96:112, :BLK]], axis=-2))
            else:
                lanes = [array[..., k * 48 : k * 48 + 48, BLK:] for k in range(3)]
                parts.append(jnp.concatenate(lanes, axis=-1))
            array = jnp.stack(parts, axis=1)
            array = array.reshape(array.shape[:2] + (2, 2, 4, 48, BLK))
            taps = array.shape[0] * array.shape[1]
            array = jnp.transpose(array, (0, 1, 4, 2, 5, 3, 6)).reshape(taps, 384, 2, 1, BLK)
            both = jnp.concatenate([array, jnp.zeros_like(array)], axis=3)
            return jnp.where(core == 0, both, both[:, :, :, ::-1]).reshape(taps, 384, 384)

        def shared(array, axis):
            array = lax.psum_scatter(array, "head", scatter_dimension=array.ndim - 1, tiled=True)
            return lax.psum_scatter(array, "dp", scatter_dimension=axis, tiled=True)

        out["first"] = shared(blocks_of(raw["first"], 2), 1)
        out["second"] = shared(blocks_of(raw["second"], 2), 1)
        both = blocks_of(raw["attend"], 3)
        joined = both[:3].reshape(3, 384, 2, 2, BLK)
        joined = jnp.transpose(joined, (1, 2, 0, 3, 4)).reshape(384, 1152)
        out["attend"] = shared(joined, 0)
        out["output"] = shared(both[3], 0)
    return (
        out["result"].reshape(images.shape),
        out["image_grad"].reshape(images.shape),
        out["embed_grad"],
        out["first"].reshape(first_kernel.shape),
        out["second"].reshape(second_kernel.shape),
        out["film"],
        out["attend"],
        out["output"],
        out["gains_out"],
        out["biases_out"],
    )


def solution(mesh):
    n = mesh.shape["dp"]
    field = P("dp", "head", None, None)
    taps = P(None, None, "dp", "head")
    both = P("dp", "head")
    return jax.shard_map(
        lambda *args: per_device(n, *args),
        mesh=mesh,
        in_specs=(field, field, P("dp"), P("dp", None), taps, taps, both, both, both, P(), P(), field),
        out_specs=(field, field, P("dp", None), taps, taps, both, both, both, P(), P()),
        check_vma=False,
    )
```

```python
import math

import jax
import jax.numpy as jnp
import numpy as np
from jax import lax
from jax.experimental import pallas as pl
from jax.experimental.pallas import tpu as pltpu
from jax.sharding import PartitionSpec as P

HEAD_DIM = 96
GROUPS = 32
STEPS = 4000
EPS = 1e-05
OFFSET = 0.008
MESH = pl.DeviceIdType.MESH
F32 = jnp.float32
BF16 = jnp.bfloat16

PX = 1024
ROW = 32
CHUNK = 256
BLK = 96
HALF = 256
NHEAD = 4


def plan(time_steps):
    fraction = (time_steps.astype(F32) + 1.0) / STEPS
    start = jnp.square(jnp.cos(jnp.float32(OFFSET / (1.0 + OFFSET) * (math.pi / 2))))
    curve = jnp.square(jnp.cos((fraction + OFFSET) / (1.0 + OFFSET) * (math.pi / 2))) / start
    return (jnp.sqrt(curve), jnp.sqrt(1.0 - curve))


def channel_lanes():
    sel = np.zeros((2, 384, HALF), np.float32)
    for block in range(4):
        for j in range(BLK):
            sel[block % 2, block * BLK + j, (block // 2) * 128 + j] = 1.0
    return sel


def block_lanes(count):
    sel = np.zeros((count * BLK, count * 128), np.float32)
    for block in range(count):
        for j in range(BLK):
            sel[block * BLK + j, block * 128 + j] = 1.0
    return sel


def group_mask():
    lane = np.arange(HALF)
    ok = lane % 128 < BLK
    group = (lane // 128) * 100 + (lane % 128) // 12
    return ((group[:, None] == group[None, :]) & ok[:, None] & ok[None, :]).astype(np.float32)


def dot(a, b):
    return lax.dot_general(a, b, (((1,), (0,)), ((), ())), preferred_element_type=F32)


def dot_nt(a, b):
    return lax.dot_general(a, b, (((1,), (1,)), ((), ())), preferred_element_type=F32)


def dot_nt_high(a, b):
    return lax.dot_general(
        a, b, (((1,), (1,)), ((), ())), preferred_element_type=F32, precision=lax.Precision.HIGHEST
    )


def dot_tn_high(a, b):
    return lax.dot_general(
        a, b, (((0,), (0,)), ((), ())), preferred_element_type=F32, precision=lax.Precision.HIGHEST
    )


def exact_dot(values, ones):
    high = values.astype(BF16).astype(F32)
    rest = values - high
    middle = rest.astype(BF16).astype(F32)
    low = rest - middle
    rows = values.shape[0]
    out = dot(jnp.concatenate([high, middle, low], axis=0).astype(BF16), ones)
    return out[:rows] + out[rows : 2 * rows] + out[2 * rows :]


def sigmoid(v):
    return 1.0 / (1.0 + jnp.exp(-v))


def silu(v):
    return v / (1.0 + jnp.exp(-v))


def silu_slope(v):
    s = sigmoid(v)
    return s * (1.0 + v * (1.0 - s))


def pack_taps(t0, t1, t2):
    t0, t1, t2 = t0[:, :BLK], t1[:, :BLK], t2[:, :BLK]
    join = lambda a, b: jnp.concatenate([a, b], axis=1)
    return jnp.concatenate(
        [
            join(t0[:32], t2[:32, :32]),
            join(t0[32:], t2[:16, 32:64]),
            join(t1[:16], t2[16:32, 32:64]),
            join(t1[16:], t2[:32, 64:]),
            join(t2[32:], jnp.zeros((16, 32), t2.dtype)),
        ],
        axis=0,
    )


def last_tap(packed):
    lanes = [packed[:32, BLK:], packed[32:64, BLK:], packed[64:96, BLK:], jnp.zeros((32, 32), packed.dtype)]
    return jnp.concatenate([jnp.concatenate(lanes, axis=1), packed[96:112]], axis=0)


def pack_four(b0, b1, b2, b3):
    return jnp.concatenate(
        [jnp.concatenate([b[:, :BLK], b3[:, 32 * k : 32 * k + 32]], axis=1) for k, b in enumerate((b0, b1, b2))],
        axis=0,
    )


def unpack_four(packed):
    size = packed.shape[0] // 3
    parts = [packed[k * size : k * size + size] for k in range(3)]
    zero = jnp.zeros((size, 32), packed.dtype)
    fourth = jnp.concatenate([p[:, BLK:] for p in parts] + [zero], axis=1)
    return [jnp.concatenate([p[:, :BLK], zero], axis=1) for p in parts] + [fourth]


def pack_pixels(full):
    half = CHUNK // 2
    return pack_four(full[:half, :128], full[half:, :128], full[:half, 128:], full[half:, 128:])


def unpack_pixels(packed):
    b0, b1, b2, b3 = unpack_four(packed)
    return jnp.concatenate([jnp.concatenate([b0, b2], axis=1), jnp.concatenate([b1, b3], axis=1)], axis=0)


INPUTS = (
    "coef",
    "images",
    "noise",
    "cot",
    "emb",
    "k1",
    "k2",
    "wf",
    "wa",
    "wo",
    "gains",
    "biases",
    "sel",
    "gmask",
    "selp",
)
OUTPUTS = (
    "ro_dst",
    "io_dst",
    "embed_grad",
    "first",
    "second",
    "film",
    "attend",
    "output",
    "gains_out",
    "biases_out",
)


class Names:
    def __init__(self, names, refs):
        for name, ref in zip(names, refs):
            setattr(self, name, ref)


def scratch_list(n, inside):
    dma = pltpu.SemaphoreType.DMA
    items = []

    def vm(name, shape, dtype):
        items.append((name, pltpu.VMEM(shape, dtype)))

    def sem(name, count):
        items.append((name + "_s", dma((count,))))
        items.append((name + "_r", dma((count,))))

    for name in ("mx", "cx", "ro", "io"):
        vm(name + "_src", (4, 384, 128), BF16)
        if name in ("mx", "cx"):
            vm(name + "_dst", (4, 384, 128), BF16)
            vm(name, (4, CHUNK, HALF), BF16)
        sem(name, 4)
    for name in ("act1", "act2"):
        vm(name, (2, PX + 2 * ROW, HALF), BF16)
        vm(name + "_t", (2, HALF, PX), BF16)
        sem(name, 4)
    vm("ai", (2, PX, HALF), BF16)
    vm("ai_t", (2, HALF, PX), BF16)
    sem("ai", 4)
    vm("att", (4, PX, 128), BF16)
    vm("att_t", (2, HALF, PX), BF16)
    sem("att", 4)
    for name in ("do", "n3", "d2", "d1"):
        vm(name + "_src", (PX, HALF), BF16)
        vm(name + "_dst", (PX, HALF), BF16)
        sem(name, 4)
    vm("v2", (PX, HALF), F32)
    vm("v3", (PX, HALF), F32)
    vm("gres", (PX, HALF), F32)
    vm("gtmp", (PX, HALF), F32)
    vm("qkv", (6, PX, 128), BF16)
    vm("kvt", (4, 128, PX), BF16)
    vm("dout", (2, PX, 128), BF16)
    vm("dproj", (6, PX, 128), BF16)
    vm("gr2", (3, PX + 2 * ROW, HALF), BF16)
    vm("gr1", (3, PX + 2 * ROW, HALF), BF16)
    vm("par", (16, 384), F32)
    vm("parown", (16, HALF), F32)
    vm("stat", (16, HALF), F32)
    vm("sums", (16, HALF), F32)
    if inside:
        vm("g1", (3, 4, 4, 112, 128), BF16)
        vm("g2", (3, 4, 4, 112, 128), BF16)
        vm("t1", (4, 4, 144, 128), BF16)
        vm("t2", (4, 4, 144, 128), BF16)
        vm("p3", (1, 4, 4, 144, 128), BF16)
        vm("g3", (4, 4, 192, 128), BF16)
        for name, nc in (("g1", 3), ("g2", 3), ("p3", 1)):
            sem(name + "z", 4 * nc)
            sem(name + "v", 4 * nc)
            sem(name + "w", 8 * nc)
        vm("sw_src", (48, 128), BF16)
        vm("sw_dst", (48, 128), BF16)
        sem("sw", 1)
        vm("sb_src", (48, 128), F32)
        vm("sb_dst", (48, 128), F32)
        sem("sb", 1)
        for name, nc, rows in (("r1", 3, 112), ("r2", 3, 112), ("r3", 1, 144)):
            vm(name + "_acc", (nc, 4, 4, rows, 128), F32)
            vm(name + "w_src", (nc, 2, 4, rows, 128), BF16)
            vm(name + "w_dst", (nc, 2, 4, rows, 128), BF16)
            vm(name + "v_src", (nc, 4, rows, 128), BF16)
            vm(name + "v_dst", (nc, 4, rows, 128), BF16)
            vm(name + "z_src", (nc, 4, rows, 128), BF16)
            vm(name + "z_dst", (nc, 4, rows, 128), BF16)
            sem(name + "w", nc)
            sem(name + "v", nc)
            sem(name + "z", nc * 4)
    vm("el", (n, 2, 768), F32)
    sem("el", n)
    vm("em", (2 * n, 768), F32)
    vm("wfp", (128, HALF), BF16)
    vm("esel", (2 * n, 128), F32)
    vm("fp", (n, 2, HALF), F32)
    vm("fr", (n, 2, HALF), F32)
    sem("fr", n)
    vm("fx", (4, 1, 128), F32)
    vm("fh", (4, 1, 128), F32)
    sem("fh", 4)
    vm("ft", (4, 1, 128), F32)
    vm("th", (4, 1, 128), F32)
    sem("th", 4)
    vm("fa", (n, 2, HALF), F32)
    sem("fa", n)
    vm("fta", (2 * n, HALF), F32)
    vm("ep", (n, 2, 128), F32)
    vm("er", (n, 2, 128), F32)
    sem("er", n)
    vm("eh", (4, n, 2, 128), F32)
    sem("eh", 4)
    vm("ad", (n, 16, HALF), F32)
    sem("ad", n)
    vm("hb", (4, 16, HALF), F32)
    sem("hb", 4)
    return items


def make_kernel(n, inside, names):
    film_rows = 768 // n

    def kernel(*refs):
        r = Names(names, refs)
        d = lax.axis_index("dp")
        h = lax.axis_index("head")
        x = h // 2
        c = h - 2 * x
        z = d // 2
        y = d - 2 * z
        sib = (d, h + 1 - 2 * c)
        xdev = (d, h + 2 - 4 * x)
        v = x + c * (y - x)
        w = y + c * (x - y)
        vdev = (d + c * (1 - 2 * y), h + (1 - c) * (2 - 4 * x))
        wdev = (d + (1 - c) * (1 - 2 * y), h + c * (2 - 4 * x))

        def slot(xx, yy):
            if inside:
                return (yy + c * (xx - yy)) * 2 + xx + c * (yy - xx)
            return yy * 2 + xx

        def rc(src, dst, send, recv, dev):
            return pltpu.make_async_remote_copy(
                src_ref=src, dst_ref=dst, send_sem=send, recv_sem=recv, device_id=dev, device_id_type=MESH
            )

        def loop(count, body):
            def step(i, carry):
                body(i)
                return carry

            lax.fori_loop(0, count, step, 0)

        def rows(i, size=CHUNK, base=0):
            return pl.ds(pl.multiple_of(base + i * size, 32), size)

        def dp_start(src_of, dst, send, recv):
            def step(k, carry):
                peer = lax.rem(d + k, n)
                rc(src_of(peer), dst.at[d], send.at[k], recv.at[d], (peer, h)).start()
                return carry

            lax.fori_loop(1, n, step, 0)

        def dp_wait(src_of, dst, send, recv):
            def step(k, carry):
                peer = lax.rem(d + k, n)
                copy = rc(src_of(peer), dst.at[peer], send.at[k], recv.at[peer], (peer, h))
                copy.wait_recv()
                copy.wait_send()
                return carry

            lax.fori_loop(1, n, step, 0)

        def head_start(src_of, dst, send, recv):
            for k in range(1, 4):
                peer = lax.rem(h + k, 4)
                rc(src_of(peer), dst.at[h], send.at[k], recv.at[h], (d, peer)).start()

        def head_wait(src_of, dst, send, recv):
            for k in range(1, 4):
                peer = lax.rem(h + k, 4)
                copy = rc(src_of(peer), dst.at[peer], send.at[k], recv.at[peer], (d, peer))
                copy.wait_recv()
                copy.wait_send()

        class Halves:
            def __init__(self, name, base):
                self.buf, self.base = getattr(r, name), base
                self.send, self.recv = getattr(r, name + "_s"), getattr(r, name + "_r")

            def at(self, core, i):
                return self.buf.at[core, rows(i, CHUNK, self.base)]

            def start(self, i):
                ref = self.at(c, i)
                rc(ref, ref, self.send.at[i], self.recv.at[i], sib).start()

            def wait(self):
                for i in range(4):
                    ref = self.at(1 - c, i)
                    copy = rc(ref, ref, self.send.at[i], self.recv.at[i], sib)
                    copy.wait_recv()
                    copy.wait_send()

        class Parts:
            def __init__(self, name):
                self.src, self.dst = getattr(r, name + "_src"), getattr(r, name + "_dst")
                self.send, self.recv = getattr(r, name + "_s"), getattr(r, name + "_r")

            def start(self, i):
                rc(self.src.at[rows(i)], self.dst.at[rows(i)], self.send.at[i], self.recv.at[i], sib).start()

            def wait(self, i):
                copy = rc(self.src.at[rows(i)], self.dst.at[rows(i)], self.send.at[i], self.recv.at[i], sib)
                copy.wait_recv()
                copy.wait_send()

        class Gather:
            def __init__(self, name):
                self.g = getattr(r, name)
                self.zs, self.zr = getattr(r, name + "z_s"), getattr(r, name + "z_r")
                self.vs, self.vr = getattr(r, name + "v_s"), getattr(r, name + "v_r")
                self.ws, self.wr = getattr(r, name + "w_s"), getattr(r, name + "w_r")

            def zcopy(self, a, k, zslot):
                ref = self.g.at[a, w * 2 + v, zslot]
                peer = (lax.rem(z + k, 4) * 2 + y, h)
                return rc(ref, ref, self.zs.at[4 * a + k], self.zr.at[4 * a + zslot], peer)

            def vcopy(self, a, vv, zz):
                ref = self.g.at[a, w * 2 + vv, zz]
                return rc(ref, ref, self.vs.at[4 * a + zz], self.vr.at[4 * a + zz], vdev)

            def wcopy(self, a, ww, vv, zz):
                ref = self.g.at[a, ww * 2 + vv, zz]
                at = 8 * a + vv * 4 + zz
                return rc(ref, ref, self.ws.at[at], self.wr.at[at], wdev)

            def own(self, a):
                for k in range(1, 4):
                    self.zcopy(a, k, z).start()
                self.vcopy(a, v, z).start()
                self.wcopy(a, w, v, z).start()

            def pass_z(self, a):
                self.vcopy(a, 1 - v, z).wait_recv()
                self.wcopy(a, w, 1 - v, z).start()

                def step(k, carry):
                    zz = lax.rem(z + k, 4)
                    self.zcopy(a, k, zz).wait_recv()
                    self.vcopy(a, v, zz).start()
                    self.wcopy(a, w, v, zz).start()
                    return carry

                lax.fori_loop(1, 4, step, 0)

            def pass_v(self, a):
                def step(k, carry):
                    zz = lax.rem(z + k, 4)
                    self.vcopy(a, 1 - v, zz).wait_recv()
                    self.wcopy(a, w, 1 - v, zz).start()
                    return carry

                lax.fori_loop(1, 4, step, 0)

            def done(self, a):
                def zstep(k, carry):
                    self.zcopy(a, k, z).wait_send()
                    return carry

                lax.fori_loop(1, 4, zstep, 0)

                def step(zz, carry):
                    self.vcopy(a, v, zz).wait_send()
                    for vv in range(2):
                        self.wcopy(a, 1 - w, vv, zz).wait_recv()
                        self.wcopy(a, w, vv, zz).wait_send()
                    return carry

                lax.fori_loop(0, 4, step, 0)

        class Reduce:
            def __init__(self, name, count):
                get = lambda tail: getattr(r, name + tail)
                self.acc, self.count = get("_acc"), count
                self.wsrc, self.wdst, self.ws, self.wr = get("w_src"), get("w_dst"), get("w_s"), get("w_r")
                self.vsrc, self.vdst, self.vs, self.vr = get("v_src"), get("v_dst"), get("v_s"), get("v_r")
                self.zsrc, self.zdst, self.zs, self.zr = get("z_src"), get("z_dst"), get("z_s"), get("z_r")

            def wcopy(self, a):
                return rc(self.wsrc.at[a], self.wdst.at[a], self.ws.at[a], self.wr.at[a], wdev)

            def vcopy(self, a):
                return rc(self.vsrc.at[a], self.vdst.at[a], self.vs.at[a], self.vr.at[a], vdev)

            def zcopy(self, a, k, dst):
                peer = lax.rem(z + k, 4)
                return rc(
                    self.zsrc.at[a, peer],
                    self.zdst.at[a, dst],
                    self.zs.at[a * 4 + k],
                    self.zr.at[a * 4 + dst],
                    (peer * 2 + y, h),
                )

            def start(self, a):
                def step(i, carry):
                    vv, zz = i // 4, lax.rem(i, 4)
                    self.wsrc[a, vv, zz] = self.acc[a, (1 - w) * 2 + vv, zz].astype(BF16)
                    return carry

                lax.fori_loop(0, 8, step, 0)
                self.wcopy(a).start()

            def second(self, a):
                self.wcopy(a).wait_recv()

                def step(zz, carry):
                    self.vsrc[a, zz] = (
                        self.acc[a, w * 2 + 1 - v, zz] + self.wdst[a, 1 - v, zz].astype(F32)
                    ).astype(BF16)
                    self.acc[a, w * 2 + v, zz] = self.acc[a, w * 2 + v, zz] + self.wdst[a, v, zz].astype(F32)
                    return carry

                lax.fori_loop(0, 4, step, 0)
                self.vcopy(a).start()

            def third(self, a):
                self.vcopy(a).wait_recv()

                def step(zz, carry):
                    total = self.acc[a, w * 2 + v, zz] + self.vdst[a, zz].astype(F32)
                    self.acc[a, w * 2 + v, zz] = total
                    self.zsrc[a, zz] = total.astype(BF16)
                    return carry

                lax.fori_loop(0, 4, step, 0)
                for k in range(1, 4):
                    self.zcopy(a, k, z).start()

            def last(self, a):
                total = self.acc[a, w * 2 + v, z]
                for k in range(1, 4):
                    peer = lax.rem(z + k, 4)
                    copy = self.zcopy(a, k, peer)
                    copy.wait_recv()
                    copy.wait_send()
                    total = total + self.zdst[a, peer].astype(F32)
                self.wcopy(a).wait_send()
                self.vcopy(a).wait_send()
                return total

        class Taps:
            def __init__(self, packed, last):
                self.packed, self.last = packed, last

            def block(self, tap, zc, xx, yy):
                a, b = tap // 3, tap % 3
                if b < 2:
                    return self.packed[a, slot(xx, yy), zc, pl.ds(b * 48, 48), :]
                return self.last[slot(xx, yy), zc, pl.ds(a * 48, 48), :]

            def unpack(self, a):
                def step(i, carry):
                    q, zz = i // 4, lax.rem(i, 4)
                    self.last[q, zz, pl.ds(a * 48, 48), :] = last_tap(self.packed[a, q, zz])
                    return carry

                lax.fori_loop(0, 16, step, 0)

        class Plain:
            def __init__(self, blocks):
                self.blocks = blocks

            def block(self, tap, zc, xx, yy):
                return self.blocks[slot(xx, yy), zc, pl.ds(tap * 48, 48), :]

            def unpack(self):
                def step(i, carry):
                    q, zz = i // 4, lax.rem(i, 4)
                    self.blocks[q, zz] = jnp.concatenate(unpack_four(r.p3[0, q, zz]), axis=0)
                    return carry

                lax.fori_loop(0, 16, step, 0)

        k1, k2, k3 = Taps(r.g1, r.t1), Taps(r.g2, r.t2), Plain(r.g3)

        def wtile(g, tap, zc, xx):
            return jnp.concatenate(
                [g.block(tap, zc, xx, 0), g.block(tap, zc, xx, 1), jnp.zeros((32, 128), BF16)], axis=0
            )

        def wtap(g, tap, zcs):
            return jnp.concatenate(
                [jnp.concatenate([wtile(g, tap, zc, xx) for xx in range(2)], axis=1) for zc in zcs], axis=0
            )

        ALL = (0, 2, 1, 3)

        def half_of(core):
            return (core, core + 2)

        def wproj(zcs):
            return jnp.concatenate(
                [
                    jnp.concatenate([wtile(k3, j, zc, xx) for xx in range(2) for j in range(3)], axis=1)
                    for zc in zcs
                ],
                axis=0,
            )

        def flat(buf, base, i, size):
            return jnp.concatenate([buf[0, rows(i, size, base), :], buf[1, rows(i, size, base), :]], axis=1)

        barrier = pltpu.get_barrier_semaphore()

        def greet(k, carry):
            pl.semaphore_signal(barrier, inc=1, device_id=(lax.rem(d + k, n), h), device_id_type=MESH)
            return carry

        lax.fori_loop(1, n, greet, 0)
        for k in range(1, 4):
            pl.semaphore_signal(barrier, inc=1, device_id=(d, lax.rem(h + k, 4)), device_id_type=MESH)
        if inside:
            for a in range(3):
                r.g1[a, w * 2 + v, z] = pack_taps(*[r.k1[3 * a + b] for b in range(3)])
        pl.semaphore_wait(barrier, n - 1 + 3)
        if inside:
            ga, gb, gc = Gather("g1"), Gather("g2"), Gather("p3")
            for a in range(3):
                ga.own(a)

        def mix(m, carry):
            field = r.coef[0, m] * r.images[m].astype(F32) + r.coef[1, m] * r.noise[m].astype(F32)
            low = field.astype(BF16)
            for core in range(2):
                r.mx_src[m * 2 + core] = pack_pixels(dot(low, r.sel[core])).astype(BF16)
            return carry

        lax.fori_loop(0, 2, mix, 0)
        head_start(lambda p: r.mx_src.at[p], r.mx_dst, r.mx_s, r.mx_r)
        r.mx_dst[h] = r.mx_src[h]

        emb = r.emb[...].astype(F32)
        r.el[d] = silu(emb).astype(BF16).astype(F32)
        dp_start(lambda p: r.el.at[d], r.el, r.el_s, r.el_r)

        if inside:
            blocks = dot(r.wa[...], r.selp[: 3 * BLK, : 3 * 128]).astype(BF16)
            r.sw_src[...] = blocks[:, 128:256]
            swap = rc(r.sw_src, r.sw_dst, r.sw_s.at[0], r.sw_r.at[0], sib)
            swap.start()
            for a in range(3):
                r.g2[a, w * 2 + v, z] = pack_taps(*[r.k2[3 * a + b] for b in range(3)])
        r.par[0:3, :] = r.gains[...]
        r.par[3:13, :] = r.biases[...]
        r.par[13:16, :] = jnp.zeros((3, 384), F32)
        r.parown[...] = exact_dot(r.par[...], r.sel[c])

        def prow(i):
            return r.parown[pl.ds(i, 1), :]

        for buf in (r.act1, r.act2):
            for core in range(2):
                buf[core, pl.ds(0, ROW), :] = jnp.zeros((ROW, HALF), BF16)
                buf[core, pl.ds(PX + ROW, ROW), :] = jnp.zeros((ROW, HALF), BF16)
        for buf in (r.gr1, r.gr2):
            for b in range(3):
                buf[b, pl.ds(0, ROW), :] = jnp.zeros((ROW, HALF), BF16)
                buf[b, pl.ds(PX + ROW, ROW), :] = jnp.zeros((ROW, HALF), BF16)
        r.wfp[...] = jnp.zeros((128, HALF), BF16)
        r.wfp[pl.ds(0, film_rows), :] = dot(r.wf[...], r.selp[: 2 * BLK, :HALF]).astype(BF16)
        if inside:
            ga.pass_z(0)
            ga.pass_z(1)
            ga.pass_v(0)
            ga.pass_z(2)
            for a in range(3):
                gb.own(a)

        count = float(PX * 12)

        def fold(vals):
            return jnp.sum(vals.reshape(CHUNK // 8, 8, HALF), axis=0)

        def sums_of(fn, k):
            def step(i, carry):
                return tuple(a + fold(b) for a, b in zip(carry, fn(i)))

            zero = jnp.zeros((8, HALF), F32)
            return lax.fori_loop(0, 4, step, (zero,) * k)

        def group_mean(part):
            return jnp.sum(exact_dot(part, r.gmask[...]), axis=0, keepdims=True) / count

        def norm(load, which, total):
            mean = group_mean(total)
            (square,) = sums_of(lambda i: (jnp.square(load(i) - mean),), 1)
            inv = lax.rsqrt(group_mean(square) + EPS)
            r.stat[pl.ds(2 * which, 1), :] = mean
            r.stat[pl.ds(2 * which + 1, 1), :] = inv
            return mean, inv

        zero8 = jnp.zeros((8, HALF), F32)

        def norm_back(sums, load_grad, load_hat, coef, inv):
            plain, cross = sums
            plain_mean, cross_mean = group_mean(coef * plain), group_mean(coef * cross)

            def chunk(i):
                return inv * (coef * load_grad(i) - plain_mean - load_hat(i) * cross_mean)

            return (
                jnp.sum(plain, axis=0, keepdims=True),
                jnp.sum(cross, axis=0, keepdims=True),
                chunk,
            )

        head_wait(lambda p: r.mx_src.at[p], r.mx_dst, r.mx_s, r.mx_r)

        def unpack_mixed(i, carry):
            vals = unpack_pixels(r.mx_dst[i])
            r.mx[i] = vals
            return carry + fold(vals.astype(F32))

        mixed_sum = lax.fori_loop(0, 4, unpack_mixed, zero8)

        def mixed(i):
            return r.mx[i].astype(F32)

        mean1, inv1 = norm(mixed, 0, mixed_sum)
        if inside:
            ga.pass_v(1)
        gain1, shift1 = prow(0), prow(3)
        act1 = Halves("act1", ROW)

        def pre1(i):
            return (mixed(i) - mean1) * inv1 * gain1 + shift1

        def first_act(i):
            r.act1[c, rows(i, CHUNK, ROW), :] = silu(pre1(i)).astype(BF16)
            act1.start(i)

        loop(4, first_act)
        if inside:
            ga.pass_v(2)

        dp_wait(lambda p: r.el.at[d], r.el, r.el_s, r.el_r)
        for j in range(n):
            r.em[pl.ds(2 * j, 2), :] = r.el[j]
        place = lax.broadcasted_iota(jnp.int32, (768, 128), 0) - film_rows * d
        lane = lax.broadcasted_iota(jnp.int32, (768, 128), 1)
        pick = jnp.where((place == lane) & (lane < film_rows), 1.0, 0.0).astype(BF16)
        r.esel[...] = dot(r.em[...].astype(BF16), pick)
        film_part = dot(r.esel[...].astype(BF16), r.wfp[...])
        for j in range(n):
            r.fp[j] = film_part[2 * j : 2 * j + 2]
        dp_start(lambda p: r.fp.at[p], r.fr, r.fr_s, r.fr_r)
        r.fr[d] = r.fp[d]
        if inside:
            swap.wait()
            got = r.sw_dst[...]
            keep0, keep2 = blocks[:, :128], blocks[:, 256:]
            r.p3[0, w * 2 + v, z] = pack_four(
                jnp.where(c == 0, keep0, got),
                jnp.where(c == 0, keep2, keep0),
                jnp.where(c == 0, got, keep2),
                r.wo[...],
            )
            gb.pass_z(0)
            gb.pass_z(1)
            gb.pass_v(0)
            gb.pass_z(2)
            gc.own(0)
        dp_wait(lambda p: r.fp.at[p], r.fr, r.fr_s, r.fr_r)
        film_sum = r.fr[0]
        for j in range(1, n):
            film_sum = film_sum + r.fr[j]
        for m in range(2):
            for core in range(2):
                r.fx[m * 2 + core] = film_sum[m : m + 1, core * 128 : core * 128 + 128]
        head_start(lambda p: r.fx.at[p], r.fh, r.fh_s, r.fh_r)
        r.fh[h] = r.fx[h]

        def split_cot(m, carry):
            for core in range(2):
                r.cx_src[m * 2 + core] = pack_pixels(dot(r.cot[m], r.sel[core])).astype(BF16)
            return carry

        lax.fori_loop(0, 2, split_cot, 0)
        head_start(lambda p: r.cx_src.at[p], r.cx_dst, r.cx_s, r.cx_r)
        r.cx_dst[h] = r.cx_src[h]

        column = lax.broadcasted_iota(jnp.int32, (CHUNK, HALF), 0) % ROW
        not_first = column > 0
        not_last = column < ROW - 1

        def from_left(vals):
            return jnp.where(not_first, pltpu.roll(vals, 1, 0), 0.0)

        def from_right(vals):
            return jnp.where(not_last, pltpu.roll(vals, CHUNK - 1, 0), 0.0)

        def transpose_act(buf, base, out):
            for core in range(2):
                for q in range(4):
                    out[core, :, pl.ds(q * CHUNK, CHUNK)] = jnp.transpose(
                        buf[core, pl.ds(base + q * CHUNK, CHUNK), :]
                    )

        def conv(buf, g, store, between):
            weights = lambda: jnp.concatenate(
                [jnp.concatenate([wtap(g, 3 * a + b, ALL) for b in range(3)], axis=1) for a in range(3)], axis=0
            )

            total = zero8
            for i in range(2):
                left = jnp.concatenate([flat(buf, ROW * a, i, 2 * CHUNK) for a in range(3)], axis=1)
                out = dot(left, weights())
                for j in range(2):
                    part = out[j * CHUNK : j * CHUNK + CHUNK]
                    part = part[:, HALF : 2 * HALF] + from_left(part[:, :HALF]) + from_right(part[:, 2 * HALF :])
                    total = total + fold(store(2 * i + j, part))
                if i == 0:
                    between()
            return total

        act1.wait()
        transpose_act(r.act1, ROW, r.act1_t)
        if inside:
            gb.pass_v(1)
            for a in range(3):
                ga.done(a)
                k1.unpack(a)

        def store_v2(i, vals):
            vals = vals + prow(6)
            r.v2[rows(i), :] = vals
            return vals

        v2_sum = conv(r.act1, k1, store_v2, (lambda: gb.pass_v(2)) if inside else lambda: None)
        head_wait(lambda p: r.fx.at[p], r.fh, r.fh_s, r.fh_r)
        scale = 1.0 + (jnp.concatenate([r.fh[0], r.fh[1]], axis=1) + prow(8))
        shift = jnp.concatenate([r.fh[2], r.fh[3]], axis=1) + prow(9)
        mean2, inv2 = norm(lambda i: r.v2[rows(i), :], 1, v2_sum)
        gain2, shift2 = prow(1), prow(4)
        act2 = Halves("act2", ROW)

        def hat2(i):
            return (r.v2[rows(i), :] - mean2) * inv2

        def pre2(i):
            return (hat2(i) * gain2 + shift2) * scale + shift

        def second_act(i):
            r.act2[c, rows(i, CHUNK, ROW), :] = silu(pre2(i)).astype(BF16)
            act2.start(i)

        loop(4, second_act)
        if inside:
            gc.pass_z(0)

        act2.wait()
        transpose_act(r.act2, ROW, r.act2_t)
        if inside:
            for a in range(3):
                gb.done(a)
                k2.unpack(a)

        def store_v3(i, vals):
            vals = mixed(i) + (vals + prow(7))
            r.v3[rows(i), :] = vals
            return vals

        v3_sum = conv(r.act2, k2, store_v3, (lambda: gc.pass_v(0)) if inside else lambda: None)
        mean3, inv3 = norm(lambda i: r.v3[rows(i), :], 2, v3_sum)
        gain3, shift3 = prow(2), prow(5)
        ai = Halves("ai", 0)

        def hat3(i):
            return (r.v3[rows(i), :] - mean3) * inv3

        def attend_in(i):
            r.ai[c, rows(i), :] = (hat3(i) * gain3 + shift3).astype(BF16)
            ai.start(i)

        loop(4, attend_in)

        if inside:
            gc.done(0)
            k3.unpack()
        head_wait(lambda p: r.cx_src.at[p], r.cx_dst, r.cx_s, r.cx_r)

        def unpack_cot(i):
            r.cx[i] = unpack_pixels(r.cx_dst[i])

        loop(4, unpack_cot)
        dop = Parts("do")

        def do_other(i):
            r.do_src[rows(i), :] = dot_nt(r.cx[i], wtap(k3, 3, half_of(1 - c))).astype(BF16)
            dop.start(i)

        loop(4, do_other)

        ai.wait()
        bias_proj = [prow(10)[:, :128], prow(10)[:, 128:], None, None, prow(11)[:, :128], prow(11)[:, 128:]]

        def project(i):
            out = dot(flat(r.ai, 0, i, CHUNK), wproj(ALL))
            for k in range(6):
                part = out[:, k * 128 : k * 128 + 128]
                if bias_proj[k] is not None:
                    part = part + bias_proj[k]
                r.qkv[k, rows(i), :] = part.astype(BF16)

        loop(4, project)

        def do_own(i):
            own = dot_nt(r.cx[i], wtap(k3, 3, half_of(c)))
            dop.wait(i)
            full = (own + r.do_dst[rows(i), :].astype(F32)).astype(BF16)
            for k in range(2):
                r.dout[k, rows(i), :] = full[:, k * 128 : k * 128 + 128]

        loop(4, do_own)

        factor = 1.0 / math.sqrt(HEAD_DIM)
        factor2 = factor * math.log2(math.e)
        att = []

        def transposes(k):
            r.kvt[k] = jnp.transpose(r.qkv[k + 2])

        loop(4, transposes)

        def att_ref(core, k):
            return r.att.at[core * 2 + k]

        def one_head(k):
            lows, grads = [], []
            for b in range(2):
                at = pl.ds(b * 2 * CHUNK, 2 * CHUNK)
                query = r.qkv[k, at, :]
                grad = r.dout[k, at, :]
                scores = dot_nt(r.qkv[2 + k], query)
                peak = jnp.max(scores, axis=0, keepdims=True)
                expo = jnp.exp2((scores - peak) * factor2)
                inverse = 1.0 / jnp.sum(expo, axis=0, keepdims=True)
                low = (expo * inverse).astype(BF16)
                got = dot(r.kvt[2 + k], low)
                r.att[2 * c + k, at, :] = jnp.transpose(got).astype(BF16)
                spread = jnp.sum(got * jnp.transpose(grad).astype(F32), axis=0, keepdims=True)
                probs_grad = dot_nt(r.qkv[4 + k], grad)
                scores_grad = ((probs_grad - spread) * inverse * expo).astype(BF16)
                back = dot(r.kvt[k], scores_grad)
                r.dproj[k, at, :] = (jnp.transpose(back) * factor).astype(BF16)
                lows.append(low)
                grads.append(scores_grad)
            ref = att_ref(c, k)
            rc(ref, ref, r.att_s.at[k], r.att_r.at[k], sib).start()
            r.dproj[4 + k] = dot(jnp.concatenate(lows, axis=1), r.dout[k]).astype(BF16)
            r.dproj[2 + k] = (dot(jnp.concatenate(grads, axis=1), r.qkv[k]) * factor).astype(BF16)

        loop(2, one_head)

        n3 = Parts("n3")

        def proj_rows(i):
            return jnp.concatenate([r.dproj[k, rows(i), :] for k in range(6)], axis=1)

        def n3_other(i):
            r.n3_src[rows(i), :] = dot_nt(proj_rows(i), wproj(half_of(1 - c))).astype(BF16)
            n3.start(i)

        loop(4, n3_other)

        for k in range(2):
            ref = att_ref(1 - c, k)
            copy = rc(ref, ref, r.att_s.at[k], r.att_r.at[k], sib)
            copy.wait_recv()
            copy.wait_send()

        def result(i):
            left = jnp.concatenate([r.att[p, rows(i), :] for p in range(4)], axis=1)
            branch = dot(left, wtap(k3, 3, ALL)) + prow(12)
            r.ro_src[i] = pack_pixels(r.v3[rows(i), :] + branch).astype(BF16)

        loop(4, result)
        head_start(lambda p: r.ro_src.at[p], r.ro_dst, r.ro_s, r.ro_r)
        r.ro_dst[h] = r.ro_src[h]

        if inside:
            red1, red2, red3 = Reduce("r1", 3), Reduce("r2", 3), Reduce("r3", 1)
            acc1, acc2, acc3 = r.r1_acc, r.r2_acc, r.r3_acc
        else:
            acc1, acc2, acc3 = r.first, r.second, r.attend

        def transpose_att(p):
            r.att_t[p // 2, pl.ds(pl.multiple_of(lax.rem(p, 2) * 128, 128), 128), :] = jnp.transpose(r.att[p])

        loop(4, transpose_att)
        transpose_act(r.ai, 0, r.ai_t)
        right = jnp.concatenate([r.dproj[k] for k in range(6)], axis=1)
        cot_rows = jnp.concatenate([r.cx[i] for i in range(4)], axis=0)
        for core in range(2):
            attend_out = dot(r.ai_t[core], right)
            output_out = dot(r.att_t[core], cot_rows)
            for k in range(2):
                for yy in range(2):
                    for xx in range(2):
                        row = k * 128 + yy * 48
                        tiles = [
                            attend_out[row : row + 48, (xx * 3 + j) * 128 : (xx * 3 + j) * 128 + 128] for j in range(3)
                        ]
                        acc3[0, slot(xx, yy), core + 2 * k] = pack_four(
                            *tiles, output_out[row : row + 48, xx * 128 : xx * 128 + 128]
                        )
        if inside:
            red3.start(0)

        def proj_sums(i, carry):
            q = jnp.concatenate([r.dproj[0, rows(i), :], r.dproj[1, rows(i), :]], axis=1).astype(F32)
            val = jnp.concatenate([r.dproj[4, rows(i), :], r.dproj[5, rows(i), :]], axis=1).astype(F32)
            return (carry[0] + fold(q), carry[1] + fold(val), carry[2] + fold(r.cx[i].astype(F32)))

        qsum, vsum, csum = lax.fori_loop(0, 4, proj_sums, (zero8, zero8, zero8))
        r.sums[pl.ds(3 + 7, 1), :] = jnp.sum(qsum, axis=0, keepdims=True)
        r.sums[pl.ds(3 + 8, 1), :] = jnp.sum(vsum, axis=0, keepdims=True)
        r.sums[pl.ds(3 + 9, 1), :] = jnp.sum(csum, axis=0, keepdims=True)
        r.sums[pl.ds(13, 3), :] = jnp.zeros((3, HALF), F32)

        def n3_own(i, carry):
            own = dot_nt(proj_rows(i), wproj(half_of(c)))
            n3.wait(i)
            vals = own + r.n3_dst[rows(i), :].astype(F32)
            r.gtmp[rows(i), :] = vals
            return carry[0] + fold(vals), carry[1] + fold(vals * hat3(i))

        sums3 = lax.fori_loop(0, 4, n3_own, (zero8, zero8))
        plain3, cross3, back3 = norm_back(sums3, lambda i: r.gtmp[rows(i), :], hat3, gain3, inv3)
        r.sums[pl.ds(2, 1), :] = cross3
        r.sums[pl.ds(3 + 2, 1), :] = plain3

        def shifted(buf, i, vals):
            buf[0, rows(i, CHUNK, ROW), :] = from_right(vals).astype(BF16)
            buf[1, rows(i, CHUNK, ROW), :] = vals.astype(BF16)
            buf[2, rows(i, CHUNK, ROW), :] = from_left(vals).astype(BF16)

        def residual_back(i, carry):
            vals = r.cx[i].astype(F32) + back3(i)
            r.gres[rows(i), :] = vals
            shifted(r.gr2, i, vals)
            return carry + fold(vals.astype(BF16).astype(F32))

        bias_two = lax.fori_loop(0, 4, residual_back, jnp.zeros((8, HALF), F32))
        r.sums[pl.ds(3 + 4, 1), :] = jnp.sum(bias_two, axis=0, keepdims=True)

        def act_back(buf, g, core, i, size):
            left = jnp.concatenate(
                [buf[b, rows(i, size, 2 * ROW - ROW * a), :] for a in range(3) for b in range(3)], axis=1
            )
            right = jnp.concatenate(
                [wtap(g, 3 * a + b, half_of(core)) for a in range(3) for b in range(3)], axis=1
            )
            return dot_nt(left, right)

        def conv_back(parts, buf, g, name):
            def other(i):
                vals = act_back(buf, g, 1 - c, i, 2 * CHUNK).astype(BF16)
                getattr(r, name + "_src")[rows(i, 2 * CHUNK), :] = vals
                parts.start(2 * i)
                parts.start(2 * i + 1)

            loop(2, other)

        def conv_back_own(parts, buf, g, name, outer, hat):
            def own(i, carry):
                vals = act_back(buf, g, c, i, 2 * CHUNK)
                for j in range(2):
                    at = 2 * i + j
                    parts.wait(at)
                    got = getattr(r, name + "_dst")[rows(at), :].astype(F32)
                    grad = (vals[j * CHUNK : j * CHUNK + CHUNK] + got) * outer(at)
                    r.gtmp[rows(at), :] = grad
                    carry = carry[0] + fold(grad), carry[1] + fold(grad * hat(at))
                return carry

            return lax.fori_loop(0, 2, own, (zero8, zero8))

        def kernel_grad(act_t, buf, acc, after):
            def step(a, carry):
                right = jnp.concatenate(
                    [buf[b, pl.ds(pl.multiple_of(2 * ROW - ROW * a, 32), PX), :] for b in range(3)], axis=1
                )
                out = dot(jnp.concatenate([act_t[0], act_t[1]], axis=0), right)
                for p, zc in enumerate(ALL):
                    for yy in range(2):
                        for xx in range(2):
                            row = p * 128 + yy * 48
                            tiles = [
                                out[row : row + 48, b * HALF + xx * 128 : b * HALF + xx * 128 + 128] for b in range(3)
                            ]
                            acc[a, slot(xx, yy), zc] = pack_taps(*tiles)
                after(a)
                return carry

            lax.fori_loop(0, 3, step, 0)

        d2 = Parts("d2")
        conv_back(d2, r.gr2, k2, "d2")
        kernel_grad(r.act2_t, r.gr2, acc2, red2.start if inside else lambda a: None)

        sums2 = conv_back_own(d2, r.gr2, k2, "d2", lambda i: silu_slope(pre2(i)), hat2)
        if inside:
            red3.second(0)

        plain2, cross2, back2 = norm_back(sums2, lambda i: r.gtmp[rows(i), :], hat2, gain2 * scale, inv2)
        r.sums[pl.ds(1, 1), :] = scale * cross2
        r.sums[pl.ds(3 + 1, 1), :] = scale * plain2
        film_scale_term = gain2 * cross2 + shift2 * plain2
        r.sums[pl.ds(3 + 5, 1), :] = film_scale_term
        r.sums[pl.ds(3 + 6, 1), :] = plain2
        for j in range(2):
            r.ft[j] = film_scale_term[:, j * 128 : j * 128 + 128]
            r.ft[2 + j] = plain2[:, j * 128 : j * 128 + 128]
        head_start(lambda p: r.ft.at[p], r.th, r.th_s, r.th_r)
        r.th[h] = r.ft[h]

        def first_back(i, carry):
            vals = back2(i)
            shifted(r.gr1, i, vals)
            return carry + fold(vals.astype(BF16).astype(F32))

        bias_one = lax.fori_loop(0, 4, first_back, jnp.zeros((8, HALF), F32))
        r.sums[pl.ds(3 + 3, 1), :] = jnp.sum(bias_one, axis=0, keepdims=True)

        d1 = Parts("d1")
        kernel_grad(r.act1_t, r.gr1, acc1, red1.start if inside else lambda a: None)
        if inside:
            for a in range(3):
                red2.second(a)
            red3.third(0)
        conv_back(d1, r.gr1, k1, "d1")

        head_wait(lambda p: r.ft.at[p], r.th, r.th_s, r.th_r)
        for m in range(2):
            r.fa[d, pl.ds(m, 1), :] = jnp.concatenate([r.th[2 * m], r.th[2 * m + 1]], axis=1)
        dp_start(lambda p: r.fa.at[d], r.fa, r.fa_s, r.fa_r)

        def hat1(i):
            return (mixed(i) - mean1) * inv1

        if inside:
            red1.second(0)
            red1.second(1)
            for a in range(3):
                red2.third(a)
        sums1 = conv_back_own(d1, r.gr1, k1, "d1", lambda i: silu_slope(pre1(i)), hat1)
        if inside:
            red1.second(2)
            red1.third(0)
            red1.third(1)

        plain1, cross1, back1 = norm_back(sums1, lambda i: r.gtmp[rows(i), :], hat1, gain1, inv1)
        r.sums[pl.ds(0, 1), :] = cross1
        r.sums[pl.ds(3, 1), :] = plain1
        r.ad[d] = r.sums[...]
        dp_start(lambda p: r.ad.at[d], r.ad, r.ad_s, r.ad_r)

        keep = r.coef[0, x]

        def image_back(i):
            r.io_src[i] = pack_pixels(keep * (r.gres[rows(i), :] + back1(i))).astype(BF16)

        loop(4, image_back)
        head_start(lambda p: r.io_src.at[p], r.io_dst, r.io_s, r.io_r)
        r.io_dst[h] = r.io_src[h]
        if inside:
            red1.third(2)

        dp_wait(lambda p: r.fa.at[d], r.fa, r.fa_s, r.fa_r)
        for j in range(n):
            r.fta[pl.ds(2 * j, 2), :] = r.fa[j]
        film_block = dot_tn_high(r.esel[...], r.fta[...])
        r.film[...] = jnp.concatenate([film_block[:film_rows, :BLK], film_block[:film_rows, 128 : 128 + BLK]], axis=1)
        embed_part = dot_nt_high(r.fta[...], r.wfp[...].astype(F32))
        for j in range(n):
            r.ep[j] = embed_part[2 * j : 2 * j + 2]
        dp_start(lambda p: r.ep.at[p], r.er, r.er_s, r.er_r)
        r.er[d] = r.ep[d]

        dp_wait(lambda p: r.ad.at[d], r.ad, r.ad_s, r.ad_r)
        total = r.ad[0]
        for j in range(1, n):
            total = total + r.ad[j]
        r.hb[h] = total
        head_start(lambda p: r.hb.at[h], r.hb, r.hb_s, r.hb_r)
        head_wait(lambda p: r.ro_src.at[p], r.ro_dst, r.ro_s, r.ro_r)

        dp_wait(lambda p: r.ep.at[p], r.er, r.er_s, r.er_r)
        r.eh[h] = r.er[...]
        head_start(lambda p: r.eh.at[h], r.eh, r.eh_s, r.eh_r)

        if inside:
            for a in range(3):
                r.second[a] = red2.last(a)

        head_wait(lambda p: r.hb.at[h], r.hb, r.hb_s, r.hb_r)
        even = r.hb[0] + r.hb[2]
        odd = r.hb[1] + r.hb[3]
        wide = jnp.concatenate(
            [even[:, :BLK], odd[:, :BLK], even[:, 128 : 128 + BLK], odd[:, 128 : 128 + BLK]], axis=1
        )
        r.gains_out[...] = wide[0:3]
        r.biases_out[...] = wide[3:13]

        head_wait(lambda p: r.eh.at[h], r.eh, r.eh_s, r.eh_r)
        pieces = []
        for j in range(n):
            piece = (r.eh[0, j] + r.eh[1, j]) + (r.eh[2, j] + r.eh[3, j])
            pieces.append(piece[:, :film_rows])
        r.embed_grad[...] = jnp.concatenate(pieces, axis=1) * silu_slope(r.emb[...].astype(F32))

        head_wait(lambda p: r.io_src.at[p], r.io_dst, r.io_s, r.io_r)

        if inside:
            tiles = unpack_four(red3.last(0))
            r.sb_src[...] = jnp.where(c == 0, tiles[2], tiles[0])
            back = rc(r.sb_src, r.sb_dst, r.sb_s.at[0], r.sb_r.at[0], sib)
            back.start()
            r.output[...] = tiles[3]
            for a in range(3):
                r.first[a] = red1.last(a)
            back.wait()
            r.attend[:, 0:128] = jnp.where(c == 0, tiles[0], tiles[1])
            r.attend[:, 128:256] = r.sb_dst[...]
            r.attend[:, 256:384] = jnp.where(c == 0, tiles[1], tiles[2])

    return kernel


def make_writer(names_in, names_out):
    def kernel(*refs):
        count = len(names_in)
        src, dst = Names(names_in, refs[:count]), Names(names_out, refs[count:])
        for name, packed in (("result", src.ro_dst), ("image_grad", src.io_dst)):
            for m in range(2):
                getattr(dst, name)[m] = dot_nt(unpack_pixels(packed[2 * m]), src.sel[0]) + dot_nt(
                    unpack_pixels(packed[2 * m + 1]), src.sel[1]
                )
        for name in ("first", "second"):
            if name in names_out:
                for a in range(3):
                    block = getattr(src, name)[a]
                    getattr(dst, name)[3 * a] = block[:48, :BLK]
                    getattr(dst, name)[3 * a + 1] = block[48:96, :BLK]
                    getattr(dst, name)[3 * a + 2] = last_tap(block)[:, :BLK]
        if "attend" in names_out:
            dst.attend[...] = jnp.concatenate([src.attend[:, j * 128 : j * 128 + BLK] for j in range(3)], axis=1)
            dst.output[...] = src.output[:, :BLK]
        for name in ("embed_grad", "film", "gains_out", "biases_out"):
            getattr(dst, name)[...] = getattr(src, name)[...]

    return kernel


def per_device(n, *args):
    (
        images,
        noise_field,
        time_steps,
        embedding,
        first_kernel,
        second_kernel,
        film_weight,
        attend_weight,
        output_weight,
        norm_gains,
        biases,
        cotangent,
    ) = args
    inside = n == 8
    keep, noise = plan(time_steps)
    coef = jnp.stack([keep, noise])
    maps, height, width, channels = images.shape
    flat_shape = (maps, height * width, channels)
    film_rows = film_weight.shape[0]
    inputs = dict(
        coef=coef,
        images=images.reshape(flat_shape),
        noise=noise_field.reshape(flat_shape),
        cot=cotangent.reshape(flat_shape),
        emb=embedding,
        k1=first_kernel.reshape((9,) + first_kernel.shape[2:]),
        k2=second_kernel.reshape((9,) + second_kernel.shape[2:]),
        wf=film_weight,
        wa=attend_weight,
        wo=output_weight,
        gains=norm_gains,
        biases=biases,
        sel=jnp.asarray(channel_lanes(), BF16),
        gmask=jnp.asarray(group_mask(), BF16),
        selp=jnp.asarray(block_lanes(3), BF16),
    )
    shapes = dict(
        ro_dst=(4, 384, 128),
        io_dst=(4, 384, 128),
        embed_grad=embedding.shape,
        first=(3, 112, 128),
        second=(3, 112, 128),
        film=film_weight.shape,
        attend=(48, 384),
        output=(48, 128),
        gains_out=norm_gains.shape,
        biases_out=biases.shape,
    )
    names_in, names_out = list(INPUTS), list(OUTPUTS)
    core = lax.axis_index("head") % 2
    if not inside:
        def whole(array, row_axis):
            array = lax.all_gather(array, "dp", axis=row_axis, tiled=True)
            return lax.all_gather(array, "head", axis=array.ndim - 1, tiled=True)

        def spread(array, count):
            taps = array.shape[0]
            array = array.reshape(taps, 4, 2, 48, 2, 2, BLK)
            array = lax.dynamic_index_in_dim(array, core, 5, keepdims=False)
            array = jnp.transpose(array, (2, 4, 1, 0, 3, 5))
            array = jnp.pad(array, ((0, 0),) * 5 + ((0, 32),))
            return array.reshape(4, 4, taps * 48, 128)

        full_a = whole(attend_weight, 0).reshape(384, 2, 3, 2, BLK)
        full_a = jnp.transpose(full_a, (2, 0, 1, 3, 4)).reshape(3, 384, 384)
        full_o = whole(output_weight, 0)[None]
        for name, last, array in (("g1", "t1", first_kernel), ("g2", "t2", second_kernel)):
            blocks = spread(whole(array, 2).reshape(9, 384, 384), 9).reshape(4, 4, 3, 3, 48, 128)
            two = blocks[:, :, :, :2].reshape(4, 4, 3, 96, 128)
            inputs[name] = jnp.transpose(jnp.pad(two, ((0, 0),) * 3 + ((0, 16), (0, 0))), (2, 0, 1, 3, 4))
            inputs[last] = blocks[:, :, :, 2].reshape(4, 4, 144, 128)
        inputs["g3"] = spread(jnp.concatenate([full_a, full_o], axis=0), 4)
        names_in += ["g1", "g2", "t1", "t2", "g3"]
        shapes["first"] = shapes["second"] = (3, 4, 4, 112, 128)
        shapes["attend"] = (1, 4, 4, 144, 128)
        del shapes["output"]
        names_out.remove("output")
    items = scratch_list(n, inside)
    smem = pl.BlockSpec(memory_space=pltpu.SMEM)
    vmem = pl.BlockSpec(memory_space=pltpu.VMEM)
    outs = pl.pallas_call(
        make_kernel(n, inside, names_in + names_out + [name for name, _ in items]),
        out_shape=[
            jax.ShapeDtypeStruct(shapes[name], BF16 if name in ("ro_dst", "io_dst") else F32) for name in names_out
        ],
        in_specs=[smem if name == "coef" else vmem for name in names_in],
        out_specs=[vmem] * len(names_out),
        scratch_shapes=[item for _, item in items],
        compiler_params=pltpu.CompilerParams(
            collective_id=0, has_side_effects=True, vmem_limit_bytes=63 * 1024 * 1024
        ),
        name="blocks",
    )(*[inputs[name] for name in names_in])
    raw = dict(zip(names_out, outs))
    final = dict(
        result=flat_shape,
        image_grad=flat_shape,
        embed_grad=embedding.shape,
        film=film_weight.shape,
        gains_out=norm_gains.shape,
        biases_out=biases.shape,
    )
    if inside:
        final.update(first=(9, 48, BLK), second=(9, 48, BLK), attend=attend_weight.shape, output=output_weight.shape)
    names_last = [name for name in names_out if inside or name not in ("first", "second", "attend")] + ["sel"]
    names_final = list(final)
    outs = pl.pallas_call(
        make_writer(names_last, names_final),
        out_shape=[jax.ShapeDtypeStruct(final[name], F32) for name in names_final],
        in_specs=[vmem] * len(names_last),
        out_specs=[vmem] * len(names_final),
        compiler_params=pltpu.CompilerParams(vmem_limit_bytes=63 * 1024 * 1024),
        name="outputs",
    )(*[inputs["sel"] if name == "sel" else raw[name] for name in names_last])
    out = dict(zip(names_final, outs))
    if not inside:

        def blocks_of(array, size):
            parts = [array[..., k * 48 : k * 48 + 48, :BLK] for k in range(size)]
            if size == 2:
                lanes = [array[..., k * 32 : k * 32 + 32, BLK:] for k in range(3)]
                lanes = jnp.concatenate(lanes, axis=-1)
                parts.append(jnp.concatenate([lanes, array[..., 96:112, :BLK]], axis=-2))
            else:
                lanes = [array[..., k * 48 : k * 48 + 48, BLK:] for k in range(3)]
                parts.append(jnp.concatenate(lanes, axis=-1))
            array = jnp.stack(parts, axis=1)
            array = array.reshape(array.shape[:2] + (2, 2, 4, 48, BLK))
            taps = array.shape[0] * array.shape[1]
            array = jnp.transpose(array, (0, 1, 4, 2, 5, 3, 6)).reshape(taps, 384, 2, 1, BLK)
            both = jnp.concatenate([array, jnp.zeros_like(array)], axis=3)
            return jnp.where(core == 0, both, both[:, :, :, ::-1]).reshape(taps, 384, 384)

        def shared(array, axis):
            array = lax.psum_scatter(array, "head", scatter_dimension=array.ndim - 1, tiled=True)
            return lax.psum_scatter(array, "dp", scatter_dimension=axis, tiled=True)

        out["first"] = shared(blocks_of(raw["first"], 2), 1)
        out["second"] = shared(blocks_of(raw["second"], 2), 1)
        both = blocks_of(raw["attend"], 3)
        joined = both[:3].reshape(3, 384, 2, 2, BLK)
        joined = jnp.transpose(joined, (1, 2, 0, 3, 4)).reshape(384, 1152)
        out["attend"] = shared(joined, 0)
        out["output"] = shared(both[3], 0)
    return (
        out["result"].reshape(images.shape),
        out["image_grad"].reshape(images.shape),
        out["embed_grad"],
        out["first"].reshape(first_kernel.shape),
        out["second"].reshape(second_kernel.shape),
        out["film"],
        out["attend"],
        out["output"],
        out["gains_out"],
        out["biases_out"],
    )


def solution(mesh):
    n = mesh.shape["dp"]
    field = P("dp", "head", None, None)
    taps = P(None, None, "dp", "head")
    both = P("dp", "head")
    return jax.shard_map(
        lambda *args: per_device(n, *args),
        mesh=mesh,
        in_specs=(field, field, P("dp"), P("dp", None), taps, taps, both, both, both, P(), P(), field),
        out_specs=(field, field, P("dp", None), taps, taps, both, both, both, P(), P()),
        check_vma=False,
    )
```

```python
import math

import jax
import jax.numpy as jnp
import numpy as np
from jax import lax
from jax.experimental import pallas as pl
from jax.experimental.pallas import tpu as pltpu
from jax.sharding import PartitionSpec as P

HEAD_DIM = 96
GROUPS = 32
STEPS = 4000
EPS = 1e-05
OFFSET = 0.008
MESH = pl.DeviceIdType.MESH
F32 = jnp.float32
BF16 = jnp.bfloat16

PX = 1024
ROW = 32
CHUNK = 256
BLK = 96
HALF = 256
NHEAD = 4


def plan(time_steps):
    fraction = (time_steps.astype(F32) + 1.0) / STEPS
    start = jnp.square(jnp.cos(jnp.float32(OFFSET / (1.0 + OFFSET) * (math.pi / 2))))
    curve = jnp.square(jnp.cos((fraction + OFFSET) / (1.0 + OFFSET) * (math.pi / 2))) / start
    return (jnp.sqrt(curve), jnp.sqrt(1.0 - curve))


def channel_lanes():
    sel = np.zeros((2, 384, HALF), np.float32)
    for block in range(4):
        for j in range(BLK):
            sel[block % 2, block * BLK + j, (block // 2) * 128 + j] = 1.0
    return sel


def block_lanes(count):
    sel = np.zeros((count * BLK, count * 128), np.float32)
    for block in range(count):
        for j in range(BLK):
            sel[block * BLK + j, block * 128 + j] = 1.0
    return sel


def group_mask():
    lane = np.arange(HALF)
    ok = lane % 128 < BLK
    group = (lane // 128) * 100 + (lane % 128) // 12
    return ((group[:, None] == group[None, :]) & ok[:, None] & ok[None, :]).astype(np.float32)


def dot(a, b):
    return lax.dot_general(a, b, (((1,), (0,)), ((), ())), preferred_element_type=F32)


def dot_nt(a, b):
    return lax.dot_general(a, b, (((1,), (1,)), ((), ())), preferred_element_type=F32)


def dot_nt_high(a, b):
    return lax.dot_general(
        a, b, (((1,), (1,)), ((), ())), preferred_element_type=F32, precision=lax.Precision.HIGHEST
    )


def dot_tn_high(a, b):
    return lax.dot_general(
        a, b, (((0,), (0,)), ((), ())), preferred_element_type=F32, precision=lax.Precision.HIGHEST
    )


def exact_dot(values, ones):
    high = values.astype(BF16).astype(F32)
    rest = values - high
    middle = rest.astype(BF16).astype(F32)
    low = rest - middle
    rows = values.shape[0]
    out = dot(jnp.concatenate([high, middle, low], axis=0).astype(BF16), ones)
    return out[:rows] + out[rows : 2 * rows] + out[2 * rows :]


def sigmoid(v):
    return 1.0 / (1.0 + jnp.exp(-v))


def silu(v):
    return v / (1.0 + jnp.exp(-v))


def silu_slope(v):
    s = sigmoid(v)
    return s * (1.0 + v * (1.0 - s))


def pack_taps(t0, t1, t2):
    t0, t1, t2 = t0[:, :BLK], t1[:, :BLK], t2[:, :BLK]
    join = lambda a, b: jnp.concatenate([a, b], axis=1)
    return jnp.concatenate(
        [
            join(t0[:32], t2[:32, :32]),
            join(t0[32:], t2[:16, 32:64]),
            join(t1[:16], t2[16:32, 32:64]),
            join(t1[16:], t2[:32, 64:]),
            join(t2[32:], jnp.zeros((16, 32), t2.dtype)),
        ],
        axis=0,
    )


def last_tap(packed):
    lanes = [packed[:32, BLK:], packed[32:64, BLK:], packed[64:96, BLK:], jnp.zeros((32, 32), packed.dtype)]
    return jnp.concatenate([jnp.concatenate(lanes, axis=1), packed[96:112]], axis=0)


def pack_four(b0, b1, b2, b3):
    return jnp.concatenate(
        [jnp.concatenate([b[:, :BLK], b3[:, 32 * k : 32 * k + 32]], axis=1) for k, b in enumerate((b0, b1, b2))],
        axis=0,
    )


def unpack_four(packed):
    size = packed.shape[0] // 3
    parts = [packed[k * size : k * size + size] for k in range(3)]
    zero = jnp.zeros((size, 32), packed.dtype)
    fourth = jnp.concatenate([p[:, BLK:] for p in parts] + [zero], axis=1)
    return [jnp.concatenate([p[:, :BLK], zero], axis=1) for p in parts] + [fourth]


def pack_pixels(full):
    half = CHUNK // 2
    return pack_four(full[:half, :128], full[half:, :128], full[:half, 128:], full[half:, 128:])


def unpack_pixels(packed):
    b0, b1, b2, b3 = unpack_four(packed)
    return jnp.concatenate([jnp.concatenate([b0, b2], axis=1), jnp.concatenate([b1, b3], axis=1)], axis=0)


INPUTS = (
    "coef",
    "images",
    "noise",
    "cot",
    "emb",
    "k1",
    "k2",
    "wf",
    "wa",
    "wo",
    "gains",
    "biases",
    "sel",
    "gmask",
    "selp",
)
OUTPUTS = (
    "ro_dst",
    "io_dst",
    "embed_grad",
    "first",
    "second",
    "film",
    "attend",
    "output",
    "gains_out",
    "biases_out",
)


class Names:
    def __init__(self, names, refs):
        for name, ref in zip(names, refs):
            setattr(self, name, ref)


def scratch_list(n, inside):
    dma = pltpu.SemaphoreType.DMA
    items = []

    def vm(name, shape, dtype):
        items.append((name, pltpu.VMEM(shape, dtype)))

    def sem(name, count):
        items.append((name + "_s", dma((count,))))
        items.append((name + "_r", dma((count,))))

    for name in ("mx", "cx", "ro", "io"):
        vm(name + "_src", (4, 384, 128), BF16)
        if name in ("mx", "cx"):
            vm(name + "_dst", (4, 384, 128), BF16)
            vm(name, (4, CHUNK, HALF), BF16)
        sem(name, 4)
    for name in ("act1", "act2"):
        vm(name, (2, PX + 2 * ROW, HALF), BF16)
        vm(name + "_t", (2, HALF, PX), BF16)
        sem(name, 2)
    vm("ai", (2, PX, HALF), BF16)
    vm("ai_t", (2, HALF, PX), BF16)
    sem("ai", 2)
    vm("att", (4, PX, 128), BF16)
    vm("att_t", (2, HALF, PX), BF16)
    sem("att", 2)
    for name in ("do", "n3", "d2", "d1"):
        vm(name + "_src", (PX, HALF), BF16)
        vm(name + "_dst", (PX, HALF), BF16)
        sem(name, 2)
    vm("v2", (PX, HALF), F32)
    vm("v3", (PX, HALF), F32)
    vm("gres", (PX, HALF), F32)
    vm("gtmp", (PX, HALF), F32)
    vm("qkv", (6, PX, 128), BF16)
    vm("kvt", (4, 128, PX), BF16)
    vm("dout", (2, PX, 128), BF16)
    vm("dproj", (6, PX, 128), BF16)
    vm("gr2", (3, PX + 2 * ROW, HALF), BF16)
    vm("gr1", (3, PX + 2 * ROW, HALF), BF16)
    vm("par", (16, 384), F32)
    vm("parown", (16, HALF), F32)
    vm("stat", (16, HALF), F32)
    vm("sums", (16, HALF), F32)
    if inside:
        vm("g1", (4, 4, 352, 128), BF16)
        vm("g2", (4, 4, 336, 128), BF16)
        vm("t1", (4, 4, 144, 128), BF16)
        vm("t2", (4, 4, 144, 128), BF16)
        vm("p3", (4, 4, 144, 128), BF16)
        vm("g3", (4, 4, 192, 128), BF16)
        for name in ("g1", "g2", "p3"):
            sem(name + "z", 4)
            sem(name + "v", 2)
            sem(name + "w", 4)
        vm("sw_src", (48, 128), BF16)
        vm("sw_dst", (48, 128), BF16)
        sem("sw", 1)
        vm("sb_src", (48, 128), F32)
        vm("sb_dst", (48, 128), F32)
        sem("sb", 1)
        for name, nc, rows in (("r1", 3, 112), ("r2", 3, 112), ("r3", 1, 144)):
            vm(name + "_acc", (nc, 4, 4, rows, 128), F32)
            vm(name + "w_src", (nc, 2, 4, rows, 128), BF16)
            vm(name + "w_dst", (nc, 2, 4, rows, 128), BF16)
            vm(name + "v_src", (nc, 4, rows, 128), BF16)
            vm(name + "v_dst", (nc, 4, rows, 128), BF16)
            vm(name + "z_src", (4, nc, rows, 128), BF16)
            vm(name + "z_dst", (4, nc, rows, 128), BF16)
            sem(name + "w", nc)
            sem(name + "v", nc)
            sem(name + "z", nc * 4)
    if not inside:
        vm("el", (n, 2, 768), F32)
        sem("el", n)
    vm("em", (2 * n, 768), F32)
    vm("wfp", (128, HALF), BF16)
    vm("esel", (2 * n, 128), F32)
    vm("fp", (n, 2, HALF), F32)
    vm("fr", (n, 2, HALF), F32)
    sem("fr", n)
    vm("fx", (4, 1, 128), F32)
    vm("fh", (4, 1, 128), F32)
    sem("fh", 4)
    vm("ft", (4, 1, 128), F32)
    vm("th", (4, 1, 128), F32)
    sem("th", 4)
    vm("fa", (n, 2, HALF), F32)
    sem("fa", n)
    vm("fta", (2 * n, HALF), F32)
    vm("ep", (n, 2, 128), F32)
    vm("er", (n, 2, 128), F32)
    sem("er", n)
    vm("eh", (4, n, 2, 128), F32)
    sem("eh", 4)
    vm("ad", (n, 16, HALF), F32)
    sem("ad", n)
    vm("hb", (4, 16, HALF), F32)
    sem("hb", 4)
    return items


def make_kernel(n, inside, names):
    film_rows = 768 // n

    def kernel(*refs):
        r = Names(names, refs)
        d = lax.axis_index("dp")
        h = lax.axis_index("head")
        x = h // 2
        c = h - 2 * x
        z = d // 2
        y = d - 2 * z
        sib = (d, h + 1 - 2 * c)
        xdev = (d, h + 2 - 4 * x)
        v = x + c * (y - x)
        w = y + c * (x - y)
        vdev = (d + c * (1 - 2 * y), h + (1 - c) * (2 - 4 * x))
        wdev = (d + (1 - c) * (1 - 2 * y), h + c * (2 - 4 * x))

        def slot(xx, yy):
            if inside:
                return (yy + c * (xx - yy)) * 2 + xx + c * (yy - xx)
            return yy * 2 + xx

        def rc(src, dst, send, recv, dev):
            return pltpu.make_async_remote_copy(
                src_ref=src, dst_ref=dst, send_sem=send, recv_sem=recv, device_id=dev, device_id_type=MESH
            )

        def loop(count, body):
            def step(i, carry):
                body(i)
                return carry

            lax.fori_loop(0, count, step, 0)

        def rows(i, size=CHUNK, base=0):
            return pl.ds(pl.multiple_of(base + i * size, 32), size)

        def dp_start(src_of, dst, send, recv):
            def step(k, carry):
                peer = lax.rem(d + k, n)
                rc(src_of(peer), dst.at[d], send.at[k], recv.at[d], (peer, h)).start()
                return carry

            lax.fori_loop(1, n, step, 0)

        def dp_wait(src_of, dst, send, recv):
            def step(k, carry):
                peer = lax.rem(d + k, n)
                copy = rc(src_of(peer), dst.at[peer], send.at[k], recv.at[peer], (peer, h))
                copy.wait_recv()
                copy.wait_send()
                return carry

            lax.fori_loop(1, n, step, 0)

        def head_start(src_of, dst, send, recv):
            for k in range(1, 4):
                peer = lax.rem(h + k, 4)
                rc(src_of(peer), dst.at[h], send.at[k], recv.at[h], (d, peer)).start()

        def head_wait(src_of, dst, send, recv):
            for k in range(1, 4):
                peer = lax.rem(h + k, 4)
                copy = rc(src_of(peer), dst.at[peer], send.at[k], recv.at[peer], (d, peer))
                copy.wait_recv()
                copy.wait_send()

        class Halves:
            def __init__(self, name, base):
                self.buf, self.base = getattr(r, name), base
                self.send, self.recv = getattr(r, name + "_s"), getattr(r, name + "_r")

            def at(self, core, i):
                return self.buf.at[core, rows(i, 2 * CHUNK, self.base)]

            def start(self, i):
                ref = self.at(c, i)
                rc(ref, ref, self.send.at[i], self.recv.at[i], sib).start()

            def fill(self, make):
                def body(i):
                    for j in range(2):
                        at = 2 * i + j
                        self.buf[c, rows(at, CHUNK, self.base), :] = make(at)
                    self.start(i)

                loop(2, body)

            def wait(self):
                for i in range(2):
                    ref = self.at(1 - c, i)
                    copy = rc(ref, ref, self.send.at[i], self.recv.at[i], sib)
                    copy.wait_recv()
                    copy.wait_send()

        class Parts:
            def __init__(self, name):
                self.src, self.dst = getattr(r, name + "_src"), getattr(r, name + "_dst")
                self.send, self.recv = getattr(r, name + "_s"), getattr(r, name + "_r")

            def copy(self, i):
                at = rows(i, 2 * CHUNK)
                return rc(self.src.at[at], self.dst.at[at], self.send.at[i], self.recv.at[i], sib)

            def fill(self, make):
                def body(i):
                    self.src[rows(i, 2 * CHUNK), :] = make(i).astype(BF16)
                    self.copy(i).start()

                loop(2, body)

            def get(self, i):
                copy = self.copy(i)
                copy.wait_recv()
                copy.wait_send()
                return self.dst[rows(i, 2 * CHUNK), :].astype(F32)

        class Gather:
            def __init__(self, name):
                self.g = getattr(r, name)
                self.zs, self.zr = getattr(r, name + "z_s"), getattr(r, name + "z_r")
                self.vs, self.vr = getattr(r, name + "v_s"), getattr(r, name + "v_r")
                self.ws, self.wr = getattr(r, name + "w_s"), getattr(r, name + "w_r")

            def zcopy(self, k):
                peer = (lax.rem(z + k, 4) * 2 + y, h)
                return rc(
                    self.g.at[w * 2 + v, 0], self.g.at[w * 2 + v, 4 - k], self.zs.at[k], self.zr.at[4 - k], peer
                )

            def vcopy(self, vv, i):
                ref = self.g.at[w * 2 + vv, pl.ds(i, 1 + 2 * i)]
                return rc(ref, ref, self.vs.at[i], self.vr.at[i], vdev)

            def wcopy(self, ww, other, i):
                ref = self.g.at[ww * 2 + v + other * (1 - 2 * v), pl.ds(i, 1 + 2 * i)]
                return rc(ref, ref, self.ws.at[2 * i + other], self.wr.at[2 * i + other], wdev)

            def own(self):
                for k in range(1, 4):
                    self.zcopy(k).start()
                self.vcopy(v, 0).start()
                self.wcopy(w, 0, 0).start()

            def pass_z(self):
                self.vcopy(1 - v, 0).wait_recv()
                self.wcopy(w, 1, 0).start()
                for k in range(1, 4):
                    self.zcopy(k).wait_recv()
                self.vcopy(v, 1).start()
                self.wcopy(w, 0, 1).start()

            def pass_v(self):
                self.vcopy(1 - v, 1).wait_recv()
                self.wcopy(w, 1, 1).start()

            def done(self):
                for k in range(1, 4):
                    self.zcopy(k).wait_send()
                for i in range(2):
                    self.vcopy(v, i).wait_send()
                    for other in range(2):
                        self.wcopy(1 - w, other, i).wait_recv()
                        self.wcopy(w, other, i).wait_send()

        class Reduce:
            def __init__(self, name, count):
                get = lambda tail: getattr(r, name + tail)
                self.acc, self.count = get("_acc"), count
                self.wsrc, self.wdst, self.ws, self.wr = get("w_src"), get("w_dst"), get("w_s"), get("w_r")
                self.vsrc, self.vdst, self.vs, self.vr = get("v_src"), get("v_dst"), get("v_s"), get("v_r")
                self.zsrc, self.zdst, self.zs, self.zr = get("z_src"), get("z_dst"), get("z_s"), get("z_r")

            def wcopy(self, a):
                return rc(self.wsrc.at[a], self.wdst.at[a], self.ws.at[a], self.wr.at[a], wdev)

            def vcopy(self, a, size):
                at = pl.ds(a, size)
                return rc(self.vsrc.at[at], self.vdst.at[at], self.vs.at[a], self.vr.at[a], vdev)

            def zcopy(self, a, size, k):
                at = pl.ds(a, size)
                return rc(
                    self.zsrc.at[k, at],
                    self.zdst.at[4 - k, at],
                    self.zs.at[a * 4 + k],
                    self.zr.at[a * 4 + 4 - k],
                    (lax.rem(z + k, 4) * 2 + y, h),
                )

            def start(self, a):
                def step(i, carry):
                    vv, zz = i // 4, lax.rem(i, 4)
                    self.wsrc[a, vv, zz] = self.acc[a, (1 - w) * 2 + vv, zz].astype(BF16)
                    return carry

                lax.fori_loop(0, 8, step, 0)
                self.wcopy(a).start()

            def second(self, first, size):
                for a in range(first, first + size):
                    self.wcopy(a).wait_recv()

                    def step(zz, carry):
                        self.vsrc[a, zz] = (
                            self.acc[a, w * 2 + 1 - v, zz] + self.wdst[a, 1 - v, zz].astype(F32)
                        ).astype(BF16)
                        return carry

                    lax.fori_loop(0, 4, step, 0)
                self.vcopy(first, size).start()

            def third(self, first, size):
                self.vcopy(first, size).wait_recv()
                for a in range(first, first + size):

                    def step(k, carry):
                        zz = lax.rem(z + k, 4)
                        total = (
                            self.acc[a, w * 2 + v, zz]
                            + self.wdst[a, v, zz].astype(F32)
                            + self.vdst[a, zz].astype(F32)
                        )
                        self.acc[a, w * 2 + v, zz] = total
                        self.zsrc[k, a] = total.astype(BF16)
                        return carry

                    lax.fori_loop(0, 4, step, 0)
                for k in range(1, 4):
                    self.zcopy(first, size, k).start()

            def finish(self, groups):
                for first, size in groups:
                    self.vcopy(first, size).wait_send()
                    for k in range(1, 4):
                        copy = self.zcopy(first, size, k)
                        copy.wait_recv()
                        copy.wait_send()
                for a in range(self.count):
                    self.wcopy(a).wait_send()

            def last(self, a):
                total = self.acc[a, w * 2 + v, z]
                for k in range(1, 4):
                    total = total + self.zdst[k, a].astype(F32)
                return total

        def rel(zc):
            return lax.rem(zc - z + 4, 4) if inside else zc

        class Taps:
            def __init__(self, packed, last):
                self.packed, self.last = packed, last

            def block(self, tap, zc, xx, yy):
                a, b = tap // 3, tap % 3
                if b < 2:
                    return self.packed[slot(xx, yy), rel(zc), pl.ds(a * 112 + b * 48, 48), :]
                return self.last[slot(xx, yy), rel(zc), pl.ds(a * 48, 48), :]

            def unpack(self):
                def step(i, carry):
                    q, zz = i // 4, lax.rem(i, 4)
                    for a in range(3):
                        self.last[q, zz, pl.ds(a * 48, 48), :] = last_tap(
                            self.packed[q, zz, pl.ds(a * 112, 112), :]
                        )
                    return carry

                lax.fori_loop(0, 16, step, 0)

        class Plain:
            def __init__(self, blocks):
                self.blocks = blocks

            def block(self, tap, zc, xx, yy):
                return self.blocks[slot(xx, yy), rel(zc), pl.ds(tap * 48, 48), :]

            def unpack(self):
                def step(i, carry):
                    q, zz = i // 4, lax.rem(i, 4)
                    self.blocks[q, zz] = jnp.concatenate(unpack_four(r.p3[q, zz]), axis=0)
                    return carry

                lax.fori_loop(0, 16, step, 0)

        k1, k2, k3 = Taps(r.g1, r.t1), Taps(r.g2, r.t2), Plain(r.g3)

        def wtile(g, tap, zc, xx):
            return jnp.concatenate(
                [g.block(tap, zc, xx, 0), g.block(tap, zc, xx, 1), jnp.zeros((32, 128), BF16)], axis=0
            )

        def wtap(g, tap, zcs):
            return jnp.concatenate(
                [jnp.concatenate([wtile(g, tap, zc, xx) for xx in range(2)], axis=1) for zc in zcs], axis=0
            )

        ALL = (0, 2, 1, 3)

        def half_of(core):
            return (core, core + 2)

        def wproj(zcs):
            return jnp.concatenate(
                [
                    jnp.concatenate([wtile(k3, j, zc, xx) for xx in range(2) for j in range(3)], axis=1)
                    for zc in zcs
                ],
                axis=0,
            )

        def flat(buf, base, i, size):
            return jnp.concatenate([buf[0, rows(i, size, base), :], buf[1, rows(i, size, base), :]], axis=1)

        barrier = pltpu.get_barrier_semaphore()

        def greet(k, carry):
            pl.semaphore_signal(barrier, inc=1, device_id=(lax.rem(d + k, n), h), device_id_type=MESH)
            return carry

        lax.fori_loop(1, n, greet, 0)
        for k in range(1, 4):
            pl.semaphore_signal(barrier, inc=1, device_id=(d, lax.rem(h + k, 4)), device_id_type=MESH)
        if inside:
            for a in range(3):
                r.g1[w * 2 + v, 0, pl.ds(a * 112, 112), :] = pack_taps(*[r.k1[3 * a + b] for b in range(3)])
            emb_low = silu(r.emb[...].astype(F32))
            emb_rows = [emb_low[m : m + 1, 128 * j : 128 * j + 128] for m in range(2) for j in range(6)]
            emb_rows.append(jnp.zeros((4, 128), F32))
            r.g1[w * 2 + v, 0, pl.ds(336, 16), :] = jnp.concatenate(emb_rows, axis=0).astype(BF16)
        pl.semaphore_wait(barrier, n - 1 + 3)
        if inside:
            ga, gb, gc = Gather("g1"), Gather("g2"), Gather("p3")
            ga.own()

        def mix(m, carry):
            field = r.coef[0, m] * r.images[m].astype(F32) + r.coef[1, m] * r.noise[m].astype(F32)
            low = field.astype(BF16)
            for core in range(2):
                r.mx_src[m * 2 + core] = pack_pixels(dot(low, r.sel[core])).astype(BF16)
            return carry

        lax.fori_loop(0, 2, mix, 0)
        head_start(lambda p: r.mx_src.at[p], r.mx_dst, r.mx_s, r.mx_r)
        r.mx_dst[h] = r.mx_src[h]

        if not inside:
            r.el[d] = silu(r.emb[...].astype(F32)).astype(BF16).astype(F32)
            dp_start(lambda p: r.el.at[d], r.el, r.el_s, r.el_r)

        if inside:
            blocks = dot(r.wa[...], r.selp[: 3 * BLK, : 3 * 128]).astype(BF16)
            r.sw_src[...] = blocks[:, 128:256]
            swap = rc(r.sw_src, r.sw_dst, r.sw_s.at[0], r.sw_r.at[0], sib)
            swap.start()
            for a in range(3):
                r.g2[w * 2 + v, 0, pl.ds(a * 112, 112), :] = pack_taps(*[r.k2[3 * a + b] for b in range(3)])
        r.par[0:3, :] = r.gains[...]
        r.par[3:13, :] = r.biases[...]
        r.par[13:16, :] = jnp.zeros((3, 384), F32)
        r.parown[...] = exact_dot(r.par[...], r.sel[c])

        def prow(i):
            return r.parown[pl.ds(i, 1), :]

        for buf in (r.act1, r.act2):
            for core in range(2):
                buf[core, pl.ds(0, ROW), :] = jnp.zeros((ROW, HALF), BF16)
                buf[core, pl.ds(PX + ROW, ROW), :] = jnp.zeros((ROW, HALF), BF16)
        for buf in (r.gr1, r.gr2):
            for b in range(3):
                buf[b, pl.ds(0, ROW), :] = jnp.zeros((ROW, HALF), BF16)
                buf[b, pl.ds(PX + ROW, ROW), :] = jnp.zeros((ROW, HALF), BF16)
        r.wfp[...] = jnp.zeros((128, HALF), BF16)
        r.wfp[pl.ds(0, film_rows), :] = dot(r.wf[...], r.selp[: 2 * BLK, :HALF]).astype(BF16)
        if inside:
            ga.pass_z()
            gb.own()

        count = float(PX * 12)

        def fold(vals):
            return jnp.sum(vals.reshape(CHUNK // 8, 8, HALF), axis=0)

        def sums_of(fn, k):
            def step(i, carry):
                return tuple(a + fold(b) for a, b in zip(carry, fn(i)))

            zero = jnp.zeros((8, HALF), F32)
            return lax.fori_loop(0, 4, step, (zero,) * k)

        def group_mean(part):
            return jnp.sum(exact_dot(part, r.gmask[...]), axis=0, keepdims=True) / count

        def norm(load, which, total):
            mean = group_mean(total)
            (square,) = sums_of(lambda i: (jnp.square(load(i) - mean),), 1)
            inv = lax.rsqrt(group_mean(square) + EPS)
            r.stat[pl.ds(2 * which, 1), :] = mean
            r.stat[pl.ds(2 * which + 1, 1), :] = inv
            return mean, inv

        zero8 = jnp.zeros((8, HALF), F32)

        def norm_back(sums, load_grad, load_hat, coef, inv):
            plain, cross = sums
            plain_mean, cross_mean = group_mean(coef * plain), group_mean(coef * cross)

            def chunk(i):
                return inv * (coef * load_grad(i) - plain_mean - load_hat(i) * cross_mean)

            return (
                jnp.sum(plain, axis=0, keepdims=True),
                jnp.sum(cross, axis=0, keepdims=True),
                chunk,
            )

        head_wait(lambda p: r.mx_src.at[p], r.mx_dst, r.mx_s, r.mx_r)

        def unpack_mixed(i, carry):
            vals = unpack_pixels(r.mx_dst[i])
            r.mx[i] = vals
            return carry + fold(vals.astype(F32))

        mixed_sum = lax.fori_loop(0, 4, unpack_mixed, zero8)

        def mixed(i):
            return r.mx[i].astype(F32)

        mean1, inv1 = norm(mixed, 0, mixed_sum)
        gain1, shift1 = prow(0), prow(3)
        act1 = Halves("act1", ROW)

        def pre1(i):
            return (mixed(i) - mean1) * inv1 * gain1 + shift1

        act1.fill(lambda i: silu(pre1(i)).astype(BF16))
        if inside:
            ga.pass_v()

        if inside:
            swap.wait()
            got = r.sw_dst[...]
            keep0, keep2 = blocks[:, :128], blocks[:, 256:]
            r.p3[w * 2 + v, 0] = pack_four(
                jnp.where(c == 0, keep0, got),
                jnp.where(c == 0, keep2, keep0),
                jnp.where(c == 0, got, keep2),
                r.wo[...],
            )
            gb.pass_z()
            gc.own()
        def split_cot(m, carry):
            for core in range(2):
                r.cx_src[m * 2 + core] = pack_pixels(dot(r.cot[m], r.sel[core])).astype(BF16)
            return carry

        lax.fori_loop(0, 2, split_cot, 0)
        head_start(lambda p: r.cx_src.at[p], r.cx_dst, r.cx_s, r.cx_r)
        r.cx_dst[h] = r.cx_src[h]

        column = lax.broadcasted_iota(jnp.int32, (1, ROW, HALF), 1)
        not_first = jnp.where(column > 0, 1.0, 0.0)
        not_last = jnp.where(column < ROW - 1, 1.0, 0.0)

        def in_rows(vals, mask):
            return (vals.reshape(CHUNK // ROW, ROW, HALF) * mask).reshape(CHUNK, HALF)

        def from_left(vals):
            return in_rows(pltpu.roll(vals, 1, 0), not_first)

        def from_right(vals):
            return in_rows(pltpu.roll(vals, CHUNK - 1, 0), not_last)

        def transpose_act(buf, base, out):
            for core in range(2):
                for q in range(4):
                    out[core, :, pl.ds(q * CHUNK, CHUNK)] = jnp.transpose(
                        buf[core, pl.ds(base + q * CHUNK, CHUNK), :]
                    )

        def conv(buf, g, store, between):
            weights = lambda: jnp.concatenate(
                [jnp.concatenate([wtap(g, 3 * a + b, ALL) for b in range(3)], axis=1) for a in range(3)], axis=0
            )

            total = zero8
            for i in range(2):
                left = jnp.concatenate([flat(buf, ROW * a, i, 2 * CHUNK) for a in range(3)], axis=1)
                out = dot(left, weights())
                for j in range(2):
                    part = out[j * CHUNK : j * CHUNK + CHUNK]
                    part = part[:, HALF : 2 * HALF] + from_left(part[:, :HALF]) + from_right(part[:, 2 * HALF :])
                    total = total + fold(store(2 * i + j, part))
                if i == 0:
                    between()
            return total

        act1.wait()
        transpose_act(r.act1, ROW, r.act1_t)
        if inside:
            ga.done()
            k1.unpack()

        if inside:
            for zz in range(4):
                for yy in range(2):
                    part = r.g1[slot(0, yy), rel(zz), pl.ds(336, 16), :].astype(F32)
                    for m in range(2):
                        for j in range(6):
                            row = m * 6 + j
                            r.em[2 * (2 * zz + yy) + m : 2 * (2 * zz + yy) + m + 1, 128 * j : 128 * j + 128] = part[
                                row : row + 1
                            ]
        else:
            dp_wait(lambda p: r.el.at[d], r.el, r.el_s, r.el_r)
            for j in range(n):
                r.em[pl.ds(2 * j, 2), :] = r.el[j]
        place = lax.broadcasted_iota(jnp.int32, (768, 128), 0) - film_rows * d
        lane = lax.broadcasted_iota(jnp.int32, (768, 128), 1)
        pick = jnp.where((place == lane) & (lane < film_rows), 1.0, 0.0).astype(BF16)
        r.esel[...] = dot(r.em[...].astype(BF16), pick)
        film_part = dot(r.esel[...].astype(BF16), r.wfp[...])
        for j in range(n):
            r.fp[j] = film_part[2 * j : 2 * j + 2]
        dp_start(lambda p: r.fp.at[p], r.fr, r.fr_s, r.fr_r)
        r.fr[d] = r.fp[d]
        def store_v2(i, vals):
            vals = vals + prow(6)
            r.v2[rows(i), :] = vals
            return vals

        v2_sum = conv(r.act1, k1, store_v2, gb.pass_v if inside else lambda: None)
        dp_wait(lambda p: r.fp.at[p], r.fr, r.fr_s, r.fr_r)
        film_sum = r.fr[0]
        for j in range(1, n):
            film_sum = film_sum + r.fr[j]
        for m in range(2):
            for core in range(2):
                r.fx[m * 2 + core] = film_sum[m : m + 1, core * 128 : core * 128 + 128]
        head_start(lambda p: r.fx.at[p], r.fh, r.fh_s, r.fh_r)
        r.fh[h] = r.fx[h]

        head_wait(lambda p: r.fx.at[p], r.fh, r.fh_s, r.fh_r)
        scale = 1.0 + (jnp.concatenate([r.fh[0], r.fh[1]], axis=1) + prow(8))
        shift = jnp.concatenate([r.fh[2], r.fh[3]], axis=1) + prow(9)
        mean2, inv2 = norm(lambda i: r.v2[rows(i), :], 1, v2_sum)
        gain2, shift2 = prow(1), prow(4)
        act2 = Halves("act2", ROW)

        def hat2(i):
            return (r.v2[rows(i), :] - mean2) * inv2

        def pre2(i):
            return (hat2(i) * gain2 + shift2) * scale + shift

        act2.fill(lambda i: silu(pre2(i)).astype(BF16))
        if inside:
            gc.pass_z()

        act2.wait()
        transpose_act(r.act2, ROW, r.act2_t)
        if inside:
            gb.done()
            k2.unpack()

        def store_v3(i, vals):
            vals = mixed(i) + (vals + prow(7))
            r.v3[rows(i), :] = vals
            return vals

        v3_sum = conv(r.act2, k2, store_v3, gc.pass_v if inside else lambda: None)
        mean3, inv3 = norm(lambda i: r.v3[rows(i), :], 2, v3_sum)
        gain3, shift3 = prow(2), prow(5)
        ai = Halves("ai", 0)

        def hat3(i):
            return (r.v3[rows(i), :] - mean3) * inv3

        ai.fill(lambda i: (hat3(i) * gain3 + shift3).astype(BF16))

        if inside:
            gc.done()
            k3.unpack()
        head_wait(lambda p: r.cx_src.at[p], r.cx_dst, r.cx_s, r.cx_r)

        def unpack_cot(i):
            r.cx[i] = unpack_pixels(r.cx_dst[i])

        loop(4, unpack_cot)
        dop = Parts("do")

        def cot_rows(i):
            return jnp.concatenate([r.cx[2 * i], r.cx[2 * i + 1]], axis=0)

        dop.fill(lambda i: dot_nt(cot_rows(i), wtap(k3, 3, half_of(1 - c))))

        ai.wait()
        bias_proj = [prow(10)[:, :128], prow(10)[:, 128:], None, None, prow(11)[:, :128], prow(11)[:, 128:]]

        def project(i):
            out = dot(flat(r.ai, 0, i, 2 * CHUNK), wproj(ALL))
            for k in range(6):
                part = out[:, k * 128 : k * 128 + 128]
                if bias_proj[k] is not None:
                    part = part + bias_proj[k]
                r.qkv[k, rows(i, 2 * CHUNK), :] = part.astype(BF16)

        loop(2, project)

        def do_own(i):
            full = (dot_nt(cot_rows(i), wtap(k3, 3, half_of(c))) + dop.get(i)).astype(BF16)
            for k in range(2):
                r.dout[k, rows(i, 2 * CHUNK), :] = full[:, k * 128 : k * 128 + 128]

        loop(2, do_own)

        factor = 1.0 / math.sqrt(HEAD_DIM)
        factor2 = factor * math.log2(math.e)
        att = []

        def transposes(k):
            r.kvt[k] = jnp.transpose(r.qkv[k + 2])

        loop(4, transposes)

        def att_copies(core):
            for i, ref in enumerate((r.att.at[pl.ds(core * 2, 2)], r.att_t.at[core])):
                yield rc(ref, ref, r.att_s.at[i], r.att_r.at[i], sib)

        def one_head(k):
            lows, grads = [], []
            for b in range(2):
                at = pl.ds(b * 2 * CHUNK, 2 * CHUNK)
                query = r.qkv[k, at, :]
                grad = r.dout[k, at, :]
                scores = dot_nt(r.qkv[2 + k], query)
                peak = jnp.max(scores, axis=0, keepdims=True)
                expo = jnp.exp2((scores - peak) * factor2)
                inverse = 1.0 / jnp.sum(expo, axis=0, keepdims=True)
                low = (expo * inverse).astype(BF16)
                got = dot(r.kvt[2 + k], low)
                got_low = got.astype(BF16)
                r.att_t[c, pl.ds(pl.multiple_of(k * 128, 128), 128), at] = got_low
                r.att[2 * c + k, at, :] = jnp.transpose(got_low)
                spread = jnp.sum(got * jnp.transpose(grad).astype(F32), axis=0, keepdims=True)
                probs_grad = dot_nt(r.qkv[4 + k], grad)
                scores_grad = ((probs_grad - spread) * inverse * expo).astype(BF16)
                back = dot(r.kvt[k], scores_grad)
                r.dproj[k, at, :] = (jnp.transpose(back) * factor).astype(BF16)
                lows.append(low)
                grads.append(scores_grad)
            r.dproj[4 + k] = dot(jnp.concatenate(lows, axis=1), r.dout[k]).astype(BF16)
            r.dproj[2 + k] = (dot(jnp.concatenate(grads, axis=1), r.qkv[k]) * factor).astype(BF16)

        loop(2, one_head)
        for copy in att_copies(c):
            copy.start()

        n3 = Parts("n3")

        def proj_rows(i):
            return jnp.concatenate([r.dproj[k, rows(i, 2 * CHUNK), :] for k in range(6)], axis=1)

        n3.fill(lambda i: dot_nt(proj_rows(i), wproj(half_of(1 - c))))

        for copy in att_copies(1 - c):
            copy.wait_recv()
            copy.wait_send()

        def result(i):
            left = jnp.concatenate([r.att[p, rows(i), :] for p in range(4)], axis=1)
            branch = dot(left, wtap(k3, 3, ALL)) + prow(12)
            r.ro_src[i] = pack_pixels(r.v3[rows(i), :] + branch).astype(BF16)

        loop(4, result)
        head_start(lambda p: r.ro_src.at[p], r.ro_dst, r.ro_s, r.ro_r)
        r.ro_dst[h] = r.ro_src[h]

        if inside:
            red1, red2, red3 = Reduce("r1", 3), Reduce("r2", 3), Reduce("r3", 1)
            acc1, acc2, acc3 = r.r1_acc, r.r2_acc, r.r3_acc
        else:
            acc1, acc2, acc3 = r.first, r.second, r.attend

        transpose_act(r.ai, 0, r.ai_t)
        right = jnp.concatenate([r.dproj[k] for k in range(6)], axis=1)
        cot_all = jnp.concatenate([r.cx[i] for i in range(4)], axis=0)
        for core in range(2):
            attend_out = dot(r.ai_t[core], right)
            output_out = dot(r.att_t[core], cot_all)
            for k in range(2):
                for yy in range(2):
                    for xx in range(2):
                        row = k * 128 + yy * 48
                        tiles = [
                            attend_out[row : row + 48, (xx * 3 + j) * 128 : (xx * 3 + j) * 128 + 128] for j in range(3)
                        ]
                        acc3[0, slot(xx, yy), core + 2 * k] = pack_four(
                            *tiles, output_out[row : row + 48, xx * 128 : xx * 128 + 128]
                        )
        if inside:
            red3.start(0)

        def proj_sums(i, carry):
            q = jnp.concatenate([r.dproj[0, rows(i), :], r.dproj[1, rows(i), :]], axis=1).astype(F32)
            val = jnp.concatenate([r.dproj[4, rows(i), :], r.dproj[5, rows(i), :]], axis=1).astype(F32)
            return (carry[0] + fold(q), carry[1] + fold(val), carry[2] + fold(r.cx[i].astype(F32)))

        qsum, vsum, csum = lax.fori_loop(0, 4, proj_sums, (zero8, zero8, zero8))
        r.sums[pl.ds(3 + 7, 1), :] = jnp.sum(qsum, axis=0, keepdims=True)
        r.sums[pl.ds(3 + 8, 1), :] = jnp.sum(vsum, axis=0, keepdims=True)
        r.sums[pl.ds(3 + 9, 1), :] = jnp.sum(csum, axis=0, keepdims=True)
        r.sums[pl.ds(13, 3), :] = jnp.zeros((3, HALF), F32)

        def n3_own(i, carry):
            both = dot_nt(proj_rows(i), wproj(half_of(c))) + n3.get(i)
            for j in range(2):
                vals = both[j * CHUNK : j * CHUNK + CHUNK]
                r.gtmp[rows(2 * i + j), :] = vals
                carry = carry[0] + fold(vals), carry[1] + fold(vals * hat3(2 * i + j))
            return carry

        sums3 = lax.fori_loop(0, 2, n3_own, (zero8, zero8))
        plain3, cross3, back3 = norm_back(sums3, lambda i: r.gtmp[rows(i), :], hat3, gain3, inv3)
        r.sums[pl.ds(2, 1), :] = cross3
        r.sums[pl.ds(3 + 2, 1), :] = plain3

        def shifted(buf, i, vals):
            buf[0, rows(i, CHUNK, ROW), :] = from_right(vals).astype(BF16)
            buf[1, rows(i, CHUNK, ROW), :] = vals.astype(BF16)
            buf[2, rows(i, CHUNK, ROW), :] = from_left(vals).astype(BF16)

        def residual_back(i, carry):
            vals = r.cx[i].astype(F32) + back3(i)
            r.gres[rows(i), :] = vals
            shifted(r.gr2, i, vals)
            return carry + fold(vals.astype(BF16).astype(F32))

        bias_two = lax.fori_loop(0, 4, residual_back, jnp.zeros((8, HALF), F32))
        r.sums[pl.ds(3 + 4, 1), :] = jnp.sum(bias_two, axis=0, keepdims=True)

        def act_back(buf, g, core, i, size):
            left = jnp.concatenate(
                [buf[b, rows(i, size, 2 * ROW - ROW * a), :] for a in range(3) for b in range(3)], axis=1
            )
            right = jnp.concatenate(
                [wtap(g, 3 * a + b, half_of(core)) for a in range(3) for b in range(3)], axis=1
            )
            return dot_nt(left, right)

        def conv_back(parts, buf, g):
            parts.fill(lambda i: act_back(buf, g, 1 - c, i, 2 * CHUNK))

        def conv_back_own(parts, buf, g, outer, hat):
            def own(i, carry):
                vals = act_back(buf, g, c, i, 2 * CHUNK) + parts.get(i)
                for j in range(2):
                    at = 2 * i + j
                    grad = vals[j * CHUNK : j * CHUNK + CHUNK] * outer(at)
                    r.gtmp[rows(at), :] = grad
                    carry = carry[0] + fold(grad), carry[1] + fold(grad * hat(at))
                return carry

            return lax.fori_loop(0, 2, own, (zero8, zero8))

        def kernel_grad(act_t, buf, acc, after):
            def step(a, carry):
                right = jnp.concatenate(
                    [buf[b, pl.ds(pl.multiple_of(2 * ROW - ROW * a, 32), PX), :] for b in range(3)], axis=1
                )
                out = dot(jnp.concatenate([act_t[0], act_t[1]], axis=0), right)
                for p, zc in enumerate(ALL):
                    for yy in range(2):
                        for xx in range(2):
                            row = p * 128 + yy * 48
                            tiles = [
                                out[row : row + 48, b * HALF + xx * 128 : b * HALF + xx * 128 + 128] for b in range(3)
                            ]
                            acc[a, slot(xx, yy), zc] = pack_taps(*tiles)
                after(a)
                return carry

            lax.fori_loop(0, 3, step, 0)

        d2 = Parts("d2")
        conv_back(d2, r.gr2, k2)
        kernel_grad(r.act2_t, r.gr2, acc2, red2.start if inside else lambda a: None)

        sums2 = conv_back_own(d2, r.gr2, k2, lambda i: silu_slope(pre2(i)), hat2)
        if inside:
            red3.second(0, 1)

        plain2, cross2, back2 = norm_back(sums2, lambda i: r.gtmp[rows(i), :], hat2, gain2 * scale, inv2)
        r.sums[pl.ds(1, 1), :] = scale * cross2
        r.sums[pl.ds(3 + 1, 1), :] = scale * plain2
        film_scale_term = gain2 * cross2 + shift2 * plain2
        r.sums[pl.ds(3 + 5, 1), :] = film_scale_term
        r.sums[pl.ds(3 + 6, 1), :] = plain2
        for j in range(2):
            r.ft[j] = film_scale_term[:, j * 128 : j * 128 + 128]
            r.ft[2 + j] = plain2[:, j * 128 : j * 128 + 128]
        head_start(lambda p: r.ft.at[p], r.th, r.th_s, r.th_r)
        r.th[h] = r.ft[h]

        def first_back(i, carry):
            vals = back2(i)
            shifted(r.gr1, i, vals)
            return carry + fold(vals.astype(BF16).astype(F32))

        bias_one = lax.fori_loop(0, 4, first_back, jnp.zeros((8, HALF), F32))
        r.sums[pl.ds(3 + 3, 1), :] = jnp.sum(bias_one, axis=0, keepdims=True)

        d1 = Parts("d1")
        kernel_grad(r.act1_t, r.gr1, acc1, red1.start if inside else lambda a: None)
        if inside:
            red2.second(0, 3)
            red3.third(0, 1)
        conv_back(d1, r.gr1, k1)

        head_wait(lambda p: r.ft.at[p], r.th, r.th_s, r.th_r)
        for m in range(2):
            r.fa[d, pl.ds(m, 1), :] = jnp.concatenate([r.th[2 * m], r.th[2 * m + 1]], axis=1)
        dp_start(lambda p: r.fa.at[d], r.fa, r.fa_s, r.fa_r)

        def hat1(i):
            return (mixed(i) - mean1) * inv1

        if inside:
            red1.second(0, 2)
            red2.third(0, 3)
        sums1 = conv_back_own(d1, r.gr1, k1, lambda i: silu_slope(pre1(i)), hat1)
        if inside:
            red1.second(2, 1)
            red1.third(0, 2)

        plain1, cross1, back1 = norm_back(sums1, lambda i: r.gtmp[rows(i), :], hat1, gain1, inv1)
        r.sums[pl.ds(0, 1), :] = cross1
        r.sums[pl.ds(3, 1), :] = plain1
        r.ad[d] = r.sums[...]
        dp_start(lambda p: r.ad.at[d], r.ad, r.ad_s, r.ad_r)

        keep = r.coef[0, x]

        def image_back(i):
            r.io_src[i] = pack_pixels(keep * (r.gres[rows(i), :] + back1(i))).astype(BF16)

        loop(4, image_back)
        head_start(lambda p: r.io_src.at[p], r.io_dst, r.io_s, r.io_r)
        r.io_dst[h] = r.io_src[h]
        if inside:
            red1.third(2, 1)

        dp_wait(lambda p: r.fa.at[d], r.fa, r.fa_s, r.fa_r)
        for j in range(n):
            r.fta[pl.ds(2 * j, 2), :] = r.fa[j]
        film_block = dot_tn_high(r.esel[...], r.fta[...])
        r.film[...] = jnp.concatenate([film_block[:film_rows, :BLK], film_block[:film_rows, 128 : 128 + BLK]], axis=1)
        embed_part = dot_nt_high(r.fta[...], r.wfp[...].astype(F32))
        for j in range(n):
            r.ep[j] = embed_part[2 * j : 2 * j + 2]
        dp_start(lambda p: r.ep.at[p], r.er, r.er_s, r.er_r)
        r.er[d] = r.ep[d]

        dp_wait(lambda p: r.ad.at[d], r.ad, r.ad_s, r.ad_r)
        total = r.ad[0]
        for j in range(1, n):
            total = total + r.ad[j]
        r.hb[h] = total
        head_start(lambda p: r.hb.at[h], r.hb, r.hb_s, r.hb_r)
        head_wait(lambda p: r.ro_src.at[p], r.ro_dst, r.ro_s, r.ro_r)

        dp_wait(lambda p: r.ep.at[p], r.er, r.er_s, r.er_r)
        r.eh[h] = r.er[...]
        head_start(lambda p: r.eh.at[h], r.eh, r.eh_s, r.eh_r)

        if inside:
            red2.finish(((0, 3),))
            for a in range(3):
                r.second[a] = red2.last(a)

        head_wait(lambda p: r.hb.at[h], r.hb, r.hb_s, r.hb_r)
        even = r.hb[0] + r.hb[2]
        odd = r.hb[1] + r.hb[3]
        wide = jnp.concatenate(
            [even[:, :BLK], odd[:, :BLK], even[:, 128 : 128 + BLK], odd[:, 128 : 128 + BLK]], axis=1
        )
        r.gains_out[...] = wide[0:3]
        r.biases_out[...] = wide[3:13]

        head_wait(lambda p: r.eh.at[h], r.eh, r.eh_s, r.eh_r)
        pieces = []
        for j in range(n):
            piece = (r.eh[0, j] + r.eh[1, j]) + (r.eh[2, j] + r.eh[3, j])
            pieces.append(piece[:, :film_rows])
        r.embed_grad[...] = jnp.concatenate(pieces, axis=1) * silu_slope(r.emb[...].astype(F32))

        head_wait(lambda p: r.io_src.at[p], r.io_dst, r.io_s, r.io_r)

        if inside:
            red3.finish(((0, 1),))
            tiles = unpack_four(red3.last(0))
            r.sb_src[...] = jnp.where(c == 0, tiles[2], tiles[0])
            back = rc(r.sb_src, r.sb_dst, r.sb_s.at[0], r.sb_r.at[0], sib)
            back.start()
            r.output[...] = tiles[3]
            red1.finish(((0, 2), (2, 1)))
            for a in range(3):
                r.first[a] = red1.last(a)
            back.wait()
            r.attend[:, 0:128] = jnp.where(c == 0, tiles[0], tiles[1])
            r.attend[:, 128:256] = r.sb_dst[...]
            r.attend[:, 256:384] = jnp.where(c == 0, tiles[1], tiles[2])

    return kernel


def make_writer(names_in, names_out):
    def kernel(*refs):
        count = len(names_in)
        src, dst = Names(names_in, refs[:count]), Names(names_out, refs[count:])
        for name, packed in (("result", src.ro_dst), ("image_grad", src.io_dst)):
            for m in range(2):
                getattr(dst, name)[m] = dot_nt(unpack_pixels(packed[2 * m]), src.sel[0]) + dot_nt(
                    unpack_pixels(packed[2 * m + 1]), src.sel[1]
                )
        for name in ("first", "second"):
            if name in names_out:
                for a in range(3):
                    block = getattr(src, name)[a]
                    getattr(dst, name)[3 * a] = block[:48, :BLK]
                    getattr(dst, name)[3 * a + 1] = block[48:96, :BLK]
                    getattr(dst, name)[3 * a + 2] = last_tap(block)[:, :BLK]
        if "attend" in names_out:
            dst.attend[...] = jnp.concatenate([src.attend[:, j * 128 : j * 128 + BLK] for j in range(3)], axis=1)
            dst.output[...] = src.output[:, :BLK]
        for name in ("embed_grad", "film", "gains_out", "biases_out"):
            getattr(dst, name)[...] = getattr(src, name)[...]

    return kernel


def per_device(n, *args):
    (
        images,
        noise_field,
        time_steps,
        embedding,
        first_kernel,
        second_kernel,
        film_weight,
        attend_weight,
        output_weight,
        norm_gains,
        biases,
        cotangent,
    ) = args
    inside = n == 8
    keep, noise = plan(time_steps)
    coef = jnp.stack([keep, noise])
    maps, height, width, channels = images.shape
    flat_shape = (maps, height * width, channels)
    film_rows = film_weight.shape[0]
    inputs = dict(
        coef=coef,
        images=images.reshape(flat_shape),
        noise=noise_field.reshape(flat_shape),
        cot=cotangent.reshape(flat_shape),
        emb=embedding,
        k1=first_kernel.reshape((9,) + first_kernel.shape[2:]),
        k2=second_kernel.reshape((9,) + second_kernel.shape[2:]),
        wf=film_weight,
        wa=attend_weight,
        wo=output_weight,
        gains=norm_gains,
        biases=biases,
        sel=jnp.asarray(channel_lanes(), BF16),
        gmask=jnp.asarray(group_mask(), BF16),
        selp=jnp.asarray(block_lanes(3), BF16),
    )
    shapes = dict(
        ro_dst=(4, 384, 128),
        io_dst=(4, 384, 128),
        embed_grad=embedding.shape,
        first=(3, 112, 128),
        second=(3, 112, 128),
        film=film_weight.shape,
        attend=(48, 384),
        output=(48, 128),
        gains_out=norm_gains.shape,
        biases_out=biases.shape,
    )
    names_in, names_out = list(INPUTS), list(OUTPUTS)
    core = lax.axis_index("head") % 2
    if not inside:
        def whole(array, row_axis):
            array = lax.all_gather(array, "dp", axis=row_axis, tiled=True)
            return lax.all_gather(array, "head", axis=array.ndim - 1, tiled=True)

        def spread(array, count):
            taps = array.shape[0]
            array = array.reshape(taps, 4, 2, 48, 2, 2, BLK)
            array = lax.dynamic_index_in_dim(array, core, 5, keepdims=False)
            array = jnp.transpose(array, (2, 4, 1, 0, 3, 5))
            array = jnp.pad(array, ((0, 0),) * 5 + ((0, 32),))
            return array.reshape(4, 4, taps * 48, 128)

        full_a = whole(attend_weight, 0).reshape(384, 2, 3, 2, BLK)
        full_a = jnp.transpose(full_a, (2, 0, 1, 3, 4)).reshape(3, 384, 384)
        full_o = whole(output_weight, 0)[None]
        for name, last, array in (("g1", "t1", first_kernel), ("g2", "t2", second_kernel)):
            blocks = spread(whole(array, 2).reshape(9, 384, 384), 9).reshape(4, 4, 3, 3, 48, 128)
            two = blocks[:, :, :, :2].reshape(4, 4, 3, 96, 128)
            inputs[name] = jnp.pad(two, ((0, 0),) * 3 + ((0, 16), (0, 0))).reshape(4, 4, 336, 128)
            inputs[last] = blocks[:, :, :, 2].reshape(4, 4, 144, 128)
        inputs["g3"] = spread(jnp.concatenate([full_a, full_o], axis=0), 4)
        names_in += ["g1", "g2", "t1", "t2", "g3"]
        shapes["first"] = shapes["second"] = (3, 4, 4, 112, 128)
        shapes["attend"] = (1, 4, 4, 144, 128)
        del shapes["output"]
        names_out.remove("output")
    items = scratch_list(n, inside)
    smem = pl.BlockSpec(memory_space=pltpu.SMEM)
    vmem = pl.BlockSpec(memory_space=pltpu.VMEM)
    outs = pl.pallas_call(
        make_kernel(n, inside, names_in + names_out + [name for name, _ in items]),
        out_shape=[
            jax.ShapeDtypeStruct(shapes[name], BF16 if name in ("ro_dst", "io_dst") else F32) for name in names_out
        ],
        in_specs=[smem if name == "coef" else vmem for name in names_in],
        out_specs=[vmem] * len(names_out),
        scratch_shapes=[item for _, item in items],
        compiler_params=pltpu.CompilerParams(
            collective_id=0, has_side_effects=True, vmem_limit_bytes=63 * 1024 * 1024
        ),
        name="blocks",
    )(*[inputs[name] for name in names_in])
    raw = dict(zip(names_out, outs))
    final = dict(
        result=flat_shape,
        image_grad=flat_shape,
        embed_grad=embedding.shape,
        film=film_weight.shape,
        gains_out=norm_gains.shape,
        biases_out=biases.shape,
    )
    if inside:
        final.update(first=(9, 48, BLK), second=(9, 48, BLK), attend=attend_weight.shape, output=output_weight.shape)
    names_last = [name for name in names_out if inside or name not in ("first", "second", "attend")] + ["sel"]
    names_final = list(final)
    outs = pl.pallas_call(
        make_writer(names_last, names_final),
        out_shape=[jax.ShapeDtypeStruct(final[name], F32) for name in names_final],
        in_specs=[vmem] * len(names_last),
        out_specs=[vmem] * len(names_final),
        compiler_params=pltpu.CompilerParams(vmem_limit_bytes=63 * 1024 * 1024),
        name="outputs",
    )(*[inputs["sel"] if name == "sel" else raw[name] for name in names_last])
    out = dict(zip(names_final, outs))
    if not inside:

        def blocks_of(array, size):
            parts = [array[..., k * 48 : k * 48 + 48, :BLK] for k in range(size)]
            if size == 2:
                lanes = [array[..., k * 32 : k * 32 + 32, BLK:] for k in range(3)]
                lanes = jnp.concatenate(lanes, axis=-1)
                parts.append(jnp.concatenate([lanes, array[..., 96:112, :BLK]], axis=-2))
            else:
                lanes = [array[..., k * 48 : k * 48 + 48, BLK:] for k in range(3)]
                parts.append(jnp.concatenate(lanes, axis=-1))
            array = jnp.stack(parts, axis=1)
            array = array.reshape(array.shape[:2] + (2, 2, 4, 48, BLK))
            taps = array.shape[0] * array.shape[1]
            array = jnp.transpose(array, (0, 1, 4, 2, 5, 3, 6)).reshape(taps, 384, 2, 1, BLK)
            both = jnp.concatenate([array, jnp.zeros_like(array)], axis=3)
            return jnp.where(core == 0, both, both[:, :, :, ::-1]).reshape(taps, 384, 384)

        def shared(array, axis):
            array = lax.psum_scatter(array, "head", scatter_dimension=array.ndim - 1, tiled=True)
            return lax.psum_scatter(array, "dp", scatter_dimension=axis, tiled=True)

        out["first"] = shared(blocks_of(raw["first"], 2), 1)
        out["second"] = shared(blocks_of(raw["second"], 2), 1)
        both = blocks_of(raw["attend"], 3)
        joined = both[:3].reshape(3, 384, 2, 2, BLK)
        joined = jnp.transpose(joined, (1, 2, 0, 3, 4)).reshape(384, 1152)
        out["attend"] = shared(joined, 0)
        out["output"] = shared(both[3], 0)
    return (
        out["result"].reshape(images.shape),
        out["image_grad"].reshape(images.shape),
        out["embed_grad"],
        out["first"].reshape(first_kernel.shape),
        out["second"].reshape(second_kernel.shape),
        out["film"],
        out["attend"],
        out["output"],
        out["gains_out"],
        out["biases_out"],
    )


def solution(mesh):
    n = mesh.shape["dp"]
    field = P("dp", "head", None, None)
    taps = P(None, None, "dp", "head")
    both = P("dp", "head")
    return jax.shard_map(
        lambda *args: per_device(n, *args),
        mesh=mesh,
        in_specs=(field, field, P("dp"), P("dp", None), taps, taps, both, both, both, P(), P(), field),
        out_specs=(field, field, P("dp", None), taps, taps, both, both, both, P(), P()),
        check_vma=False,
    )
```

```python
import math

import jax
import jax.numpy as jnp
import numpy as np
from jax import lax
from jax.experimental import pallas as pl
from jax.experimental.pallas import tpu as pltpu
from jax.sharding import PartitionSpec as P

HEAD_DIM = 96
GROUPS = 32
STEPS = 4000
EPS = 1e-05
OFFSET = 0.008
MESH = pl.DeviceIdType.MESH
F32 = jnp.float32
BF16 = jnp.bfloat16

PX = 1024
ROW = 32
CHUNK = 256
BLK = 96
HALF = 256
NHEAD = 4


def plan(time_steps):
    fraction = (time_steps.astype(F32) + 1.0) / STEPS
    start = jnp.square(jnp.cos(jnp.float32(OFFSET / (1.0 + OFFSET) * (math.pi / 2))))
    curve = jnp.square(jnp.cos((fraction + OFFSET) / (1.0 + OFFSET) * (math.pi / 2))) / start
    return (jnp.sqrt(curve), jnp.sqrt(1.0 - curve))


def channel_lanes():
    sel = np.zeros((2, 384, HALF), np.float32)
    for block in range(4):
        for j in range(BLK):
            sel[block % 2, block * BLK + j, (block // 2) * 128 + j] = 1.0
    return sel


def block_lanes(count):
    sel = np.zeros((count * BLK, count * 128), np.float32)
    for block in range(count):
        for j in range(BLK):
            sel[block * BLK + j, block * 128 + j] = 1.0
    return sel


def group_mask():
    lane = np.arange(HALF)
    ok = lane % 128 < BLK
    group = (lane // 128) * 100 + (lane % 128) // 12
    return ((group[:, None] == group[None, :]) & ok[:, None] & ok[None, :]).astype(np.float32)


def dot(a, b):
    return lax.dot_general(a, b, (((1,), (0,)), ((), ())), preferred_element_type=F32)


def dot_nt(a, b):
    return lax.dot_general(a, b, (((1,), (1,)), ((), ())), preferred_element_type=F32)


def dot_nt_high(a, b):
    return lax.dot_general(
        a, b, (((1,), (1,)), ((), ())), preferred_element_type=F32, precision=lax.Precision.HIGHEST
    )


def dot_tn_high(a, b):
    return lax.dot_general(
        a, b, (((0,), (0,)), ((), ())), preferred_element_type=F32, precision=lax.Precision.HIGHEST
    )


def exact_dot(values, ones):
    high = values.astype(BF16).astype(F32)
    rest = values - high
    middle = rest.astype(BF16).astype(F32)
    low = rest - middle
    rows = values.shape[0]
    out = dot(jnp.concatenate([high, middle, low], axis=0).astype(BF16), ones)
    return out[:rows] + out[rows : 2 * rows] + out[2 * rows :]


def sigmoid(v):
    return 0.5 + 0.5 * jnp.tanh(0.5 * v)


def silu(v):
    return v * sigmoid(v)


def silu_slope(v):
    s = sigmoid(v)
    return s * (1.0 + v * (1.0 - s))


def pack_taps(t0, t1, t2):
    t0, t1, t2 = t0[:, :BLK], t1[:, :BLK], t2[:, :BLK]
    join = lambda a, b: jnp.concatenate([a, b], axis=1)
    return jnp.concatenate(
        [
            join(t0[:32], t2[:32, :32]),
            join(t0[32:], t2[:16, 32:64]),
            join(t1[:16], t2[16:32, 32:64]),
            join(t1[16:], t2[:32, 64:]),
            join(t2[32:], jnp.zeros((16, 32), t2.dtype)),
        ],
        axis=0,
    )


def last_tap(packed):
    lanes = [packed[:32, BLK:], packed[32:64, BLK:], packed[64:96, BLK:], jnp.zeros((32, 32), packed.dtype)]
    return jnp.concatenate([jnp.concatenate(lanes, axis=1), packed[96:112]], axis=0)


def pack_four(b0, b1, b2, b3):
    return jnp.concatenate(
        [jnp.concatenate([b[:, :BLK], b3[:, 32 * k : 32 * k + 32]], axis=1) for k, b in enumerate((b0, b1, b2))],
        axis=0,
    )


def unpack_four(packed):
    size = packed.shape[0] // 3
    parts = [packed[k * size : k * size + size] for k in range(3)]
    zero = jnp.zeros((size, 32), packed.dtype)
    fourth = jnp.concatenate([p[:, BLK:] for p in parts] + [zero], axis=1)
    return [jnp.concatenate([p[:, :BLK], zero], axis=1) for p in parts] + [fourth]


def pack_pixels(full):
    half = CHUNK // 2
    return pack_four(full[:half, :128], full[half:, :128], full[:half, 128:], full[half:, 128:])


def unpack_pixels(packed):
    b0, b1, b2, b3 = unpack_four(packed)
    return jnp.concatenate([jnp.concatenate([b0, b2], axis=1), jnp.concatenate([b1, b3], axis=1)], axis=0)


INPUTS = (
    "coef",
    "images",
    "noise",
    "cot",
    "emb",
    "k1",
    "k2",
    "wf",
    "wa",
    "wo",
    "gains",
    "biases",
    "sel",
    "gmask",
    "selp",
)
OUTPUTS = (
    "ro_dst",
    "io_dst",
    "embed_grad",
    "first",
    "second",
    "film",
    "attend",
    "output",
    "gains_out",
    "biases_out",
)


class Names:
    def __init__(self, names, refs):
        for name, ref in zip(names, refs):
            setattr(self, name, ref)


def scratch_list(n, inside):
    dma = pltpu.SemaphoreType.DMA
    items = []

    def vm(name, shape, dtype):
        items.append((name, pltpu.VMEM(shape, dtype)))

    def sem(name, count):
        items.append((name + "_s", dma((count,))))
        items.append((name + "_r", dma((count,))))

    for name in ("mx", "cx", "ro", "io"):
        vm(name + "_src", (4, 384, 128), BF16)
        if name in ("mx", "cx"):
            vm(name + "_dst", (4, 384, 128), BF16)
            vm(name, (4, CHUNK, HALF), BF16)
        sem(name, 4)
    for name in ("act1", "act2"):
        vm(name, (2, PX + 2 * ROW, HALF), BF16)
        vm(name + "_t", (2, HALF, PX), BF16)
        sem(name, 4)
    vm("ai", (2, PX, HALF), BF16)
    vm("ai_t", (2, HALF, PX), BF16)
    sem("ai", 4)
    vm("att", (4, PX, 128), BF16)
    vm("att_t", (2, HALF, PX), BF16)
    sem("att", 2)
    for name in ("do", "n3", "d2", "d1"):
        vm(name + "_src", (PX, HALF), BF16)
        vm(name + "_dst", (PX, HALF), BF16)
        sem(name, 2)
    vm("v2", (PX, HALF), F32)
    vm("v3", (PX, HALF), F32)
    vm("gres", (PX, HALF), F32)
    vm("gtmp", (PX, HALF), F32)
    vm("qkv", (6, PX, 128), BF16)
    vm("kvt", (4, 128, PX), BF16)
    vm("dout", (2, PX, 128), BF16)
    vm("dproj", (6, PX, 128), BF16)
    vm("gr2", (3, PX + 2 * ROW, HALF), BF16)
    vm("gr1", (3, PX + 2 * ROW, HALF), BF16)
    vm("par", (16, 384), F32)
    vm("parown", (16, HALF), F32)
    vm("stat", (16, HALF), F32)
    vm("sums", (16, HALF), F32)
    if inside:
        vm("g1", (4, 4, 336, 128), BF16)
        vm("g2", (4, 4, 336, 128), BF16)
        vm("t1", (4, 4, 144, 128), BF16)
        vm("t2", (4, 4, 144, 128), BF16)
        vm("p3", (4, 4, 144, 128), BF16)
        vm("g3", (4, 4, 192, 128), BF16)
        for name in ("g1", "g2", "p3"):
            sem(name + "z", 4)
            sem(name + "v", 4)
            sem(name + "w", 8)
        vm("sw_src", (48, 128), BF16)
        vm("sw_dst", (48, 128), BF16)
        sem("sw", 1)
        vm("sb_src", (48, 128), F32)
        vm("sb_dst", (48, 128), F32)
        sem("sb", 1)
        for name, nc, rows in (("r1", 3, 112), ("r2", 3, 112), ("r3", 1, 144)):
            vm(name + "_acc", (nc, 4, 4, rows, 128), F32)
            vm(name + "w_src", (nc, 2, 4, rows, 128), BF16)
            vm(name + "w_dst", (nc, 2, 4, rows, 128), BF16)
            vm(name + "v_src", (nc, 4, rows, 128), BF16)
            vm(name + "v_dst", (nc, 4, rows, 128), BF16)
            vm(name + "z_src", (4, nc, rows, 128), BF16)
            vm(name + "z_dst", (4, nc, rows, 128), BF16)
            sem(name + "w", nc)
            sem(name + "v", nc)
            sem(name + "z", nc * 4)
    vm("el", (n, 2, 768), F32)
    sem("el", n)
    vm("em", (2 * n, 768), F32)
    vm("wfp", (128, HALF), BF16)
    vm("esel", (2 * n, 128), F32)
    vm("fp", (n, 2, HALF), F32)
    vm("fr", (n, 2, HALF), F32)
    sem("fr", n)
    vm("fx", (4, 1, 128), F32)
    vm("fh", (4, 1, 128), F32)
    sem("fh", 4)
    vm("ft", (4, 1, 128), F32)
    vm("th", (4, 1, 128), F32)
    sem("th", 4)
    vm("fa", (n, 2, HALF), F32)
    sem("fa", n)
    vm("fta", (2 * n, HALF), F32)
    vm("ep", (n, 2, 128), F32)
    vm("er", (n, 2, 128), F32)
    sem("er", n)
    vm("eh", (4, n, 2, 128), F32)
    sem("eh", 4)
    vm("ad", (n, 16, HALF), F32)
    sem("ad", n)
    vm("hb", (4, 16, HALF), F32)
    sem("hb", 4)
    return items


def make_kernel(n, inside, names):
    film_rows = 768 // n

    def kernel(*refs):
        r = Names(names, refs)
        d = lax.axis_index("dp")
        h = lax.axis_index("head")
        x = h // 2
        c = h - 2 * x
        z = d // 2
        y = d - 2 * z
        sib = (d, h + 1 - 2 * c)
        xdev = (d, h + 2 - 4 * x)
        v = x + c * (y - x)
        w = y + c * (x - y)
        vdev = (d + c * (1 - 2 * y), h + (1 - c) * (2 - 4 * x))
        wdev = (d + (1 - c) * (1 - 2 * y), h + c * (2 - 4 * x))

        def slot(xx, yy):
            if inside:
                return (yy + c * (xx - yy)) * 2 + xx + c * (yy - xx)
            return yy * 2 + xx

        def rc(src, dst, send, recv, dev):
            return pltpu.make_async_remote_copy(
                src_ref=src, dst_ref=dst, send_sem=send, recv_sem=recv, device_id=dev, device_id_type=MESH
            )

        def loop(count, body):
            def step(i, carry):
                body(i)
                return carry

            lax.fori_loop(0, count, step, 0)

        def each(count, body):
            for i in range(count):
                body(i)

        def rows(i, size=CHUNK, base=0):
            return pl.ds(pl.multiple_of(base + i * size, 32), size)

        def dp_start(src_of, dst, send, recv):
            def step(k, carry):
                peer = lax.rem(d + k, n)
                rc(src_of(peer), dst.at[d], send.at[k], recv.at[d], (peer, h)).start()
                return carry

            lax.fori_loop(1, n, step, 0)

        def dp_wait(src_of, dst, send, recv):
            def step(k, carry):
                peer = lax.rem(d + k, n)
                copy = rc(src_of(peer), dst.at[peer], send.at[k], recv.at[peer], (peer, h))
                copy.wait_recv()
                copy.wait_send()
                return carry

            lax.fori_loop(1, n, step, 0)

        def head_start(src_of, dst, send, recv):
            for k in range(1, 4):
                peer = lax.rem(h + k, 4)
                rc(src_of(peer), dst.at[h], send.at[k], recv.at[h], (d, peer)).start()

        def head_wait(src_of, dst, send, recv):
            for k in range(1, 4):
                peer = lax.rem(h + k, 4)
                copy = rc(src_of(peer), dst.at[peer], send.at[k], recv.at[peer], (d, peer))
                copy.wait_recv()
                copy.wait_send()

        class Halves:
            def __init__(self, name, base):
                self.buf, self.base = getattr(r, name), base
                self.send, self.recv = getattr(r, name + "_s"), getattr(r, name + "_r")

            def at(self, core, i):
                return self.buf.at[core, rows(i, CHUNK, self.base)]

            def fill(self, make):
                def body(i):
                    self.buf[c, rows(i, CHUNK, self.base), :] = make(i)
                    ref = self.at(c, i)
                    rc(ref, ref, self.send.at[i], self.recv.at[i], sib).start()

                loop(4, body)

            def wait(self):
                for i in range(4):
                    ref = self.at(1 - c, i)
                    copy = rc(ref, ref, self.send.at[i], self.recv.at[i], sib)
                    copy.wait_recv()
                    copy.wait_send()

        class Parts:
            def __init__(self, name):
                self.src, self.dst = getattr(r, name + "_src"), getattr(r, name + "_dst")
                self.send, self.recv = getattr(r, name + "_s"), getattr(r, name + "_r")

            def copy(self, i):
                at = rows(i, 2 * CHUNK)
                return rc(self.src.at[at], self.dst.at[at], self.send.at[i], self.recv.at[i], sib)

            def fill(self, make):
                def body(i):
                    self.src[rows(i, 2 * CHUNK), :] = make(i).astype(BF16)
                    self.copy(i).start()

                each(2, body)

            def get(self, i):
                copy = self.copy(i)
                copy.wait_recv()
                copy.wait_send()
                return self.dst[rows(i, 2 * CHUNK), :].astype(F32)

        class Gather:
            def __init__(self, name):
                self.g = getattr(r, name)
                self.zs, self.zr = getattr(r, name + "z_s"), getattr(r, name + "z_r")
                self.vs, self.vr = getattr(r, name + "v_s"), getattr(r, name + "v_r")
                self.ws, self.wr = getattr(r, name + "w_s"), getattr(r, name + "w_r")

            def zcopy(self, k):
                peer = (lax.rem(z + k, 4) * 2 + y, h)
                return rc(
                    self.g.at[w * 2 + v, 0], self.g.at[w * 2 + v, 4 - k], self.zs.at[k], self.zr.at[4 - k], peer
                )

            def vcopy(self, vv, i):
                ref = self.g.at[w * 2 + vv, i]
                return rc(ref, ref, self.vs.at[i], self.vr.at[i], vdev)

            def wcopy(self, ww, other, i):
                ref = self.g.at[ww * 2 + v + other * (1 - 2 * v), i]
                return rc(ref, ref, self.ws.at[2 * i + other], self.wr.at[2 * i + other], wdev)

            def own(self):
                for k in range(1, 4):
                    self.zcopy(k).start()
                self.vcopy(v, 0).start()
                self.wcopy(w, 0, 0).start()

            def pass_z(self):
                self.vcopy(1 - v, 0).wait_recv()
                self.wcopy(w, 1, 0).start()
                for k in range(1, 4):
                    self.zcopy(k).wait_recv()
                    self.vcopy(v, 4 - k).start()
                    self.wcopy(w, 0, 4 - k).start()

            def pass_v(self):
                for k in range(1, 4):
                    self.vcopy(1 - v, 4 - k).wait_recv()
                    self.wcopy(w, 1, 4 - k).start()

            def done(self):
                for k in range(1, 4):
                    self.zcopy(k).wait_send()
                for i in range(4):
                    self.vcopy(v, i).wait_send()
                    for other in range(2):
                        self.wcopy(1 - w, other, i).wait_recv()
                        self.wcopy(w, other, i).wait_send()

        class Reduce:
            def __init__(self, name, count):
                get = lambda tail: getattr(r, name + tail)
                self.acc, self.count = get("_acc"), count
                self.wsrc, self.wdst, self.ws, self.wr = get("w_src"), get("w_dst"), get("w_s"), get("w_r")
                self.vsrc, self.vdst, self.vs, self.vr = get("v_src"), get("v_dst"), get("v_s"), get("v_r")
                self.zsrc, self.zdst, self.zs, self.zr = get("z_src"), get("z_dst"), get("z_s"), get("z_r")

            def wcopy(self, a):
                return rc(self.wsrc.at[a], self.wdst.at[a], self.ws.at[a], self.wr.at[a], wdev)

            def vcopy(self, a, size):
                at = pl.ds(a, size)
                return rc(self.vsrc.at[at], self.vdst.at[at], self.vs.at[a], self.vr.at[a], vdev)

            def zcopy(self, a, size, k):
                at = pl.ds(a, size)
                return rc(
                    self.zsrc.at[k, at],
                    self.zdst.at[4 - k, at],
                    self.zs.at[a * 4 + k],
                    self.zr.at[a * 4 + 4 - k],
                    (lax.rem(z + k, 4) * 2 + y, h),
                )

            def start(self, a):
                def step(i, carry):
                    vv, zz = i // 4, lax.rem(i, 4)
                    self.wsrc[a, vv, zz] = self.acc[a, (1 - w) * 2 + vv, zz].astype(BF16)
                    return carry

                lax.fori_loop(0, 8, step, 0)
                self.wcopy(a).start()

            def second(self, first, size):
                for a in range(first, first + size):
                    self.wcopy(a).wait_recv()

                    def step(zz, carry):
                        self.vsrc[a, zz] = (
                            self.acc[a, w * 2 + 1 - v, zz] + self.wdst[a, 1 - v, zz].astype(F32)
                        ).astype(BF16)
                        return carry

                    lax.fori_loop(0, 4, step, 0)
                self.vcopy(first, size).start()

            def third(self, first, size):
                self.vcopy(first, size).wait_recv()
                for a in range(first, first + size):

                    def step(k, carry):
                        zz = lax.rem(z + k, 4)
                        total = (
                            self.acc[a, w * 2 + v, zz]
                            + self.wdst[a, v, zz].astype(F32)
                            + self.vdst[a, zz].astype(F32)
                        )
                        self.acc[a, w * 2 + v, zz] = total
                        self.zsrc[k, a] = total.astype(BF16)
                        return carry

                    lax.fori_loop(0, 4, step, 0)
                for k in range(1, 4):
                    self.zcopy(first, size, k).start()

            def finish(self, groups):
                for first, size in groups:
                    self.vcopy(first, size).wait_send()
                    for k in range(1, 4):
                        copy = self.zcopy(first, size, k)
                        copy.wait_recv()
                        copy.wait_send()
                for a in range(self.count):
                    self.wcopy(a).wait_send()

            def last(self, a):
                total = self.acc[a, w * 2 + v, z]
                for k in range(1, 4):
                    total = total + self.zdst[k, a].astype(F32)
                return total

        def rel(zc):
            return lax.rem(zc - z + 4, 4) if inside else zc

        class Taps:
            def __init__(self, packed, last):
                self.packed, self.last = packed, last

            def block(self, tap, zc, xx, yy):
                a, b = tap // 3, tap % 3
                if b < 2:
                    return self.packed[slot(xx, yy), rel(zc), pl.ds(a * 112 + b * 48, 48), :]
                return self.last[slot(xx, yy), rel(zc), pl.ds(a * 48, 48), :]

            def unpack(self):
                def step(i, carry):
                    q, zz = i // 4, lax.rem(i, 4)
                    for a in range(3):
                        self.last[q, zz, pl.ds(a * 48, 48), :] = last_tap(
                            self.packed[q, zz, pl.ds(a * 112, 112), :]
                        )
                    return carry

                lax.fori_loop(0, 16, step, 0)

        class Plain:
            def __init__(self, blocks):
                self.blocks = blocks

            def block(self, tap, zc, xx, yy):
                return self.blocks[slot(xx, yy), rel(zc), pl.ds(tap * 48, 48), :]

            def unpack(self):
                def step(i, carry):
                    q, zz = i // 4, lax.rem(i, 4)
                    self.blocks[q, zz] = jnp.concatenate(unpack_four(r.p3[q, zz]), axis=0)
                    return carry

                lax.fori_loop(0, 16, step, 0)

        k1, k2, k3 = Taps(r.g1, r.t1), Taps(r.g2, r.t2), Plain(r.g3)

        def wtile(g, tap, zc, xx):
            return jnp.concatenate(
                [g.block(tap, zc, xx, 0), g.block(tap, zc, xx, 1), jnp.zeros((32, 128), BF16)], axis=0
            )

        def wtap(g, tap, zcs):
            return jnp.concatenate(
                [jnp.concatenate([wtile(g, tap, zc, xx) for xx in range(2)], axis=1) for zc in zcs], axis=0
            )

        ALL = (0, 2, 1, 3)

        def half_of(core):
            return (core, core + 2)

        def wproj(zcs):
            return jnp.concatenate(
                [
                    jnp.concatenate([wtile(k3, j, zc, xx) for xx in range(2) for j in range(3)], axis=1)
                    for zc in zcs
                ],
                axis=0,
            )

        def flat(buf, base, i, size):
            return jnp.concatenate([buf[0, rows(i, size, base), :], buf[1, rows(i, size, base), :]], axis=1)

        barrier = pltpu.get_barrier_semaphore()

        def greet(k, carry):
            pl.semaphore_signal(barrier, inc=1, device_id=(lax.rem(d + k, n), h), device_id_type=MESH)
            return carry

        lax.fori_loop(1, n, greet, 0)
        for k in range(1, 4):
            pl.semaphore_signal(barrier, inc=1, device_id=(d, lax.rem(h + k, 4)), device_id_type=MESH)
        if inside:
            for a in range(3):
                r.g1[w * 2 + v, 0, pl.ds(a * 112, 112), :] = pack_taps(*[r.k1[3 * a + b] for b in range(3)])
        pl.semaphore_wait(barrier, n - 1 + 3)
        if inside:
            ga, gb, gc = Gather("g1"), Gather("g2"), Gather("p3")
            ga.own()

        def mix(m, carry):
            field = r.coef[0, m] * r.images[m].astype(F32) + r.coef[1, m] * r.noise[m].astype(F32)
            low = field.astype(BF16)
            for core in range(2):
                r.mx_src[m * 2 + core] = pack_pixels(dot(low, r.sel[core])).astype(BF16)
            return carry

        lax.fori_loop(0, 2, mix, 0)
        head_start(lambda p: r.mx_src.at[p], r.mx_dst, r.mx_s, r.mx_r)
        r.mx_dst[h] = r.mx_src[h]

        r.el[d] = silu(r.emb[...].astype(F32)).astype(BF16).astype(F32)
        dp_start(lambda p: r.el.at[d], r.el, r.el_s, r.el_r)

        if inside:
            blocks = dot(r.wa[...], r.selp[: 3 * BLK, : 3 * 128]).astype(BF16)
            r.sw_src[...] = blocks[:, 128:256]
            swap = rc(r.sw_src, r.sw_dst, r.sw_s.at[0], r.sw_r.at[0], sib)
            swap.start()
            for a in range(3):
                r.g2[w * 2 + v, 0, pl.ds(a * 112, 112), :] = pack_taps(*[r.k2[3 * a + b] for b in range(3)])
        r.par[0:3, :] = r.gains[...]
        r.par[3:13, :] = r.biases[...]
        r.par[13:16, :] = jnp.zeros((3, 384), F32)
        r.parown[...] = exact_dot(r.par[...], r.sel[c])

        def prow(i):
            return r.parown[pl.ds(i, 1), :]

        for buf in (r.act1, r.act2):
            for core in range(2):
                buf[core, pl.ds(0, ROW), :] = jnp.zeros((ROW, HALF), BF16)
                buf[core, pl.ds(PX + ROW, ROW), :] = jnp.zeros((ROW, HALF), BF16)
        for buf in (r.gr1, r.gr2):
            for b in range(3):
                buf[b, pl.ds(0, ROW), :] = jnp.zeros((ROW, HALF), BF16)
                buf[b, pl.ds(PX + ROW, ROW), :] = jnp.zeros((ROW, HALF), BF16)
        r.wfp[...] = jnp.zeros((128, HALF), BF16)
        r.wfp[pl.ds(0, film_rows), :] = dot(r.wf[...], r.selp[: 2 * BLK, :HALF]).astype(BF16)
        if inside:
            ga.pass_z()
            gb.own()

        count = float(PX * 12)

        def fold(vals):
            return jnp.sum(vals.reshape(CHUNK // 8, 8, HALF), axis=0)

        def sums_of(fn, k):
            def step(i, carry):
                return tuple(a + fold(b) for a, b in zip(carry, fn(i)))

            zero = jnp.zeros((8, HALF), F32)
            return lax.fori_loop(0, 4, step, (zero,) * k)

        def group_mean(part):
            return jnp.sum(exact_dot(part, r.gmask[...]), axis=0, keepdims=True) / count

        def norm(load, which, total):
            mean = group_mean(total)
            (square,) = sums_of(lambda i: (jnp.square(load(i) - mean),), 1)
            inv = lax.rsqrt(group_mean(square) + EPS)
            r.stat[pl.ds(2 * which, 1), :] = mean
            r.stat[pl.ds(2 * which + 1, 1), :] = inv
            return mean, inv

        zero8 = jnp.zeros((8, HALF), F32)

        def norm_back(sums, load_grad, load_hat, coef, inv):
            plain, cross = sums
            plain_mean, cross_mean = group_mean(coef * plain), group_mean(coef * cross)
            outer, base, slope = inv * coef, inv * plain_mean, inv * cross_mean

            def chunk(i):
                return outer * load_grad(i) - base - load_hat(i) * slope

            return (
                jnp.sum(plain, axis=0, keepdims=True),
                jnp.sum(cross, axis=0, keepdims=True),
                chunk,
            )

        head_wait(lambda p: r.mx_src.at[p], r.mx_dst, r.mx_s, r.mx_r)

        def unpack_mixed(i, carry):
            vals = unpack_pixels(r.mx_dst[i])
            r.mx[i] = vals
            return carry + fold(vals.astype(F32))

        mixed_sum = lax.fori_loop(0, 4, unpack_mixed, zero8)

        def mixed(i):
            return r.mx[i].astype(F32)

        mean1, inv1 = norm(mixed, 0, mixed_sum)
        gain1, shift1 = prow(0), prow(3)
        act1 = Halves("act1", ROW)

        def affine(mean, inv, gain, shift):
            return inv * gain, shift - mean * (inv * gain)

        mul1, add1 = affine(mean1, inv1, gain1, shift1)

        def pre1(i):
            return mixed(i) * mul1 + add1

        act1.fill(lambda i: silu(pre1(i)).astype(BF16))
        if inside:
            ga.pass_v()

        dp_wait(lambda p: r.el.at[d], r.el, r.el_s, r.el_r)
        for j in range(n):
            r.em[pl.ds(2 * j, 2), :] = r.el[j]
        place = lax.broadcasted_iota(jnp.int32, (768, 128), 0) - film_rows * d
        lane = lax.broadcasted_iota(jnp.int32, (768, 128), 1)
        pick = jnp.where((place == lane) & (lane < film_rows), 1.0, 0.0).astype(BF16)
        r.esel[...] = dot(r.em[...].astype(BF16), pick)
        film_part = dot(r.esel[...].astype(BF16), r.wfp[...])
        for j in range(n):
            r.fp[j] = film_part[2 * j : 2 * j + 2]
        dp_start(lambda p: r.fp.at[p], r.fr, r.fr_s, r.fr_r)
        r.fr[d] = r.fp[d]
        if inside:
            swap.wait()
            got = r.sw_dst[...]
            keep0, keep2 = blocks[:, :128], blocks[:, 256:]
            r.p3[w * 2 + v, 0] = pack_four(
                jnp.where(c == 0, keep0, got),
                jnp.where(c == 0, keep2, keep0),
                jnp.where(c == 0, got, keep2),
                r.wo[...],
            )
            gb.pass_z()
            gc.own()
        def split_cot(m, carry):
            for core in range(2):
                r.cx_src[m * 2 + core] = pack_pixels(dot(r.cot[m], r.sel[core])).astype(BF16)
            return carry

        lax.fori_loop(0, 2, split_cot, 0)
        head_start(lambda p: r.cx_src.at[p], r.cx_dst, r.cx_s, r.cx_r)
        r.cx_dst[h] = r.cx_src[h]

        column = lax.broadcasted_iota(jnp.int32, (1, ROW, HALF), 1)
        not_first = jnp.where(column > 0, 1.0, 0.0)
        not_last = jnp.where(column < ROW - 1, 1.0, 0.0)

        def in_rows(vals, mask):
            return (vals.reshape(CHUNK // ROW, ROW, HALF) * mask).reshape(CHUNK, HALF)

        def from_left(vals):
            return in_rows(pltpu.roll(vals, 1, 0), not_first)

        def from_right(vals):
            return in_rows(pltpu.roll(vals, CHUNK - 1, 0), not_last)

        def transpose_act(buf, base, out):
            for core in range(2):
                for q in range(4):
                    out[core, :, pl.ds(q * CHUNK, CHUNK)] = jnp.transpose(
                        buf[core, pl.ds(base + q * CHUNK, CHUNK), :]
                    )

        def conv(buf, g, store, between):
            weights = lambda: jnp.concatenate(
                [jnp.concatenate([wtap(g, 3 * a + b, ALL) for b in range(3)], axis=1) for a in range(3)], axis=0
            )

            total = zero8
            for i in range(2):
                left = jnp.concatenate([flat(buf, ROW * a, i, 2 * CHUNK) for a in range(3)], axis=1)
                out = dot(left, weights())
                for j in range(2):
                    part = out[j * CHUNK : j * CHUNK + CHUNK]
                    part = part[:, HALF : 2 * HALF] + from_left(part[:, :HALF]) + from_right(part[:, 2 * HALF :])
                    total = total + fold(store(2 * i + j, part))
                if i == 0:
                    between()
            return total

        act1.wait()
        transpose_act(r.act1, ROW, r.act1_t)
        if inside:
            ga.done()
            k1.unpack()

        def store_v2(i, vals):
            vals = vals + prow(6)
            r.v2[rows(i), :] = vals
            return vals

        v2_sum = conv(r.act1, k1, store_v2, gb.pass_v if inside else lambda: None)
        dp_wait(lambda p: r.fp.at[p], r.fr, r.fr_s, r.fr_r)
        film_sum = r.fr[0]
        for j in range(1, n):
            film_sum = film_sum + r.fr[j]
        for m in range(2):
            for core in range(2):
                r.fx[m * 2 + core] = film_sum[m : m + 1, core * 128 : core * 128 + 128]
        head_start(lambda p: r.fx.at[p], r.fh, r.fh_s, r.fh_r)
        r.fh[h] = r.fx[h]

        head_wait(lambda p: r.fx.at[p], r.fh, r.fh_s, r.fh_r)
        scale = 1.0 + (jnp.concatenate([r.fh[0], r.fh[1]], axis=1) + prow(8))
        shift = jnp.concatenate([r.fh[2], r.fh[3]], axis=1) + prow(9)
        mean2, inv2 = norm(lambda i: r.v2[rows(i), :], 1, v2_sum)
        gain2, shift2 = prow(1), prow(4)
        act2 = Halves("act2", ROW)

        def hat2(i):
            return (r.v2[rows(i), :] - mean2) * inv2

        mul2, add2 = affine(mean2, inv2, gain2 * scale, shift2 * scale + shift)

        def pre2(i):
            return r.v2[rows(i), :] * mul2 + add2

        act2.fill(lambda i: silu(pre2(i)).astype(BF16))
        if inside:
            gc.pass_z()

        act2.wait()
        transpose_act(r.act2, ROW, r.act2_t)
        if inside:
            gb.done()
            k2.unpack()

        def store_v3(i, vals):
            vals = mixed(i) + (vals + prow(7))
            r.v3[rows(i), :] = vals
            return vals

        v3_sum = conv(r.act2, k2, store_v3, gc.pass_v if inside else lambda: None)
        mean3, inv3 = norm(lambda i: r.v3[rows(i), :], 2, v3_sum)
        gain3, shift3 = prow(2), prow(5)
        ai = Halves("ai", 0)

        def hat3(i):
            return (r.v3[rows(i), :] - mean3) * inv3

        mul3, add3 = affine(mean3, inv3, gain3, shift3)
        ai.fill(lambda i: (r.v3[rows(i), :] * mul3 + add3).astype(BF16))

        if inside:
            gc.done()
            k3.unpack()
        head_wait(lambda p: r.cx_src.at[p], r.cx_dst, r.cx_s, r.cx_r)

        def unpack_cot(i):
            r.cx[i] = unpack_pixels(r.cx_dst[i])

        loop(4, unpack_cot)
        dop = Parts("do")

        def cot_rows(i):
            return jnp.concatenate([r.cx[2 * i], r.cx[2 * i + 1]], axis=0)

        dop.fill(lambda i: dot_nt(cot_rows(i), wtap(k3, 3, half_of(1 - c))))

        ai.wait()
        bias_proj = [prow(10)[:, :128], prow(10)[:, 128:], None, None, prow(11)[:, :128], prow(11)[:, 128:]]

        def project(i):
            out = dot(flat(r.ai, 0, i, 2 * CHUNK), wproj(ALL))
            for k in range(6):
                part = out[:, k * 128 : k * 128 + 128]
                if bias_proj[k] is not None:
                    part = part + bias_proj[k]
                r.qkv[k, rows(i, 2 * CHUNK), :] = part.astype(BF16)

        each(2, project)

        def do_own(i):
            full = (dot_nt(cot_rows(i), wtap(k3, 3, half_of(c))) + dop.get(i)).astype(BF16)
            for k in range(2):
                r.dout[k, rows(i, 2 * CHUNK), :] = full[:, k * 128 : k * 128 + 128]

        each(2, do_own)

        factor = 1.0 / math.sqrt(HEAD_DIM)
        factor2 = factor * math.log2(math.e)
        att = []

        def transposes(k):
            r.kvt[k] = jnp.transpose(r.qkv[k + 2])

        loop(4, transposes)

        def att_copies(core):
            for i, ref in enumerate((r.att.at[pl.ds(core * 2, 2)], r.att_t.at[core])):
                yield rc(ref, ref, r.att_s.at[i], r.att_r.at[i], sib)

        def one_head(k):
            lows, grads = [], []
            for b in range(2):
                at = pl.ds(b * 2 * CHUNK, 2 * CHUNK)
                query = r.qkv[k, at, :]
                grad = r.dout[k, at, :]
                scores = dot_nt(r.qkv[2 + k], query)
                peak = jnp.max(scores, axis=0, keepdims=True)
                expo = jnp.exp2((scores - peak) * factor2)
                inverse = 1.0 / jnp.sum(expo, axis=0, keepdims=True)
                low = (expo * inverse).astype(BF16)
                got = dot(r.kvt[2 + k], low)
                got_low = got.astype(BF16)
                r.att_t[c, pl.ds(pl.multiple_of(k * 128, 128), 128), at] = got_low
                r.att[2 * c + k, at, :] = jnp.transpose(got_low)
                spread = jnp.sum(got * jnp.transpose(grad).astype(F32), axis=0, keepdims=True)
                probs_grad = dot_nt(r.qkv[4 + k], grad)
                scores_grad = ((probs_grad - spread) * inverse * expo).astype(BF16)
                back = dot(r.kvt[k], scores_grad)
                r.dproj[k, at, :] = (jnp.transpose(back) * factor).astype(BF16)
                lows.append(low)
                grads.append(scores_grad)
            r.dproj[4 + k] = dot(jnp.concatenate(lows, axis=1), r.dout[k]).astype(BF16)
            r.dproj[2 + k] = (dot(jnp.concatenate(grads, axis=1), r.qkv[k]) * factor).astype(BF16)

        loop(2, one_head)
        for copy in att_copies(c):
            copy.start()

        n3 = Parts("n3")

        def proj_rows(i):
            return jnp.concatenate([r.dproj[k, rows(i, 2 * CHUNK), :] for k in range(6)], axis=1)

        n3.fill(lambda i: dot_nt(proj_rows(i), wproj(half_of(1 - c))))

        for copy in att_copies(1 - c):
            copy.wait_recv()
            copy.wait_send()

        def result(i):
            left = jnp.concatenate([r.att[p, rows(i), :] for p in range(4)], axis=1)
            branch = dot(left, wtap(k3, 3, ALL)) + prow(12)
            r.ro_src[i] = pack_pixels(r.v3[rows(i), :] + branch).astype(BF16)

        loop(4, result)
        head_start(lambda p: r.ro_src.at[p], r.ro_dst, r.ro_s, r.ro_r)
        r.ro_dst[h] = r.ro_src[h]

        if inside:
            red1, red2, red3 = Reduce("r1", 3), Reduce("r2", 3), Reduce("r3", 1)
            acc1, acc2, acc3 = r.r1_acc, r.r2_acc, r.r3_acc
        else:
            acc1, acc2, acc3 = r.first, r.second, r.attend

        transpose_act(r.ai, 0, r.ai_t)
        right = jnp.concatenate([r.dproj[k] for k in range(6)], axis=1)
        cot_all = jnp.concatenate([r.cx[i] for i in range(4)], axis=0)
        for core in range(2):
            attend_out = dot(r.ai_t[core], right)
            output_out = dot(r.att_t[core], cot_all)
            for k in range(2):
                for yy in range(2):
                    for xx in range(2):
                        row = k * 128 + yy * 48
                        tiles = [
                            attend_out[row : row + 48, (xx * 3 + j) * 128 : (xx * 3 + j) * 128 + 128] for j in range(3)
                        ]
                        acc3[0, slot(xx, yy), core + 2 * k] = pack_four(
                            *tiles, output_out[row : row + 48, xx * 128 : xx * 128 + 128]
                        )
        if inside:
            red3.start(0)

        def proj_sums(i, carry):
            q = jnp.concatenate([r.dproj[0, rows(i), :], r.dproj[1, rows(i), :]], axis=1).astype(F32)
            val = jnp.concatenate([r.dproj[4, rows(i), :], r.dproj[5, rows(i), :]], axis=1).astype(F32)
            return (carry[0] + fold(q), carry[1] + fold(val), carry[2] + fold(r.cx[i].astype(F32)))

        qsum, vsum, csum = lax.fori_loop(0, 4, proj_sums, (zero8, zero8, zero8))
        r.sums[pl.ds(3 + 7, 1), :] = jnp.sum(qsum, axis=0, keepdims=True)
        r.sums[pl.ds(3 + 8, 1), :] = jnp.sum(vsum, axis=0, keepdims=True)
        r.sums[pl.ds(3 + 9, 1), :] = jnp.sum(csum, axis=0, keepdims=True)
        r.sums[pl.ds(13, 3), :] = jnp.zeros((3, HALF), F32)

        def n3_own(i, carry):
            both = dot_nt(proj_rows(i), wproj(half_of(c))) + n3.get(i)
            for j in range(2):
                vals = both[j * CHUNK : j * CHUNK + CHUNK]
                r.gtmp[rows(2 * i + j), :] = vals
                carry = carry[0] + fold(vals), carry[1] + fold(vals * hat3(2 * i + j))
            return carry

        sums3 = n3_own(1, n3_own(0, (zero8, zero8)))
        plain3, cross3, back3 = norm_back(sums3, lambda i: r.gtmp[rows(i), :], hat3, gain3, inv3)
        r.sums[pl.ds(2, 1), :] = cross3
        r.sums[pl.ds(3 + 2, 1), :] = plain3

        def shifted(buf, i, vals):
            buf[0, rows(i, CHUNK, ROW), :] = from_right(vals).astype(BF16)
            buf[1, rows(i, CHUNK, ROW), :] = vals.astype(BF16)
            buf[2, rows(i, CHUNK, ROW), :] = from_left(vals).astype(BF16)

        def residual_back(i, carry):
            vals = r.cx[i].astype(F32) + back3(i)
            r.gres[rows(i), :] = vals
            shifted(r.gr2, i, vals)
            return carry + fold(vals.astype(BF16).astype(F32))

        bias_two = lax.fori_loop(0, 4, residual_back, jnp.zeros((8, HALF), F32))
        r.sums[pl.ds(3 + 4, 1), :] = jnp.sum(bias_two, axis=0, keepdims=True)

        def act_back(buf, g, core, i, size):
            left = jnp.concatenate(
                [buf[b, rows(i, size, 2 * ROW - ROW * a), :] for a in range(3) for b in range(3)], axis=1
            )
            right = jnp.concatenate(
                [wtap(g, 3 * a + b, half_of(core)) for a in range(3) for b in range(3)], axis=1
            )
            return dot_nt(left, right)

        def conv_back(parts, buf, g):
            parts.fill(lambda i: act_back(buf, g, 1 - c, i, 2 * CHUNK))

        def conv_back_own(parts, buf, g, outer, hat):
            def own(i, carry):
                vals = act_back(buf, g, c, i, 2 * CHUNK) + parts.get(i)
                for j in range(2):
                    at = 2 * i + j
                    grad = vals[j * CHUNK : j * CHUNK + CHUNK] * outer(at)
                    r.gtmp[rows(at), :] = grad
                    carry = carry[0] + fold(grad), carry[1] + fold(grad * hat(at))
                return carry

            return own(1, own(0, (zero8, zero8)))

        def kernel_grad(act_t, buf, acc, after):
            def step(a):
                right = jnp.concatenate([buf[b, pl.ds(2 * ROW - ROW * a, PX), :] for b in range(3)], axis=1)
                out = dot(jnp.concatenate([act_t[0], act_t[1]], axis=0), right)
                for p, zc in enumerate(ALL):
                    for yy in range(2):
                        for xx in range(2):
                            row = p * 128 + yy * 48
                            tiles = [
                                out[row : row + 48, b * HALF + xx * 128 : b * HALF + xx * 128 + 128] for b in range(3)
                            ]
                            acc[a, slot(xx, yy), zc] = pack_taps(*tiles)
                after(a)

            each(3, step)

        d2 = Parts("d2")
        conv_back(d2, r.gr2, k2)
        kernel_grad(r.act2_t, r.gr2, acc2, red2.start if inside else lambda a: None)

        sums2 = conv_back_own(d2, r.gr2, k2, lambda i: silu_slope(pre2(i)), hat2)
        if inside:
            red3.second(0, 1)

        plain2, cross2, back2 = norm_back(sums2, lambda i: r.gtmp[rows(i), :], hat2, gain2 * scale, inv2)
        r.sums[pl.ds(1, 1), :] = scale * cross2
        r.sums[pl.ds(3 + 1, 1), :] = scale * plain2
        film_scale_term = gain2 * cross2 + shift2 * plain2
        r.sums[pl.ds(3 + 5, 1), :] = film_scale_term
        r.sums[pl.ds(3 + 6, 1), :] = plain2
        for j in range(2):
            r.ft[j] = film_scale_term[:, j * 128 : j * 128 + 128]
            r.ft[2 + j] = plain2[:, j * 128 : j * 128 + 128]
        head_start(lambda p: r.ft.at[p], r.th, r.th_s, r.th_r)
        r.th[h] = r.ft[h]

        def first_back(i, carry):
            vals = back2(i)
            shifted(r.gr1, i, vals)
            return carry + fold(vals.astype(BF16).astype(F32))

        bias_one = lax.fori_loop(0, 4, first_back, jnp.zeros((8, HALF), F32))
        r.sums[pl.ds(3 + 3, 1), :] = jnp.sum(bias_one, axis=0, keepdims=True)

        d1 = Parts("d1")
        if inside:
            red2.second(0, 3)
            red3.third(0, 1)
        kernel_grad(r.act1_t, r.gr1, acc1, red1.start if inside else lambda a: None)
        if inside:
            red2.third(0, 3)
        conv_back(d1, r.gr1, k1)

        head_wait(lambda p: r.ft.at[p], r.th, r.th_s, r.th_r)
        for m in range(2):
            r.fa[d, pl.ds(m, 1), :] = jnp.concatenate([r.th[2 * m], r.th[2 * m + 1]], axis=1)
        dp_start(lambda p: r.fa.at[d], r.fa, r.fa_s, r.fa_r)

        def hat1(i):
            return (mixed(i) - mean1) * inv1

        if inside:
            red1.second(0, 2)
        sums1 = conv_back_own(d1, r.gr1, k1, lambda i: silu_slope(pre1(i)), hat1)
        if inside:
            red1.second(2, 1)
            red1.third(0, 2)

        plain1, cross1, back1 = norm_back(sums1, lambda i: r.gtmp[rows(i), :], hat1, gain1, inv1)
        r.sums[pl.ds(0, 1), :] = cross1
        r.sums[pl.ds(3, 1), :] = plain1
        r.ad[d] = r.sums[...]
        dp_start(lambda p: r.ad.at[d], r.ad, r.ad_s, r.ad_r)

        keep = r.coef[0, x]

        def image_back(i):
            r.io_src[i] = pack_pixels(keep * (r.gres[rows(i), :] + back1(i))).astype(BF16)

        loop(4, image_back)
        head_start(lambda p: r.io_src.at[p], r.io_dst, r.io_s, r.io_r)
        r.io_dst[h] = r.io_src[h]
        if inside:
            red1.third(2, 1)

        dp_wait(lambda p: r.fa.at[d], r.fa, r.fa_s, r.fa_r)
        for j in range(n):
            r.fta[pl.ds(2 * j, 2), :] = r.fa[j]
        film_block = dot_tn_high(r.esel[...], r.fta[...])
        r.film[...] = jnp.concatenate([film_block[:film_rows, :BLK], film_block[:film_rows, 128 : 128 + BLK]], axis=1)
        embed_part = dot_nt_high(r.fta[...], r.wfp[...].astype(F32))
        for j in range(n):
            r.ep[j] = embed_part[2 * j : 2 * j + 2]
        dp_start(lambda p: r.ep.at[p], r.er, r.er_s, r.er_r)
        r.er[d] = r.ep[d]

        dp_wait(lambda p: r.ad.at[d], r.ad, r.ad_s, r.ad_r)
        total = r.ad[0]
        for j in range(1, n):
            total = total + r.ad[j]
        r.hb[h] = total
        head_start(lambda p: r.hb.at[h], r.hb, r.hb_s, r.hb_r)
        head_wait(lambda p: r.ro_src.at[p], r.ro_dst, r.ro_s, r.ro_r)

        dp_wait(lambda p: r.ep.at[p], r.er, r.er_s, r.er_r)
        r.eh[h] = r.er[...]
        head_start(lambda p: r.eh.at[h], r.eh, r.eh_s, r.eh_r)

        if inside:
            red2.finish(((0, 3),))
            for a in range(3):
                r.second[a] = red2.last(a)

        head_wait(lambda p: r.hb.at[h], r.hb, r.hb_s, r.hb_r)
        even = r.hb[0] + r.hb[2]
        odd = r.hb[1] + r.hb[3]
        wide = jnp.concatenate(
            [even[:, :BLK], odd[:, :BLK], even[:, 128 : 128 + BLK], odd[:, 128 : 128 + BLK]], axis=1
        )
        r.gains_out[...] = wide[0:3]
        r.biases_out[...] = wide[3:13]

        head_wait(lambda p: r.eh.at[h], r.eh, r.eh_s, r.eh_r)
        pieces = []
        for j in range(n):
            piece = (r.eh[0, j] + r.eh[1, j]) + (r.eh[2, j] + r.eh[3, j])
            pieces.append(piece[:, :film_rows])
        r.embed_grad[...] = jnp.concatenate(pieces, axis=1) * silu_slope(r.emb[...].astype(F32))

        head_wait(lambda p: r.io_src.at[p], r.io_dst, r.io_s, r.io_r)

        if inside:
            red3.finish(((0, 1),))
            tiles = unpack_four(red3.last(0))
            r.sb_src[...] = jnp.where(c == 0, tiles[2], tiles[0])
            back = rc(r.sb_src, r.sb_dst, r.sb_s.at[0], r.sb_r.at[0], sib)
            back.start()
            r.output[...] = tiles[3]
            red1.finish(((0, 2), (2, 1)))
            for a in range(3):
                r.first[a] = red1.last(a)
            back.wait()
            r.attend[:, 0:128] = jnp.where(c == 0, tiles[0], tiles[1])
            r.attend[:, 128:256] = r.sb_dst[...]
            r.attend[:, 256:384] = jnp.where(c == 0, tiles[1], tiles[2])

    return kernel


def make_writer(names_in, names_out):
    def kernel(*refs):
        count = len(names_in)
        src, dst = Names(names_in, refs[:count]), Names(names_out, refs[count:])
        for name, packed in (("result", src.ro_dst), ("image_grad", src.io_dst)):
            for m in range(2):
                getattr(dst, name)[m] = dot_nt(unpack_pixels(packed[2 * m]), src.sel[0]) + dot_nt(
                    unpack_pixels(packed[2 * m + 1]), src.sel[1]
                )
        for name in ("first", "second"):
            if name in names_out:
                for a in range(3):
                    block = getattr(src, name)[a]
                    getattr(dst, name)[3 * a] = block[:48, :BLK]
                    getattr(dst, name)[3 * a + 1] = block[48:96, :BLK]
                    getattr(dst, name)[3 * a + 2] = last_tap(block)[:, :BLK]
        if "attend" in names_out:
            dst.attend[...] = jnp.concatenate([src.attend[:, j * 128 : j * 128 + BLK] for j in range(3)], axis=1)
            dst.output[...] = src.output[:, :BLK]
        for name in ("embed_grad", "film", "gains_out", "biases_out"):
            getattr(dst, name)[...] = getattr(src, name)[...]

    return kernel


def per_device(n, *args):
    (
        images,
        noise_field,
        time_steps,
        embedding,
        first_kernel,
        second_kernel,
        film_weight,
        attend_weight,
        output_weight,
        norm_gains,
        biases,
        cotangent,
    ) = args
    inside = n == 8
    keep, noise = plan(time_steps)
    coef = jnp.stack([keep, noise])
    maps, height, width, channels = images.shape
    flat_shape = (maps, height * width, channels)
    film_rows = film_weight.shape[0]
    inputs = dict(
        coef=coef,
        images=images.reshape(flat_shape),
        noise=noise_field.reshape(flat_shape),
        cot=cotangent.reshape(flat_shape),
        emb=embedding,
        k1=first_kernel.reshape((9,) + first_kernel.shape[2:]),
        k2=second_kernel.reshape((9,) + second_kernel.shape[2:]),
        wf=film_weight,
        wa=attend_weight,
        wo=output_weight,
        gains=norm_gains,
        biases=biases,
        sel=jnp.asarray(channel_lanes(), BF16),
        gmask=jnp.asarray(group_mask(), BF16),
        selp=jnp.asarray(block_lanes(3), BF16),
    )
    shapes = dict(
        ro_dst=(4, 384, 128),
        io_dst=(4, 384, 128),
        embed_grad=embedding.shape,
        first=(3, 112, 128),
        second=(3, 112, 128),
        film=film_weight.shape,
        attend=(48, 384),
        output=(48, 128),
        gains_out=norm_gains.shape,
        biases_out=biases.shape,
    )
    names_in, names_out = list(INPUTS), list(OUTPUTS)
    core = lax.axis_index("head") % 2
    if not inside:
        def whole(array, row_axis):
            array = lax.all_gather(array, "dp", axis=row_axis, tiled=True)
            return lax.all_gather(array, "head", axis=array.ndim - 1, tiled=True)

        def spread(array, count):
            taps = array.shape[0]
            array = array.reshape(taps, 4, 2, 48, 2, 2, BLK)
            array = lax.dynamic_index_in_dim(array, core, 5, keepdims=False)
            array = jnp.transpose(array, (2, 4, 1, 0, 3, 5))
            array = jnp.pad(array, ((0, 0),) * 5 + ((0, 32),))
            return array.reshape(4, 4, taps * 48, 128)

        full_a = whole(attend_weight, 0).reshape(384, 2, 3, 2, BLK)
        full_a = jnp.transpose(full_a, (2, 0, 1, 3, 4)).reshape(3, 384, 384)
        full_o = whole(output_weight, 0)[None]
        for name, last, array in (("g1", "t1", first_kernel), ("g2", "t2", second_kernel)):
            blocks = spread(whole(array, 2).reshape(9, 384, 384), 9).reshape(4, 4, 3, 3, 48, 128)
            two = blocks[:, :, :, :2].reshape(4, 4, 3, 96, 128)
            inputs[name] = jnp.pad(two, ((0, 0),) * 3 + ((0, 16), (0, 0))).reshape(4, 4, 336, 128)
            inputs[last] = blocks[:, :, :, 2].reshape(4, 4, 144, 128)
        inputs["g3"] = spread(jnp.concatenate([full_a, full_o], axis=0), 4)
        names_in += ["g1", "g2", "t1", "t2", "g3"]
        shapes["first"] = shapes["second"] = (3, 4, 4, 112, 128)
        shapes["attend"] = (1, 4, 4, 144, 128)
        del shapes["output"]
        names_out.remove("output")
    items = scratch_list(n, inside)
    smem = pl.BlockSpec(memory_space=pltpu.SMEM)
    vmem = pl.BlockSpec(memory_space=pltpu.VMEM)
    outs = pl.pallas_call(
        make_kernel(n, inside, names_in + names_out + [name for name, _ in items]),
        out_shape=[
            jax.ShapeDtypeStruct(shapes[name], BF16 if name in ("ro_dst", "io_dst") else F32) for name in names_out
        ],
        in_specs=[smem if name == "coef" else vmem for name in names_in],
        out_specs=[vmem] * len(names_out),
        scratch_shapes=[item for _, item in items],
        compiler_params=pltpu.CompilerParams(
            collective_id=0, has_side_effects=True, vmem_limit_bytes=63 * 1024 * 1024
        ),
        name="blocks",
    )(*[inputs[name] for name in names_in])
    raw = dict(zip(names_out, outs))
    final = dict(
        result=flat_shape,
        image_grad=flat_shape,
        embed_grad=embedding.shape,
        film=film_weight.shape,
        gains_out=norm_gains.shape,
        biases_out=biases.shape,
    )
    if inside:
        final.update(first=(9, 48, BLK), second=(9, 48, BLK), attend=attend_weight.shape, output=output_weight.shape)
    names_last = [name for name in names_out if inside or name not in ("first", "second", "attend")] + ["sel"]
    names_final = list(final)
    outs = pl.pallas_call(
        make_writer(names_last, names_final),
        out_shape=[jax.ShapeDtypeStruct(final[name], F32) for name in names_final],
        in_specs=[vmem] * len(names_last),
        out_specs=[vmem] * len(names_final),
        compiler_params=pltpu.CompilerParams(vmem_limit_bytes=63 * 1024 * 1024),
        name="outputs",
    )(*[inputs["sel"] if name == "sel" else raw[name] for name in names_last])
    out = dict(zip(names_final, outs))
    if not inside:

        def blocks_of(array, size):
            parts = [array[..., k * 48 : k * 48 + 48, :BLK] for k in range(size)]
            if size == 2:
                lanes = [array[..., k * 32 : k * 32 + 32, BLK:] for k in range(3)]
                lanes = jnp.concatenate(lanes, axis=-1)
                parts.append(jnp.concatenate([lanes, array[..., 96:112, :BLK]], axis=-2))
            else:
                lanes = [array[..., k * 48 : k * 48 + 48, BLK:] for k in range(3)]
                parts.append(jnp.concatenate(lanes, axis=-1))
            array = jnp.stack(parts, axis=1)
            array = array.reshape(array.shape[:2] + (2, 2, 4, 48, BLK))
            taps = array.shape[0] * array.shape[1]
            array = jnp.transpose(array, (0, 1, 4, 2, 5, 3, 6)).reshape(taps, 384, 2, 1, BLK)
            both = jnp.concatenate([array, jnp.zeros_like(array)], axis=3)
            return jnp.where(core == 0, both, both[:, :, :, ::-1]).reshape(taps, 384, 384)

        def shared(array, axis):
            array = lax.psum_scatter(array, "head", scatter_dimension=array.ndim - 1, tiled=True)
            return lax.psum_scatter(array, "dp", scatter_dimension=axis, tiled=True)

        out["first"] = shared(blocks_of(raw["first"], 2), 1)
        out["second"] = shared(blocks_of(raw["second"], 2), 1)
        both = blocks_of(raw["attend"], 3)
        joined = both[:3].reshape(3, 384, 2, 2, BLK)
        joined = jnp.transpose(joined, (1, 2, 0, 3, 4)).reshape(384, 1152)
        out["attend"] = shared(joined, 0)
        out["output"] = shared(both[3], 0)
    return (
        out["result"].reshape(images.shape),
        out["image_grad"].reshape(images.shape),
        out["embed_grad"],
        out["first"].reshape(first_kernel.shape),
        out["second"].reshape(second_kernel.shape),
        out["film"],
        out["attend"],
        out["output"],
        out["gains_out"],
        out["biases_out"],
    )


def solution(mesh):
    n = mesh.shape["dp"]
    field = P("dp", "head", None, None)
    taps = P(None, None, "dp", "head")
    both = P("dp", "head")
    return jax.shard_map(
        lambda *args: per_device(n, *args),
        mesh=mesh,
        in_specs=(field, field, P("dp"), P("dp", None), taps, taps, both, both, both, P(), P(), field),
        out_specs=(field, field, P("dp", None), taps, taps, both, both, both, P(), P()),
        check_vma=False,
    )
```

```python
import math

import jax
import jax.numpy as jnp
import numpy as np
from jax import lax
from jax.experimental import pallas as pl
from jax.experimental.pallas import tpu as pltpu
from jax.sharding import PartitionSpec as P

HEAD_DIM = 96
GROUPS = 32
STEPS = 4000
EPS = 1e-05
OFFSET = 0.008
MESH = pl.DeviceIdType.MESH
F32 = jnp.float32
BF16 = jnp.bfloat16

PX = 1024
ROW = 32
CHUNK = 256
BLK = 96
HALF = 256
NHEAD = 4


def plan(time_steps):
    fraction = (time_steps.astype(F32) + 1.0) / STEPS
    start = jnp.square(jnp.cos(jnp.float32(OFFSET / (1.0 + OFFSET) * (math.pi / 2))))
    curve = jnp.square(jnp.cos((fraction + OFFSET) / (1.0 + OFFSET) * (math.pi / 2))) / start
    return (jnp.sqrt(curve), jnp.sqrt(1.0 - curve))


def channel_lanes():
    sel = np.zeros((2, 384, HALF), np.float32)
    for block in range(4):
        for j in range(BLK):
            sel[block % 2, block * BLK + j, (block // 2) * 128 + j] = 1.0
    return sel


def block_lanes(count):
    sel = np.zeros((count * BLK, count * 128), np.float32)
    for block in range(count):
        for j in range(BLK):
            sel[block * BLK + j, block * 128 + j] = 1.0
    return sel


def group_mask():
    lane = np.arange(HALF)
    ok = lane % 128 < BLK
    group = (lane // 128) * 100 + (lane % 128) // 12
    return ((group[:, None] == group[None, :]) & ok[:, None] & ok[None, :]).astype(np.float32)


def dot(a, b):
    return lax.dot_general(a, b, (((1,), (0,)), ((), ())), preferred_element_type=F32)


def dot_nt(a, b):
    return lax.dot_general(a, b, (((1,), (1,)), ((), ())), preferred_element_type=F32)


def dot_nt_high(a, b):
    return lax.dot_general(
        a, b, (((1,), (1,)), ((), ())), preferred_element_type=F32, precision=lax.Precision.HIGHEST
    )


def dot_tn_high(a, b):
    return lax.dot_general(
        a, b, (((0,), (0,)), ((), ())), preferred_element_type=F32, precision=lax.Precision.HIGHEST
    )


def exact_dot(values, ones):
    high = values.astype(BF16).astype(F32)
    rest = values - high
    middle = rest.astype(BF16).astype(F32)
    low = rest - middle
    rows = values.shape[0]
    out = dot(jnp.concatenate([high, middle, low], axis=0).astype(BF16), ones)
    return out[:rows] + out[rows : 2 * rows] + out[2 * rows :]


def sigmoid(v):
    return 0.5 + 0.5 * jnp.tanh(0.5 * v)


def silu(v):
    return v * sigmoid(v)


def silu_slope(v):
    s = sigmoid(v)
    return s * (1.0 + v * (1.0 - s))


def pack_taps(t0, t1, t2):
    t0, t1, t2 = t0[:, :BLK], t1[:, :BLK], t2[:, :BLK]
    join = lambda a, b: jnp.concatenate([a, b], axis=1)
    return jnp.concatenate(
        [
            join(t0[:32], t2[:32, :32]),
            join(t0[32:], t2[:16, 32:64]),
            join(t1[:16], t2[16:32, 32:64]),
            join(t1[16:], t2[:32, 64:]),
            join(t2[32:], jnp.zeros((16, 32), t2.dtype)),
        ],
        axis=0,
    )


def last_tap(packed):
    lanes = [packed[:32, BLK:], packed[32:64, BLK:], packed[64:96, BLK:], jnp.zeros((32, 32), packed.dtype)]
    return jnp.concatenate([jnp.concatenate(lanes, axis=1), packed[96:112]], axis=0)


def pack_four(b0, b1, b2, b3):
    return jnp.concatenate(
        [jnp.concatenate([b[:, :BLK], b3[:, 32 * k : 32 * k + 32]], axis=1) for k, b in enumerate((b0, b1, b2))],
        axis=0,
    )


def unpack_four(packed):
    size = packed.shape[0] // 3
    parts = [packed[k * size : k * size + size] for k in range(3)]
    zero = jnp.zeros((size, 32), packed.dtype)
    fourth = jnp.concatenate([p[:, BLK:] for p in parts] + [zero], axis=1)
    return [jnp.concatenate([p[:, :BLK], zero], axis=1) for p in parts] + [fourth]


def pack_pixels(full):
    half = CHUNK // 2
    return pack_four(full[:half, :128], full[half:, :128], full[:half, 128:], full[half:, 128:])


def unpack_pixels(packed):
    b0, b1, b2, b3 = unpack_four(packed)
    return jnp.concatenate([jnp.concatenate([b0, b2], axis=1), jnp.concatenate([b1, b3], axis=1)], axis=0)


INPUTS = (
    "coef",
    "images",
    "noise",
    "cot",
    "emb",
    "k1",
    "k2",
    "wf",
    "wa",
    "wo",
    "gains",
    "biases",
    "sel",
    "gmask",
    "selp",
)
OUTPUTS = (
    "ro_dst",
    "io_dst",
    "embed_grad",
    "first",
    "second",
    "film",
    "attend",
    "output",
    "gains_out",
    "biases_out",
)


class Names:
    def __init__(self, names, refs):
        for name, ref in zip(names, refs):
            setattr(self, name, ref)


def scratch_list(n, inside):
    dma = pltpu.SemaphoreType.DMA
    items = []

    def vm(name, shape, dtype):
        items.append((name, pltpu.VMEM(shape, dtype)))

    def sem(name, count):
        items.append((name + "_s", dma((count,))))
        items.append((name + "_r", dma((count,))))

    for name in ("mx", "cx", "ro", "io"):
        vm(name + "_src", (4, 384, 128), BF16)
        if name in ("mx", "cx"):
            vm(name + "_dst", (4, 384, 128), BF16)
            vm(name, (4, CHUNK, HALF), BF16)
        sem(name, 4)
    for name in ("act1", "act2"):
        vm(name, (2, PX + 2 * ROW, HALF), BF16)
        vm(name + "_t", (2, HALF, PX), BF16)
        sem(name, 4)
    vm("ai", (2, PX, HALF), BF16)
    vm("ai_t", (2, HALF, PX), BF16)
    sem("ai", 4)
    vm("att", (4, PX, 128), BF16)
    vm("att_t", (2, HALF, PX), BF16)
    sem("att", 2)
    for name in ("do", "n3", "d2", "d1"):
        vm(name + "_src", (PX, HALF), BF16)
        vm(name + "_dst", (PX, HALF), BF16)
        sem(name, 4)
    vm("v2", (PX, HALF), F32)
    vm("v3", (PX, HALF), F32)
    vm("gres", (PX, HALF), F32)
    vm("gtmp", (PX, HALF), F32)
    vm("qkv", (6, PX, 128), BF16)
    vm("kvt", (4, 128, PX), BF16)
    vm("dout", (2, PX, 128), BF16)
    vm("dproj", (6, PX, 128), BF16)
    vm("low", (2, 4, PX, CHUNK), BF16)
    vm("slow", (2, 4, PX, CHUNK), BF16)
    vm("got", (2, 4, 128, CHUNK), BF16)
    vm("gr2", (3, PX + 2 * ROW, HALF), BF16)
    vm("gr1", (3, PX + 2 * ROW, HALF), BF16)
    vm("par", (16, 384), F32)
    vm("parown", (16, HALF), F32)
    vm("stat", (16, HALF), F32)
    vm("sums", (16, HALF), F32)
    if inside:
        vm("g1", (4, 4, 336, 128), BF16)
        vm("g2", (4, 4, 336, 128), BF16)
        vm("t1", (4, 4, 144, 128), BF16)
        vm("t2", (4, 4, 144, 128), BF16)
        vm("p3", (4, 4, 144, 128), BF16)
        vm("g3", (4, 4, 192, 128), BF16)
        for name in ("g1", "g2", "p3"):
            sem(name + "z", 4)
            sem(name + "v", 4)
            sem(name + "w", 8)
        vm("sw_src", (48, 128), BF16)
        vm("sw_dst", (48, 128), BF16)
        sem("sw", 1)
        vm("sb_src", (48, 128), F32)
        vm("sb_dst", (48, 128), F32)
        sem("sb", 1)
        for name, nc, rows in (("r1", 3, 112), ("r2", 3, 112), ("r3", 1, 144)):
            vm(name + "_acc", (nc, 4, 4, rows, 128), F32)
            vm(name + "w_src", (nc, 2, 4, rows, 128), BF16)
            vm(name + "w_dst", (nc, 2, 4, rows, 128), BF16)
            vm(name + "v_src", (nc, 4, rows, 128), BF16)
            vm(name + "v_dst", (nc, 4, rows, 128), BF16)
            vm(name + "z_src", (4, nc, rows, 128), BF16)
            vm(name + "z_dst", (4, nc, rows, 128), BF16)
            sem(name + "w", nc)
            sem(name + "v", nc)
            sem(name + "z", nc * 4)
    vm("el", (n, 2, 768), F32)
    sem("el", n)
    vm("em", (2 * n, 768), F32)
    vm("wfp", (128, HALF), BF16)
    vm("esel", (2 * n, 128), F32)
    vm("fp", (n, 2, HALF), F32)
    vm("fr", (n, 2, HALF), F32)
    sem("fr", n)
    vm("fx", (4, 1, 128), F32)
    vm("fh", (4, 1, 128), F32)
    sem("fh", 4)
    vm("ft", (4, 1, 128), F32)
    vm("th", (4, 1, 128), F32)
    sem("th", 4)
    vm("fa", (n, 2, HALF), F32)
    sem("fa", n)
    vm("fta", (2 * n, HALF), F32)
    vm("ep", (n, 2, 128), F32)
    vm("er", (n, 2, 128), F32)
    sem("er", n)
    vm("eh", (4, n, 2, 128), F32)
    sem("eh", 4)
    vm("ad", (n, 16, HALF), F32)
    sem("ad", n)
    vm("hb", (4, 16, HALF), F32)
    sem("hb", 4)
    return items


def make_kernel(n, inside, names):
    film_rows = 768 // n

    def kernel(*refs):
        r = Names(names, refs)
        d = lax.axis_index("dp")
        h = lax.axis_index("head")
        x = h // 2
        c = h - 2 * x
        z = d // 2
        y = d - 2 * z
        sib = (d, h + 1 - 2 * c)
        xdev = (d, h + 2 - 4 * x)
        v = x + c * (y - x)
        w = y + c * (x - y)
        vdev = (d + c * (1 - 2 * y), h + (1 - c) * (2 - 4 * x))
        wdev = (d + (1 - c) * (1 - 2 * y), h + c * (2 - 4 * x))

        def slot(xx, yy):
            if inside:
                return (yy + c * (xx - yy)) * 2 + xx + c * (yy - xx)
            return yy * 2 + xx

        def rc(src, dst, send, recv, dev):
            return pltpu.make_async_remote_copy(
                src_ref=src, dst_ref=dst, send_sem=send, recv_sem=recv, device_id=dev, device_id_type=MESH
            )

        def loop(count, body):
            def step(i, carry):
                body(i)
                return carry

            lax.fori_loop(0, count, step, 0)

        def each(count, body):
            for i in range(count):
                body(i)

        def rows(i, size=CHUNK, base=0):
            return pl.ds(pl.multiple_of(base + i * size, 32), size)

        def dp_start(src_of, dst, send, recv):
            def step(k, carry):
                peer = lax.rem(d + k, n)
                rc(src_of(peer), dst.at[d], send.at[k], recv.at[d], (peer, h)).start()
                return carry

            lax.fori_loop(1, n, step, 0)

        def dp_wait(src_of, dst, send, recv):
            def step(k, carry):
                peer = lax.rem(d + k, n)
                copy = rc(src_of(peer), dst.at[peer], send.at[k], recv.at[peer], (peer, h))
                copy.wait_recv()
                copy.wait_send()
                return carry

            lax.fori_loop(1, n, step, 0)

        def head_start(src_of, dst, send, recv):
            for k in range(1, 4):
                peer = lax.rem(h + k, 4)
                rc(src_of(peer), dst.at[h], send.at[k], recv.at[h], (d, peer)).start()

        def head_wait(src_of, dst, send, recv):
            for k in range(1, 4):
                peer = lax.rem(h + k, 4)
                copy = rc(src_of(peer), dst.at[peer], send.at[k], recv.at[peer], (d, peer))
                copy.wait_recv()
                copy.wait_send()

        class Halves:
            def __init__(self, name, base):
                self.buf, self.base = getattr(r, name), base
                self.send, self.recv = getattr(r, name + "_s"), getattr(r, name + "_r")

            def at(self, core, i):
                return self.buf.at[core, rows(i, CHUNK, self.base)]

            def fill(self, make):
                def body(i):
                    self.buf[c, rows(i, CHUNK, self.base), :] = make(i)
                    ref = self.at(c, i)
                    rc(ref, ref, self.send.at[i], self.recv.at[i], sib).start()

                loop(4, body)

            def wait(self):
                for i in range(4):
                    ref = self.at(1 - c, i)
                    copy = rc(ref, ref, self.send.at[i], self.recv.at[i], sib)
                    copy.wait_recv()
                    copy.wait_send()

        class Parts:
            def __init__(self, name):
                self.src, self.dst = getattr(r, name + "_src"), getattr(r, name + "_dst")
                self.send, self.recv = getattr(r, name + "_s"), getattr(r, name + "_r")

            def copy(self, i):
                at = rows(i)
                return rc(self.src.at[at], self.dst.at[at], self.send.at[i], self.recv.at[i], sib)

            def both(self, make):
                def body(t):
                    part, i = t // 4, lax.rem(t, 4)
                    out = make(part + (1 - c) * (1 - 2 * part), i)

                    @pl.when(part == 0)
                    def _():
                        self.src[rows(i), :] = out.astype(BF16)
                        self.copy(i).start()

                    @pl.when(part == 1)
                    def _():
                        r.gtmp[rows(i), :] = out

                loop(8, body)

            def get(self, i):
                copy = self.copy(i)
                copy.wait_recv()
                copy.wait_send()
                return r.gtmp[rows(i), :] + self.dst[rows(i), :].astype(F32)

        class Gather:
            def __init__(self, name):
                self.g = getattr(r, name)
                self.zs, self.zr = getattr(r, name + "z_s"), getattr(r, name + "z_r")
                self.vs, self.vr = getattr(r, name + "v_s"), getattr(r, name + "v_r")
                self.ws, self.wr = getattr(r, name + "w_s"), getattr(r, name + "w_r")

            def zcopy(self, k):
                peer = (lax.rem(z + k, 4) * 2 + y, h)
                return rc(
                    self.g.at[w * 2 + v, 0], self.g.at[w * 2 + v, 4 - k], self.zs.at[k], self.zr.at[4 - k], peer
                )

            def vcopy(self, vv, i):
                ref = self.g.at[w * 2 + vv, i]
                return rc(ref, ref, self.vs.at[i], self.vr.at[i], vdev)

            def wcopy(self, ww, other, i):
                ref = self.g.at[ww * 2 + v + other * (1 - 2 * v), i]
                return rc(ref, ref, self.ws.at[2 * i + other], self.wr.at[2 * i + other], wdev)

            def own(self):
                for k in range(1, 4):
                    self.zcopy(k).start()
                self.vcopy(v, 0).start()
                self.wcopy(w, 0, 0).start()

            def pass_z(self):
                self.vcopy(1 - v, 0).wait_recv()
                self.wcopy(w, 1, 0).start()
                for k in range(1, 4):
                    self.zcopy(k).wait_recv()
                    self.vcopy(v, 4 - k).start()
                    self.wcopy(w, 0, 4 - k).start()

            def pass_v(self):
                for k in range(1, 4):
                    self.vcopy(1 - v, 4 - k).wait_recv()
                    self.wcopy(w, 1, 4 - k).start()

            def done(self):
                for k in range(1, 4):
                    self.zcopy(k).wait_send()
                for i in range(4):
                    self.vcopy(v, i).wait_send()
                    for other in range(2):
                        self.wcopy(1 - w, other, i).wait_recv()
                        self.wcopy(w, other, i).wait_send()

        class Reduce:
            def __init__(self, name, count):
                get = lambda tail: getattr(r, name + tail)
                self.acc, self.count = get("_acc"), count
                self.wsrc, self.wdst, self.ws, self.wr = get("w_src"), get("w_dst"), get("w_s"), get("w_r")
                self.vsrc, self.vdst, self.vs, self.vr = get("v_src"), get("v_dst"), get("v_s"), get("v_r")
                self.zsrc, self.zdst, self.zs, self.zr = get("z_src"), get("z_dst"), get("z_s"), get("z_r")

            def wcopy(self, a):
                return rc(self.wsrc.at[a], self.wdst.at[a], self.ws.at[a], self.wr.at[a], wdev)

            def vcopy(self, a, size):
                at = pl.ds(a, size)
                return rc(self.vsrc.at[at], self.vdst.at[at], self.vs.at[a], self.vr.at[a], vdev)

            def zcopy(self, a, size, k):
                at = pl.ds(a, size)
                return rc(
                    self.zsrc.at[k, at],
                    self.zdst.at[4 - k, at],
                    self.zs.at[a * 4 + k],
                    self.zr.at[a * 4 + 4 - k],
                    (lax.rem(z + k, 4) * 2 + y, h),
                )

            def start(self, a):
                def step(i, carry):
                    vv, zz = i // 4, lax.rem(i, 4)
                    self.wsrc[a, vv, zz] = self.acc[a, (1 - w) * 2 + vv, zz].astype(BF16)
                    return carry

                lax.fori_loop(0, 8, step, 0)
                self.wcopy(a).start()

            def second(self, first, size):
                for a in range(first, first + size):
                    self.wcopy(a).wait_recv()

                    def step(zz, carry):
                        self.vsrc[a, zz] = (
                            self.acc[a, w * 2 + 1 - v, zz] + self.wdst[a, 1 - v, zz].astype(F32)
                        ).astype(BF16)
                        return carry

                    lax.fori_loop(0, 4, step, 0)
                self.vcopy(first, size).start()

            def third(self, first, size):
                self.vcopy(first, size).wait_recv()
                for a in range(first, first + size):

                    def step(k, carry):
                        zz = lax.rem(z + k, 4)
                        total = (
                            self.acc[a, w * 2 + v, zz]
                            + self.wdst[a, v, zz].astype(F32)
                            + self.vdst[a, zz].astype(F32)
                        )
                        self.acc[a, w * 2 + v, zz] = total
                        self.zsrc[k, a] = total.astype(BF16)
                        return carry

                    lax.fori_loop(0, 4, step, 0)
                for k in range(1, 4):
                    self.zcopy(first, size, k).start()

            def finish(self, groups):
                for first, size in groups:
                    self.vcopy(first, size).wait_send()
                    for k in range(1, 4):
                        copy = self.zcopy(first, size, k)
                        copy.wait_recv()
                        copy.wait_send()
                for a in range(self.count):
                    self.wcopy(a).wait_send()

            def last(self, a):
                total = self.acc[a, w * 2 + v, z]
                for k in range(1, 4):
                    total = total + self.zdst[k, a].astype(F32)
                return total

        def rel(zc):
            return lax.rem(zc - z + 4, 4) if inside else zc

        class Taps:
            def __init__(self, packed, last):
                self.packed, self.last = packed, last

            def block(self, tap, zc, xx, yy):
                a, b = tap // 3, tap % 3
                if b < 2:
                    return self.packed[slot(xx, yy), rel(zc), pl.ds(a * 112 + b * 48, 48), :]
                return self.last[slot(xx, yy), rel(zc), pl.ds(a * 48, 48), :]

            def unpack(self):
                def step(i, carry):
                    q, zz = i // 4, lax.rem(i, 4)
                    for a in range(3):
                        self.last[q, zz, pl.ds(a * 48, 48), :] = last_tap(
                            self.packed[q, zz, pl.ds(a * 112, 112), :]
                        )
                    return carry

                lax.fori_loop(0, 16, step, 0)

        class Plain:
            def __init__(self, blocks):
                self.blocks = blocks

            def block(self, tap, zc, xx, yy):
                return self.blocks[slot(xx, yy), rel(zc), pl.ds(tap * 48, 48), :]

            def unpack(self):
                def step(i, carry):
                    q, zz = i // 4, lax.rem(i, 4)
                    self.blocks[q, zz] = jnp.concatenate(unpack_four(r.p3[q, zz]), axis=0)
                    return carry

                lax.fori_loop(0, 16, step, 0)

        k1, k2, k3 = Taps(r.g1, r.t1), Taps(r.g2, r.t2), Plain(r.g3)

        def wtile(g, tap, zc, xx):
            return jnp.concatenate(
                [g.block(tap, zc, xx, 0), g.block(tap, zc, xx, 1), jnp.zeros((32, 128), BF16)], axis=0
            )

        def wtap(g, tap, zcs):
            return jnp.concatenate(
                [jnp.concatenate([wtile(g, tap, zc, xx) for xx in range(2)], axis=1) for zc in zcs], axis=0
            )

        ALL = (0, 2, 1, 3)

        def half_of(core):
            return (core, core + 2)

        def wproj(zcs):
            return jnp.concatenate(
                [
                    jnp.concatenate([wtile(k3, j, zc, xx) for xx in range(2) for j in range(3)], axis=1)
                    for zc in zcs
                ],
                axis=0,
            )

        def flat(buf, base, i, size):
            return jnp.concatenate([buf[0, rows(i, size, base), :], buf[1, rows(i, size, base), :]], axis=1)

        barrier = pltpu.get_barrier_semaphore()

        def greet(k, carry):
            pl.semaphore_signal(barrier, inc=1, device_id=(lax.rem(d + k, n), h), device_id_type=MESH)
            return carry

        lax.fori_loop(1, n, greet, 0)
        for k in range(1, 4):
            pl.semaphore_signal(barrier, inc=1, device_id=(d, lax.rem(h + k, 4)), device_id_type=MESH)
        if inside:
            for a in range(3):
                r.g1[w * 2 + v, 0, pl.ds(a * 112, 112), :] = pack_taps(*[r.k1[3 * a + b] for b in range(3)])
        pl.semaphore_wait(barrier, n - 1 + 3)
        if inside:
            ga, gb, gc = Gather("g1"), Gather("g2"), Gather("p3")
            ga.own()

        def mix(m, carry):
            field = r.coef[0, m] * r.images[m].astype(F32) + r.coef[1, m] * r.noise[m].astype(F32)
            low = field.astype(BF16)
            for core in range(2):
                r.mx_src[m * 2 + core] = pack_pixels(dot(low, r.sel[core])).astype(BF16)
            return carry

        lax.fori_loop(0, 2, mix, 0)
        head_start(lambda p: r.mx_src.at[p], r.mx_dst, r.mx_s, r.mx_r)
        r.mx_dst[h] = r.mx_src[h]

        r.el[d] = silu(r.emb[...].astype(F32)).astype(BF16).astype(F32)
        dp_start(lambda p: r.el.at[d], r.el, r.el_s, r.el_r)

        if inside:
            blocks = dot(r.wa[...], r.selp[: 3 * BLK, : 3 * 128]).astype(BF16)
            r.sw_src[...] = blocks[:, 128:256]
            swap = rc(r.sw_src, r.sw_dst, r.sw_s.at[0], r.sw_r.at[0], sib)
            swap.start()
            for a in range(3):
                r.g2[w * 2 + v, 0, pl.ds(a * 112, 112), :] = pack_taps(*[r.k2[3 * a + b] for b in range(3)])
        r.par[0:3, :] = r.gains[...]
        r.par[3:13, :] = r.biases[...]
        r.par[13:16, :] = jnp.zeros((3, 384), F32)
        r.parown[...] = exact_dot(r.par[...], r.sel[c])

        def prow(i):
            return r.parown[pl.ds(i, 1), :]

        for buf in (r.act1, r.act2):
            for core in range(2):
                buf[core, pl.ds(0, ROW), :] = jnp.zeros((ROW, HALF), BF16)
                buf[core, pl.ds(PX + ROW, ROW), :] = jnp.zeros((ROW, HALF), BF16)
        for buf in (r.gr1, r.gr2):
            for b in range(3):
                buf[b, pl.ds(0, ROW), :] = jnp.zeros((ROW, HALF), BF16)
                buf[b, pl.ds(PX + ROW, ROW), :] = jnp.zeros((ROW, HALF), BF16)
        r.wfp[...] = jnp.zeros((128, HALF), BF16)
        r.wfp[pl.ds(0, film_rows), :] = dot(r.wf[...], r.selp[: 2 * BLK, :HALF]).astype(BF16)
        if inside:
            ga.pass_z()
            gb.own()

        count = float(PX * 12)

        def fold(vals):
            return jnp.sum(vals.reshape(CHUNK // 8, 8, HALF), axis=0)

        def sums_of(fn, k):
            def step(i, carry):
                return tuple(a + fold(b) for a, b in zip(carry, fn(i)))

            zero = jnp.zeros((8, HALF), F32)
            return lax.fori_loop(0, 4, step, (zero,) * k)

        def group_mean(part):
            return jnp.sum(exact_dot(part, r.gmask[...]), axis=0, keepdims=True) / count

        def norm(load, which, total):
            mean = group_mean(total)
            (square,) = sums_of(lambda i: (jnp.square(load(i) - mean),), 1)
            inv = lax.rsqrt(group_mean(square) + EPS)
            r.stat[pl.ds(2 * which, 1), :] = mean
            r.stat[pl.ds(2 * which + 1, 1), :] = inv
            return mean, inv

        zero8 = jnp.zeros((8, HALF), F32)

        def norm_back(sums, load_grad, load_hat, coef, inv):
            plain, cross = sums
            plain_mean, cross_mean = group_mean(coef * plain), group_mean(coef * cross)
            outer, base, slope = inv * coef, inv * plain_mean, inv * cross_mean

            def chunk(i):
                return outer * load_grad(i) - base - load_hat(i) * slope

            return (
                jnp.sum(plain, axis=0, keepdims=True),
                jnp.sum(cross, axis=0, keepdims=True),
                chunk,
            )

        head_wait(lambda p: r.mx_src.at[p], r.mx_dst, r.mx_s, r.mx_r)

        def unpack_mixed(i, carry):
            vals = unpack_pixels(r.mx_dst[i])
            r.mx[i] = vals
            return carry + fold(vals.astype(F32))

        mixed_sum = lax.fori_loop(0, 4, unpack_mixed, zero8)

        def mixed(i):
            return r.mx[i].astype(F32)

        mean1, inv1 = norm(mixed, 0, mixed_sum)
        gain1, shift1 = prow(0), prow(3)
        act1 = Halves("act1", ROW)

        def affine(mean, inv, gain, shift):
            return inv * gain, shift - mean * (inv * gain)

        mul1, add1 = affine(mean1, inv1, gain1, shift1)

        def pre1(i):
            return mixed(i) * mul1 + add1

        act1.fill(lambda i: silu(pre1(i)).astype(BF16))
        if inside:
            ga.pass_v()

        dp_wait(lambda p: r.el.at[d], r.el, r.el_s, r.el_r)
        for j in range(n):
            r.em[pl.ds(2 * j, 2), :] = r.el[j]
        place = lax.broadcasted_iota(jnp.int32, (768, 128), 0) - film_rows * d
        lane = lax.broadcasted_iota(jnp.int32, (768, 128), 1)
        pick = jnp.where((place == lane) & (lane < film_rows), 1.0, 0.0).astype(BF16)
        r.esel[...] = dot(r.em[...].astype(BF16), pick)
        film_part = dot(r.esel[...].astype(BF16), r.wfp[...])
        for j in range(n):
            r.fp[j] = film_part[2 * j : 2 * j + 2]
        dp_start(lambda p: r.fp.at[p], r.fr, r.fr_s, r.fr_r)
        r.fr[d] = r.fp[d]
        if inside:
            swap.wait()
            got = r.sw_dst[...]
            keep0, keep2 = blocks[:, :128], blocks[:, 256:]
            r.p3[w * 2 + v, 0] = pack_four(
                jnp.where(c == 0, keep0, got),
                jnp.where(c == 0, keep2, keep0),
                jnp.where(c == 0, got, keep2),
                r.wo[...],
            )
            gb.pass_z()
            gc.own()
        def split_cot(m, carry):
            for core in range(2):
                r.cx_src[m * 2 + core] = pack_pixels(dot(r.cot[m], r.sel[core])).astype(BF16)
            return carry

        lax.fori_loop(0, 2, split_cot, 0)
        head_start(lambda p: r.cx_src.at[p], r.cx_dst, r.cx_s, r.cx_r)
        r.cx_dst[h] = r.cx_src[h]

        column = lax.broadcasted_iota(jnp.int32, (1, ROW, HALF), 1)
        not_first = jnp.where(column > 0, 1.0, 0.0)
        not_last = jnp.where(column < ROW - 1, 1.0, 0.0)

        def in_rows(vals, mask):
            return (vals.reshape(CHUNK // ROW, ROW, HALF) * mask).reshape(CHUNK, HALF)

        def from_left(vals):
            return in_rows(pltpu.roll(vals, 1, 0), not_first)

        def from_right(vals):
            return in_rows(pltpu.roll(vals, CHUNK - 1, 0), not_last)

        def transpose_act(buf, base, out):
            def step(core):
                for q in range(4):
                    out[core, :, pl.ds(q * CHUNK, CHUNK)] = jnp.transpose(
                        buf[core, pl.ds(base + q * CHUNK, CHUNK), :]
                    )

            loop(2, step)

        def conv(buf, g, store, between):
            weights = lambda: jnp.concatenate(
                [jnp.concatenate([wtap(g, 3 * a + b, ALL) for b in range(3)], axis=1) for a in range(3)], axis=0
            )

            def step(i, total):
                left = jnp.concatenate([flat(buf, ROW * a, i, CHUNK) for a in range(3)], axis=1)
                part = dot(left, weights())
                part = part[:, HALF : 2 * HALF] + from_left(part[:, :HALF]) + from_right(part[:, 2 * HALF :])
                total = total + fold(store(i, part))
                pl.when(i == 1)(between)
                return total

            return lax.fori_loop(0, 4, step, zero8)

        act1.wait()
        transpose_act(r.act1, ROW, r.act1_t)
        if inside:
            ga.done()
            k1.unpack()

        def store_v2(i, vals):
            vals = vals + prow(6)
            r.v2[rows(i), :] = vals
            return vals

        v2_sum = conv(r.act1, k1, store_v2, gb.pass_v if inside else lambda: None)
        dp_wait(lambda p: r.fp.at[p], r.fr, r.fr_s, r.fr_r)
        film_sum = r.fr[0]
        for j in range(1, n):
            film_sum = film_sum + r.fr[j]
        for m in range(2):
            for core in range(2):
                r.fx[m * 2 + core] = film_sum[m : m + 1, core * 128 : core * 128 + 128]
        head_start(lambda p: r.fx.at[p], r.fh, r.fh_s, r.fh_r)
        r.fh[h] = r.fx[h]

        head_wait(lambda p: r.fx.at[p], r.fh, r.fh_s, r.fh_r)
        scale = 1.0 + (jnp.concatenate([r.fh[0], r.fh[1]], axis=1) + prow(8))
        shift = jnp.concatenate([r.fh[2], r.fh[3]], axis=1) + prow(9)
        mean2, inv2 = norm(lambda i: r.v2[rows(i), :], 1, v2_sum)
        gain2, shift2 = prow(1), prow(4)
        act2 = Halves("act2", ROW)

        def hat2(i):
            return (r.v2[rows(i), :] - mean2) * inv2

        mul2, add2 = affine(mean2, inv2, gain2 * scale, shift2 * scale + shift)

        def pre2(i):
            return r.v2[rows(i), :] * mul2 + add2

        act2.fill(lambda i: silu(pre2(i)).astype(BF16))
        if inside:
            gc.pass_z()

        act2.wait()
        transpose_act(r.act2, ROW, r.act2_t)
        if inside:
            gb.done()
            k2.unpack()

        def store_v3(i, vals):
            vals = mixed(i) + (vals + prow(7))
            r.v3[rows(i), :] = vals
            return vals

        v3_sum = conv(r.act2, k2, store_v3, gc.pass_v if inside else lambda: None)
        mean3, inv3 = norm(lambda i: r.v3[rows(i), :], 2, v3_sum)
        gain3, shift3 = prow(2), prow(5)
        ai = Halves("ai", 0)

        def hat3(i):
            return (r.v3[rows(i), :] - mean3) * inv3

        mul3, add3 = affine(mean3, inv3, gain3, shift3)
        ai.fill(lambda i: (r.v3[rows(i), :] * mul3 + add3).astype(BF16))

        if inside:
            gc.done()
            k3.unpack()
        head_wait(lambda p: r.cx_src.at[p], r.cx_dst, r.cx_s, r.cx_r)

        def unpack_cot(i):
            r.cx[i] = unpack_pixels(r.cx_dst[i])

        loop(4, unpack_cot)
        dop = Parts("do")

        dop.both(lambda core, i: dot_nt(r.cx[i], wtap(k3, 3, half_of(core))))

        ai.wait()
        bias_proj = [prow(10)[:, :128], prow(10)[:, 128:], None, None, prow(11)[:, :128], prow(11)[:, 128:]]

        def project(i):
            out = dot(flat(r.ai, 0, i, CHUNK), wproj(ALL))
            for k in range(6):
                part = out[:, k * 128 : k * 128 + 128]
                if bias_proj[k] is not None:
                    part = part + bias_proj[k]
                r.qkv[k, rows(i), :] = part.astype(BF16)

        loop(4, project)

        def do_own(i):
            full = dop.get(i).astype(BF16)
            for k in range(2):
                r.dout[k, rows(i), :] = full[:, k * 128 : k * 128 + 128]

        loop(4, do_own)

        factor = 1.0 / math.sqrt(HEAD_DIM)
        factor2 = factor * math.log2(math.e)
        att = []

        def transposes(k):
            r.kvt[k] = jnp.transpose(r.qkv[k + 2])

        loop(4, transposes)

        def att_copies(core):
            for i, ref in enumerate((r.att.at[pl.ds(core * 2, 2)], r.att_t.at[core])):
                yield rc(ref, ref, r.att_s.at[i], r.att_r.at[i], sib)

        def one_block(t):
            k, b = t // 4, lax.rem(t, 4)
            query = r.qkv[k, rows(b), :]
            grad = r.dout[k, rows(b), :]
            scores = dot_nt(r.qkv[2 + k], query)
            peak = jnp.max(scores, axis=0, keepdims=True)
            expo = jnp.exp2((scores - peak) * factor2)
            inverse = 1.0 / jnp.sum(expo, axis=0, keepdims=True)
            low = (expo * inverse).astype(BF16)
            r.low[k, b] = low
            got = dot(r.kvt[2 + k], low)
            got_low = got.astype(BF16)
            r.got[k, b] = got_low
            r.att[2 * c + k, rows(b), :] = jnp.transpose(got_low)
            spread = jnp.sum(got * jnp.transpose(grad).astype(F32), axis=0, keepdims=True)
            probs_grad = dot_nt(r.qkv[4 + k], grad)
            scores_grad = ((probs_grad - spread) * inverse * expo).astype(BF16)
            r.slow[k, b] = scores_grad
            back = dot(r.kvt[k], scores_grad)
            r.dproj[k, rows(b), :] = (jnp.transpose(back) * factor).astype(BF16)

        loop(8, one_block)
        for k in range(2):
            for b in range(4):
                r.att_t[c, pl.ds(k * 128, 128), pl.ds(b * CHUNK, CHUNK)] = r.got[k, b]

        def over_queries(t):
            k, i = t // 4, lax.rem(t, 4)
            lows = jnp.concatenate([r.low[k, b, rows(i), :] for b in range(4)], axis=1)
            grads = jnp.concatenate([r.slow[k, b, rows(i), :] for b in range(4)], axis=1)
            r.dproj[4 + k, rows(i), :] = dot(lows, r.dout[k]).astype(BF16)
            r.dproj[2 + k, rows(i), :] = (dot(grads, r.qkv[k]) * factor).astype(BF16)

        for copy in att_copies(c):
            copy.start()
        loop(8, over_queries)

        n3 = Parts("n3")

        def proj_rows(i):
            return jnp.concatenate([r.dproj[k, rows(i), :] for k in range(6)], axis=1)

        n3.both(lambda core, i: dot_nt(proj_rows(i), wproj(half_of(core))))

        for copy in att_copies(1 - c):
            copy.wait_recv()
            copy.wait_send()

        def result(i):
            left = jnp.concatenate([r.att[p, rows(i), :] for p in range(4)], axis=1)
            branch = dot(left, wtap(k3, 3, ALL)) + prow(12)
            r.ro_src[i] = pack_pixels(r.v3[rows(i), :] + branch).astype(BF16)

        loop(4, result)
        head_start(lambda p: r.ro_src.at[p], r.ro_dst, r.ro_s, r.ro_r)
        r.ro_dst[h] = r.ro_src[h]

        if inside:
            red1, red2, red3 = Reduce("r1", 3), Reduce("r2", 3), Reduce("r3", 1)
            acc1, acc2, acc3 = r.r1_acc, r.r2_acc, r.r3_acc
        else:
            acc1, acc2, acc3 = r.first, r.second, r.attend

        transpose_act(r.ai, 0, r.ai_t)
        right = lambda: jnp.concatenate([r.dproj[k] for k in range(6)], axis=1)
        cot_all = lambda: jnp.concatenate([r.cx[i] for i in range(4)], axis=0)

        def attend_grads(core):
            attend_out = dot(r.ai_t[core], right())
            output_out = dot(r.att_t[core], cot_all())
            for k in range(2):
                for yy in range(2):
                    for xx in range(2):
                        row = k * 128 + yy * 48
                        tiles = [
                            attend_out[row : row + 48, (xx * 3 + j) * 128 : (xx * 3 + j) * 128 + 128] for j in range(3)
                        ]
                        acc3[0, slot(xx, yy), core + 2 * k] = pack_four(
                            *tiles, output_out[row : row + 48, xx * 128 : xx * 128 + 128]
                        )

        loop(2, attend_grads)
        if inside:
            red3.start(0)

        def proj_sums(i, carry):
            q = jnp.concatenate([r.dproj[0, rows(i), :], r.dproj[1, rows(i), :]], axis=1).astype(F32)
            val = jnp.concatenate([r.dproj[4, rows(i), :], r.dproj[5, rows(i), :]], axis=1).astype(F32)
            return (carry[0] + fold(q), carry[1] + fold(val), carry[2] + fold(r.cx[i].astype(F32)))

        qsum, vsum, csum = lax.fori_loop(0, 4, proj_sums, (zero8, zero8, zero8))
        r.sums[pl.ds(3 + 7, 1), :] = jnp.sum(qsum, axis=0, keepdims=True)
        r.sums[pl.ds(3 + 8, 1), :] = jnp.sum(vsum, axis=0, keepdims=True)
        r.sums[pl.ds(3 + 9, 1), :] = jnp.sum(csum, axis=0, keepdims=True)
        r.sums[pl.ds(13, 3), :] = jnp.zeros((3, HALF), F32)

        def n3_own(i, carry):
            vals = n3.get(i)
            r.gtmp[rows(i), :] = vals
            return carry[0] + fold(vals), carry[1] + fold(vals * hat3(i))

        sums3 = lax.fori_loop(0, 4, n3_own, (zero8, zero8))
        plain3, cross3, back3 = norm_back(sums3, lambda i: r.gtmp[rows(i), :], hat3, gain3, inv3)
        r.sums[pl.ds(2, 1), :] = cross3
        r.sums[pl.ds(3 + 2, 1), :] = plain3

        def shifted(buf, i, vals):
            buf[0, rows(i, CHUNK, ROW), :] = from_right(vals).astype(BF16)
            buf[1, rows(i, CHUNK, ROW), :] = vals.astype(BF16)
            buf[2, rows(i, CHUNK, ROW), :] = from_left(vals).astype(BF16)

        def residual_back(i, carry):
            vals = r.cx[i].astype(F32) + back3(i)
            r.gres[rows(i), :] = vals
            shifted(r.gr2, i, vals)
            return carry + fold(vals.astype(BF16).astype(F32))

        bias_two = lax.fori_loop(0, 4, residual_back, jnp.zeros((8, HALF), F32))
        r.sums[pl.ds(3 + 4, 1), :] = jnp.sum(bias_two, axis=0, keepdims=True)

        def act_back(buf, g, core, i, size):
            left = jnp.concatenate(
                [buf[b, rows(i, size, 2 * ROW - ROW * a), :] for a in range(3) for b in range(3)], axis=1
            )
            right = jnp.concatenate(
                [wtap(g, 3 * a + b, half_of(core)) for a in range(3) for b in range(3)], axis=1
            )
            return dot_nt(left, right)

        def conv_back(parts, buf, g):
            parts.both(lambda core, i: act_back(buf, g, core, i, CHUNK))

        def conv_back_own(parts, outer, hat):
            def own(i, carry):
                grad = parts.get(i) * outer(i)
                r.gtmp[rows(i), :] = grad
                return carry[0] + fold(grad), carry[1] + fold(grad * hat(i))

            return lax.fori_loop(0, 4, own, (zero8, zero8))

        def kernel_grad(act_t, buf, acc, after):
            def step(t):
                a, core = t // 2, lax.rem(t, 2)
                at = pl.ds(pl.multiple_of(2 * ROW - ROW * a, 32), PX)
                out = dot(act_t[core], jnp.concatenate([buf[b, at, :] for b in range(3)], axis=1))
                for k in range(2):
                    for yy in range(2):
                        for xx in range(2):
                            row = k * 128 + yy * 48
                            tiles = [
                                out[row : row + 48, b * HALF + xx * 128 : b * HALF + xx * 128 + 128] for b in range(3)
                            ]
                            acc[a, slot(xx, yy), core + 2 * k] = pack_taps(*tiles)
                pl.when(core == 1)(lambda: after(a))

            loop(6, step)

        d2 = Parts("d2")
        conv_back(d2, r.gr2, k2)
        kernel_grad(r.act2_t, r.gr2, acc2, red2.start if inside else lambda a: None)

        sums2 = conv_back_own(d2, lambda i: silu_slope(pre2(i)), hat2)
        if inside:
            red3.second(0, 1)

        plain2, cross2, back2 = norm_back(sums2, lambda i: r.gtmp[rows(i), :], hat2, gain2 * scale, inv2)
        r.sums[pl.ds(1, 1), :] = scale * cross2
        r.sums[pl.ds(3 + 1, 1), :] = scale * plain2
        film_scale_term = gain2 * cross2 + shift2 * plain2
        r.sums[pl.ds(3 + 5, 1), :] = film_scale_term
        r.sums[pl.ds(3 + 6, 1), :] = plain2
        for j in range(2):
            r.ft[j] = film_scale_term[:, j * 128 : j * 128 + 128]
            r.ft[2 + j] = plain2[:, j * 128 : j * 128 + 128]
        head_start(lambda p: r.ft.at[p], r.th, r.th_s, r.th_r)
        r.th[h] = r.ft[h]

        def first_back(i, carry):
            vals = back2(i)
            shifted(r.gr1, i, vals)
            return carry + fold(vals.astype(BF16).astype(F32))

        bias_one = lax.fori_loop(0, 4, first_back, jnp.zeros((8, HALF), F32))
        r.sums[pl.ds(3 + 3, 1), :] = jnp.sum(bias_one, axis=0, keepdims=True)

        d1 = Parts("d1")
        if inside:
            red2.second(0, 3)
            red3.third(0, 1)
        kernel_grad(r.act1_t, r.gr1, acc1, red1.start if inside else lambda a: None)
        if inside:
            red2.third(0, 3)
        conv_back(d1, r.gr1, k1)

        head_wait(lambda p: r.ft.at[p], r.th, r.th_s, r.th_r)
        for m in range(2):
            r.fa[d, pl.ds(m, 1), :] = jnp.concatenate([r.th[2 * m], r.th[2 * m + 1]], axis=1)
        dp_start(lambda p: r.fa.at[d], r.fa, r.fa_s, r.fa_r)

        def hat1(i):
            return (mixed(i) - mean1) * inv1

        if inside:
            red1.second(0, 2)
        sums1 = conv_back_own(d1, lambda i: silu_slope(pre1(i)), hat1)
        if inside:
            red1.second(2, 1)
            red1.third(0, 2)

        plain1, cross1, back1 = norm_back(sums1, lambda i: r.gtmp[rows(i), :], hat1, gain1, inv1)
        r.sums[pl.ds(0, 1), :] = cross1
        r.sums[pl.ds(3, 1), :] = plain1
        r.ad[d] = r.sums[...]
        dp_start(lambda p: r.ad.at[d], r.ad, r.ad_s, r.ad_r)

        keep = r.coef[0, x]

        def image_back(i):
            r.io_src[i] = pack_pixels(keep * (r.gres[rows(i), :] + back1(i))).astype(BF16)

        loop(4, image_back)
        head_start(lambda p: r.io_src.at[p], r.io_dst, r.io_s, r.io_r)
        r.io_dst[h] = r.io_src[h]
        if inside:
            red1.third(2, 1)

        dp_wait(lambda p: r.fa.at[d], r.fa, r.fa_s, r.fa_r)
        for j in range(n):
            r.fta[pl.ds(2 * j, 2), :] = r.fa[j]
        film_block = dot_tn_high(r.esel[...], r.fta[...])
        r.film[...] = jnp.concatenate([film_block[:film_rows, :BLK], film_block[:film_rows, 128 : 128 + BLK]], axis=1)
        embed_part = dot_nt_high(r.fta[...], r.wfp[...].astype(F32))
        for j in range(n):
            r.ep[j] = embed_part[2 * j : 2 * j + 2]
        dp_start(lambda p: r.ep.at[p], r.er, r.er_s, r.er_r)
        r.er[d] = r.ep[d]

        dp_wait(lambda p: r.ad.at[d], r.ad, r.ad_s, r.ad_r)
        total = r.ad[0]
        for j in range(1, n):
            total = total + r.ad[j]
        r.hb[h] = total
        head_start(lambda p: r.hb.at[h], r.hb, r.hb_s, r.hb_r)
        head_wait(lambda p: r.ro_src.at[p], r.ro_dst, r.ro_s, r.ro_r)

        dp_wait(lambda p: r.ep.at[p], r.er, r.er_s, r.er_r)
        r.eh[h] = r.er[...]
        head_start(lambda p: r.eh.at[h], r.eh, r.eh_s, r.eh_r)

        if inside:
            red2.finish(((0, 3),))
            for a in range(3):
                r.second[a] = red2.last(a)

        head_wait(lambda p: r.hb.at[h], r.hb, r.hb_s, r.hb_r)
        even = r.hb[0] + r.hb[2]
        odd = r.hb[1] + r.hb[3]
        wide = jnp.concatenate(
            [even[:, :BLK], odd[:, :BLK], even[:, 128 : 128 + BLK], odd[:, 128 : 128 + BLK]], axis=1
        )
        r.gains_out[...] = wide[0:3]
        r.biases_out[...] = wide[3:13]

        head_wait(lambda p: r.eh.at[h], r.eh, r.eh_s, r.eh_r)
        pieces = []
        for j in range(n):
            piece = (r.eh[0, j] + r.eh[1, j]) + (r.eh[2, j] + r.eh[3, j])
            pieces.append(piece[:, :film_rows])
        r.embed_grad[...] = jnp.concatenate(pieces, axis=1) * silu_slope(r.emb[...].astype(F32))

        head_wait(lambda p: r.io_src.at[p], r.io_dst, r.io_s, r.io_r)

        if inside:
            red3.finish(((0, 1),))
            tiles = unpack_four(red3.last(0))
            r.sb_src[...] = jnp.where(c == 0, tiles[2], tiles[0])
            back = rc(r.sb_src, r.sb_dst, r.sb_s.at[0], r.sb_r.at[0], sib)
            back.start()
            r.output[...] = tiles[3]
            red1.finish(((0, 2), (2, 1)))
            for a in range(3):
                r.first[a] = red1.last(a)
            back.wait()
            r.attend[:, 0:128] = jnp.where(c == 0, tiles[0], tiles[1])
            r.attend[:, 128:256] = r.sb_dst[...]
            r.attend[:, 256:384] = jnp.where(c == 0, tiles[1], tiles[2])

    return kernel


def make_writer(names_in, names_out):
    def kernel(*refs):
        count = len(names_in)
        src, dst = Names(names_in, refs[:count]), Names(names_out, refs[count:])
        for name, packed in (("result", src.ro_dst), ("image_grad", src.io_dst)):
            for m in range(2):
                getattr(dst, name)[m] = dot_nt(unpack_pixels(packed[2 * m]), src.sel[0]) + dot_nt(
                    unpack_pixels(packed[2 * m + 1]), src.sel[1]
                )
        for name in ("first", "second"):
            if name in names_out:
                for a in range(3):
                    block = getattr(src, name)[a]
                    getattr(dst, name)[3 * a] = block[:48, :BLK]
                    getattr(dst, name)[3 * a + 1] = block[48:96, :BLK]
                    getattr(dst, name)[3 * a + 2] = last_tap(block)[:, :BLK]
        if "attend" in names_out:
            dst.attend[...] = jnp.concatenate([src.attend[:, j * 128 : j * 128 + BLK] for j in range(3)], axis=1)
            dst.output[...] = src.output[:, :BLK]
        for name in ("embed_grad", "film", "gains_out", "biases_out"):
            getattr(dst, name)[...] = getattr(src, name)[...]

    return kernel


def per_device(n, *args):
    (
        images,
        noise_field,
        time_steps,
        embedding,
        first_kernel,
        second_kernel,
        film_weight,
        attend_weight,
        output_weight,
        norm_gains,
        biases,
        cotangent,
    ) = args
    inside = n == 8
    keep, noise = plan(time_steps)
    coef = jnp.stack([keep, noise])
    maps, height, width, channels = images.shape
    flat_shape = (maps, height * width, channels)
    film_rows = film_weight.shape[0]
    inputs = dict(
        coef=coef,
        images=images.reshape(flat_shape),
        noise=noise_field.reshape(flat_shape),
        cot=cotangent.reshape(flat_shape),
        emb=embedding,
        k1=first_kernel.reshape((9,) + first_kernel.shape[2:]),
        k2=second_kernel.reshape((9,) + second_kernel.shape[2:]),
        wf=film_weight,
        wa=attend_weight,
        wo=output_weight,
        gains=norm_gains,
        biases=biases,
        sel=jnp.asarray(channel_lanes(), BF16),
        gmask=jnp.asarray(group_mask(), BF16),
        selp=jnp.asarray(block_lanes(3), BF16),
    )
    shapes = dict(
        ro_dst=(4, 384, 128),
        io_dst=(4, 384, 128),
        embed_grad=embedding.shape,
        first=(3, 112, 128),
        second=(3, 112, 128),
        film=film_weight.shape,
        attend=(48, 384),
        output=(48, 128),
        gains_out=norm_gains.shape,
        biases_out=biases.shape,
    )
    names_in, names_out = list(INPUTS), list(OUTPUTS)
    core = lax.axis_index("head") % 2
    if not inside:
        def whole(array, row_axis):
            array = lax.all_gather(array, "dp", axis=row_axis, tiled=True)
            return lax.all_gather(array, "head", axis=array.ndim - 1, tiled=True)

        def spread(array, count):
            taps = array.shape[0]
            array = array.reshape(taps, 4, 2, 48, 2, 2, BLK)
            array = lax.dynamic_index_in_dim(array, core, 5, keepdims=False)
            array = jnp.transpose(array, (2, 4, 1, 0, 3, 5))
            array = jnp.pad(array, ((0, 0),) * 5 + ((0, 32),))
            return array.reshape(4, 4, taps * 48, 128)

        full_a = whole(attend_weight, 0).reshape(384, 2, 3, 2, BLK)
        full_a = jnp.transpose(full_a, (2, 0, 1, 3, 4)).reshape(3, 384, 384)
        full_o = whole(output_weight, 0)[None]
        for name, last, array in (("g1", "t1", first_kernel), ("g2", "t2", second_kernel)):
            blocks = spread(whole(array, 2).reshape(9, 384, 384), 9).reshape(4, 4, 3, 3, 48, 128)
            two = blocks[:, :, :, :2].reshape(4, 4, 3, 96, 128)
            inputs[name] = jnp.pad(two, ((0, 0),) * 3 + ((0, 16), (0, 0))).reshape(4, 4, 336, 128)
            inputs[last] = blocks[:, :, :, 2].reshape(4, 4, 144, 128)
        inputs["g3"] = spread(jnp.concatenate([full_a, full_o], axis=0), 4)
        names_in += ["g1", "g2", "t1", "t2", "g3"]
        shapes["first"] = shapes["second"] = (3, 4, 4, 112, 128)
        shapes["attend"] = (1, 4, 4, 144, 128)
        del shapes["output"]
        names_out.remove("output")
    items = scratch_list(n, inside)
    smem = pl.BlockSpec(memory_space=pltpu.SMEM)
    vmem = pl.BlockSpec(memory_space=pltpu.VMEM)
    outs = pl.pallas_call(
        make_kernel(n, inside, names_in + names_out + [name for name, _ in items]),
        out_shape=[
            jax.ShapeDtypeStruct(shapes[name], BF16 if name in ("ro_dst", "io_dst") else F32) for name in names_out
        ],
        in_specs=[smem if name == "coef" else vmem for name in names_in],
        out_specs=[vmem] * len(names_out),
        scratch_shapes=[item for _, item in items],
        compiler_params=pltpu.CompilerParams(
            collective_id=0, has_side_effects=True, vmem_limit_bytes=63 * 1024 * 1024
        ),
        name="blocks",
    )(*[inputs[name] for name in names_in])
    raw = dict(zip(names_out, outs))
    final = dict(
        result=flat_shape,
        image_grad=flat_shape,
        embed_grad=embedding.shape,
        film=film_weight.shape,
        gains_out=norm_gains.shape,
        biases_out=biases.shape,
    )
    if inside:
        final.update(first=(9, 48, BLK), second=(9, 48, BLK), attend=attend_weight.shape, output=output_weight.shape)
    names_last = [name for name in names_out if inside or name not in ("first", "second", "attend")] + ["sel"]
    names_final = list(final)
    outs = pl.pallas_call(
        make_writer(names_last, names_final),
        out_shape=[jax.ShapeDtypeStruct(final[name], F32) for name in names_final],
        in_specs=[vmem] * len(names_last),
        out_specs=[vmem] * len(names_final),
        compiler_params=pltpu.CompilerParams(vmem_limit_bytes=63 * 1024 * 1024),
        name="outputs",
    )(*[inputs["sel"] if name == "sel" else raw[name] for name in names_last])
    out = dict(zip(names_final, outs))
    if not inside:

        def blocks_of(array, size):
            parts = [array[..., k * 48 : k * 48 + 48, :BLK] for k in range(size)]
            if size == 2:
                lanes = [array[..., k * 32 : k * 32 + 32, BLK:] for k in range(3)]
                lanes = jnp.concatenate(lanes, axis=-1)
                parts.append(jnp.concatenate([lanes, array[..., 96:112, :BLK]], axis=-2))
            else:
                lanes = [array[..., k * 48 : k * 48 + 48, BLK:] for k in range(3)]
                parts.append(jnp.concatenate(lanes, axis=-1))
            array = jnp.stack(parts, axis=1)
            array = array.reshape(array.shape[:2] + (2, 2, 4, 48, BLK))
            taps = array.shape[0] * array.shape[1]
            array = jnp.transpose(array, (0, 1, 4, 2, 5, 3, 6)).reshape(taps, 384, 2, 1, BLK)
            both = jnp.concatenate([array, jnp.zeros_like(array)], axis=3)
            return jnp.where(core == 0, both, both[:, :, :, ::-1]).reshape(taps, 384, 384)

        def shared(array, axis):
            array = lax.psum_scatter(array, "head", scatter_dimension=array.ndim - 1, tiled=True)
            return lax.psum_scatter(array, "dp", scatter_dimension=axis, tiled=True)

        out["first"] = shared(blocks_of(raw["first"], 2), 1)
        out["second"] = shared(blocks_of(raw["second"], 2), 1)
        both = blocks_of(raw["attend"], 3)
        joined = both[:3].reshape(3, 384, 2, 2, BLK)
        joined = jnp.transpose(joined, (1, 2, 0, 3, 4)).reshape(384, 1152)
        out["attend"] = shared(joined, 0)
        out["output"] = shared(both[3], 0)
    return (
        out["result"].reshape(images.shape),
        out["image_grad"].reshape(images.shape),
        out["embed_grad"],
        out["first"].reshape(first_kernel.shape),
        out["second"].reshape(second_kernel.shape),
        out["film"],
        out["attend"],
        out["output"],
        out["gains_out"],
        out["biases_out"],
    )


def solution(mesh):
    n = mesh.shape["dp"]
    field = P("dp", "head", None, None)
    taps = P(None, None, "dp", "head")
    both = P("dp", "head")
    return jax.shard_map(
        lambda *args: per_device(n, *args),
        mesh=mesh,
        in_specs=(field, field, P("dp"), P("dp", None), taps, taps, both, both, both, P(), P(), field),
        out_specs=(field, field, P("dp", None), taps, taps, both, both, both, P(), P()),
        check_vma=False,
    )
```

```python
import math

import jax
import jax.numpy as jnp
import numpy as np
from jax import lax
from jax.experimental import pallas as pl
from jax.experimental.pallas import tpu as pltpu
from jax.sharding import PartitionSpec as P

HEAD_DIM = 96
GROUPS = 32
STEPS = 4000
EPS = 1e-05
OFFSET = 0.008
MESH = pl.DeviceIdType.MESH
F32 = jnp.float32
BF16 = jnp.bfloat16

PX = 1024
ROW = 32
CHUNK = 256
BLK = 96
HALF = 256
NHEAD = 4


def plan(time_steps):
    fraction = (time_steps.astype(F32) + 1.0) / STEPS
    start = jnp.square(jnp.cos(jnp.float32(OFFSET / (1.0 + OFFSET) * (math.pi / 2))))
    curve = jnp.square(jnp.cos((fraction + OFFSET) / (1.0 + OFFSET) * (math.pi / 2))) / start
    return (jnp.sqrt(curve), jnp.sqrt(1.0 - curve))


def channel_lanes():
    sel = np.zeros((2, 384, HALF), np.float32)
    for block in range(4):
        for j in range(BLK):
            sel[block % 2, block * BLK + j, (block // 2) * 128 + j] = 1.0
    return sel


def block_lanes(count):
    sel = np.zeros((count * BLK, count * 128), np.float32)
    for block in range(count):
        for j in range(BLK):
            sel[block * BLK + j, block * 128 + j] = 1.0
    return sel


def group_mask():
    lane = np.arange(HALF)
    ok = lane % 128 < BLK
    group = (lane // 128) * 100 + (lane % 128) // 12
    return ((group[:, None] == group[None, :]) & ok[:, None] & ok[None, :]).astype(np.float32)


def dot(a, b):
    return lax.dot_general(a, b, (((1,), (0,)), ((), ())), preferred_element_type=F32)


def dot_nt(a, b):
    return lax.dot_general(a, b, (((1,), (1,)), ((), ())), preferred_element_type=F32)


def dot_nt_high(a, b):
    return lax.dot_general(
        a, b, (((1,), (1,)), ((), ())), preferred_element_type=F32, precision=lax.Precision.HIGHEST
    )


def dot_tn_high(a, b):
    return lax.dot_general(
        a, b, (((0,), (0,)), ((), ())), preferred_element_type=F32, precision=lax.Precision.HIGHEST
    )


def exact_dot(values, ones):
    high = values.astype(BF16).astype(F32)
    rest = values - high
    middle = rest.astype(BF16).astype(F32)
    low = rest - middle
    rows = values.shape[0]
    out = dot(jnp.concatenate([high, middle, low], axis=0).astype(BF16), ones)
    return out[:rows] + out[rows : 2 * rows] + out[2 * rows :]


def sigmoid(v):
    return 0.5 + 0.5 * jnp.tanh(0.5 * v)


def silu(v):
    return v * sigmoid(v)


def silu_slope(v):
    s = sigmoid(v)
    return s * (1.0 + v * (1.0 - s))


def pack_taps(t0, t1, t2):
    t0, t1, t2 = t0[:, :BLK], t1[:, :BLK], t2[:, :BLK]
    join = lambda a, b: jnp.concatenate([a, b], axis=1)
    return jnp.concatenate(
        [
            join(t0[:32], t2[:32, :32]),
            join(t0[32:], t2[:16, 32:64]),
            join(t1[:16], t2[16:32, 32:64]),
            join(t1[16:], t2[:32, 64:]),
            join(t2[32:], jnp.zeros((16, 32), t2.dtype)),
        ],
        axis=0,
    )


def last_tap(packed):
    lanes = [packed[:32, BLK:], packed[32:64, BLK:], packed[64:96, BLK:], jnp.zeros((32, 32), packed.dtype)]
    return jnp.concatenate([jnp.concatenate(lanes, axis=1), packed[96:112]], axis=0)


def pack_four(b0, b1, b2, b3):
    return jnp.concatenate(
        [jnp.concatenate([b[:, :BLK], b3[:, 32 * k : 32 * k + 32]], axis=1) for k, b in enumerate((b0, b1, b2))],
        axis=0,
    )


def unpack_four(packed):
    size = packed.shape[0] // 3
    parts = [packed[k * size : k * size + size] for k in range(3)]
    zero = jnp.zeros((size, 32), packed.dtype)
    fourth = jnp.concatenate([p[:, BLK:] for p in parts] + [zero], axis=1)
    return [jnp.concatenate([p[:, :BLK], zero], axis=1) for p in parts] + [fourth]


def pack_pixels(full):
    half = CHUNK // 2
    return pack_four(full[:half, :128], full[half:, :128], full[:half, 128:], full[half:, 128:])


def unpack_pixels(packed):
    b0, b1, b2, b3 = unpack_four(packed)
    return jnp.concatenate([jnp.concatenate([b0, b2], axis=1), jnp.concatenate([b1, b3], axis=1)], axis=0)


INPUTS = (
    "coef",
    "images",
    "noise",
    "cot",
    "emb",
    "k1",
    "k2",
    "wf",
    "wa",
    "wo",
    "gains",
    "biases",
    "sel",
    "gmask",
    "selp",
)
OUTPUTS = (
    "ro_dst",
    "io_dst",
    "embed_grad",
    "first",
    "second",
    "film",
    "attend",
    "output",
    "gains_out",
    "biases_out",
)


class Names:
    def __init__(self, names, refs):
        for name, ref in zip(names, refs):
            setattr(self, name, ref)


def scratch_list(n, inside):
    dma = pltpu.SemaphoreType.DMA
    items = []

    def vm(name, shape, dtype):
        items.append((name, pltpu.VMEM(shape, dtype)))

    def sem(name, count):
        items.append((name + "_s", dma((count,))))
        items.append((name + "_r", dma((count,))))

    for name in ("mx", "cx", "ro", "io"):
        vm(name + "_src", (4, 384, 128), BF16)
        if name in ("mx", "cx"):
            vm(name + "_dst", (4, 384, 128), BF16)
            vm(name, (4, CHUNK, HALF), BF16)
        sem(name, 4)
    for name in ("act1", "act2"):
        vm(name, (2, PX + 2 * ROW, HALF), BF16)
        vm(name + "_t", (2, HALF, PX), BF16)
        sem(name, 4)
    vm("ai", (2, PX, HALF), BF16)
    vm("ai_t", (2, HALF, PX), BF16)
    sem("ai", 4)
    vm("att", (4, PX, 128), BF16)
    vm("att_t", (2, HALF, PX), BF16)
    sem("att", 2)
    for name in ("do", "n3", "d2", "d1"):
        vm(name + "_src", (PX, HALF), BF16)
        vm(name + "_dst", (PX, HALF), BF16)
        sem(name, 1)
    vm("v2", (PX, HALF), F32)
    vm("v3", (PX, HALF), F32)
    vm("gres", (PX, HALF), F32)
    vm("gtmp", (PX, HALF), F32)
    vm("conv", (3, PX, HALF), F32)
    vm("qkv", (6, PX, 128), BF16)
    vm("kvt", (4, 128, PX), BF16)
    vm("dout", (2, PX, 128), BF16)
    vm("dproj", (6, PX, 128), BF16)
    vm("gr2", (3, PX + 2 * ROW, HALF), BF16)
    vm("gr1", (3, PX + 2 * ROW, HALF), BF16)
    vm("par", (16, 384), F32)
    vm("parown", (16, HALF), F32)
    vm("stat", (16, HALF), F32)
    vm("sums", (16, HALF), F32)
    if inside:
        vm("g1", (4, 4, 336, 128), BF16)
        vm("g2", (4, 4, 336, 128), BF16)
        vm("t1", (4, 4, 144, 128), BF16)
        vm("t2", (4, 4, 144, 128), BF16)
        vm("p3", (4, 4, 144, 128), BF16)
        vm("g3", (4, 4, 192, 128), BF16)
        for name in ("g1", "g2", "p3"):
            sem(name + "z", 4)
            sem(name + "v", 4)
            sem(name + "w", 8)
        vm("sw_src", (48, 128), BF16)
        vm("sw_dst", (48, 128), BF16)
        sem("sw", 1)
        vm("sb_src", (48, 128), F32)
        vm("sb_dst", (48, 128), F32)
        sem("sb", 1)
        for name, nc, rows in (("r1", 3, 112), ("r2", 3, 112), ("r3", 1, 144)):
            vm(name + "_acc", (nc, 4, 4, rows, 128), F32)
            vm(name + "w_src", (nc, 2, 4, rows, 128), BF16)
            vm(name + "w_dst", (nc, 2, 4, rows, 128), BF16)
            vm(name + "v_src", (nc, 4, rows, 128), BF16)
            vm(name + "v_dst", (nc, 4, rows, 128), BF16)
            vm(name + "z_src", (4, nc, rows, 128), BF16)
            vm(name + "z_dst", (4, nc, rows, 128), BF16)
            sem(name + "w", nc)
            sem(name + "v", nc)
            sem(name + "z", nc * 4)
    vm("el", (n, 2, 768), F32)
    sem("el", n)
    vm("em", (2 * n, 768), F32)
    vm("wfp", (128, HALF), BF16)
    vm("esel", (2 * n, 128), F32)
    vm("fp", (n, 2, HALF), F32)
    vm("fr", (n, 2, HALF), F32)
    sem("fr", n)
    vm("fx", (4, 1, 128), F32)
    vm("fh", (4, 1, 128), F32)
    sem("fh", 4)
    vm("ft", (4, 1, 128), F32)
    vm("th", (4, 1, 128), F32)
    sem("th", 4)
    vm("fa", (n, 2, HALF), F32)
    sem("fa", n)
    vm("fta", (2 * n, HALF), F32)
    vm("ep", (n, 2, 128), F32)
    vm("er", (n, 2, 128), F32)
    sem("er", n)
    vm("eh", (4, n, 2, 128), F32)
    sem("eh", 4)
    vm("ad", (n, 16, HALF), F32)
    sem("ad", n)
    vm("hb", (4, 16, HALF), F32)
    sem("hb", 4)
    return items


def make_kernel(n, inside, names):
    film_rows = 768 // n

    def kernel(*refs):
        r = Names(names, refs)
        d = lax.axis_index("dp")
        h = lax.axis_index("head")
        x = h // 2
        c = h - 2 * x
        z = d // 2
        y = d - 2 * z
        sib = (d, h + 1 - 2 * c)
        xdev = (d, h + 2 - 4 * x)
        v = x + c * (y - x)
        w = y + c * (x - y)
        vdev = (d + c * (1 - 2 * y), h + (1 - c) * (2 - 4 * x))
        wdev = (d + (1 - c) * (1 - 2 * y), h + c * (2 - 4 * x))

        def slot(xx, yy):
            if inside:
                return (yy + c * (xx - yy)) * 2 + xx + c * (yy - xx)
            return yy * 2 + xx

        def rc(src, dst, send, recv, dev):
            return pltpu.make_async_remote_copy(
                src_ref=src, dst_ref=dst, send_sem=send, recv_sem=recv, device_id=dev, device_id_type=MESH
            )

        def loop(count, body):
            def step(i, carry):
                body(i)
                return carry

            lax.fori_loop(0, count, step, 0)

        def each(count, body):
            for i in range(count):
                body(i)

        def rows(i, size=CHUNK, base=0):
            return pl.ds(pl.multiple_of(base + i * size, 32), size)

        def dp_start(src_of, dst, send, recv):
            def step(k, carry):
                peer = lax.rem(d + k, n)
                rc(src_of(peer), dst.at[d], send.at[k], recv.at[d], (peer, h)).start()
                return carry

            lax.fori_loop(1, n, step, 0)

        def dp_wait(src_of, dst, send, recv):
            def step(k, carry):
                peer = lax.rem(d + k, n)
                copy = rc(src_of(peer), dst.at[peer], send.at[k], recv.at[peer], (peer, h))
                copy.wait_recv()
                copy.wait_send()
                return carry

            lax.fori_loop(1, n, step, 0)

        def head_start(src_of, dst, send, recv):
            for k in range(1, 4):
                peer = lax.rem(h + k, 4)
                rc(src_of(peer), dst.at[h], send.at[k], recv.at[h], (d, peer)).start()

        def head_wait(src_of, dst, send, recv):
            for k in range(1, 4):
                peer = lax.rem(h + k, 4)
                copy = rc(src_of(peer), dst.at[peer], send.at[k], recv.at[peer], (d, peer))
                copy.wait_recv()
                copy.wait_send()

        class Halves:
            def __init__(self, name, base):
                self.buf, self.base = getattr(r, name), base
                self.send, self.recv = getattr(r, name + "_s"), getattr(r, name + "_r")

            def at(self, core, i):
                return self.buf.at[core, rows(i, CHUNK, self.base)]

            def fill(self, make):
                def body(i):
                    self.buf[c, rows(i, CHUNK, self.base), :] = make(i)
                    ref = self.at(c, i)
                    rc(ref, ref, self.send.at[i], self.recv.at[i], sib).start()

                loop(4, body)

            def wait(self):
                for i in range(4):
                    ref = self.at(1 - c, i)
                    copy = rc(ref, ref, self.send.at[i], self.recv.at[i], sib)
                    copy.wait_recv()
                    copy.wait_send()

        class Parts:
            def __init__(self, name):
                self.src, self.dst = getattr(r, name + "_src"), getattr(r, name + "_dst")
                self.send, self.recv = getattr(r, name + "_s"), getattr(r, name + "_r")

            def copy(self):
                return rc(self.src, self.dst, self.send.at[0], self.recv.at[0], sib)

            def both(self, make):
                self.src[...] = make(1 - c).astype(BF16)
                self.copy().start()
                r.gtmp[...] = make(c)

            def wait(self):
                copy = self.copy()
                copy.wait_recv()
                copy.wait_send()

            def get(self, i):
                return r.gtmp[rows(i), :] + self.dst[rows(i), :].astype(F32)

        class Gather:
            def __init__(self, name):
                self.g = getattr(r, name)
                self.zs, self.zr = getattr(r, name + "z_s"), getattr(r, name + "z_r")
                self.vs, self.vr = getattr(r, name + "v_s"), getattr(r, name + "v_r")
                self.ws, self.wr = getattr(r, name + "w_s"), getattr(r, name + "w_r")

            def zcopy(self, k):
                peer = (lax.rem(z + k, 4) * 2 + y, h)
                return rc(
                    self.g.at[w * 2 + v, 0], self.g.at[w * 2 + v, 4 - k], self.zs.at[k], self.zr.at[4 - k], peer
                )

            def vcopy(self, vv, i):
                ref = self.g.at[w * 2 + vv, i]
                return rc(ref, ref, self.vs.at[i], self.vr.at[i], vdev)

            def wcopy(self, ww, other, i):
                ref = self.g.at[ww * 2 + v + other * (1 - 2 * v), i]
                return rc(ref, ref, self.ws.at[2 * i + other], self.wr.at[2 * i + other], wdev)

            def own(self):
                for k in range(1, 4):
                    self.zcopy(k).start()
                self.vcopy(v, 0).start()
                self.wcopy(w, 0, 0).start()

            def pass_z(self):
                self.vcopy(1 - v, 0).wait_recv()
                self.wcopy(w, 1, 0).start()
                for k in range(1, 4):
                    self.zcopy(k).wait_recv()
                    self.vcopy(v, 4 - k).start()
                    self.wcopy(w, 0, 4 - k).start()

            def pass_v(self):
                for k in range(1, 4):
                    self.vcopy(1 - v, 4 - k).wait_recv()
                    self.wcopy(w, 1, 4 - k).start()

            def done(self):
                for k in range(1, 4):
                    self.zcopy(k).wait_send()
                for i in range(4):
                    self.vcopy(v, i).wait_send()
                    for other in range(2):
                        self.wcopy(1 - w, other, i).wait_recv()
                        self.wcopy(w, other, i).wait_send()

        class Reduce:
            def __init__(self, name, count):
                get = lambda tail: getattr(r, name + tail)
                self.acc, self.count = get("_acc"), count
                self.wsrc, self.wdst, self.ws, self.wr = get("w_src"), get("w_dst"), get("w_s"), get("w_r")
                self.vsrc, self.vdst, self.vs, self.vr = get("v_src"), get("v_dst"), get("v_s"), get("v_r")
                self.zsrc, self.zdst, self.zs, self.zr = get("z_src"), get("z_dst"), get("z_s"), get("z_r")

            def wcopy(self, a):
                return rc(self.wsrc.at[a], self.wdst.at[a], self.ws.at[a], self.wr.at[a], wdev)

            def vcopy(self, a, size):
                at = pl.ds(a, size)
                return rc(self.vsrc.at[at], self.vdst.at[at], self.vs.at[a], self.vr.at[a], vdev)

            def zcopy(self, a, size, k):
                at = pl.ds(a, size)
                return rc(
                    self.zsrc.at[k, at],
                    self.zdst.at[4 - k, at],
                    self.zs.at[a * 4 + k],
                    self.zr.at[a * 4 + 4 - k],
                    (lax.rem(z + k, 4) * 2 + y, h),
                )

            def start(self, a):
                def step(i, carry):
                    vv, zz = i // 4, lax.rem(i, 4)
                    self.wsrc[a, vv, zz] = self.acc[a, (1 - w) * 2 + vv, zz].astype(BF16)
                    return carry

                lax.fori_loop(0, 8, step, 0)
                self.wcopy(a).start()

            def second(self, first, size):
                for a in range(first, first + size):
                    self.wcopy(a).wait_recv()

                    def step(zz, carry):
                        self.vsrc[a, zz] = (
                            self.acc[a, w * 2 + 1 - v, zz] + self.wdst[a, 1 - v, zz].astype(F32)
                        ).astype(BF16)
                        return carry

                    lax.fori_loop(0, 4, step, 0)
                self.vcopy(first, size).start()

            def third(self, first, size):
                self.vcopy(first, size).wait_recv()
                for a in range(first, first + size):

                    def step(k, carry):
                        zz = lax.rem(z + k, 4)
                        total = (
                            self.acc[a, w * 2 + v, zz]
                            + self.wdst[a, v, zz].astype(F32)
                            + self.vdst[a, zz].astype(F32)
                        )
                        self.acc[a, w * 2 + v, zz] = total
                        self.zsrc[k, a] = total.astype(BF16)
                        return carry

                    lax.fori_loop(0, 4, step, 0)
                for k in range(1, 4):
                    self.zcopy(first, size, k).start()

            def finish(self, groups):
                for first, size in groups:
                    self.vcopy(first, size).wait_send()
                    for k in range(1, 4):
                        copy = self.zcopy(first, size, k)
                        copy.wait_recv()
                        copy.wait_send()
                for a in range(self.count):
                    self.wcopy(a).wait_send()

            def last(self, a):
                total = self.acc[a, w * 2 + v, z]
                for k in range(1, 4):
                    total = total + self.zdst[k, a].astype(F32)
                return total

        def rel(zc):
            return lax.rem(zc - z + 4, 4) if inside else zc

        class Taps:
            def __init__(self, packed, last):
                self.packed, self.last = packed, last

            def block(self, tap, zc, xx, yy):
                a, b = tap // 3, tap % 3
                if b < 2:
                    return self.packed[slot(xx, yy), rel(zc), pl.ds(a * 112 + b * 48, 48), :]
                return self.last[slot(xx, yy), rel(zc), pl.ds(a * 48, 48), :]

            def unpack(self):
                def step(i, carry):
                    q, zz = i // 4, lax.rem(i, 4)
                    for a in range(3):
                        self.last[q, zz, pl.ds(a * 48, 48), :] = last_tap(
                            self.packed[q, zz, pl.ds(a * 112, 112), :]
                        )
                    return carry

                lax.fori_loop(0, 16, step, 0)

        class Plain:
            def __init__(self, blocks):
                self.blocks = blocks

            def block(self, tap, zc, xx, yy):
                return self.blocks[slot(xx, yy), rel(zc), pl.ds(tap * 48, 48), :]

            def unpack(self):
                def step(i, carry):
                    q, zz = i // 4, lax.rem(i, 4)
                    self.blocks[q, zz] = jnp.concatenate(unpack_four(r.p3[q, zz]), axis=0)
                    return carry

                lax.fori_loop(0, 16, step, 0)

        k1, k2, k3 = Taps(r.g1, r.t1), Taps(r.g2, r.t2), Plain(r.g3)

        def wtile(g, tap, zc, xx):
            return jnp.concatenate(
                [g.block(tap, zc, xx, 0), g.block(tap, zc, xx, 1), jnp.zeros((32, 128), BF16)], axis=0
            )

        def wtap(g, tap, zcs):
            return jnp.concatenate(
                [jnp.concatenate([wtile(g, tap, zc, xx) for xx in range(2)], axis=1) for zc in zcs], axis=0
            )

        ALL = (0, 2, 1, 3)

        def half_of(core):
            return (core, core + 2)

        def wproj(zcs):
            return jnp.concatenate(
                [
                    jnp.concatenate([wtile(k3, j, zc, xx) for xx in range(2) for j in range(3)], axis=1)
                    for zc in zcs
                ],
                axis=0,
            )

        def flat(buf, base, i, size):
            return jnp.concatenate([buf[0, rows(i, size, base), :], buf[1, rows(i, size, base), :]], axis=1)

        barrier = pltpu.get_barrier_semaphore()

        def greet(k, carry):
            pl.semaphore_signal(barrier, inc=1, device_id=(lax.rem(d + k, n), h), device_id_type=MESH)
            return carry

        lax.fori_loop(1, n, greet, 0)
        for k in range(1, 4):
            pl.semaphore_signal(barrier, inc=1, device_id=(d, lax.rem(h + k, 4)), device_id_type=MESH)
        if inside:
            for a in range(3):
                r.g1[w * 2 + v, 0, pl.ds(a * 112, 112), :] = pack_taps(*[r.k1[3 * a + b] for b in range(3)])
        pl.semaphore_wait(barrier, n - 1 + 3)
        if inside:
            ga, gb, gc = Gather("g1"), Gather("g2"), Gather("p3")
            ga.own()

        def mix(m, carry):
            field = r.coef[0, m] * r.images[m].astype(F32) + r.coef[1, m] * r.noise[m].astype(F32)
            low = field.astype(BF16)
            for core in range(2):
                r.mx_src[m * 2 + core] = pack_pixels(dot(low, r.sel[core])).astype(BF16)
            return carry

        lax.fori_loop(0, 2, mix, 0)
        head_start(lambda p: r.mx_src.at[p], r.mx_dst, r.mx_s, r.mx_r)
        r.mx_dst[h] = r.mx_src[h]

        r.el[d] = silu(r.emb[...].astype(F32)).astype(BF16).astype(F32)
        dp_start(lambda p: r.el.at[d], r.el, r.el_s, r.el_r)

        if inside:
            blocks = dot(r.wa[...], r.selp[: 3 * BLK, : 3 * 128]).astype(BF16)
            r.sw_src[...] = blocks[:, 128:256]
            swap = rc(r.sw_src, r.sw_dst, r.sw_s.at[0], r.sw_r.at[0], sib)
            swap.start()
            for a in range(3):
                r.g2[w * 2 + v, 0, pl.ds(a * 112, 112), :] = pack_taps(*[r.k2[3 * a + b] for b in range(3)])
        r.par[0:3, :] = r.gains[...]
        r.par[3:13, :] = r.biases[...]
        r.par[13:16, :] = jnp.zeros((3, 384), F32)
        r.parown[...] = exact_dot(r.par[...], r.sel[c])

        def prow(i):
            return r.parown[pl.ds(i, 1), :]

        for buf in (r.act1, r.act2):
            for core in range(2):
                buf[core, pl.ds(0, ROW), :] = jnp.zeros((ROW, HALF), BF16)
                buf[core, pl.ds(PX + ROW, ROW), :] = jnp.zeros((ROW, HALF), BF16)
        for buf in (r.gr1, r.gr2):
            for b in range(3):
                buf[b, pl.ds(0, ROW), :] = jnp.zeros((ROW, HALF), BF16)
                buf[b, pl.ds(PX + ROW, ROW), :] = jnp.zeros((ROW, HALF), BF16)
        r.wfp[...] = jnp.zeros((128, HALF), BF16)
        r.wfp[pl.ds(0, film_rows), :] = dot(r.wf[...], r.selp[: 2 * BLK, :HALF]).astype(BF16)
        if inside:
            ga.pass_z()
            gb.own()

        count = float(PX * 12)

        def fold(vals):
            return jnp.sum(vals.reshape(CHUNK // 8, 8, HALF), axis=0)

        def sums_of(fn, k):
            def step(i, carry):
                return tuple(a + fold(b) for a, b in zip(carry, fn(i)))

            zero = jnp.zeros((8, HALF), F32)
            return lax.fori_loop(0, 4, step, (zero,) * k)

        def group_mean(part):
            return jnp.sum(exact_dot(part, r.gmask[...]), axis=0, keepdims=True) / count

        def norm(load, which, total):
            mean = group_mean(total)
            (square,) = sums_of(lambda i: (jnp.square(load(i) - mean),), 1)
            inv = lax.rsqrt(group_mean(square) + EPS)
            r.stat[pl.ds(2 * which, 1), :] = mean
            r.stat[pl.ds(2 * which + 1, 1), :] = inv
            return mean, inv

        zero8 = jnp.zeros((8, HALF), F32)

        def norm_back(sums, load_grad, load_hat, coef, inv):
            plain, cross = sums
            plain_mean, cross_mean = group_mean(coef * plain), group_mean(coef * cross)
            outer, base, slope = inv * coef, inv * plain_mean, inv * cross_mean

            def chunk(i):
                return outer * load_grad(i) - base - load_hat(i) * slope

            return (
                jnp.sum(plain, axis=0, keepdims=True),
                jnp.sum(cross, axis=0, keepdims=True),
                chunk,
            )

        head_wait(lambda p: r.mx_src.at[p], r.mx_dst, r.mx_s, r.mx_r)

        def unpack_mixed(i, carry):
            vals = unpack_pixels(r.mx_dst[i])
            r.mx[i] = vals
            return carry + fold(vals.astype(F32))

        mixed_sum = lax.fori_loop(0, 4, unpack_mixed, zero8)

        def mixed(i):
            return r.mx[i].astype(F32)

        mean1, inv1 = norm(mixed, 0, mixed_sum)
        gain1, shift1 = prow(0), prow(3)
        act1 = Halves("act1", ROW)

        def affine(mean, inv, gain, shift):
            return inv * gain, shift - mean * (inv * gain)

        mul1, add1 = affine(mean1, inv1, gain1, shift1)

        def pre1(i):
            return mixed(i) * mul1 + add1

        act1.fill(lambda i: silu(pre1(i)).astype(BF16))
        if inside:
            ga.pass_v()

        dp_wait(lambda p: r.el.at[d], r.el, r.el_s, r.el_r)
        for j in range(n):
            r.em[pl.ds(2 * j, 2), :] = r.el[j]
        place = lax.broadcasted_iota(jnp.int32, (768, 128), 0) - film_rows * d
        lane = lax.broadcasted_iota(jnp.int32, (768, 128), 1)
        pick = jnp.where((place == lane) & (lane < film_rows), 1.0, 0.0).astype(BF16)
        r.esel[...] = dot(r.em[...].astype(BF16), pick)
        film_part = dot(r.esel[...].astype(BF16), r.wfp[...])
        for j in range(n):
            r.fp[j] = film_part[2 * j : 2 * j + 2]
        dp_start(lambda p: r.fp.at[p], r.fr, r.fr_s, r.fr_r)
        r.fr[d] = r.fp[d]
        if inside:
            swap.wait()
            got = r.sw_dst[...]
            keep0, keep2 = blocks[:, :128], blocks[:, 256:]
            r.p3[w * 2 + v, 0] = pack_four(
                jnp.where(c == 0, keep0, got),
                jnp.where(c == 0, keep2, keep0),
                jnp.where(c == 0, got, keep2),
                r.wo[...],
            )
            gb.pass_z()
            gc.own()
        def split_cot(m, carry):
            for core in range(2):
                r.cx_src[m * 2 + core] = pack_pixels(dot(r.cot[m], r.sel[core])).astype(BF16)
            return carry

        lax.fori_loop(0, 2, split_cot, 0)
        head_start(lambda p: r.cx_src.at[p], r.cx_dst, r.cx_s, r.cx_r)
        r.cx_dst[h] = r.cx_src[h]

        column = lax.broadcasted_iota(jnp.int32, (1, ROW, HALF), 1)
        not_first = jnp.where(column > 0, 1.0, 0.0)
        not_last = jnp.where(column < ROW - 1, 1.0, 0.0)

        def in_rows(vals, mask):
            return (vals.reshape(CHUNK // ROW, ROW, HALF) * mask).reshape(CHUNK, HALF)

        def from_left(vals):
            return in_rows(pltpu.roll(vals, 1, 0), not_first)

        def from_right(vals):
            return in_rows(pltpu.roll(vals, CHUNK - 1, 0), not_last)

        def transpose_act(buf, base, out):
            for core in range(2):
                for q in range(4):
                    out[core, :, pl.ds(q * CHUNK, CHUNK)] = jnp.transpose(
                        buf[core, pl.ds(base + q * CHUNK, CHUNK), :]
                    )

        def conv(buf, g, store, between):
            for b in range(3):
                left = jnp.concatenate([flat(buf, ROW * a, 0, PX) for a in range(3)], axis=1)
                r.conv[b] = dot(left, jnp.concatenate([wtap(g, 3 * a + b, ALL) for a in range(3)], axis=0))
                if b == 0:
                    between()

            def step(i, total):
                part = r.conv[1, rows(i), :] + from_left(r.conv[0, rows(i), :]) + from_right(r.conv[2, rows(i), :])
                return total + fold(store(i, part))

            return lax.fori_loop(0, 4, step, zero8)

        act1.wait()
        transpose_act(r.act1, ROW, r.act1_t)
        if inside:
            ga.done()
            k1.unpack()

        def store_v2(i, vals):
            vals = vals + prow(6)
            r.v2[rows(i), :] = vals
            return vals

        v2_sum = conv(r.act1, k1, store_v2, gb.pass_v if inside else lambda: None)
        dp_wait(lambda p: r.fp.at[p], r.fr, r.fr_s, r.fr_r)
        film_sum = r.fr[0]
        for j in range(1, n):
            film_sum = film_sum + r.fr[j]
        for m in range(2):
            for core in range(2):
                r.fx[m * 2 + core] = film_sum[m : m + 1, core * 128 : core * 128 + 128]
        head_start(lambda p: r.fx.at[p], r.fh, r.fh_s, r.fh_r)
        r.fh[h] = r.fx[h]

        head_wait(lambda p: r.fx.at[p], r.fh, r.fh_s, r.fh_r)
        scale = 1.0 + (jnp.concatenate([r.fh[0], r.fh[1]], axis=1) + prow(8))
        shift = jnp.concatenate([r.fh[2], r.fh[3]], axis=1) + prow(9)
        mean2, inv2 = norm(lambda i: r.v2[rows(i), :], 1, v2_sum)
        gain2, shift2 = prow(1), prow(4)
        act2 = Halves("act2", ROW)

        def hat2(i):
            return (r.v2[rows(i), :] - mean2) * inv2

        mul2, add2 = affine(mean2, inv2, gain2 * scale, shift2 * scale + shift)

        def pre2(i):
            return r.v2[rows(i), :] * mul2 + add2

        act2.fill(lambda i: silu(pre2(i)).astype(BF16))
        if inside:
            gc.pass_z()

        act2.wait()
        transpose_act(r.act2, ROW, r.act2_t)
        if inside:
            gb.done()
            k2.unpack()

        def store_v3(i, vals):
            vals = mixed(i) + (vals + prow(7))
            r.v3[rows(i), :] = vals
            return vals

        v3_sum = conv(r.act2, k2, store_v3, gc.pass_v if inside else lambda: None)
        mean3, inv3 = norm(lambda i: r.v3[rows(i), :], 2, v3_sum)
        gain3, shift3 = prow(2), prow(5)
        ai = Halves("ai", 0)

        def hat3(i):
            return (r.v3[rows(i), :] - mean3) * inv3

        mul3, add3 = affine(mean3, inv3, gain3, shift3)
        ai.fill(lambda i: (r.v3[rows(i), :] * mul3 + add3).astype(BF16))

        if inside:
            gc.done()
            k3.unpack()
        head_wait(lambda p: r.cx_src.at[p], r.cx_dst, r.cx_s, r.cx_r)

        def unpack_cot(i):
            r.cx[i] = unpack_pixels(r.cx_dst[i])

        loop(4, unpack_cot)
        dop = Parts("do")

        def cot_all():
            return jnp.concatenate([r.cx[i] for i in range(4)], axis=0)

        dop.both(lambda core: dot_nt(cot_all(), wtap(k3, 3, half_of(core))))

        ai.wait()
        bias_proj = [prow(10)[:, :128], prow(10)[:, 128:], None, None, prow(11)[:, :128], prow(11)[:, 128:]]

        out = dot(flat(r.ai, 0, 0, PX), wproj(ALL))
        for k in range(6):
            part = out[:, k * 128 : k * 128 + 128]
            if bias_proj[k] is not None:
                part = part + bias_proj[k]
            r.qkv[k] = part.astype(BF16)
        dop.wait()

        def do_own(i):
            full = dop.get(i).astype(BF16)
            for k in range(2):
                r.dout[k, rows(i), :] = full[:, k * 128 : k * 128 + 128]

        loop(4, do_own)

        factor = 1.0 / math.sqrt(HEAD_DIM)
        factor2 = factor * math.log2(math.e)
        att = []

        def transposes(k):
            r.kvt[k] = jnp.transpose(r.qkv[k + 2])

        loop(4, transposes)

        def att_copies(core):
            for i, ref in enumerate((r.att.at[pl.ds(core * 2, 2)], r.att_t.at[core])):
                yield rc(ref, ref, r.att_s.at[i], r.att_r.at[i], sib)

        def one_head(k):
            lows, grads = [], []
            for b in range(2):
                at = pl.ds(b * 2 * CHUNK, 2 * CHUNK)
                query = r.qkv[k, at, :]
                grad = r.dout[k, at, :]
                scores = dot_nt(r.qkv[2 + k], query)
                peak = jnp.max(scores, axis=0, keepdims=True)
                expo = jnp.exp2((scores - peak) * factor2)
                inverse = 1.0 / jnp.sum(expo, axis=0, keepdims=True)
                low = (expo * inverse).astype(BF16)
                got = dot(r.kvt[2 + k], low)
                got_low = got.astype(BF16)
                r.att_t[c, pl.ds(pl.multiple_of(k * 128, 128), 128), at] = got_low
                r.att[2 * c + k, at, :] = jnp.transpose(got_low)
                spread = jnp.sum(got * jnp.transpose(grad).astype(F32), axis=0, keepdims=True)
                probs_grad = dot_nt(r.qkv[4 + k], grad)
                scores_grad = ((probs_grad - spread) * inverse * expo).astype(BF16)
                back = dot(r.kvt[k], scores_grad)
                r.dproj[k, at, :] = (jnp.transpose(back) * factor).astype(BF16)
                lows.append(low)
                grads.append(scores_grad)
            r.dproj[4 + k] = dot(jnp.concatenate(lows, axis=1), r.dout[k]).astype(BF16)
            r.dproj[2 + k] = (dot(jnp.concatenate(grads, axis=1), r.qkv[k]) * factor).astype(BF16)

        loop(2, one_head)
        for copy in att_copies(c):
            copy.start()

        n3 = Parts("n3")

        def proj_rows():
            return jnp.concatenate([r.dproj[k] for k in range(6)], axis=1)

        n3.both(lambda core: dot_nt(proj_rows(), wproj(half_of(core))))

        for copy in att_copies(1 - c):
            copy.wait_recv()
            copy.wait_send()

        def result(i):
            left = jnp.concatenate([r.att[p, rows(i), :] for p in range(4)], axis=1)
            branch = dot(left, wtap(k3, 3, ALL)) + prow(12)
            r.ro_src[i] = pack_pixels(r.v3[rows(i), :] + branch).astype(BF16)

        loop(4, result)
        head_start(lambda p: r.ro_src.at[p], r.ro_dst, r.ro_s, r.ro_r)
        r.ro_dst[h] = r.ro_src[h]

        if inside:
            red1, red2, red3 = Reduce("r1", 3), Reduce("r2", 3), Reduce("r3", 1)
            acc1, acc2, acc3 = r.r1_acc, r.r2_acc, r.r3_acc
        else:
            acc1, acc2, acc3 = r.first, r.second, r.attend

        transpose_act(r.ai, 0, r.ai_t)
        attend_out = dot(jnp.concatenate([r.ai_t[0], r.ai_t[1]], axis=0), proj_rows())
        output_out = dot(jnp.concatenate([r.att_t[0], r.att_t[1]], axis=0), cot_all())
        for p, zc in enumerate(ALL):
            for yy in range(2):
                for xx in range(2):
                    row = p * 128 + yy * 48
                    tiles = [
                        attend_out[row : row + 48, (xx * 3 + j) * 128 : (xx * 3 + j) * 128 + 128] for j in range(3)
                    ]
                    acc3[0, slot(xx, yy), zc] = pack_four(
                        *tiles, output_out[row : row + 48, xx * 128 : xx * 128 + 128]
                    )
        if inside:
            red3.start(0)

        def proj_sums(i, carry):
            q = jnp.concatenate([r.dproj[0, rows(i), :], r.dproj[1, rows(i), :]], axis=1).astype(F32)
            val = jnp.concatenate([r.dproj[4, rows(i), :], r.dproj[5, rows(i), :]], axis=1).astype(F32)
            return (carry[0] + fold(q), carry[1] + fold(val), carry[2] + fold(r.cx[i].astype(F32)))

        qsum, vsum, csum = lax.fori_loop(0, 4, proj_sums, (zero8, zero8, zero8))
        r.sums[pl.ds(3 + 7, 1), :] = jnp.sum(qsum, axis=0, keepdims=True)
        r.sums[pl.ds(3 + 8, 1), :] = jnp.sum(vsum, axis=0, keepdims=True)
        r.sums[pl.ds(3 + 9, 1), :] = jnp.sum(csum, axis=0, keepdims=True)
        r.sums[pl.ds(13, 3), :] = jnp.zeros((3, HALF), F32)

        def n3_own(i, carry):
            vals = n3.get(i)
            r.gtmp[rows(i), :] = vals
            return carry[0] + fold(vals), carry[1] + fold(vals * hat3(i))

        n3.wait()
        sums3 = lax.fori_loop(0, 4, n3_own, (zero8, zero8))
        plain3, cross3, back3 = norm_back(sums3, lambda i: r.gtmp[rows(i), :], hat3, gain3, inv3)
        r.sums[pl.ds(2, 1), :] = cross3
        r.sums[pl.ds(3 + 2, 1), :] = plain3

        def shifted(buf, i, vals):
            buf[0, rows(i, CHUNK, ROW), :] = from_right(vals).astype(BF16)
            buf[1, rows(i, CHUNK, ROW), :] = vals.astype(BF16)
            buf[2, rows(i, CHUNK, ROW), :] = from_left(vals).astype(BF16)

        def residual_back(i, carry):
            vals = r.cx[i].astype(F32) + back3(i)
            r.gres[rows(i), :] = vals
            shifted(r.gr2, i, vals)
            return carry + fold(vals.astype(BF16).astype(F32))

        bias_two = lax.fori_loop(0, 4, residual_back, jnp.zeros((8, HALF), F32))
        r.sums[pl.ds(3 + 4, 1), :] = jnp.sum(bias_two, axis=0, keepdims=True)

        def act_back(buf, g, core):
            left = jnp.concatenate(
                [buf[b, pl.ds(2 * ROW - ROW * a, PX), :] for a in range(3) for b in range(3)], axis=1
            )
            right = jnp.concatenate(
                [wtap(g, 3 * a + b, half_of(core)) for a in range(3) for b in range(3)], axis=1
            )
            return dot_nt(left, right)

        def conv_back(parts, buf, g):
            parts.both(lambda core: act_back(buf, g, core))

        def conv_back_own(parts, outer, hat):
            parts.wait()

            def own(i, carry):
                grad = parts.get(i) * outer(i)
                r.gtmp[rows(i), :] = grad
                return carry[0] + fold(grad), carry[1] + fold(grad * hat(i))

            return lax.fori_loop(0, 4, own, (zero8, zero8))

        def kernel_grad(act_t, buf, acc, after):
            def step(a):
                right = jnp.concatenate([buf[b, pl.ds(2 * ROW - ROW * a, PX), :] for b in range(3)], axis=1)
                out = dot(jnp.concatenate([act_t[0], act_t[1]], axis=0), right)
                for p, zc in enumerate(ALL):
                    for yy in range(2):
                        for xx in range(2):
                            row = p * 128 + yy * 48
                            tiles = [
                                out[row : row + 48, b * HALF + xx * 128 : b * HALF + xx * 128 + 128] for b in range(3)
                            ]
                            acc[a, slot(xx, yy), zc] = pack_taps(*tiles)
                after(a)

            each(3, step)

        d2 = Parts("d2")
        conv_back(d2, r.gr2, k2)
        kernel_grad(r.act2_t, r.gr2, acc2, red2.start if inside else lambda a: None)

        sums2 = conv_back_own(d2, lambda i: silu_slope(pre2(i)), hat2)
        if inside:
            red3.second(0, 1)

        plain2, cross2, back2 = norm_back(sums2, lambda i: r.gtmp[rows(i), :], hat2, gain2 * scale, inv2)
        r.sums[pl.ds(1, 1), :] = scale * cross2
        r.sums[pl.ds(3 + 1, 1), :] = scale * plain2
        film_scale_term = gain2 * cross2 + shift2 * plain2
        r.sums[pl.ds(3 + 5, 1), :] = film_scale_term
        r.sums[pl.ds(3 + 6, 1), :] = plain2
        for j in range(2):
            r.ft[j] = film_scale_term[:, j * 128 : j * 128 + 128]
            r.ft[2 + j] = plain2[:, j * 128 : j * 128 + 128]
        head_start(lambda p: r.ft.at[p], r.th, r.th_s, r.th_r)
        r.th[h] = r.ft[h]

        def first_back(i, carry):
            vals = back2(i)
            shifted(r.gr1, i, vals)
            return carry + fold(vals.astype(BF16).astype(F32))

        bias_one = lax.fori_loop(0, 4, first_back, jnp.zeros((8, HALF), F32))
        r.sums[pl.ds(3 + 3, 1), :] = jnp.sum(bias_one, axis=0, keepdims=True)

        d1 = Parts("d1")
        if inside:
            red2.second(0, 3)
            red3.third(0, 1)
        kernel_grad(r.act1_t, r.gr1, acc1, red1.start if inside else lambda a: None)
        if inside:
            red2.third(0, 3)
        conv_back(d1, r.gr1, k1)

        head_wait(lambda p: r.ft.at[p], r.th, r.th_s, r.th_r)
        for m in range(2):
            r.fa[d, pl.ds(m, 1), :] = jnp.concatenate([r.th[2 * m], r.th[2 * m + 1]], axis=1)
        dp_start(lambda p: r.fa.at[d], r.fa, r.fa_s, r.fa_r)

        def hat1(i):
            return (mixed(i) - mean1) * inv1

        if inside:
            red1.second(0, 2)
        sums1 = conv_back_own(d1, lambda i: silu_slope(pre1(i)), hat1)
        if inside:
            red1.second(2, 1)
            red1.third(0, 2)

        plain1, cross1, back1 = norm_back(sums1, lambda i: r.gtmp[rows(i), :], hat1, gain1, inv1)
        r.sums[pl.ds(0, 1), :] = cross1
        r.sums[pl.ds(3, 1), :] = plain1
        r.ad[d] = r.sums[...]
        dp_start(lambda p: r.ad.at[d], r.ad, r.ad_s, r.ad_r)

        keep = r.coef[0, x]

        def image_back(i):
            r.io_src[i] = pack_pixels(keep * (r.gres[rows(i), :] + back1(i))).astype(BF16)

        loop(4, image_back)
        head_start(lambda p: r.io_src.at[p], r.io_dst, r.io_s, r.io_r)
        r.io_dst[h] = r.io_src[h]
        if inside:
            red1.third(2, 1)

        dp_wait(lambda p: r.fa.at[d], r.fa, r.fa_s, r.fa_r)
        for j in range(n):
            r.fta[pl.ds(2 * j, 2), :] = r.fa[j]
        film_block = dot_tn_high(r.esel[...], r.fta[...])
        r.film[...] = jnp.concatenate([film_block[:film_rows, :BLK], film_block[:film_rows, 128 : 128 + BLK]], axis=1)
        embed_part = dot_nt_high(r.fta[...], r.wfp[...].astype(F32))
        for j in range(n):
            r.ep[j] = embed_part[2 * j : 2 * j + 2]
        dp_start(lambda p: r.ep.at[p], r.er, r.er_s, r.er_r)
        r.er[d] = r.ep[d]

        dp_wait(lambda p: r.ad.at[d], r.ad, r.ad_s, r.ad_r)
        total = r.ad[0]
        for j in range(1, n):
            total = total + r.ad[j]
        r.hb[h] = total
        head_start(lambda p: r.hb.at[h], r.hb, r.hb_s, r.hb_r)
        head_wait(lambda p: r.ro_src.at[p], r.ro_dst, r.ro_s, r.ro_r)

        dp_wait(lambda p: r.ep.at[p], r.er, r.er_s, r.er_r)
        r.eh[h] = r.er[...]
        head_start(lambda p: r.eh.at[h], r.eh, r.eh_s, r.eh_r)

        if inside:
            red2.finish(((0, 3),))
            for a in range(3):
                r.second[a] = red2.last(a)

        head_wait(lambda p: r.hb.at[h], r.hb, r.hb_s, r.hb_r)
        even = r.hb[0] + r.hb[2]
        odd = r.hb[1] + r.hb[3]
        wide = jnp.concatenate(
            [even[:, :BLK], odd[:, :BLK], even[:, 128 : 128 + BLK], odd[:, 128 : 128 + BLK]], axis=1
        )
        r.gains_out[...] = wide[0:3]
        r.biases_out[...] = wide[3:13]

        head_wait(lambda p: r.eh.at[h], r.eh, r.eh_s, r.eh_r)
        pieces = []
        for j in range(n):
            piece = (r.eh[0, j] + r.eh[1, j]) + (r.eh[2, j] + r.eh[3, j])
            pieces.append(piece[:, :film_rows])
        r.embed_grad[...] = jnp.concatenate(pieces, axis=1) * silu_slope(r.emb[...].astype(F32))

        head_wait(lambda p: r.io_src.at[p], r.io_dst, r.io_s, r.io_r)

        if inside:
            red3.finish(((0, 1),))
            tiles = unpack_four(red3.last(0))
            r.sb_src[...] = jnp.where(c == 0, tiles[2], tiles[0])
            back = rc(r.sb_src, r.sb_dst, r.sb_s.at[0], r.sb_r.at[0], sib)
            back.start()
            r.output[...] = tiles[3]
            red1.finish(((0, 2), (2, 1)))
            for a in range(3):
                r.first[a] = red1.last(a)
            back.wait()
            r.attend[:, 0:128] = jnp.where(c == 0, tiles[0], tiles[1])
            r.attend[:, 128:256] = r.sb_dst[...]
            r.attend[:, 256:384] = jnp.where(c == 0, tiles[1], tiles[2])

    return kernel


def make_writer(names_in, names_out):
    def kernel(*refs):
        count = len(names_in)
        src, dst = Names(names_in, refs[:count]), Names(names_out, refs[count:])
        for name, packed in (("result", src.ro_dst), ("image_grad", src.io_dst)):
            for m in range(2):
                getattr(dst, name)[m] = dot_nt(unpack_pixels(packed[2 * m]), src.sel[0]) + dot_nt(
                    unpack_pixels(packed[2 * m + 1]), src.sel[1]
                )
        for name in ("first", "second"):
            if name in names_out:
                for a in range(3):
                    block = getattr(src, name)[a]
                    getattr(dst, name)[3 * a] = block[:48, :BLK]
                    getattr(dst, name)[3 * a + 1] = block[48:96, :BLK]
                    getattr(dst, name)[3 * a + 2] = last_tap(block)[:, :BLK]
        if "attend" in names_out:
            dst.attend[...] = jnp.concatenate([src.attend[:, j * 128 : j * 128 + BLK] for j in range(3)], axis=1)
            dst.output[...] = src.output[:, :BLK]
        for name in ("embed_grad", "film", "gains_out", "biases_out"):
            getattr(dst, name)[...] = getattr(src, name)[...]

    return kernel


def per_device(n, *args):
    (
        images,
        noise_field,
        time_steps,
        embedding,
        first_kernel,
        second_kernel,
        film_weight,
        attend_weight,
        output_weight,
        norm_gains,
        biases,
        cotangent,
    ) = args
    inside = n == 8
    keep, noise = plan(time_steps)
    coef = jnp.stack([keep, noise])
    maps, height, width, channels = images.shape
    flat_shape = (maps, height * width, channels)
    film_rows = film_weight.shape[0]
    inputs = dict(
        coef=coef,
        images=images.reshape(flat_shape),
        noise=noise_field.reshape(flat_shape),
        cot=cotangent.reshape(flat_shape),
        emb=embedding,
        k1=first_kernel.reshape((9,) + first_kernel.shape[2:]),
        k2=second_kernel.reshape((9,) + second_kernel.shape[2:]),
        wf=film_weight,
        wa=attend_weight,
        wo=output_weight,
        gains=norm_gains,
        biases=biases,
        sel=jnp.asarray(channel_lanes(), BF16),
        gmask=jnp.asarray(group_mask(), BF16),
        selp=jnp.asarray(block_lanes(3), BF16),
    )
    shapes = dict(
        ro_dst=(4, 384, 128),
        io_dst=(4, 384, 128),
        embed_grad=embedding.shape,
        first=(3, 112, 128),
        second=(3, 112, 128),
        film=film_weight.shape,
        attend=(48, 384),
        output=(48, 128),
        gains_out=norm_gains.shape,
        biases_out=biases.shape,
    )
    names_in, names_out = list(INPUTS), list(OUTPUTS)
    core = lax.axis_index("head") % 2
    if not inside:
        def whole(array, row_axis):
            array = lax.all_gather(array, "dp", axis=row_axis, tiled=True)
            return lax.all_gather(array, "head", axis=array.ndim - 1, tiled=True)

        def spread(array, count):
            taps = array.shape[0]
            array = array.reshape(taps, 4, 2, 48, 2, 2, BLK)
            array = lax.dynamic_index_in_dim(array, core, 5, keepdims=False)
            array = jnp.transpose(array, (2, 4, 1, 0, 3, 5))
            array = jnp.pad(array, ((0, 0),) * 5 + ((0, 32),))
            return array.reshape(4, 4, taps * 48, 128)

        full_a = whole(attend_weight, 0).reshape(384, 2, 3, 2, BLK)
        full_a = jnp.transpose(full_a, (2, 0, 1, 3, 4)).reshape(3, 384, 384)
        full_o = whole(output_weight, 0)[None]
        for name, last, array in (("g1", "t1", first_kernel), ("g2", "t2", second_kernel)):
            blocks = spread(whole(array, 2).reshape(9, 384, 384), 9).reshape(4, 4, 3, 3, 48, 128)
            two = blocks[:, :, :, :2].reshape(4, 4, 3, 96, 128)
            inputs[name] = jnp.pad(two, ((0, 0),) * 3 + ((0, 16), (0, 0))).reshape(4, 4, 336, 128)
            inputs[last] = blocks[:, :, :, 2].reshape(4, 4, 144, 128)
        inputs["g3"] = spread(jnp.concatenate([full_a, full_o], axis=0), 4)
        names_in += ["g1", "g2", "t1", "t2", "g3"]
        shapes["first"] = shapes["second"] = (3, 4, 4, 112, 128)
        shapes["attend"] = (1, 4, 4, 144, 128)
        del shapes["output"]
        names_out.remove("output")
    items = scratch_list(n, inside)
    smem = pl.BlockSpec(memory_space=pltpu.SMEM)
    vmem = pl.BlockSpec(memory_space=pltpu.VMEM)
    outs = pl.pallas_call(
        make_kernel(n, inside, names_in + names_out + [name for name, _ in items]),
        out_shape=[
            jax.ShapeDtypeStruct(shapes[name], BF16 if name in ("ro_dst", "io_dst") else F32) for name in names_out
        ],
        in_specs=[smem if name == "coef" else vmem for name in names_in],
        out_specs=[vmem] * len(names_out),
        scratch_shapes=[item for _, item in items],
        compiler_params=pltpu.CompilerParams(
            collective_id=0, has_side_effects=True, vmem_limit_bytes=63 * 1024 * 1024
        ),
        name="blocks",
    )(*[inputs[name] for name in names_in])
    raw = dict(zip(names_out, outs))
    final = dict(
        result=flat_shape,
        image_grad=flat_shape,
        embed_grad=embedding.shape,
        film=film_weight.shape,
        gains_out=norm_gains.shape,
        biases_out=biases.shape,
    )
    if inside:
        final.update(first=(9, 48, BLK), second=(9, 48, BLK), attend=attend_weight.shape, output=output_weight.shape)
    names_last = [name for name in names_out if inside or name not in ("first", "second", "attend")] + ["sel"]
    names_final = list(final)
    outs = pl.pallas_call(
        make_writer(names_last, names_final),
        out_shape=[jax.ShapeDtypeStruct(final[name], F32) for name in names_final],
        in_specs=[vmem] * len(names_last),
        out_specs=[vmem] * len(names_final),
        compiler_params=pltpu.CompilerParams(vmem_limit_bytes=63 * 1024 * 1024),
        name="outputs",
    )(*[inputs["sel"] if name == "sel" else raw[name] for name in names_last])
    out = dict(zip(names_final, outs))
    if not inside:

        def blocks_of(array, size):
            parts = [array[..., k * 48 : k * 48 + 48, :BLK] for k in range(size)]
            if size == 2:
                lanes = [array[..., k * 32 : k * 32 + 32, BLK:] for k in range(3)]
                lanes = jnp.concatenate(lanes, axis=-1)
                parts.append(jnp.concatenate([lanes, array[..., 96:112, :BLK]], axis=-2))
            else:
                lanes = [array[..., k * 48 : k * 48 + 48, BLK:] for k in range(3)]
                parts.append(jnp.concatenate(lanes, axis=-1))
            array = jnp.stack(parts, axis=1)
            array = array.reshape(array.shape[:2] + (2, 2, 4, 48, BLK))
            taps = array.shape[0] * array.shape[1]
            array = jnp.transpose(array, (0, 1, 4, 2, 5, 3, 6)).reshape(taps, 384, 2, 1, BLK)
            both = jnp.concatenate([array, jnp.zeros_like(array)], axis=3)
            return jnp.where(core == 0, both, both[:, :, :, ::-1]).reshape(taps, 384, 384)

        def shared(array, axis):
            array = lax.psum_scatter(array, "head", scatter_dimension=array.ndim - 1, tiled=True)
            return lax.psum_scatter(array, "dp", scatter_dimension=axis, tiled=True)

        out["first"] = shared(blocks_of(raw["first"], 2), 1)
        out["second"] = shared(blocks_of(raw["second"], 2), 1)
        both = blocks_of(raw["attend"], 3)
        joined = both[:3].reshape(3, 384, 2, 2, BLK)
        joined = jnp.transpose(joined, (1, 2, 0, 3, 4)).reshape(384, 1152)
        out["attend"] = shared(joined, 0)
        out["output"] = shared(both[3], 0)
    return (
        out["result"].reshape(images.shape),
        out["image_grad"].reshape(images.shape),
        out["embed_grad"],
        out["first"].reshape(first_kernel.shape),
        out["second"].reshape(second_kernel.shape),
        out["film"],
        out["attend"],
        out["output"],
        out["gains_out"],
        out["biases_out"],
    )


def solution(mesh):
    n = mesh.shape["dp"]
    field = P("dp", "head", None, None)
    taps = P(None, None, "dp", "head")
    both = P("dp", "head")
    return jax.shard_map(
        lambda *args: per_device(n, *args),
        mesh=mesh,
        in_specs=(field, field, P("dp"), P("dp", None), taps, taps, both, both, both, P(), P(), field),
        out_specs=(field, field, P("dp", None), taps, taps, both, both, both, P(), P()),
        check_vma=False,
    )
```

```python
import math

import jax
import jax.numpy as jnp
import numpy as np
from jax import lax
from jax.experimental import pallas as pl
from jax.experimental.pallas import tpu as pltpu
from jax.sharding import PartitionSpec as P

HEAD_DIM = 96
GROUPS = 32
STEPS = 4000
EPS = 1e-05
OFFSET = 0.008
MESH = pl.DeviceIdType.MESH
F32 = jnp.float32
BF16 = jnp.bfloat16

PX = 1024
ROW = 32
CHUNK = 256
BLK = 96
HALF = 256
NHEAD = 4


def plan(time_steps):
    fraction = (time_steps.astype(F32) + 1.0) / STEPS
    start = jnp.square(jnp.cos(jnp.float32(OFFSET / (1.0 + OFFSET) * (math.pi / 2))))
    curve = jnp.square(jnp.cos((fraction + OFFSET) / (1.0 + OFFSET) * (math.pi / 2))) / start
    return (jnp.sqrt(curve), jnp.sqrt(1.0 - curve))


def channel_lanes():
    sel = np.zeros((2, 384, HALF), np.float32)
    for block in range(4):
        for j in range(BLK):
            sel[block % 2, block * BLK + j, (block // 2) * 128 + j] = 1.0
    return sel


def block_lanes(count):
    sel = np.zeros((count * BLK, count * 128), np.float32)
    for block in range(count):
        for j in range(BLK):
            sel[block * BLK + j, block * 128 + j] = 1.0
    return sel


def group_mask():
    lane = np.arange(HALF)
    ok = lane % 128 < BLK
    group = (lane // 128) * 100 + (lane % 128) // 12
    return ((group[:, None] == group[None, :]) & ok[:, None] & ok[None, :]).astype(np.float32)


def dot(a, b):
    return lax.dot_general(a, b, (((1,), (0,)), ((), ())), preferred_element_type=F32)


def dot_nt(a, b):
    return lax.dot_general(a, b, (((1,), (1,)), ((), ())), preferred_element_type=F32)


def dot_nt_high(a, b):
    return lax.dot_general(
        a, b, (((1,), (1,)), ((), ())), preferred_element_type=F32, precision=lax.Precision.HIGHEST
    )


def dot_tn_high(a, b):
    return lax.dot_general(
        a, b, (((0,), (0,)), ((), ())), preferred_element_type=F32, precision=lax.Precision.HIGHEST
    )


def exact_dot(values, ones):
    high = values.astype(BF16).astype(F32)
    rest = values - high
    middle = rest.astype(BF16).astype(F32)
    low = rest - middle
    rows = values.shape[0]
    out = dot(jnp.concatenate([high, middle, low], axis=0).astype(BF16), ones)
    return out[:rows] + out[rows : 2 * rows] + out[2 * rows :]


def sigmoid(v):
    return 0.5 + 0.5 * jnp.tanh(0.5 * v)


def silu(v):
    return v * sigmoid(v)


def silu_slope(v):
    s = sigmoid(v)
    return s * (1.0 + v * (1.0 - s))


def pack_taps(t0, t1, t2):
    t0, t1, t2 = t0[:, :BLK], t1[:, :BLK], t2[:, :BLK]
    join = lambda a, b: jnp.concatenate([a, b], axis=1)
    return jnp.concatenate(
        [
            join(t0[:32], t2[:32, :32]),
            join(t0[32:], t2[:16, 32:64]),
            join(t1[:16], t2[16:32, 32:64]),
            join(t1[16:], t2[:32, 64:]),
            join(t2[32:], jnp.zeros((16, 32), t2.dtype)),
        ],
        axis=0,
    )


def last_tap(packed):
    lanes = [packed[:32, BLK:], packed[32:64, BLK:], packed[64:96, BLK:], jnp.zeros((32, 32), packed.dtype)]
    return jnp.concatenate([jnp.concatenate(lanes, axis=1), packed[96:112]], axis=0)


def pack_four(b0, b1, b2, b3):
    return jnp.concatenate(
        [jnp.concatenate([b[:, :BLK], b3[:, 32 * k : 32 * k + 32]], axis=1) for k, b in enumerate((b0, b1, b2))],
        axis=0,
    )


def unpack_four(packed):
    size = packed.shape[0] // 3
    parts = [packed[k * size : k * size + size] for k in range(3)]
    zero = jnp.zeros((size, 32), packed.dtype)
    fourth = jnp.concatenate([p[:, BLK:] for p in parts] + [zero], axis=1)
    return [jnp.concatenate([p[:, :BLK], zero], axis=1) for p in parts] + [fourth]


def pack_pixels(full):
    half = CHUNK // 2
    return pack_four(full[:half, :128], full[half:, :128], full[:half, 128:], full[half:, 128:])


def unpack_pixels(packed):
    b0, b1, b2, b3 = unpack_four(packed)
    return jnp.concatenate([jnp.concatenate([b0, b2], axis=1), jnp.concatenate([b1, b3], axis=1)], axis=0)


INPUTS = (
    "coef",
    "images",
    "noise",
    "cot",
    "emb",
    "k1",
    "k2",
    "wf",
    "wa",
    "wo",
    "gains",
    "biases",
    "sel",
    "gmask",
    "selp",
)
OUTPUTS = (
    "ro_dst",
    "io_dst",
    "embed_grad",
    "first",
    "second",
    "film",
    "attend",
    "output",
    "gains_out",
    "biases_out",
)


class Names:
    def __init__(self, names, refs):
        for name, ref in zip(names, refs):
            setattr(self, name, ref)


def scratch_list(n, inside):
    dma = pltpu.SemaphoreType.DMA
    items = []

    def vm(name, shape, dtype):
        items.append((name, pltpu.VMEM(shape, dtype)))

    def sem(name, count):
        items.append((name + "_s", dma((count,))))
        items.append((name + "_r", dma((count,))))

    for name in ("mx", "cx", "ro", "io"):
        vm(name + "_src", (4, 384, 128), BF16)
        if name in ("mx", "cx"):
            vm(name + "_dst", (4, 384, 128), BF16)
            vm(name, (4, CHUNK, HALF), BF16)
        sem(name, 4)
    for name in ("act1", "act2"):
        vm(name, (2, PX + 2 * ROW, HALF), BF16)
        vm(name + "_t", (2, HALF, PX), BF16)
        sem(name, 4)
    vm("ai", (2, PX, HALF), BF16)
    vm("ai_t", (2, HALF, PX), BF16)
    sem("ai", 4)
    vm("att", (4, PX, 128), BF16)
    vm("att_t", (2, HALF, PX), BF16)
    sem("att", 4)
    for name in ("do", "n3", "d2", "d1"):
        vm(name + "_src", (PX, HALF), BF16)
        vm(name + "_dst", (PX, HALF), BF16)
        sem(name, 2)
    vm("v2", (PX, HALF), F32)
    vm("v3", (PX, HALF), F32)
    vm("gres", (PX, HALF), F32)
    vm("gtmp", (PX, HALF), F32)
    vm("part", (PX, 3 * HALF), F32)
    vm("qkv", (6, PX, 128), BF16)
    vm("kvt", (4, 128, PX), BF16)
    vm("dout", (2, PX, 128), BF16)
    vm("dproj", (6, PX, 128), BF16)
    vm("gr2", (3, PX + 2 * ROW, HALF), BF16)
    vm("gr1", (3, PX + 2 * ROW, HALF), BF16)
    vm("par", (16, 384), F32)
    vm("parown", (16, HALF), F32)
    vm("stat", (16, HALF), F32)
    vm("sums", (16, HALF), F32)
    if inside:
        vm("g1", (4, 4, 336, 128), BF16)
        vm("g2", (4, 4, 336, 128), BF16)
        vm("t1", (4, 4, 144, 128), BF16)
        vm("t2", (4, 4, 144, 128), BF16)
        vm("p3", (4, 4, 144, 128), BF16)
        vm("g3", (4, 4, 192, 128), BF16)
        for name in ("g1", "g2", "p3"):
            sem(name + "z", 4)
            sem(name + "v", 4)
            sem(name + "w", 8)
        vm("sw_src", (48, 128), BF16)
        vm("sw_dst", (48, 128), BF16)
        sem("sw", 1)
        vm("sb_src", (48, 128), F32)
        vm("sb_dst", (48, 128), F32)
        sem("sb", 1)
        for name, nc, rows in (("r1", 3, 112), ("r2", 3, 112), ("r3", 1, 144)):
            vm(name + "_acc", (nc, 4, 4, rows, 128), F32)
            vm(name + "w_src", (nc, 2, 4, rows, 128), BF16)
            vm(name + "w_dst", (nc, 2, 4, rows, 128), BF16)
            vm(name + "v_src", (nc, 4, rows, 128), BF16)
            vm(name + "v_dst", (nc, 4, rows, 128), BF16)
            vm(name + "z_src", (4, nc, rows, 128), BF16)
            vm(name + "z_dst", (4, nc, rows, 128), BF16)
            sem(name + "w", nc)
            sem(name + "v", nc)
            sem(name + "z", nc * 4)
    vm("el", (n, 2, 768), F32)
    sem("el", n)
    vm("em", (2 * n, 768), F32)
    vm("wfp", (128, HALF), BF16)
    vm("esel", (2 * n, 128), F32)
    vm("fp", (n, 2, HALF), F32)
    vm("fr", (n, 2, HALF), F32)
    sem("fr", n)
    vm("fx", (4, 1, 128), F32)
    vm("fh", (4, 1, 128), F32)
    sem("fh", 4)
    vm("ft", (4, 1, 128), F32)
    vm("th", (4, 1, 128), F32)
    sem("th", 4)
    vm("fa", (n, 2, HALF), F32)
    sem("fa", n)
    vm("fta", (2 * n, HALF), F32)
    vm("ep", (n, 2, 128), F32)
    vm("er", (n, 2, 128), F32)
    sem("er", n)
    vm("eh", (4, n, 2, 128), F32)
    sem("eh", 4)
    vm("ad", (n, 16, HALF), F32)
    sem("ad", n)
    vm("hb", (4, 16, HALF), F32)
    sem("hb", 4)
    return items


def make_kernel(n, inside, names):
    film_rows = 768 // n

    def kernel(*refs):
        r = Names(names, refs)
        d = lax.axis_index("dp")
        h = lax.axis_index("head")
        x = h // 2
        c = h - 2 * x
        z = d // 2
        y = d - 2 * z
        sib = (d, h + 1 - 2 * c)
        xdev = (d, h + 2 - 4 * x)
        v = x + c * (y - x)
        w = y + c * (x - y)
        vdev = (d + c * (1 - 2 * y), h + (1 - c) * (2 - 4 * x))
        wdev = (d + (1 - c) * (1 - 2 * y), h + c * (2 - 4 * x))

        def slot(xx, yy):
            if inside:
                return (yy + c * (xx - yy)) * 2 + xx + c * (yy - xx)
            return yy * 2 + xx

        def rc(src, dst, send, recv, dev):
            return pltpu.make_async_remote_copy(
                src_ref=src, dst_ref=dst, send_sem=send, recv_sem=recv, device_id=dev, device_id_type=MESH
            )

        def loop(count, body):
            def step(i, carry):
                body(i)
                return carry

            lax.fori_loop(0, count, step, 0)

        def each(count, body):
            for i in range(count):
                body(i)

        def rows(i, size=CHUNK, base=0):
            return pl.ds(pl.multiple_of(base + i * size, 32), size)

        def dp_start(src_of, dst, send, recv):
            def step(k, carry):
                peer = lax.rem(d + k, n)
                rc(src_of(peer), dst.at[d], send.at[k], recv.at[d], (peer, h)).start()
                return carry

            lax.fori_loop(1, n, step, 0)

        def dp_wait(src_of, dst, send, recv):
            def step(k, carry):
                peer = lax.rem(d + k, n)
                copy = rc(src_of(peer), dst.at[peer], send.at[k], recv.at[peer], (peer, h))
                copy.wait_recv()
                copy.wait_send()
                return carry

            lax.fori_loop(1, n, step, 0)

        def head_start(src_of, dst, send, recv):
            for k in range(1, 4):
                peer = lax.rem(h + k, 4)
                rc(src_of(peer), dst.at[h], send.at[k], recv.at[h], (d, peer)).start()

        def head_wait(src_of, dst, send, recv):
            for k in range(1, 4):
                peer = lax.rem(h + k, 4)
                copy = rc(src_of(peer), dst.at[peer], send.at[k], recv.at[peer], (d, peer))
                copy.wait_recv()
                copy.wait_send()

        class Halves:
            def __init__(self, name, base):
                self.buf, self.base = getattr(r, name), base
                self.send, self.recv = getattr(r, name + "_s"), getattr(r, name + "_r")

            def at(self, core, i):
                return self.buf.at[core, rows(i, CHUNK, self.base)]

            def fill(self, make):
                def body(i):
                    self.buf[c, rows(i, CHUNK, self.base), :] = make(i)
                    ref = self.at(c, i)
                    rc(ref, ref, self.send.at[i], self.recv.at[i], sib).start()

                loop(4, body)

            def wait(self):
                for i in range(4):
                    ref = self.at(1 - c, i)
                    copy = rc(ref, ref, self.send.at[i], self.recv.at[i], sib)
                    copy.wait_recv()
                    copy.wait_send()

        class Parts:
            def __init__(self, name):
                self.src, self.dst = getattr(r, name + "_src"), getattr(r, name + "_dst")
                self.send, self.recv = getattr(r, name + "_s"), getattr(r, name + "_r")

            def copy(self, i):
                at = rows(i, 2 * CHUNK)
                return rc(self.src.at[at], self.dst.at[at], self.send.at[i], self.recv.at[i], sib)

            def fill(self, make):
                def body(i):
                    self.src[rows(i, 2 * CHUNK), :] = make(i).astype(BF16)
                    self.copy(i).start()

                each(2, body)

            def get(self, i):
                copy = self.copy(i)
                copy.wait_recv()
                copy.wait_send()
                return self.dst[rows(i, 2 * CHUNK), :].astype(F32)

        class Gather:
            def __init__(self, name):
                self.g = getattr(r, name)
                self.zs, self.zr = getattr(r, name + "z_s"), getattr(r, name + "z_r")
                self.vs, self.vr = getattr(r, name + "v_s"), getattr(r, name + "v_r")
                self.ws, self.wr = getattr(r, name + "w_s"), getattr(r, name + "w_r")

            def zcopy(self, k):
                peer = (lax.rem(z + k, 4) * 2 + y, h)
                return rc(
                    self.g.at[w * 2 + v, 0], self.g.at[w * 2 + v, 4 - k], self.zs.at[k], self.zr.at[4 - k], peer
                )

            def vcopy(self, vv, i):
                ref = self.g.at[w * 2 + vv, i]
                return rc(ref, ref, self.vs.at[i], self.vr.at[i], vdev)

            def wcopy(self, ww, other, i):
                ref = self.g.at[ww * 2 + v + other * (1 - 2 * v), i]
                return rc(ref, ref, self.ws.at[2 * i + other], self.wr.at[2 * i + other], wdev)

            def own(self):
                for k in range(1, 4):
                    self.zcopy(k).start()
                self.vcopy(v, 0).start()
                self.wcopy(w, 0, 0).start()

            def pass_z(self):
                self.vcopy(1 - v, 0).wait_recv()
                self.wcopy(w, 1, 0).start()
                for k in range(1, 4):
                    self.zcopy(k).wait_recv()
                    self.vcopy(v, 4 - k).start()
                    self.wcopy(w, 0, 4 - k).start()

            def pass_v(self):
                for k in range(1, 4):
                    self.vcopy(1 - v, 4 - k).wait_recv()
                    self.wcopy(w, 1, 4 - k).start()

            def done(self):
                for k in range(1, 4):
                    self.zcopy(k).wait_send()
                for i in range(4):
                    self.vcopy(v, i).wait_send()
                    for other in range(2):
                        self.wcopy(1 - w, other, i).wait_recv()
                        self.wcopy(w, other, i).wait_send()

        class Reduce:
            def __init__(self, name, count):
                get = lambda tail: getattr(r, name + tail)
                self.acc, self.count = get("_acc"), count
                self.wsrc, self.wdst, self.ws, self.wr = get("w_src"), get("w_dst"), get("w_s"), get("w_r")
                self.vsrc, self.vdst, self.vs, self.vr = get("v_src"), get("v_dst"), get("v_s"), get("v_r")
                self.zsrc, self.zdst, self.zs, self.zr = get("z_src"), get("z_dst"), get("z_s"), get("z_r")

            def wcopy(self, a):
                return rc(self.wsrc.at[a], self.wdst.at[a], self.ws.at[a], self.wr.at[a], wdev)

            def vcopy(self, a, size):
                at = pl.ds(a, size)
                return rc(self.vsrc.at[at], self.vdst.at[at], self.vs.at[a], self.vr.at[a], vdev)

            def zcopy(self, a, size, k):
                at = pl.ds(a, size)
                return rc(
                    self.zsrc.at[k, at],
                    self.zdst.at[4 - k, at],
                    self.zs.at[a * 4 + k],
                    self.zr.at[a * 4 + 4 - k],
                    (lax.rem(z + k, 4) * 2 + y, h),
                )

            def start(self, a):
                def step(i, carry):
                    vv, zz = i // 4, lax.rem(i, 4)
                    self.wsrc[a, vv, zz] = self.acc[a, (1 - w) * 2 + vv, zz].astype(BF16)
                    return carry

                lax.fori_loop(0, 8, step, 0)
                self.wcopy(a).start()

            def second(self, first, size):
                for a in range(first, first + size):
                    self.wcopy(a).wait_recv()

                    def step(zz, carry):
                        self.vsrc[a, zz] = (
                            self.acc[a, w * 2 + 1 - v, zz] + self.wdst[a, 1 - v, zz].astype(F32)
                        ).astype(BF16)
                        return carry

                    lax.fori_loop(0, 4, step, 0)
                self.vcopy(first, size).start()

            def third(self, first, size):
                self.vcopy(first, size).wait_recv()
                for a in range(first, first + size):

                    def step(k, carry):
                        zz = lax.rem(z + k, 4)
                        total = (
                            self.acc[a, w * 2 + v, zz]
                            + self.wdst[a, v, zz].astype(F32)
                            + self.vdst[a, zz].astype(F32)
                        )
                        self.acc[a, w * 2 + v, zz] = total
                        self.zsrc[k, a] = total.astype(BF16)
                        return carry

                    lax.fori_loop(0, 4, step, 0)
                for k in range(1, 4):
                    self.zcopy(first, size, k).start()

            def finish(self, groups):
                for first, size in groups:
                    self.vcopy(first, size).wait_send()
                    for k in range(1, 4):
                        copy = self.zcopy(first, size, k)
                        copy.wait_recv()
                        copy.wait_send()
                for a in range(self.count):
                    self.wcopy(a).wait_send()

            def last(self, a):
                total = self.acc[a, w * 2 + v, z]
                for k in range(1, 4):
                    total = total + self.zdst[k, a].astype(F32)
                return total

        def rel(zc):
            return lax.rem(zc - z + 4, 4) if inside else zc

        class Taps:
            def __init__(self, packed, last):
                self.packed, self.last = packed, last

            def block(self, tap, zc, xx, yy):
                a, b = tap // 3, tap % 3
                if b < 2:
                    return self.packed[slot(xx, yy), rel(zc), pl.ds(a * 112 + b * 48, 48), :]
                return self.last[slot(xx, yy), rel(zc), pl.ds(a * 48, 48), :]

            def unpack(self):
                def step(i, carry):
                    q, zz = i // 4, lax.rem(i, 4)
                    for a in range(3):
                        self.last[q, zz, pl.ds(a * 48, 48), :] = last_tap(
                            self.packed[q, zz, pl.ds(a * 112, 112), :]
                        )
                    return carry

                lax.fori_loop(0, 16, step, 0)

        class Plain:
            def __init__(self, blocks):
                self.blocks = blocks

            def block(self, tap, zc, xx, yy):
                return self.blocks[slot(xx, yy), rel(zc), pl.ds(tap * 48, 48), :]

            def unpack(self):
                def step(i, carry):
                    q, zz = i // 4, lax.rem(i, 4)
                    self.blocks[q, zz] = jnp.concatenate(unpack_four(r.p3[q, zz]), axis=0)
                    return carry

                lax.fori_loop(0, 16, step, 0)

        k1, k2, k3 = Taps(r.g1, r.t1), Taps(r.g2, r.t2), Plain(r.g3)

        def wtile(g, tap, zc, xx):
            return jnp.concatenate(
                [g.block(tap, zc, xx, 0), g.block(tap, zc, xx, 1), jnp.zeros((32, 128), BF16)], axis=0
            )

        def wtap(g, tap, zcs):
            return jnp.concatenate(
                [jnp.concatenate([wtile(g, tap, zc, xx) for xx in range(2)], axis=1) for zc in zcs], axis=0
            )

        ALL = (0, 2, 1, 3)

        def half_of(core):
            return (core, core + 2)

        def wproj(zcs):
            return jnp.concatenate(
                [
                    jnp.concatenate([wtile(k3, j, zc, xx) for xx in range(2) for j in range(3)], axis=1)
                    for zc in zcs
                ],
                axis=0,
            )

        def flat(buf, base, i, size):
            return jnp.concatenate([buf[0, rows(i, size, base), :], buf[1, rows(i, size, base), :]], axis=1)

        barrier = pltpu.get_barrier_semaphore()

        def greet(k, carry):
            pl.semaphore_signal(barrier, inc=1, device_id=(lax.rem(d + k, n), h), device_id_type=MESH)
            return carry

        lax.fori_loop(1, n, greet, 0)
        for k in range(1, 4):
            pl.semaphore_signal(barrier, inc=1, device_id=(d, lax.rem(h + k, 4)), device_id_type=MESH)
        if inside:
            for a in range(3):
                r.g1[w * 2 + v, 0, pl.ds(a * 112, 112), :] = pack_taps(*[r.k1[3 * a + b] for b in range(3)])
        pl.semaphore_wait(barrier, n - 1 + 3)
        if inside:
            ga, gb, gc = Gather("g1"), Gather("g2"), Gather("p3")
            ga.own()

        def mix(m, carry):
            field = r.coef[0, m] * r.images[m].astype(F32) + r.coef[1, m] * r.noise[m].astype(F32)
            low = field.astype(BF16)
            for core in range(2):
                r.mx_src[m * 2 + core] = pack_pixels(dot(low, r.sel[core])).astype(BF16)
            return carry

        lax.fori_loop(0, 2, mix, 0)
        head_start(lambda p: r.mx_src.at[p], r.mx_dst, r.mx_s, r.mx_r)
        r.mx_dst[h] = r.mx_src[h]

        r.el[d] = silu(r.emb[...].astype(F32)).astype(BF16).astype(F32)
        dp_start(lambda p: r.el.at[d], r.el, r.el_s, r.el_r)

        if inside:
            blocks = dot(r.wa[...], r.selp[: 3 * BLK, : 3 * 128]).astype(BF16)
            r.sw_src[...] = blocks[:, 128:256]
            swap = rc(r.sw_src, r.sw_dst, r.sw_s.at[0], r.sw_r.at[0], sib)
            swap.start()
            for a in range(3):
                r.g2[w * 2 + v, 0, pl.ds(a * 112, 112), :] = pack_taps(*[r.k2[3 * a + b] for b in range(3)])
        r.par[0:3, :] = r.gains[...]
        r.par[3:13, :] = r.biases[...]
        r.par[13:16, :] = jnp.zeros((3, 384), F32)
        r.parown[...] = exact_dot(r.par[...], r.sel[c])

        def prow(i):
            return r.parown[pl.ds(i, 1), :]

        for buf in (r.act1, r.act2):
            for core in range(2):
                buf[core, pl.ds(0, ROW), :] = jnp.zeros((ROW, HALF), BF16)
                buf[core, pl.ds(PX + ROW, ROW), :] = jnp.zeros((ROW, HALF), BF16)
        for buf in (r.gr1, r.gr2):
            for b in range(3):
                buf[b, pl.ds(0, ROW), :] = jnp.zeros((ROW, HALF), BF16)
                buf[b, pl.ds(PX + ROW, ROW), :] = jnp.zeros((ROW, HALF), BF16)
        r.wfp[...] = jnp.zeros((128, HALF), BF16)
        r.wfp[pl.ds(0, film_rows), :] = dot(r.wf[...], r.selp[: 2 * BLK, :HALF]).astype(BF16)
        if inside:
            ga.pass_z()
            gb.own()

        count = float(PX * 12)

        def fold(vals):
            return jnp.sum(vals.reshape(CHUNK // 8, 8, HALF), axis=0)

        def sums_of(fn, k):
            def step(i, carry):
                return tuple(a + fold(b) for a, b in zip(carry, fn(i)))

            zero = jnp.zeros((8, HALF), F32)
            return lax.fori_loop(0, 4, step, (zero,) * k)

        def group_mean(part):
            return jnp.sum(exact_dot(part, r.gmask[...]), axis=0, keepdims=True) / count

        def norm(load, which, total):
            mean = group_mean(total)
            (square,) = sums_of(lambda i: (jnp.square(load(i) - mean),), 1)
            inv = lax.rsqrt(group_mean(square) + EPS)
            r.stat[pl.ds(2 * which, 1), :] = mean
            r.stat[pl.ds(2 * which + 1, 1), :] = inv
            return mean, inv

        zero8 = jnp.zeros((8, HALF), F32)

        def norm_back(sums, load_grad, load_hat, coef, inv):
            plain, cross = sums
            plain_mean, cross_mean = group_mean(coef * plain), group_mean(coef * cross)
            outer, base, slope = inv * coef, inv * plain_mean, inv * cross_mean

            def chunk(i):
                return outer * load_grad(i) - base - load_hat(i) * slope

            return (
                jnp.sum(plain, axis=0, keepdims=True),
                jnp.sum(cross, axis=0, keepdims=True),
                chunk,
            )

        head_wait(lambda p: r.mx_src.at[p], r.mx_dst, r.mx_s, r.mx_r)

        def unpack_mixed(i, carry):
            vals = unpack_pixels(r.mx_dst[i])
            r.mx[i] = vals
            return carry + fold(vals.astype(F32))

        mixed_sum = lax.fori_loop(0, 4, unpack_mixed, zero8)

        def mixed(i):
            return r.mx[i].astype(F32)

        mean1, inv1 = norm(mixed, 0, mixed_sum)
        gain1, shift1 = prow(0), prow(3)
        act1 = Halves("act1", ROW)

        def affine(mean, inv, gain, shift):
            return inv * gain, shift - mean * (inv * gain)

        mul1, add1 = affine(mean1, inv1, gain1, shift1)

        def pre1(i):
            return mixed(i) * mul1 + add1

        act1.fill(lambda i: silu(pre1(i)).astype(BF16))
        if inside:
            ga.pass_v()

        dp_wait(lambda p: r.el.at[d], r.el, r.el_s, r.el_r)
        for j in range(n):
            r.em[pl.ds(2 * j, 2), :] = r.el[j]
        place = lax.broadcasted_iota(jnp.int32, (768, 128), 0) - film_rows * d
        lane = lax.broadcasted_iota(jnp.int32, (768, 128), 1)
        pick = jnp.where((place == lane) & (lane < film_rows), 1.0, 0.0).astype(BF16)
        r.esel[...] = dot(r.em[...].astype(BF16), pick)
        film_part = dot(r.esel[...].astype(BF16), r.wfp[...])
        for j in range(n):
            r.fp[j] = film_part[2 * j : 2 * j + 2]
        dp_start(lambda p: r.fp.at[p], r.fr, r.fr_s, r.fr_r)
        r.fr[d] = r.fp[d]
        if inside:
            swap.wait()
            got = r.sw_dst[...]
            keep0, keep2 = blocks[:, :128], blocks[:, 256:]
            r.p3[w * 2 + v, 0] = pack_four(
                jnp.where(c == 0, keep0, got),
                jnp.where(c == 0, keep2, keep0),
                jnp.where(c == 0, got, keep2),
                r.wo[...],
            )
            gb.pass_z()
            gc.own()
        def split_cot(m, carry):
            for core in range(2):
                r.cx_src[m * 2 + core] = pack_pixels(dot(r.cot[m], r.sel[core])).astype(BF16)
            return carry

        lax.fori_loop(0, 2, split_cot, 0)
        column = lax.broadcasted_iota(jnp.int32, (1, ROW, HALF), 1)
        not_first = jnp.where(column > 0, 1.0, 0.0)
        not_last = jnp.where(column < ROW - 1, 1.0, 0.0)

        def in_rows(vals, mask):
            return (vals.reshape(CHUNK // ROW, ROW, HALF) * mask).reshape(CHUNK, HALF)

        def from_left(vals):
            return in_rows(pltpu.roll(vals, 1, 0), not_first)

        def from_right(vals):
            return in_rows(pltpu.roll(vals, CHUNK - 1, 0), not_last)

        def transpose_act(buf, base, out, core):
            for q in range(4):
                out[core, :, pl.ds(q * CHUNK, CHUNK)] = jnp.transpose(
                    buf[core, pl.ds(base + q * CHUNK, CHUNK), :]
                )

        def conv(buf, g, store, between, wait=None):
            weights = lambda: jnp.concatenate(
                [jnp.concatenate([wtap(g, 3 * a + b, ALL) for b in range(3)], axis=1) for a in range(3)], axis=0
            )

            def taps(core, b):
                return jnp.concatenate([wtap(g, 3 * a + b, half_of(core)) for a in range(3)], axis=0)

            def half(core, i):
                left = jnp.concatenate(
                    [buf[core, pl.ds(ROW * a + 2 * CHUNK * i, 2 * CHUNK), :] for a in range(3)], axis=1
                )
                return dot(left, jnp.concatenate([taps(core, b) for b in range(3)], axis=1))

            def combine(i, out):
                total = zero8
                for j in range(2):
                    part = out[j * CHUNK : j * CHUNK + CHUNK]
                    part = part[:, HALF : 2 * HALF] + from_left(part[:, :HALF]) + from_right(part[:, 2 * HALF :])
                    total = total + fold(store(2 * i + j, part))
                return total

            total = zero8
            if wait is None:
                for i in range(2):
                    left = jnp.concatenate([flat(buf, ROW * a, i, 2 * CHUNK) for a in range(3)], axis=1)
                    total = total + combine(i, dot(left, weights()))
                    if i == 0:
                        between()
                return total
            for i in range(2):
                r.part[pl.ds(2 * CHUNK * i, 2 * CHUNK), :] = half(c, i)
            wait()
            for i in range(2):
                total = total + combine(i, r.part[pl.ds(2 * CHUNK * i, 2 * CHUNK), :] + half(1 - c, i))
                if i == 0:
                    between()
            return total

        act1.wait()
        for core in range(2):
            transpose_act(r.act1, ROW, r.act1_t, core)
        if inside:
            ga.done()
            k1.unpack()

        def store_v2(i, vals):
            vals = vals + prow(6)
            r.v2[rows(i), :] = vals
            return vals

        v2_sum = conv(r.act1, k1, store_v2, gb.pass_v if inside else lambda: None)
        dp_wait(lambda p: r.fp.at[p], r.fr, r.fr_s, r.fr_r)
        film_sum = r.fr[0]
        for j in range(1, n):
            film_sum = film_sum + r.fr[j]
        for m in range(2):
            for core in range(2):
                r.fx[m * 2 + core] = film_sum[m : m + 1, core * 128 : core * 128 + 128]
        head_start(lambda p: r.fx.at[p], r.fh, r.fh_s, r.fh_r)
        r.fh[h] = r.fx[h]

        head_wait(lambda p: r.fx.at[p], r.fh, r.fh_s, r.fh_r)
        scale = 1.0 + (jnp.concatenate([r.fh[0], r.fh[1]], axis=1) + prow(8))
        shift = jnp.concatenate([r.fh[2], r.fh[3]], axis=1) + prow(9)
        head_start(lambda p: r.cx_src.at[p], r.cx_dst, r.cx_s, r.cx_r)
        r.cx_dst[h] = r.cx_src[h]
        mean2, inv2 = norm(lambda i: r.v2[rows(i), :], 1, v2_sum)
        gain2, shift2 = prow(1), prow(4)
        act2 = Halves("act2", ROW)

        def hat2(i):
            return (r.v2[rows(i), :] - mean2) * inv2

        mul2, add2 = affine(mean2, inv2, gain2 * scale, shift2 * scale + shift)

        def pre2(i):
            return r.v2[rows(i), :] * mul2 + add2

        act2.fill(lambda i: silu(pre2(i)).astype(BF16))
        if inside:
            gc.pass_z()

        transpose_act(r.act2, ROW, r.act2_t, c)
        if inside:
            gb.done()
            k2.unpack()

        def store_v3(i, vals):
            vals = mixed(i) + (vals + prow(7))
            r.v3[rows(i), :] = vals
            return vals

        v3_sum = conv(r.act2, k2, store_v3, gc.pass_v if inside else lambda: None, act2.wait)
        mean3, inv3 = norm(lambda i: r.v3[rows(i), :], 2, v3_sum)
        gain3, shift3 = prow(2), prow(5)
        ai = Halves("ai", 0)

        def hat3(i):
            return (r.v3[rows(i), :] - mean3) * inv3

        mul3, add3 = affine(mean3, inv3, gain3, shift3)
        ai.fill(lambda i: (r.v3[rows(i), :] * mul3 + add3).astype(BF16))

        if inside:
            gc.done()
            k3.unpack()
        for i in range(2):
            at = pl.ds(2 * CHUNK * i, 2 * CHUNK)
            r.part[at, :] = dot(r.ai[c, at, :], wproj(half_of(c)))
        transpose_act(r.act2, ROW, r.act2_t, 1 - c)
        transpose_act(r.ai, 0, r.ai_t, c)
        head_wait(lambda p: r.cx_src.at[p], r.cx_dst, r.cx_s, r.cx_r)

        def unpack_cot(i):
            r.cx[i] = unpack_pixels(r.cx_dst[i])

        loop(4, unpack_cot)
        dop = Parts("do")

        def cot_rows(i):
            return jnp.concatenate([r.cx[2 * i], r.cx[2 * i + 1]], axis=0)

        dop.fill(lambda i: dot_nt(cot_rows(i), wtap(k3, 3, half_of(1 - c))))

        ai.wait()
        bias_proj = [prow(10)[:, :128], prow(10)[:, 128:], None, None, prow(11)[:, :128], prow(11)[:, 128:]]

        def project(i):
            at = rows(i, 2 * CHUNK)
            out = r.part[at, :] + dot(r.ai[1 - c, at, :], wproj(half_of(1 - c)))
            for k in range(6):
                part = out[:, k * 128 : k * 128 + 128]
                if bias_proj[k] is not None:
                    part = part + bias_proj[k]
                r.qkv[k, at, :] = part.astype(BF16)

        each(2, project)

        def do_own(i):
            full = (dot_nt(cot_rows(i), wtap(k3, 3, half_of(c))) + dop.get(i)).astype(BF16)
            for k in range(2):
                r.dout[k, rows(i, 2 * CHUNK), :] = full[:, k * 128 : k * 128 + 128]

        each(2, do_own)

        factor = 1.0 / math.sqrt(HEAD_DIM)
        factor2 = factor * math.log2(math.e)
        att = []

        def transposes(k):
            r.kvt[k] = jnp.transpose(r.qkv[k + 2])

        loop(4, transposes)

        def att_copy(core, k):
            ref = r.att.at[core * 2 + k]
            return rc(ref, ref, r.att_s.at[k], r.att_r.at[k], sib)

        def att_t_copy(core, k):
            ref = r.att_t.at[core, pl.ds(pl.multiple_of(k * 128, 128), 128)]
            return rc(ref, ref, r.att_s.at[2 + k], r.att_r.at[2 + k], sib)

        def one_head(k):
            lows, grads = [], []
            for b in range(2):
                at = pl.ds(b * 2 * CHUNK, 2 * CHUNK)
                query = r.qkv[k, at, :]
                grad = r.dout[k, at, :]
                scores = dot_nt(r.qkv[2 + k], query)
                peak = jnp.max(scores, axis=0, keepdims=True)
                expo = jnp.exp2((scores - peak) * factor2)
                inverse = 1.0 / jnp.sum(expo, axis=0, keepdims=True)
                low = (expo * inverse).astype(BF16)
                got = dot(r.kvt[2 + k], low)
                got_low = got.astype(BF16)
                r.att_t[c, pl.ds(pl.multiple_of(k * 128, 128), 128), at] = got_low
                r.att[2 * c + k, at, :] = jnp.transpose(got_low)
                spread = jnp.sum(got * jnp.transpose(grad).astype(F32), axis=0, keepdims=True)
                probs_grad = dot_nt(r.qkv[4 + k], grad)
                scores_grad = ((probs_grad - spread) * inverse * expo).astype(BF16)
                back = dot(r.kvt[k], scores_grad)
                r.dproj[k, at, :] = (jnp.transpose(back) * factor).astype(BF16)
                lows.append(low)
                grads.append(scores_grad)
            att_copy(c, k).start()
            att_t_copy(c, k).start()
            r.dproj[4 + k] = dot(jnp.concatenate(lows, axis=1), r.dout[k]).astype(BF16)
            r.dproj[2 + k] = (dot(jnp.concatenate(grads, axis=1), r.qkv[k]) * factor).astype(BF16)

        loop(2, one_head)

        n3 = Parts("n3")

        def proj_rows(i):
            return jnp.concatenate([r.dproj[k, rows(i, 2 * CHUNK), :] for k in range(6)], axis=1)

        n3.fill(lambda i: dot_nt(proj_rows(i), wproj(half_of(1 - c))))

        for k in range(2):
            copy = att_copy(1 - c, k)
            copy.wait_recv()
            copy.wait_send()

        def result(i):
            left = jnp.concatenate([r.att[p, rows(i), :] for p in range(4)], axis=1)
            branch = dot(left, wtap(k3, 3, ALL)) + prow(12)
            r.ro_src[i] = pack_pixels(r.v3[rows(i), :] + branch).astype(BF16)

        loop(4, result)
        head_start(lambda p: r.ro_src.at[p], r.ro_dst, r.ro_s, r.ro_r)
        r.ro_dst[h] = r.ro_src[h]

        if inside:
            red1, red2, red3 = Reduce("r1", 3), Reduce("r2", 3), Reduce("r3", 1)
            acc1, acc2, acc3 = r.r1_acc, r.r2_acc, r.r3_acc
        else:
            acc1, acc2, acc3 = r.first, r.second, r.attend

        transpose_act(r.ai, 0, r.ai_t, 1 - c)
        for k in range(2):
            copy = att_t_copy(1 - c, k)
            copy.wait_recv()
            copy.wait_send()
        right = jnp.concatenate([r.dproj[k] for k in range(6)], axis=1)
        cot_all = jnp.concatenate([r.cx[i] for i in range(4)], axis=0)
        for core in range(2):
            attend_out = dot(r.ai_t[core], right)
            output_out = dot(r.att_t[core], cot_all)
            for k in range(2):
                for yy in range(2):
                    for xx in range(2):
                        row = k * 128 + yy * 48
                        tiles = [
                            attend_out[row : row + 48, (xx * 3 + j) * 128 : (xx * 3 + j) * 128 + 128] for j in range(3)
                        ]
                        acc3[0, slot(xx, yy), core + 2 * k] = pack_four(
                            *tiles, output_out[row : row + 48, xx * 128 : xx * 128 + 128]
                        )
        if inside:
            red3.start(0)

        def proj_sums(i, carry):
            q = jnp.concatenate([r.dproj[0, rows(i), :], r.dproj[1, rows(i), :]], axis=1).astype(F32)
            val = jnp.concatenate([r.dproj[4, rows(i), :], r.dproj[5, rows(i), :]], axis=1).astype(F32)
            return (carry[0] + fold(q), carry[1] + fold(val), carry[2] + fold(r.cx[i].astype(F32)))

        qsum, vsum, csum = lax.fori_loop(0, 4, proj_sums, (zero8, zero8, zero8))
        r.sums[pl.ds(3 + 7, 1), :] = jnp.sum(qsum, axis=0, keepdims=True)
        r.sums[pl.ds(3 + 8, 1), :] = jnp.sum(vsum, axis=0, keepdims=True)
        r.sums[pl.ds(3 + 9, 1), :] = jnp.sum(csum, axis=0, keepdims=True)
        r.sums[pl.ds(13, 3), :] = jnp.zeros((3, HALF), F32)

        def n3_own(i, carry):
            both = dot_nt(proj_rows(i), wproj(half_of(c))) + n3.get(i)
            for j in range(2):
                vals = both[j * CHUNK : j * CHUNK + CHUNK]
                r.gtmp[rows(2 * i + j), :] = vals
                carry = carry[0] + fold(vals), carry[1] + fold(vals * hat3(2 * i + j))
            return carry

        sums3 = n3_own(1, n3_own(0, (zero8, zero8)))
        plain3, cross3, back3 = norm_back(sums3, lambda i: r.gtmp[rows(i), :], hat3, gain3, inv3)
        r.sums[pl.ds(2, 1), :] = cross3
        r.sums[pl.ds(3 + 2, 1), :] = plain3

        def shifted(buf, i, vals):
            buf[0, rows(i, CHUNK, ROW), :] = from_right(vals).astype(BF16)
            buf[1, rows(i, CHUNK, ROW), :] = vals.astype(BF16)
            buf[2, rows(i, CHUNK, ROW), :] = from_left(vals).astype(BF16)

        def residual_back(i, carry):
            vals = r.cx[i].astype(F32) + back3(i)
            r.gres[rows(i), :] = vals
            shifted(r.gr2, i, vals)
            return carry + fold(vals.astype(BF16).astype(F32))

        bias_two = lax.fori_loop(0, 4, residual_back, jnp.zeros((8, HALF), F32))
        r.sums[pl.ds(3 + 4, 1), :] = jnp.sum(bias_two, axis=0, keepdims=True)

        def act_back(buf, g, core, i, size):
            left = jnp.concatenate(
                [buf[b, rows(i, size, 2 * ROW - ROW * a), :] for a in range(3) for b in range(3)], axis=1
            )
            right = jnp.concatenate(
                [wtap(g, 3 * a + b, half_of(core)) for a in range(3) for b in range(3)], axis=1
            )
            return dot_nt(left, right)

        def conv_back(parts, buf, g):
            parts.fill(lambda i: act_back(buf, g, 1 - c, i, 2 * CHUNK))

        def conv_back_own(parts, buf, g, outer, hat):
            def own(i, carry):
                vals = act_back(buf, g, c, i, 2 * CHUNK) + parts.get(i)
                for j in range(2):
                    at = 2 * i + j
                    grad = vals[j * CHUNK : j * CHUNK + CHUNK] * outer(at)
                    r.gtmp[rows(at), :] = grad
                    carry = carry[0] + fold(grad), carry[1] + fold(grad * hat(at))
                return carry

            return own(1, own(0, (zero8, zero8)))

        def kernel_grad(act_t, buf, acc, after):
            def step(a):
                right = jnp.concatenate([buf[b, pl.ds(2 * ROW - ROW * a, PX), :] for b in range(3)], axis=1)
                out = dot(jnp.concatenate([act_t[0], act_t[1]], axis=0), right)
                for p, zc in enumerate(ALL):
                    for yy in range(2):
                        for xx in range(2):
                            row = p * 128 + yy * 48
                            tiles = [
                                out[row : row + 48, b * HALF + xx * 128 : b * HALF + xx * 128 + 128] for b in range(3)
                            ]
                            acc[a, slot(xx, yy), zc] = pack_taps(*tiles)
                after(a)

            each(3, step)

        d2 = Parts("d2")
        conv_back(d2, r.gr2, k2)
        kernel_grad(r.act2_t, r.gr2, acc2, red2.start if inside else lambda a: None)

        sums2 = conv_back_own(d2, r.gr2, k2, lambda i: silu_slope(pre2(i)), hat2)
        if inside:
            red3.second(0, 1)

        plain2, cross2, back2 = norm_back(sums2, lambda i: r.gtmp[rows(i), :], hat2, gain2 * scale, inv2)
        r.sums[pl.ds(1, 1), :] = scale * cross2
        r.sums[pl.ds(3 + 1, 1), :] = scale * plain2
        film_scale_term = gain2 * cross2 + shift2 * plain2
        r.sums[pl.ds(3 + 5, 1), :] = film_scale_term
        r.sums[pl.ds(3 + 6, 1), :] = plain2
        for j in range(2):
            r.ft[j] = film_scale_term[:, j * 128 : j * 128 + 128]
            r.ft[2 + j] = plain2[:, j * 128 : j * 128 + 128]
        head_start(lambda p: r.ft.at[p], r.th, r.th_s, r.th_r)
        r.th[h] = r.ft[h]

        def first_back(i, carry):
            vals = back2(i)
            shifted(r.gr1, i, vals)
            return carry + fold(vals.astype(BF16).astype(F32))

        bias_one = lax.fori_loop(0, 4, first_back, jnp.zeros((8, HALF), F32))
        r.sums[pl.ds(3 + 3, 1), :] = jnp.sum(bias_one, axis=0, keepdims=True)

        d1 = Parts("d1")
        kernel_grad(r.act1_t, r.gr1, acc1, red1.start if inside else lambda a: None)
        if inside:
            red2.second(0, 3)
            red3.third(0, 1)
        conv_back(d1, r.gr1, k1)

        head_wait(lambda p: r.ft.at[p], r.th, r.th_s, r.th_r)
        for m in range(2):
            r.fa[d, pl.ds(m, 1), :] = jnp.concatenate([r.th[2 * m], r.th[2 * m + 1]], axis=1)
        dp_start(lambda p: r.fa.at[d], r.fa, r.fa_s, r.fa_r)

        def hat1(i):
            return (mixed(i) - mean1) * inv1

        if inside:
            red1.second(0, 2)
            red2.third(0, 3)
        sums1 = conv_back_own(d1, r.gr1, k1, lambda i: silu_slope(pre1(i)), hat1)
        if inside:
            red1.second(2, 1)
            red1.third(0, 2)

        plain1, cross1, back1 = norm_back(sums1, lambda i: r.gtmp[rows(i), :], hat1, gain1, inv1)
        r.sums[pl.ds(0, 1), :] = cross1
        r.sums[pl.ds(3, 1), :] = plain1
        r.ad[d] = r.sums[...]
        dp_start(lambda p: r.ad.at[d], r.ad, r.ad_s, r.ad_r)

        keep = r.coef[0, x]

        def image_back(i):
            r.io_src[i] = pack_pixels(keep * (r.gres[rows(i), :] + back1(i))).astype(BF16)

        loop(4, image_back)
        head_start(lambda p: r.io_src.at[p], r.io_dst, r.io_s, r.io_r)
        r.io_dst[h] = r.io_src[h]
        if inside:
            red1.third(2, 1)

        dp_wait(lambda p: r.fa.at[d], r.fa, r.fa_s, r.fa_r)
        for j in range(n):
            r.fta[pl.ds(2 * j, 2), :] = r.fa[j]
        film_block = dot_tn_high(r.esel[...], r.fta[...])
        r.film[...] = jnp.concatenate([film_block[:film_rows, :BLK], film_block[:film_rows, 128 : 128 + BLK]], axis=1)
        embed_part = dot_nt_high(r.fta[...], r.wfp[...].astype(F32))
        for j in range(n):
            r.ep[j] = embed_part[2 * j : 2 * j + 2]
        dp_start(lambda p: r.ep.at[p], r.er, r.er_s, r.er_r)
        r.er[d] = r.ep[d]

        dp_wait(lambda p: r.ad.at[d], r.ad, r.ad_s, r.ad_r)
        total = r.ad[0]
        for j in range(1, n):
            total = total + r.ad[j]
        r.hb[h] = total
        head_start(lambda p: r.hb.at[h], r.hb, r.hb_s, r.hb_r)
        head_wait(lambda p: r.ro_src.at[p], r.ro_dst, r.ro_s, r.ro_r)

        dp_wait(lambda p: r.ep.at[p], r.er, r.er_s, r.er_r)
        r.eh[h] = r.er[...]
        head_start(lambda p: r.eh.at[h], r.eh, r.eh_s, r.eh_r)

        if inside:
            red2.finish(((0, 3),))
            for a in range(3):
                r.second[a] = red2.last(a)

        head_wait(lambda p: r.hb.at[h], r.hb, r.hb_s, r.hb_r)
        even = r.hb[0] + r.hb[2]
        odd = r.hb[1] + r.hb[3]
        wide = jnp.concatenate(
            [even[:, :BLK], odd[:, :BLK], even[:, 128 : 128 + BLK], odd[:, 128 : 128 + BLK]], axis=1
        )
        r.gains_out[...] = wide[0:3]
        r.biases_out[...] = wide[3:13]

        head_wait(lambda p: r.eh.at[h], r.eh, r.eh_s, r.eh_r)
        pieces = []
        for j in range(n):
            piece = (r.eh[0, j] + r.eh[1, j]) + (r.eh[2, j] + r.eh[3, j])
            pieces.append(piece[:, :film_rows])
        r.embed_grad[...] = jnp.concatenate(pieces, axis=1) * silu_slope(r.emb[...].astype(F32))

        head_wait(lambda p: r.io_src.at[p], r.io_dst, r.io_s, r.io_r)

        if inside:
            red3.finish(((0, 1),))
            tiles = unpack_four(red3.last(0))
            r.sb_src[...] = jnp.where(c == 0, tiles[2], tiles[0])
            back = rc(r.sb_src, r.sb_dst, r.sb_s.at[0], r.sb_r.at[0], sib)
            back.start()
            r.output[...] = tiles[3]
            red1.finish(((0, 2), (2, 1)))
            for a in range(3):
                r.first[a] = red1.last(a)
            back.wait()
            r.attend[:, 0:128] = jnp.where(c == 0, tiles[0], tiles[1])
            r.attend[:, 128:256] = r.sb_dst[...]
            r.attend[:, 256:384] = jnp.where(c == 0, tiles[1], tiles[2])

    return kernel


def make_writer(names_in, names_out):
    def kernel(*refs):
        count = len(names_in)
        src, dst = Names(names_in, refs[:count]), Names(names_out, refs[count:])
        for name, packed in (("result", src.ro_dst), ("image_grad", src.io_dst)):
            for m in range(2):
                getattr(dst, name)[m] = dot_nt(unpack_pixels(packed[2 * m]), src.sel[0]) + dot_nt(
                    unpack_pixels(packed[2 * m + 1]), src.sel[1]
                )
        for name in ("first", "second"):
            if name in names_out:
                for a in range(3):
                    block = getattr(src, name)[a]
                    getattr(dst, name)[3 * a] = block[:48, :BLK]
                    getattr(dst, name)[3 * a + 1] = block[48:96, :BLK]
                    getattr(dst, name)[3 * a + 2] = last_tap(block)[:, :BLK]
        if "attend" in names_out:
            dst.attend[...] = jnp.concatenate([src.attend[:, j * 128 : j * 128 + BLK] for j in range(3)], axis=1)
            dst.output[...] = src.output[:, :BLK]
        for name in ("embed_grad", "film", "gains_out", "biases_out"):
            getattr(dst, name)[...] = getattr(src, name)[...]

    return kernel


def per_device(n, *args):
    (
        images,
        noise_field,
        time_steps,
        embedding,
        first_kernel,
        second_kernel,
        film_weight,
        attend_weight,
        output_weight,
        norm_gains,
        biases,
        cotangent,
    ) = args
    inside = n == 8
    keep, noise = plan(time_steps)
    coef = jnp.stack([keep, noise])
    maps, height, width, channels = images.shape
    flat_shape = (maps, height * width, channels)
    film_rows = film_weight.shape[0]
    inputs = dict(
        coef=coef,
        images=images.reshape(flat_shape),
        noise=noise_field.reshape(flat_shape),
        cot=cotangent.reshape(flat_shape),
        emb=embedding,
        k1=first_kernel.reshape((9,) + first_kernel.shape[2:]),
        k2=second_kernel.reshape((9,) + second_kernel.shape[2:]),
        wf=film_weight,
        wa=attend_weight,
        wo=output_weight,
        gains=norm_gains,
        biases=biases,
        sel=jnp.asarray(channel_lanes(), BF16),
        gmask=jnp.asarray(group_mask(), BF16),
        selp=jnp.asarray(block_lanes(3), BF16),
    )
    shapes = dict(
        ro_dst=(4, 384, 128),
        io_dst=(4, 384, 128),
        embed_grad=embedding.shape,
        first=(3, 112, 128),
        second=(3, 112, 128),
        film=film_weight.shape,
        attend=(48, 384),
        output=(48, 128),
        gains_out=norm_gains.shape,
        biases_out=biases.shape,
    )
    names_in, names_out = list(INPUTS), list(OUTPUTS)
    core = lax.axis_index("head") % 2
    if not inside:
        def whole(array, row_axis):
            array = lax.all_gather(array, "dp", axis=row_axis, tiled=True)
            return lax.all_gather(array, "head", axis=array.ndim - 1, tiled=True)

        def spread(array, count):
            taps = array.shape[0]
            array = array.reshape(taps, 4, 2, 48, 2, 2, BLK)
            array = lax.dynamic_index_in_dim(array, core, 5, keepdims=False)
            array = jnp.transpose(array, (2, 4, 1, 0, 3, 5))
            array = jnp.pad(array, ((0, 0),) * 5 + ((0, 32),))
            return array.reshape(4, 4, taps * 48, 128)

        full_a = whole(attend_weight, 0).reshape(384, 2, 3, 2, BLK)
        full_a = jnp.transpose(full_a, (2, 0, 1, 3, 4)).reshape(3, 384, 384)
        full_o = whole(output_weight, 0)[None]
        for name, last, array in (("g1", "t1", first_kernel), ("g2", "t2", second_kernel)):
            blocks = spread(whole(array, 2).reshape(9, 384, 384), 9).reshape(4, 4, 3, 3, 48, 128)
            two = blocks[:, :, :, :2].reshape(4, 4, 3, 96, 128)
            inputs[name] = jnp.pad(two, ((0, 0),) * 3 + ((0, 16), (0, 0))).reshape(4, 4, 336, 128)
            inputs[last] = blocks[:, :, :, 2].reshape(4, 4, 144, 128)
        inputs["g3"] = spread(jnp.concatenate([full_a, full_o], axis=0), 4)
        names_in += ["g1", "g2", "t1", "t2", "g3"]
        shapes["first"] = shapes["second"] = (3, 4, 4, 112, 128)
        shapes["attend"] = (1, 4, 4, 144, 128)
        del shapes["output"]
        names_out.remove("output")
    items = scratch_list(n, inside)
    smem = pl.BlockSpec(memory_space=pltpu.SMEM)
    vmem = pl.BlockSpec(memory_space=pltpu.VMEM)
    outs = pl.pallas_call(
        make_kernel(n, inside, names_in + names_out + [name for name, _ in items]),
        out_shape=[
            jax.ShapeDtypeStruct(shapes[name], BF16 if name in ("ro_dst", "io_dst") else F32) for name in names_out
        ],
        in_specs=[smem if name == "coef" else vmem for name in names_in],
        out_specs=[vmem] * len(names_out),
        scratch_shapes=[item for _, item in items],
        compiler_params=pltpu.CompilerParams(
            collective_id=0, has_side_effects=True, vmem_limit_bytes=63 * 1024 * 1024
        ),
        name="blocks",
    )(*[inputs[name] for name in names_in])
    raw = dict(zip(names_out, outs))
    final = dict(
        result=flat_shape,
        image_grad=flat_shape,
        embed_grad=embedding.shape,
        film=film_weight.shape,
        gains_out=norm_gains.shape,
        biases_out=biases.shape,
    )
    if inside:
        final.update(first=(9, 48, BLK), second=(9, 48, BLK), attend=attend_weight.shape, output=output_weight.shape)
    names_last = [name for name in names_out if inside or name not in ("first", "second", "attend")] + ["sel"]
    names_final = list(final)
    outs = pl.pallas_call(
        make_writer(names_last, names_final),
        out_shape=[jax.ShapeDtypeStruct(final[name], F32) for name in names_final],
        in_specs=[vmem] * len(names_last),
        out_specs=[vmem] * len(names_final),
        compiler_params=pltpu.CompilerParams(vmem_limit_bytes=63 * 1024 * 1024),
        name="outputs",
    )(*[inputs["sel"] if name == "sel" else raw[name] for name in names_last])
    out = dict(zip(names_final, outs))
    if not inside:

        def blocks_of(array, size):
            parts = [array[..., k * 48 : k * 48 + 48, :BLK] for k in range(size)]
            if size == 2:
                lanes = [array[..., k * 32 : k * 32 + 32, BLK:] for k in range(3)]
                lanes = jnp.concatenate(lanes, axis=-1)
                parts.append(jnp.concatenate([lanes, array[..., 96:112, :BLK]], axis=-2))
            else:
                lanes = [array[..., k * 48 : k * 48 + 48, BLK:] for k in range(3)]
                parts.append(jnp.concatenate(lanes, axis=-1))
            array = jnp.stack(parts, axis=1)
            array = array.reshape(array.shape[:2] + (2, 2, 4, 48, BLK))
            taps = array.shape[0] * array.shape[1]
            array = jnp.transpose(array, (0, 1, 4, 2, 5, 3, 6)).reshape(taps, 384, 2, 1, BLK)
            both = jnp.concatenate([array, jnp.zeros_like(array)], axis=3)
            return jnp.where(core == 0, both, both[:, :, :, ::-1]).reshape(taps, 384, 384)

        def shared(array, axis):
            array = lax.psum_scatter(array, "head", scatter_dimension=array.ndim - 1, tiled=True)
            return lax.psum_scatter(array, "dp", scatter_dimension=axis, tiled=True)

        out["first"] = shared(blocks_of(raw["first"], 2), 1)
        out["second"] = shared(blocks_of(raw["second"], 2), 1)
        both = blocks_of(raw["attend"], 3)
        joined = both[:3].reshape(3, 384, 2, 2, BLK)
        joined = jnp.transpose(joined, (1, 2, 0, 3, 4)).reshape(384, 1152)
        out["attend"] = shared(joined, 0)
        out["output"] = shared(both[3], 0)
    return (
        out["result"].reshape(images.shape),
        out["image_grad"].reshape(images.shape),
        out["embed_grad"],
        out["first"].reshape(first_kernel.shape),
        out["second"].reshape(second_kernel.shape),
        out["film"],
        out["attend"],
        out["output"],
        out["gains_out"],
        out["biases_out"],
    )


def solution(mesh):
    n = mesh.shape["dp"]
    field = P("dp", "head", None, None)
    taps = P(None, None, "dp", "head")
    both = P("dp", "head")
    return jax.shard_map(
        lambda *args: per_device(n, *args),
        mesh=mesh,
        in_specs=(field, field, P("dp"), P("dp", None), taps, taps, both, both, both, P(), P(), field),
        out_specs=(field, field, P("dp", None), taps, taps, both, both, both, P(), P()),
        check_vma=False,
    )
```

```python
import math

import jax
import jax.numpy as jnp
import numpy as np
from jax import lax
from jax.experimental import pallas as pl
from jax.experimental.pallas import tpu as pltpu
from jax.sharding import PartitionSpec as P

HEAD_DIM = 96
GROUPS = 32
STEPS = 4000
EPS = 1e-05
OFFSET = 0.008
MESH = pl.DeviceIdType.MESH
F32 = jnp.float32
BF16 = jnp.bfloat16

PX = 1024
ROW = 32
CHUNK = 256
BLK = 96
HALF = 256
NHEAD = 4


def plan(time_steps):
    fraction = (time_steps.astype(F32) + 1.0) / STEPS
    start = jnp.square(jnp.cos(jnp.float32(OFFSET / (1.0 + OFFSET) * (math.pi / 2))))
    curve = jnp.square(jnp.cos((fraction + OFFSET) / (1.0 + OFFSET) * (math.pi / 2))) / start
    return (jnp.sqrt(curve), jnp.sqrt(1.0 - curve))


def channel_lanes():
    sel = np.zeros((2, 384, HALF), np.float32)
    for block in range(4):
        for j in range(BLK):
            sel[block % 2, block * BLK + j, (block // 2) * 128 + j] = 1.0
    return sel


def block_lanes(count):
    sel = np.zeros((count * BLK, count * 128), np.float32)
    for block in range(count):
        for j in range(BLK):
            sel[block * BLK + j, block * 128 + j] = 1.0
    return sel


def group_mask():
    lane = np.arange(HALF)
    ok = lane % 128 < BLK
    group = (lane // 128) * 100 + (lane % 128) // 12
    return ((group[:, None] == group[None, :]) & ok[:, None] & ok[None, :]).astype(np.float32)


def dot(a, b):
    return lax.dot_general(a, b, (((1,), (0,)), ((), ())), preferred_element_type=F32)


def dot_nt(a, b):
    return lax.dot_general(a, b, (((1,), (1,)), ((), ())), preferred_element_type=F32)


def dot_nt_high(a, b):
    return lax.dot_general(
        a, b, (((1,), (1,)), ((), ())), preferred_element_type=F32, precision=lax.Precision.HIGHEST
    )


def dot_tn_high(a, b):
    return lax.dot_general(
        a, b, (((0,), (0,)), ((), ())), preferred_element_type=F32, precision=lax.Precision.HIGHEST
    )


def exact_dot(values, ones):
    high = values.astype(BF16).astype(F32)
    rest = values - high
    middle = rest.astype(BF16).astype(F32)
    low = rest - middle
    rows = values.shape[0]
    out = dot(jnp.concatenate([high, middle, low], axis=0).astype(BF16), ones)
    return out[:rows] + out[rows : 2 * rows] + out[2 * rows :]


def sigmoid(v):
    return 0.5 + 0.5 * jnp.tanh(0.5 * v)


def silu(v):
    return v * sigmoid(v)


def silu_slope(v):
    s = sigmoid(v)
    return s * (1.0 + v * (1.0 - s))


def pack_taps(t0, t1, t2):
    t0, t1, t2 = t0[:, :BLK], t1[:, :BLK], t2[:, :BLK]
    join = lambda a, b: jnp.concatenate([a, b], axis=1)
    return jnp.concatenate(
        [
            join(t0[:32], t2[:32, :32]),
            join(t0[32:], t2[:16, 32:64]),
            join(t1[:16], t2[16:32, 32:64]),
            join(t1[16:], t2[:32, 64:]),
            join(t2[32:], jnp.zeros((16, 32), t2.dtype)),
        ],
        axis=0,
    )


def last_tap(packed):
    lanes = [packed[:32, BLK:], packed[32:64, BLK:], packed[64:96, BLK:], jnp.zeros((32, 32), packed.dtype)]
    return jnp.concatenate([jnp.concatenate(lanes, axis=1), packed[96:112]], axis=0)


def pack_four(b0, b1, b2, b3):
    return jnp.concatenate(
        [jnp.concatenate([b[:, :BLK], b3[:, 32 * k : 32 * k + 32]], axis=1) for k, b in enumerate((b0, b1, b2))],
        axis=0,
    )


def unpack_four(packed):
    size = packed.shape[0] // 3
    parts = [packed[k * size : k * size + size] for k in range(3)]
    zero = jnp.zeros((size, 32), packed.dtype)
    fourth = jnp.concatenate([p[:, BLK:] for p in parts] + [zero], axis=1)
    return [jnp.concatenate([p[:, :BLK], zero], axis=1) for p in parts] + [fourth]


def pack_pixels(full):
    half = CHUNK // 2
    return pack_four(full[:half, :128], full[half:, :128], full[:half, 128:], full[half:, 128:])


def unpack_pixels(packed):
    b0, b1, b2, b3 = unpack_four(packed)
    return jnp.concatenate([jnp.concatenate([b0, b2], axis=1), jnp.concatenate([b1, b3], axis=1)], axis=0)


INPUTS = (
    "coef",
    "images",
    "noise",
    "cot",
    "emb",
    "k1",
    "k2",
    "wf",
    "wa",
    "wo",
    "gains",
    "biases",
    "sel",
    "gmask",
    "selp",
)
OUTPUTS = (
    "ro_dst",
    "io_dst",
    "embed_grad",
    "first",
    "second",
    "film",
    "attend",
    "output",
    "gains_out",
    "biases_out",
)


class Names:
    def __init__(self, names, refs):
        for name, ref in zip(names, refs):
            setattr(self, name, ref)


def scratch_list(n, inside):
    dma = pltpu.SemaphoreType.DMA
    items = []

    def vm(name, shape, dtype):
        items.append((name, pltpu.VMEM(shape, dtype)))

    def sem(name, count):
        items.append((name + "_s", dma((count,))))
        items.append((name + "_r", dma((count,))))

    for name in ("mx", "cx", "ro", "io"):
        vm(name + "_src", (4, 384, 128), BF16)
        if name in ("mx", "cx"):
            vm(name + "_dst", (4, 384, 128), BF16)
            vm(name, (4, CHUNK, HALF), BF16)
        sem(name, 4)
    for name in ("act1", "act2"):
        vm(name, (2, PX + 2 * ROW, HALF), BF16)
        vm(name + "_t", (2, HALF, PX), BF16)
        sem(name, 4)
    vm("ai", (2, PX, HALF), BF16)
    vm("ai_t", (2, HALF, PX), BF16)
    sem("ai", 4)
    vm("att", (4, PX, 128), BF16)
    vm("att_t", (2, HALF, PX), BF16)
    sem("att", 4)
    for name in ("do", "n3", "d2", "d1"):
        vm(name + "_src", (PX, HALF), BF16)
        vm(name + "_dst", (PX, HALF), BF16)
        sem(name, 2)
    vm("v2", (PX, HALF), F32)
    vm("v3", (PX, HALF), F32)
    vm("gres", (PX, HALF), F32)
    vm("gtmp", (PX, HALF), F32)
    vm("qkv", (6, PX, 128), BF16)
    vm("kvt", (4, 128, PX), BF16)
    vm("dout", (2, PX, 128), BF16)
    vm("dproj", (6, PX, 128), BF16)
    vm("gr2", (3, PX + 2 * ROW, HALF), BF16)
    vm("gr1", (3, PX + 2 * ROW, HALF), BF16)
    vm("par", (16, 384), F32)
    vm("parown", (16, HALF), F32)
    vm("stat", (16, HALF), F32)
    vm("sums", (16, HALF), F32)
    if inside:
        vm("g1", (4, 4, 336, 128), BF16)
        vm("g2", (4, 4, 336, 128), BF16)
        vm("t1", (4, 4, 144, 128), BF16)
        vm("t2", (4, 4, 144, 128), BF16)
        vm("p3", (4, 4, 144, 128), BF16)
        vm("g3", (4, 4, 192, 128), BF16)
        for name in ("g1", "g2", "p3"):
            sem(name + "z", 4)
            sem(name + "v", 4)
            sem(name + "w", 8)
        vm("sw_src", (48, 128), BF16)
        vm("sw_dst", (48, 128), BF16)
        sem("sw", 1)
        vm("sb_src", (48, 128), F32)
        vm("sb_dst", (48, 128), F32)
        sem("sb", 1)
        for name, nc, rows in (("r1", 3, 112), ("r2", 3, 112), ("r3", 1, 144)):
            vm(name + "_acc", (nc, 4, 4, rows, 128), F32)
            vm(name + "w_src", (nc, 2, 4, rows, 128), BF16)
            vm(name + "w_dst", (nc, 2, 4, rows, 128), BF16)
            vm(name + "v_src", (nc, 4, rows, 128), BF16)
            vm(name + "v_dst", (nc, 4, rows, 128), BF16)
            vm(name + "z_src", (4, nc, rows, 128), BF16)
            vm(name + "z_dst", (4, nc, rows, 128), BF16)
            sem(name + "w", nc)
            sem(name + "v", nc)
            sem(name + "z", nc * 4)
    vm("el", (n, 2, 768), F32)
    sem("el", n)
    vm("em", (2 * n, 768), F32)
    vm("wfp", (128, HALF), BF16)
    vm("esel", (2 * n, 128), F32)
    vm("fp", (n, 2, HALF), F32)
    vm("fr", (n, 2, HALF), F32)
    sem("fr", n)
    vm("fx", (4, 1, 128), F32)
    vm("fh", (4, 1, 128), F32)
    sem("fh", 4)
    vm("ft", (4, 1, 128), F32)
    vm("th", (4, 1, 128), F32)
    sem("th", 4)
    vm("fa", (n, 2, HALF), F32)
    sem("fa", n)
    vm("fta", (2 * n, HALF), F32)
    vm("ep", (n, 2, 128), F32)
    vm("er", (n, 2, 128), F32)
    sem("er", n)
    vm("eh", (4, n, 2, 128), F32)
    sem("eh", 4)
    vm("ad", (n, 16, HALF), F32)
    sem("ad", n)
    vm("hb", (4, 16, HALF), F32)
    sem("hb", 4)
    return items


def make_kernel(n, inside, names):
    film_rows = 768 // n

    def kernel(*refs):
        r = Names(names, refs)
        d = lax.axis_index("dp")
        h = lax.axis_index("head")
        x = h // 2
        c = h - 2 * x
        z = d // 2
        y = d - 2 * z
        sib = (d, h + 1 - 2 * c)
        xdev = (d, h + 2 - 4 * x)
        v = x + c * (y - x)
        w = y + c * (x - y)
        vdev = (d + c * (1 - 2 * y), h + (1 - c) * (2 - 4 * x))
        wdev = (d + (1 - c) * (1 - 2 * y), h + c * (2 - 4 * x))

        def slot(xx, yy):
            if inside:
                return (yy + c * (xx - yy)) * 2 + xx + c * (yy - xx)
            return yy * 2 + xx

        def rc(src, dst, send, recv, dev):
            return pltpu.make_async_remote_copy(
                src_ref=src, dst_ref=dst, send_sem=send, recv_sem=recv, device_id=dev, device_id_type=MESH
            )

        def loop(count, body):
            def step(i, carry):
                body(i)
                return carry

            lax.fori_loop(0, count, step, 0)

        def each(count, body):
            for i in range(count):
                body(i)

        def rows(i, size=CHUNK, base=0):
            return pl.ds(pl.multiple_of(base + i * size, 32), size)

        def dp_start(src_of, dst, send, recv):
            def step(k, carry):
                peer = lax.rem(d + k, n)
                rc(src_of(peer), dst.at[d], send.at[k], recv.at[d], (peer, h)).start()
                return carry

            lax.fori_loop(1, n, step, 0)

        def dp_wait(src_of, dst, send, recv):
            def step(k, carry):
                peer = lax.rem(d + k, n)
                copy = rc(src_of(peer), dst.at[peer], send.at[k], recv.at[peer], (peer, h))
                copy.wait_recv()
                copy.wait_send()
                return carry

            lax.fori_loop(1, n, step, 0)

        def head_start(src_of, dst, send, recv):
            for k in range(1, 4):
                peer = lax.rem(h + k, 4)
                rc(src_of(peer), dst.at[h], send.at[k], recv.at[h], (d, peer)).start()

        def head_wait(src_of, dst, send, recv):
            for k in range(1, 4):
                peer = lax.rem(h + k, 4)
                copy = rc(src_of(peer), dst.at[peer], send.at[k], recv.at[peer], (d, peer))
                copy.wait_recv()
                copy.wait_send()

        class Halves:
            def __init__(self, name, base):
                self.buf, self.base = getattr(r, name), base
                self.send, self.recv = getattr(r, name + "_s"), getattr(r, name + "_r")

            def at(self, core, i):
                return self.buf.at[core, rows(i, CHUNK, self.base)]

            def fill(self, make):
                def body(i):
                    self.buf[c, rows(i, CHUNK, self.base), :] = make(i)
                    ref = self.at(c, i)
                    rc(ref, ref, self.send.at[i], self.recv.at[i], sib).start()

                loop(4, body)

            def wait(self):
                for i in range(4):
                    ref = self.at(1 - c, i)
                    copy = rc(ref, ref, self.send.at[i], self.recv.at[i], sib)
                    copy.wait_recv()
                    copy.wait_send()

        class Parts:
            def __init__(self, name):
                self.src, self.dst = getattr(r, name + "_src"), getattr(r, name + "_dst")
                self.send, self.recv = getattr(r, name + "_s"), getattr(r, name + "_r")

            def copy(self, i):
                at = rows(i, 2 * CHUNK)
                return rc(self.src.at[at], self.dst.at[at], self.send.at[i], self.recv.at[i], sib)

            def fill(self, make):
                def body(i):
                    self.src[rows(i, 2 * CHUNK), :] = make(i).astype(BF16)
                    self.copy(i).start()

                each(2, body)

            def get(self, i):
                copy = self.copy(i)
                copy.wait_recv()
                copy.wait_send()
                return self.dst[rows(i, 2 * CHUNK), :].astype(F32)

        class Gather:
            def __init__(self, name):
                self.g = getattr(r, name)
                self.zs, self.zr = getattr(r, name + "z_s"), getattr(r, name + "z_r")
                self.vs, self.vr = getattr(r, name + "v_s"), getattr(r, name + "v_r")
                self.ws, self.wr = getattr(r, name + "w_s"), getattr(r, name + "w_r")

            def zcopy(self, k):
                peer = (lax.rem(z + k, 4) * 2 + y, h)
                return rc(
                    self.g.at[w * 2 + v, 0], self.g.at[w * 2 + v, 4 - k], self.zs.at[k], self.zr.at[4 - k], peer
                )

            def vcopy(self, vv, i):
                ref = self.g.at[w * 2 + vv, i]
                return rc(ref, ref, self.vs.at[i], self.vr.at[i], vdev)

            def wcopy(self, ww, other, i):
                ref = self.g.at[ww * 2 + v + other * (1 - 2 * v), i]
                return rc(ref, ref, self.ws.at[2 * i + other], self.wr.at[2 * i + other], wdev)

            def own(self):
                for k in range(1, 4):
                    self.zcopy(k).start()
                self.vcopy(v, 0).start()
                self.wcopy(w, 0, 0).start()

            def pass_z(self):
                self.vcopy(1 - v, 0).wait_recv()
                self.wcopy(w, 1, 0).start()
                for k in range(1, 4):
                    self.zcopy(k).wait_recv()
                    self.vcopy(v, 4 - k).start()
                    self.wcopy(w, 0, 4 - k).start()

            def pass_v(self):
                for k in range(1, 4):
                    self.vcopy(1 - v, 4 - k).wait_recv()
                    self.wcopy(w, 1, 4 - k).start()

            def done(self):
                for k in range(1, 4):
                    self.zcopy(k).wait_send()
                for i in range(4):
                    self.vcopy(v, i).wait_send()
                    for other in range(2):
                        self.wcopy(1 - w, other, i).wait_recv()
                        self.wcopy(w, other, i).wait_send()

        class Reduce:
            def __init__(self, name, count):
                get = lambda tail: getattr(r, name + tail)
                self.acc, self.count = get("_acc"), count
                self.wsrc, self.wdst, self.ws, self.wr = get("w_src"), get("w_dst"), get("w_s"), get("w_r")
                self.vsrc, self.vdst, self.vs, self.vr = get("v_src"), get("v_dst"), get("v_s"), get("v_r")
                self.zsrc, self.zdst, self.zs, self.zr = get("z_src"), get("z_dst"), get("z_s"), get("z_r")

            def wcopy(self, a):
                return rc(self.wsrc.at[a], self.wdst.at[a], self.ws.at[a], self.wr.at[a], wdev)

            def vcopy(self, a, size):
                at = pl.ds(a, size)
                return rc(self.vsrc.at[at], self.vdst.at[at], self.vs.at[a], self.vr.at[a], vdev)

            def zcopy(self, a, size, k):
                at = pl.ds(a, size)
                return rc(
                    self.zsrc.at[k, at],
                    self.zdst.at[4 - k, at],
                    self.zs.at[a * 4 + k],
                    self.zr.at[a * 4 + 4 - k],
                    (lax.rem(z + k, 4) * 2 + y, h),
                )

            def start(self, a):
                def step(i, carry):
                    vv, zz = i // 4, lax.rem(i, 4)
                    self.wsrc[a, vv, zz] = self.acc[a, (1 - w) * 2 + vv, zz].astype(BF16)
                    return carry

                lax.fori_loop(0, 8, step, 0)
                self.wcopy(a).start()

            def second(self, first, size):
                for a in range(first, first + size):
                    self.wcopy(a).wait_recv()

                    def step(zz, carry):
                        self.vsrc[a, zz] = (
                            self.acc[a, w * 2 + 1 - v, zz] + self.wdst[a, 1 - v, zz].astype(F32)
                        ).astype(BF16)
                        return carry

                    lax.fori_loop(0, 4, step, 0)
                self.vcopy(first, size).start()

            def third(self, first, size):
                self.vcopy(first, size).wait_recv()
                for a in range(first, first + size):

                    def step(k, carry):
                        zz = lax.rem(z + k, 4)
                        total = (
                            self.acc[a, w * 2 + v, zz]
                            + self.wdst[a, v, zz].astype(F32)
                            + self.vdst[a, zz].astype(F32)
                        )
                        self.acc[a, w * 2 + v, zz] = total
                        self.zsrc[k, a] = total.astype(BF16)
                        return carry

                    lax.fori_loop(0, 4, step, 0)
                for k in range(1, 4):
                    self.zcopy(first, size, k).start()

            def finish(self, groups):
                for first, size in groups:
                    self.vcopy(first, size).wait_send()
                    for k in range(1, 4):
                        copy = self.zcopy(first, size, k)
                        copy.wait_recv()
                        copy.wait_send()
                for a in range(self.count):
                    self.wcopy(a).wait_send()

            def last(self, a):
                total = self.acc[a, w * 2 + v, z]
                for k in range(1, 4):
                    total = total + self.zdst[k, a].astype(F32)
                return total

        def rel(zc):
            return lax.rem(zc - z + 4, 4) if inside else zc

        class Taps:
            def __init__(self, packed, last):
                self.packed, self.last = packed, last

            def block(self, tap, zc, xx, yy):
                a, b = tap // 3, tap % 3
                if b < 2:
                    return self.packed[slot(xx, yy), rel(zc), pl.ds(a * 112 + b * 48, 48), :]
                return self.last[slot(xx, yy), rel(zc), pl.ds(a * 48, 48), :]

            def unpack(self):
                def step(i, carry):
                    q, zz = i // 4, lax.rem(i, 4)
                    for a in range(3):
                        self.last[q, zz, pl.ds(a * 48, 48), :] = last_tap(
                            self.packed[q, zz, pl.ds(a * 112, 112), :]
                        )
                    return carry

                lax.fori_loop(0, 16, step, 0)

        class Plain:
            def __init__(self, blocks):
                self.blocks = blocks

            def block(self, tap, zc, xx, yy):
                return self.blocks[slot(xx, yy), rel(zc), pl.ds(tap * 48, 48), :]

            def unpack(self):
                def step(i, carry):
                    q, zz = i // 4, lax.rem(i, 4)
                    self.blocks[q, zz] = jnp.concatenate(unpack_four(r.p3[q, zz]), axis=0)
                    return carry

                lax.fori_loop(0, 16, step, 0)

        k1, k2, k3 = Taps(r.g1, r.t1), Taps(r.g2, r.t2), Plain(r.g3)

        def wtile(g, tap, zc, xx):
            return jnp.concatenate(
                [g.block(tap, zc, xx, 0), g.block(tap, zc, xx, 1), jnp.zeros((32, 128), BF16)], axis=0
            )

        def wtap(g, tap, zcs):
            return jnp.concatenate(
                [jnp.concatenate([wtile(g, tap, zc, xx) for xx in range(2)], axis=1) for zc in zcs], axis=0
            )

        ALL = (0, 2, 1, 3)

        def half_of(core):
            return (core, core + 2)

        def wproj(zcs):
            return jnp.concatenate(
                [
                    jnp.concatenate([wtile(k3, j, zc, xx) for xx in range(2) for j in range(3)], axis=1)
                    for zc in zcs
                ],
                axis=0,
            )

        def flat(buf, base, i, size):
            return jnp.concatenate([buf[0, rows(i, size, base), :], buf[1, rows(i, size, base), :]], axis=1)

        barrier = pltpu.get_barrier_semaphore()

        def greet(k, carry):
            pl.semaphore_signal(barrier, inc=1, device_id=(lax.rem(d + k, n), h), device_id_type=MESH)
            return carry

        lax.fori_loop(1, n, greet, 0)
        for k in range(1, 4):
            pl.semaphore_signal(barrier, inc=1, device_id=(d, lax.rem(h + k, 4)), device_id_type=MESH)
        if inside:
            for a in range(3):
                r.g1[w * 2 + v, 0, pl.ds(a * 112, 112), :] = pack_taps(*[r.k1[3 * a + b] for b in range(3)])
        pl.semaphore_wait(barrier, n - 1 + 3)
        if inside:
            ga, gb, gc = Gather("g1"), Gather("g2"), Gather("p3")
            ga.own()

        def mix(m, carry):
            field = r.coef[0, m] * r.images[m].astype(F32) + r.coef[1, m] * r.noise[m].astype(F32)
            low = field.astype(BF16)
            for core in range(2):
                r.mx_src[m * 2 + core] = pack_pixels(dot(low, r.sel[core])).astype(BF16)
            return carry

        lax.fori_loop(0, 2, mix, 0)
        head_start(lambda p: r.mx_src.at[p], r.mx_dst, r.mx_s, r.mx_r)
        r.mx_dst[h] = r.mx_src[h]

        r.el[d] = silu(r.emb[...].astype(F32)).astype(BF16).astype(F32)
        dp_start(lambda p: r.el.at[d], r.el, r.el_s, r.el_r)

        if inside:
            blocks = dot(r.wa[...], r.selp[: 3 * BLK, : 3 * 128]).astype(BF16)
            r.sw_src[...] = blocks[:, 128:256]
            swap = rc(r.sw_src, r.sw_dst, r.sw_s.at[0], r.sw_r.at[0], sib)
            swap.start()
            for a in range(3):
                r.g2[w * 2 + v, 0, pl.ds(a * 112, 112), :] = pack_taps(*[r.k2[3 * a + b] for b in range(3)])
        r.par[0:3, :] = r.gains[...]
        r.par[3:13, :] = r.biases[...]
        r.par[13:16, :] = jnp.zeros((3, 384), F32)
        r.parown[...] = exact_dot(r.par[...], r.sel[c])

        def prow(i):
            return r.parown[pl.ds(i, 1), :]

        for buf in (r.act1, r.act2):
            for core in range(2):
                buf[core, pl.ds(0, ROW), :] = jnp.zeros((ROW, HALF), BF16)
                buf[core, pl.ds(PX + ROW, ROW), :] = jnp.zeros((ROW, HALF), BF16)
        for buf in (r.gr1, r.gr2):
            for b in range(3):
                buf[b, pl.ds(0, ROW), :] = jnp.zeros((ROW, HALF), BF16)
                buf[b, pl.ds(PX + ROW, ROW), :] = jnp.zeros((ROW, HALF), BF16)
        r.wfp[...] = jnp.zeros((128, HALF), BF16)
        r.wfp[pl.ds(0, film_rows), :] = dot(r.wf[...], r.selp[: 2 * BLK, :HALF]).astype(BF16)
        if inside:
            ga.pass_z()
            gb.own()

        count = float(PX * 12)

        def fold(vals):
            return jnp.sum(vals.reshape(CHUNK // 8, 8, HALF), axis=0)

        def sums_of(fn, k):
            def step(i, carry):
                return tuple(a + fold(b) for a, b in zip(carry, fn(i)))

            zero = jnp.zeros((8, HALF), F32)
            return lax.fori_loop(0, 4, step, (zero,) * k)

        def group_mean(part):
            return jnp.sum(exact_dot(part, r.gmask[...]), axis=0, keepdims=True) / count

        def norm(load, which, total):
            mean = group_mean(total)
            (square,) = sums_of(lambda i: (jnp.square(load(i) - mean),), 1)
            inv = lax.rsqrt(group_mean(square) + EPS)
            r.stat[pl.ds(2 * which, 1), :] = mean
            r.stat[pl.ds(2 * which + 1, 1), :] = inv
            return mean, inv

        zero8 = jnp.zeros((8, HALF), F32)

        def norm_back(sums, load_grad, load_hat, coef, inv):
            plain, cross = sums
            plain_mean, cross_mean = group_mean(coef * plain), group_mean(coef * cross)
            outer, base, slope = inv * coef, inv * plain_mean, inv * cross_mean

            def chunk(i):
                return outer * load_grad(i) - base - load_hat(i) * slope

            return (
                jnp.sum(plain, axis=0, keepdims=True),
                jnp.sum(cross, axis=0, keepdims=True),
                chunk,
            )

        head_wait(lambda p: r.mx_src.at[p], r.mx_dst, r.mx_s, r.mx_r)

        def unpack_mixed(i, carry):
            vals = unpack_pixels(r.mx_dst[i])
            r.mx[i] = vals
            return carry + fold(vals.astype(F32))

        mixed_sum = lax.fori_loop(0, 4, unpack_mixed, zero8)

        def mixed(i):
            return r.mx[i].astype(F32)

        mean1, inv1 = norm(mixed, 0, mixed_sum)
        gain1, shift1 = prow(0), prow(3)
        act1 = Halves("act1", ROW)

        def affine(mean, inv, gain, shift):
            return inv * gain, shift - mean * (inv * gain)

        mul1, add1 = affine(mean1, inv1, gain1, shift1)

        def pre1(i):
            return mixed(i) * mul1 + add1

        act1.fill(lambda i: silu(pre1(i)).astype(BF16))
        if inside:
            ga.pass_v()

        dp_wait(lambda p: r.el.at[d], r.el, r.el_s, r.el_r)
        for j in range(n):
            r.em[pl.ds(2 * j, 2), :] = r.el[j]
        place = lax.broadcasted_iota(jnp.int32, (768, 128), 0) - film_rows * d
        lane = lax.broadcasted_iota(jnp.int32, (768, 128), 1)
        pick = jnp.where((place == lane) & (lane < film_rows), 1.0, 0.0).astype(BF16)
        r.esel[...] = dot(r.em[...].astype(BF16), pick)
        film_part = dot(r.esel[...].astype(BF16), r.wfp[...])
        for j in range(n):
            r.fp[j] = film_part[2 * j : 2 * j + 2]
        dp_start(lambda p: r.fp.at[p], r.fr, r.fr_s, r.fr_r)
        r.fr[d] = r.fp[d]
        if inside:
            swap.wait()
            got = r.sw_dst[...]
            keep0, keep2 = blocks[:, :128], blocks[:, 256:]
            r.p3[w * 2 + v, 0] = pack_four(
                jnp.where(c == 0, keep0, got),
                jnp.where(c == 0, keep2, keep0),
                jnp.where(c == 0, got, keep2),
                r.wo[...],
            )
            gb.pass_z()
            gc.own()
        def split_cot(m, carry):
            for core in range(2):
                r.cx_src[m * 2 + core] = pack_pixels(dot(r.cot[m], r.sel[core])).astype(BF16)
            return carry

        lax.fori_loop(0, 2, split_cot, 0)
        column = lax.broadcasted_iota(jnp.int32, (1, ROW, HALF), 1)
        not_first = jnp.where(column > 0, 1.0, 0.0)
        not_last = jnp.where(column < ROW - 1, 1.0, 0.0)

        def in_rows(vals, mask):
            return (vals.reshape(CHUNK // ROW, ROW, HALF) * mask).reshape(CHUNK, HALF)

        def from_left(vals):
            return in_rows(pltpu.roll(vals, 1, 0), not_first)

        def from_right(vals):
            return in_rows(pltpu.roll(vals, CHUNK - 1, 0), not_last)

        def transpose_act(buf, base, out):
            for core in range(2):
                for q in range(4):
                    out[core, :, pl.ds(q * CHUNK, CHUNK)] = jnp.transpose(
                        buf[core, pl.ds(base + q * CHUNK, CHUNK), :]
                    )

        def conv(buf, g, store, between):
            weights = lambda: jnp.concatenate(
                [jnp.concatenate([wtap(g, 3 * a + b, ALL) for b in range(3)], axis=1) for a in range(3)], axis=0
            )

            total = zero8
            for i in range(2):
                left = jnp.concatenate([flat(buf, ROW * a, i, 2 * CHUNK) for a in range(3)], axis=1)
                out = dot(left, weights())
                for j in range(2):
                    part = out[j * CHUNK : j * CHUNK + CHUNK]
                    part = part[:, HALF : 2 * HALF] + from_left(part[:, :HALF]) + from_right(part[:, 2 * HALF :])
                    total = total + fold(store(2 * i + j, part))
                if i == 0:
                    between()
            return total

        act1.wait()
        transpose_act(r.act1, ROW, r.act1_t)
        if inside:
            ga.done()
            k1.unpack()

        def store_v2(i, vals):
            vals = vals + prow(6)
            r.v2[rows(i), :] = vals
            return vals

        v2_sum = conv(r.act1, k1, store_v2, gb.pass_v if inside else lambda: None)
        dp_wait(lambda p: r.fp.at[p], r.fr, r.fr_s, r.fr_r)
        film_sum = r.fr[0]
        for j in range(1, n):
            film_sum = film_sum + r.fr[j]
        for m in range(2):
            for core in range(2):
                r.fx[m * 2 + core] = film_sum[m : m + 1, core * 128 : core * 128 + 128]
        head_start(lambda p: r.fx.at[p], r.fh, r.fh_s, r.fh_r)
        r.fh[h] = r.fx[h]

        head_wait(lambda p: r.fx.at[p], r.fh, r.fh_s, r.fh_r)
        scale = 1.0 + (jnp.concatenate([r.fh[0], r.fh[1]], axis=1) + prow(8))
        shift = jnp.concatenate([r.fh[2], r.fh[3]], axis=1) + prow(9)
        head_start(lambda p: r.cx_src.at[p], r.cx_dst, r.cx_s, r.cx_r)
        r.cx_dst[h] = r.cx_src[h]
        mean2, inv2 = norm(lambda i: r.v2[rows(i), :], 1, v2_sum)
        gain2, shift2 = prow(1), prow(4)
        act2 = Halves("act2", ROW)

        def hat2(i):
            return (r.v2[rows(i), :] - mean2) * inv2

        mul2, add2 = affine(mean2, inv2, gain2 * scale, shift2 * scale + shift)

        def pre2(i):
            return r.v2[rows(i), :] * mul2 + add2

        act2.fill(lambda i: silu(pre2(i)).astype(BF16))
        if inside:
            gc.pass_z()

        act2.wait()
        transpose_act(r.act2, ROW, r.act2_t)
        if inside:
            gb.done()
            k2.unpack()

        def store_v3(i, vals):
            vals = mixed(i) + (vals + prow(7))
            r.v3[rows(i), :] = vals
            return vals

        v3_sum = conv(r.act2, k2, store_v3, gc.pass_v if inside else lambda: None)
        mean3, inv3 = norm(lambda i: r.v3[rows(i), :], 2, v3_sum)
        gain3, shift3 = prow(2), prow(5)
        ai = Halves("ai", 0)

        def hat3(i):
            return (r.v3[rows(i), :] - mean3) * inv3

        mul3, add3 = affine(mean3, inv3, gain3, shift3)
        ai.fill(lambda i: (r.v3[rows(i), :] * mul3 + add3).astype(BF16))

        if inside:
            gc.done()
            k3.unpack()
        head_wait(lambda p: r.cx_src.at[p], r.cx_dst, r.cx_s, r.cx_r)

        def unpack_cot(i):
            r.cx[i] = unpack_pixels(r.cx_dst[i])

        loop(4, unpack_cot)
        dop = Parts("do")

        def cot_rows(i):
            return jnp.concatenate([r.cx[2 * i], r.cx[2 * i + 1]], axis=0)

        dop.fill(lambda i: dot_nt(cot_rows(i), wtap(k3, 3, half_of(1 - c))))

        ai.wait()
        bias_proj = [prow(10)[:, :128], prow(10)[:, 128:], None, None, prow(11)[:, :128], prow(11)[:, 128:]]

        def project(i):
            out = dot(flat(r.ai, 0, i, 2 * CHUNK), wproj(ALL))
            for k in range(6):
                part = out[:, k * 128 : k * 128 + 128]
                if bias_proj[k] is not None:
                    part = part + bias_proj[k]
                r.qkv[k, rows(i, 2 * CHUNK), :] = part.astype(BF16)

        each(2, project)

        def do_own(i):
            full = (dot_nt(cot_rows(i), wtap(k3, 3, half_of(c))) + dop.get(i)).astype(BF16)
            for k in range(2):
                r.dout[k, rows(i, 2 * CHUNK), :] = full[:, k * 128 : k * 128 + 128]

        each(2, do_own)

        factor = 1.0 / math.sqrt(HEAD_DIM)
        factor2 = factor * math.log2(math.e)
        att = []

        def transposes(k):
            r.kvt[k] = jnp.transpose(r.qkv[k + 2])

        loop(4, transposes)

        def att_copy(core, k):
            ref = r.att.at[core * 2 + k]
            return rc(ref, ref, r.att_s.at[k], r.att_r.at[k], sib)

        def att_t_copy(core, k):
            ref = r.att_t.at[core, pl.ds(pl.multiple_of(k * 128, 128), 128)]
            return rc(ref, ref, r.att_s.at[2 + k], r.att_r.at[2 + k], sib)

        def one_head(k):
            lows, grads = [], []
            for b in range(2):
                at = pl.ds(b * 2 * CHUNK, 2 * CHUNK)
                query = r.qkv[k, at, :]
                grad = r.dout[k, at, :]
                scores = dot_nt(r.qkv[2 + k], query)
                peak = jnp.max(scores, axis=0, keepdims=True)
                expo = jnp.exp2((scores - peak) * factor2)
                inverse = 1.0 / jnp.sum(expo, axis=0, keepdims=True)
                low = (expo * inverse).astype(BF16)
                got = dot(r.kvt[2 + k], low)
                got_low = got.astype(BF16)
                r.att_t[c, pl.ds(pl.multiple_of(k * 128, 128), 128), at] = got_low
                r.att[2 * c + k, at, :] = jnp.transpose(got_low)
                spread = jnp.sum(got * jnp.transpose(grad).astype(F32), axis=0, keepdims=True)
                probs_grad = dot_nt(r.qkv[4 + k], grad)
                scores_grad = ((probs_grad - spread) * inverse * expo).astype(BF16)
                back = dot(r.kvt[k], scores_grad)
                r.dproj[k, at, :] = (jnp.transpose(back) * factor).astype(BF16)
                lows.append(low)
                grads.append(scores_grad)
            att_copy(c, k).start()
            att_t_copy(c, k).start()
            r.dproj[4 + k] = dot(jnp.concatenate(lows, axis=1), r.dout[k]).astype(BF16)
            r.dproj[2 + k] = (dot(jnp.concatenate(grads, axis=1), r.qkv[k]) * factor).astype(BF16)

        loop(2, one_head)

        n3 = Parts("n3")

        def proj_rows(i):
            return jnp.concatenate([r.dproj[k, rows(i, 2 * CHUNK), :] for k in range(6)], axis=1)

        n3.fill(lambda i: dot_nt(proj_rows(i), wproj(half_of(1 - c))))

        for k in range(2):
            copy = att_copy(1 - c, k)
            copy.wait_recv()
            copy.wait_send()

        def result(i):
            left = jnp.concatenate([r.att[p, rows(i), :] for p in range(4)], axis=1)
            branch = dot(left, wtap(k3, 3, ALL)) + prow(12)
            r.ro_src[i] = pack_pixels(r.v3[rows(i), :] + branch).astype(BF16)

        loop(4, result)
        head_start(lambda p: r.ro_src.at[p], r.ro_dst, r.ro_s, r.ro_r)
        r.ro_dst[h] = r.ro_src[h]

        if inside:
            red1, red2, red3 = Reduce("r1", 3), Reduce("r2", 3), Reduce("r3", 1)
            acc1, acc2, acc3 = r.r1_acc, r.r2_acc, r.r3_acc
        else:
            acc1, acc2, acc3 = r.first, r.second, r.attend

        transpose_act(r.ai, 0, r.ai_t)
        for k in range(2):
            copy = att_t_copy(1 - c, k)
            copy.wait_recv()
            copy.wait_send()
        right = jnp.concatenate([r.dproj[k] for k in range(6)], axis=1)
        cot_all = jnp.concatenate([r.cx[i] for i in range(4)], axis=0)
        for core in range(2):
            attend_out = dot(r.ai_t[core], right)
            output_out = dot(r.att_t[core], cot_all)
            for k in range(2):
                for yy in range(2):
                    for xx in range(2):
                        row = k * 128 + yy * 48
                        tiles = [
                            attend_out[row : row + 48, (xx * 3 + j) * 128 : (xx * 3 + j) * 128 + 128] for j in range(3)
                        ]
                        acc3[0, slot(xx, yy), core + 2 * k] = pack_four(
                            *tiles, output_out[row : row + 48, xx * 128 : xx * 128 + 128]
                        )
        if inside:
            red3.start(0)

        def proj_sums(i, carry):
            q = jnp.concatenate([r.dproj[0, rows(i), :], r.dproj[1, rows(i), :]], axis=1).astype(F32)
            val = jnp.concatenate([r.dproj[4, rows(i), :], r.dproj[5, rows(i), :]], axis=1).astype(F32)
            return (carry[0] + fold(q), carry[1] + fold(val), carry[2] + fold(r.cx[i].astype(F32)))

        qsum, vsum, csum = lax.fori_loop(0, 4, proj_sums, (zero8, zero8, zero8))
        r.sums[pl.ds(3 + 7, 1), :] = jnp.sum(qsum, axis=0, keepdims=True)
        r.sums[pl.ds(3 + 8, 1), :] = jnp.sum(vsum, axis=0, keepdims=True)
        r.sums[pl.ds(3 + 9, 1), :] = jnp.sum(csum, axis=0, keepdims=True)
        r.sums[pl.ds(13, 3), :] = jnp.zeros((3, HALF), F32)

        def n3_own(i, carry):
            both = dot_nt(proj_rows(i), wproj(half_of(c))) + n3.get(i)
            for j in range(2):
                vals = both[j * CHUNK : j * CHUNK + CHUNK]
                r.gtmp[rows(2 * i + j), :] = vals
                carry = carry[0] + fold(vals), carry[1] + fold(vals * hat3(2 * i + j))
            return carry

        sums3 = n3_own(1, n3_own(0, (zero8, zero8)))
        plain3, cross3, back3 = norm_back(sums3, lambda i: r.gtmp[rows(i), :], hat3, gain3, inv3)
        r.sums[pl.ds(2, 1), :] = cross3
        r.sums[pl.ds(3 + 2, 1), :] = plain3

        def shifted(buf, i, vals):
            buf[0, rows(i, CHUNK, ROW), :] = from_right(vals).astype(BF16)
            buf[1, rows(i, CHUNK, ROW), :] = vals.astype(BF16)
            buf[2, rows(i, CHUNK, ROW), :] = from_left(vals).astype(BF16)

        def residual_back(i, carry):
            vals = r.cx[i].astype(F32) + back3(i)
            r.gres[rows(i), :] = vals
            shifted(r.gr2, i, vals)
            return carry + fold(vals.astype(BF16).astype(F32))

        bias_two = lax.fori_loop(0, 4, residual_back, jnp.zeros((8, HALF), F32))
        r.sums[pl.ds(3 + 4, 1), :] = jnp.sum(bias_two, axis=0, keepdims=True)

        def act_back(buf, g, core, i, size):
            left = jnp.concatenate(
                [buf[b, rows(i, size, 2 * ROW - ROW * a), :] for a in range(3) for b in range(3)], axis=1
            )
            right = jnp.concatenate(
                [wtap(g, 3 * a + b, half_of(core)) for a in range(3) for b in range(3)], axis=1
            )
            return dot_nt(left, right)

        def conv_back(parts, buf, g):
            parts.fill(lambda i: act_back(buf, g, 1 - c, i, 2 * CHUNK))

        def conv_back_own(parts, buf, g, outer, hat):
            def own(i, carry):
                vals = act_back(buf, g, c, i, 2 * CHUNK) + parts.get(i)
                for j in range(2):
                    at = 2 * i + j
                    grad = vals[j * CHUNK : j * CHUNK + CHUNK] * outer(at)
                    r.gtmp[rows(at), :] = grad
                    carry = carry[0] + fold(grad), carry[1] + fold(grad * hat(at))
                return carry

            return own(1, own(0, (zero8, zero8)))

        def kernel_grad(act_t, buf, acc, after):
            def step(a):
                right = jnp.concatenate([buf[b, pl.ds(2 * ROW - ROW * a, PX), :] for b in range(3)], axis=1)
                out = dot(jnp.concatenate([act_t[0], act_t[1]], axis=0), right)
                for p, zc in enumerate(ALL):
                    for yy in range(2):
                        for xx in range(2):
                            row = p * 128 + yy * 48
                            tiles = [
                                out[row : row + 48, b * HALF + xx * 128 : b * HALF + xx * 128 + 128] for b in range(3)
                            ]
                            acc[a, slot(xx, yy), zc] = pack_taps(*tiles)
                after(a)

            each(3, step)

        serve = inside
        d2 = Parts("d2")
        kernel_grad(r.act2_t, r.gr2, acc2, red2.start if inside else lambda a: None)
        if serve:
            red3.second(0, 1)
        conv_back(d2, r.gr2, k2)
        if serve:
            red2.second(0, 1)
        sums2 = conv_back_own(d2, r.gr2, k2, lambda i: silu_slope(pre2(i)), hat2)
        if serve:
            red2.second(1, 1)
            red3.third(0, 1)

        plain2, cross2, back2 = norm_back(sums2, lambda i: r.gtmp[rows(i), :], hat2, gain2 * scale, inv2)
        r.sums[pl.ds(1, 1), :] = scale * cross2
        r.sums[pl.ds(3 + 1, 1), :] = scale * plain2
        film_scale_term = gain2 * cross2 + shift2 * plain2
        r.sums[pl.ds(3 + 5, 1), :] = film_scale_term
        r.sums[pl.ds(3 + 6, 1), :] = plain2
        for j in range(2):
            r.ft[j] = film_scale_term[:, j * 128 : j * 128 + 128]
            r.ft[2 + j] = plain2[:, j * 128 : j * 128 + 128]
        head_start(lambda p: r.ft.at[p], r.th, r.th_s, r.th_r)
        r.th[h] = r.ft[h]

        def first_back(i, carry):
            vals = back2(i)
            shifted(r.gr1, i, vals)
            return carry + fold(vals.astype(BF16).astype(F32))

        bias_one = lax.fori_loop(0, 4, first_back, jnp.zeros((8, HALF), F32))
        r.sums[pl.ds(3 + 3, 1), :] = jnp.sum(bias_one, axis=0, keepdims=True)

        if serve:
            red2.second(2, 1)
            red2.third(0, 1)
            red2.third(1, 1)

        head_wait(lambda p: r.ft.at[p], r.th, r.th_s, r.th_r)
        for m in range(2):
            r.fa[d, pl.ds(m, 1), :] = jnp.concatenate([r.th[2 * m], r.th[2 * m + 1]], axis=1)
        dp_start(lambda p: r.fa.at[d], r.fa, r.fa_s, r.fa_r)

        d1 = Parts("d1")

        def after_chunk(a):
            if serve:
                red1.start(a)
                if a == 1:
                    red2.third(2, 1)

        kernel_grad(r.act1_t, r.gr1, acc1, after_chunk)
        conv_back(d1, r.gr1, k1)
        if serve:
            red1.second(0, 1)

        dp_wait(lambda p: r.fa.at[d], r.fa, r.fa_s, r.fa_r)
        for j in range(n):
            r.fta[pl.ds(2 * j, 2), :] = r.fa[j]
        film_block = dot_tn_high(r.esel[...], r.fta[...])
        r.film[...] = jnp.concatenate([film_block[:film_rows, :BLK], film_block[:film_rows, 128 : 128 + BLK]], axis=1)
        embed_part = dot_nt_high(r.fta[...], r.wfp[...].astype(F32))
        for j in range(n):
            r.ep[j] = embed_part[2 * j : 2 * j + 2]
        dp_start(lambda p: r.ep.at[p], r.er, r.er_s, r.er_r)
        r.er[d] = r.ep[d]

        def hat1(i):
            return (mixed(i) - mean1) * inv1

        sums1 = conv_back_own(d1, r.gr1, k1, lambda i: silu_slope(pre1(i)), hat1)
        if serve:
            red1.second(1, 1)

        dp_wait(lambda p: r.ep.at[p], r.er, r.er_s, r.er_r)
        r.eh[h] = r.er[...]
        head_start(lambda p: r.eh.at[h], r.eh, r.eh_s, r.eh_r)
        plain1, cross1, back1 = norm_back(sums1, lambda i: r.gtmp[rows(i), :], hat1, gain1, inv1)
        r.sums[pl.ds(0, 1), :] = cross1
        r.sums[pl.ds(3, 1), :] = plain1
        r.ad[d] = r.sums[...]
        dp_start(lambda p: r.ad.at[d], r.ad, r.ad_s, r.ad_r)

        if serve:
            red1.second(2, 1)
            red1.third(0, 1)
        keep = r.coef[0, x]

        def image_back(i):
            r.io_src[i] = pack_pixels(keep * (r.gres[rows(i), :] + back1(i))).astype(BF16)

        loop(4, image_back)
        head_start(lambda p: r.io_src.at[p], r.io_dst, r.io_s, r.io_r)
        r.io_dst[h] = r.io_src[h]
        if serve:
            red1.third(1, 1)
            red1.third(2, 1)

        dp_wait(lambda p: r.ad.at[d], r.ad, r.ad_s, r.ad_r)
        total = r.ad[0]
        for j in range(1, n):
            total = total + r.ad[j]
        r.hb[h] = total
        head_start(lambda p: r.hb.at[h], r.hb, r.hb_s, r.hb_r)
        head_wait(lambda p: r.ro_src.at[p], r.ro_dst, r.ro_s, r.ro_r)

        if inside:
            red2.finish(((0, 1), (1, 1), (2, 1)))
            for a in range(3):
                r.second[a] = red2.last(a)

        head_wait(lambda p: r.hb.at[h], r.hb, r.hb_s, r.hb_r)
        even = r.hb[0] + r.hb[2]
        odd = r.hb[1] + r.hb[3]
        wide = jnp.concatenate(
            [even[:, :BLK], odd[:, :BLK], even[:, 128 : 128 + BLK], odd[:, 128 : 128 + BLK]], axis=1
        )
        r.gains_out[...] = wide[0:3]
        r.biases_out[...] = wide[3:13]

        head_wait(lambda p: r.eh.at[h], r.eh, r.eh_s, r.eh_r)
        pieces = []
        for j in range(n):
            piece = (r.eh[0, j] + r.eh[1, j]) + (r.eh[2, j] + r.eh[3, j])
            pieces.append(piece[:, :film_rows])
        r.embed_grad[...] = jnp.concatenate(pieces, axis=1) * silu_slope(r.emb[...].astype(F32))

        head_wait(lambda p: r.io_src.at[p], r.io_dst, r.io_s, r.io_r)

        if inside:
            red3.finish(((0, 1),))
            tiles = unpack_four(red3.last(0))
            r.sb_src[...] = jnp.where(c == 0, tiles[2], tiles[0])
            back = rc(r.sb_src, r.sb_dst, r.sb_s.at[0], r.sb_r.at[0], sib)
            back.start()
            r.output[...] = tiles[3]
            red1.finish(((0, 1), (1, 1), (2, 1)))
            for a in range(3):
                r.first[a] = red1.last(a)
            back.wait()
            r.attend[:, 0:128] = jnp.where(c == 0, tiles[0], tiles[1])
            r.attend[:, 128:256] = r.sb_dst[...]
            r.attend[:, 256:384] = jnp.where(c == 0, tiles[1], tiles[2])

    return kernel


def make_writer(names_in, names_out):
    def kernel(*refs):
        count = len(names_in)
        src, dst = Names(names_in, refs[:count]), Names(names_out, refs[count:])
        for name, packed in (("result", src.ro_dst), ("image_grad", src.io_dst)):
            for m in range(2):
                getattr(dst, name)[m] = dot_nt(unpack_pixels(packed[2 * m]), src.sel[0]) + dot_nt(
                    unpack_pixels(packed[2 * m + 1]), src.sel[1]
                )
        for name in ("first", "second"):
            if name in names_out:
                for a in range(3):
                    block = getattr(src, name)[a]
                    getattr(dst, name)[3 * a] = block[:48, :BLK]
                    getattr(dst, name)[3 * a + 1] = block[48:96, :BLK]
                    getattr(dst, name)[3 * a + 2] = last_tap(block)[:, :BLK]
        if "attend" in names_out:
            dst.attend[...] = jnp.concatenate([src.attend[:, j * 128 : j * 128 + BLK] for j in range(3)], axis=1)
            dst.output[...] = src.output[:, :BLK]
        for name in ("embed_grad", "film", "gains_out", "biases_out"):
            getattr(dst, name)[...] = getattr(src, name)[...]

    return kernel


def per_device(n, *args):
    (
        images,
        noise_field,
        time_steps,
        embedding,
        first_kernel,
        second_kernel,
        film_weight,
        attend_weight,
        output_weight,
        norm_gains,
        biases,
        cotangent,
    ) = args
    inside = n == 8
    keep, noise = plan(time_steps)
    coef = jnp.stack([keep, noise])
    maps, height, width, channels = images.shape
    flat_shape = (maps, height * width, channels)
    film_rows = film_weight.shape[0]
    inputs = dict(
        coef=coef,
        images=images.reshape(flat_shape),
        noise=noise_field.reshape(flat_shape),
        cot=cotangent.reshape(flat_shape),
        emb=embedding,
        k1=first_kernel.reshape((9,) + first_kernel.shape[2:]),
        k2=second_kernel.reshape((9,) + second_kernel.shape[2:]),
        wf=film_weight,
        wa=attend_weight,
        wo=output_weight,
        gains=norm_gains,
        biases=biases,
        sel=jnp.asarray(channel_lanes(), BF16),
        gmask=jnp.asarray(group_mask(), BF16),
        selp=jnp.asarray(block_lanes(3), BF16),
    )
    shapes = dict(
        ro_dst=(4, 384, 128),
        io_dst=(4, 384, 128),
        embed_grad=embedding.shape,
        first=(3, 112, 128),
        second=(3, 112, 128),
        film=film_weight.shape,
        attend=(48, 384),
        output=(48, 128),
        gains_out=norm_gains.shape,
        biases_out=biases.shape,
    )
    names_in, names_out = list(INPUTS), list(OUTPUTS)
    core = lax.axis_index("head") % 2
    if not inside:
        def whole(array, row_axis):
            array = lax.all_gather(array, "dp", axis=row_axis, tiled=True)
            return lax.all_gather(array, "head", axis=array.ndim - 1, tiled=True)

        def spread(array, count):
            taps = array.shape[0]
            array = array.reshape(taps, 4, 2, 48, 2, 2, BLK)
            array = lax.dynamic_index_in_dim(array, core, 5, keepdims=False)
            array = jnp.transpose(array, (2, 4, 1, 0, 3, 5))
            array = jnp.pad(array, ((0, 0),) * 5 + ((0, 32),))
            return array.reshape(4, 4, taps * 48, 128)

        full_a = whole(attend_weight, 0).reshape(384, 2, 3, 2, BLK)
        full_a = jnp.transpose(full_a, (2, 0, 1, 3, 4)).reshape(3, 384, 384)
        full_o = whole(output_weight, 0)[None]
        for name, last, array in (("g1", "t1", first_kernel), ("g2", "t2", second_kernel)):
            blocks = spread(whole(array, 2).reshape(9, 384, 384), 9).reshape(4, 4, 3, 3, 48, 128)
            two = blocks[:, :, :, :2].reshape(4, 4, 3, 96, 128)
            inputs[name] = jnp.pad(two, ((0, 0),) * 3 + ((0, 16), (0, 0))).reshape(4, 4, 336, 128)
            inputs[last] = blocks[:, :, :, 2].reshape(4, 4, 144, 128)
        inputs["g3"] = spread(jnp.concatenate([full_a, full_o], axis=0), 4)
        names_in += ["g1", "g2", "t1", "t2", "g3"]
        shapes["first"] = shapes["second"] = (3, 4, 4, 112, 128)
        shapes["attend"] = (1, 4, 4, 144, 128)
        del shapes["output"]
        names_out.remove("output")
    items = scratch_list(n, inside)
    smem = pl.BlockSpec(memory_space=pltpu.SMEM)
    vmem = pl.BlockSpec(memory_space=pltpu.VMEM)
    outs = pl.pallas_call(
        make_kernel(n, inside, names_in + names_out + [name for name, _ in items]),
        out_shape=[
            jax.ShapeDtypeStruct(shapes[name], BF16 if name in ("ro_dst", "io_dst") else F32) for name in names_out
        ],
        in_specs=[smem if name == "coef" else vmem for name in names_in],
        out_specs=[vmem] * len(names_out),
        scratch_shapes=[item for _, item in items],
        compiler_params=pltpu.CompilerParams(
            collective_id=0, has_side_effects=True, vmem_limit_bytes=63 * 1024 * 1024
        ),
        name="blocks",
    )(*[inputs[name] for name in names_in])
    raw = dict(zip(names_out, outs))
    final = dict(
        result=flat_shape,
        image_grad=flat_shape,
        embed_grad=embedding.shape,
        film=film_weight.shape,
        gains_out=norm_gains.shape,
        biases_out=biases.shape,
    )
    if inside:
        final.update(first=(9, 48, BLK), second=(9, 48, BLK), attend=attend_weight.shape, output=output_weight.shape)
    names_last = [name for name in names_out if inside or name not in ("first", "second", "attend")] + ["sel"]
    names_final = list(final)
    outs = pl.pallas_call(
        make_writer(names_last, names_final),
        out_shape=[jax.ShapeDtypeStruct(final[name], F32) for name in names_final],
        in_specs=[vmem] * len(names_last),
        out_specs=[vmem] * len(names_final),
        compiler_params=pltpu.CompilerParams(vmem_limit_bytes=63 * 1024 * 1024),
        name="outputs",
    )(*[inputs["sel"] if name == "sel" else raw[name] for name in names_last])
    out = dict(zip(names_final, outs))
    if not inside:

        def blocks_of(array, size):
            parts = [array[..., k * 48 : k * 48 + 48, :BLK] for k in range(size)]
            if size == 2:
                lanes = [array[..., k * 32 : k * 32 + 32, BLK:] for k in range(3)]
                lanes = jnp.concatenate(lanes, axis=-1)
                parts.append(jnp.concatenate([lanes, array[..., 96:112, :BLK]], axis=-2))
            else:
                lanes = [array[..., k * 48 : k * 48 + 48, BLK:] for k in range(3)]
                parts.append(jnp.concatenate(lanes, axis=-1))
            array = jnp.stack(parts, axis=1)
            array = array.reshape(array.shape[:2] + (2, 2, 4, 48, BLK))
            taps = array.shape[0] * array.shape[1]
            array = jnp.transpose(array, (0, 1, 4, 2, 5, 3, 6)).reshape(taps, 384, 2, 1, BLK)
            both = jnp.concatenate([array, jnp.zeros_like(array)], axis=3)
            return jnp.where(core == 0, both, both[:, :, :, ::-1]).reshape(taps, 384, 384)

        def shared(array, axis):
            array = lax.psum_scatter(array, "head", scatter_dimension=array.ndim - 1, tiled=True)
            return lax.psum_scatter(array, "dp", scatter_dimension=axis, tiled=True)

        out["first"] = shared(blocks_of(raw["first"], 2), 1)
        out["second"] = shared(blocks_of(raw["second"], 2), 1)
        both = blocks_of(raw["attend"], 3)
        joined = both[:3].reshape(3, 384, 2, 2, BLK)
        joined = jnp.transpose(joined, (1, 2, 0, 3, 4)).reshape(384, 1152)
        out["attend"] = shared(joined, 0)
        out["output"] = shared(both[3], 0)
    return (
        out["result"].reshape(images.shape),
        out["image_grad"].reshape(images.shape),
        out["embed_grad"],
        out["first"].reshape(first_kernel.shape),
        out["second"].reshape(second_kernel.shape),
        out["film"],
        out["attend"],
        out["output"],
        out["gains_out"],
        out["biases_out"],
    )


def solution(mesh):
    n = mesh.shape["dp"]
    field = P("dp", "head", None, None)
    taps = P(None, None, "dp", "head")
    both = P("dp", "head")
    return jax.shard_map(
        lambda *args: per_device(n, *args),
        mesh=mesh,
        in_specs=(field, field, P("dp"), P("dp", None), taps, taps, both, both, both, P(), P(), field),
        out_specs=(field, field, P("dp", None), taps, taps, both, both, both, P(), P()),
        check_vma=False,
    )
```

```python
import math

import jax
import jax.numpy as jnp
import numpy as np
from jax import lax
from jax.experimental import pallas as pl
from jax.experimental.pallas import tpu as pltpu
from jax.sharding import PartitionSpec as P

HEAD_DIM = 96
GROUPS = 32
STEPS = 4000
EPS = 1e-05
OFFSET = 0.008
MESH = pl.DeviceIdType.MESH
F32 = jnp.float32
BF16 = jnp.bfloat16

PX = 1024
ROW = 32
CHUNK = 256
BLK = 96
HALF = 256
NHEAD = 4


def plan(time_steps):
    fraction = (time_steps.astype(F32) + 1.0) / STEPS
    start = jnp.square(jnp.cos(jnp.float32(OFFSET / (1.0 + OFFSET) * (math.pi / 2))))
    curve = jnp.square(jnp.cos((fraction + OFFSET) / (1.0 + OFFSET) * (math.pi / 2))) / start
    return (jnp.sqrt(curve), jnp.sqrt(1.0 - curve))


def channel_lanes():
    sel = np.zeros((2, 384, HALF), np.float32)
    for block in range(4):
        for j in range(BLK):
            sel[block % 2, block * BLK + j, (block // 2) * 128 + j] = 1.0
    return sel


def block_lanes(count):
    sel = np.zeros((count * BLK, count * 128), np.float32)
    for block in range(count):
        for j in range(BLK):
            sel[block * BLK + j, block * 128 + j] = 1.0
    return sel


def group_mask():
    lane = np.arange(HALF)
    ok = lane % 128 < BLK
    group = (lane // 128) * 100 + (lane % 128) // 12
    return ((group[:, None] == group[None, :]) & ok[:, None] & ok[None, :]).astype(np.float32)


def dot(a, b):
    return lax.dot_general(a, b, (((1,), (0,)), ((), ())), preferred_element_type=F32)


def dot_nt(a, b):
    return lax.dot_general(a, b, (((1,), (1,)), ((), ())), preferred_element_type=F32)


def dot_nt_high(a, b):
    return lax.dot_general(
        a, b, (((1,), (1,)), ((), ())), preferred_element_type=F32, precision=lax.Precision.HIGHEST
    )


def dot_tn_high(a, b):
    return lax.dot_general(
        a, b, (((0,), (0,)), ((), ())), preferred_element_type=F32, precision=lax.Precision.HIGHEST
    )


def exact_dot(values, ones):
    high = values.astype(BF16).astype(F32)
    rest = values - high
    middle = rest.astype(BF16).astype(F32)
    low = rest - middle
    rows = values.shape[0]
    out = dot(jnp.concatenate([high, middle, low], axis=0).astype(BF16), ones)
    return out[:rows] + out[rows : 2 * rows] + out[2 * rows :]


def sigmoid(v):
    return 0.5 + 0.5 * jnp.tanh(0.5 * v)


def silu(v):
    return v * sigmoid(v)


def silu_slope(v):
    s = sigmoid(v)
    return s * (1.0 + v * (1.0 - s))


def pack_taps(t0, t1, t2):
    t0, t1, t2 = t0[:, :BLK], t1[:, :BLK], t2[:, :BLK]
    join = lambda a, b: jnp.concatenate([a, b], axis=1)
    return jnp.concatenate(
        [
            join(t0[:32], t2[:32, :32]),
            join(t0[32:], t2[:16, 32:64]),
            join(t1[:16], t2[16:32, 32:64]),
            join(t1[16:], t2[:32, 64:]),
            join(t2[32:], jnp.zeros((16, 32), t2.dtype)),
        ],
        axis=0,
    )


def last_tap(packed):
    lanes = [packed[:32, BLK:], packed[32:64, BLK:], packed[64:96, BLK:], jnp.zeros((32, 32), packed.dtype)]
    return jnp.concatenate([jnp.concatenate(lanes, axis=1), packed[96:112]], axis=0)


def pack_four(b0, b1, b2, b3):
    return jnp.concatenate(
        [jnp.concatenate([b[:, :BLK], b3[:, 32 * k : 32 * k + 32]], axis=1) for k, b in enumerate((b0, b1, b2))],
        axis=0,
    )


def unpack_four(packed):
    size = packed.shape[0] // 3
    parts = [packed[k * size : k * size + size] for k in range(3)]
    zero = jnp.zeros((size, 32), packed.dtype)
    fourth = jnp.concatenate([p[:, BLK:] for p in parts] + [zero], axis=1)
    return [jnp.concatenate([p[:, :BLK], zero], axis=1) for p in parts] + [fourth]


def pack_pixels(full):
    half = CHUNK // 2
    return pack_four(full[:half, :128], full[half:, :128], full[:half, 128:], full[half:, 128:])


def unpack_pixels(packed):
    b0, b1, b2, b3 = unpack_four(packed)
    return jnp.concatenate([jnp.concatenate([b0, b2], axis=1), jnp.concatenate([b1, b3], axis=1)], axis=0)


INPUTS = (
    "coef",
    "images",
    "noise",
    "cot",
    "emb",
    "k1",
    "k2",
    "wf",
    "wa",
    "wo",
    "gains",
    "biases",
    "sel",
    "gmask",
    "selp",
)
OUTPUTS = (
    "ro_dst",
    "io_dst",
    "embed_grad",
    "first",
    "second",
    "film",
    "attend",
    "output",
    "gains_out",
    "biases_out",
)


class Names:
    def __init__(self, names, refs):
        for name, ref in zip(names, refs):
            setattr(self, name, ref)


def scratch_list(n, inside):
    dma = pltpu.SemaphoreType.DMA
    items = []

    def vm(name, shape, dtype):
        items.append((name, pltpu.VMEM(shape, dtype)))

    def sem(name, count):
        items.append((name + "_s", dma((count,))))
        items.append((name + "_r", dma((count,))))

    for name in ("mx", "cx", "ro", "io"):
        vm(name + "_src", (4, 384, 128), BF16)
        if name in ("mx", "cx"):
            vm(name + "_dst", (4, 384, 128), BF16)
            vm(name, (4, CHUNK, HALF), BF16)
        sem(name, 4)
    for name in ("act1", "act2"):
        vm(name, (2, PX + 2 * ROW, HALF), BF16)
        vm(name + "_t", (2, HALF, PX), BF16)
        sem(name, 4)
        sem(name + "_t", 1)
    vm("ai", (2, PX, HALF), BF16)
    vm("ai_t", (2, HALF, PX), BF16)
    sem("ai_t", 1)
    sem("ai", 4)
    vm("att", (4, PX, 128), BF16)
    vm("att_t", (2, HALF, PX), BF16)
    sem("att", 4)
    for name in ("do", "n3", "d2", "d1"):
        vm(name + "_src", (PX, HALF), BF16)
        vm(name + "_dst", (PX, HALF), BF16)
        sem(name, 2)
    vm("v2", (PX, HALF), F32)
    vm("v3", (PX, HALF), F32)
    vm("gres", (PX, HALF), F32)
    vm("gtmp", (PX, HALF), F32)
    vm("qkv", (6, PX, 128), BF16)
    vm("kvt", (4, 128, PX), BF16)
    vm("dout", (2, PX, 128), BF16)
    vm("dproj", (6, PX, 128), BF16)
    vm("gr2", (3, PX + 2 * ROW, HALF), BF16)
    vm("gr1", (3, PX + 2 * ROW, HALF), BF16)
    vm("par", (16, 384), F32)
    vm("parown", (16, HALF), F32)
    vm("stat", (16, HALF), F32)
    vm("sums", (16, HALF), F32)
    if inside:
        vm("g1", (4, 4, 336, 128), BF16)
        vm("g2", (4, 4, 336, 128), BF16)
        vm("t1", (4, 4, 144, 128), BF16)
        vm("t2", (4, 4, 144, 128), BF16)
        vm("p3", (4, 4, 144, 128), BF16)
        vm("g3", (4, 4, 192, 128), BF16)
        for name in ("g1", "g2", "p3"):
            sem(name + "z", 4)
            sem(name + "v", 4)
            sem(name + "w", 8)
        vm("sw_src", (48, 128), BF16)
        vm("sw_dst", (48, 128), BF16)
        sem("sw", 1)
        vm("sb_src", (48, 128), F32)
        vm("sb_dst", (48, 128), F32)
        sem("sb", 1)
        for name, nc, rows in (("r1", 3, 112), ("r2", 3, 112), ("r3", 1, 144)):
            vm(name + "_acc", (nc, 4, 4, rows, 128), F32)
            vm(name + "w_src", (nc, 2, 4, rows, 128), BF16)
            vm(name + "w_dst", (nc, 2, 4, rows, 128), BF16)
            vm(name + "v_src", (nc, 4, rows, 128), BF16)
            vm(name + "v_dst", (nc, 4, rows, 128), BF16)
            vm(name + "z_src", (4, nc, rows, 128), BF16)
            vm(name + "z_dst", (4, nc, rows, 128), BF16)
            sem(name + "w", nc)
            sem(name + "v", nc)
            sem(name + "z", nc * 4)
    vm("el", (n, 2, 768), F32)
    sem("el", n)
    vm("em", (2 * n, 768), F32)
    vm("wfp", (128, HALF), BF16)
    vm("esel", (2 * n, 128), F32)
    vm("fp", (n, 2, HALF), F32)
    vm("fr", (n, 2, HALF), F32)
    sem("fr", n)
    vm("fx", (4, 1, 128), F32)
    vm("fh", (4, 1, 128), F32)
    sem("fh", 4)
    vm("ft", (4, 1, 128), F32)
    vm("th", (4, 1, 128), F32)
    sem("th", 4)
    vm("fa", (n, 2, HALF), F32)
    sem("fa", n)
    vm("fta", (2 * n, HALF), F32)
    vm("ep", (n, 2, 128), F32)
    vm("er", (n, 2, 128), F32)
    sem("er", n)
    vm("eh", (4, n, 2, 128), F32)
    sem("eh", 4)
    vm("ad", (n, 16, HALF), F32)
    sem("ad", n)
    vm("hb", (4, 16, HALF), F32)
    sem("hb", 4)
    return items


def make_kernel(n, inside, names):
    film_rows = 768 // n

    def kernel(*refs):
        r = Names(names, refs)
        d = lax.axis_index("dp")
        h = lax.axis_index("head")
        x = h // 2
        c = h - 2 * x
        z = d // 2
        y = d - 2 * z
        sib = (d, h + 1 - 2 * c)
        xdev = (d, h + 2 - 4 * x)
        v = x + c * (y - x)
        w = y + c * (x - y)
        vdev = (d + c * (1 - 2 * y), h + (1 - c) * (2 - 4 * x))
        wdev = (d + (1 - c) * (1 - 2 * y), h + c * (2 - 4 * x))

        def slot(xx, yy):
            if inside:
                return (yy + c * (xx - yy)) * 2 + xx + c * (yy - xx)
            return yy * 2 + xx

        def rc(src, dst, send, recv, dev):
            return pltpu.make_async_remote_copy(
                src_ref=src, dst_ref=dst, send_sem=send, recv_sem=recv, device_id=dev, device_id_type=MESH
            )

        def loop(count, body):
            def step(i, carry):
                body(i)
                return carry

            lax.fori_loop(0, count, step, 0)

        def each(count, body):
            for i in range(count):
                body(i)

        def rows(i, size=CHUNK, base=0):
            return pl.ds(pl.multiple_of(base + i * size, 32), size)

        def dp_start(src_of, dst, send, recv):
            def step(k, carry):
                peer = lax.rem(d + k, n)
                rc(src_of(peer), dst.at[d], send.at[k], recv.at[d], (peer, h)).start()
                return carry

            lax.fori_loop(1, n, step, 0)

        def dp_wait(src_of, dst, send, recv):
            def step(k, carry):
                peer = lax.rem(d + k, n)
                copy = rc(src_of(peer), dst.at[peer], send.at[k], recv.at[peer], (peer, h))
                copy.wait_recv()
                copy.wait_send()
                return carry

            lax.fori_loop(1, n, step, 0)

        def head_start(src_of, dst, send, recv):
            for k in range(1, 4):
                peer = lax.rem(h + k, 4)
                rc(src_of(peer), dst.at[h], send.at[k], recv.at[h], (d, peer)).start()

        def head_wait(src_of, dst, send, recv):
            for k in range(1, 4):
                peer = lax.rem(h + k, 4)
                copy = rc(src_of(peer), dst.at[peer], send.at[k], recv.at[peer], (d, peer))
                copy.wait_recv()
                copy.wait_send()

        class Halves:
            def __init__(self, name, base):
                self.buf, self.base = getattr(r, name), base
                self.send, self.recv = getattr(r, name + "_s"), getattr(r, name + "_r")

            def at(self, core, i):
                return self.buf.at[core, rows(i, CHUNK, self.base)]

            def fill(self, make):
                def body(i):
                    self.buf[c, rows(i, CHUNK, self.base), :] = make(i)
                    ref = self.at(c, i)
                    rc(ref, ref, self.send.at[i], self.recv.at[i], sib).start()

                loop(4, body)

            def wait(self):
                for i in range(4):
                    ref = self.at(1 - c, i)
                    copy = rc(ref, ref, self.send.at[i], self.recv.at[i], sib)
                    copy.wait_recv()
                    copy.wait_send()

        class Parts:
            def __init__(self, name):
                self.src, self.dst = getattr(r, name + "_src"), getattr(r, name + "_dst")
                self.send, self.recv = getattr(r, name + "_s"), getattr(r, name + "_r")

            def copy(self, i):
                at = rows(i, 2 * CHUNK)
                return rc(self.src.at[at], self.dst.at[at], self.send.at[i], self.recv.at[i], sib)

            def fill(self, make):
                def body(i):
                    self.src[rows(i, 2 * CHUNK), :] = make(i).astype(BF16)
                    self.copy(i).start()

                each(2, body)

            def get(self, i):
                copy = self.copy(i)
                copy.wait_recv()
                copy.wait_send()
                return self.dst[rows(i, 2 * CHUNK), :].astype(F32)

        class Gather:
            def __init__(self, name):
                self.g = getattr(r, name)
                self.zs, self.zr = getattr(r, name + "z_s"), getattr(r, name + "z_r")
                self.vs, self.vr = getattr(r, name + "v_s"), getattr(r, name + "v_r")
                self.ws, self.wr = getattr(r, name + "w_s"), getattr(r, name + "w_r")

            def zcopy(self, k):
                peer = (lax.rem(z + k, 4) * 2 + y, h)
                return rc(
                    self.g.at[w * 2 + v, 0], self.g.at[w * 2 + v, 4 - k], self.zs.at[k], self.zr.at[4 - k], peer
                )

            def vcopy(self, vv, i):
                ref = self.g.at[w * 2 + vv, i]
                return rc(ref, ref, self.vs.at[i], self.vr.at[i], vdev)

            def wcopy(self, ww, other, i):
                ref = self.g.at[ww * 2 + v + other * (1 - 2 * v), i]
                return rc(ref, ref, self.ws.at[2 * i + other], self.wr.at[2 * i + other], wdev)

            def own(self):
                for k in range(1, 4):
                    self.zcopy(k).start()
                self.vcopy(v, 0).start()
                self.wcopy(w, 0, 0).start()

            def pass_own(self):
                self.vcopy(1 - v, 0).wait_recv()
                self.wcopy(w, 1, 0).start()

            def pass_z(self, *ks):
                for k in ks:
                    self.zcopy(k).wait_recv()
                    self.vcopy(v, 4 - k).start()
                    self.wcopy(w, 0, 4 - k).start()

            def pass_v(self, *ks):
                for k in ks:
                    self.vcopy(1 - v, 4 - k).wait_recv()
                    self.wcopy(w, 1, 4 - k).start()

            def done(self):
                for k in range(1, 4):
                    self.zcopy(k).wait_send()
                for i in range(4):
                    self.vcopy(v, i).wait_send()
                    for other in range(2):
                        self.wcopy(1 - w, other, i).wait_recv()
                        self.wcopy(w, other, i).wait_send()

        class Reduce:
            def __init__(self, name, count):
                get = lambda tail: getattr(r, name + tail)
                self.acc, self.count = get("_acc"), count
                self.wsrc, self.wdst, self.ws, self.wr = get("w_src"), get("w_dst"), get("w_s"), get("w_r")
                self.vsrc, self.vdst, self.vs, self.vr = get("v_src"), get("v_dst"), get("v_s"), get("v_r")
                self.zsrc, self.zdst, self.zs, self.zr = get("z_src"), get("z_dst"), get("z_s"), get("z_r")

            def wcopy(self, a):
                return rc(self.wsrc.at[a], self.wdst.at[a], self.ws.at[a], self.wr.at[a], wdev)

            def vcopy(self, a, size):
                at = pl.ds(a, size)
                return rc(self.vsrc.at[at], self.vdst.at[at], self.vs.at[a], self.vr.at[a], vdev)

            def zcopy(self, a, size, k):
                at = pl.ds(a, size)
                return rc(
                    self.zsrc.at[k, at],
                    self.zdst.at[4 - k, at],
                    self.zs.at[a * 4 + k],
                    self.zr.at[a * 4 + 4 - k],
                    (lax.rem(z + k, 4) * 2 + y, h),
                )

            def start(self, a):
                def step(i, carry):
                    vv, zz = i // 4, lax.rem(i, 4)
                    self.wsrc[a, vv, zz] = self.acc[a, (1 - w) * 2 + vv, zz].astype(BF16)
                    return carry

                lax.fori_loop(0, 8, step, 0)
                self.wcopy(a).start()

            def second(self, first, size):
                for a in range(first, first + size):
                    self.wcopy(a).wait_recv()

                    def step(zz, carry):
                        self.vsrc[a, zz] = (
                            self.acc[a, w * 2 + 1 - v, zz] + self.wdst[a, 1 - v, zz].astype(F32)
                        ).astype(BF16)
                        return carry

                    lax.fori_loop(0, 4, step, 0)
                self.vcopy(first, size).start()

            def third(self, first, size):
                self.vcopy(first, size).wait_recv()
                for a in range(first, first + size):

                    def step(k, carry):
                        zz = lax.rem(z + k, 4)
                        total = (
                            self.acc[a, w * 2 + v, zz]
                            + self.wdst[a, v, zz].astype(F32)
                            + self.vdst[a, zz].astype(F32)
                        )
                        self.acc[a, w * 2 + v, zz] = total
                        self.zsrc[k, a] = total.astype(BF16)
                        return carry

                    lax.fori_loop(0, 4, step, 0)
                for k in range(1, 4):
                    self.zcopy(first, size, k).start()

            def finish(self, groups):
                for first, size in groups:
                    self.vcopy(first, size).wait_send()
                    for k in range(1, 4):
                        copy = self.zcopy(first, size, k)
                        copy.wait_recv()
                        copy.wait_send()
                for a in range(self.count):
                    self.wcopy(a).wait_send()

            def last(self, a):
                total = self.acc[a, w * 2 + v, z]
                for k in range(1, 4):
                    total = total + self.zdst[k, a].astype(F32)
                return total

        def rel(zc):
            return lax.rem(zc - z + 4, 4) if inside else zc

        class Taps:
            def __init__(self, packed, last):
                self.packed, self.last = packed, last

            def block(self, tap, zc, xx, yy):
                a, b = tap // 3, tap % 3
                if b < 2:
                    return self.packed[slot(xx, yy), rel(zc), pl.ds(a * 112 + b * 48, 48), :]
                return self.last[slot(xx, yy), rel(zc), pl.ds(a * 48, 48), :]

            def unpack(self):
                def step(i, carry):
                    q, zz = i // 4, lax.rem(i, 4)
                    for a in range(3):
                        self.last[q, zz, pl.ds(a * 48, 48), :] = last_tap(
                            self.packed[q, zz, pl.ds(a * 112, 112), :]
                        )
                    return carry

                lax.fori_loop(0, 16, step, 0)

        class Plain:
            def __init__(self, blocks):
                self.blocks = blocks

            def block(self, tap, zc, xx, yy):
                return self.blocks[slot(xx, yy), rel(zc), pl.ds(tap * 48, 48), :]

            def unpack(self):
                def step(i, carry):
                    q, zz = i // 4, lax.rem(i, 4)
                    self.blocks[q, zz] = jnp.concatenate(unpack_four(r.p3[q, zz]), axis=0)
                    return carry

                lax.fori_loop(0, 16, step, 0)

        k1, k2, k3 = Taps(r.g1, r.t1), Taps(r.g2, r.t2), Plain(r.g3)

        def wtile(g, tap, zc, xx):
            return jnp.concatenate(
                [g.block(tap, zc, xx, 0), g.block(tap, zc, xx, 1), jnp.zeros((32, 128), BF16)], axis=0
            )

        def wtap(g, tap, zcs):
            return jnp.concatenate(
                [jnp.concatenate([wtile(g, tap, zc, xx) for xx in range(2)], axis=1) for zc in zcs], axis=0
            )

        ALL = (0, 2, 1, 3)

        def half_of(core):
            return (core, core + 2)

        def wproj(zcs):
            return jnp.concatenate(
                [
                    jnp.concatenate([wtile(k3, j, zc, xx) for xx in range(2) for j in range(3)], axis=1)
                    for zc in zcs
                ],
                axis=0,
            )

        def flat(buf, base, i, size):
            return jnp.concatenate([buf[0, rows(i, size, base), :], buf[1, rows(i, size, base), :]], axis=1)

        barrier = pltpu.get_barrier_semaphore()

        def greet(k, carry):
            pl.semaphore_signal(barrier, inc=1, device_id=(lax.rem(d + k, n), h), device_id_type=MESH)
            return carry

        lax.fori_loop(1, n, greet, 0)
        for k in range(1, 4):
            pl.semaphore_signal(barrier, inc=1, device_id=(d, lax.rem(h + k, 4)), device_id_type=MESH)
        if inside:
            for a in range(3):
                r.g1[w * 2 + v, 0, pl.ds(a * 112, 112), :] = pack_taps(*[r.k1[3 * a + b] for b in range(3)])
        pl.semaphore_wait(barrier, n - 1 + 3)
        if inside:
            ga, gb, gc = Gather("g1"), Gather("g2"), Gather("p3")
            ga.own()

        def mix(m, carry):
            field = r.coef[0, m] * r.images[m].astype(F32) + r.coef[1, m] * r.noise[m].astype(F32)
            low = field.astype(BF16)
            for core in range(2):
                r.mx_src[m * 2 + core] = pack_pixels(dot(low, r.sel[core])).astype(BF16)
            return carry

        lax.fori_loop(0, 2, mix, 0)
        head_start(lambda p: r.mx_src.at[p], r.mx_dst, r.mx_s, r.mx_r)
        r.mx_dst[h] = r.mx_src[h]
        if inside:
            ga.pass_own()

        r.el[d] = silu(r.emb[...].astype(F32)).astype(BF16).astype(F32)
        dp_start(lambda p: r.el.at[d], r.el, r.el_s, r.el_r)

        if inside:
            blocks = dot(r.wa[...], r.selp[: 3 * BLK, : 3 * 128]).astype(BF16)
            r.sw_src[...] = blocks[:, 128:256]
            swap = rc(r.sw_src, r.sw_dst, r.sw_s.at[0], r.sw_r.at[0], sib)
            swap.start()
            for a in range(3):
                r.g2[w * 2 + v, 0, pl.ds(a * 112, 112), :] = pack_taps(*[r.k2[3 * a + b] for b in range(3)])
        r.par[0:3, :] = r.gains[...]
        r.par[3:13, :] = r.biases[...]
        r.par[13:16, :] = jnp.zeros((3, 384), F32)
        r.parown[...] = exact_dot(r.par[...], r.sel[c])

        def prow(i):
            return r.parown[pl.ds(i, 1), :]

        for buf in (r.act1, r.act2):
            for core in range(2):
                buf[core, pl.ds(0, ROW), :] = jnp.zeros((ROW, HALF), BF16)
                buf[core, pl.ds(PX + ROW, ROW), :] = jnp.zeros((ROW, HALF), BF16)
        for buf in (r.gr1, r.gr2):
            for b in range(3):
                buf[b, pl.ds(0, ROW), :] = jnp.zeros((ROW, HALF), BF16)
                buf[b, pl.ds(PX + ROW, ROW), :] = jnp.zeros((ROW, HALF), BF16)
        r.wfp[...] = jnp.zeros((128, HALF), BF16)
        r.wfp[pl.ds(0, film_rows), :] = dot(r.wf[...], r.selp[: 2 * BLK, :HALF]).astype(BF16)
        if inside:
            ga.pass_z(1, 3, 2)
            gb.own()

        count = float(PX * 12)

        def fold(vals):
            return jnp.sum(vals.reshape(CHUNK // 8, 8, HALF), axis=0)

        def sums_of(fn, k):
            def step(i, carry):
                return tuple(a + fold(b) for a, b in zip(carry, fn(i)))

            zero = jnp.zeros((8, HALF), F32)
            return lax.fori_loop(0, 4, step, (zero,) * k)

        def group_mean(part):
            return jnp.sum(exact_dot(part, r.gmask[...]), axis=0, keepdims=True) / count

        def norm(load, which, total):
            mean = group_mean(total)
            (square,) = sums_of(lambda i: (jnp.square(load(i) - mean),), 1)
            inv = lax.rsqrt(group_mean(square) + EPS)
            r.stat[pl.ds(2 * which, 1), :] = mean
            r.stat[pl.ds(2 * which + 1, 1), :] = inv
            return mean, inv

        zero8 = jnp.zeros((8, HALF), F32)

        def norm_back(sums, load_grad, load_hat, coef, inv):
            plain, cross = sums
            means = exact_dot(jnp.concatenate([coef * plain, coef * cross], axis=0), r.gmask[...])
            plain_mean = jnp.sum(means[:8], axis=0, keepdims=True) / count
            cross_mean = jnp.sum(means[8:], axis=0, keepdims=True) / count
            outer, base, slope = inv * coef, inv * plain_mean, inv * cross_mean

            def chunk(i):
                return outer * load_grad(i) - base - load_hat(i) * slope

            return (
                jnp.sum(plain, axis=0, keepdims=True),
                jnp.sum(cross, axis=0, keepdims=True),
                chunk,
            )

        def transposed(name, core):
            ref = getattr(r, name).at[core]
            return rc(ref, ref, getattr(r, name + "_s").at[0], getattr(r, name + "_r").at[0], sib)

        def transpose_act(buf, base, name):
            out = getattr(r, name)
            for q in range(4):
                out[c, :, pl.ds(q * CHUNK, CHUNK)] = jnp.transpose(buf[c, pl.ds(base + q * CHUNK, CHUNK), :])
            transposed(name, c).start()

        def transposed_wait(name):
            copy = transposed(name, 1 - c)
            copy.wait_recv()
            copy.wait_send()

        head_wait(lambda p: r.mx_src.at[p], r.mx_dst, r.mx_s, r.mx_r)

        def unpack_mixed(i, carry):
            vals = unpack_pixels(r.mx_dst[i])
            r.mx[i] = vals
            return carry + fold(vals.astype(F32))

        mixed_sum = lax.fori_loop(0, 4, unpack_mixed, zero8)

        def mixed(i):
            return r.mx[i].astype(F32)

        if inside:
            ga.pass_v(1, 3)
        mean1, inv1 = norm(mixed, 0, mixed_sum)
        if inside:
            ga.pass_v(2)
        gain1, shift1 = prow(0), prow(3)
        act1 = Halves("act1", ROW)

        def affine(mean, inv, gain, shift):
            return inv * gain, shift - mean * (inv * gain)

        mul1, add1 = affine(mean1, inv1, gain1, shift1)

        def pre1(i):
            return mixed(i) * mul1 + add1

        act1.fill(lambda i: silu(pre1(i)).astype(BF16))
        dp_wait(lambda p: r.el.at[d], r.el, r.el_s, r.el_r)
        for j in range(n):
            r.em[pl.ds(2 * j, 2), :] = r.el[j]
        place = lax.broadcasted_iota(jnp.int32, (768, 128), 0) - film_rows * d
        lane = lax.broadcasted_iota(jnp.int32, (768, 128), 1)
        pick = jnp.where((place == lane) & (lane < film_rows), 1.0, 0.0).astype(BF16)
        r.esel[...] = dot(r.em[...].astype(BF16), pick)
        film_part = dot(r.esel[...].astype(BF16), r.wfp[...])
        for j in range(n):
            r.fp[j] = film_part[2 * j : 2 * j + 2]
        dp_start(lambda p: r.fp.at[p], r.fr, r.fr_s, r.fr_r)
        r.fr[d] = r.fp[d]
        if inside:
            swap.wait()
            got = r.sw_dst[...]
            keep0, keep2 = blocks[:, :128], blocks[:, 256:]
            r.p3[w * 2 + v, 0] = pack_four(
                jnp.where(c == 0, keep0, got),
                jnp.where(c == 0, keep2, keep0),
                jnp.where(c == 0, got, keep2),
                r.wo[...],
            )
        act1.wait()
        transpose_act(r.act1, ROW, "act1_t")
        if inside:
            gb.pass_own()
            gb.pass_z(1, 3, 2)
            gc.own()
        def split_cot(m, carry):
            for core in range(2):
                r.cx_src[m * 2 + core] = pack_pixels(dot(r.cot[m], r.sel[core])).astype(BF16)
            return carry

        lax.fori_loop(0, 2, split_cot, 0)
        column = lax.broadcasted_iota(jnp.int32, (1, ROW, HALF), 1)
        not_first = jnp.where(column > 0, 1.0, 0.0)
        not_last = jnp.where(column < ROW - 1, 1.0, 0.0)

        def in_rows(vals, mask):
            return (vals.reshape(CHUNK // ROW, ROW, HALF) * mask).reshape(CHUNK, HALF)

        def from_left(vals):
            return in_rows(pltpu.roll(vals, 1, 0), not_first)

        def from_right(vals):
            return in_rows(pltpu.roll(vals, CHUNK - 1, 0), not_last)

        def conv(buf, g, store, between):
            weights = lambda: jnp.concatenate(
                [jnp.concatenate([wtap(g, 3 * a + b, ALL) for b in range(3)], axis=1) for a in range(3)], axis=0
            )

            total = zero8
            for i in range(2):
                left = jnp.concatenate([flat(buf, ROW * a, i, 2 * CHUNK) for a in range(3)], axis=1)
                out = dot(left, weights())
                for j in range(2):
                    part = out[j * CHUNK : j * CHUNK + CHUNK]
                    part = part[:, HALF : 2 * HALF] + from_left(part[:, :HALF]) + from_right(part[:, 2 * HALF :])
                    total = total + fold(store(2 * i + j, part))
                if i == 0:
                    between()
            return total

        if inside:
            ga.done()
            k1.unpack()

        dp_wait(lambda p: r.fp.at[p], r.fr, r.fr_s, r.fr_r)
        film_sum = r.fr[0]
        for j in range(1, n):
            film_sum = film_sum + r.fr[j]
        for m in range(2):
            for core in range(2):
                r.fx[m * 2 + core] = film_sum[m : m + 1, core * 128 : core * 128 + 128]
        head_start(lambda p: r.fx.at[p], r.fh, r.fh_s, r.fh_r)
        r.fh[h] = r.fx[h]

        def store_v2(i, vals):
            vals = vals + prow(6)
            r.v2[rows(i), :] = vals
            return vals

        v2_sum = conv(r.act1, k1, store_v2, (lambda: gb.pass_v(1, 3, 2)) if inside else lambda: None)
        head_wait(lambda p: r.fx.at[p], r.fh, r.fh_s, r.fh_r)
        scale = 1.0 + (jnp.concatenate([r.fh[0], r.fh[1]], axis=1) + prow(8))
        shift = jnp.concatenate([r.fh[2], r.fh[3]], axis=1) + prow(9)
        head_start(lambda p: r.cx_src.at[p], r.cx_dst, r.cx_s, r.cx_r)
        r.cx_dst[h] = r.cx_src[h]
        mean2, inv2 = norm(lambda i: r.v2[rows(i), :], 1, v2_sum)
        gain2, shift2 = prow(1), prow(4)
        act2 = Halves("act2", ROW)

        def hat2(i):
            return (r.v2[rows(i), :] - mean2) * inv2

        mul2, add2 = affine(mean2, inv2, gain2 * scale, shift2 * scale + shift)

        def pre2(i):
            return r.v2[rows(i), :] * mul2 + add2

        act2.fill(lambda i: silu(pre2(i)).astype(BF16))
        if inside:
            gc.pass_own()
            gc.pass_z(1, 3, 2)

        transpose_act(r.act2, ROW, "act2_t")
        act2.wait()
        if inside:
            gb.done()
            k2.unpack()

        def store_v3(i, vals):
            vals = mixed(i) + (vals + prow(7))
            r.v3[rows(i), :] = vals
            return vals

        v3_sum = conv(r.act2, k2, store_v3, (lambda: gc.pass_v(1, 3, 2)) if inside else lambda: None)
        mean3, inv3 = norm(lambda i: r.v3[rows(i), :], 2, v3_sum)
        gain3, shift3 = prow(2), prow(5)
        ai = Halves("ai", 0)

        def hat3(i):
            return (r.v3[rows(i), :] - mean3) * inv3

        mul3, add3 = affine(mean3, inv3, gain3, shift3)
        ai.fill(lambda i: (r.v3[rows(i), :] * mul3 + add3).astype(BF16))
        transpose_act(r.ai, 0, "ai_t")

        if inside:
            gc.done()
            k3.unpack()
        head_wait(lambda p: r.cx_src.at[p], r.cx_dst, r.cx_s, r.cx_r)

        def unpack_cot(i):
            r.cx[i] = unpack_pixels(r.cx_dst[i])

        loop(4, unpack_cot)
        dop = Parts("do")

        def cot_rows(i):
            return jnp.concatenate([r.cx[2 * i], r.cx[2 * i + 1]], axis=0)

        dop.fill(lambda i: dot_nt(cot_rows(i), wtap(k3, 3, half_of(1 - c))))

        ai.wait()
        bias_proj = [prow(10)[:, :128], prow(10)[:, 128:], None, None, prow(11)[:, :128], prow(11)[:, 128:]]

        def project(i):
            out = dot(flat(r.ai, 0, i, 2 * CHUNK), wproj(ALL))
            for k in range(6):
                part = out[:, k * 128 : k * 128 + 128]
                if bias_proj[k] is not None:
                    part = part + bias_proj[k]
                r.qkv[k, rows(i, 2 * CHUNK), :] = part.astype(BF16)

        each(2, project)

        def do_own(i):
            full = (dot_nt(cot_rows(i), wtap(k3, 3, half_of(c))) + dop.get(i)).astype(BF16)
            for k in range(2):
                r.dout[k, rows(i, 2 * CHUNK), :] = full[:, k * 128 : k * 128 + 128]

        each(2, do_own)

        factor = 1.0 / math.sqrt(HEAD_DIM)
        factor2 = factor * math.log2(math.e)
        att = []

        def transposes(k):
            r.kvt[k] = jnp.transpose(r.qkv[k + 2])

        loop(4, transposes)

        def att_copy(core, k):
            ref = r.att.at[core * 2 + k]
            return rc(ref, ref, r.att_s.at[k], r.att_r.at[k], sib)

        def att_t_copy(core, k):
            ref = r.att_t.at[core, pl.ds(pl.multiple_of(k * 128, 128), 128)]
            return rc(ref, ref, r.att_s.at[2 + k], r.att_r.at[2 + k], sib)

        def one_head(k):
            lows, grads = [], []
            for b in range(2):
                at = pl.ds(b * 2 * CHUNK, 2 * CHUNK)
                query = r.qkv[k, at, :]
                grad = r.dout[k, at, :]
                scores = dot_nt(r.qkv[2 + k], query)
                peak = jnp.max(scores, axis=0, keepdims=True)
                expo = jnp.exp2((scores - peak) * factor2)
                inverse = 1.0 / jnp.sum(expo, axis=0, keepdims=True)
                low = (expo * inverse).astype(BF16)
                got = dot(r.kvt[2 + k], low)
                got_low = got.astype(BF16)
                r.att_t[c, pl.ds(pl.multiple_of(k * 128, 128), 128), at] = got_low
                r.att[2 * c + k, at, :] = jnp.transpose(got_low)
                spread = jnp.sum(got * jnp.transpose(grad).astype(F32), axis=0, keepdims=True)
                probs_grad = dot_nt(r.qkv[4 + k], grad)
                scores_grad = ((probs_grad - spread) * inverse * expo).astype(BF16)
                back = dot(r.kvt[k], scores_grad)
                r.dproj[k, at, :] = (jnp.transpose(back) * factor).astype(BF16)
                lows.append(low)
                grads.append(scores_grad)
            att_copy(c, k).start()
            att_t_copy(c, k).start()
            r.dproj[4 + k] = dot(jnp.concatenate(lows, axis=1), r.dout[k]).astype(BF16)
            r.dproj[2 + k] = (dot(jnp.concatenate(grads, axis=1), r.qkv[k]) * factor).astype(BF16)

        loop(2, one_head)

        n3 = Parts("n3")

        def proj_rows(i):
            return jnp.concatenate([r.dproj[k, rows(i, 2 * CHUNK), :] for k in range(6)], axis=1)

        n3.fill(lambda i: dot_nt(proj_rows(i), wproj(half_of(1 - c))))

        for k in range(2):
            copy = att_copy(1 - c, k)
            copy.wait_recv()
            copy.wait_send()

        def result(i):
            left = jnp.concatenate([r.att[p, rows(i), :] for p in range(4)], axis=1)
            branch = dot(left, wtap(k3, 3, ALL)) + prow(12)
            r.ro_src[i] = pack_pixels(r.v3[rows(i), :] + branch).astype(BF16)

        loop(4, result)
        head_start(lambda p: r.ro_src.at[p], r.ro_dst, r.ro_s, r.ro_r)
        r.ro_dst[h] = r.ro_src[h]

        if inside:
            red1, red2, red3 = Reduce("r1", 3), Reduce("r2", 3), Reduce("r3", 1)
            acc1, acc2, acc3 = r.r1_acc, r.r2_acc, r.r3_acc
        else:
            acc1, acc2, acc3 = r.first, r.second, r.attend

        transposed_wait("ai_t")
        for k in range(2):
            copy = att_t_copy(1 - c, k)
            copy.wait_recv()
            copy.wait_send()
        right = jnp.concatenate([r.dproj[k] for k in range(6)], axis=1)
        cot_all = jnp.concatenate([r.cx[i] for i in range(4)], axis=0)
        for core in range(2):
            attend_out = dot(r.ai_t[core], right)
            output_out = dot(r.att_t[core], cot_all)
            for k in range(2):
                for yy in range(2):
                    for xx in range(2):
                        row = k * 128 + yy * 48
                        tiles = [
                            attend_out[row : row + 48, (xx * 3 + j) * 128 : (xx * 3 + j) * 128 + 128] for j in range(3)
                        ]
                        acc3[0, slot(xx, yy), core + 2 * k] = pack_four(
                            *tiles, output_out[row : row + 48, xx * 128 : xx * 128 + 128]
                        )
        if inside:
            red3.start(0)

        def proj_sums(i, carry):
            q = jnp.concatenate([r.dproj[0, rows(i), :], r.dproj[1, rows(i), :]], axis=1).astype(F32)
            val = jnp.concatenate([r.dproj[4, rows(i), :], r.dproj[5, rows(i), :]], axis=1).astype(F32)
            return (carry[0] + fold(q), carry[1] + fold(val), carry[2] + fold(r.cx[i].astype(F32)))

        qsum, vsum, csum = lax.fori_loop(0, 4, proj_sums, (zero8, zero8, zero8))
        r.sums[pl.ds(3 + 7, 1), :] = jnp.sum(qsum, axis=0, keepdims=True)
        r.sums[pl.ds(3 + 8, 1), :] = jnp.sum(vsum, axis=0, keepdims=True)
        r.sums[pl.ds(3 + 9, 1), :] = jnp.sum(csum, axis=0, keepdims=True)
        r.sums[pl.ds(13, 3), :] = jnp.zeros((3, HALF), F32)

        def n3_own(i, carry):
            both = dot_nt(proj_rows(i), wproj(half_of(c))) + n3.get(i)
            for j in range(2):
                vals = both[j * CHUNK : j * CHUNK + CHUNK]
                r.gtmp[rows(2 * i + j), :] = vals
                carry = carry[0] + fold(vals), carry[1] + fold(vals * hat3(2 * i + j))
            return carry

        sums3 = n3_own(1, n3_own(0, (zero8, zero8)))
        plain3, cross3, back3 = norm_back(sums3, lambda i: r.gtmp[rows(i), :], hat3, gain3, inv3)
        r.sums[pl.ds(2, 1), :] = cross3
        r.sums[pl.ds(3 + 2, 1), :] = plain3

        def shifted(buf, i, vals):
            buf[0, rows(i, CHUNK, ROW), :] = from_right(vals).astype(BF16)
            buf[1, rows(i, CHUNK, ROW), :] = vals.astype(BF16)
            buf[2, rows(i, CHUNK, ROW), :] = from_left(vals).astype(BF16)

        def residual_back(i, carry):
            vals = r.cx[i].astype(F32) + back3(i)
            r.gres[rows(i), :] = vals
            shifted(r.gr2, i, vals)
            return carry + fold(vals.astype(BF16).astype(F32))

        bias_two = lax.fori_loop(0, 4, residual_back, jnp.zeros((8, HALF), F32))
        r.sums[pl.ds(3 + 4, 1), :] = jnp.sum(bias_two, axis=0, keepdims=True)

        def act_back(buf, g, core, i, size):
            left = jnp.concatenate(
                [buf[b, rows(i, size, 2 * ROW - ROW * a), :] for a in range(3) for b in range(3)], axis=1
            )
            right = jnp.concatenate(
                [wtap(g, 3 * a + b, half_of(core)) for a in range(3) for b in range(3)], axis=1
            )
            return dot_nt(left, right)

        def conv_back(parts, buf, g):
            parts.fill(lambda i: act_back(buf, g, 1 - c, i, 2 * CHUNK))

        def conv_back_own(parts, buf, g, outer, hat):
            def own(i, carry):
                vals = act_back(buf, g, c, i, 2 * CHUNK) + parts.get(i)
                for j in range(2):
                    at = 2 * i + j
                    grad = vals[j * CHUNK : j * CHUNK + CHUNK] * outer(at)
                    r.gtmp[rows(at), :] = grad
                    carry = carry[0] + fold(grad), carry[1] + fold(grad * hat(at))
                return carry

            return own(1, own(0, (zero8, zero8)))

        def kernel_grad(act_t, buf, acc, after):
            def step(a):
                right = jnp.concatenate([buf[b, pl.ds(2 * ROW - ROW * a, PX), :] for b in range(3)], axis=1)
                out = dot(jnp.concatenate([act_t[0], act_t[1]], axis=0), right)
                for p, zc in enumerate(ALL):
                    for yy in range(2):
                        for xx in range(2):
                            row = p * 128 + yy * 48
                            tiles = [
                                out[row : row + 48, b * HALF + xx * 128 : b * HALF + xx * 128 + 128] for b in range(3)
                            ]
                            acc[a, slot(xx, yy), zc] = pack_taps(*tiles)
                after(a)

            each(3, step)

        serve = inside
        d2 = Parts("d2")
        transposed_wait("act2_t")
        kernel_grad(r.act2_t, r.gr2, acc2, red2.start if inside else lambda a: None)
        if serve:
            red3.second(0, 1)
        conv_back(d2, r.gr2, k2)
        if serve:
            red2.second(0, 1)
        sums2 = conv_back_own(d2, r.gr2, k2, lambda i: silu_slope(pre2(i)), hat2)
        if serve:
            red2.second(1, 1)
            red3.third(0, 1)

        plain2, cross2, back2 = norm_back(sums2, lambda i: r.gtmp[rows(i), :], hat2, gain2 * scale, inv2)
        r.sums[pl.ds(1, 1), :] = scale * cross2
        r.sums[pl.ds(3 + 1, 1), :] = scale * plain2
        film_scale_term = gain2 * cross2 + shift2 * plain2
        r.sums[pl.ds(3 + 5, 1), :] = film_scale_term
        r.sums[pl.ds(3 + 6, 1), :] = plain2
        for j in range(2):
            r.ft[j] = film_scale_term[:, j * 128 : j * 128 + 128]
            r.ft[2 + j] = plain2[:, j * 128 : j * 128 + 128]
        head_start(lambda p: r.ft.at[p], r.th, r.th_s, r.th_r)
        r.th[h] = r.ft[h]

        def first_back(i, carry):
            vals = back2(i)
            shifted(r.gr1, i, vals)
            return carry + fold(vals.astype(BF16).astype(F32))

        bias_one = lax.fori_loop(0, 4, first_back, jnp.zeros((8, HALF), F32))
        r.sums[pl.ds(3 + 3, 1), :] = jnp.sum(bias_one, axis=0, keepdims=True)

        if serve:
            red2.second(2, 1)
            red2.third(0, 1)
            red2.third(1, 1)

        head_wait(lambda p: r.ft.at[p], r.th, r.th_s, r.th_r)
        for m in range(2):
            r.fa[d, pl.ds(m, 1), :] = jnp.concatenate([r.th[2 * m], r.th[2 * m + 1]], axis=1)
        dp_start(lambda p: r.fa.at[d], r.fa, r.fa_s, r.fa_r)

        d1 = Parts("d1")

        def after_chunk(a):
            if serve:
                red1.start(a)
                if a == 1:
                    red2.third(2, 1)

        transposed_wait("act1_t")
        kernel_grad(r.act1_t, r.gr1, acc1, after_chunk)
        conv_back(d1, r.gr1, k1)
        if serve:
            red1.second(0, 1)

        dp_wait(lambda p: r.fa.at[d], r.fa, r.fa_s, r.fa_r)
        for j in range(n):
            r.fta[pl.ds(2 * j, 2), :] = r.fa[j]
        film_block = dot_tn_high(r.esel[...], r.fta[...])
        r.film[...] = jnp.concatenate([film_block[:film_rows, :BLK], film_block[:film_rows, 128 : 128 + BLK]], axis=1)
        embed_part = dot_nt_high(r.fta[...], r.wfp[...].astype(F32))
        for j in range(n):
            r.ep[j] = embed_part[2 * j : 2 * j + 2]
        dp_start(lambda p: r.ep.at[p], r.er, r.er_s, r.er_r)
        r.er[d] = r.ep[d]

        def hat1(i):
            return (mixed(i) - mean1) * inv1

        sums1 = conv_back_own(d1, r.gr1, k1, lambda i: silu_slope(pre1(i)), hat1)
        if serve:
            red1.second(1, 1)

        dp_wait(lambda p: r.ep.at[p], r.er, r.er_s, r.er_r)
        r.eh[h] = r.er[...]
        head_start(lambda p: r.eh.at[h], r.eh, r.eh_s, r.eh_r)
        plain1, cross1, back1 = norm_back(sums1, lambda i: r.gtmp[rows(i), :], hat1, gain1, inv1)
        r.sums[pl.ds(0, 1), :] = cross1
        r.sums[pl.ds(3, 1), :] = plain1
        r.ad[d] = r.sums[...]
        dp_start(lambda p: r.ad.at[d], r.ad, r.ad_s, r.ad_r)

        if serve:
            red1.second(2, 1)
            red1.third(0, 1)
        keep = r.coef[0, x]

        def image_back(i):
            r.io_src[i] = pack_pixels(keep * (r.gres[rows(i), :] + back1(i))).astype(BF16)

        loop(4, image_back)
        head_start(lambda p: r.io_src.at[p], r.io_dst, r.io_s, r.io_r)
        r.io_dst[h] = r.io_src[h]
        if serve:
            red1.third(1, 1)
            red1.third(2, 1)

        dp_wait(lambda p: r.ad.at[d], r.ad, r.ad_s, r.ad_r)
        total = r.ad[0]
        for j in range(1, n):
            total = total + r.ad[j]
        r.hb[h] = total
        head_start(lambda p: r.hb.at[h], r.hb, r.hb_s, r.hb_r)
        head_wait(lambda p: r.ro_src.at[p], r.ro_dst, r.ro_s, r.ro_r)

        if inside:
            red2.finish(((0, 1), (1, 1), (2, 1)))
            for a in range(3):
                r.second[a] = red2.last(a)

        head_wait(lambda p: r.hb.at[h], r.hb, r.hb_s, r.hb_r)
        even = r.hb[0] + r.hb[2]
        odd = r.hb[1] + r.hb[3]
        wide = jnp.concatenate(
            [even[:, :BLK], odd[:, :BLK], even[:, 128 : 128 + BLK], odd[:, 128 : 128 + BLK]], axis=1
        )
        r.gains_out[...] = wide[0:3]
        r.biases_out[...] = wide[3:13]

        head_wait(lambda p: r.eh.at[h], r.eh, r.eh_s, r.eh_r)
        pieces = []
        for j in range(n):
            piece = (r.eh[0, j] + r.eh[1, j]) + (r.eh[2, j] + r.eh[3, j])
            pieces.append(piece[:, :film_rows])
        r.embed_grad[...] = jnp.concatenate(pieces, axis=1) * silu_slope(r.emb[...].astype(F32))

        head_wait(lambda p: r.io_src.at[p], r.io_dst, r.io_s, r.io_r)

        if inside:
            red3.finish(((0, 1),))
            tiles = unpack_four(red3.last(0))
            r.sb_src[...] = jnp.where(c == 0, tiles[2], tiles[0])
            back = rc(r.sb_src, r.sb_dst, r.sb_s.at[0], r.sb_r.at[0], sib)
            back.start()
            r.output[...] = tiles[3]
            red1.finish(((0, 1), (1, 1), (2, 1)))
            for a in range(3):
                r.first[a] = red1.last(a)
            back.wait()
            r.attend[:, 0:128] = jnp.where(c == 0, tiles[0], tiles[1])
            r.attend[:, 128:256] = r.sb_dst[...]
            r.attend[:, 256:384] = jnp.where(c == 0, tiles[1], tiles[2])

    return kernel


def make_writer(names_in, names_out):
    def kernel(*refs):
        count = len(names_in)
        src, dst = Names(names_in, refs[:count]), Names(names_out, refs[count:])
        for name, packed in (("result", src.ro_dst), ("image_grad", src.io_dst)):
            for m in range(2):
                getattr(dst, name)[m] = dot_nt(unpack_pixels(packed[2 * m]), src.sel[0]) + dot_nt(
                    unpack_pixels(packed[2 * m + 1]), src.sel[1]
                )
        for name in ("first", "second"):
            if name in names_out:
                for a in range(3):
                    block = getattr(src, name)[a]
                    getattr(dst, name)[3 * a] = block[:48, :BLK]
                    getattr(dst, name)[3 * a + 1] = block[48:96, :BLK]
                    getattr(dst, name)[3 * a + 2] = last_tap(block)[:, :BLK]
        if "attend" in names_out:
            dst.attend[...] = jnp.concatenate([src.attend[:, j * 128 : j * 128 + BLK] for j in range(3)], axis=1)
            dst.output[...] = src.output[:, :BLK]
        for name in ("embed_grad", "film", "gains_out", "biases_out"):
            getattr(dst, name)[...] = getattr(src, name)[...]

    return kernel


def per_device(n, *args):
    (
        images,
        noise_field,
        time_steps,
        embedding,
        first_kernel,
        second_kernel,
        film_weight,
        attend_weight,
        output_weight,
        norm_gains,
        biases,
        cotangent,
    ) = args
    inside = n == 8
    keep, noise = plan(time_steps)
    coef = jnp.stack([keep, noise])
    maps, height, width, channels = images.shape
    flat_shape = (maps, height * width, channels)
    film_rows = film_weight.shape[0]
    inputs = dict(
        coef=coef,
        images=images.reshape(flat_shape),
        noise=noise_field.reshape(flat_shape),
        cot=cotangent.reshape(flat_shape),
        emb=embedding,
        k1=first_kernel.reshape((9,) + first_kernel.shape[2:]),
        k2=second_kernel.reshape((9,) + second_kernel.shape[2:]),
        wf=film_weight,
        wa=attend_weight,
        wo=output_weight,
        gains=norm_gains,
        biases=biases,
        sel=jnp.asarray(channel_lanes(), BF16),
        gmask=jnp.asarray(group_mask(), BF16),
        selp=jnp.asarray(block_lanes(3), BF16),
    )
    shapes = dict(
        ro_dst=(4, 384, 128),
        io_dst=(4, 384, 128),
        embed_grad=embedding.shape,
        first=(3, 112, 128),
        second=(3, 112, 128),
        film=film_weight.shape,
        attend=(48, 384),
        output=(48, 128),
        gains_out=norm_gains.shape,
        biases_out=biases.shape,
    )
    names_in, names_out = list(INPUTS), list(OUTPUTS)
    core = lax.axis_index("head") % 2
    if not inside:
        def whole(array, row_axis):
            array = lax.all_gather(array, "dp", axis=row_axis, tiled=True)
            return lax.all_gather(array, "head", axis=array.ndim - 1, tiled=True)

        def spread(array, count):
            taps = array.shape[0]
            array = array.reshape(taps, 4, 2, 48, 2, 2, BLK)
            array = lax.dynamic_index_in_dim(array, core, 5, keepdims=False)
            array = jnp.transpose(array, (2, 4, 1, 0, 3, 5))
            array = jnp.pad(array, ((0, 0),) * 5 + ((0, 32),))
            return array.reshape(4, 4, taps * 48, 128)

        full_a = whole(attend_weight, 0).reshape(384, 2, 3, 2, BLK)
        full_a = jnp.transpose(full_a, (2, 0, 1, 3, 4)).reshape(3, 384, 384)
        full_o = whole(output_weight, 0)[None]
        for name, last, array in (("g1", "t1", first_kernel), ("g2", "t2", second_kernel)):
            blocks = spread(whole(array, 2).reshape(9, 384, 384), 9).reshape(4, 4, 3, 3, 48, 128)
            two = blocks[:, :, :, :2].reshape(4, 4, 3, 96, 128)
            inputs[name] = jnp.pad(two, ((0, 0),) * 3 + ((0, 16), (0, 0))).reshape(4, 4, 336, 128)
            inputs[last] = blocks[:, :, :, 2].reshape(4, 4, 144, 128)
        inputs["g3"] = spread(jnp.concatenate([full_a, full_o], axis=0), 4)
        names_in += ["g1", "g2", "t1", "t2", "g3"]
        shapes["first"] = shapes["second"] = (3, 4, 4, 112, 128)
        shapes["attend"] = (1, 4, 4, 144, 128)
        del shapes["output"]
        names_out.remove("output")
    items = scratch_list(n, inside)
    smem = pl.BlockSpec(memory_space=pltpu.SMEM)
    vmem = pl.BlockSpec(memory_space=pltpu.VMEM)
    outs = pl.pallas_call(
        make_kernel(n, inside, names_in + names_out + [name for name, _ in items]),
        out_shape=[
            jax.ShapeDtypeStruct(shapes[name], BF16 if name in ("ro_dst", "io_dst") else F32) for name in names_out
        ],
        in_specs=[smem if name == "coef" else vmem for name in names_in],
        out_specs=[vmem] * len(names_out),
        scratch_shapes=[item for _, item in items],
        compiler_params=pltpu.CompilerParams(
            collective_id=0, has_side_effects=True, vmem_limit_bytes=63 * 1024 * 1024
        ),
        name="blocks",
    )(*[inputs[name] for name in names_in])
    raw = dict(zip(names_out, outs))
    final = dict(
        result=flat_shape,
        image_grad=flat_shape,
        embed_grad=embedding.shape,
        film=film_weight.shape,
        gains_out=norm_gains.shape,
        biases_out=biases.shape,
    )
    if inside:
        final.update(first=(9, 48, BLK), second=(9, 48, BLK), attend=attend_weight.shape, output=output_weight.shape)
    names_last = [name for name in names_out if inside or name not in ("first", "second", "attend")] + ["sel"]
    names_final = list(final)
    outs = pl.pallas_call(
        make_writer(names_last, names_final),
        out_shape=[jax.ShapeDtypeStruct(final[name], F32) for name in names_final],
        in_specs=[vmem] * len(names_last),
        out_specs=[vmem] * len(names_final),
        compiler_params=pltpu.CompilerParams(vmem_limit_bytes=63 * 1024 * 1024),
        name="outputs",
    )(*[inputs["sel"] if name == "sel" else raw[name] for name in names_last])
    out = dict(zip(names_final, outs))
    if not inside:

        def blocks_of(array, size):
            parts = [array[..., k * 48 : k * 48 + 48, :BLK] for k in range(size)]
            if size == 2:
                lanes = [array[..., k * 32 : k * 32 + 32, BLK:] for k in range(3)]
                lanes = jnp.concatenate(lanes, axis=-1)
                parts.append(jnp.concatenate([lanes, array[..., 96:112, :BLK]], axis=-2))
            else:
                lanes = [array[..., k * 48 : k * 48 + 48, BLK:] for k in range(3)]
                parts.append(jnp.concatenate(lanes, axis=-1))
            array = jnp.stack(parts, axis=1)
            array = array.reshape(array.shape[:2] + (2, 2, 4, 48, BLK))
            taps = array.shape[0] * array.shape[1]
            array = jnp.transpose(array, (0, 1, 4, 2, 5, 3, 6)).reshape(taps, 384, 2, 1, BLK)
            both = jnp.concatenate([array, jnp.zeros_like(array)], axis=3)
            return jnp.where(core == 0, both, both[:, :, :, ::-1]).reshape(taps, 384, 384)

        def shared(array, axis):
            array = lax.psum_scatter(array, "head", scatter_dimension=array.ndim - 1, tiled=True)
            return lax.psum_scatter(array, "dp", scatter_dimension=axis, tiled=True)

        out["first"] = shared(blocks_of(raw["first"], 2), 1)
        out["second"] = shared(blocks_of(raw["second"], 2), 1)
        both = blocks_of(raw["attend"], 3)
        joined = both[:3].reshape(3, 384, 2, 2, BLK)
        joined = jnp.transpose(joined, (1, 2, 0, 3, 4)).reshape(384, 1152)
        out["attend"] = shared(joined, 0)
        out["output"] = shared(both[3], 0)
    return (
        out["result"].reshape(images.shape),
        out["image_grad"].reshape(images.shape),
        out["embed_grad"],
        out["first"].reshape(first_kernel.shape),
        out["second"].reshape(second_kernel.shape),
        out["film"],
        out["attend"],
        out["output"],
        out["gains_out"],
        out["biases_out"],
    )


def solution(mesh):
    n = mesh.shape["dp"]
    field = P("dp", "head", None, None)
    taps = P(None, None, "dp", "head")
    both = P("dp", "head")
    return jax.shard_map(
        lambda *args: per_device(n, *args),
        mesh=mesh,
        in_specs=(field, field, P("dp"), P("dp", None), taps, taps, both, both, both, P(), P(), field),
        out_specs=(field, field, P("dp", None), taps, taps, both, both, both, P(), P()),
        check_vma=False,
    )
```

```python
import math

import jax
import jax.numpy as jnp
import numpy as np
from jax import lax
from jax.experimental import pallas as pl
from jax.experimental.pallas import tpu as pltpu
from jax.sharding import PartitionSpec as P

HEAD_DIM = 96
GROUPS = 32
STEPS = 4000
EPS = 1e-05
OFFSET = 0.008
MESH = pl.DeviceIdType.MESH
F32 = jnp.float32
BF16 = jnp.bfloat16

PX = 1024
ROW = 32
CHUNK = 256
BLK = 96
HALF = 256
NHEAD = 4


def plan(time_step, lanes):
    fraction = (jnp.full((1, lanes), time_step, jnp.int32).astype(F32) + 1.0) / STEPS
    start = math.cos(OFFSET / (1.0 + OFFSET) * (math.pi / 2)) ** 2
    curve = jnp.square(jnp.cos((fraction + OFFSET) / (1.0 + OFFSET) * (math.pi / 2))) / start
    return (jnp.sqrt(curve), jnp.sqrt(jnp.maximum(1.0 - curve, 0.0)))


def channel_lanes():
    sel = np.zeros((2, 384, HALF), np.float32)
    for block in range(4):
        for j in range(BLK):
            sel[block % 2, block * BLK + j, (block // 2) * 128 + j] = 1.0
    return sel


def block_lanes(count):
    sel = np.zeros((count * BLK, count * 128), np.float32)
    for block in range(count):
        for j in range(BLK):
            sel[block * BLK + j, block * 128 + j] = 1.0
    return sel


def group_mask():
    lane = np.arange(HALF)
    ok = lane % 128 < BLK
    group = (lane // 128) * 100 + (lane % 128) // 12
    return ((group[:, None] == group[None, :]) & ok[:, None] & ok[None, :]).astype(np.float32)


def dot(a, b):
    return lax.dot_general(a, b, (((1,), (0,)), ((), ())), preferred_element_type=F32)


def dot_nt(a, b):
    return lax.dot_general(a, b, (((1,), (1,)), ((), ())), preferred_element_type=F32)


def dot_nt_high(a, b):
    return lax.dot_general(
        a, b, (((1,), (1,)), ((), ())), preferred_element_type=F32, precision=lax.Precision.HIGHEST
    )


def dot_tn_high(a, b):
    return lax.dot_general(
        a, b, (((0,), (0,)), ((), ())), preferred_element_type=F32, precision=lax.Precision.HIGHEST
    )


def exact_dot(values, ones):
    high = values.astype(BF16).astype(F32)
    rest = values - high
    middle = rest.astype(BF16).astype(F32)
    low = rest - middle
    rows = values.shape[0]
    out = dot(jnp.concatenate([high, middle, low], axis=0).astype(BF16), ones)
    return out[:rows] + out[rows : 2 * rows] + out[2 * rows :]


def sigmoid(v):
    return 0.5 + 0.5 * jnp.tanh(0.5 * v)


def silu(v):
    return v * sigmoid(v)


def silu_slope(v):
    s = sigmoid(v)
    return s * (1.0 + v * (1.0 - s))


def pack_taps(t0, t1, t2):
    t0, t1, t2 = t0[:, :BLK], t1[:, :BLK], t2[:, :BLK]
    join = lambda a, b: jnp.concatenate([a, b], axis=1)
    return jnp.concatenate(
        [
            join(t0[:32], t2[:32, :32]),
            join(t0[32:], t2[:16, 32:64]),
            join(t1[:16], t2[16:32, 32:64]),
            join(t1[16:], t2[:32, 64:]),
            join(t2[32:], jnp.zeros((16, 32), t2.dtype)),
        ],
        axis=0,
    )


def last_tap(packed):
    lanes = [packed[:32, BLK:], packed[32:64, BLK:], packed[64:96, BLK:], jnp.zeros((32, 32), packed.dtype)]
    return jnp.concatenate([jnp.concatenate(lanes, axis=1), packed[96:112]], axis=0)


def pack_four(b0, b1, b2, b3):
    return jnp.concatenate(
        [jnp.concatenate([b[:, :BLK], b3[:, 32 * k : 32 * k + 32]], axis=1) for k, b in enumerate((b0, b1, b2))],
        axis=0,
    )


def unpack_four(packed):
    size = packed.shape[0] // 3
    parts = [packed[k * size : k * size + size] for k in range(3)]
    zero = jnp.zeros((size, 32), packed.dtype)
    fourth = jnp.concatenate([p[:, BLK:] for p in parts] + [zero], axis=1)
    return [jnp.concatenate([p[:, :BLK], zero], axis=1) for p in parts] + [fourth]


def pack_pixels(full):
    half = CHUNK // 2
    return pack_four(full[:half, :128], full[half:, :128], full[:half, 128:], full[half:, 128:])


def unpack_pixels(packed):
    b0, b1, b2, b3 = unpack_four(packed)
    return jnp.concatenate([jnp.concatenate([b0, b2], axis=1), jnp.concatenate([b1, b3], axis=1)], axis=0)


INPUTS = (
    "steps",
    "images",
    "noise",
    "cot",
    "emb",
    "k1",
    "k2",
    "wf",
    "wa",
    "wo",
    "gains",
    "biases",
    "sel",
    "gmask",
    "selp",
)
OUTPUTS = (
    "ro_dst",
    "io_dst",
    "embed_grad",
    "first",
    "second",
    "film",
    "attend",
    "output",
    "gains_out",
    "biases_out",
)


class Names:
    def __init__(self, names, refs):
        for name, ref in zip(names, refs):
            setattr(self, name, ref)


def scratch_list(n, inside):
    dma = pltpu.SemaphoreType.DMA
    items = []

    def vm(name, shape, dtype):
        items.append((name, pltpu.VMEM(shape, dtype)))

    def sem(name, count):
        items.append((name + "_s", dma((count,))))
        items.append((name + "_r", dma((count,))))

    for name in ("mx", "cx", "ro", "io"):
        vm(name + "_src", (4, 384, 128), BF16)
        if name in ("mx", "cx"):
            vm(name + "_dst", (4, 384, 128), BF16)
            vm(name, (4, CHUNK, HALF), BF16)
        sem(name, 4)
    for name in ("act1", "act2"):
        vm(name, (2, PX + 2 * ROW, HALF), BF16)
        vm(name + "_t", (2, HALF, PX), BF16)
        sem(name, 4)
        sem(name + "_t", 1)
    vm("ai", (2, PX, HALF), BF16)
    vm("ai_t", (2, HALF, PX), BF16)
    sem("ai_t", 1)
    sem("ai", 4)
    vm("att", (4, PX, 128), BF16)
    vm("att_t", (2, HALF, PX), BF16)
    sem("att", 4)
    for name in ("do", "n3", "d2", "d1"):
        vm(name + "_src", (PX, HALF), BF16)
        vm(name + "_dst", (PX, HALF), BF16)
        sem(name, 2)
    vm("v2", (PX, HALF), F32)
    vm("v3", (PX, HALF), F32)
    vm("gres", (PX, HALF), F32)
    vm("gtmp", (PX, HALF), F32)
    vm("qkv", (6, PX, 128), BF16)
    vm("kvt", (4, 128, PX), BF16)
    vm("dout", (2, PX, 128), BF16)
    vm("dproj", (6, PX, 128), BF16)
    vm("gr2", (3, PX + 2 * ROW, HALF), BF16)
    vm("gr1", (3, PX + 2 * ROW, HALF), BF16)
    vm("par", (16, 384), F32)
    vm("parown", (16, HALF), F32)
    vm("stat", (16, HALF), F32)
    vm("sums", (16, HALF), F32)
    if inside:
        vm("g1", (4, 4, 336, 128), BF16)
        vm("g2", (4, 4, 336, 128), BF16)
        vm("t1", (4, 4, 144, 128), BF16)
        vm("t2", (4, 4, 144, 128), BF16)
        vm("p3", (4, 4, 144, 128), BF16)
        vm("g3", (4, 4, 192, 128), BF16)
        for name in ("g1", "g2", "p3"):
            sem(name + "z", 4)
            sem(name + "v", 4)
            sem(name + "w", 8)
        vm("sw_src", (48, 128), BF16)
        vm("sw_dst", (48, 128), BF16)
        sem("sw", 1)
        vm("sb_src", (48, 128), F32)
        vm("sb_dst", (48, 128), F32)
        sem("sb", 1)
        for name, nc, rows in (("r1", 3, 112), ("r2", 3, 112), ("r3", 1, 144)):
            vm(name + "_acc", (nc, 4, 4, rows, 128), F32)
            vm(name + "w_src", (nc, 2, 4, rows, 128), BF16)
            vm(name + "w_dst", (nc, 2, 4, rows, 128), BF16)
            vm(name + "v_src", (nc, 4, rows, 128), BF16)
            vm(name + "v_dst", (nc, 4, rows, 128), BF16)
            vm(name + "z_src", (4, nc, rows, 128), BF16)
            vm(name + "z_dst", (4, nc, rows, 128), BF16)
            sem(name + "w", nc)
            sem(name + "v", nc)
            sem(name + "z", nc * 4)
    vm("el", (n, 2, 768), F32)
    sem("el", n)
    vm("em", (2 * n, 768), F32)
    vm("wfp", (128, HALF), BF16)
    vm("esel", (2 * n, 128), F32)
    vm("fp", (n, 2, HALF), F32)
    vm("fr", (n, 2, HALF), F32)
    sem("fr", n)
    vm("fx", (4, 1, 128), F32)
    vm("fh", (4, 1, 128), F32)
    sem("fh", 4)
    vm("ft", (4, 1, 128), F32)
    vm("th", (4, 1, 128), F32)
    sem("th", 4)
    vm("fa", (n, 2, HALF), F32)
    sem("fa", n)
    vm("fta", (2 * n, HALF), F32)
    vm("ep", (n, 2, 128), F32)
    vm("er", (n, 2, 128), F32)
    sem("er", n)
    vm("eh", (4, n, 2, 128), F32)
    sem("eh", 4)
    vm("ad", (n, 16, HALF), F32)
    sem("ad", n)
    vm("hb", (4, 16, HALF), F32)
    sem("hb", 4)
    return items


def make_kernel(n, inside, names):
    film_rows = 768 // n

    def kernel(*refs):
        r = Names(names, refs)
        d = lax.axis_index("dp")
        h = lax.axis_index("head")
        x = h // 2
        c = h - 2 * x
        z = d // 2
        y = d - 2 * z
        sib = (d, h + 1 - 2 * c)
        xdev = (d, h + 2 - 4 * x)
        v = x + c * (y - x)
        w = y + c * (x - y)
        vdev = (d + c * (1 - 2 * y), h + (1 - c) * (2 - 4 * x))
        wdev = (d + (1 - c) * (1 - 2 * y), h + c * (2 - 4 * x))

        def slot(xx, yy):
            if inside:
                return (yy + c * (xx - yy)) * 2 + xx + c * (yy - xx)
            return yy * 2 + xx

        def rc(src, dst, send, recv, dev):
            return pltpu.make_async_remote_copy(
                src_ref=src, dst_ref=dst, send_sem=send, recv_sem=recv, device_id=dev, device_id_type=MESH
            )

        def loop(count, body):
            def step(i, carry):
                body(i)
                return carry

            lax.fori_loop(0, count, step, 0)

        def each(count, body):
            for i in range(count):
                body(i)

        def rows(i, size=CHUNK, base=0):
            return pl.ds(pl.multiple_of(base + i * size, 32), size)

        def dp_start(src_of, dst, send, recv):
            def step(k, carry):
                peer = lax.rem(d + k, n)
                rc(src_of(peer), dst.at[d], send.at[k], recv.at[d], (peer, h)).start()
                return carry

            lax.fori_loop(1, n, step, 0)

        def dp_wait(src_of, dst, send, recv):
            def step(k, carry):
                peer = lax.rem(d + k, n)
                copy = rc(src_of(peer), dst.at[peer], send.at[k], recv.at[peer], (peer, h))
                copy.wait_recv()
                copy.wait_send()
                return carry

            lax.fori_loop(1, n, step, 0)

        def head_start(src_of, dst, send, recv):
            for k in range(1, 4):
                peer = lax.rem(h + k, 4)
                rc(src_of(peer), dst.at[h], send.at[k], recv.at[h], (d, peer)).start()

        def head_wait(src_of, dst, send, recv):
            for k in range(1, 4):
                peer = lax.rem(h + k, 4)
                copy = rc(src_of(peer), dst.at[peer], send.at[k], recv.at[peer], (d, peer))
                copy.wait_recv()
                copy.wait_send()

        class Halves:
            def __init__(self, name, base):
                self.buf, self.base = getattr(r, name), base
                self.send, self.recv = getattr(r, name + "_s"), getattr(r, name + "_r")

            def at(self, core, i):
                return self.buf.at[core, rows(i, CHUNK, self.base)]

            def fill(self, make):
                def body(i):
                    self.buf[c, rows(i, CHUNK, self.base), :] = make(i)
                    ref = self.at(c, i)
                    rc(ref, ref, self.send.at[i], self.recv.at[i], sib).start()

                loop(4, body)

            def wait(self):
                for i in range(4):
                    ref = self.at(1 - c, i)
                    copy = rc(ref, ref, self.send.at[i], self.recv.at[i], sib)
                    copy.wait_recv()
                    copy.wait_send()

        class Parts:
            def __init__(self, name):
                self.src, self.dst = getattr(r, name + "_src"), getattr(r, name + "_dst")
                self.send, self.recv = getattr(r, name + "_s"), getattr(r, name + "_r")

            def copy(self, i):
                at = rows(i, 2 * CHUNK)
                return rc(self.src.at[at], self.dst.at[at], self.send.at[i], self.recv.at[i], sib)

            def fill(self, make):
                def body(i):
                    self.src[rows(i, 2 * CHUNK), :] = make(i).astype(BF16)
                    self.copy(i).start()

                each(2, body)

            def get(self, i):
                copy = self.copy(i)
                copy.wait_recv()
                copy.wait_send()
                return self.dst[rows(i, 2 * CHUNK), :].astype(F32)

        class Gather:
            def __init__(self, name):
                self.g = getattr(r, name)
                self.zs, self.zr = getattr(r, name + "z_s"), getattr(r, name + "z_r")
                self.vs, self.vr = getattr(r, name + "v_s"), getattr(r, name + "v_r")
                self.ws, self.wr = getattr(r, name + "w_s"), getattr(r, name + "w_r")

            def zcopy(self, k):
                peer = (lax.rem(z + k, 4) * 2 + y, h)
                return rc(
                    self.g.at[w * 2 + v, 0], self.g.at[w * 2 + v, 4 - k], self.zs.at[k], self.zr.at[4 - k], peer
                )

            def vcopy(self, vv, i):
                ref = self.g.at[w * 2 + vv, i]
                return rc(ref, ref, self.vs.at[i], self.vr.at[i], vdev)

            def wcopy(self, ww, other, i):
                ref = self.g.at[ww * 2 + v + other * (1 - 2 * v), i]
                return rc(ref, ref, self.ws.at[2 * i + other], self.wr.at[2 * i + other], wdev)

            def own(self):
                for k in range(1, 4):
                    self.zcopy(k).start()
                self.vcopy(v, 0).start()
                self.wcopy(w, 0, 0).start()

            def pass_own(self):
                self.vcopy(1 - v, 0).wait_recv()
                self.wcopy(w, 1, 0).start()

            def pass_z(self, *ks):
                for k in ks:
                    self.zcopy(k).wait_recv()
                    self.vcopy(v, 4 - k).start()
                    self.wcopy(w, 0, 4 - k).start()

            def pass_v(self, *ks):
                for k in ks:
                    self.vcopy(1 - v, 4 - k).wait_recv()
                    self.wcopy(w, 1, 4 - k).start()

            def done(self):
                for i in range(4):
                    for other in range(2):
                        self.wcopy(1 - w, other, i).wait_recv()

            def finish(self):
                for k in range(1, 4):
                    self.zcopy(k).wait_send()
                for i in range(4):
                    self.vcopy(v, i).wait_send()
                    for other in range(2):
                        self.wcopy(w, other, i).wait_send()

        class Reduce:
            def __init__(self, name, count):
                get = lambda tail: getattr(r, name + tail)
                self.acc, self.count = get("_acc"), count
                self.wsrc, self.wdst, self.ws, self.wr = get("w_src"), get("w_dst"), get("w_s"), get("w_r")
                self.vsrc, self.vdst, self.vs, self.vr = get("v_src"), get("v_dst"), get("v_s"), get("v_r")
                self.zsrc, self.zdst, self.zs, self.zr = get("z_src"), get("z_dst"), get("z_s"), get("z_r")

            def wcopy(self, a):
                return rc(self.wsrc.at[a], self.wdst.at[a], self.ws.at[a], self.wr.at[a], wdev)

            def vcopy(self, a, size):
                at = pl.ds(a, size)
                return rc(self.vsrc.at[at], self.vdst.at[at], self.vs.at[a], self.vr.at[a], vdev)

            def zcopy(self, a, size, k):
                at = pl.ds(a, size)
                return rc(
                    self.zsrc.at[k, at],
                    self.zdst.at[4 - k, at],
                    self.zs.at[a * 4 + k],
                    self.zr.at[a * 4 + 4 - k],
                    (lax.rem(z + k, 4) * 2 + y, h),
                )

            def start(self, a):
                def step(i, carry):
                    vv, zz = i // 4, lax.rem(i, 4)
                    self.wsrc[a, vv, zz] = self.acc[a, (1 - w) * 2 + vv, zz].astype(BF16)
                    return carry

                lax.fori_loop(0, 8, step, 0)
                self.wcopy(a).start()

            def second(self, first, size):
                for a in range(first, first + size):
                    self.wcopy(a).wait_recv()

                    def step(zz, carry):
                        self.vsrc[a, zz] = (
                            self.acc[a, w * 2 + 1 - v, zz] + self.wdst[a, 1 - v, zz].astype(F32)
                        ).astype(BF16)
                        return carry

                    lax.fori_loop(0, 4, step, 0)
                self.vcopy(first, size).start()

            def third(self, first, size):
                self.vcopy(first, size).wait_recv()
                for a in range(first, first + size):

                    def step(k, carry):
                        zz = lax.rem(z + k, 4)
                        total = (
                            self.acc[a, w * 2 + v, zz]
                            + self.wdst[a, v, zz].astype(F32)
                            + self.vdst[a, zz].astype(F32)
                        )
                        self.acc[a, w * 2 + v, zz] = total
                        self.zsrc[k, a] = total.astype(BF16)
                        return carry

                    lax.fori_loop(0, 4, step, 0)
                for k in range(1, 4):
                    self.zcopy(first, size, k).start()

            def finish(self, groups):
                for first, size in groups:
                    self.vcopy(first, size).wait_send()
                    for k in range(1, 4):
                        copy = self.zcopy(first, size, k)
                        copy.wait_recv()
                        copy.wait_send()
                for a in range(self.count):
                    self.wcopy(a).wait_send()

            def last(self, a):
                total = self.acc[a, w * 2 + v, z]
                for k in range(1, 4):
                    total = total + self.zdst[k, a].astype(F32)
                return total

        def rel(zc):
            return lax.rem(zc - z + 4, 4) if inside else zc

        class Taps:
            def __init__(self, packed, last):
                self.packed, self.last = packed, last

            def block(self, tap, zc, xx, yy):
                a, b = tap // 3, tap % 3
                if b < 2:
                    return self.packed[slot(xx, yy), rel(zc), pl.ds(a * 112 + b * 48, 48), :]
                return self.last[slot(xx, yy), rel(zc), pl.ds(a * 48, 48), :]

            def unpack(self, ww):
                def step(i, carry):
                    q, zz = ww * 2 + i // 4, lax.rem(i, 4)
                    for a in range(3):
                        self.last[q, zz, pl.ds(a * 48, 48), :] = last_tap(
                            self.packed[q, zz, pl.ds(a * 112, 112), :]
                        )
                    return carry

                lax.fori_loop(0, 8, step, 0)

        class Plain:
            def __init__(self, blocks):
                self.blocks = blocks

            def block(self, tap, zc, xx, yy):
                return self.blocks[slot(xx, yy), rel(zc), pl.ds(tap * 48, 48), :]

            def unpack(self, ww):
                def step(i, carry):
                    q, zz = ww * 2 + i // 4, lax.rem(i, 4)
                    self.blocks[q, zz] = jnp.concatenate(unpack_four(r.p3[q, zz]), axis=0)
                    return carry

                lax.fori_loop(0, 8, step, 0)

        k1, k2, k3 = Taps(r.g1, r.t1), Taps(r.g2, r.t2), Plain(r.g3)

        def wtile(g, tap, zc, xx):
            return jnp.concatenate(
                [g.block(tap, zc, xx, 0), g.block(tap, zc, xx, 1), jnp.zeros((32, 128), BF16)], axis=0
            )

        def wtap(g, tap, zcs):
            return jnp.concatenate(
                [jnp.concatenate([wtile(g, tap, zc, xx) for xx in range(2)], axis=1) for zc in zcs], axis=0
            )

        ALL = (0, 2, 1, 3)

        def half_of(core):
            return (core, core + 2)

        def wproj(zcs):
            return jnp.concatenate(
                [
                    jnp.concatenate([wtile(k3, j, zc, xx) for xx in range(2) for j in range(3)], axis=1)
                    for zc in zcs
                ],
                axis=0,
            )

        def flat(buf, base, i, size):
            return jnp.concatenate([buf[0, rows(i, size, base), :], buf[1, rows(i, size, base), :]], axis=1)

        barrier = pltpu.get_barrier_semaphore()

        def greet(k, carry):
            pl.semaphore_signal(barrier, inc=1, device_id=(lax.rem(d + k, n), h), device_id_type=MESH)
            return carry

        lax.fori_loop(1, n, greet, 0)
        for k in range(1, 4):
            pl.semaphore_signal(barrier, inc=1, device_id=(d, lax.rem(h + k, 4)), device_id_type=MESH)
        if inside:
            for a in range(3):
                r.g1[w * 2 + v, 0, pl.ds(a * 112, 112), :] = pack_taps(*[r.k1[3 * a + b] for b in range(3)])
        pl.semaphore_wait(barrier, n - 1 + 3)
        if inside:
            ga, gb, gc = Gather("g1"), Gather("g2"), Gather("p3")
            ga.own()

        def mix(m, carry):
            keep, spread = plan(r.steps[m], 384)
            field = keep * r.images[m].astype(F32) + spread * r.noise[m].astype(F32)
            low = field.astype(BF16)
            for core in range(2):
                r.mx_src[m * 2 + core] = pack_pixels(dot(low, r.sel[core])).astype(BF16)
            return carry

        lax.fori_loop(0, 2, mix, 0)
        head_start(lambda p: r.mx_src.at[p], r.mx_dst, r.mx_s, r.mx_r)
        r.mx_dst[h] = r.mx_src[h]
        if inside:
            ga.pass_own()

        r.el[d] = silu(r.emb[...].astype(F32)).astype(BF16).astype(F32)
        dp_start(lambda p: r.el.at[d], r.el, r.el_s, r.el_r)

        if inside:
            blocks = dot(r.wa[...], r.selp[: 3 * BLK, : 3 * 128]).astype(BF16)
            r.sw_src[...] = blocks[:, 128:256]
            swap = rc(r.sw_src, r.sw_dst, r.sw_s.at[0], r.sw_r.at[0], sib)
            swap.start()
            for a in range(3):
                r.g2[w * 2 + v, 0, pl.ds(a * 112, 112), :] = pack_taps(*[r.k2[3 * a + b] for b in range(3)])
        r.par[0:3, :] = r.gains[...]
        r.par[3:13, :] = r.biases[...]
        r.par[13:16, :] = jnp.zeros((3, 384), F32)
        r.parown[...] = exact_dot(r.par[...], r.sel[c])

        def prow(i):
            return r.parown[pl.ds(i, 1), :]

        for buf in (r.act1, r.act2):
            for core in range(2):
                buf[core, pl.ds(0, ROW), :] = jnp.zeros((ROW, HALF), BF16)
                buf[core, pl.ds(PX + ROW, ROW), :] = jnp.zeros((ROW, HALF), BF16)
        for buf in (r.gr1, r.gr2):
            for b in range(3):
                buf[b, pl.ds(0, ROW), :] = jnp.zeros((ROW, HALF), BF16)
                buf[b, pl.ds(PX + ROW, ROW), :] = jnp.zeros((ROW, HALF), BF16)
        r.wfp[...] = jnp.zeros((128, HALF), BF16)
        r.wfp[pl.ds(0, film_rows), :] = dot(r.wf[...], r.selp[: 2 * BLK, :HALF]).astype(BF16)
        if inside:
            ga.pass_z(1, 3, 2)
            gb.own()

        count = float(PX * 12)

        def fold(vals):
            return jnp.sum(vals.reshape(CHUNK // 8, 8, HALF), axis=0)

        def sums_of(fn, k):
            def step(i, carry):
                return tuple(a + fold(b) for a, b in zip(carry, fn(i)))

            zero = jnp.zeros((8, HALF), F32)
            return lax.fori_loop(0, 4, step, (zero,) * k)

        def group_mean(part):
            return jnp.sum(exact_dot(part, r.gmask[...]), axis=0, keepdims=True) / count

        def norm(load, which, total):
            mean = group_mean(total)
            (square,) = sums_of(lambda i: (jnp.square(load(i) - mean),), 1)
            inv = lax.rsqrt(group_mean(square) + EPS)
            r.stat[pl.ds(2 * which, 1), :] = mean
            r.stat[pl.ds(2 * which + 1, 1), :] = inv
            return mean, inv

        zero8 = jnp.zeros((8, HALF), F32)

        def norm_back(sums, load_grad, load_hat, coef, inv):
            plain, cross = sums
            means = exact_dot(jnp.concatenate([coef * plain, coef * cross], axis=0), r.gmask[...])
            plain_mean = jnp.sum(means[:8], axis=0, keepdims=True) / count
            cross_mean = jnp.sum(means[8:], axis=0, keepdims=True) / count
            outer, base, slope = inv * coef, inv * plain_mean, inv * cross_mean

            def chunk(i):
                return outer * load_grad(i) - base - load_hat(i) * slope

            return (
                jnp.sum(plain, axis=0, keepdims=True),
                jnp.sum(cross, axis=0, keepdims=True),
                chunk,
            )

        def transposed(name, core):
            ref = getattr(r, name).at[core]
            return rc(ref, ref, getattr(r, name + "_s").at[0], getattr(r, name + "_r").at[0], sib)

        def transpose_act(buf, base, name):
            out = getattr(r, name)
            for q in range(4):
                out[c, :, pl.ds(q * CHUNK, CHUNK)] = jnp.transpose(buf[c, pl.ds(base + q * CHUNK, CHUNK), :])
            transposed(name, c).start()

        def transposed_wait(name):
            copy = transposed(name, 1 - c)
            copy.wait_recv()
            copy.wait_send()

        head_wait(lambda p: r.mx_src.at[p], r.mx_dst, r.mx_s, r.mx_r)

        def unpack_mixed(i, carry):
            vals = unpack_pixels(r.mx_dst[i])
            r.mx[i] = vals
            return carry + fold(vals.astype(F32))

        mixed_sum = lax.fori_loop(0, 4, unpack_mixed, zero8)

        def mixed(i):
            return r.mx[i].astype(F32)

        if inside:
            ga.pass_v(1, 3)
        mean1, inv1 = norm(mixed, 0, mixed_sum)
        if inside:
            ga.pass_v(2)
        gain1, shift1 = prow(0), prow(3)
        act1 = Halves("act1", ROW)

        def affine(mean, inv, gain, shift):
            return inv * gain, shift - mean * (inv * gain)

        mul1, add1 = affine(mean1, inv1, gain1, shift1)

        def pre1(i):
            return mixed(i) * mul1 + add1

        act1.fill(lambda i: silu(pre1(i)).astype(BF16))
        dp_wait(lambda p: r.el.at[d], r.el, r.el_s, r.el_r)
        for j in range(n):
            r.em[pl.ds(2 * j, 2), :] = r.el[j]
        place = lax.broadcasted_iota(jnp.int32, (768, 128), 0) - film_rows * d
        lane = lax.broadcasted_iota(jnp.int32, (768, 128), 1)
        pick = jnp.where((place == lane) & (lane < film_rows), 1.0, 0.0).astype(BF16)
        r.esel[...] = dot(r.em[...].astype(BF16), pick)
        film_part = dot(r.esel[...].astype(BF16), r.wfp[...])
        for j in range(n):
            r.fp[j] = film_part[2 * j : 2 * j + 2]
        dp_start(lambda p: r.fp.at[p], r.fr, r.fr_s, r.fr_r)
        r.fr[d] = r.fp[d]
        if inside:
            swap.wait()
            got = r.sw_dst[...]
            keep0, keep2 = blocks[:, :128], blocks[:, 256:]
            r.p3[w * 2 + v, 0] = pack_four(
                jnp.where(c == 0, keep0, got),
                jnp.where(c == 0, keep2, keep0),
                jnp.where(c == 0, got, keep2),
                r.wo[...],
            )
        act1.wait()
        transpose_act(r.act1, ROW, "act1_t")
        if inside:
            gb.pass_own()
            gb.pass_z(1, 3, 2)
            gc.own()
        def split_cot(m, carry):
            for core in range(2):
                r.cx_src[m * 2 + core] = pack_pixels(dot(r.cot[m], r.sel[core])).astype(BF16)
            return carry

        lax.fori_loop(0, 2, split_cot, 0)
        column = lax.broadcasted_iota(jnp.int32, (1, ROW, HALF), 1)
        not_first = jnp.where(column > 0, 1.0, 0.0)
        not_last = jnp.where(column < ROW - 1, 1.0, 0.0)

        def in_rows(vals, mask):
            return (vals.reshape(CHUNK // ROW, ROW, HALF) * mask).reshape(CHUNK, HALF)

        def from_left(vals):
            return in_rows(pltpu.roll(vals, 1, 0), not_first)

        def from_right(vals):
            return in_rows(pltpu.roll(vals, CHUNK - 1, 0), not_last)

        def conv(buf, g, store, between):
            weights = lambda: jnp.concatenate(
                [jnp.concatenate([wtap(g, 3 * a + b, ALL) for b in range(3)], axis=1) for a in range(3)], axis=0
            )

            total = zero8
            for i in range(2):
                left = jnp.concatenate([flat(buf, ROW * a, i, 2 * CHUNK) for a in range(3)], axis=1)
                out = dot(left, weights())
                for j in range(2):
                    part = out[j * CHUNK : j * CHUNK + CHUNK]
                    part = part[:, HALF : 2 * HALF] + from_left(part[:, :HALF]) + from_right(part[:, 2 * HALF :])
                    total = total + fold(store(2 * i + j, part))
                if i == 0:
                    between()
            return total

        if inside:
            k1.unpack(w)
            ga.done()
            k1.unpack(1 - w)

        dp_wait(lambda p: r.fp.at[p], r.fr, r.fr_s, r.fr_r)
        film_sum = r.fr[0]
        for j in range(1, n):
            film_sum = film_sum + r.fr[j]
        for m in range(2):
            for core in range(2):
                r.fx[m * 2 + core] = film_sum[m : m + 1, core * 128 : core * 128 + 128]
        head_start(lambda p: r.fx.at[p], r.fh, r.fh_s, r.fh_r)
        r.fh[h] = r.fx[h]

        def store_v2(i, vals):
            vals = vals + prow(6)
            r.v2[rows(i), :] = vals
            return vals

        v2_sum = conv(r.act1, k1, store_v2, (lambda: gb.pass_v(1, 3, 2)) if inside else lambda: None)
        head_wait(lambda p: r.fx.at[p], r.fh, r.fh_s, r.fh_r)
        scale = 1.0 + (jnp.concatenate([r.fh[0], r.fh[1]], axis=1) + prow(8))
        shift = jnp.concatenate([r.fh[2], r.fh[3]], axis=1) + prow(9)
        head_start(lambda p: r.cx_src.at[p], r.cx_dst, r.cx_s, r.cx_r)
        r.cx_dst[h] = r.cx_src[h]
        mean2, inv2 = norm(lambda i: r.v2[rows(i), :], 1, v2_sum)
        gain2, shift2 = prow(1), prow(4)
        act2 = Halves("act2", ROW)

        def hat2(i):
            return (r.v2[rows(i), :] - mean2) * inv2

        mul2, add2 = affine(mean2, inv2, gain2 * scale, shift2 * scale + shift)

        def pre2(i):
            return r.v2[rows(i), :] * mul2 + add2

        act2.fill(lambda i: silu(pre2(i)).astype(BF16))
        if inside:
            gc.pass_own()
            gc.pass_z(1, 3, 2)

        transpose_act(r.act2, ROW, "act2_t")
        act2.wait()
        if inside:
            k2.unpack(w)
            gb.done()
            k2.unpack(1 - w)

        def store_v3(i, vals):
            vals = mixed(i) + (vals + prow(7))
            r.v3[rows(i), :] = vals
            return vals

        v3_sum = conv(r.act2, k2, store_v3, (lambda: gc.pass_v(1, 3, 2)) if inside else lambda: None)
        mean3, inv3 = norm(lambda i: r.v3[rows(i), :], 2, v3_sum)
        gain3, shift3 = prow(2), prow(5)
        ai = Halves("ai", 0)

        def hat3(i):
            return (r.v3[rows(i), :] - mean3) * inv3

        mul3, add3 = affine(mean3, inv3, gain3, shift3)
        ai.fill(lambda i: (r.v3[rows(i), :] * mul3 + add3).astype(BF16))
        transpose_act(r.ai, 0, "ai_t")

        if inside:
            k3.unpack(w)
            gc.done()
            k3.unpack(1 - w)
        head_wait(lambda p: r.cx_src.at[p], r.cx_dst, r.cx_s, r.cx_r)

        def unpack_cot(i):
            r.cx[i] = unpack_pixels(r.cx_dst[i])

        loop(4, unpack_cot)
        dop = Parts("do")

        def cot_rows(i):
            return jnp.concatenate([r.cx[2 * i], r.cx[2 * i + 1]], axis=0)

        dop.fill(lambda i: dot_nt(cot_rows(i), wtap(k3, 3, half_of(1 - c))))

        ai.wait()
        bias_proj = [prow(10)[:, :128], prow(10)[:, 128:], None, None, prow(11)[:, :128], prow(11)[:, 128:]]

        def project(i):
            out = dot(flat(r.ai, 0, i, 2 * CHUNK), wproj(ALL))
            for k in range(6):
                part = out[:, k * 128 : k * 128 + 128]
                if bias_proj[k] is not None:
                    part = part + bias_proj[k]
                r.qkv[k, rows(i, 2 * CHUNK), :] = part.astype(BF16)

        each(2, project)

        def do_own(i):
            full = (dot_nt(cot_rows(i), wtap(k3, 3, half_of(c))) + dop.get(i)).astype(BF16)
            for k in range(2):
                r.dout[k, rows(i, 2 * CHUNK), :] = full[:, k * 128 : k * 128 + 128]

        each(2, do_own)

        factor = 1.0 / math.sqrt(HEAD_DIM)
        factor2 = factor * math.log2(math.e)
        att = []

        def transposes(k):
            r.kvt[k] = jnp.transpose(r.qkv[k + 2])

        loop(4, transposes)

        def att_copy(core, k):
            ref = r.att.at[core * 2 + k]
            return rc(ref, ref, r.att_s.at[k], r.att_r.at[k], sib)

        def att_t_copy(core, k):
            ref = r.att_t.at[core, pl.ds(pl.multiple_of(k * 128, 128), 128)]
            return rc(ref, ref, r.att_s.at[2 + k], r.att_r.at[2 + k], sib)

        def one_head(k):
            lows, grads = [], []
            for b in range(2):
                at = pl.ds(b * 2 * CHUNK, 2 * CHUNK)
                query = r.qkv[k, at, :]
                grad = r.dout[k, at, :]
                scores = dot_nt(r.qkv[2 + k], query)
                peak = jnp.max(scores, axis=0, keepdims=True)
                expo = jnp.exp2((scores - peak) * factor2)
                inverse = 1.0 / jnp.sum(expo, axis=0, keepdims=True)
                low = (expo * inverse).astype(BF16)
                got = dot(r.kvt[2 + k], low)
                got_low = got.astype(BF16)
                r.att_t[c, pl.ds(pl.multiple_of(k * 128, 128), 128), at] = got_low
                r.att[2 * c + k, at, :] = jnp.transpose(got_low)
                spread = jnp.sum(got * jnp.transpose(grad).astype(F32), axis=0, keepdims=True)
                probs_grad = dot_nt(r.qkv[4 + k], grad)
                scores_grad = ((probs_grad - spread) * inverse * expo).astype(BF16)
                back = dot(r.kvt[k], scores_grad)
                r.dproj[k, at, :] = (jnp.transpose(back) * factor).astype(BF16)
                lows.append(low)
                grads.append(scores_grad)
            att_copy(c, k).start()
            att_t_copy(c, k).start()
            r.dproj[4 + k] = dot(jnp.concatenate(lows, axis=1), r.dout[k]).astype(BF16)
            r.dproj[2 + k] = (dot(jnp.concatenate(grads, axis=1), r.qkv[k]) * factor).astype(BF16)

        loop(2, one_head)

        n3 = Parts("n3")

        def proj_rows(i):
            return jnp.concatenate([r.dproj[k, rows(i, 2 * CHUNK), :] for k in range(6)], axis=1)

        n3.fill(lambda i: dot_nt(proj_rows(i), wproj(half_of(1 - c))))

        def rows_of(act_t):
            return jnp.concatenate([act_t[p // 2, pl.ds(p % 2 * 128, BLK), :] for p in range(4)], axis=0)

        for k in range(2):
            copy = att_copy(1 - c, k)
            copy.wait_recv()
            copy.wait_send()

        def result(i):
            left = jnp.concatenate([r.att[p, rows(i), :] for p in range(4)], axis=1)
            branch = dot(left, wtap(k3, 3, ALL)) + prow(12)
            r.ro_src[i] = pack_pixels(r.v3[rows(i), :] + branch).astype(BF16)

        loop(4, result)
        head_start(lambda p: r.ro_src.at[p], r.ro_dst, r.ro_s, r.ro_r)
        r.ro_dst[h] = r.ro_src[h]

        if inside:
            red1, red2, red3 = Reduce("r1", 3), Reduce("r2", 3), Reduce("r3", 1)
            acc1, acc2, acc3 = r.r1_acc, r.r2_acc, r.r3_acc
        else:
            acc1, acc2, acc3 = r.first, r.second, r.attend

        transposed_wait("ai_t")
        for k in range(2):
            copy = att_t_copy(1 - c, k)
            copy.wait_recv()
            copy.wait_send()
        right = jnp.concatenate([r.dproj[k] for k in range(6)], axis=1)
        cot_all = jnp.concatenate([r.cx[i] for i in range(4)], axis=0)
        attend_out = dot(rows_of(r.ai_t), right)
        output_out = dot(rows_of(r.att_t), cot_all)
        for p, zc in enumerate(ALL):
            for yy in range(2):
                for xx in range(2):
                    row = p * BLK + yy * 48
                    tiles = [
                        attend_out[row : row + 48, (xx * 3 + j) * 128 : (xx * 3 + j) * 128 + 128] for j in range(3)
                    ]
                    acc3[0, slot(xx, yy), zc] = pack_four(
                        *tiles, output_out[row : row + 48, xx * 128 : xx * 128 + 128]
                    )
        if inside:
            red3.start(0)

        def proj_sums(i, carry):
            q = jnp.concatenate([r.dproj[0, rows(i), :], r.dproj[1, rows(i), :]], axis=1).astype(F32)
            val = jnp.concatenate([r.dproj[4, rows(i), :], r.dproj[5, rows(i), :]], axis=1).astype(F32)
            return (carry[0] + fold(q), carry[1] + fold(val), carry[2] + fold(r.cx[i].astype(F32)))

        qsum, vsum, csum = lax.fori_loop(0, 4, proj_sums, (zero8, zero8, zero8))
        r.sums[pl.ds(3 + 7, 1), :] = jnp.sum(qsum, axis=0, keepdims=True)
        r.sums[pl.ds(3 + 8, 1), :] = jnp.sum(vsum, axis=0, keepdims=True)
        r.sums[pl.ds(3 + 9, 1), :] = jnp.sum(csum, axis=0, keepdims=True)
        r.sums[pl.ds(13, 3), :] = jnp.zeros((3, HALF), F32)

        def n3_own(i, carry):
            both = dot_nt(proj_rows(i), wproj(half_of(c))) + n3.get(i)
            for j in range(2):
                vals = both[j * CHUNK : j * CHUNK + CHUNK]
                r.gtmp[rows(2 * i + j), :] = vals
                carry = carry[0] + fold(vals), carry[1] + fold(vals * hat3(2 * i + j))
            return carry

        sums3 = n3_own(1, n3_own(0, (zero8, zero8)))
        plain3, cross3, back3 = norm_back(sums3, lambda i: r.gtmp[rows(i), :], hat3, gain3, inv3)
        r.sums[pl.ds(2, 1), :] = cross3
        r.sums[pl.ds(3 + 2, 1), :] = plain3

        def shifted(buf, i, vals):
            buf[0, rows(i, CHUNK, ROW), :] = from_right(vals).astype(BF16)
            buf[1, rows(i, CHUNK, ROW), :] = vals.astype(BF16)
            buf[2, rows(i, CHUNK, ROW), :] = from_left(vals).astype(BF16)

        def residual_back(i, carry):
            vals = r.cx[i].astype(F32) + back3(i)
            r.gres[rows(i), :] = vals
            shifted(r.gr2, i, vals)
            return carry + fold(vals.astype(BF16).astype(F32))

        bias_two = lax.fori_loop(0, 4, residual_back, jnp.zeros((8, HALF), F32))
        r.sums[pl.ds(3 + 4, 1), :] = jnp.sum(bias_two, axis=0, keepdims=True)

        def act_back(buf, g, core, i, size):
            left = jnp.concatenate(
                [buf[b, rows(i, size, 2 * ROW - ROW * a), :] for a in range(3) for b in range(3)], axis=1
            )
            right = jnp.concatenate(
                [wtap(g, 3 * a + b, half_of(core)) for a in range(3) for b in range(3)], axis=1
            )
            return dot_nt(left, right)

        def conv_back(parts, buf, g):
            parts.fill(lambda i: act_back(buf, g, 1 - c, i, 2 * CHUNK))

        def conv_back_own(parts, buf, g, outer, hat):
            def own(i, carry):
                vals = act_back(buf, g, c, i, 2 * CHUNK) + parts.get(i)
                for j in range(2):
                    at = 2 * i + j
                    grad = vals[j * CHUNK : j * CHUNK + CHUNK] * outer(at)
                    r.gtmp[rows(at), :] = grad
                    carry = carry[0] + fold(grad), carry[1] + fold(grad * hat(at))
                return carry

            return own(1, own(0, (zero8, zero8)))

        def kernel_grad(act_t, buf, acc, after):
            def step(a):
                right = jnp.concatenate([buf[b, pl.ds(2 * ROW - ROW * a, PX), :] for b in range(3)], axis=1)
                out = dot(rows_of(act_t), right)
                for p, zc in enumerate(ALL):
                    for yy in range(2):
                        for xx in range(2):
                            row = p * BLK + yy * 48
                            tiles = [
                                out[row : row + 48, b * HALF + xx * 128 : b * HALF + xx * 128 + 128] for b in range(3)
                            ]
                            acc[a, slot(xx, yy), zc] = pack_taps(*tiles)
                after(a)

            each(3, step)

        serve = inside
        d2 = Parts("d2")
        transposed_wait("act2_t")
        kernel_grad(r.act2_t, r.gr2, acc2, red2.start if inside else lambda a: None)
        if serve:
            red3.second(0, 1)
        conv_back(d2, r.gr2, k2)
        if serve:
            red2.second(0, 1)
        sums2 = conv_back_own(d2, r.gr2, k2, lambda i: silu_slope(pre2(i)), hat2)
        if serve:
            red2.second(1, 1)
            red3.third(0, 1)

        plain2, cross2, back2 = norm_back(sums2, lambda i: r.gtmp[rows(i), :], hat2, gain2 * scale, inv2)
        r.sums[pl.ds(1, 1), :] = scale * cross2
        r.sums[pl.ds(3 + 1, 1), :] = scale * plain2
        film_scale_term = gain2 * cross2 + shift2 * plain2
        r.sums[pl.ds(3 + 5, 1), :] = film_scale_term
        r.sums[pl.ds(3 + 6, 1), :] = plain2
        for j in range(2):
            r.ft[j] = film_scale_term[:, j * 128 : j * 128 + 128]
            r.ft[2 + j] = plain2[:, j * 128 : j * 128 + 128]
        head_start(lambda p: r.ft.at[p], r.th, r.th_s, r.th_r)
        r.th[h] = r.ft[h]

        def first_back(i, carry):
            vals = back2(i)
            shifted(r.gr1, i, vals)
            return carry + fold(vals.astype(BF16).astype(F32))

        bias_one = lax.fori_loop(0, 4, first_back, jnp.zeros((8, HALF), F32))
        r.sums[pl.ds(3 + 3, 1), :] = jnp.sum(bias_one, axis=0, keepdims=True)

        if serve:
            red2.second(2, 1)
            red2.third(0, 1)
            red2.third(1, 1)

        head_wait(lambda p: r.ft.at[p], r.th, r.th_s, r.th_r)
        for m in range(2):
            r.fa[d, pl.ds(m, 1), :] = jnp.concatenate([r.th[2 * m], r.th[2 * m + 1]], axis=1)
        dp_start(lambda p: r.fa.at[d], r.fa, r.fa_s, r.fa_r)

        d1 = Parts("d1")

        def after_chunk(a):
            if serve:
                red1.start(a)
                if a == 1:
                    red2.third(2, 1)

        transposed_wait("act1_t")
        kernel_grad(r.act1_t, r.gr1, acc1, after_chunk)
        conv_back(d1, r.gr1, k1)
        if serve:
            red1.second(0, 1)

        dp_wait(lambda p: r.fa.at[d], r.fa, r.fa_s, r.fa_r)
        for j in range(n):
            r.fta[pl.ds(2 * j, 2), :] = r.fa[j]
        film_block = dot_tn_high(r.esel[...], r.fta[...])
        r.film[...] = jnp.concatenate([film_block[:film_rows, :BLK], film_block[:film_rows, 128 : 128 + BLK]], axis=1)
        embed_part = dot_nt_high(r.fta[...], r.wfp[...].astype(F32))
        for j in range(n):
            r.ep[j] = embed_part[2 * j : 2 * j + 2]
        dp_start(lambda p: r.ep.at[p], r.er, r.er_s, r.er_r)
        r.er[d] = r.ep[d]

        def hat1(i):
            return (mixed(i) - mean1) * inv1

        sums1 = conv_back_own(d1, r.gr1, k1, lambda i: silu_slope(pre1(i)), hat1)
        if serve:
            red1.second(1, 1)

        dp_wait(lambda p: r.ep.at[p], r.er, r.er_s, r.er_r)
        r.eh[h] = r.er[...]
        head_start(lambda p: r.eh.at[h], r.eh, r.eh_s, r.eh_r)
        plain1, cross1, back1 = norm_back(sums1, lambda i: r.gtmp[rows(i), :], hat1, gain1, inv1)
        r.sums[pl.ds(0, 1), :] = cross1
        r.sums[pl.ds(3, 1), :] = plain1
        r.ad[d] = r.sums[...]
        dp_start(lambda p: r.ad.at[d], r.ad, r.ad_s, r.ad_r)

        if serve:
            red1.second(2, 1)
            red1.third(0, 1)
        keep, _ = plan(r.steps[x], HALF)

        def image_back(i):
            r.io_src[i] = pack_pixels(keep * (r.gres[rows(i), :] + back1(i))).astype(BF16)

        loop(4, image_back)
        head_start(lambda p: r.io_src.at[p], r.io_dst, r.io_s, r.io_r)
        r.io_dst[h] = r.io_src[h]
        if serve:
            red1.third(1, 1)
            red1.third(2, 1)

        dp_wait(lambda p: r.ad.at[d], r.ad, r.ad_s, r.ad_r)
        total = r.ad[0]
        for j in range(1, n):
            total = total + r.ad[j]
        r.hb[h] = total
        head_start(lambda p: r.hb.at[h], r.hb, r.hb_s, r.hb_r)
        head_wait(lambda p: r.ro_src.at[p], r.ro_dst, r.ro_s, r.ro_r)

        if inside:
            red2.finish(((0, 1), (1, 1), (2, 1)))
            for a in range(3):
                r.second[a] = red2.last(a)

        head_wait(lambda p: r.hb.at[h], r.hb, r.hb_s, r.hb_r)
        even = r.hb[0] + r.hb[2]
        odd = r.hb[1] + r.hb[3]
        wide = jnp.concatenate(
            [even[:, :BLK], odd[:, :BLK], even[:, 128 : 128 + BLK], odd[:, 128 : 128 + BLK]], axis=1
        )
        r.gains_out[...] = wide[0:3]
        r.biases_out[...] = wide[3:13]

        head_wait(lambda p: r.eh.at[h], r.eh, r.eh_s, r.eh_r)
        pieces = []
        for j in range(n):
            piece = (r.eh[0, j] + r.eh[1, j]) + (r.eh[2, j] + r.eh[3, j])
            pieces.append(piece[:, :film_rows])
        r.embed_grad[...] = jnp.concatenate(pieces, axis=1) * silu_slope(r.emb[...].astype(F32))

        head_wait(lambda p: r.io_src.at[p], r.io_dst, r.io_s, r.io_r)

        if inside:
            red3.finish(((0, 1),))
            tiles = unpack_four(red3.last(0))
            r.sb_src[...] = jnp.where(c == 0, tiles[2], tiles[0])
            back = rc(r.sb_src, r.sb_dst, r.sb_s.at[0], r.sb_r.at[0], sib)
            back.start()
            r.output[...] = tiles[3]
            for part in (ga, gb, gc):
                part.finish()
            red1.finish(((0, 1), (1, 1), (2, 1)))
            for a in range(3):
                r.first[a] = red1.last(a)
            back.wait()
            r.attend[:, 0:128] = jnp.where(c == 0, tiles[0], tiles[1])
            r.attend[:, 128:256] = r.sb_dst[...]
            r.attend[:, 256:384] = jnp.where(c == 0, tiles[1], tiles[2])

    return kernel


def make_writer(names_in, names_out):
    def kernel(*refs):
        count, wide = len(names_in), len(names_out)
        far_in, far_out = refs[:count], refs[count : count + wide]
        near_in, near_out = refs[count + wide : 2 * count + wide], refs[2 * count + wide : 2 * count + 2 * wide]
        sem_in, sem_out = refs[-2:]
        src, dst = Names(names_in, near_in), Names(names_out, near_out)
        loads = {
            name: pltpu.make_async_copy(far_in[i], near_in[i], sem_in.at[i]) for i, name in enumerate(names_in)
        }
        stores = {
            name: pltpu.make_async_copy(near_out[i], far_out[i], sem_out.at[i]) for i, name in enumerate(names_out)
        }
        for name in ("sel", "ro_dst", "io_dst"):
            loads[name].start()
        for name in names_in:
            if name not in ("sel", "ro_dst", "io_dst"):
                loads[name].start()
        loads["sel"].wait()
        for name, packed in (("result", "ro_dst"), ("image_grad", "io_dst")):
            loads[packed].wait()
            ref = getattr(src, packed)
            for m in range(2):
                getattr(dst, name)[m] = dot_nt(unpack_pixels(ref[2 * m]), src.sel[0]) + dot_nt(
                    unpack_pixels(ref[2 * m + 1]), src.sel[1]
                )
            stores[name].start()
        for name in ("first", "second"):
            if name in names_out:
                loads[name].wait()
                for a in range(3):
                    block = getattr(src, name)[a]
                    getattr(dst, name)[3 * a] = block[:48, :BLK]
                    getattr(dst, name)[3 * a + 1] = block[48:96, :BLK]
                    getattr(dst, name)[3 * a + 2] = last_tap(block)[:, :BLK]
                stores[name].start()
        if "attend" in names_out:
            loads["attend"].wait()
            dst.attend[...] = jnp.concatenate([src.attend[:, j * 128 : j * 128 + BLK] for j in range(3)], axis=1)
            stores["attend"].start()
            loads["output"].wait()
            dst.output[...] = src.output[:, :BLK]
            stores["output"].start()
        for name in ("embed_grad", "film", "gains_out", "biases_out"):
            loads[name].wait()
            getattr(dst, name)[...] = getattr(src, name)[...]
            stores[name].start()
        for name in names_out:
            stores[name].wait()

    return kernel


def per_device(n, *args):
    (
        images,
        noise_field,
        time_steps,
        embedding,
        first_kernel,
        second_kernel,
        film_weight,
        attend_weight,
        output_weight,
        norm_gains,
        biases,
        cotangent,
    ) = args
    inside = n == 8
    maps, height, width, channels = images.shape
    flat_shape = (maps, height * width, channels)
    film_rows = film_weight.shape[0]
    inputs = dict(
        steps=time_steps,
        images=images.reshape(flat_shape),
        noise=noise_field.reshape(flat_shape),
        cot=cotangent.reshape(flat_shape),
        emb=embedding,
        k1=first_kernel.reshape((9,) + first_kernel.shape[2:]),
        k2=second_kernel.reshape((9,) + second_kernel.shape[2:]),
        wf=film_weight,
        wa=attend_weight,
        wo=output_weight,
        gains=norm_gains,
        biases=biases,
        sel=jnp.asarray(channel_lanes(), BF16),
        gmask=jnp.asarray(group_mask(), BF16),
        selp=jnp.asarray(block_lanes(3), BF16),
    )
    shapes = dict(
        ro_dst=(4, 384, 128),
        io_dst=(4, 384, 128),
        embed_grad=embedding.shape,
        first=(3, 112, 128),
        second=(3, 112, 128),
        film=film_weight.shape,
        attend=(48, 384),
        output=(48, 128),
        gains_out=norm_gains.shape,
        biases_out=biases.shape,
    )
    names_in, names_out = list(INPUTS), list(OUTPUTS)
    core = lax.axis_index("head") % 2
    if not inside:
        def whole(array, row_axis):
            array = lax.all_gather(array, "dp", axis=row_axis, tiled=True)
            return lax.all_gather(array, "head", axis=array.ndim - 1, tiled=True)

        def spread(array, count):
            taps = array.shape[0]
            array = array.reshape(taps, 4, 2, 48, 2, 2, BLK)
            array = lax.dynamic_index_in_dim(array, core, 5, keepdims=False)
            array = jnp.transpose(array, (2, 4, 1, 0, 3, 5))
            array = jnp.pad(array, ((0, 0),) * 5 + ((0, 32),))
            return array.reshape(4, 4, taps * 48, 128)

        full_a = whole(attend_weight, 0).reshape(384, 2, 3, 2, BLK)
        full_a = jnp.transpose(full_a, (2, 0, 1, 3, 4)).reshape(3, 384, 384)
        full_o = whole(output_weight, 0)[None]
        for name, last, array in (("g1", "t1", first_kernel), ("g2", "t2", second_kernel)):
            blocks = spread(whole(array, 2).reshape(9, 384, 384), 9).reshape(4, 4, 3, 3, 48, 128)
            two = blocks[:, :, :, :2].reshape(4, 4, 3, 96, 128)
            inputs[name] = jnp.pad(two, ((0, 0),) * 3 + ((0, 16), (0, 0))).reshape(4, 4, 336, 128)
            inputs[last] = blocks[:, :, :, 2].reshape(4, 4, 144, 128)
        inputs["g3"] = spread(jnp.concatenate([full_a, full_o], axis=0), 4)
        names_in += ["g1", "g2", "t1", "t2", "g3"]
        shapes["first"] = shapes["second"] = (3, 4, 4, 112, 128)
        shapes["attend"] = (1, 4, 4, 144, 128)
        del shapes["output"]
        names_out.remove("output")
    items = scratch_list(n, inside)
    smem = pl.BlockSpec(memory_space=pltpu.SMEM)
    vmem = pl.BlockSpec(memory_space=pltpu.VMEM)
    outs = pl.pallas_call(
        make_kernel(n, inside, names_in + names_out + [name for name, _ in items]),
        out_shape=[
            jax.ShapeDtypeStruct(shapes[name], BF16 if name in ("ro_dst", "io_dst") else F32) for name in names_out
        ],
        in_specs=[smem if name == "steps" else vmem for name in names_in],
        out_specs=[vmem] * len(names_out),
        scratch_shapes=[item for _, item in items],
        compiler_params=pltpu.CompilerParams(
            collective_id=0, has_side_effects=True, vmem_limit_bytes=63 * 1024 * 1024
        ),
        name="blocks",
    )(*[inputs[name] for name in names_in])
    raw = dict(zip(names_out, outs))
    final = dict(
        result=flat_shape,
        image_grad=flat_shape,
        embed_grad=embedding.shape,
        film=film_weight.shape,
        gains_out=norm_gains.shape,
        biases_out=biases.shape,
    )
    if inside:
        final.update(first=(9, 48, BLK), second=(9, 48, BLK), attend=attend_weight.shape, output=output_weight.shape)
    names_last = [name for name in names_out if inside or name not in ("first", "second", "attend")] + ["sel"]
    names_final = list(final)
    given = [inputs["sel"] if name == "sel" else raw[name] for name in names_last]
    far = pl.BlockSpec(memory_space=pl.ANY)
    outs = pl.pallas_call(
        make_writer(names_last, names_final),
        out_shape=[jax.ShapeDtypeStruct(final[name], F32) for name in names_final],
        in_specs=[far] * len(names_last),
        out_specs=[far] * len(names_final),
        scratch_shapes=[pltpu.VMEM(array.shape, array.dtype) for array in given]
        + [pltpu.VMEM(final[name], F32) for name in names_final]
        + [pltpu.SemaphoreType.DMA((len(names_last),)), pltpu.SemaphoreType.DMA((len(names_final),))],
        compiler_params=pltpu.CompilerParams(vmem_limit_bytes=63 * 1024 * 1024),
        name="outputs",
    )(*given)
    out = dict(zip(names_final, outs))
    if not inside:

        def blocks_of(array, size):
            parts = [array[..., k * 48 : k * 48 + 48, :BLK] for k in range(size)]
            if size == 2:
                lanes = [array[..., k * 32 : k * 32 + 32, BLK:] for k in range(3)]
                lanes = jnp.concatenate(lanes, axis=-1)
                parts.append(jnp.concatenate([lanes, array[..., 96:112, :BLK]], axis=-2))
            else:
                lanes = [array[..., k * 48 : k * 48 + 48, BLK:] for k in range(3)]
                parts.append(jnp.concatenate(lanes, axis=-1))
            array = jnp.stack(parts, axis=1)
            array = array.reshape(array.shape[:2] + (2, 2, 4, 48, BLK))
            taps = array.shape[0] * array.shape[1]
            array = jnp.transpose(array, (0, 1, 4, 2, 5, 3, 6)).reshape(taps, 384, 2, 1, BLK)
            both = jnp.concatenate([array, jnp.zeros_like(array)], axis=3)
            return jnp.where(core == 0, both, both[:, :, :, ::-1]).reshape(taps, 384, 384)

        def shared(array, axis):
            array = lax.psum_scatter(array, "head", scatter_dimension=array.ndim - 1, tiled=True)
            return lax.psum_scatter(array, "dp", scatter_dimension=axis, tiled=True)

        out["first"] = shared(blocks_of(raw["first"], 2), 1)
        out["second"] = shared(blocks_of(raw["second"], 2), 1)
        both = blocks_of(raw["attend"], 3)
        joined = both[:3].reshape(3, 384, 2, 2, BLK)
        joined = jnp.transpose(joined, (1, 2, 0, 3, 4)).reshape(384, 1152)
        out["attend"] = shared(joined, 0)
        out["output"] = shared(both[3], 0)
    return (
        out["result"].reshape(images.shape),
        out["image_grad"].reshape(images.shape),
        out["embed_grad"],
        out["first"].reshape(first_kernel.shape),
        out["second"].reshape(second_kernel.shape),
        out["film"],
        out["attend"],
        out["output"],
        out["gains_out"],
        out["biases_out"],
    )


def solution(mesh):
    n = mesh.shape["dp"]
    field = P("dp", "head", None, None)
    taps = P(None, None, "dp", "head")
    both = P("dp", "head")
    return jax.shard_map(
        lambda *args: per_device(n, *args),
        mesh=mesh,
        in_specs=(field, field, P("dp"), P("dp", None), taps, taps, both, both, both, P(), P(), field),
        out_specs=(field, field, P("dp", None), taps, taps, both, both, both, P(), P()),
        check_vma=False,
    )
```

```python
import math

import jax
import jax.numpy as jnp
import numpy as np
from jax import lax
from jax.experimental import pallas as pl
from jax.experimental.pallas import tpu as pltpu
from jax.sharding import PartitionSpec as P

HEAD_DIM = 96
GROUPS = 32
STEPS = 4000
EPS = 1e-05
OFFSET = 0.008
MESH = pl.DeviceIdType.MESH
F32 = jnp.float32
BF16 = jnp.bfloat16

PX = 1024
ROW = 32
CHUNK = 256
BLK = 96
HALF = 256
NHEAD = 4


def plan(time_step, lanes):
    fraction = (jnp.full((1, lanes), time_step, jnp.int32).astype(F32) + 1.0) / STEPS
    start = math.cos(OFFSET / (1.0 + OFFSET) * (math.pi / 2)) ** 2
    curve = jnp.square(jnp.cos((fraction + OFFSET) / (1.0 + OFFSET) * (math.pi / 2))) / start
    return (jnp.sqrt(curve), jnp.sqrt(jnp.maximum(1.0 - curve, 0.0)))


def channel_lanes():
    sel = np.zeros((2, 384, HALF), np.float32)
    for block in range(4):
        for j in range(BLK):
            sel[block % 2, block * BLK + j, (block // 2) * 128 + j] = 1.0
    return sel


def block_lanes(count):
    sel = np.zeros((count * BLK, count * 128), np.float32)
    for block in range(count):
        for j in range(BLK):
            sel[block * BLK + j, block * 128 + j] = 1.0
    return sel


def group_mask():
    lane = np.arange(HALF)
    ok = lane % 128 < BLK
    group = (lane // 128) * 100 + (lane % 128) // 12
    return ((group[:, None] == group[None, :]) & ok[:, None] & ok[None, :]).astype(np.float32)


def dot(a, b):
    return lax.dot_general(a, b, (((1,), (0,)), ((), ())), preferred_element_type=F32)


def dot_nt(a, b):
    return lax.dot_general(a, b, (((1,), (1,)), ((), ())), preferred_element_type=F32)


def dot_nt_high(a, b):
    return lax.dot_general(
        a, b, (((1,), (1,)), ((), ())), preferred_element_type=F32, precision=lax.Precision.HIGHEST
    )


def dot_tn_high(a, b):
    return lax.dot_general(
        a, b, (((0,), (0,)), ((), ())), preferred_element_type=F32, precision=lax.Precision.HIGHEST
    )


def exact_dot(values, ones):
    high = values.astype(BF16).astype(F32)
    rest = values - high
    middle = rest.astype(BF16).astype(F32)
    low = rest - middle
    rows = values.shape[0]
    out = dot(jnp.concatenate([high, middle, low], axis=0).astype(BF16), ones)
    return out[:rows] + out[rows : 2 * rows] + out[2 * rows :]


def sigmoid(v):
    return 0.5 + 0.5 * jnp.tanh(0.5 * v)


def silu(v):
    return v * sigmoid(v)


def silu_slope(v):
    s = sigmoid(v)
    return s * (1.0 + v * (1.0 - s))


def pack_taps(t0, t1, t2):
    t0, t1, t2 = t0[:, :BLK], t1[:, :BLK], t2[:, :BLK]
    join = lambda a, b: jnp.concatenate([a, b], axis=1)
    return jnp.concatenate(
        [
            join(t0[:32], t2[:32, :32]),
            join(t0[32:], t2[:16, 32:64]),
            join(t1[:16], t2[16:32, 32:64]),
            join(t1[16:], t2[:32, 64:]),
            join(t2[32:], jnp.zeros((16, 32), t2.dtype)),
        ],
        axis=0,
    )


def last_tap(packed):
    lanes = [packed[:32, BLK:], packed[32:64, BLK:], packed[64:96, BLK:], jnp.zeros((32, 32), packed.dtype)]
    return jnp.concatenate([jnp.concatenate(lanes, axis=1), packed[96:112]], axis=0)


def pack_four(b0, b1, b2, b3):
    return jnp.concatenate(
        [jnp.concatenate([b[:, :BLK], b3[:, 32 * k : 32 * k + 32]], axis=1) for k, b in enumerate((b0, b1, b2))],
        axis=0,
    )


def unpack_four(packed):
    size = packed.shape[0] // 3
    parts = [packed[k * size : k * size + size] for k in range(3)]
    zero = jnp.zeros((size, 32), packed.dtype)
    fourth = jnp.concatenate([p[:, BLK:] for p in parts] + [zero], axis=1)
    return [jnp.concatenate([p[:, :BLK], zero], axis=1) for p in parts] + [fourth]


def pack_pixels(full):
    half = CHUNK // 2
    return pack_four(full[:half, :128], full[half:, :128], full[:half, 128:], full[half:, 128:])


def unpack_pixels(packed):
    b0, b1, b2, b3 = unpack_four(packed)
    return jnp.concatenate([jnp.concatenate([b0, b2], axis=1), jnp.concatenate([b1, b3], axis=1)], axis=0)


INPUTS = (
    "steps",
    "images",
    "noise",
    "cot",
    "emb",
    "k1",
    "k2",
    "wf",
    "wa",
    "wo",
    "gains",
    "biases",
    "sel",
    "gmask",
    "selp",
)
OUTPUTS = (
    "ro_dst",
    "io_dst",
    "embed_grad",
    "first",
    "second",
    "film",
    "attend",
    "output",
    "gains_out",
    "biases_out",
)


class Names:
    def __init__(self, names, refs):
        for name, ref in zip(names, refs):
            setattr(self, name, ref)


def scratch_list(n, inside):
    dma = pltpu.SemaphoreType.DMA
    items = []

    def vm(name, shape, dtype):
        items.append((name, pltpu.VMEM(shape, dtype)))

    def sem(name, count):
        items.append((name + "_s", dma((count,))))
        items.append((name + "_r", dma((count,))))

    for name in ("mx", "cx", "ro", "io"):
        vm(name + "_src", (4, 384, 128), BF16)
        if name in ("mx", "cx"):
            vm(name + "_dst", (4, 384, 128), BF16)
            vm(name, (4, CHUNK, HALF), BF16)
        sem(name, 4)
    for name in ("act1", "act2"):
        vm(name, (2, PX + 2 * ROW, HALF), BF16)
        vm(name + "_t", (2, HALF, PX), BF16)
        sem(name, 4)
        sem(name + "_t", 1)
    vm("ai", (2, PX, HALF), BF16)
    vm("ai_t", (2, HALF, PX), BF16)
    sem("ai_t", 1)
    sem("ai", 4)
    vm("att", (4, PX, 128), BF16)
    vm("att_t", (2, HALF, PX), BF16)
    sem("att", 4)
    for name in ("do", "n3", "d2", "d1"):
        vm(name + "_src", (PX, HALF), BF16)
        vm(name + "_dst", (PX, HALF), BF16)
        sem(name, 1)
    vm("v2", (PX, HALF), F32)
    vm("v3", (PX, HALF), F32)
    vm("gres", (PX, HALF), F32)
    vm("gtmp", (PX, HALF), F32)
    vm("conv", (3, PX, HALF), F32)
    vm("qkv", (6, PX, 128), BF16)
    vm("kvt", (4, 128, PX), BF16)
    vm("dout", (2, PX, 128), BF16)
    vm("dproj", (6, PX, 128), BF16)
    vm("gr2", (3, PX + 2 * ROW, HALF), BF16)
    vm("gr1", (3, PX + 2 * ROW, HALF), BF16)
    vm("par", (16, 384), F32)
    vm("parown", (16, HALF), F32)
    vm("stat", (16, HALF), F32)
    vm("sums", (16, HALF), F32)
    if inside:
        vm("g1", (4, 4, 336, 128), BF16)
        vm("g2", (4, 4, 336, 128), BF16)
        vm("t1", (4, 4, 144, 128), BF16)
        vm("t2", (4, 4, 144, 128), BF16)
        vm("p3", (4, 4, 144, 128), BF16)
        vm("g3", (4, 4, 192, 128), BF16)
        for name in ("g1", "g2", "p3"):
            sem(name + "z", 4)
            sem(name + "v", 4)
            sem(name + "w", 8)
        vm("sw_src", (48, 128), BF16)
        vm("sw_dst", (48, 128), BF16)
        sem("sw", 1)
        vm("sb_src", (48, 128), F32)
        vm("sb_dst", (48, 128), F32)
        sem("sb", 1)
        for name, nc, rows in (("r1", 3, 112), ("r2", 3, 112), ("r3", 1, 144)):
            vm(name + "_acc", (nc, 4, 4, rows, 128), F32)
            vm(name + "w_src", (nc, 2, 4, rows, 128), BF16)
            vm(name + "w_dst", (nc, 2, 4, rows, 128), BF16)
            vm(name + "v_src", (nc, 4, rows, 128), BF16)
            vm(name + "v_dst", (nc, 4, rows, 128), BF16)
            vm(name + "z_src", (4, nc, rows, 128), BF16)
            vm(name + "z_dst", (4, nc, rows, 128), BF16)
            sem(name + "w", nc)
            sem(name + "v", nc)
            sem(name + "z", nc * 4)
    vm("el", (n, 2, 768), F32)
    sem("el", n)
    vm("em", (2 * n, 768), F32)
    vm("wfp", (128, HALF), BF16)
    vm("esel", (2 * n, 128), F32)
    vm("fp", (n, 2, HALF), F32)
    vm("fr", (n, 2, HALF), F32)
    sem("fr", n)
    vm("fx", (4, 1, 128), F32)
    vm("fh", (4, 1, 128), F32)
    sem("fh", 4)
    vm("ft", (4, 1, 128), F32)
    vm("th", (4, 1, 128), F32)
    sem("th", 4)
    vm("fa", (n, 2, HALF), F32)
    sem("fa", n)
    vm("fta", (2 * n, HALF), F32)
    vm("ep", (n, 2, 128), F32)
    vm("er", (n, 2, 128), F32)
    sem("er", n)
    vm("eh", (4, n, 2, 128), F32)
    sem("eh", 4)
    vm("ad", (n, 16, HALF), F32)
    sem("ad", n)
    vm("hb", (4, 16, HALF), F32)
    sem("hb", 4)
    return items


def make_kernel(n, inside, names):
    film_rows = 768 // n

    def kernel(*refs):
        r = Names(names, refs)
        d = lax.axis_index("dp")
        h = lax.axis_index("head")
        x = h // 2
        c = h - 2 * x
        z = d // 2
        y = d - 2 * z
        sib = (d, h + 1 - 2 * c)
        xdev = (d, h + 2 - 4 * x)
        v = x + c * (y - x)
        w = y + c * (x - y)
        vdev = (d + c * (1 - 2 * y), h + (1 - c) * (2 - 4 * x))
        wdev = (d + (1 - c) * (1 - 2 * y), h + c * (2 - 4 * x))

        def slot(xx, yy):
            if inside:
                return (yy + c * (xx - yy)) * 2 + xx + c * (yy - xx)
            return yy * 2 + xx

        def rc(src, dst, send, recv, dev):
            return pltpu.make_async_remote_copy(
                src_ref=src, dst_ref=dst, send_sem=send, recv_sem=recv, device_id=dev, device_id_type=MESH
            )

        def loop(count, body):
            def step(i, carry):
                body(i)
                return carry

            lax.fori_loop(0, count, step, 0)

        def each(count, body):
            for i in range(count):
                body(i)

        def rows(i, size=CHUNK, base=0):
            return pl.ds(pl.multiple_of(base + i * size, 32), size)

        def dp_start(src_of, dst, send, recv):
            def step(k, carry):
                peer = lax.rem(d + k, n)
                rc(src_of(peer), dst.at[d], send.at[k], recv.at[d], (peer, h)).start()
                return carry

            lax.fori_loop(1, n, step, 0)

        def dp_wait(src_of, dst, send, recv):
            def step(k, carry):
                peer = lax.rem(d + k, n)
                copy = rc(src_of(peer), dst.at[peer], send.at[k], recv.at[peer], (peer, h))
                copy.wait_recv()
                copy.wait_send()
                return carry

            lax.fori_loop(1, n, step, 0)

        def head_start(src_of, dst, send, recv):
            for k in range(1, 4):
                peer = lax.rem(h + k, 4)
                rc(src_of(peer), dst.at[h], send.at[k], recv.at[h], (d, peer)).start()

        def head_wait(src_of, dst, send, recv):
            for k in range(1, 4):
                peer = lax.rem(h + k, 4)
                copy = rc(src_of(peer), dst.at[peer], send.at[k], recv.at[peer], (d, peer))
                copy.wait_recv()
                copy.wait_send()

        class Halves:
            def __init__(self, name, base):
                self.buf, self.base = getattr(r, name), base
                self.send, self.recv = getattr(r, name + "_s"), getattr(r, name + "_r")

            def at(self, core, i):
                return self.buf.at[core, rows(i, CHUNK, self.base)]

            def fill(self, make):
                def body(i):
                    self.buf[c, rows(i, CHUNK, self.base), :] = make(i)
                    ref = self.at(c, i)
                    rc(ref, ref, self.send.at[i], self.recv.at[i], sib).start()

                loop(4, body)

            def wait(self):
                for i in range(4):
                    ref = self.at(1 - c, i)
                    copy = rc(ref, ref, self.send.at[i], self.recv.at[i], sib)
                    copy.wait_recv()
                    copy.wait_send()

        class Parts:
            def __init__(self, name):
                self.src, self.dst = getattr(r, name + "_src"), getattr(r, name + "_dst")
                self.send, self.recv = getattr(r, name + "_s"), getattr(r, name + "_r")

            def copy(self):
                return rc(self.src, self.dst, self.send.at[0], self.recv.at[0], sib)

            def both(self, make):
                self.src[...] = make(1 - c).astype(BF16)
                self.copy().start()
                r.gtmp[...] = make(c)

            def wait(self):
                copy = self.copy()
                copy.wait_recv()
                copy.wait_send()

            def get(self, i):
                return r.gtmp[rows(i), :] + self.dst[rows(i), :].astype(F32)

        class Gather:
            def __init__(self, name):
                self.g = getattr(r, name)
                self.zs, self.zr = getattr(r, name + "z_s"), getattr(r, name + "z_r")
                self.vs, self.vr = getattr(r, name + "v_s"), getattr(r, name + "v_r")
                self.ws, self.wr = getattr(r, name + "w_s"), getattr(r, name + "w_r")

            def zcopy(self, k):
                peer = (lax.rem(z + k, 4) * 2 + y, h)
                return rc(
                    self.g.at[w * 2 + v, 0], self.g.at[w * 2 + v, 4 - k], self.zs.at[k], self.zr.at[4 - k], peer
                )

            def vcopy(self, vv, i):
                ref = self.g.at[w * 2 + vv, i]
                return rc(ref, ref, self.vs.at[i], self.vr.at[i], vdev)

            def wcopy(self, ww, other, i):
                ref = self.g.at[ww * 2 + v + other * (1 - 2 * v), i]
                return rc(ref, ref, self.ws.at[2 * i + other], self.wr.at[2 * i + other], wdev)

            def own(self):
                for k in range(1, 4):
                    self.zcopy(k).start()
                self.vcopy(v, 0).start()
                self.wcopy(w, 0, 0).start()

            def pass_own(self):
                self.vcopy(1 - v, 0).wait_recv()
                self.wcopy(w, 1, 0).start()

            def pass_z(self, *ks):
                for k in ks:
                    self.zcopy(k).wait_recv()
                    self.vcopy(v, 4 - k).start()
                    self.wcopy(w, 0, 4 - k).start()

            def pass_v(self, *ks):
                for k in ks:
                    self.vcopy(1 - v, 4 - k).wait_recv()
                    self.wcopy(w, 1, 4 - k).start()

            def done(self):
                for i in range(4):
                    for other in range(2):
                        self.wcopy(1 - w, other, i).wait_recv()

            def finish(self):
                for k in range(1, 4):
                    self.zcopy(k).wait_send()
                for i in range(4):
                    self.vcopy(v, i).wait_send()
                    for other in range(2):
                        self.wcopy(w, other, i).wait_send()

        class Reduce:
            def __init__(self, name, count):
                get = lambda tail: getattr(r, name + tail)
                self.acc, self.count = get("_acc"), count
                self.wsrc, self.wdst, self.ws, self.wr = get("w_src"), get("w_dst"), get("w_s"), get("w_r")
                self.vsrc, self.vdst, self.vs, self.vr = get("v_src"), get("v_dst"), get("v_s"), get("v_r")
                self.zsrc, self.zdst, self.zs, self.zr = get("z_src"), get("z_dst"), get("z_s"), get("z_r")

            def wcopy(self, a):
                return rc(self.wsrc.at[a], self.wdst.at[a], self.ws.at[a], self.wr.at[a], wdev)

            def vcopy(self, a, size):
                at = pl.ds(a, size)
                return rc(self.vsrc.at[at], self.vdst.at[at], self.vs.at[a], self.vr.at[a], vdev)

            def zcopy(self, a, size, k):
                at = pl.ds(a, size)
                return rc(
                    self.zsrc.at[k, at],
                    self.zdst.at[4 - k, at],
                    self.zs.at[a * 4 + k],
                    self.zr.at[a * 4 + 4 - k],
                    (lax.rem(z + k, 4) * 2 + y, h),
                )

            def start(self, a):
                def step(i, carry):
                    vv, zz = i // 4, lax.rem(i, 4)
                    self.wsrc[a, vv, zz] = self.acc[a, (1 - w) * 2 + vv, zz].astype(BF16)
                    return carry

                lax.fori_loop(0, 8, step, 0)
                self.wcopy(a).start()

            def second(self, first, size):
                for a in range(first, first + size):
                    self.wcopy(a).wait_recv()

                    def step(zz, carry):
                        self.vsrc[a, zz] = (
                            self.acc[a, w * 2 + 1 - v, zz] + self.wdst[a, 1 - v, zz].astype(F32)
                        ).astype(BF16)
                        return carry

                    lax.fori_loop(0, 4, step, 0)
                self.vcopy(first, size).start()

            def third(self, first, size):
                self.vcopy(first, size).wait_recv()
                for a in range(first, first + size):

                    def step(k, carry):
                        zz = lax.rem(z + k, 4)
                        total = (
                            self.acc[a, w * 2 + v, zz]
                            + self.wdst[a, v, zz].astype(F32)
                            + self.vdst[a, zz].astype(F32)
                        )
                        self.acc[a, w * 2 + v, zz] = total
                        self.zsrc[k, a] = total.astype(BF16)
                        return carry

                    lax.fori_loop(0, 4, step, 0)
                for k in range(1, 4):
                    self.zcopy(first, size, k).start()

            def finish(self, groups):
                for first, size in groups:
                    self.vcopy(first, size).wait_send()
                    for k in range(1, 4):
                        copy = self.zcopy(first, size, k)
                        copy.wait_recv()
                        copy.wait_send()
                for a in range(self.count):
                    self.wcopy(a).wait_send()

            def last(self, a):
                total = self.acc[a, w * 2 + v, z]
                for k in range(1, 4):
                    total = total + self.zdst[k, a].astype(F32)
                return total

        def rel(zc):
            return lax.rem(zc - z + 4, 4) if inside else zc

        class Taps:
            def __init__(self, packed, last):
                self.packed, self.last = packed, last

            def block(self, tap, zc, xx, yy):
                a, b = tap // 3, tap % 3
                if b < 2:
                    return self.packed[slot(xx, yy), rel(zc), pl.ds(a * 112 + b * 48, 48), :]
                return self.last[slot(xx, yy), rel(zc), pl.ds(a * 48, 48), :]

            def unpack(self, ww):
                def step(i, carry):
                    q, zz = ww * 2 + i // 4, lax.rem(i, 4)
                    for a in range(3):
                        self.last[q, zz, pl.ds(a * 48, 48), :] = last_tap(
                            self.packed[q, zz, pl.ds(a * 112, 112), :]
                        )
                    return carry

                lax.fori_loop(0, 8, step, 0)

        class Plain:
            def __init__(self, blocks):
                self.blocks = blocks

            def block(self, tap, zc, xx, yy):
                return self.blocks[slot(xx, yy), rel(zc), pl.ds(tap * 48, 48), :]

            def unpack(self, ww):
                def step(i, carry):
                    q, zz = ww * 2 + i // 4, lax.rem(i, 4)
                    self.blocks[q, zz] = jnp.concatenate(unpack_four(r.p3[q, zz]), axis=0)
                    return carry

                lax.fori_loop(0, 8, step, 0)

        k1, k2, k3 = Taps(r.g1, r.t1), Taps(r.g2, r.t2), Plain(r.g3)

        def wtile(g, tap, zc, xx):
            return jnp.concatenate(
                [g.block(tap, zc, xx, 0), g.block(tap, zc, xx, 1), jnp.zeros((32, 128), BF16)], axis=0
            )

        def wtap(g, tap, zcs):
            return jnp.concatenate(
                [jnp.concatenate([wtile(g, tap, zc, xx) for xx in range(2)], axis=1) for zc in zcs], axis=0
            )

        ALL = (0, 2, 1, 3)

        def half_of(core):
            return (core, core + 2)

        def wproj(zcs):
            return jnp.concatenate(
                [
                    jnp.concatenate([wtile(k3, j, zc, xx) for xx in range(2) for j in range(3)], axis=1)
                    for zc in zcs
                ],
                axis=0,
            )

        def flat(buf, base, i, size):
            return jnp.concatenate([buf[0, rows(i, size, base), :], buf[1, rows(i, size, base), :]], axis=1)

        barrier = pltpu.get_barrier_semaphore()

        def greet(k, carry):
            pl.semaphore_signal(barrier, inc=1, device_id=(lax.rem(d + k, n), h), device_id_type=MESH)
            return carry

        lax.fori_loop(1, n, greet, 0)
        for k in range(1, 4):
            pl.semaphore_signal(barrier, inc=1, device_id=(d, lax.rem(h + k, 4)), device_id_type=MESH)
        if inside:
            for a in range(3):
                r.g1[w * 2 + v, 0, pl.ds(a * 112, 112), :] = pack_taps(*[r.k1[3 * a + b] for b in range(3)])
        pl.semaphore_wait(barrier, n - 1 + 3)
        if inside:
            ga, gb, gc = Gather("g1"), Gather("g2"), Gather("p3")
            ga.own()

        def mix(m, carry):
            keep, spread = plan(r.steps[m], 384)
            field = keep * r.images[m].astype(F32) + spread * r.noise[m].astype(F32)
            low = field.astype(BF16)
            for core in range(2):
                r.mx_src[m * 2 + core] = pack_pixels(dot(low, r.sel[core])).astype(BF16)
            return carry

        lax.fori_loop(0, 2, mix, 0)
        head_start(lambda p: r.mx_src.at[p], r.mx_dst, r.mx_s, r.mx_r)
        r.mx_dst[h] = r.mx_src[h]
        if inside:
            ga.pass_own()

        r.el[d] = silu(r.emb[...].astype(F32)).astype(BF16).astype(F32)
        dp_start(lambda p: r.el.at[d], r.el, r.el_s, r.el_r)

        if inside:
            blocks = dot(r.wa[...], r.selp[: 3 * BLK, : 3 * 128]).astype(BF16)
            r.sw_src[...] = blocks[:, 128:256]
            swap = rc(r.sw_src, r.sw_dst, r.sw_s.at[0], r.sw_r.at[0], sib)
            swap.start()
            for a in range(3):
                r.g2[w * 2 + v, 0, pl.ds(a * 112, 112), :] = pack_taps(*[r.k2[3 * a + b] for b in range(3)])
        r.par[0:3, :] = r.gains[...]
        r.par[3:13, :] = r.biases[...]
        r.par[13:16, :] = jnp.zeros((3, 384), F32)
        r.parown[...] = exact_dot(r.par[...], r.sel[c])

        def prow(i):
            return r.parown[pl.ds(i, 1), :]

        for buf in (r.act1, r.act2):
            for core in range(2):
                buf[core, pl.ds(0, ROW), :] = jnp.zeros((ROW, HALF), BF16)
                buf[core, pl.ds(PX + ROW, ROW), :] = jnp.zeros((ROW, HALF), BF16)
        for buf in (r.gr1, r.gr2):
            for b in range(3):
                buf[b, pl.ds(0, ROW), :] = jnp.zeros((ROW, HALF), BF16)
                buf[b, pl.ds(PX + ROW, ROW), :] = jnp.zeros((ROW, HALF), BF16)
        r.wfp[...] = jnp.zeros((128, HALF), BF16)
        r.wfp[pl.ds(0, film_rows), :] = dot(r.wf[...], r.selp[: 2 * BLK, :HALF]).astype(BF16)
        if inside:
            ga.pass_z(1, 3, 2)
            gb.own()

        count = float(PX * 12)

        def fold(vals):
            return jnp.sum(vals.reshape(CHUNK // 8, 8, HALF), axis=0)

        def sums_of(fn, k):
            def step(i, carry):
                return tuple(a + fold(b) for a, b in zip(carry, fn(i)))

            zero = jnp.zeros((8, HALF), F32)
            return lax.fori_loop(0, 4, step, (zero,) * k)

        def group_mean(part):
            return jnp.sum(exact_dot(part, r.gmask[...]), axis=0, keepdims=True) / count

        def norm(load, which, total):
            mean = group_mean(total)
            (square,) = sums_of(lambda i: (jnp.square(load(i) - mean),), 1)
            inv = lax.rsqrt(group_mean(square) + EPS)
            r.stat[pl.ds(2 * which, 1), :] = mean
            r.stat[pl.ds(2 * which + 1, 1), :] = inv
            return mean, inv

        zero8 = jnp.zeros((8, HALF), F32)

        def norm_back(sums, load_grad, load_hat, coef, inv):
            plain, cross = sums
            means = exact_dot(jnp.concatenate([coef * plain, coef * cross], axis=0), r.gmask[...])
            plain_mean = jnp.sum(means[:8], axis=0, keepdims=True) / count
            cross_mean = jnp.sum(means[8:], axis=0, keepdims=True) / count
            outer, base, slope = inv * coef, inv * plain_mean, inv * cross_mean

            def chunk(i):
                return outer * load_grad(i) - base - load_hat(i) * slope

            return (
                jnp.sum(plain, axis=0, keepdims=True),
                jnp.sum(cross, axis=0, keepdims=True),
                chunk,
            )

        def transposed(name, core):
            ref = getattr(r, name).at[core]
            return rc(ref, ref, getattr(r, name + "_s").at[0], getattr(r, name + "_r").at[0], sib)

        def transpose_act(buf, base, name):
            out = getattr(r, name)
            for q in range(4):
                out[c, :, pl.ds(q * CHUNK, CHUNK)] = jnp.transpose(buf[c, pl.ds(base + q * CHUNK, CHUNK), :])
            transposed(name, c).start()

        def transposed_wait(name):
            copy = transposed(name, 1 - c)
            copy.wait_recv()
            copy.wait_send()

        head_wait(lambda p: r.mx_src.at[p], r.mx_dst, r.mx_s, r.mx_r)

        def unpack_mixed(i, carry):
            vals = unpack_pixels(r.mx_dst[i])
            r.mx[i] = vals
            return carry + fold(vals.astype(F32))

        mixed_sum = lax.fori_loop(0, 4, unpack_mixed, zero8)

        def mixed(i):
            return r.mx[i].astype(F32)

        if inside:
            ga.pass_v(1, 3)
        mean1, inv1 = norm(mixed, 0, mixed_sum)
        if inside:
            ga.pass_v(2)
        gain1, shift1 = prow(0), prow(3)
        act1 = Halves("act1", ROW)

        def affine(mean, inv, gain, shift):
            return inv * gain, shift - mean * (inv * gain)

        mul1, add1 = affine(mean1, inv1, gain1, shift1)

        def pre1(i):
            return mixed(i) * mul1 + add1

        act1.fill(lambda i: silu(pre1(i)).astype(BF16))
        dp_wait(lambda p: r.el.at[d], r.el, r.el_s, r.el_r)
        for j in range(n):
            r.em[pl.ds(2 * j, 2), :] = r.el[j]
        place = lax.broadcasted_iota(jnp.int32, (768, 128), 0) - film_rows * d
        lane = lax.broadcasted_iota(jnp.int32, (768, 128), 1)
        pick = jnp.where((place == lane) & (lane < film_rows), 1.0, 0.0).astype(BF16)
        r.esel[...] = dot(r.em[...].astype(BF16), pick)
        film_part = dot(r.esel[...].astype(BF16), r.wfp[...])
        for j in range(n):
            r.fp[j] = film_part[2 * j : 2 * j + 2]
        dp_start(lambda p: r.fp.at[p], r.fr, r.fr_s, r.fr_r)
        r.fr[d] = r.fp[d]
        if inside:
            swap.wait()
            got = r.sw_dst[...]
            keep0, keep2 = blocks[:, :128], blocks[:, 256:]
            r.p3[w * 2 + v, 0] = pack_four(
                jnp.where(c == 0, keep0, got),
                jnp.where(c == 0, keep2, keep0),
                jnp.where(c == 0, got, keep2),
                r.wo[...],
            )
        act1.wait()
        transpose_act(r.act1, ROW, "act1_t")
        if inside:
            gb.pass_own()
            gb.pass_z(1, 3, 2)
            gc.own()
        def split_cot(m, carry):
            for core in range(2):
                r.cx_src[m * 2 + core] = pack_pixels(dot(r.cot[m], r.sel[core])).astype(BF16)
            return carry

        lax.fori_loop(0, 2, split_cot, 0)
        column = lax.broadcasted_iota(jnp.int32, (1, ROW, HALF), 1)
        not_first = jnp.where(column > 0, 1.0, 0.0)
        not_last = jnp.where(column < ROW - 1, 1.0, 0.0)

        def in_rows(vals, mask):
            return (vals.reshape(CHUNK // ROW, ROW, HALF) * mask).reshape(CHUNK, HALF)

        def from_left(vals):
            return in_rows(pltpu.roll(vals, 1, 0), not_first)

        def from_right(vals):
            return in_rows(pltpu.roll(vals, CHUNK - 1, 0), not_last)

        def conv(buf, g, store, between):
            for b in range(3):
                left = jnp.concatenate([flat(buf, ROW * a, 0, PX) for a in range(3)], axis=1)
                r.conv[b] = dot(left, jnp.concatenate([wtap(g, 3 * a + b, ALL) for a in range(3)], axis=0))
                if b == 0:
                    between()

            def step(i, total):
                part = r.conv[1, rows(i), :] + from_left(r.conv[0, rows(i), :]) + from_right(r.conv[2, rows(i), :])
                return total + fold(store(i, part))

            return lax.fori_loop(0, 4, step, zero8)

        if inside:
            k1.unpack(w)
            ga.done()
            k1.unpack(1 - w)

        dp_wait(lambda p: r.fp.at[p], r.fr, r.fr_s, r.fr_r)
        film_sum = r.fr[0]
        for j in range(1, n):
            film_sum = film_sum + r.fr[j]
        for m in range(2):
            for core in range(2):
                r.fx[m * 2 + core] = film_sum[m : m + 1, core * 128 : core * 128 + 128]
        head_start(lambda p: r.fx.at[p], r.fh, r.fh_s, r.fh_r)
        r.fh[h] = r.fx[h]

        def store_v2(i, vals):
            vals = vals + prow(6)
            r.v2[rows(i), :] = vals
            return vals

        v2_sum = conv(r.act1, k1, store_v2, (lambda: gb.pass_v(1, 3, 2)) if inside else lambda: None)
        head_wait(lambda p: r.fx.at[p], r.fh, r.fh_s, r.fh_r)
        scale = 1.0 + (jnp.concatenate([r.fh[0], r.fh[1]], axis=1) + prow(8))
        shift = jnp.concatenate([r.fh[2], r.fh[3]], axis=1) + prow(9)
        head_start(lambda p: r.cx_src.at[p], r.cx_dst, r.cx_s, r.cx_r)
        r.cx_dst[h] = r.cx_src[h]
        mean2, inv2 = norm(lambda i: r.v2[rows(i), :], 1, v2_sum)
        gain2, shift2 = prow(1), prow(4)
        act2 = Halves("act2", ROW)

        def hat2(i):
            return (r.v2[rows(i), :] - mean2) * inv2

        mul2, add2 = affine(mean2, inv2, gain2 * scale, shift2 * scale + shift)

        def pre2(i):
            return r.v2[rows(i), :] * mul2 + add2

        act2.fill(lambda i: silu(pre2(i)).astype(BF16))
        if inside:
            gc.pass_own()
            gc.pass_z(1, 3, 2)

        transpose_act(r.act2, ROW, "act2_t")
        act2.wait()
        if inside:
            k2.unpack(w)
            gb.done()
            k2.unpack(1 - w)

        def store_v3(i, vals):
            vals = mixed(i) + (vals + prow(7))
            r.v3[rows(i), :] = vals
            return vals

        v3_sum = conv(r.act2, k2, store_v3, (lambda: gc.pass_v(1, 3, 2)) if inside else lambda: None)
        mean3, inv3 = norm(lambda i: r.v3[rows(i), :], 2, v3_sum)
        gain3, shift3 = prow(2), prow(5)
        ai = Halves("ai", 0)

        def hat3(i):
            return (r.v3[rows(i), :] - mean3) * inv3

        mul3, add3 = affine(mean3, inv3, gain3, shift3)
        ai.fill(lambda i: (r.v3[rows(i), :] * mul3 + add3).astype(BF16))
        transpose_act(r.ai, 0, "ai_t")

        if inside:
            k3.unpack(w)
            gc.done()
            k3.unpack(1 - w)
        head_wait(lambda p: r.cx_src.at[p], r.cx_dst, r.cx_s, r.cx_r)

        def unpack_cot(i):
            r.cx[i] = unpack_pixels(r.cx_dst[i])

        loop(4, unpack_cot)
        dop = Parts("do")

        def cot_all():
            return jnp.concatenate([r.cx[i] for i in range(4)], axis=0)

        dop.both(lambda core: dot_nt(cot_all(), wtap(k3, 3, half_of(core))))

        ai.wait()
        bias_proj = [prow(10)[:, :128], prow(10)[:, 128:], None, None, prow(11)[:, :128], prow(11)[:, 128:]]

        out = dot(flat(r.ai, 0, 0, PX), wproj(ALL))
        for k in range(6):
            part = out[:, k * 128 : k * 128 + 128]
            if bias_proj[k] is not None:
                part = part + bias_proj[k]
            r.qkv[k] = part.astype(BF16)
        dop.wait()

        def do_own(i):
            full = dop.get(i).astype(BF16)
            for k in range(2):
                r.dout[k, rows(i), :] = full[:, k * 128 : k * 128 + 128]

        loop(4, do_own)

        factor = 1.0 / math.sqrt(HEAD_DIM)
        factor2 = factor * math.log2(math.e)
        att = []

        def transposes(k):
            r.kvt[k] = jnp.transpose(r.qkv[k + 2])

        loop(4, transposes)

        def att_copy(core, k):
            ref = r.att.at[core * 2 + k]
            return rc(ref, ref, r.att_s.at[k], r.att_r.at[k], sib)

        def att_t_copy(core, k):
            ref = r.att_t.at[core, pl.ds(pl.multiple_of(k * 128, 128), 128)]
            return rc(ref, ref, r.att_s.at[2 + k], r.att_r.at[2 + k], sib)

        def one_head(k):
            lows, grads = [], []
            for b in range(2):
                at = pl.ds(b * 2 * CHUNK, 2 * CHUNK)
                query = r.qkv[k, at, :]
                grad = r.dout[k, at, :]
                scores = dot_nt(r.qkv[2 + k], query)
                peak = jnp.max(scores, axis=0, keepdims=True)
                expo = jnp.exp2((scores - peak) * factor2)
                inverse = 1.0 / jnp.sum(expo, axis=0, keepdims=True)
                low = (expo * inverse).astype(BF16)
                got = dot(r.kvt[2 + k], low)
                got_low = got.astype(BF16)
                r.att_t[c, pl.ds(pl.multiple_of(k * 128, 128), 128), at] = got_low
                r.att[2 * c + k, at, :] = jnp.transpose(got_low)
                spread = jnp.sum(got * jnp.transpose(grad).astype(F32), axis=0, keepdims=True)
                probs_grad = dot_nt(r.qkv[4 + k], grad)
                scores_grad = ((probs_grad - spread) * inverse * expo).astype(BF16)
                back = dot(r.kvt[k], scores_grad)
                r.dproj[k, at, :] = (jnp.transpose(back) * factor).astype(BF16)
                lows.append(low)
                grads.append(scores_grad)
            att_copy(c, k).start()
            att_t_copy(c, k).start()
            r.dproj[4 + k] = dot(jnp.concatenate(lows, axis=1), r.dout[k]).astype(BF16)
            r.dproj[2 + k] = (dot(jnp.concatenate(grads, axis=1), r.qkv[k]) * factor).astype(BF16)

        loop(2, one_head)

        n3 = Parts("n3")

        def proj_rows():
            return jnp.concatenate([r.dproj[k] for k in range(6)], axis=1)

        n3.both(lambda core: dot_nt(proj_rows(), wproj(half_of(core))))

        def rows_of(act_t):
            return jnp.concatenate([act_t[p // 2, pl.ds(p % 2 * 128, BLK), :] for p in range(4)], axis=0)

        for k in range(2):
            copy = att_copy(1 - c, k)
            copy.wait_recv()
            copy.wait_send()

        def result(i):
            left = jnp.concatenate([r.att[p, rows(i), :] for p in range(4)], axis=1)
            branch = dot(left, wtap(k3, 3, ALL)) + prow(12)
            r.ro_src[i] = pack_pixels(r.v3[rows(i), :] + branch).astype(BF16)

        loop(4, result)
        head_start(lambda p: r.ro_src.at[p], r.ro_dst, r.ro_s, r.ro_r)
        r.ro_dst[h] = r.ro_src[h]

        if inside:
            red1, red2, red3 = Reduce("r1", 3), Reduce("r2", 3), Reduce("r3", 1)
            acc1, acc2, acc3 = r.r1_acc, r.r2_acc, r.r3_acc
        else:
            acc1, acc2, acc3 = r.first, r.second, r.attend

        transposed_wait("ai_t")
        for k in range(2):
            copy = att_t_copy(1 - c, k)
            copy.wait_recv()
            copy.wait_send()
        attend_out = dot(rows_of(r.ai_t), proj_rows())
        output_out = dot(rows_of(r.att_t), cot_all())
        for p, zc in enumerate(ALL):
            for yy in range(2):
                for xx in range(2):
                    row = p * BLK + yy * 48
                    tiles = [
                        attend_out[row : row + 48, (xx * 3 + j) * 128 : (xx * 3 + j) * 128 + 128] for j in range(3)
                    ]
                    acc3[0, slot(xx, yy), zc] = pack_four(
                        *tiles, output_out[row : row + 48, xx * 128 : xx * 128 + 128]
                    )
        if inside:
            red3.start(0)

        def proj_sums(i, carry):
            q = jnp.concatenate([r.dproj[0, rows(i), :], r.dproj[1, rows(i), :]], axis=1).astype(F32)
            val = jnp.concatenate([r.dproj[4, rows(i), :], r.dproj[5, rows(i), :]], axis=1).astype(F32)
            return (carry[0] + fold(q), carry[1] + fold(val), carry[2] + fold(r.cx[i].astype(F32)))

        qsum, vsum, csum = lax.fori_loop(0, 4, proj_sums, (zero8, zero8, zero8))
        r.sums[pl.ds(3 + 7, 1), :] = jnp.sum(qsum, axis=0, keepdims=True)
        r.sums[pl.ds(3 + 8, 1), :] = jnp.sum(vsum, axis=0, keepdims=True)
        r.sums[pl.ds(3 + 9, 1), :] = jnp.sum(csum, axis=0, keepdims=True)
        r.sums[pl.ds(13, 3), :] = jnp.zeros((3, HALF), F32)

        def n3_own(i, carry):
            vals = n3.get(i)
            r.gtmp[rows(i), :] = vals
            return carry[0] + fold(vals), carry[1] + fold(vals * hat3(i))

        n3.wait()
        sums3 = lax.fori_loop(0, 4, n3_own, (zero8, zero8))
        plain3, cross3, back3 = norm_back(sums3, lambda i: r.gtmp[rows(i), :], hat3, gain3, inv3)
        r.sums[pl.ds(2, 1), :] = cross3
        r.sums[pl.ds(3 + 2, 1), :] = plain3

        def shifted(buf, i, vals):
            buf[0, rows(i, CHUNK, ROW), :] = from_right(vals).astype(BF16)
            buf[1, rows(i, CHUNK, ROW), :] = vals.astype(BF16)
            buf[2, rows(i, CHUNK, ROW), :] = from_left(vals).astype(BF16)

        def residual_back(i, carry):
            vals = r.cx[i].astype(F32) + back3(i)
            r.gres[rows(i), :] = vals
            shifted(r.gr2, i, vals)
            return carry + fold(vals.astype(BF16).astype(F32))

        bias_two = lax.fori_loop(0, 4, residual_back, jnp.zeros((8, HALF), F32))
        r.sums[pl.ds(3 + 4, 1), :] = jnp.sum(bias_two, axis=0, keepdims=True)

        def act_back(buf, g, core):
            left = jnp.concatenate(
                [buf[b, pl.ds(2 * ROW - ROW * a, PX), :] for a in range(3) for b in range(3)], axis=1
            )
            right = jnp.concatenate(
                [wtap(g, 3 * a + b, half_of(core)) for a in range(3) for b in range(3)], axis=1
            )
            return dot_nt(left, right)

        def conv_back(parts, buf, g):
            parts.both(lambda core: act_back(buf, g, core))

        def conv_back_own(parts, outer, hat):
            parts.wait()

            def own(i, carry):
                grad = parts.get(i) * outer(i)
                r.gtmp[rows(i), :] = grad
                return carry[0] + fold(grad), carry[1] + fold(grad * hat(i))

            return lax.fori_loop(0, 4, own, (zero8, zero8))

        def kernel_grad(act_t, buf, acc, after):
            def step(a):
                right = jnp.concatenate([buf[b, pl.ds(2 * ROW - ROW * a, PX), :] for b in range(3)], axis=1)
                out = dot(rows_of(act_t), right)
                for p, zc in enumerate(ALL):
                    for yy in range(2):
                        for xx in range(2):
                            row = p * BLK + yy * 48
                            tiles = [
                                out[row : row + 48, b * HALF + xx * 128 : b * HALF + xx * 128 + 128] for b in range(3)
                            ]
                            acc[a, slot(xx, yy), zc] = pack_taps(*tiles)
                after(a)

            each(3, step)

        serve = inside
        d2 = Parts("d2")
        transposed_wait("act2_t")
        kernel_grad(r.act2_t, r.gr2, acc2, red2.start if inside else lambda a: None)
        if serve:
            red3.second(0, 1)
        conv_back(d2, r.gr2, k2)
        if serve:
            red2.second(0, 1)
        sums2 = conv_back_own(d2, lambda i: silu_slope(pre2(i)), hat2)
        if serve:
            red2.second(1, 1)
            red3.third(0, 1)

        plain2, cross2, back2 = norm_back(sums2, lambda i: r.gtmp[rows(i), :], hat2, gain2 * scale, inv2)
        r.sums[pl.ds(1, 1), :] = scale * cross2
        r.sums[pl.ds(3 + 1, 1), :] = scale * plain2
        film_scale_term = gain2 * cross2 + shift2 * plain2
        r.sums[pl.ds(3 + 5, 1), :] = film_scale_term
        r.sums[pl.ds(3 + 6, 1), :] = plain2
        for j in range(2):
            r.ft[j] = film_scale_term[:, j * 128 : j * 128 + 128]
            r.ft[2 + j] = plain2[:, j * 128 : j * 128 + 128]
        head_start(lambda p: r.ft.at[p], r.th, r.th_s, r.th_r)
        r.th[h] = r.ft[h]

        def first_back(i, carry):
            vals = back2(i)
            shifted(r.gr1, i, vals)
            return carry + fold(vals.astype(BF16).astype(F32))

        bias_one = lax.fori_loop(0, 4, first_back, jnp.zeros((8, HALF), F32))
        r.sums[pl.ds(3 + 3, 1), :] = jnp.sum(bias_one, axis=0, keepdims=True)

        if serve:
            red2.second(2, 1)
            red2.third(0, 1)
            red2.third(1, 1)

        head_wait(lambda p: r.ft.at[p], r.th, r.th_s, r.th_r)
        for m in range(2):
            r.fa[d, pl.ds(m, 1), :] = jnp.concatenate([r.th[2 * m], r.th[2 * m + 1]], axis=1)
        dp_start(lambda p: r.fa.at[d], r.fa, r.fa_s, r.fa_r)

        d1 = Parts("d1")

        def after_chunk(a):
            if serve:
                red1.start(a)
                if a == 1:
                    red2.third(2, 1)

        transposed_wait("act1_t")
        kernel_grad(r.act1_t, r.gr1, acc1, after_chunk)
        conv_back(d1, r.gr1, k1)
        if serve:
            red1.second(0, 1)

        dp_wait(lambda p: r.fa.at[d], r.fa, r.fa_s, r.fa_r)
        for j in range(n):
            r.fta[pl.ds(2 * j, 2), :] = r.fa[j]
        film_block = dot_tn_high(r.esel[...], r.fta[...])
        r.film[...] = jnp.concatenate([film_block[:film_rows, :BLK], film_block[:film_rows, 128 : 128 + BLK]], axis=1)
        embed_part = dot_nt_high(r.fta[...], r.wfp[...].astype(F32))
        for j in range(n):
            r.ep[j] = embed_part[2 * j : 2 * j + 2]
        dp_start(lambda p: r.ep.at[p], r.er, r.er_s, r.er_r)
        r.er[d] = r.ep[d]

        def hat1(i):
            return (mixed(i) - mean1) * inv1

        sums1 = conv_back_own(d1, lambda i: silu_slope(pre1(i)), hat1)
        if serve:
            red1.second(1, 1)

        dp_wait(lambda p: r.ep.at[p], r.er, r.er_s, r.er_r)
        r.eh[h] = r.er[...]
        head_start(lambda p: r.eh.at[h], r.eh, r.eh_s, r.eh_r)
        plain1, cross1, back1 = norm_back(sums1, lambda i: r.gtmp[rows(i), :], hat1, gain1, inv1)
        r.sums[pl.ds(0, 1), :] = cross1
        r.sums[pl.ds(3, 1), :] = plain1
        r.ad[d] = r.sums[...]
        dp_start(lambda p: r.ad.at[d], r.ad, r.ad_s, r.ad_r)

        if serve:
            red1.second(2, 1)
            red1.third(0, 1)
        keep, _ = plan(r.steps[x], HALF)

        def image_back(i):
            r.io_src[i] = pack_pixels(keep * (r.gres[rows(i), :] + back1(i))).astype(BF16)

        loop(4, image_back)
        head_start(lambda p: r.io_src.at[p], r.io_dst, r.io_s, r.io_r)
        r.io_dst[h] = r.io_src[h]
        if serve:
            red1.third(1, 1)
            red1.third(2, 1)

        dp_wait(lambda p: r.ad.at[d], r.ad, r.ad_s, r.ad_r)
        total = r.ad[0]
        for j in range(1, n):
            total = total + r.ad[j]
        r.hb[h] = total
        head_start(lambda p: r.hb.at[h], r.hb, r.hb_s, r.hb_r)
        head_wait(lambda p: r.ro_src.at[p], r.ro_dst, r.ro_s, r.ro_r)

        if inside:
            red2.finish(((0, 1), (1, 1), (2, 1)))
            for a in range(3):
                r.second[a] = red2.last(a)

        head_wait(lambda p: r.hb.at[h], r.hb, r.hb_s, r.hb_r)
        even = r.hb[0] + r.hb[2]
        odd = r.hb[1] + r.hb[3]
        wide = jnp.concatenate(
            [even[:, :BLK], odd[:, :BLK], even[:, 128 : 128 + BLK], odd[:, 128 : 128 + BLK]], axis=1
        )
        r.gains_out[...] = wide[0:3]
        r.biases_out[...] = wide[3:13]

        head_wait(lambda p: r.eh.at[h], r.eh, r.eh_s, r.eh_r)
        pieces = []
        for j in range(n):
            piece = (r.eh[0, j] + r.eh[1, j]) + (r.eh[2, j] + r.eh[3, j])
            pieces.append(piece[:, :film_rows])
        r.embed_grad[...] = jnp.concatenate(pieces, axis=1) * silu_slope(r.emb[...].astype(F32))

        head_wait(lambda p: r.io_src.at[p], r.io_dst, r.io_s, r.io_r)

        if inside:
            red3.finish(((0, 1),))
            tiles = unpack_four(red3.last(0))
            r.sb_src[...] = jnp.where(c == 0, tiles[2], tiles[0])
            back = rc(r.sb_src, r.sb_dst, r.sb_s.at[0], r.sb_r.at[0], sib)
            back.start()
            r.output[...] = tiles[3]
            for part in (ga, gb, gc):
                part.finish()
            red1.finish(((0, 1), (1, 1), (2, 1)))
            for a in range(3):
                r.first[a] = red1.last(a)
            back.wait()
            r.attend[:, 0:128] = jnp.where(c == 0, tiles[0], tiles[1])
            r.attend[:, 128:256] = r.sb_dst[...]
            r.attend[:, 256:384] = jnp.where(c == 0, tiles[1], tiles[2])

    return kernel


def make_writer(names_in, names_out):
    def kernel(*refs):
        count, wide = len(names_in), len(names_out)
        far_in, far_out = refs[:count], refs[count : count + wide]
        near_in, near_out = refs[count + wide : 2 * count + wide], refs[2 * count + wide : 2 * count + 2 * wide]
        sem_in, sem_out = refs[-2:]
        src, dst = Names(names_in, near_in), Names(names_out, near_out)
        loads = {
            name: pltpu.make_async_copy(far_in[i], near_in[i], sem_in.at[i]) for i, name in enumerate(names_in)
        }
        stores = {
            name: pltpu.make_async_copy(near_out[i], far_out[i], sem_out.at[i]) for i, name in enumerate(names_out)
        }
        for name in ("sel", "ro_dst", "io_dst"):
            loads[name].start()
        for name in names_in:
            if name not in ("sel", "ro_dst", "io_dst"):
                loads[name].start()
        loads["sel"].wait()
        for name, packed in (("result", "ro_dst"), ("image_grad", "io_dst")):
            loads[packed].wait()
            ref = getattr(src, packed)
            for m in range(2):
                getattr(dst, name)[m] = dot_nt(unpack_pixels(ref[2 * m]), src.sel[0]) + dot_nt(
                    unpack_pixels(ref[2 * m + 1]), src.sel[1]
                )
            stores[name].start()
        for name in ("first", "second"):
            if name in names_out:
                loads[name].wait()
                for a in range(3):
                    block = getattr(src, name)[a]
                    getattr(dst, name)[3 * a] = block[:48, :BLK]
                    getattr(dst, name)[3 * a + 1] = block[48:96, :BLK]
                    getattr(dst, name)[3 * a + 2] = last_tap(block)[:, :BLK]
                stores[name].start()
        if "attend" in names_out:
            loads["attend"].wait()
            dst.attend[...] = jnp.concatenate([src.attend[:, j * 128 : j * 128 + BLK] for j in range(3)], axis=1)
            stores["attend"].start()
            loads["output"].wait()
            dst.output[...] = src.output[:, :BLK]
            stores["output"].start()
        for name in ("embed_grad", "film", "gains_out", "biases_out"):
            loads[name].wait()
            getattr(dst, name)[...] = getattr(src, name)[...]
            stores[name].start()
        for name in names_out:
            stores[name].wait()

    return kernel


def per_device(n, *args):
    (
        images,
        noise_field,
        time_steps,
        embedding,
        first_kernel,
        second_kernel,
        film_weight,
        attend_weight,
        output_weight,
        norm_gains,
        biases,
        cotangent,
    ) = args
    inside = n == 8
    maps, height, width, channels = images.shape
    flat_shape = (maps, height * width, channels)
    film_rows = film_weight.shape[0]
    inputs = dict(
        steps=time_steps,
        images=images.reshape(flat_shape),
        noise=noise_field.reshape(flat_shape),
        cot=cotangent.reshape(flat_shape),
        emb=embedding,
        k1=first_kernel.reshape((9,) + first_kernel.shape[2:]),
        k2=second_kernel.reshape((9,) + second_kernel.shape[2:]),
        wf=film_weight,
        wa=attend_weight,
        wo=output_weight,
        gains=norm_gains,
        biases=biases,
        sel=jnp.asarray(channel_lanes(), BF16),
        gmask=jnp.asarray(group_mask(), BF16),
        selp=jnp.asarray(block_lanes(3), BF16),
    )
    shapes = dict(
        ro_dst=(4, 384, 128),
        io_dst=(4, 384, 128),
        embed_grad=embedding.shape,
        first=(3, 112, 128),
        second=(3, 112, 128),
        film=film_weight.shape,
        attend=(48, 384),
        output=(48, 128),
        gains_out=norm_gains.shape,
        biases_out=biases.shape,
    )
    names_in, names_out = list(INPUTS), list(OUTPUTS)
    core = lax.axis_index("head") % 2
    if not inside:
        def whole(array, row_axis):
            array = lax.all_gather(array, "dp", axis=row_axis, tiled=True)
            return lax.all_gather(array, "head", axis=array.ndim - 1, tiled=True)

        def spread(array, count):
            taps = array.shape[0]
            array = array.reshape(taps, 4, 2, 48, 2, 2, BLK)
            array = lax.dynamic_index_in_dim(array, core, 5, keepdims=False)
            array = jnp.transpose(array, (2, 4, 1, 0, 3, 5))
            array = jnp.pad(array, ((0, 0),) * 5 + ((0, 32),))
            return array.reshape(4, 4, taps * 48, 128)

        full_a = whole(attend_weight, 0).reshape(384, 2, 3, 2, BLK)
        full_a = jnp.transpose(full_a, (2, 0, 1, 3, 4)).reshape(3, 384, 384)
        full_o = whole(output_weight, 0)[None]
        for name, last, array in (("g1", "t1", first_kernel), ("g2", "t2", second_kernel)):
            blocks = spread(whole(array, 2).reshape(9, 384, 384), 9).reshape(4, 4, 3, 3, 48, 128)
            two = blocks[:, :, :, :2].reshape(4, 4, 3, 96, 128)
            inputs[name] = jnp.pad(two, ((0, 0),) * 3 + ((0, 16), (0, 0))).reshape(4, 4, 336, 128)
            inputs[last] = blocks[:, :, :, 2].reshape(4, 4, 144, 128)
        inputs["g3"] = spread(jnp.concatenate([full_a, full_o], axis=0), 4)
        names_in += ["g1", "g2", "t1", "t2", "g3"]
        shapes["first"] = shapes["second"] = (3, 4, 4, 112, 128)
        shapes["attend"] = (1, 4, 4, 144, 128)
        del shapes["output"]
        names_out.remove("output")
    items = scratch_list(n, inside)
    smem = pl.BlockSpec(memory_space=pltpu.SMEM)
    vmem = pl.BlockSpec(memory_space=pltpu.VMEM)
    outs = pl.pallas_call(
        make_kernel(n, inside, names_in + names_out + [name for name, _ in items]),
        out_shape=[
            jax.ShapeDtypeStruct(shapes[name], BF16 if name in ("ro_dst", "io_dst") else F32) for name in names_out
        ],
        in_specs=[smem if name == "steps" else vmem for name in names_in],
        out_specs=[vmem] * len(names_out),
        scratch_shapes=[item for _, item in items],
        compiler_params=pltpu.CompilerParams(
            collective_id=0, has_side_effects=True, vmem_limit_bytes=63 * 1024 * 1024
        ),
        name="blocks",
    )(*[inputs[name] for name in names_in])
    raw = dict(zip(names_out, outs))
    final = dict(
        result=flat_shape,
        image_grad=flat_shape,
        embed_grad=embedding.shape,
        film=film_weight.shape,
        gains_out=norm_gains.shape,
        biases_out=biases.shape,
    )
    if inside:
        final.update(first=(9, 48, BLK), second=(9, 48, BLK), attend=attend_weight.shape, output=output_weight.shape)
    names_last = [name for name in names_out if inside or name not in ("first", "second", "attend")] + ["sel"]
    names_final = list(final)
    given = [inputs["sel"] if name == "sel" else raw[name] for name in names_last]
    far = pl.BlockSpec(memory_space=pl.ANY)
    outs = pl.pallas_call(
        make_writer(names_last, names_final),
        out_shape=[jax.ShapeDtypeStruct(final[name], F32) for name in names_final],
        in_specs=[far] * len(names_last),
        out_specs=[far] * len(names_final),
        scratch_shapes=[pltpu.VMEM(array.shape, array.dtype) for array in given]
        + [pltpu.VMEM(final[name], F32) for name in names_final]
        + [pltpu.SemaphoreType.DMA((len(names_last),)), pltpu.SemaphoreType.DMA((len(names_final),))],
        compiler_params=pltpu.CompilerParams(vmem_limit_bytes=63 * 1024 * 1024),
        name="outputs",
    )(*given)
    out = dict(zip(names_final, outs))
    if not inside:

        def blocks_of(array, size):
            parts = [array[..., k * 48 : k * 48 + 48, :BLK] for k in range(size)]
            if size == 2:
                lanes = [array[..., k * 32 : k * 32 + 32, BLK:] for k in range(3)]
                lanes = jnp.concatenate(lanes, axis=-1)
                parts.append(jnp.concatenate([lanes, array[..., 96:112, :BLK]], axis=-2))
            else:
                lanes = [array[..., k * 48 : k * 48 + 48, BLK:] for k in range(3)]
                parts.append(jnp.concatenate(lanes, axis=-1))
            array = jnp.stack(parts, axis=1)
            array = array.reshape(array.shape[:2] + (2, 2, 4, 48, BLK))
            taps = array.shape[0] * array.shape[1]
            array = jnp.transpose(array, (0, 1, 4, 2, 5, 3, 6)).reshape(taps, 384, 2, 1, BLK)
            both = jnp.concatenate([array, jnp.zeros_like(array)], axis=3)
            return jnp.where(core == 0, both, both[:, :, :, ::-1]).reshape(taps, 384, 384)

        def shared(array, axis):
            array = lax.psum_scatter(array, "head", scatter_dimension=array.ndim - 1, tiled=True)
            return lax.psum_scatter(array, "dp", scatter_dimension=axis, tiled=True)

        out["first"] = shared(blocks_of(raw["first"], 2), 1)
        out["second"] = shared(blocks_of(raw["second"], 2), 1)
        both = blocks_of(raw["attend"], 3)
        joined = both[:3].reshape(3, 384, 2, 2, BLK)
        joined = jnp.transpose(joined, (1, 2, 0, 3, 4)).reshape(384, 1152)
        out["attend"] = shared(joined, 0)
        out["output"] = shared(both[3], 0)
    return (
        out["result"].reshape(images.shape),
        out["image_grad"].reshape(images.shape),
        out["embed_grad"],
        out["first"].reshape(first_kernel.shape),
        out["second"].reshape(second_kernel.shape),
        out["film"],
        out["attend"],
        out["output"],
        out["gains_out"],
        out["biases_out"],
    )


def solution(mesh):
    n = mesh.shape["dp"]
    field = P("dp", "head", None, None)
    taps = P(None, None, "dp", "head")
    both = P("dp", "head")
    return jax.shard_map(
        lambda *args: per_device(n, *args),
        mesh=mesh,
        in_specs=(field, field, P("dp"), P("dp", None), taps, taps, both, both, both, P(), P(), field),
        out_specs=(field, field, P("dp", None), taps, taps, both, both, both, P(), P()),
        check_vma=False,
    )
```

```python
import math

import jax
import jax.numpy as jnp
import numpy as np
from jax import lax
from jax.experimental import pallas as pl
from jax.experimental.pallas import tpu as pltpu
from jax.sharding import PartitionSpec as P

HEAD_DIM = 96
GROUPS = 32
STEPS = 4000
EPS = 1e-05
OFFSET = 0.008
MESH = pl.DeviceIdType.MESH
F32 = jnp.float32
BF16 = jnp.bfloat16

PX = 1024
ROW = 32
CHUNK = 256
BLK = 96
HALF = 256
NHEAD = 4


def plan(time_step, lanes):
    fraction = (jnp.full((1, lanes), time_step, jnp.int32).astype(F32) + 1.0) / STEPS
    start = math.cos(OFFSET / (1.0 + OFFSET) * (math.pi / 2)) ** 2
    curve = jnp.square(jnp.cos((fraction + OFFSET) / (1.0 + OFFSET) * (math.pi / 2))) / start
    return (jnp.sqrt(curve), jnp.sqrt(jnp.maximum(1.0 - curve, 0.0)))


def channel_lanes():
    sel = np.zeros((2, 384, HALF), np.float32)
    for block in range(4):
        for j in range(BLK):
            sel[block % 2, block * BLK + j, (block // 2) * 128 + j] = 1.0
    return sel


def block_lanes(count):
    sel = np.zeros((count * BLK, count * 128), np.float32)
    for block in range(count):
        for j in range(BLK):
            sel[block * BLK + j, block * 128 + j] = 1.0
    return sel


def group_mask():
    lane = np.arange(HALF)
    ok = lane % 128 < BLK
    group = (lane // 128) * 100 + (lane % 128) // 12
    return ((group[:, None] == group[None, :]) & ok[:, None] & ok[None, :]).astype(np.float32)


def dot(a, b):
    return lax.dot_general(a, b, (((1,), (0,)), ((), ())), preferred_element_type=F32)


def dot_nt(a, b):
    return lax.dot_general(a, b, (((1,), (1,)), ((), ())), preferred_element_type=F32)


def dot_nt_high(a, b):
    return lax.dot_general(
        a, b, (((1,), (1,)), ((), ())), preferred_element_type=F32, precision=lax.Precision.HIGHEST
    )


def dot_tn_high(a, b):
    return lax.dot_general(
        a, b, (((0,), (0,)), ((), ())), preferred_element_type=F32, precision=lax.Precision.HIGHEST
    )


def exact_dot(values, ones):
    high = values.astype(BF16).astype(F32)
    rest = values - high
    middle = rest.astype(BF16).astype(F32)
    low = rest - middle
    rows = values.shape[0]
    out = dot(jnp.concatenate([high, middle, low], axis=0).astype(BF16), ones)
    return out[:rows] + out[rows : 2 * rows] + out[2 * rows :]


def sigmoid(v):
    return 0.5 + 0.5 * jnp.tanh(0.5 * v)


def silu(v):
    return v * sigmoid(v)


def silu_slope(v):
    s = sigmoid(v)
    return s * (1.0 + v * (1.0 - s))


def pack_taps(t0, t1, t2):
    t0, t1, t2 = t0[:, :BLK], t1[:, :BLK], t2[:, :BLK]
    join = lambda a, b: jnp.concatenate([a, b], axis=1)
    return jnp.concatenate(
        [
            join(t0[:32], t2[:32, :32]),
            join(t0[32:], t2[:16, 32:64]),
            join(t1[:16], t2[16:32, 32:64]),
            join(t1[16:], t2[:32, 64:]),
            join(t2[32:], jnp.zeros((16, 32), t2.dtype)),
        ],
        axis=0,
    )


def last_tap(packed):
    lanes = [packed[:32, BLK:], packed[32:64, BLK:], packed[64:96, BLK:], jnp.zeros((32, 32), packed.dtype)]
    return jnp.concatenate([jnp.concatenate(lanes, axis=1), packed[96:112]], axis=0)


def pack_four(b0, b1, b2, b3):
    return jnp.concatenate(
        [jnp.concatenate([b[:, :BLK], b3[:, 32 * k : 32 * k + 32]], axis=1) for k, b in enumerate((b0, b1, b2))],
        axis=0,
    )


def unpack_four(packed):
    size = packed.shape[0] // 3
    parts = [packed[k * size : k * size + size] for k in range(3)]
    zero = jnp.zeros((size, 32), packed.dtype)
    fourth = jnp.concatenate([p[:, BLK:] for p in parts] + [zero], axis=1)
    return [jnp.concatenate([p[:, :BLK], zero], axis=1) for p in parts] + [fourth]


def pack_pixels(full):
    half = CHUNK // 2
    return pack_four(full[:half, :128], full[half:, :128], full[:half, 128:], full[half:, 128:])


def unpack_pixels(packed):
    b0, b1, b2, b3 = unpack_four(packed)
    return jnp.concatenate([jnp.concatenate([b0, b2], axis=1), jnp.concatenate([b1, b3], axis=1)], axis=0)


INPUTS = (
    "steps",
    "images",
    "noise",
    "cot",
    "emb",
    "k1",
    "k2",
    "wf",
    "wa",
    "wo",
    "gains",
    "biases",
    "sel",
    "gmask",
    "selp",
)
OUTPUTS = (
    "ro_dst",
    "io_dst",
    "embed_grad",
    "first",
    "second",
    "film",
    "attend",
    "output",
    "gains_out",
    "biases_out",
)


FAR = (
    "images",
    "noise",
    "cot",
    "sel",
    "selp",
    "k2",
    "wa",
    "wf",
    "gmask",
)


class Names:
    def __init__(self, names, refs):
        for name, ref in zip(names, refs):
            setattr(self, name, ref)


def scratch_list(n, inside, inputs):
    dma = pltpu.SemaphoreType.DMA
    items = []

    def vm(name, shape, dtype):
        items.append((name, pltpu.VMEM(shape, dtype)))

    def sem(name, count):
        items.append((name + "_s", dma((count,))))
        items.append((name + "_r", dma((count,))))

    for name in FAR:
        vm(name, inputs[name].shape, inputs[name].dtype)
    items.append(("far_s", dma((len(FAR),))))
    for name in ("mx", "cx", "ro", "io"):
        vm(name + "_src", (4, 384, 128), BF16)
        if name in ("mx", "cx"):
            vm(name + "_dst", (4, 384, 128), BF16)
            vm(name, (4, CHUNK, HALF), BF16)
        sem(name, 4)
    for name in ("act1", "act2"):
        vm(name, (2, PX + 2 * ROW, HALF), BF16)
        vm(name + "_t", (2, HALF, PX), BF16)
        sem(name, 4)
        sem(name + "_t", 1)
    vm("ai", (2, PX, HALF), BF16)
    vm("ai_t", (2, HALF, PX), BF16)
    sem("ai_t", 1)
    sem("ai", 4)
    vm("att", (4, PX, 128), BF16)
    vm("att_t", (2, HALF, PX), BF16)
    sem("att", 4)
    for name in ("do", "n3", "d2", "d1"):
        vm(name + "_src", (PX, HALF), BF16)
        vm(name + "_dst", (PX, HALF), BF16)
        sem(name, 2)
    vm("v2", (PX, HALF), F32)
    vm("v3", (PX, HALF), F32)
    vm("gres", (PX, HALF), F32)
    vm("gtmp", (PX, HALF), F32)
    vm("qkv", (6, PX, 128), BF16)
    vm("kvt", (4, 128, PX), BF16)
    vm("dout", (2, PX, 128), BF16)
    vm("dproj", (6, PX, 128), BF16)
    vm("gr2", (3, PX + 2 * ROW, HALF), BF16)
    vm("gr1", (3, PX + 2 * ROW, HALF), BF16)
    vm("par", (16, 384), F32)
    vm("parown", (16, HALF), F32)
    vm("stat", (16, HALF), F32)
    vm("sums", (16, HALF), F32)
    if inside:
        vm("g1", (4, 4, 336, 128), BF16)
        vm("g2", (4, 4, 336, 128), BF16)
        vm("t1", (4, 4, 144, 128), BF16)
        vm("t2", (4, 4, 144, 128), BF16)
        vm("p3", (4, 4, 144, 128), BF16)
        vm("g3", (4, 4, 192, 128), BF16)
        for name in ("g1", "g2", "p3"):
            sem(name + "z", 4)
            sem(name + "v", 4)
            sem(name + "w", 8)
        vm("sw_src", (48, 128), BF16)
        vm("sw_dst", (48, 128), BF16)
        sem("sw", 1)
        vm("sb_src", (48, 128), F32)
        vm("sb_dst", (48, 128), F32)
        sem("sb", 1)
        for name, nc, rows in (("r1", 3, 112), ("r2", 3, 112), ("r3", 1, 144)):
            vm(name + "_acc", (nc, 4, 4, rows, 128), BF16)
            vm(name + "_own", (nc, rows, 128), F32)
            vm(name + "w_dst", (nc, 2, 4, rows, 128), BF16)
            vm(name + "v_src", (nc, 4, rows, 128), BF16)
            vm(name + "v_dst", (nc, 4, rows, 128), BF16)
            vm(name + "z_src", (4, nc, rows, 128), BF16)
            vm(name + "z_dst", (4, nc, rows, 128), BF16)
            sem(name + "w", nc)
            sem(name + "v", nc)
            sem(name + "z", nc * 4)
    vm("el", (n, 2, 768), F32)
    sem("el", n)
    vm("em", (2 * n, 768), F32)
    vm("wfp", (128, HALF), BF16)
    vm("esel", (2 * n, 128), F32)
    vm("fp", (n, 2, HALF), F32)
    vm("fr", (n, 2, HALF), F32)
    sem("fr", n)
    vm("fx", (4, 1, 128), F32)
    vm("fh", (4, 1, 128), F32)
    sem("fh", 4)
    vm("ft", (4, 1, 128), F32)
    vm("th", (4, 1, 128), F32)
    sem("th", 4)
    vm("fa", (n, 2, HALF), F32)
    sem("fa", n)
    vm("fta", (2 * n, HALF), F32)
    vm("ep", (n, 2, 128), F32)
    vm("er", (n, 2, 128), F32)
    sem("er", n)
    vm("eh", (4, n, 2, 128), F32)
    sem("eh", 4)
    vm("ad", (n, 16, HALF), F32)
    sem("ad", n)
    vm("hb", (4, 16, HALF), F32)
    sem("hb", 4)
    return items


def make_kernel(n, inside, names):
    film_rows = 768 // n

    def kernel(*refs):
        r = Names(names, refs)
        d = lax.axis_index("dp")
        h = lax.axis_index("head")
        x = h // 2
        c = h - 2 * x
        z = d // 2
        y = d - 2 * z
        sib = (d, h + 1 - 2 * c)
        xdev = (d, h + 2 - 4 * x)
        v = x + c * (y - x)
        w = y + c * (x - y)
        vdev = (d + c * (1 - 2 * y), h + (1 - c) * (2 - 4 * x))
        wdev = (d + (1 - c) * (1 - 2 * y), h + c * (2 - 4 * x))

        def slot(xx, yy):
            if inside:
                return (yy + c * (xx - yy)) * 2 + xx + c * (yy - xx)
            return yy * 2 + xx

        def rc(src, dst, send, recv, dev):
            return pltpu.make_async_remote_copy(
                src_ref=src, dst_ref=dst, send_sem=send, recv_sem=recv, device_id=dev, device_id_type=MESH
            )

        def loop(count, body):
            def step(i, carry):
                body(i)
                return carry

            lax.fori_loop(0, count, step, 0)

        def each(count, body):
            for i in range(count):
                body(i)

        def rows(i, size=CHUNK, base=0):
            return pl.ds(pl.multiple_of(base + i * size, 32), size)

        def dp_start(src_of, dst, send, recv):
            def step(k, carry):
                peer = lax.rem(d + k, n)
                rc(src_of(peer), dst.at[d], send.at[k], recv.at[d], (peer, h)).start()
                return carry

            lax.fori_loop(1, n, step, 0)

        def dp_wait(src_of, dst, send, recv):
            def step(k, carry):
                peer = lax.rem(d + k, n)
                copy = rc(src_of(peer), dst.at[peer], send.at[k], recv.at[peer], (peer, h))
                copy.wait_recv()
                copy.wait_send()
                return carry

            lax.fori_loop(1, n, step, 0)

        def head_start(src_of, dst, send, recv):
            for k in range(1, 4):
                peer = lax.rem(h + k, 4)
                rc(src_of(peer), dst.at[h], send.at[k], recv.at[h], (d, peer)).start()

        def head_wait(src_of, dst, send, recv):
            for k in range(1, 4):
                peer = lax.rem(h + k, 4)
                copy = rc(src_of(peer), dst.at[peer], send.at[k], recv.at[peer], (d, peer))
                copy.wait_recv()
                copy.wait_send()

        class Halves:
            def __init__(self, name, base):
                self.buf, self.base = getattr(r, name), base
                self.send, self.recv = getattr(r, name + "_s"), getattr(r, name + "_r")

            def at(self, core, i):
                return self.buf.at[core, rows(i, CHUNK, self.base)]

            def fill(self, make):
                def body(i):
                    self.buf[c, rows(i, CHUNK, self.base), :] = make(i)
                    ref = self.at(c, i)
                    rc(ref, ref, self.send.at[i], self.recv.at[i], sib).start()

                loop(4, body)

            def wait(self):
                for i in range(4):
                    ref = self.at(1 - c, i)
                    copy = rc(ref, ref, self.send.at[i], self.recv.at[i], sib)
                    copy.wait_recv()
                    copy.wait_send()

        class Parts:
            def __init__(self, name):
                self.src, self.dst = getattr(r, name + "_src"), getattr(r, name + "_dst")
                self.send, self.recv = getattr(r, name + "_s"), getattr(r, name + "_r")

            def copy(self, i):
                at = rows(i, 2 * CHUNK)
                return rc(self.src.at[at], self.dst.at[at], self.send.at[i], self.recv.at[i], sib)

            def fill(self, make):
                def body(i):
                    self.src[rows(i, 2 * CHUNK), :] = make(i).astype(BF16)
                    self.copy(i).start()

                each(2, body)

            def get(self, i):
                copy = self.copy(i)
                copy.wait_recv()
                copy.wait_send()
                return self.dst[rows(i, 2 * CHUNK), :].astype(F32)

        class Gather:
            def __init__(self, name):
                self.g = getattr(r, name)
                self.zs, self.zr = getattr(r, name + "z_s"), getattr(r, name + "z_r")
                self.vs, self.vr = getattr(r, name + "v_s"), getattr(r, name + "v_r")
                self.ws, self.wr = getattr(r, name + "w_s"), getattr(r, name + "w_r")

            def zcopy(self, k):
                peer = (lax.rem(z + k, 4) * 2 + y, h)
                return rc(
                    self.g.at[w * 2 + v, 0], self.g.at[w * 2 + v, 4 - k], self.zs.at[k], self.zr.at[4 - k], peer
                )

            def vcopy(self, vv, i):
                ref = self.g.at[w * 2 + vv, i]
                return rc(ref, ref, self.vs.at[i], self.vr.at[i], vdev)

            def wcopy(self, ww, other, i):
                ref = self.g.at[ww * 2 + v + other * (1 - 2 * v), i]
                return rc(ref, ref, self.ws.at[2 * i + other], self.wr.at[2 * i + other], wdev)

            def own(self):
                for k in range(1, 4):
                    self.zcopy(k).start()
                self.vcopy(v, 0).start()
                self.wcopy(w, 0, 0).start()

            def pass_own(self):
                self.vcopy(1 - v, 0).wait_recv()
                self.wcopy(w, 1, 0).start()

            def pass_z(self, *ks):
                for k in ks:
                    self.zcopy(k).wait_recv()
                    self.vcopy(v, 4 - k).start()
                    self.wcopy(w, 0, 4 - k).start()

            def pass_v(self, *ks):
                for k in ks:
                    self.vcopy(1 - v, 4 - k).wait_recv()
                    self.wcopy(w, 1, 4 - k).start()

            def done(self):
                for i in range(4):
                    for other in range(2):
                        self.wcopy(1 - w, other, i).wait_recv()

            def finish(self):
                for k in range(1, 4):
                    self.zcopy(k).wait_send()
                for i in range(4):
                    self.vcopy(v, i).wait_send()
                    for other in range(2):
                        self.wcopy(w, other, i).wait_send()

        class Reduce:
            def __init__(self, name, count):
                get = lambda tail: getattr(r, name + tail)
                self.acc, self.count = get("_acc"), count
                self.wdst, self.ws, self.wr, self.own = get("w_dst"), get("w_s"), get("w_r"), get("_own")
                self.vsrc, self.vdst, self.vs, self.vr = get("v_src"), get("v_dst"), get("v_s"), get("v_r")
                self.zsrc, self.zdst, self.zs, self.zr = get("z_src"), get("z_dst"), get("z_s"), get("z_r")

            def wcopy(self, a):
                ref = self.acc.at[a, pl.ds((1 - w) * 2, 2)]
                return rc(ref, self.wdst.at[a], self.ws.at[a], self.wr.at[a], wdev)

            def vcopy(self, a, size):
                at = pl.ds(a, size)
                return rc(self.vsrc.at[at], self.vdst.at[at], self.vs.at[a], self.vr.at[a], vdev)

            def zcopy(self, a, size, k):
                at = pl.ds(a, size)
                return rc(
                    self.zsrc.at[k, at],
                    self.zdst.at[4 - k, at],
                    self.zs.at[a * 4 + k],
                    self.zr.at[a * 4 + 4 - k],
                    (lax.rem(z + k, 4) * 2 + y, h),
                )

            def start(self, a):
                self.wcopy(a).start()

            def second(self, first, size):
                for a in range(first, first + size):
                    self.wcopy(a).wait_recv()

                    def step(zz, carry):
                        self.vsrc[a, zz] = (
                            self.acc[a, w * 2 + 1 - v, zz].astype(F32) + self.wdst[a, 1 - v, zz].astype(F32)
                        ).astype(BF16)
                        return carry

                    lax.fori_loop(0, 4, step, 0)
                self.vcopy(first, size).start()

            def third(self, first, size):
                self.vcopy(first, size).wait_recv()
                for a in range(first, first + size):

                    for k in range(4):
                        zz = lax.rem(z + k, 4)
                        total = (
                            self.acc[a, w * 2 + v, zz].astype(F32)
                            + self.wdst[a, v, zz].astype(F32)
                            + self.vdst[a, zz].astype(F32)
                        )
                        if k == 0:
                            self.own[a] = total
                        else:
                            self.zsrc[k, a] = total.astype(BF16)
                for k in range(1, 4):
                    self.zcopy(first, size, k).start()

            def finish(self, groups):
                for first, size in groups:
                    self.vcopy(first, size).wait_send()
                    for k in range(1, 4):
                        copy = self.zcopy(first, size, k)
                        copy.wait_recv()
                        copy.wait_send()
                for a in range(self.count):
                    self.wcopy(a).wait_send()

            def last(self, a):
                total = self.own[a]
                for k in range(1, 4):
                    total = total + self.zdst[k, a].astype(F32)
                return total

        def rel(zc):
            return lax.rem(zc - z + 4, 4) if inside else zc

        class Taps:
            def __init__(self, packed, last):
                self.packed, self.last = packed, last

            def block(self, tap, zc, xx, yy):
                a, b = tap // 3, tap % 3
                if b < 2:
                    return self.packed[slot(xx, yy), rel(zc), pl.ds(a * 112 + b * 48, 48), :]
                return self.last[slot(xx, yy), rel(zc), pl.ds(a * 48, 48), :]

            def unpack(self, ww):
                def step(i, carry):
                    q, zz = ww * 2 + i // 4, lax.rem(i, 4)
                    for a in range(3):
                        self.last[q, zz, pl.ds(a * 48, 48), :] = last_tap(
                            self.packed[q, zz, pl.ds(a * 112, 112), :]
                        )
                    return carry

                lax.fori_loop(0, 8, step, 0)

        class Plain:
            def __init__(self, blocks):
                self.blocks = blocks

            def block(self, tap, zc, xx, yy):
                return self.blocks[slot(xx, yy), rel(zc), pl.ds(tap * 48, 48), :]

            def unpack(self, ww):
                def step(i, carry):
                    q, zz = ww * 2 + i // 4, lax.rem(i, 4)
                    self.blocks[q, zz] = jnp.concatenate(unpack_four(r.p3[q, zz]), axis=0)
                    return carry

                lax.fori_loop(0, 8, step, 0)

        k1, k2, k3 = Taps(r.g1, r.t1), Taps(r.g2, r.t2), Plain(r.g3)

        def wtile(g, tap, zc, xx):
            return jnp.concatenate(
                [g.block(tap, zc, xx, 0), g.block(tap, zc, xx, 1), jnp.zeros((32, 128), BF16)], axis=0
            )

        def wtap(g, tap, zcs):
            return jnp.concatenate(
                [jnp.concatenate([wtile(g, tap, zc, xx) for xx in range(2)], axis=1) for zc in zcs], axis=0
            )

        ALL = (0, 2, 1, 3)

        def half_of(core):
            return (core, core + 2)

        def wproj(zcs):
            return jnp.concatenate(
                [
                    jnp.concatenate([wtile(k3, j, zc, xx) for xx in range(2) for j in range(3)], axis=1)
                    for zc in zcs
                ],
                axis=0,
            )

        def flat(buf, base, i, size):
            return jnp.concatenate([buf[0, rows(i, size, base), :], buf[1, rows(i, size, base), :]], axis=1)

        barrier = pltpu.get_barrier_semaphore()

        def greet(k, carry):
            pl.semaphore_signal(barrier, inc=1, device_id=(lax.rem(d + k, n), h), device_id_type=MESH)
            return carry

        lax.fori_loop(1, n, greet, 0)
        for k in range(1, 4):
            pl.semaphore_signal(barrier, inc=1, device_id=(d, lax.rem(h + k, 4)), device_id_type=MESH)
        def fetch(name):
            return pltpu.make_async_copy(getattr(r, name + "_far"), getattr(r, name), r.far_s.at[FAR.index(name)])

        for name in FAR:
            fetch(name).start()
        if inside:
            for a in range(3):
                r.g1[w * 2 + v, 0, pl.ds(a * 112, 112), :] = pack_taps(*[r.k1[3 * a + b] for b in range(3)])
        pl.semaphore_wait(barrier, n - 1 + 3)
        if inside:
            ga, gb, gc = Gather("g1"), Gather("g2"), Gather("p3")
            ga.own()

        for name in FAR:
            fetch(name).wait()
        def head_copy(src, dst, send, recv, k):
            peer = lax.rem(h + k, 4)
            return rc(src.at[peer], dst.at[h], send.at[k], recv.at[h], (d, peer))

        for step in range(2):
            m = x + (1 - step) * (1 - 2 * x)
            keep, spread = plan(r.steps[m], 384)
            low = (keep * r.images[m].astype(F32) + spread * r.noise[m].astype(F32)).astype(BF16)
            for core in range(2):
                r.mx_src[m * 2 + core] = pack_pixels(dot(low, r.sel[core])).astype(BF16)
            for k in (2, 3 - 2 * c) if step == 0 else (1 + 2 * c,):
                head_copy(r.mx_src, r.mx_dst, r.mx_s, r.mx_r, k).start()
        r.mx_dst[h] = r.mx_src[h]
        if inside:
            ga.pass_own()

        r.el[d] = silu(r.emb[...].astype(F32)).astype(BF16).astype(F32)
        dp_start(lambda p: r.el.at[d], r.el, r.el_s, r.el_r)

        if inside:
            blocks = dot(r.wa[...], r.selp[: 3 * BLK, : 3 * 128]).astype(BF16)
            r.sw_src[...] = blocks[:, 128:256]
            swap = rc(r.sw_src, r.sw_dst, r.sw_s.at[0], r.sw_r.at[0], sib)
            swap.start()
            for a in range(3):
                r.g2[w * 2 + v, 0, pl.ds(a * 112, 112), :] = pack_taps(*[r.k2[3 * a + b] for b in range(3)])
        r.par[0:3, :] = r.gains[...]
        r.par[3:13, :] = r.biases[...]
        r.par[13:16, :] = jnp.zeros((3, 384), F32)
        r.parown[...] = exact_dot(r.par[...], r.sel[c])

        def prow(i):
            return r.parown[pl.ds(i, 1), :]

        for buf in (r.act1, r.act2):
            for core in range(2):
                buf[core, pl.ds(0, ROW), :] = jnp.zeros((ROW, HALF), BF16)
                buf[core, pl.ds(PX + ROW, ROW), :] = jnp.zeros((ROW, HALF), BF16)
        for buf in (r.gr1, r.gr2):
            for b in range(3):
                buf[b, pl.ds(0, ROW), :] = jnp.zeros((ROW, HALF), BF16)
                buf[b, pl.ds(PX + ROW, ROW), :] = jnp.zeros((ROW, HALF), BF16)
        r.wfp[...] = jnp.zeros((128, HALF), BF16)
        r.wfp[pl.ds(0, film_rows), :] = dot(r.wf[...], r.selp[: 2 * BLK, :HALF]).astype(BF16)
        if inside:
            ga.pass_z(1, 3, 2)
            gb.own()

        count = float(PX * 12)

        def fold(vals):
            return jnp.sum(vals.reshape(CHUNK // 8, 8, HALF), axis=0)

        def sums_of(fn, k):
            def step(i, carry):
                return tuple(a + fold(b) for a, b in zip(carry, fn(i)))

            zero = jnp.zeros((8, HALF), F32)
            return lax.fori_loop(0, 4, step, (zero,) * k)

        def group_mean(part):
            return jnp.sum(exact_dot(part, r.gmask[...]), axis=0, keepdims=True) / count

        def norm(load, which, total):
            mean = group_mean(total)
            (square,) = sums_of(lambda i: (jnp.square(load(i) - mean),), 1)
            inv = lax.rsqrt(group_mean(square) + EPS)
            r.stat[pl.ds(2 * which, 1), :] = mean
            r.stat[pl.ds(2 * which + 1, 1), :] = inv
            return mean, inv

        zero8 = jnp.zeros((8, HALF), F32)

        def norm_back(sums, load_grad, load_hat, coef, inv):
            plain, cross = sums
            means = exact_dot(jnp.concatenate([coef * plain, coef * cross], axis=0), r.gmask[...])
            plain_mean = jnp.sum(means[:8], axis=0, keepdims=True) / count
            cross_mean = jnp.sum(means[8:], axis=0, keepdims=True) / count
            outer, base, slope = inv * coef, inv * plain_mean, inv * cross_mean

            def chunk(i):
                return outer * load_grad(i) - base - load_hat(i) * slope

            return (
                jnp.sum(plain, axis=0, keepdims=True),
                jnp.sum(cross, axis=0, keepdims=True),
                chunk,
            )

        def transposed(name, core):
            ref = getattr(r, name).at[core]
            return rc(ref, ref, getattr(r, name + "_s").at[0], getattr(r, name + "_r").at[0], sib)

        def transpose_act(buf, base, name):
            out = getattr(r, name)
            for q in range(4):
                out[c, :, pl.ds(q * CHUNK, CHUNK)] = jnp.transpose(buf[c, pl.ds(base + q * CHUNK, CHUNK), :])
            transposed(name, c).start()

        def transposed_wait(name):
            copy = transposed(name, 1 - c)
            copy.wait_recv()
            copy.wait_send()

        head_wait(lambda p: r.mx_src.at[p], r.mx_dst, r.mx_s, r.mx_r)

        def unpack_mixed(i, carry):
            vals = unpack_pixels(r.mx_dst[i])
            r.mx[i] = vals
            return carry + fold(vals.astype(F32))

        mixed_sum = lax.fori_loop(0, 4, unpack_mixed, zero8)

        def mixed(i):
            return r.mx[i].astype(F32)

        if inside:
            ga.pass_v(1, 3)
        mean1, inv1 = norm(mixed, 0, mixed_sum)
        if inside:
            ga.pass_v(2)
        gain1, shift1 = prow(0), prow(3)
        act1 = Halves("act1", ROW)

        def affine(mean, inv, gain, shift):
            return inv * gain, shift - mean * (inv * gain)

        mul1, add1 = affine(mean1, inv1, gain1, shift1)

        def pre1(i):
            return mixed(i) * mul1 + add1

        act1.fill(lambda i: silu(pre1(i)).astype(BF16))
        dp_wait(lambda p: r.el.at[d], r.el, r.el_s, r.el_r)
        for j in range(n):
            r.em[pl.ds(2 * j, 2), :] = r.el[j]
        place = lax.broadcasted_iota(jnp.int32, (768, 128), 0) - film_rows * d
        lane = lax.broadcasted_iota(jnp.int32, (768, 128), 1)
        pick = jnp.where((place == lane) & (lane < film_rows), 1.0, 0.0).astype(BF16)
        r.esel[...] = dot(r.em[...].astype(BF16), pick)
        film_part = dot(r.esel[...].astype(BF16), r.wfp[...])
        for j in range(n):
            r.fp[j] = film_part[2 * j : 2 * j + 2]
        dp_start(lambda p: r.fp.at[p], r.fr, r.fr_s, r.fr_r)
        r.fr[d] = r.fp[d]
        if inside:
            swap.wait()
            got = r.sw_dst[...]
            keep0, keep2 = blocks[:, :128], blocks[:, 256:]
            r.p3[w * 2 + v, 0] = pack_four(
                jnp.where(c == 0, keep0, got),
                jnp.where(c == 0, keep2, keep0),
                jnp.where(c == 0, got, keep2),
                r.wo[...],
            )
        act1.wait()
        transpose_act(r.act1, ROW, "act1_t")
        if inside:
            gb.pass_own()
            gb.pass_z(1, 3, 2)
            gc.own()
        def split_cot(m, carry):
            for core in range(2):
                r.cx_src[m * 2 + core] = pack_pixels(dot(r.cot[m], r.sel[core])).astype(BF16)
            return carry

        lax.fori_loop(0, 2, split_cot, 0)
        column = lax.broadcasted_iota(jnp.int32, (1, ROW, HALF), 1)
        not_first = jnp.where(column > 0, 1.0, 0.0)
        not_last = jnp.where(column < ROW - 1, 1.0, 0.0)

        def in_rows(vals, mask):
            return (vals.reshape(CHUNK // ROW, ROW, HALF) * mask).reshape(CHUNK, HALF)

        def from_left(vals):
            return in_rows(pltpu.roll(vals, 1, 0), not_first)

        def from_right(vals):
            return in_rows(pltpu.roll(vals, CHUNK - 1, 0), not_last)

        def conv(buf, g, store, between):
            weights = lambda: jnp.concatenate(
                [jnp.concatenate([wtap(g, 3 * a + b, ALL) for b in range(3)], axis=1) for a in range(3)], axis=0
            )

            total = zero8
            for i in range(2):
                left = jnp.concatenate([flat(buf, ROW * a, i, 2 * CHUNK) for a in range(3)], axis=1)
                out = dot(left, weights())
                for j in range(2):
                    part = out[j * CHUNK : j * CHUNK + CHUNK]
                    part = part[:, HALF : 2 * HALF] + from_left(part[:, :HALF]) + from_right(part[:, 2 * HALF :])
                    total = total + fold(store(2 * i + j, part))
                if i == 0:
                    between()
            return total

        if inside:
            k1.unpack(w)
            ga.done()
            k1.unpack(1 - w)

        dp_wait(lambda p: r.fp.at[p], r.fr, r.fr_s, r.fr_r)
        film_sum = r.fr[0]
        for j in range(1, n):
            film_sum = film_sum + r.fr[j]
        for m in range(2):
            for core in range(2):
                r.fx[m * 2 + core] = film_sum[m : m + 1, core * 128 : core * 128 + 128]
        head_start(lambda p: r.fx.at[p], r.fh, r.fh_s, r.fh_r)
        r.fh[h] = r.fx[h]

        def store_v2(i, vals):
            vals = vals + prow(6)
            r.v2[rows(i), :] = vals
            return vals

        v2_sum = conv(r.act1, k1, store_v2, (lambda: gb.pass_v(1, 3, 2)) if inside else lambda: None)
        head_wait(lambda p: r.fx.at[p], r.fh, r.fh_s, r.fh_r)
        scale = 1.0 + (jnp.concatenate([r.fh[0], r.fh[1]], axis=1) + prow(8))
        shift = jnp.concatenate([r.fh[2], r.fh[3]], axis=1) + prow(9)
        head_start(lambda p: r.cx_src.at[p], r.cx_dst, r.cx_s, r.cx_r)
        r.cx_dst[h] = r.cx_src[h]
        mean2, inv2 = norm(lambda i: r.v2[rows(i), :], 1, v2_sum)
        gain2, shift2 = prow(1), prow(4)
        act2 = Halves("act2", ROW)

        def hat2(i):
            return (r.v2[rows(i), :] - mean2) * inv2

        mul2, add2 = affine(mean2, inv2, gain2 * scale, shift2 * scale + shift)

        def pre2(i):
            return r.v2[rows(i), :] * mul2 + add2

        act2.fill(lambda i: silu(pre2(i)).astype(BF16))
        if inside:
            gc.pass_own()
            gc.pass_z(1, 3, 2)

        transpose_act(r.act2, ROW, "act2_t")
        act2.wait()
        if inside:
            k2.unpack(w)
            gb.done()
            k2.unpack(1 - w)

        def store_v3(i, vals):
            vals = mixed(i) + (vals + prow(7))
            r.v3[rows(i), :] = vals
            return vals

        v3_sum = conv(r.act2, k2, store_v3, (lambda: gc.pass_v(1, 3, 2)) if inside else lambda: None)
        mean3, inv3 = norm(lambda i: r.v3[rows(i), :], 2, v3_sum)
        gain3, shift3 = prow(2), prow(5)
        ai = Halves("ai", 0)

        def hat3(i):
            return (r.v3[rows(i), :] - mean3) * inv3

        mul3, add3 = affine(mean3, inv3, gain3, shift3)
        ai.fill(lambda i: (r.v3[rows(i), :] * mul3 + add3).astype(BF16))
        transpose_act(r.ai, 0, "ai_t")

        if inside:
            k3.unpack(w)
            gc.done()
            k3.unpack(1 - w)
        head_wait(lambda p: r.cx_src.at[p], r.cx_dst, r.cx_s, r.cx_r)

        def unpack_cot(i):
            r.cx[i] = unpack_pixels(r.cx_dst[i])

        loop(4, unpack_cot)
        dop = Parts("do")

        def cot_rows(i):
            return jnp.concatenate([r.cx[2 * i], r.cx[2 * i + 1]], axis=0)

        dop.fill(lambda i: dot_nt(cot_rows(i), wtap(k3, 3, half_of(1 - c))))

        ai.wait()
        bias_proj = [prow(10)[:, :128], prow(10)[:, 128:], None, None, prow(11)[:, :128], prow(11)[:, 128:]]

        def project(i):
            out = dot(flat(r.ai, 0, i, 2 * CHUNK), wproj(ALL))
            for k in range(6):
                part = out[:, k * 128 : k * 128 + 128]
                if bias_proj[k] is not None:
                    part = part + bias_proj[k]
                r.qkv[k, rows(i, 2 * CHUNK), :] = part.astype(BF16)

        each(2, project)

        def do_own(i):
            full = (dot_nt(cot_rows(i), wtap(k3, 3, half_of(c))) + dop.get(i)).astype(BF16)
            for k in range(2):
                r.dout[k, rows(i, 2 * CHUNK), :] = full[:, k * 128 : k * 128 + 128]

        each(2, do_own)

        factor = 1.0 / math.sqrt(HEAD_DIM)
        factor2 = factor * math.log2(math.e)
        att = []

        def transposes(k):
            r.kvt[k] = jnp.transpose(r.qkv[k + 2])

        loop(4, transposes)

        def att_copy(core, k):
            ref = r.att.at[core * 2 + k]
            return rc(ref, ref, r.att_s.at[k], r.att_r.at[k], sib)

        def att_t_copy(core, k):
            ref = r.att_t.at[core, pl.ds(pl.multiple_of(k * 128, 128), 128)]
            return rc(ref, ref, r.att_s.at[2 + k], r.att_r.at[2 + k], sib)

        def one_head(k):
            lows, grads = [], []
            for b in range(2):
                at = pl.ds(b * 2 * CHUNK, 2 * CHUNK)
                query = r.qkv[k, at, :]
                grad = r.dout[k, at, :]
                scores = dot_nt(r.qkv[2 + k], query)
                peak = jnp.max(scores, axis=0, keepdims=True)
                expo = jnp.exp2((scores - peak) * factor2)
                inverse = 1.0 / jnp.sum(expo, axis=0, keepdims=True)
                low = (expo * inverse).astype(BF16)
                got = dot(r.kvt[2 + k], low)
                got_low = got.astype(BF16)
                r.att_t[c, pl.ds(pl.multiple_of(k * 128, 128), 128), at] = got_low
                r.att[2 * c + k, at, :] = jnp.transpose(got_low)
                spread = jnp.sum(got * jnp.transpose(grad).astype(F32), axis=0, keepdims=True)
                probs_grad = dot_nt(r.qkv[4 + k], grad)
                scores_grad = ((probs_grad - spread) * inverse * expo).astype(BF16)
                back = dot(r.kvt[k], scores_grad)
                r.dproj[k, at, :] = (jnp.transpose(back) * factor).astype(BF16)
                lows.append(low)
                grads.append(scores_grad)
            att_copy(c, k).start()
            att_t_copy(c, k).start()
            r.dproj[4 + k] = dot(jnp.concatenate(lows, axis=1), r.dout[k]).astype(BF16)
            r.dproj[2 + k] = (dot(jnp.concatenate(grads, axis=1), r.qkv[k]) * factor).astype(BF16)

        loop(2, one_head)

        n3 = Parts("n3")

        def proj_rows(i):
            return jnp.concatenate([r.dproj[k, rows(i, 2 * CHUNK), :] for k in range(6)], axis=1)

        n3.fill(lambda i: dot_nt(proj_rows(i), wproj(half_of(1 - c))))

        def rows_of(act_t):
            return jnp.concatenate([act_t[p // 2, pl.ds(p % 2 * 128, BLK), :] for p in range(4)], axis=0)

        for k in range(2):
            copy = att_copy(1 - c, k)
            copy.wait_recv()
            copy.wait_send()

        def result(i):
            left = jnp.concatenate([r.att[p, rows(i), :] for p in range(4)], axis=1)
            branch = dot(left, wtap(k3, 3, ALL)) + prow(12)
            r.ro_src[i] = pack_pixels(r.v3[rows(i), :] + branch).astype(BF16)

        loop(4, result)
        head_start(lambda p: r.ro_src.at[p], r.ro_dst, r.ro_s, r.ro_r)
        r.ro_dst[h] = r.ro_src[h]

        if inside:
            red1, red2, red3 = Reduce("r1", 3), Reduce("r2", 3), Reduce("r3", 1)
            acc1, acc2, acc3 = r.r1_acc, r.r2_acc, r.r3_acc
        else:
            acc1, acc2, acc3 = r.first, r.second, r.attend

        transposed_wait("ai_t")
        for k in range(2):
            copy = att_t_copy(1 - c, k)
            copy.wait_recv()
            copy.wait_send()
        right = jnp.concatenate([r.dproj[k] for k in range(6)], axis=1)
        cot_all = jnp.concatenate([r.cx[i] for i in range(4)], axis=0)
        attend_out = dot(rows_of(r.ai_t), right)
        output_out = dot(rows_of(r.att_t), cot_all)
        for p, zc in enumerate(ALL):
            for yy in range(2):
                for xx in range(2):
                    row = p * BLK + yy * 48
                    tiles = [
                        attend_out[row : row + 48, (xx * 3 + j) * 128 : (xx * 3 + j) * 128 + 128] for j in range(3)
                    ]
                    acc3[0, slot(xx, yy), zc] = pack_four(
                        *tiles, output_out[row : row + 48, xx * 128 : xx * 128 + 128]
                    ).astype(acc3.dtype)
        if inside:
            red3.start(0)

        def proj_sums(i, carry):
            q = jnp.concatenate([r.dproj[0, rows(i), :], r.dproj[1, rows(i), :]], axis=1).astype(F32)
            val = jnp.concatenate([r.dproj[4, rows(i), :], r.dproj[5, rows(i), :]], axis=1).astype(F32)
            return (carry[0] + fold(q), carry[1] + fold(val), carry[2] + fold(r.cx[i].astype(F32)))

        qsum, vsum, csum = lax.fori_loop(0, 4, proj_sums, (zero8, zero8, zero8))
        r.sums[pl.ds(3 + 7, 1), :] = jnp.sum(qsum, axis=0, keepdims=True)
        r.sums[pl.ds(3 + 8, 1), :] = jnp.sum(vsum, axis=0, keepdims=True)
        r.sums[pl.ds(3 + 9, 1), :] = jnp.sum(csum, axis=0, keepdims=True)
        r.sums[pl.ds(13, 3), :] = jnp.zeros((3, HALF), F32)

        def n3_own(i, carry):
            both = dot_nt(proj_rows(i), wproj(half_of(c))) + n3.get(i)
            for j in range(2):
                vals = both[j * CHUNK : j * CHUNK + CHUNK]
                r.gtmp[rows(2 * i + j), :] = vals
                carry = carry[0] + fold(vals), carry[1] + fold(vals * hat3(2 * i + j))
            return carry

        sums3 = n3_own(1, n3_own(0, (zero8, zero8)))
        plain3, cross3, back3 = norm_back(sums3, lambda i: r.gtmp[rows(i), :], hat3, gain3, inv3)
        r.sums[pl.ds(2, 1), :] = cross3
        r.sums[pl.ds(3 + 2, 1), :] = plain3

        def shifted(buf, i, vals):
            buf[0, rows(i, CHUNK, ROW), :] = from_right(vals).astype(BF16)
            buf[1, rows(i, CHUNK, ROW), :] = vals.astype(BF16)
            buf[2, rows(i, CHUNK, ROW), :] = from_left(vals).astype(BF16)

        def residual_back(i, carry):
            vals = r.cx[i].astype(F32) + back3(i)
            r.gres[rows(i), :] = vals
            shifted(r.gr2, i, vals)
            return carry + fold(vals.astype(BF16).astype(F32))

        bias_two = lax.fori_loop(0, 4, residual_back, jnp.zeros((8, HALF), F32))
        r.sums[pl.ds(3 + 4, 1), :] = jnp.sum(bias_two, axis=0, keepdims=True)

        def act_back(buf, g, core, i, size):
            left = jnp.concatenate(
                [buf[b, rows(i, size, 2 * ROW - ROW * a), :] for a in range(3) for b in range(3)], axis=1
            )
            right = jnp.concatenate(
                [wtap(g, 3 * a + b, half_of(core)) for a in range(3) for b in range(3)], axis=1
            )
            return dot_nt(left, right)

        def conv_back(parts, buf, g):
            parts.fill(lambda i: act_back(buf, g, 1 - c, i, 2 * CHUNK))

        def conv_back_own(parts, buf, g, outer, hat):
            def own(i, carry):
                vals = act_back(buf, g, c, i, 2 * CHUNK) + parts.get(i)
                for j in range(2):
                    at = 2 * i + j
                    grad = vals[j * CHUNK : j * CHUNK + CHUNK] * outer(at)
                    r.gtmp[rows(at), :] = grad
                    carry = carry[0] + fold(grad), carry[1] + fold(grad * hat(at))
                return carry

            return own(1, own(0, (zero8, zero8)))

        def kernel_grad(act_t, buf, acc, after):
            def step(a):
                right = jnp.concatenate([buf[b, pl.ds(2 * ROW - ROW * a, PX), :] for b in range(3)], axis=1)
                out = dot(rows_of(act_t), right)
                for p, zc in enumerate(ALL):
                    for yy in range(2):
                        for xx in range(2):
                            row = p * BLK + yy * 48
                            tiles = [
                                out[row : row + 48, b * HALF + xx * 128 : b * HALF + xx * 128 + 128].astype(acc.dtype)
                                for b in range(3)
                            ]
                            acc[a, slot(xx, yy), zc] = pack_taps(*tiles)
                after(a)

            each(3, step)

        serve = inside
        d2 = Parts("d2")
        transposed_wait("act2_t")
        kernel_grad(r.act2_t, r.gr2, acc2, red2.start if inside else lambda a: None)
        if serve:
            red3.second(0, 1)
        conv_back(d2, r.gr2, k2)
        if serve:
            red2.second(0, 1)
        sums2 = conv_back_own(d2, r.gr2, k2, lambda i: silu_slope(pre2(i)), hat2)
        if serve:
            red2.second(1, 1)
            red3.third(0, 1)

        plain2, cross2, back2 = norm_back(sums2, lambda i: r.gtmp[rows(i), :], hat2, gain2 * scale, inv2)
        r.sums[pl.ds(1, 1), :] = scale * cross2
        r.sums[pl.ds(3 + 1, 1), :] = scale * plain2
        film_scale_term = gain2 * cross2 + shift2 * plain2
        r.sums[pl.ds(3 + 5, 1), :] = film_scale_term
        r.sums[pl.ds(3 + 6, 1), :] = plain2
        for j in range(2):
            r.ft[j] = film_scale_term[:, j * 128 : j * 128 + 128]
            r.ft[2 + j] = plain2[:, j * 128 : j * 128 + 128]
        head_start(lambda p: r.ft.at[p], r.th, r.th_s, r.th_r)
        r.th[h] = r.ft[h]

        def first_back(i, carry):
            vals = back2(i)
            shifted(r.gr1, i, vals)
            return carry + fold(vals.astype(BF16).astype(F32))

        bias_one = lax.fori_loop(0, 4, first_back, jnp.zeros((8, HALF), F32))
        r.sums[pl.ds(3 + 3, 1), :] = jnp.sum(bias_one, axis=0, keepdims=True)

        if serve:
            red2.second(2, 1)
            red2.third(0, 1)
            red2.third(1, 1)

        head_wait(lambda p: r.ft.at[p], r.th, r.th_s, r.th_r)
        for m in range(2):
            r.fa[d, pl.ds(m, 1), :] = jnp.concatenate([r.th[2 * m], r.th[2 * m + 1]], axis=1)
        dp_start(lambda p: r.fa.at[d], r.fa, r.fa_s, r.fa_r)

        d1 = Parts("d1")

        def after_chunk(a):
            if serve:
                red1.start(a)
                if a == 1:
                    red2.third(2, 1)

        transposed_wait("act1_t")
        kernel_grad(r.act1_t, r.gr1, acc1, after_chunk)
        conv_back(d1, r.gr1, k1)
        if serve:
            red1.second(0, 1)

        dp_wait(lambda p: r.fa.at[d], r.fa, r.fa_s, r.fa_r)
        for j in range(n):
            r.fta[pl.ds(2 * j, 2), :] = r.fa[j]
        film_block = dot_tn_high(r.esel[...], r.fta[...])
        r.film[...] = jnp.concatenate([film_block[:film_rows, :BLK], film_block[:film_rows, 128 : 128 + BLK]], axis=1)
        embed_part = dot_nt_high(r.fta[...], r.wfp[...].astype(F32))
        for j in range(n):
            r.ep[j] = embed_part[2 * j : 2 * j + 2]
        dp_start(lambda p: r.ep.at[p], r.er, r.er_s, r.er_r)
        r.er[d] = r.ep[d]

        def hat1(i):
            return (mixed(i) - mean1) * inv1

        sums1 = conv_back_own(d1, r.gr1, k1, lambda i: silu_slope(pre1(i)), hat1)
        if serve:
            red1.second(1, 1)

        dp_wait(lambda p: r.ep.at[p], r.er, r.er_s, r.er_r)
        r.eh[h] = r.er[...]
        head_start(lambda p: r.eh.at[h], r.eh, r.eh_s, r.eh_r)
        plain1, cross1, back1 = norm_back(sums1, lambda i: r.gtmp[rows(i), :], hat1, gain1, inv1)
        r.sums[pl.ds(0, 1), :] = cross1
        r.sums[pl.ds(3, 1), :] = plain1
        r.ad[d] = r.sums[...]
        dp_start(lambda p: r.ad.at[d], r.ad, r.ad_s, r.ad_r)

        if serve:
            red1.second(2, 1)
            red1.third(0, 1)
        keep, _ = plan(r.steps[x], HALF)

        def image_back(i):
            return pack_pixels(keep * (r.gres[rows(i), :] + back1(i))).astype(BF16)

        for k in (2, 1, 3):
            peer = lax.rem(h + k, 4)
            r.io_src[peer] = image_back(peer)
            rc(r.io_src.at[peer], r.io_dst.at[h], r.io_s.at[k], r.io_r.at[h], (d, peer)).start()
        r.io_dst[h] = image_back(h)
        if serve:
            red1.third(1, 1)
            red1.third(2, 1)

        dp_wait(lambda p: r.ad.at[d], r.ad, r.ad_s, r.ad_r)
        total = r.ad[0]
        for j in range(1, n):
            total = total + r.ad[j]
        r.hb[h] = total
        head_start(lambda p: r.hb.at[h], r.hb, r.hb_s, r.hb_r)
        head_wait(lambda p: r.ro_src.at[p], r.ro_dst, r.ro_s, r.ro_r)

        if inside:
            red2.finish(((0, 1), (1, 1), (2, 1)))
            for a in range(3):
                r.second[a] = red2.last(a)

        head_wait(lambda p: r.hb.at[h], r.hb, r.hb_s, r.hb_r)
        even = r.hb[0] + r.hb[2]
        odd = r.hb[1] + r.hb[3]
        wide = jnp.concatenate(
            [even[:, :BLK], odd[:, :BLK], even[:, 128 : 128 + BLK], odd[:, 128 : 128 + BLK]], axis=1
        )
        r.gains_out[...] = wide[0:3]
        r.biases_out[...] = wide[3:13]

        head_wait(lambda p: r.eh.at[h], r.eh, r.eh_s, r.eh_r)
        pieces = []
        for j in range(n):
            piece = (r.eh[0, j] + r.eh[1, j]) + (r.eh[2, j] + r.eh[3, j])
            pieces.append(piece[:, :film_rows])
        r.embed_grad[...] = jnp.concatenate(pieces, axis=1) * silu_slope(r.emb[...].astype(F32))

        head_wait(lambda p: r.io_src.at[p], r.io_dst, r.io_s, r.io_r)

        if inside:
            red3.finish(((0, 1),))
            tiles = unpack_four(red3.last(0))
            r.sb_src[...] = jnp.where(c == 0, tiles[2], tiles[0])
            back = rc(r.sb_src, r.sb_dst, r.sb_s.at[0], r.sb_r.at[0], sib)
            back.start()
            r.output[...] = tiles[3]
            for part in (ga, gb, gc):
                part.finish()
            red1.finish(((0, 1), (1, 1), (2, 1)))
            for a in range(3):
                r.first[a] = red1.last(a)
            back.wait()
            r.attend[:, 0:128] = jnp.where(c == 0, tiles[0], tiles[1])
            r.attend[:, 128:256] = r.sb_dst[...]
            r.attend[:, 256:384] = jnp.where(c == 0, tiles[1], tiles[2])

    return kernel


def make_writer(names_in, names_out):
    def kernel(*refs):
        count, wide = len(names_in), len(names_out)
        far_in, far_out = refs[:count], refs[count : count + wide]
        near_in, near_out = refs[count + wide : 2 * count + wide], refs[2 * count + wide : 2 * count + 2 * wide]
        sem_in, sem_out = refs[-2:]
        src, dst = Names(names_in, near_in), Names(names_out, near_out)
        loads = {
            name: pltpu.make_async_copy(far_in[i], near_in[i], sem_in.at[i]) for i, name in enumerate(names_in)
        }
        stores = {
            name: pltpu.make_async_copy(near_out[i], far_out[i], sem_out.at[i]) for i, name in enumerate(names_out)
        }
        for name in ("sel", "ro_dst", "io_dst"):
            loads[name].start()
        for name in names_in:
            if name not in ("sel", "ro_dst", "io_dst"):
                loads[name].start()
        loads["sel"].wait()
        for name, packed in (("result", "ro_dst"), ("image_grad", "io_dst")):
            loads[packed].wait()
            ref = getattr(src, packed)
            for m in range(2):
                getattr(dst, name)[m] = dot_nt(unpack_pixels(ref[2 * m]), src.sel[0]) + dot_nt(
                    unpack_pixels(ref[2 * m + 1]), src.sel[1]
                )
            stores[name].start()
        for name in ("first", "second"):
            if name in names_out:
                loads[name].wait()
                for a in range(3):
                    block = getattr(src, name)[a]
                    getattr(dst, name)[3 * a] = block[:48, :BLK]
                    getattr(dst, name)[3 * a + 1] = block[48:96, :BLK]
                    getattr(dst, name)[3 * a + 2] = last_tap(block)[:, :BLK]
                stores[name].start()
        if "attend" in names_out:
            loads["attend"].wait()
            dst.attend[...] = jnp.concatenate([src.attend[:, j * 128 : j * 128 + BLK] for j in range(3)], axis=1)
            stores["attend"].start()
            loads["output"].wait()
            dst.output[...] = src.output[:, :BLK]
            stores["output"].start()
        for name in ("embed_grad", "film", "gains_out", "biases_out"):
            loads[name].wait()
            getattr(dst, name)[...] = getattr(src, name)[...]
            stores[name].start()
        for name in names_out:
            stores[name].wait()

    return kernel


def per_device(n, *args):
    (
        images,
        noise_field,
        time_steps,
        embedding,
        first_kernel,
        second_kernel,
        film_weight,
        attend_weight,
        output_weight,
        norm_gains,
        biases,
        cotangent,
    ) = args
    inside = n == 8
    maps, height, width, channels = images.shape
    flat_shape = (maps, height * width, channels)
    film_rows = film_weight.shape[0]
    inputs = dict(
        steps=time_steps,
        images=images.reshape(flat_shape),
        noise=noise_field.reshape(flat_shape),
        cot=cotangent.reshape(flat_shape),
        emb=embedding,
        k1=first_kernel.reshape((9,) + first_kernel.shape[2:]),
        k2=second_kernel.reshape((9,) + second_kernel.shape[2:]),
        wf=film_weight,
        wa=attend_weight,
        wo=output_weight,
        gains=norm_gains,
        biases=biases,
        sel=jnp.asarray(channel_lanes(), BF16),
        gmask=jnp.asarray(group_mask(), BF16),
        selp=jnp.asarray(block_lanes(3), BF16),
    )
    shapes = dict(
        ro_dst=(4, 384, 128),
        io_dst=(4, 384, 128),
        embed_grad=embedding.shape,
        first=(3, 112, 128),
        second=(3, 112, 128),
        film=film_weight.shape,
        attend=(48, 384),
        output=(48, 128),
        gains_out=norm_gains.shape,
        biases_out=biases.shape,
    )
    names_in, names_out = list(INPUTS), list(OUTPUTS)
    core = lax.axis_index("head") % 2
    if not inside:
        def whole(array, row_axis):
            array = lax.all_gather(array, "dp", axis=row_axis, tiled=True)
            return lax.all_gather(array, "head", axis=array.ndim - 1, tiled=True)

        def spread(array, count):
            taps = array.shape[0]
            array = array.reshape(taps, 4, 2, 48, 2, 2, BLK)
            array = lax.dynamic_index_in_dim(array, core, 5, keepdims=False)
            array = jnp.transpose(array, (2, 4, 1, 0, 3, 5))
            array = jnp.pad(array, ((0, 0),) * 5 + ((0, 32),))
            return array.reshape(4, 4, taps * 48, 128)

        full_a = whole(attend_weight, 0).reshape(384, 2, 3, 2, BLK)
        full_a = jnp.transpose(full_a, (2, 0, 1, 3, 4)).reshape(3, 384, 384)
        full_o = whole(output_weight, 0)[None]
        for name, last, array in (("g1", "t1", first_kernel), ("g2", "t2", second_kernel)):
            blocks = spread(whole(array, 2).reshape(9, 384, 384), 9).reshape(4, 4, 3, 3, 48, 128)
            two = blocks[:, :, :, :2].reshape(4, 4, 3, 96, 128)
            inputs[name] = jnp.pad(two, ((0, 0),) * 3 + ((0, 16), (0, 0))).reshape(4, 4, 336, 128)
            inputs[last] = blocks[:, :, :, 2].reshape(4, 4, 144, 128)
        inputs["g3"] = spread(jnp.concatenate([full_a, full_o], axis=0), 4)
        names_in += ["g1", "g2", "t1", "t2", "g3"]
        shapes["first"] = shapes["second"] = (3, 4, 4, 112, 128)
        shapes["attend"] = (1, 4, 4, 144, 128)
        del shapes["output"]
        names_out.remove("output")
    items = scratch_list(n, inside, inputs)
    smem = pl.BlockSpec(memory_space=pltpu.SMEM)
    vmem = pl.BlockSpec(memory_space=pltpu.VMEM)
    outs = pl.pallas_call(
        make_kernel(
            n,
            inside,
            [name + "_far" if name in FAR else name for name in names_in] + names_out + [name for name, _ in items],
        ),
        out_shape=[
            jax.ShapeDtypeStruct(shapes[name], BF16 if name in ("ro_dst", "io_dst") else F32) for name in names_out
        ],
        in_specs=[
            smem if name == "steps" else pl.BlockSpec(memory_space=pl.ANY) if name in FAR else vmem
            for name in names_in
        ],
        out_specs=[vmem] * len(names_out),
        scratch_shapes=[item for _, item in items],
        compiler_params=pltpu.CompilerParams(
            collective_id=0, has_side_effects=True, vmem_limit_bytes=63 * 1024 * 1024
        ),
        name="blocks",
    )(*[inputs[name] for name in names_in])
    raw = dict(zip(names_out, outs))
    final = dict(
        result=flat_shape,
        image_grad=flat_shape,
        embed_grad=embedding.shape,
        film=film_weight.shape,
        gains_out=norm_gains.shape,
        biases_out=biases.shape,
    )
    if inside:
        final.update(first=(9, 48, BLK), second=(9, 48, BLK), attend=attend_weight.shape, output=output_weight.shape)
    names_last = [name for name in names_out if inside or name not in ("first", "second", "attend")] + ["sel"]
    names_final = list(final)
    given = [inputs["sel"] if name == "sel" else raw[name] for name in names_last]
    far = pl.BlockSpec(memory_space=pl.ANY)
    outs = pl.pallas_call(
        make_writer(names_last, names_final),
        out_shape=[jax.ShapeDtypeStruct(final[name], F32) for name in names_final],
        in_specs=[far] * len(names_last),
        out_specs=[far] * len(names_final),
        scratch_shapes=[pltpu.VMEM(array.shape, array.dtype) for array in given]
        + [pltpu.VMEM(final[name], F32) for name in names_final]
        + [pltpu.SemaphoreType.DMA((len(names_last),)), pltpu.SemaphoreType.DMA((len(names_final),))],
        compiler_params=pltpu.CompilerParams(vmem_limit_bytes=63 * 1024 * 1024),
        name="outputs",
    )(*given)
    out = dict(zip(names_final, outs))
    if not inside:

        def blocks_of(array, size):
            parts = [array[..., k * 48 : k * 48 + 48, :BLK] for k in range(size)]
            if size == 2:
                lanes = [array[..., k * 32 : k * 32 + 32, BLK:] for k in range(3)]
                lanes = jnp.concatenate(lanes, axis=-1)
                parts.append(jnp.concatenate([lanes, array[..., 96:112, :BLK]], axis=-2))
            else:
                lanes = [array[..., k * 48 : k * 48 + 48, BLK:] for k in range(3)]
                parts.append(jnp.concatenate(lanes, axis=-1))
            array = jnp.stack(parts, axis=1)
            array = array.reshape(array.shape[:2] + (2, 2, 4, 48, BLK))
            taps = array.shape[0] * array.shape[1]
            array = jnp.transpose(array, (0, 1, 4, 2, 5, 3, 6)).reshape(taps, 384, 2, 1, BLK)
            both = jnp.concatenate([array, jnp.zeros_like(array)], axis=3)
            return jnp.where(core == 0, both, both[:, :, :, ::-1]).reshape(taps, 384, 384)

        def shared(array, axis):
            array = lax.psum_scatter(array, "head", scatter_dimension=array.ndim - 1, tiled=True)
            return lax.psum_scatter(array, "dp", scatter_dimension=axis, tiled=True)

        out["first"] = shared(blocks_of(raw["first"], 2), 1)
        out["second"] = shared(blocks_of(raw["second"], 2), 1)
        both = blocks_of(raw["attend"], 3)
        joined = both[:3].reshape(3, 384, 2, 2, BLK)
        joined = jnp.transpose(joined, (1, 2, 0, 3, 4)).reshape(384, 1152)
        out["attend"] = shared(joined, 0)
        out["output"] = shared(both[3], 0)
    return (
        out["result"].reshape(images.shape),
        out["image_grad"].reshape(images.shape),
        out["embed_grad"],
        out["first"].reshape(first_kernel.shape),
        out["second"].reshape(second_kernel.shape),
        out["film"],
        out["attend"],
        out["output"],
        out["gains_out"],
        out["biases_out"],
    )


def solution(mesh):
    n = mesh.shape["dp"]
    field = P("dp", "head", None, None)
    taps = P(None, None, "dp", "head")
    both = P("dp", "head")
    return jax.shard_map(
        lambda *args: per_device(n, *args),
        mesh=mesh,
        in_specs=(field, field, P("dp"), P("dp", None), taps, taps, both, both, both, P(), P(), field),
        out_specs=(field, field, P("dp", None), taps, taps, both, both, both, P(), P()),
        check_vma=False,
    )
```

```python
import math

import jax
import jax.numpy as jnp
import numpy as np
from jax import lax
from jax.experimental import pallas as pl
from jax.experimental.pallas import tpu as pltpu
from jax.sharding import PartitionSpec as P

HEAD_DIM = 96
GROUPS = 32
STEPS = 4000
EPS = 1e-05
OFFSET = 0.008
MESH = pl.DeviceIdType.MESH
F32 = jnp.float32
BF16 = jnp.bfloat16

PX = 1024
ROW = 32
CHUNK = 256
BLK = 96
HALF = 256
NHEAD = 4


def plan(time_step, lanes):
    fraction = (jnp.full((1, lanes), time_step, jnp.int32).astype(F32) + 1.0) / STEPS
    start = math.cos(OFFSET / (1.0 + OFFSET) * (math.pi / 2)) ** 2
    curve = jnp.square(jnp.cos((fraction + OFFSET) / (1.0 + OFFSET) * (math.pi / 2))) / start
    return (jnp.sqrt(curve), jnp.sqrt(jnp.maximum(1.0 - curve, 0.0)))


def channel_lanes():
    sel = np.zeros((2, 384, HALF), np.float32)
    for block in range(4):
        for j in range(BLK):
            sel[block % 2, block * BLK + j, (block // 2) * 128 + j] = 1.0
    return sel


def block_lanes(count):
    sel = np.zeros((count * BLK, count * 128), np.float32)
    for block in range(count):
        for j in range(BLK):
            sel[block * BLK + j, block * 128 + j] = 1.0
    return sel


def group_mask():
    lane = np.arange(HALF)
    ok = lane % 128 < BLK
    group = (lane // 128) * 100 + (lane % 128) // 12
    return ((group[:, None] == group[None, :]) & ok[:, None] & ok[None, :]).astype(np.float32)


def dot(a, b):
    return lax.dot_general(a, b, (((1,), (0,)), ((), ())), preferred_element_type=F32)


def dot_nt(a, b):
    return lax.dot_general(a, b, (((1,), (1,)), ((), ())), preferred_element_type=F32)


def dot_nt_high(a, b):
    return lax.dot_general(
        a, b, (((1,), (1,)), ((), ())), preferred_element_type=F32, precision=lax.Precision.HIGHEST
    )


def dot_tn_high(a, b):
    return lax.dot_general(
        a, b, (((0,), (0,)), ((), ())), preferred_element_type=F32, precision=lax.Precision.HIGHEST
    )


def exact_dot(values, ones):
    high = values.astype(BF16).astype(F32)
    rest = values - high
    middle = rest.astype(BF16).astype(F32)
    low = rest - middle
    rows = values.shape[0]
    out = dot(jnp.concatenate([high, middle, low], axis=0).astype(BF16), ones)
    return out[:rows] + out[rows : 2 * rows] + out[2 * rows :]


def sigmoid(v):
    return 0.5 + 0.5 * jnp.tanh(0.5 * v)


def silu(v):
    return v * sigmoid(v)


def silu_slope(v):
    s = sigmoid(v)
    return s * (1.0 + v * (1.0 - s))


def pack_taps(t0, t1, t2):
    t0, t1, t2 = t0[:, :BLK], t1[:, :BLK], t2[:, :BLK]
    join = lambda a, b: jnp.concatenate([a, b], axis=1)
    return jnp.concatenate(
        [
            join(t0[:32], t2[:32, :32]),
            join(t0[32:], t2[:16, 32:64]),
            join(t1[:16], t2[16:32, 32:64]),
            join(t1[16:], t2[:32, 64:]),
            join(t2[32:], jnp.zeros((16, 32), t2.dtype)),
        ],
        axis=0,
    )


def last_tap(packed):
    lanes = [packed[:32, BLK:], packed[32:64, BLK:], packed[64:96, BLK:], jnp.zeros((32, 32), packed.dtype)]
    return jnp.concatenate([jnp.concatenate(lanes, axis=1), packed[96:112]], axis=0)


def pack_four(b0, b1, b2, b3):
    return jnp.concatenate(
        [jnp.concatenate([b[:, :BLK], b3[:, 32 * k : 32 * k + 32]], axis=1) for k, b in enumerate((b0, b1, b2))],
        axis=0,
    )


def unpack_four(packed):
    size = packed.shape[0] // 3
    parts = [packed[k * size : k * size + size] for k in range(3)]
    zero = jnp.zeros((size, 32), packed.dtype)
    fourth = jnp.concatenate([p[:, BLK:] for p in parts] + [zero], axis=1)
    return [jnp.concatenate([p[:, :BLK], zero], axis=1) for p in parts] + [fourth]


def pack_pixels(full):
    half = CHUNK // 2
    return pack_four(full[:half, :128], full[half:, :128], full[:half, 128:], full[half:, 128:])


def unpack_pixels(packed):
    b0, b1, b2, b3 = unpack_four(packed)
    return jnp.concatenate([jnp.concatenate([b0, b2], axis=1), jnp.concatenate([b1, b3], axis=1)], axis=0)


INPUTS = (
    "steps",
    "images",
    "noise",
    "cot",
    "emb",
    "k1",
    "k2",
    "wf",
    "wa",
    "wo",
    "gains",
    "biases",
    "sel",
    "gmask",
    "selp",
)
OUTPUTS = (
    "ro_dst",
    "io_dst",
    "embed_grad",
    "first",
    "second",
    "film",
    "attend",
    "output",
    "gains_out",
    "biases_out",
)


FAR = (
    "images",
    "noise",
    "cot",
    "sel",
    "selp",
    "k2",
    "wa",
    "wf",
    "gmask",
)


class Names:
    def __init__(self, names, refs):
        for name, ref in zip(names, refs):
            setattr(self, name, ref)


def scratch_list(n, inside, inputs):
    dma = pltpu.SemaphoreType.DMA
    items = []

    def vm(name, shape, dtype):
        items.append((name, pltpu.VMEM(shape, dtype)))

    def sem(name, count):
        items.append((name + "_s", dma((count,))))
        items.append((name + "_r", dma((count,))))

    for name in FAR:
        vm(name, inputs[name].shape, inputs[name].dtype)
    items.append(("far_s", dma((len(FAR),))))
    for name in ("mx", "cx", "ro", "io"):
        vm(name + "_src", (4, 384, 128), BF16)
        if name in ("mx", "cx"):
            vm(name + "_dst", (4, 384, 128), BF16)
            vm(name, (4, CHUNK, HALF), BF16)
        sem(name, 4)
    for name in ("act1", "act2"):
        vm(name, (2, PX + 2 * ROW, HALF), BF16)
        vm(name + "_t", (2, HALF, PX), BF16)
        sem(name, 4)
        sem(name + "_t", 1)
    vm("ai", (2, PX, HALF), BF16)
    vm("ai_t", (2, HALF, PX), BF16)
    sem("ai_t", 1)
    sem("ai", 4)
    vm("att", (4, PX, 128), BF16)
    vm("att_t", (2, HALF, PX), BF16)
    sem("att", 4)
    for name in ("do", "n3", "d2", "d1"):
        vm(name + "_src", (PX, HALF), BF16)
        vm(name + "_dst", (PX, HALF), BF16)
        sem(name, 2)
    vm("v2", (PX, HALF), F32)
    vm("v3", (PX, HALF), F32)
    vm("gres", (PX, HALF), F32)
    vm("gtmp", (PX, HALF), F32)
    vm("qkv", (6, PX, 128), BF16)
    vm("kvt", (4, 128, PX), BF16)
    vm("dout", (2, PX, 128), BF16)
    vm("dproj", (6, PX, 128), BF16)
    vm("gr2", (3, PX + 2 * ROW, HALF), BF16)
    vm("gr1", (3, PX + 2 * ROW, HALF), BF16)
    vm("par", (16, 384), F32)
    vm("parown", (16, HALF), F32)
    vm("stat", (16, HALF), F32)
    vm("sums", (16, HALF), F32)
    if inside:
        vm("g1", (4, 4, 336, 128), BF16)
        vm("g2", (4, 4, 336, 128), BF16)
        vm("t1", (4, 4, 144, 128), BF16)
        vm("t2", (4, 4, 144, 128), BF16)
        vm("p3", (4, 4, 144, 128), BF16)
        vm("g3", (4, 4, 192, 128), BF16)
        for name in ("g1", "g2", "p3"):
            sem(name + "z", 4)
            sem(name + "v", 4)
            sem(name + "w", 8)
        vm("sw_src", (48, 128), BF16)
        vm("sw_dst", (48, 128), BF16)
        sem("sw", 1)
        vm("sb_src", (48, 128), F32)
        vm("sb_dst", (48, 128), F32)
        sem("sb", 1)
        for name, nc, rows in (("r1", 3, 112), ("r2", 3, 112), ("r3", 1, 144)):
            vm(name + "_acc", (nc, 4, 4, rows, 128), BF16)
            vm(name + "_own", (nc, rows, 128), F32)
            vm(name + "w_dst", (nc, 2, 4, rows, 128), BF16)
            vm(name + "v_src", (nc, 4, rows, 128), BF16)
            vm(name + "v_dst", (nc, 4, rows, 128), BF16)
            vm(name + "z_src", (4, nc, rows, 128), BF16)
            vm(name + "z_dst", (4, nc, rows, 128), BF16)
            sem(name + "w", nc)
            sem(name + "v", nc)
            sem(name + "z", nc * 4)
    vm("el", (n, 2, 768), F32)
    sem("el", n)
    vm("em", (2 * n, 768), F32)
    vm("wfp", (128, HALF), BF16)
    vm("esel", (2 * n, 128), F32)
    vm("fp", (n, 2, HALF), F32)
    vm("fr", (n, 2, HALF), F32)
    sem("fr", n)
    vm("fx", (4, 1, 128), F32)
    vm("fh", (4, 1, 128), F32)
    sem("fh", 4)
    vm("ft", (4, 1, 128), F32)
    vm("th", (4, 1, 128), F32)
    sem("th", 4)
    vm("fa", (n, 2, HALF), F32)
    sem("fa", n)
    vm("fta", (2 * n, HALF), F32)
    vm("ep", (n, 2, 128), F32)
    vm("er", (n, 2, 128), F32)
    sem("er", n)
    vm("eh", (4, n, 2, 128), F32)
    sem("eh", 4)
    vm("ad", (n, 16, HALF), F32)
    sem("ad", n)
    vm("hb", (4, 16, HALF), F32)
    sem("hb", 4)
    return items


def make_kernel(n, inside, names):
    film_rows = 768 // n

    def kernel(*refs):
        r = Names(names, refs)
        d = lax.axis_index("dp")
        h = lax.axis_index("head")
        x = h // 2
        c = h - 2 * x
        z = d // 2
        y = d - 2 * z
        sib = (d, h + 1 - 2 * c)
        xdev = (d, h + 2 - 4 * x)
        v = x + c * (y - x)
        w = y + c * (x - y)
        vdev = (d + c * (1 - 2 * y), h + (1 - c) * (2 - 4 * x))
        wdev = (d + (1 - c) * (1 - 2 * y), h + c * (2 - 4 * x))

        def slot(xx, yy, o=c):
            if inside:
                return (yy + o * (xx - yy)) * 2 + xx + o * (yy - xx)
            return yy * 2 + xx

        def order(split, i):
            return c * (i // 2) if split else c

        def rc(src, dst, send, recv, dev):
            return pltpu.make_async_remote_copy(
                src_ref=src, dst_ref=dst, send_sem=send, recv_sem=recv, device_id=dev, device_id_type=MESH
            )

        def loop(count, body):
            def step(i, carry):
                body(i)
                return carry

            lax.fori_loop(0, count, step, 0)

        def each(count, body):
            for i in range(count):
                body(i)

        def rows(i, size=CHUNK, base=0):
            return pl.ds(pl.multiple_of(base + i * size, 32), size)

        def dp_start(src_of, dst, send, recv):
            def step(k, carry):
                peer = lax.rem(d + k, n)
                rc(src_of(peer), dst.at[d], send.at[k], recv.at[d], (peer, h)).start()
                return carry

            lax.fori_loop(1, n, step, 0)

        def dp_wait(src_of, dst, send, recv):
            def step(k, carry):
                peer = lax.rem(d + k, n)
                copy = rc(src_of(peer), dst.at[peer], send.at[k], recv.at[peer], (peer, h))
                copy.wait_recv()
                copy.wait_send()
                return carry

            lax.fori_loop(1, n, step, 0)

        def head_start(src_of, dst, send, recv):
            for k in range(1, 4):
                peer = lax.rem(h + k, 4)
                rc(src_of(peer), dst.at[h], send.at[k], recv.at[h], (d, peer)).start()

        def head_wait(src_of, dst, send, recv):
            for k in range(1, 4):
                peer = lax.rem(h + k, 4)
                copy = rc(src_of(peer), dst.at[peer], send.at[k], recv.at[peer], (d, peer))
                copy.wait_recv()
                copy.wait_send()

        class Halves:
            def __init__(self, name, base):
                self.buf, self.base = getattr(r, name), base
                self.send, self.recv = getattr(r, name + "_s"), getattr(r, name + "_r")

            def at(self, core, i):
                return self.buf.at[core, rows(i, CHUNK, self.base)]

            def fill(self, make):
                def body(i):
                    self.buf[c, rows(i, CHUNK, self.base), :] = make(i)
                    ref = self.at(c, i)
                    rc(ref, ref, self.send.at[i], self.recv.at[i], sib).start()

                loop(4, body)

            def wait(self):
                for i in range(4):
                    ref = self.at(1 - c, i)
                    copy = rc(ref, ref, self.send.at[i], self.recv.at[i], sib)
                    copy.wait_recv()
                    copy.wait_send()

        class Parts:
            def __init__(self, name):
                self.src, self.dst = getattr(r, name + "_src"), getattr(r, name + "_dst")
                self.send, self.recv = getattr(r, name + "_s"), getattr(r, name + "_r")

            def copy(self, i):
                at = rows(i, 2 * CHUNK)
                return rc(self.src.at[at], self.dst.at[at], self.send.at[i], self.recv.at[i], sib)

            def fill(self, make):
                def body(i):
                    self.src[rows(i, 2 * CHUNK), :] = make(i).astype(BF16)
                    self.copy(i).start()

                each(2, body)

            def get(self, i):
                copy = self.copy(i)
                copy.wait_recv()
                copy.wait_send()
                return self.dst[rows(i, 2 * CHUNK), :].astype(F32)

        class Gather:
            def __init__(self, name, split):
                self.g, self.split = getattr(r, name), split
                self.zs, self.zr = getattr(r, name + "z_s"), getattr(r, name + "z_r")
                self.vs, self.vr = getattr(r, name + "v_s"), getattr(r, name + "v_r")
                self.ws, self.wr = getattr(r, name + "w_s"), getattr(r, name + "w_r")

            def at(self, i, far_w, far_v):
                o = order(self.split, i)
                vv, ww = x + o * (y - x), y + o * (x - y)
                return (ww + far_w * (1 - 2 * ww)) * 2 + vv + far_v * (1 - 2 * vv)

            def zcopy(self, k):
                peer = (lax.rem(z + k, 4) * 2 + y, h)
                src, dst = self.g.at[self.at(0, 0, 0), 0], self.g.at[self.at(4 - k, 0, 0), 4 - k]
                return rc(src, dst, self.zs.at[k], self.zr.at[4 - k], peer)

            def vcopy(self, far_v, i):
                o = order(self.split, i)
                ref = self.g.at[self.at(i, 0, far_v), i]
                dev = (d + o * (1 - 2 * y), h + (1 - o) * (2 - 4 * x))
                return rc(ref, ref, self.vs.at[i], self.vr.at[i], dev)

            def wcopy(self, far_w, far_v, i):
                o = order(self.split, i)
                ref = self.g.at[self.at(i, far_w, far_v), i]
                dev = (d + (1 - o) * (1 - 2 * y), h + o * (2 - 4 * x))
                return rc(ref, ref, self.ws.at[2 * i + far_v], self.wr.at[2 * i + far_v], dev)

            def own(self):
                for k in range(1, 4):
                    self.zcopy(k).start()
                self.vcopy(0, 0).start()
                self.wcopy(0, 0, 0).start()

            def pass_own(self):
                self.vcopy(1, 0).wait_recv()
                self.wcopy(0, 1, 0).start()

            def pass_z(self, *ks):
                for k in ks:
                    self.zcopy(k).wait_recv()
                    self.vcopy(0, 4 - k).start()
                    self.wcopy(0, 0, 4 - k).start()

            def pass_v(self, *ks):
                for k in ks:
                    self.vcopy(1, 4 - k).wait_recv()
                    self.wcopy(0, 1, 4 - k).start()

            def done(self):
                for i in range(4):
                    for far_v in range(2):
                        self.wcopy(1, far_v, i).wait_recv()

            def finish(self):
                for k in range(1, 4):
                    self.zcopy(k).wait_send()
                for i in range(4):
                    self.vcopy(0, i).wait_send()
                    for far_v in range(2):
                        self.wcopy(0, far_v, i).wait_send()

            def blocks(self, far_w):
                return [(self.at(i, far_w, far_v), i) for i in range(4) for far_v in range(2)]

        class Reduce:
            def __init__(self, name, count):
                get = lambda tail: getattr(r, name + tail)
                self.acc, self.count = get("_acc"), count
                self.wdst, self.ws, self.wr, self.own = get("w_dst"), get("w_s"), get("w_r"), get("_own")
                self.vsrc, self.vdst, self.vs, self.vr = get("v_src"), get("v_dst"), get("v_s"), get("v_r")
                self.zsrc, self.zdst, self.zs, self.zr = get("z_src"), get("z_dst"), get("z_s"), get("z_r")

            def wcopy(self, a):
                ref = self.acc.at[a, pl.ds((1 - w) * 2, 2)]
                return rc(ref, self.wdst.at[a], self.ws.at[a], self.wr.at[a], wdev)

            def vcopy(self, a, size):
                at = pl.ds(a, size)
                return rc(self.vsrc.at[at], self.vdst.at[at], self.vs.at[a], self.vr.at[a], vdev)

            def zcopy(self, a, size, k):
                at = pl.ds(a, size)
                return rc(
                    self.zsrc.at[k, at],
                    self.zdst.at[4 - k, at],
                    self.zs.at[a * 4 + k],
                    self.zr.at[a * 4 + 4 - k],
                    (lax.rem(z + k, 4) * 2 + y, h),
                )

            def start(self, a):
                self.wcopy(a).start()

            def second(self, first, size):
                for a in range(first, first + size):
                    self.wcopy(a).wait_recv()

                    def step(zz, carry):
                        self.vsrc[a, zz] = (
                            self.acc[a, w * 2 + 1 - v, zz].astype(F32) + self.wdst[a, 1 - v, zz].astype(F32)
                        ).astype(BF16)
                        return carry

                    lax.fori_loop(0, 4, step, 0)
                self.vcopy(first, size).start()

            def third(self, first, size):
                self.vcopy(first, size).wait_recv()
                for a in range(first, first + size):

                    for k in range(4):
                        zz = lax.rem(z + k, 4)
                        total = (
                            self.acc[a, w * 2 + v, zz].astype(F32)
                            + self.wdst[a, v, zz].astype(F32)
                            + self.vdst[a, zz].astype(F32)
                        )
                        if k == 0:
                            self.own[a] = total
                        else:
                            self.zsrc[k, a] = total.astype(BF16)
                for k in range(1, 4):
                    self.zcopy(first, size, k).start()

            def finish(self, groups):
                for first, size in groups:
                    self.vcopy(first, size).wait_send()
                    for k in range(1, 4):
                        copy = self.zcopy(first, size, k)
                        copy.wait_recv()
                        copy.wait_send()
                for a in range(self.count):
                    self.wcopy(a).wait_send()

            def last(self, a):
                total = self.own[a]
                for k in range(1, 4):
                    total = total + self.zdst[k, a].astype(F32)
                return total

        def rel(zc):
            return lax.rem(zc - z + 4, 4) if inside else zc

        def where_is(split, xx, yy, zc):
            i = rel(zc)
            return slot(xx, yy, order(split, i)), i

        class Taps:
            def __init__(self, packed, last, split):
                self.packed, self.last, self.split = packed, last, split

            def block(self, tap, zc, xx, yy):
                a, b = tap // 3, tap % 3
                q, i = where_is(self.split, xx, yy, zc)
                if b < 2:
                    return self.packed[q, i, pl.ds(a * 112 + b * 48, 48), :]
                return self.last[q, i, pl.ds(a * 48, 48), :]

            def unpack(self, places):
                for q, i in places:
                    for a in range(3):
                        self.last[q, i, pl.ds(a * 48, 48), :] = last_tap(self.packed[q, i, pl.ds(a * 112, 112), :])

        class Plain:
            def __init__(self, blocks, split):
                self.blocks, self.split = blocks, split

            def block(self, tap, zc, xx, yy):
                q, i = where_is(self.split, xx, yy, zc)
                return self.blocks[q, i, pl.ds(tap * 48, 48), :]

            def unpack(self, places):
                for q, i in places:
                    self.blocks[q, i] = jnp.concatenate(unpack_four(r.p3[q, i]), axis=0)

        k1, k2, k3 = Taps(r.g1, r.t1, True), Taps(r.g2, r.t2, False), Plain(r.g3, True)

        def wtile(g, tap, zc, xx):
            return jnp.concatenate(
                [g.block(tap, zc, xx, 0), g.block(tap, zc, xx, 1), jnp.zeros((32, 128), BF16)], axis=0
            )

        def wtap(g, tap, zcs):
            return jnp.concatenate(
                [jnp.concatenate([wtile(g, tap, zc, xx) for xx in range(2)], axis=1) for zc in zcs], axis=0
            )

        ALL = (0, 2, 1, 3)

        def half_of(core):
            return (core, core + 2)

        def wproj(zcs):
            return jnp.concatenate(
                [
                    jnp.concatenate([wtile(k3, j, zc, xx) for xx in range(2) for j in range(3)], axis=1)
                    for zc in zcs
                ],
                axis=0,
            )

        def flat(buf, base, i, size):
            return jnp.concatenate([buf[0, rows(i, size, base), :], buf[1, rows(i, size, base), :]], axis=1)

        barrier = pltpu.get_barrier_semaphore()

        def greet(k, carry):
            pl.semaphore_signal(barrier, inc=1, device_id=(lax.rem(d + k, n), h), device_id_type=MESH)
            return carry

        lax.fori_loop(1, n, greet, 0)
        for k in range(1, 4):
            pl.semaphore_signal(barrier, inc=1, device_id=(d, lax.rem(h + k, 4)), device_id_type=MESH)
        def fetch(name):
            return pltpu.make_async_copy(getattr(r, name + "_far"), getattr(r, name), r.far_s.at[FAR.index(name)])

        for name in FAR:
            fetch(name).start()
        if inside:
            ga, gb, gc = Gather("g1", True), Gather("g2", False), Gather("p3", True)
            for a in range(3):
                r.g1[ga.at(0, 0, 0), 0, pl.ds(a * 112, 112), :] = pack_taps(*[r.k1[3 * a + b] for b in range(3)])
        pl.semaphore_wait(barrier, n - 1 + 3)
        if inside:
            ga.own()

        for name in FAR:
            fetch(name).wait()
        def head_copy(src, dst, send, recv, k):
            peer = lax.rem(h + k, 4)
            return rc(src.at[peer], dst.at[h], send.at[k], recv.at[h], (d, peer))

        for step in range(2):
            m = x + (1 - step) * (1 - 2 * x)
            keep, spread = plan(r.steps[m], 384)
            low = (keep * r.images[m].astype(F32) + spread * r.noise[m].astype(F32)).astype(BF16)
            for core in range(2):
                r.mx_src[m * 2 + core] = pack_pixels(dot(low, r.sel[core])).astype(BF16)
            for k in (2, 3 - 2 * c) if step == 0 else (1 + 2 * c,):
                head_copy(r.mx_src, r.mx_dst, r.mx_s, r.mx_r, k).start()
        r.mx_dst[h] = r.mx_src[h]
        if inside:
            ga.pass_own()

        r.el[d] = silu(r.emb[...].astype(F32)).astype(BF16).astype(F32)
        dp_start(lambda p: r.el.at[d], r.el, r.el_s, r.el_r)

        if inside:
            blocks = dot(r.wa[...], r.selp[: 3 * BLK, : 3 * 128]).astype(BF16)
            r.sw_src[...] = blocks[:, 128:256]
            swap = rc(r.sw_src, r.sw_dst, r.sw_s.at[0], r.sw_r.at[0], sib)
            swap.start()
            for a in range(3):
                r.g2[gb.at(0, 0, 0), 0, pl.ds(a * 112, 112), :] = pack_taps(*[r.k2[3 * a + b] for b in range(3)])
        r.par[0:3, :] = r.gains[...]
        r.par[3:13, :] = r.biases[...]
        r.par[13:16, :] = jnp.zeros((3, 384), F32)
        r.parown[...] = exact_dot(r.par[...], r.sel[c])

        def prow(i):
            return r.parown[pl.ds(i, 1), :]

        for buf in (r.act1, r.act2):
            for core in range(2):
                buf[core, pl.ds(0, ROW), :] = jnp.zeros((ROW, HALF), BF16)
                buf[core, pl.ds(PX + ROW, ROW), :] = jnp.zeros((ROW, HALF), BF16)
        for buf in (r.gr1, r.gr2):
            for b in range(3):
                buf[b, pl.ds(0, ROW), :] = jnp.zeros((ROW, HALF), BF16)
                buf[b, pl.ds(PX + ROW, ROW), :] = jnp.zeros((ROW, HALF), BF16)
        r.wfp[...] = jnp.zeros((128, HALF), BF16)
        r.wfp[pl.ds(0, film_rows), :] = dot(r.wf[...], r.selp[: 2 * BLK, :HALF]).astype(BF16)
        if inside:
            ga.pass_z(1, 3, 2)
            gb.own()

        count = float(PX * 12)

        def fold(vals):
            return jnp.sum(vals.reshape(CHUNK // 8, 8, HALF), axis=0)

        def sums_of(fn, k):
            def step(i, carry):
                return tuple(a + fold(b) for a, b in zip(carry, fn(i)))

            zero = jnp.zeros((8, HALF), F32)
            return lax.fori_loop(0, 4, step, (zero,) * k)

        def group_mean(part):
            return jnp.sum(exact_dot(part, r.gmask[...]), axis=0, keepdims=True) / count

        def norm(load, which, total):
            mean = group_mean(total)
            (square,) = sums_of(lambda i: (jnp.square(load(i) - mean),), 1)
            inv = lax.rsqrt(group_mean(square) + EPS)
            r.stat[pl.ds(2 * which, 1), :] = mean
            r.stat[pl.ds(2 * which + 1, 1), :] = inv
            return mean, inv

        zero8 = jnp.zeros((8, HALF), F32)

        def norm_back(sums, load_grad, load_hat, coef, inv):
            plain, cross = sums
            means = exact_dot(jnp.concatenate([coef * plain, coef * cross], axis=0), r.gmask[...])
            plain_mean = jnp.sum(means[:8], axis=0, keepdims=True) / count
            cross_mean = jnp.sum(means[8:], axis=0, keepdims=True) / count
            outer, base, slope = inv * coef, inv * plain_mean, inv * cross_mean

            def chunk(i):
                return outer * load_grad(i) - base - load_hat(i) * slope

            return (
                jnp.sum(plain, axis=0, keepdims=True),
                jnp.sum(cross, axis=0, keepdims=True),
                chunk,
            )

        def transposed(name, core):
            ref = getattr(r, name).at[core]
            return rc(ref, ref, getattr(r, name + "_s").at[0], getattr(r, name + "_r").at[0], sib)

        def transpose_act(buf, base, name):
            out = getattr(r, name)
            for q in range(4):
                out[c, :, pl.ds(q * CHUNK, CHUNK)] = jnp.transpose(buf[c, pl.ds(base + q * CHUNK, CHUNK), :])
            transposed(name, c).start()

        def transposed_wait(name):
            copy = transposed(name, 1 - c)
            copy.wait_recv()
            copy.wait_send()

        head_wait(lambda p: r.mx_src.at[p], r.mx_dst, r.mx_s, r.mx_r)

        def unpack_mixed(i, carry):
            vals = unpack_pixels(r.mx_dst[i])
            r.mx[i] = vals
            return carry + fold(vals.astype(F32))

        mixed_sum = lax.fori_loop(0, 4, unpack_mixed, zero8)

        def mixed(i):
            return r.mx[i].astype(F32)

        if inside:
            ga.pass_v(1, 3)
        mean1, inv1 = norm(mixed, 0, mixed_sum)
        if inside:
            ga.pass_v(2)
        gain1, shift1 = prow(0), prow(3)
        act1 = Halves("act1", ROW)

        def affine(mean, inv, gain, shift):
            return inv * gain, shift - mean * (inv * gain)

        mul1, add1 = affine(mean1, inv1, gain1, shift1)

        def pre1(i):
            return mixed(i) * mul1 + add1

        act1.fill(lambda i: silu(pre1(i)).astype(BF16))
        dp_wait(lambda p: r.el.at[d], r.el, r.el_s, r.el_r)
        for j in range(n):
            r.em[pl.ds(2 * j, 2), :] = r.el[j]
        place = lax.broadcasted_iota(jnp.int32, (768, 128), 0) - film_rows * d
        lane = lax.broadcasted_iota(jnp.int32, (768, 128), 1)
        pick = jnp.where((place == lane) & (lane < film_rows), 1.0, 0.0).astype(BF16)
        r.esel[...] = dot(r.em[...].astype(BF16), pick)
        film_part = dot(r.esel[...].astype(BF16), r.wfp[...])
        for j in range(n):
            r.fp[j] = film_part[2 * j : 2 * j + 2]
        dp_start(lambda p: r.fp.at[p], r.fr, r.fr_s, r.fr_r)
        r.fr[d] = r.fp[d]
        if inside:
            swap.wait()
            got = r.sw_dst[...]
            keep0, keep2 = blocks[:, :128], blocks[:, 256:]
            r.p3[gc.at(0, 0, 0), 0] = pack_four(
                jnp.where(c == 0, keep0, got),
                jnp.where(c == 0, keep2, keep0),
                jnp.where(c == 0, got, keep2),
                r.wo[...],
            )
        act1.wait()
        transpose_act(r.act1, ROW, "act1_t")
        if inside:
            gb.pass_own()
            gb.pass_z(1, 3, 2)
            gc.own()
        def split_cot(m, carry):
            for core in range(2):
                r.cx_src[m * 2 + core] = pack_pixels(dot(r.cot[m], r.sel[core])).astype(BF16)
            return carry

        lax.fori_loop(0, 2, split_cot, 0)
        column = lax.broadcasted_iota(jnp.int32, (1, ROW, HALF), 1)
        not_first = jnp.where(column > 0, 1.0, 0.0)
        not_last = jnp.where(column < ROW - 1, 1.0, 0.0)

        def in_rows(vals, mask):
            return (vals.reshape(CHUNK // ROW, ROW, HALF) * mask).reshape(CHUNK, HALF)

        def from_left(vals):
            return in_rows(pltpu.roll(vals, 1, 0), not_first)

        def from_right(vals):
            return in_rows(pltpu.roll(vals, CHUNK - 1, 0), not_last)

        def conv(buf, g, store, between):
            weights = lambda: jnp.concatenate(
                [jnp.concatenate([wtap(g, 3 * a + b, ALL) for b in range(3)], axis=1) for a in range(3)], axis=0
            )

            total = zero8
            for i in range(2):
                left = jnp.concatenate([flat(buf, ROW * a, i, 2 * CHUNK) for a in range(3)], axis=1)
                out = dot(left, weights())
                for j in range(2):
                    part = out[j * CHUNK : j * CHUNK + CHUNK]
                    part = part[:, HALF : 2 * HALF] + from_left(part[:, :HALF]) + from_right(part[:, 2 * HALF :])
                    total = total + fold(store(2 * i + j, part))
                if i == 0:
                    between()
            return total

        if inside:
            k1.unpack(ga.blocks(0))
            ga.done()
            k1.unpack(ga.blocks(1))

        dp_wait(lambda p: r.fp.at[p], r.fr, r.fr_s, r.fr_r)
        film_sum = r.fr[0]
        for j in range(1, n):
            film_sum = film_sum + r.fr[j]
        for m in range(2):
            for core in range(2):
                r.fx[m * 2 + core] = film_sum[m : m + 1, core * 128 : core * 128 + 128]
        head_start(lambda p: r.fx.at[p], r.fh, r.fh_s, r.fh_r)
        r.fh[h] = r.fx[h]

        def store_v2(i, vals):
            vals = vals + prow(6)
            r.v2[rows(i), :] = vals
            return vals

        v2_sum = conv(r.act1, k1, store_v2, (lambda: gb.pass_v(1, 3, 2)) if inside else lambda: None)
        head_wait(lambda p: r.fx.at[p], r.fh, r.fh_s, r.fh_r)
        scale = 1.0 + (jnp.concatenate([r.fh[0], r.fh[1]], axis=1) + prow(8))
        shift = jnp.concatenate([r.fh[2], r.fh[3]], axis=1) + prow(9)
        head_start(lambda p: r.cx_src.at[p], r.cx_dst, r.cx_s, r.cx_r)
        r.cx_dst[h] = r.cx_src[h]
        mean2, inv2 = norm(lambda i: r.v2[rows(i), :], 1, v2_sum)
        gain2, shift2 = prow(1), prow(4)
        act2 = Halves("act2", ROW)

        def hat2(i):
            return (r.v2[rows(i), :] - mean2) * inv2

        mul2, add2 = affine(mean2, inv2, gain2 * scale, shift2 * scale + shift)

        def pre2(i):
            return r.v2[rows(i), :] * mul2 + add2

        act2.fill(lambda i: silu(pre2(i)).astype(BF16))
        if inside:
            gc.pass_own()
            gc.pass_z(1, 3, 2)

        transpose_act(r.act2, ROW, "act2_t")
        act2.wait()
        if inside:
            k2.unpack(gb.blocks(0))
            gb.done()
            k2.unpack(gb.blocks(1))

        def store_v3(i, vals):
            vals = mixed(i) + (vals + prow(7))
            r.v3[rows(i), :] = vals
            return vals

        v3_sum = conv(r.act2, k2, store_v3, (lambda: gc.pass_v(1, 3, 2)) if inside else lambda: None)
        mean3, inv3 = norm(lambda i: r.v3[rows(i), :], 2, v3_sum)
        gain3, shift3 = prow(2), prow(5)
        ai = Halves("ai", 0)

        def hat3(i):
            return (r.v3[rows(i), :] - mean3) * inv3

        mul3, add3 = affine(mean3, inv3, gain3, shift3)
        ai.fill(lambda i: (r.v3[rows(i), :] * mul3 + add3).astype(BF16))
        transpose_act(r.ai, 0, "ai_t")

        if inside:
            k3.unpack(gc.blocks(0))
            gc.done()
            k3.unpack(gc.blocks(1))
        head_wait(lambda p: r.cx_src.at[p], r.cx_dst, r.cx_s, r.cx_r)

        def unpack_cot(i):
            r.cx[i] = unpack_pixels(r.cx_dst[i])

        loop(4, unpack_cot)
        dop = Parts("do")

        def cot_rows(i):
            return jnp.concatenate([r.cx[2 * i], r.cx[2 * i + 1]], axis=0)

        dop.fill(lambda i: dot_nt(cot_rows(i), wtap(k3, 3, half_of(1 - c))))

        ai.wait()
        bias_proj = [prow(10)[:, :128], prow(10)[:, 128:], None, None, prow(11)[:, :128], prow(11)[:, 128:]]

        def project(i):
            out = dot(flat(r.ai, 0, i, 2 * CHUNK), wproj(ALL))
            for k in range(6):
                part = out[:, k * 128 : k * 128 + 128]
                if bias_proj[k] is not None:
                    part = part + bias_proj[k]
                r.qkv[k, rows(i, 2 * CHUNK), :] = part.astype(BF16)

        each(2, project)

        def do_own(i):
            full = (dot_nt(cot_rows(i), wtap(k3, 3, half_of(c))) + dop.get(i)).astype(BF16)
            for k in range(2):
                r.dout[k, rows(i, 2 * CHUNK), :] = full[:, k * 128 : k * 128 + 128]

        each(2, do_own)

        factor = 1.0 / math.sqrt(HEAD_DIM)
        factor2 = factor * math.log2(math.e)
        att = []

        def transposes(k):
            r.kvt[k] = jnp.transpose(r.qkv[k + 2])

        loop(4, transposes)

        def att_copy(core, k):
            ref = r.att.at[core * 2 + k]
            return rc(ref, ref, r.att_s.at[k], r.att_r.at[k], sib)

        def att_t_copy(core, k):
            ref = r.att_t.at[core, pl.ds(pl.multiple_of(k * 128, 128), 128)]
            return rc(ref, ref, r.att_s.at[2 + k], r.att_r.at[2 + k], sib)

        def one_head(k):
            lows, grads = [], []
            for b in range(2):
                at = pl.ds(b * 2 * CHUNK, 2 * CHUNK)
                query = r.qkv[k, at, :]
                grad = r.dout[k, at, :]
                scores = dot_nt(r.qkv[2 + k], query)
                peak = jnp.max(scores, axis=0, keepdims=True)
                expo = jnp.exp2((scores - peak) * factor2)
                inverse = 1.0 / jnp.sum(expo, axis=0, keepdims=True)
                low = (expo * inverse).astype(BF16)
                got = dot(r.kvt[2 + k], low)
                got_low = got.astype(BF16)
                r.att_t[c, pl.ds(pl.multiple_of(k * 128, 128), 128), at] = got_low
                r.att[2 * c + k, at, :] = jnp.transpose(got_low)
                spread = jnp.sum(got * jnp.transpose(grad).astype(F32), axis=0, keepdims=True)
                probs_grad = dot_nt(r.qkv[4 + k], grad)
                scores_grad = ((probs_grad - spread) * inverse * expo).astype(BF16)
                back = dot(r.kvt[k], scores_grad)
                r.dproj[k, at, :] = (jnp.transpose(back) * factor).astype(BF16)
                lows.append(low)
                grads.append(scores_grad)
            att_copy(c, k).start()
            att_t_copy(c, k).start()
            r.dproj[4 + k] = dot(jnp.concatenate(lows, axis=1), r.dout[k]).astype(BF16)
            r.dproj[2 + k] = (dot(jnp.concatenate(grads, axis=1), r.qkv[k]) * factor).astype(BF16)

        loop(2, one_head)

        n3 = Parts("n3")

        def proj_rows(i):
            return jnp.concatenate([r.dproj[k, rows(i, 2 * CHUNK), :] for k in range(6)], axis=1)

        n3.fill(lambda i: dot_nt(proj_rows(i), wproj(half_of(1 - c))))

        def rows_of(act_t):
            return jnp.concatenate([act_t[p // 2, pl.ds(p % 2 * 128, BLK), :] for p in range(4)], axis=0)

        for k in range(2):
            copy = att_copy(1 - c, k)
            copy.wait_recv()
            copy.wait_send()

        def result(i):
            left = jnp.concatenate([r.att[p, rows(i), :] for p in range(4)], axis=1)
            branch = dot(left, wtap(k3, 3, ALL)) + prow(12)
            r.ro_src[i] = pack_pixels(r.v3[rows(i), :] + branch).astype(BF16)

        loop(4, result)
        head_start(lambda p: r.ro_src.at[p], r.ro_dst, r.ro_s, r.ro_r)
        r.ro_dst[h] = r.ro_src[h]

        if inside:
            red1, red2, red3 = Reduce("r1", 3), Reduce("r2", 3), Reduce("r3", 1)
            acc1, acc2, acc3 = r.r1_acc, r.r2_acc, r.r3_acc
        else:
            acc1, acc2, acc3 = r.first, r.second, r.attend

        transposed_wait("ai_t")
        for k in range(2):
            copy = att_t_copy(1 - c, k)
            copy.wait_recv()
            copy.wait_send()
        right = jnp.concatenate([r.dproj[k] for k in range(6)], axis=1)
        cot_all = jnp.concatenate([r.cx[i] for i in range(4)], axis=0)
        attend_out = dot(rows_of(r.ai_t), right)
        output_out = dot(rows_of(r.att_t), cot_all)
        for p, zc in enumerate(ALL):
            for yy in range(2):
                for xx in range(2):
                    row = p * BLK + yy * 48
                    tiles = [
                        attend_out[row : row + 48, (xx * 3 + j) * 128 : (xx * 3 + j) * 128 + 128] for j in range(3)
                    ]
                    acc3[0, slot(xx, yy), zc] = pack_four(
                        *tiles, output_out[row : row + 48, xx * 128 : xx * 128 + 128]
                    ).astype(acc3.dtype)
        if inside:
            red3.start(0)

        def proj_sums(i, carry):
            q = jnp.concatenate([r.dproj[0, rows(i), :], r.dproj[1, rows(i), :]], axis=1).astype(F32)
            val = jnp.concatenate([r.dproj[4, rows(i), :], r.dproj[5, rows(i), :]], axis=1).astype(F32)
            return (carry[0] + fold(q), carry[1] + fold(val), carry[2] + fold(r.cx[i].astype(F32)))

        qsum, vsum, csum = lax.fori_loop(0, 4, proj_sums, (zero8, zero8, zero8))
        r.sums[pl.ds(3 + 7, 1), :] = jnp.sum(qsum, axis=0, keepdims=True)
        r.sums[pl.ds(3 + 8, 1), :] = jnp.sum(vsum, axis=0, keepdims=True)
        r.sums[pl.ds(3 + 9, 1), :] = jnp.sum(csum, axis=0, keepdims=True)
        r.sums[pl.ds(13, 3), :] = jnp.zeros((3, HALF), F32)

        def n3_own(i, carry):
            both = dot_nt(proj_rows(i), wproj(half_of(c))) + n3.get(i)
            for j in range(2):
                vals = both[j * CHUNK : j * CHUNK + CHUNK]
                r.gtmp[rows(2 * i + j), :] = vals
                carry = carry[0] + fold(vals), carry[1] + fold(vals * hat3(2 * i + j))
            return carry

        sums3 = n3_own(1, n3_own(0, (zero8, zero8)))
        plain3, cross3, back3 = norm_back(sums3, lambda i: r.gtmp[rows(i), :], hat3, gain3, inv3)
        r.sums[pl.ds(2, 1), :] = cross3
        r.sums[pl.ds(3 + 2, 1), :] = plain3

        def shifted(buf, i, vals):
            buf[0, rows(i, CHUNK, ROW), :] = from_right(vals).astype(BF16)
            buf[1, rows(i, CHUNK, ROW), :] = vals.astype(BF16)
            buf[2, rows(i, CHUNK, ROW), :] = from_left(vals).astype(BF16)

        def residual_back(i, carry):
            vals = r.cx[i].astype(F32) + back3(i)
            r.gres[rows(i), :] = vals
            shifted(r.gr2, i, vals)
            return carry + fold(vals.astype(BF16).astype(F32))

        bias_two = lax.fori_loop(0, 4, residual_back, jnp.zeros((8, HALF), F32))
        r.sums[pl.ds(3 + 4, 1), :] = jnp.sum(bias_two, axis=0, keepdims=True)

        def act_back(buf, g, core, i, size):
            left = jnp.concatenate(
                [buf[b, rows(i, size, 2 * ROW - ROW * a), :] for a in range(3) for b in range(3)], axis=1
            )
            right = jnp.concatenate(
                [wtap(g, 3 * a + b, half_of(core)) for a in range(3) for b in range(3)], axis=1
            )
            return dot_nt(left, right)

        def conv_back(parts, buf, g):
            parts.fill(lambda i: act_back(buf, g, 1 - c, i, 2 * CHUNK))

        def conv_back_own(parts, buf, g, outer, hat):
            def own(i, carry):
                vals = act_back(buf, g, c, i, 2 * CHUNK) + parts.get(i)
                for j in range(2):
                    at = 2 * i + j
                    grad = vals[j * CHUNK : j * CHUNK + CHUNK] * outer(at)
                    r.gtmp[rows(at), :] = grad
                    carry = carry[0] + fold(grad), carry[1] + fold(grad * hat(at))
                return carry

            return own(1, own(0, (zero8, zero8)))

        def kernel_grad(act_t, buf, acc, after):
            def step(a):
                right = jnp.concatenate([buf[b, pl.ds(2 * ROW - ROW * a, PX), :] for b in range(3)], axis=1)
                out = dot(rows_of(act_t), right)
                for p, zc in enumerate(ALL):
                    for yy in range(2):
                        for xx in range(2):
                            row = p * BLK + yy * 48
                            tiles = [
                                out[row : row + 48, b * HALF + xx * 128 : b * HALF + xx * 128 + 128].astype(acc.dtype)
                                for b in range(3)
                            ]
                            acc[a, slot(xx, yy), zc] = pack_taps(*tiles)
                after(a)

            each(3, step)

        serve = inside
        d2 = Parts("d2")
        transposed_wait("act2_t")
        kernel_grad(r.act2_t, r.gr2, acc2, red2.start if inside else lambda a: None)
        if serve:
            red3.second(0, 1)
        conv_back(d2, r.gr2, k2)
        if serve:
            red2.second(0, 1)
        sums2 = conv_back_own(d2, r.gr2, k2, lambda i: silu_slope(pre2(i)), hat2)
        if serve:
            red2.second(1, 1)
            red3.third(0, 1)

        plain2, cross2, back2 = norm_back(sums2, lambda i: r.gtmp[rows(i), :], hat2, gain2 * scale, inv2)
        r.sums[pl.ds(1, 1), :] = scale * cross2
        r.sums[pl.ds(3 + 1, 1), :] = scale * plain2
        film_scale_term = gain2 * cross2 + shift2 * plain2
        r.sums[pl.ds(3 + 5, 1), :] = film_scale_term
        r.sums[pl.ds(3 + 6, 1), :] = plain2
        for j in range(2):
            r.ft[j] = film_scale_term[:, j * 128 : j * 128 + 128]
            r.ft[2 + j] = plain2[:, j * 128 : j * 128 + 128]
        head_start(lambda p: r.ft.at[p], r.th, r.th_s, r.th_r)
        r.th[h] = r.ft[h]

        def first_back(i, carry):
            vals = back2(i)
            shifted(r.gr1, i, vals)
            return carry + fold(vals.astype(BF16).astype(F32))

        bias_one = lax.fori_loop(0, 4, first_back, jnp.zeros((8, HALF), F32))
        r.sums[pl.ds(3 + 3, 1), :] = jnp.sum(bias_one, axis=0, keepdims=True)

        if serve:
            red2.second(2, 1)
            red2.third(0, 1)
            red2.third(1, 1)

        head_wait(lambda p: r.ft.at[p], r.th, r.th_s, r.th_r)
        for m in range(2):
            r.fa[d, pl.ds(m, 1), :] = jnp.concatenate([r.th[2 * m], r.th[2 * m + 1]], axis=1)
        dp_start(lambda p: r.fa.at[d], r.fa, r.fa_s, r.fa_r)

        d1 = Parts("d1")

        def after_chunk(a):
            if serve:
                red1.start(a)
                if a == 1:
                    red2.third(2, 1)

        transposed_wait("act1_t")
        kernel_grad(r.act1_t, r.gr1, acc1, after_chunk)
        conv_back(d1, r.gr1, k1)
        if serve:
            red1.second(0, 1)

        dp_wait(lambda p: r.fa.at[d], r.fa, r.fa_s, r.fa_r)
        for j in range(n):
            r.fta[pl.ds(2 * j, 2), :] = r.fa[j]
        film_block = dot_tn_high(r.esel[...], r.fta[...])
        r.film[...] = jnp.concatenate([film_block[:film_rows, :BLK], film_block[:film_rows, 128 : 128 + BLK]], axis=1)
        embed_part = dot_nt_high(r.fta[...], r.wfp[...].astype(F32))
        for j in range(n):
            r.ep[j] = embed_part[2 * j : 2 * j + 2]
        dp_start(lambda p: r.ep.at[p], r.er, r.er_s, r.er_r)
        r.er[d] = r.ep[d]

        def hat1(i):
            return (mixed(i) - mean1) * inv1

        sums1 = conv_back_own(d1, r.gr1, k1, lambda i: silu_slope(pre1(i)), hat1)
        if serve:
            red1.second(1, 1)

        dp_wait(lambda p: r.ep.at[p], r.er, r.er_s, r.er_r)
        r.eh[h] = r.er[...]
        head_start(lambda p: r.eh.at[h], r.eh, r.eh_s, r.eh_r)
        plain1, cross1, back1 = norm_back(sums1, lambda i: r.gtmp[rows(i), :], hat1, gain1, inv1)
        r.sums[pl.ds(0, 1), :] = cross1
        r.sums[pl.ds(3, 1), :] = plain1
        r.ad[d] = r.sums[...]
        dp_start(lambda p: r.ad.at[d], r.ad, r.ad_s, r.ad_r)

        if serve:
            red1.second(2, 1)
            red1.third(0, 1)
        keep, _ = plan(r.steps[x], HALF)

        def image_back(i):
            return pack_pixels(keep * (r.gres[rows(i), :] + back1(i))).astype(BF16)

        for k in (2, 1, 3):
            peer = lax.rem(h + k, 4)
            r.io_src[peer] = image_back(peer)
            rc(r.io_src.at[peer], r.io_dst.at[h], r.io_s.at[k], r.io_r.at[h], (d, peer)).start()
        r.io_dst[h] = image_back(h)
        if serve:
            red1.third(1, 1)
            red1.third(2, 1)

        dp_wait(lambda p: r.ad.at[d], r.ad, r.ad_s, r.ad_r)
        total = r.ad[0]
        for j in range(1, n):
            total = total + r.ad[j]
        r.hb[h] = total
        head_start(lambda p: r.hb.at[h], r.hb, r.hb_s, r.hb_r)
        head_wait(lambda p: r.ro_src.at[p], r.ro_dst, r.ro_s, r.ro_r)

        if inside:
            red2.finish(((0, 1), (1, 1), (2, 1)))
            for a in range(3):
                r.second[a] = red2.last(a)

        head_wait(lambda p: r.hb.at[h], r.hb, r.hb_s, r.hb_r)
        even = r.hb[0] + r.hb[2]
        odd = r.hb[1] + r.hb[3]
        wide = jnp.concatenate(
            [even[:, :BLK], odd[:, :BLK], even[:, 128 : 128 + BLK], odd[:, 128 : 128 + BLK]], axis=1
        )
        r.gains_out[...] = wide[0:3]
        r.biases_out[...] = wide[3:13]

        head_wait(lambda p: r.eh.at[h], r.eh, r.eh_s, r.eh_r)
        pieces = []
        for j in range(n):
            piece = (r.eh[0, j] + r.eh[1, j]) + (r.eh[2, j] + r.eh[3, j])
            pieces.append(piece[:, :film_rows])
        r.embed_grad[...] = jnp.concatenate(pieces, axis=1) * silu_slope(r.emb[...].astype(F32))

        head_wait(lambda p: r.io_src.at[p], r.io_dst, r.io_s, r.io_r)

        if inside:
            red3.finish(((0, 1),))
            tiles = unpack_four(red3.last(0))
            r.sb_src[...] = jnp.where(c == 0, tiles[2], tiles[0])
            back = rc(r.sb_src, r.sb_dst, r.sb_s.at[0], r.sb_r.at[0], sib)
            back.start()
            r.output[...] = tiles[3]
            for part in (ga, gb, gc):
                part.finish()
            red1.finish(((0, 1), (1, 1), (2, 1)))
            for a in range(3):
                r.first[a] = red1.last(a)
            back.wait()
            r.attend[:, 0:128] = jnp.where(c == 0, tiles[0], tiles[1])
            r.attend[:, 128:256] = r.sb_dst[...]
            r.attend[:, 256:384] = jnp.where(c == 0, tiles[1], tiles[2])

    return kernel


def make_writer(names_in, names_out):
    def kernel(*refs):
        count, wide = len(names_in), len(names_out)
        far_in, far_out = refs[:count], refs[count : count + wide]
        near_in, near_out = refs[count + wide : 2 * count + wide], refs[2 * count + wide : 2 * count + 2 * wide]
        sem_in, sem_out = refs[-2:]
        src, dst = Names(names_in, near_in), Names(names_out, near_out)
        loads = {
            name: pltpu.make_async_copy(far_in[i], near_in[i], sem_in.at[i]) for i, name in enumerate(names_in)
        }
        stores = {
            name: pltpu.make_async_copy(near_out[i], far_out[i], sem_out.at[i]) for i, name in enumerate(names_out)
        }
        for name in ("sel", "ro_dst", "io_dst"):
            loads[name].start()
        for name in names_in:
            if name not in ("sel", "ro_dst", "io_dst"):
                loads[name].start()
        loads["sel"].wait()
        for name, packed in (("result", "ro_dst"), ("image_grad", "io_dst")):
            loads[packed].wait()
            ref = getattr(src, packed)
            for m in range(2):
                getattr(dst, name)[m] = dot_nt(unpack_pixels(ref[2 * m]), src.sel[0]) + dot_nt(
                    unpack_pixels(ref[2 * m + 1]), src.sel[1]
                )
            stores[name].start()
        for name in ("first", "second"):
            if name in names_out:
                loads[name].wait()
                for a in range(3):
                    block = getattr(src, name)[a]
                    getattr(dst, name)[3 * a] = block[:48, :BLK]
                    getattr(dst, name)[3 * a + 1] = block[48:96, :BLK]
                    getattr(dst, name)[3 * a + 2] = last_tap(block)[:, :BLK]
                stores[name].start()
        if "attend" in names_out:
            loads["attend"].wait()
            dst.attend[...] = jnp.concatenate([src.attend[:, j * 128 : j * 128 + BLK] for j in range(3)], axis=1)
            stores["attend"].start()
            loads["output"].wait()
            dst.output[...] = src.output[:, :BLK]
            stores["output"].start()
        for name in ("embed_grad", "film", "gains_out", "biases_out"):
            loads[name].wait()
            getattr(dst, name)[...] = getattr(src, name)[...]
            stores[name].start()
        for name in names_out:
            stores[name].wait()

    return kernel


def per_device(n, *args):
    (
        images,
        noise_field,
        time_steps,
        embedding,
        first_kernel,
        second_kernel,
        film_weight,
        attend_weight,
        output_weight,
        norm_gains,
        biases,
        cotangent,
    ) = args
    inside = n == 8
    maps, height, width, channels = images.shape
    flat_shape = (maps, height * width, channels)
    film_rows = film_weight.shape[0]
    inputs = dict(
        steps=time_steps,
        images=images.reshape(flat_shape),
        noise=noise_field.reshape(flat_shape),
        cot=cotangent.reshape(flat_shape),
        emb=embedding,
        k1=first_kernel.reshape((9,) + first_kernel.shape[2:]),
        k2=second_kernel.reshape((9,) + second_kernel.shape[2:]),
        wf=film_weight,
        wa=attend_weight,
        wo=output_weight,
        gains=norm_gains,
        biases=biases,
        sel=jnp.asarray(channel_lanes(), BF16),
        gmask=jnp.asarray(group_mask(), BF16),
        selp=jnp.asarray(block_lanes(3), BF16),
    )
    shapes = dict(
        ro_dst=(4, 384, 128),
        io_dst=(4, 384, 128),
        embed_grad=embedding.shape,
        first=(3, 112, 128),
        second=(3, 112, 128),
        film=film_weight.shape,
        attend=(48, 384),
        output=(48, 128),
        gains_out=norm_gains.shape,
        biases_out=biases.shape,
    )
    names_in, names_out = list(INPUTS), list(OUTPUTS)
    core = lax.axis_index("head") % 2
    if not inside:
        def whole(array, row_axis):
            array = lax.all_gather(array, "dp", axis=row_axis, tiled=True)
            return lax.all_gather(array, "head", axis=array.ndim - 1, tiled=True)

        def spread(array, count):
            taps = array.shape[0]
            array = array.reshape(taps, 4, 2, 48, 2, 2, BLK)
            array = lax.dynamic_index_in_dim(array, core, 5, keepdims=False)
            array = jnp.transpose(array, (2, 4, 1, 0, 3, 5))
            array = jnp.pad(array, ((0, 0),) * 5 + ((0, 32),))
            return array.reshape(4, 4, taps * 48, 128)

        full_a = whole(attend_weight, 0).reshape(384, 2, 3, 2, BLK)
        full_a = jnp.transpose(full_a, (2, 0, 1, 3, 4)).reshape(3, 384, 384)
        full_o = whole(output_weight, 0)[None]
        for name, last, array in (("g1", "t1", first_kernel), ("g2", "t2", second_kernel)):
            blocks = spread(whole(array, 2).reshape(9, 384, 384), 9).reshape(4, 4, 3, 3, 48, 128)
            two = blocks[:, :, :, :2].reshape(4, 4, 3, 96, 128)
            inputs[name] = jnp.pad(two, ((0, 0),) * 3 + ((0, 16), (0, 0))).reshape(4, 4, 336, 128)
            inputs[last] = blocks[:, :, :, 2].reshape(4, 4, 144, 128)
        inputs["g3"] = spread(jnp.concatenate([full_a, full_o], axis=0), 4)
        names_in += ["g1", "g2", "t1", "t2", "g3"]
        shapes["first"] = shapes["second"] = (3, 4, 4, 112, 128)
        shapes["attend"] = (1, 4, 4, 144, 128)
        del shapes["output"]
        names_out.remove("output")
    items = scratch_list(n, inside, inputs)
    smem = pl.BlockSpec(memory_space=pltpu.SMEM)
    vmem = pl.BlockSpec(memory_space=pltpu.VMEM)
    outs = pl.pallas_call(
        make_kernel(
            n,
            inside,
            [name + "_far" if name in FAR else name for name in names_in] + names_out + [name for name, _ in items],
        ),
        out_shape=[
            jax.ShapeDtypeStruct(shapes[name], BF16 if name in ("ro_dst", "io_dst") else F32) for name in names_out
        ],
        in_specs=[
            smem if name == "steps" else pl.BlockSpec(memory_space=pl.ANY) if name in FAR else vmem
            for name in names_in
        ],
        out_specs=[vmem] * len(names_out),
        scratch_shapes=[item for _, item in items],
        compiler_params=pltpu.CompilerParams(
            collective_id=0, has_side_effects=True, vmem_limit_bytes=63 * 1024 * 1024
        ),
        name="blocks",
    )(*[inputs[name] for name in names_in])
    raw = dict(zip(names_out, outs))
    final = dict(
        result=flat_shape,
        image_grad=flat_shape,
        embed_grad=embedding.shape,
        film=film_weight.shape,
        gains_out=norm_gains.shape,
        biases_out=biases.shape,
    )
    if inside:
        final.update(first=(9, 48, BLK), second=(9, 48, BLK), attend=attend_weight.shape, output=output_weight.shape)
    names_last = [name for name in names_out if inside or name not in ("first", "second", "attend")] + ["sel"]
    names_final = list(final)
    given = [inputs["sel"] if name == "sel" else raw[name] for name in names_last]
    far = pl.BlockSpec(memory_space=pl.ANY)
    outs = pl.pallas_call(
        make_writer(names_last, names_final),
        out_shape=[jax.ShapeDtypeStruct(final[name], F32) for name in names_final],
        in_specs=[far] * len(names_last),
        out_specs=[far] * len(names_final),
        scratch_shapes=[pltpu.VMEM(array.shape, array.dtype) for array in given]
        + [pltpu.VMEM(final[name], F32) for name in names_final]
        + [pltpu.SemaphoreType.DMA((len(names_last),)), pltpu.SemaphoreType.DMA((len(names_final),))],
        compiler_params=pltpu.CompilerParams(vmem_limit_bytes=63 * 1024 * 1024),
        name="outputs",
    )(*given)
    out = dict(zip(names_final, outs))
    if not inside:

        def blocks_of(array, size):
            parts = [array[..., k * 48 : k * 48 + 48, :BLK] for k in range(size)]
            if size == 2:
                lanes = [array[..., k * 32 : k * 32 + 32, BLK:] for k in range(3)]
                lanes = jnp.concatenate(lanes, axis=-1)
                parts.append(jnp.concatenate([lanes, array[..., 96:112, :BLK]], axis=-2))
            else:
                lanes = [array[..., k * 48 : k * 48 + 48, BLK:] for k in range(3)]
                parts.append(jnp.concatenate(lanes, axis=-1))
            array = jnp.stack(parts, axis=1)
            array = array.reshape(array.shape[:2] + (2, 2, 4, 48, BLK))
            taps = array.shape[0] * array.shape[1]
            array = jnp.transpose(array, (0, 1, 4, 2, 5, 3, 6)).reshape(taps, 384, 2, 1, BLK)
            both = jnp.concatenate([array, jnp.zeros_like(array)], axis=3)
            return jnp.where(core == 0, both, both[:, :, :, ::-1]).reshape(taps, 384, 384)

        def shared(array, axis):
            array = lax.psum_scatter(array, "head", scatter_dimension=array.ndim - 1, tiled=True)
            return lax.psum_scatter(array, "dp", scatter_dimension=axis, tiled=True)

        out["first"] = shared(blocks_of(raw["first"], 2), 1)
        out["second"] = shared(blocks_of(raw["second"], 2), 1)
        both = blocks_of(raw["attend"], 3)
        joined = both[:3].reshape(3, 384, 2, 2, BLK)
        joined = jnp.transpose(joined, (1, 2, 0, 3, 4)).reshape(384, 1152)
        out["attend"] = shared(joined, 0)
        out["output"] = shared(both[3], 0)
    return (
        out["result"].reshape(images.shape),
        out["image_grad"].reshape(images.shape),
        out["embed_grad"],
        out["first"].reshape(first_kernel.shape),
        out["second"].reshape(second_kernel.shape),
        out["film"],
        out["attend"],
        out["output"],
        out["gains_out"],
        out["biases_out"],
    )


def solution(mesh):
    n = mesh.shape["dp"]
    field = P("dp", "head", None, None)
    taps = P(None, None, "dp", "head")
    both = P("dp", "head")
    return jax.shard_map(
        lambda *args: per_device(n, *args),
        mesh=mesh,
        in_specs=(field, field, P("dp"), P("dp", None), taps, taps, both, both, both, P(), P(), field),
        out_specs=(field, field, P("dp", None), taps, taps, both, both, both, P(), P()),
        check_vma=False,
    )
```

```python
import math

import jax
import jax.numpy as jnp
import numpy as np
from jax import lax
from jax.experimental import pallas as pl
from jax.experimental.pallas import tpu as pltpu
from jax.sharding import PartitionSpec as P

HEAD_DIM = 96
GROUPS = 32
STEPS = 4000
EPS = 1e-05
OFFSET = 0.008
MESH = pl.DeviceIdType.MESH
F32 = jnp.float32
BF16 = jnp.bfloat16

PX = 1024
ROW = 32
CHUNK = 256
BLK = 96
HALF = 256
NHEAD = 4


def plan(time_step, lanes):
    fraction = (jnp.full((1, lanes), time_step, jnp.int32).astype(F32) + 1.0) / STEPS
    start = math.cos(OFFSET / (1.0 + OFFSET) * (math.pi / 2)) ** 2
    curve = jnp.square(jnp.cos((fraction + OFFSET) / (1.0 + OFFSET) * (math.pi / 2))) / start
    return (jnp.sqrt(curve), jnp.sqrt(jnp.maximum(1.0 - curve, 0.0)))


def channel_lanes():
    sel = np.zeros((2, 384, HALF), np.float32)
    for block in range(4):
        for j in range(BLK):
            sel[block % 2, block * BLK + j, (block // 2) * 128 + j] = 1.0
    return sel


def block_lanes(count):
    sel = np.zeros((count * BLK, count * 128), np.float32)
    for block in range(count):
        for j in range(BLK):
            sel[block * BLK + j, block * 128 + j] = 1.0
    return sel


def group_mask():
    lane = np.arange(HALF)
    ok = lane % 128 < BLK
    group = (lane // 128) * 100 + (lane % 128) // 12
    return ((group[:, None] == group[None, :]) & ok[:, None] & ok[None, :]).astype(np.float32)


def dot(a, b):
    return lax.dot_general(a, b, (((1,), (0,)), ((), ())), preferred_element_type=F32)


def dot_nt(a, b):
    return lax.dot_general(a, b, (((1,), (1,)), ((), ())), preferred_element_type=F32)


def dot_nt_high(a, b):
    return lax.dot_general(
        a, b, (((1,), (1,)), ((), ())), preferred_element_type=F32, precision=lax.Precision.HIGHEST
    )


def dot_tn_high(a, b):
    return lax.dot_general(
        a, b, (((0,), (0,)), ((), ())), preferred_element_type=F32, precision=lax.Precision.HIGHEST
    )


def exact_dot(values, ones):
    high = values.astype(BF16).astype(F32)
    rest = values - high
    middle = rest.astype(BF16).astype(F32)
    low = rest - middle
    rows = values.shape[0]
    out = dot(jnp.concatenate([high, middle, low], axis=0).astype(BF16), ones)
    return out[:rows] + out[rows : 2 * rows] + out[2 * rows :]


def sigmoid(v):
    return 0.5 + 0.5 * jnp.tanh(0.5 * v)


def silu(v):
    return v * sigmoid(v)


def silu_slope(v):
    s = sigmoid(v)
    return s * (1.0 + v * (1.0 - s))


def pack_taps(t0, t1, t2):
    t0, t1, t2 = t0[:, :BLK], t1[:, :BLK], t2[:, :BLK]
    join = lambda a, b: jnp.concatenate([a, b], axis=1)
    return jnp.concatenate(
        [
            join(t0[:32], t2[:32, :32]),
            join(t0[32:], t2[:16, 32:64]),
            join(t1[:16], t2[16:32, 32:64]),
            join(t1[16:], t2[:32, 64:]),
            join(t2[32:], jnp.zeros((16, 32), t2.dtype)),
        ],
        axis=0,
    )


def last_tap(packed):
    lanes = [packed[:32, BLK:], packed[32:64, BLK:], packed[64:96, BLK:], jnp.zeros((32, 32), packed.dtype)]
    return jnp.concatenate([jnp.concatenate(lanes, axis=1), packed[96:112]], axis=0)


def pack_four(b0, b1, b2, b3):
    return jnp.concatenate(
        [jnp.concatenate([b[:, :BLK], b3[:, 32 * k : 32 * k + 32]], axis=1) for k, b in enumerate((b0, b1, b2))],
        axis=0,
    )


def unpack_four(packed):
    size = packed.shape[0] // 3
    parts = [packed[k * size : k * size + size] for k in range(3)]
    zero = jnp.zeros((size, 32), packed.dtype)
    fourth = jnp.concatenate([p[:, BLK:] for p in parts] + [zero], axis=1)
    return [jnp.concatenate([p[:, :BLK], zero], axis=1) for p in parts] + [fourth]


def pack_pixels(full):
    half = CHUNK // 2
    return pack_four(full[:half, :128], full[half:, :128], full[:half, 128:], full[half:, 128:])


def unpack_pixels(packed):
    b0, b1, b2, b3 = unpack_four(packed)
    return jnp.concatenate([jnp.concatenate([b0, b2], axis=1), jnp.concatenate([b1, b3], axis=1)], axis=0)


INPUTS = (
    "steps",
    "images",
    "noise",
    "cot",
    "emb",
    "k1",
    "k2",
    "wf",
    "wa",
    "wo",
    "gains",
    "biases",
    "sel",
    "gmask",
    "selp",
)
OUTPUTS = (
    "ro_dst",
    "io_dst",
    "embed_grad",
    "first",
    "second",
    "film",
    "attend",
    "output",
    "gains_out",
    "biases_out",
)


FAR = (
    "images",
    "noise",
    "cot",
    "sel",
    "selp",
    "k2",
    "wa",
    "wf",
    "gmask",
)


class Names:
    def __init__(self, names, refs):
        for name, ref in zip(names, refs):
            setattr(self, name, ref)


def scratch_list(n, inside, inputs):
    dma = pltpu.SemaphoreType.DMA
    items = []

    def vm(name, shape, dtype):
        items.append((name, pltpu.VMEM(shape, dtype)))

    def sem(name, count):
        items.append((name + "_s", dma((count,))))
        items.append((name + "_r", dma((count,))))

    for name in FAR:
        vm(name, inputs[name].shape, inputs[name].dtype)
    items.append(("far_s", dma((len(FAR),))))
    for name in ("mx", "cx", "ro", "io"):
        vm(name + "_src", (4, 384, 128), BF16)
        if name in ("mx", "cx"):
            vm(name + "_dst", (4, 384, 128), BF16)
            vm(name, (4, CHUNK, HALF), BF16)
        sem(name, 4)
    for name in ("act1", "act2"):
        vm(name, (2, PX + 2 * ROW, HALF), BF16)
        vm(name + "_t", (2, HALF, PX), BF16)
        sem(name, 4)
        sem(name + "_t", 1)
    vm("ai", (2, PX, HALF), BF16)
    vm("ai_t", (2, HALF, PX), BF16)
    sem("ai_t", 1)
    sem("ai", 4)
    vm("att", (4, PX, 128), BF16)
    vm("att_t", (2, HALF, PX), BF16)
    sem("att", 4)
    for name in ("do", "n3", "d2", "d1"):
        vm(name + "_src", (PX, HALF), BF16)
        vm(name + "_dst", (PX, HALF), BF16)
        sem(name, 2)
    vm("v2", (PX, HALF), F32)
    vm("v3", (PX, HALF), F32)
    vm("gres", (PX, HALF), F32)
    vm("gtmp", (PX, HALF), F32)
    vm("qkv", (6, PX, 128), BF16)
    vm("kvt", (4, 128, PX), BF16)
    vm("dout", (2, PX, 128), BF16)
    vm("dproj", (6, PX, 128), BF16)
    vm("gr2", (3, PX + 2 * ROW, HALF), BF16)
    vm("gr1", (3, PX + 2 * ROW, HALF), BF16)
    vm("par", (16, 384), F32)
    vm("parown", (16, HALF), F32)
    vm("stat", (16, HALF), F32)
    vm("sums", (16, HALF), F32)
    if inside:
        vm("g1", (4, 4, 336, 128), BF16)
        vm("g2", (4, 4, 336, 128), BF16)
        vm("t1", (4, 4, 144, 128), BF16)
        vm("t2", (4, 4, 144, 128), BF16)
        vm("p3", (4, 4, 144, 128), BF16)
        vm("g3", (4, 4, 192, 128), BF16)
        for name in ("g1", "g2", "p3"):
            sem(name + "z", 4)
            sem(name + "v", 4)
            sem(name + "w", 8)
        vm("sw_src", (48, 128), BF16)
        vm("sw_dst", (48, 128), BF16)
        sem("sw", 1)
        vm("sb_src", (48, 128), F32)
        vm("sb_dst", (48, 128), F32)
        sem("sb", 1)
        for name, nc, rows in (("r1", 3, 112), ("r2", 3, 112), ("r3", 1, 144)):
            vm(name + "_acc", (nc, 4, 4, rows, 128), BF16)
            vm(name + "_own", (nc, rows, 128), F32)
            vm(name + "w_dst", (nc, 2, 4, rows, 128), BF16)
            vm(name + "v_src", (nc, 4, rows, 128), BF16)
            vm(name + "v_dst", (nc, 4, rows, 128), BF16)
            vm(name + "z_src", (4, nc, rows, 128), BF16)
            vm(name + "z_dst", (4, nc, rows, 128), BF16)
            sem(name + "w", nc)
            sem(name + "v", nc)
            sem(name + "z", nc * 4)
    vm("el", (n, 2, 768), F32)
    sem("el", n)
    vm("em", (2 * n, 768), F32)
    vm("wfp", (128, HALF), BF16)
    vm("esel", (2 * n, 128), F32)
    vm("fp", (n, 2, HALF), F32)
    vm("fr", (n, 2, HALF), F32)
    sem("fr", n)
    vm("fx", (4, 1, 128), F32)
    vm("fh", (4, 1, 128), F32)
    sem("fh", 4)
    vm("ft", (4, 1, 128), F32)
    vm("th", (4, 1, 128), F32)
    sem("th", 4)
    vm("fa", (n, 2, HALF), F32)
    sem("fa", n)
    vm("fta", (2 * n, HALF), F32)
    vm("ep", (n, 2, 128), F32)
    vm("er", (n, 2, 128), F32)
    sem("er", n)
    vm("eh", (4, n, 2, 128), F32)
    sem("eh", 4)
    vm("ad", (n, 16, HALF), F32)
    sem("ad", n)
    vm("hb", (4, 16, HALF), F32)
    sem("hb", 4)
    return items


def make_kernel(n, inside, names):
    film_rows = 768 // n

    def kernel(*refs):
        r = Names(names, refs)
        d = lax.axis_index("dp")
        h = lax.axis_index("head")
        x = h // 2
        c = h - 2 * x
        z = d // 2
        y = d - 2 * z
        sib = (d, h + 1 - 2 * c)
        xdev = (d, h + 2 - 4 * x)
        v = x + c * (y - x)
        w = y + c * (x - y)
        vdev = (d + c * (1 - 2 * y), h + (1 - c) * (2 - 4 * x))
        wdev = (d + (1 - c) * (1 - 2 * y), h + c * (2 - 4 * x))

        def slot(xx, yy, o=c):
            if inside:
                return (yy + o * (xx - yy)) * 2 + xx + o * (yy - xx)
            return yy * 2 + xx

        def order(split, i):
            return c * (i // 2) if split else c

        def rc(src, dst, send, recv, dev):
            return pltpu.make_async_remote_copy(
                src_ref=src, dst_ref=dst, send_sem=send, recv_sem=recv, device_id=dev, device_id_type=MESH
            )

        def loop(count, body):
            def step(i, carry):
                body(i)
                return carry

            lax.fori_loop(0, count, step, 0)

        def each(count, body):
            for i in range(count):
                body(i)

        def rows(i, size=CHUNK, base=0):
            return pl.ds(pl.multiple_of(base + i * size, 32), size)

        def dp_start(src_of, dst, send, recv):
            def step(k, carry):
                peer = lax.rem(d + k, n)
                rc(src_of(peer), dst.at[d], send.at[k], recv.at[d], (peer, h)).start()
                return carry

            lax.fori_loop(1, n, step, 0)

        def dp_wait(src_of, dst, send, recv):
            def step(k, carry):
                peer = lax.rem(d + k, n)
                copy = rc(src_of(peer), dst.at[peer], send.at[k], recv.at[peer], (peer, h))
                copy.wait_recv()
                copy.wait_send()
                return carry

            lax.fori_loop(1, n, step, 0)

        def head_start(src_of, dst, send, recv):
            for k in range(1, 4):
                peer = lax.rem(h + k, 4)
                rc(src_of(peer), dst.at[h], send.at[k], recv.at[h], (d, peer)).start()

        def head_wait(src_of, dst, send, recv):
            for k in range(1, 4):
                peer = lax.rem(h + k, 4)
                copy = rc(src_of(peer), dst.at[peer], send.at[k], recv.at[peer], (d, peer))
                copy.wait_recv()
                copy.wait_send()

        class Halves:
            def __init__(self, name, base):
                self.buf, self.base = getattr(r, name), base
                self.send, self.recv = getattr(r, name + "_s"), getattr(r, name + "_r")

            def at(self, core, i):
                return self.buf.at[core, rows(i, CHUNK, self.base)]

            def fill(self, make):
                def body(i):
                    self.buf[c, rows(i, CHUNK, self.base), :] = make(i)
                    ref = self.at(c, i)
                    rc(ref, ref, self.send.at[i], self.recv.at[i], sib).start()

                loop(4, body)

            def wait(self):
                for i in range(4):
                    ref = self.at(1 - c, i)
                    copy = rc(ref, ref, self.send.at[i], self.recv.at[i], sib)
                    copy.wait_recv()
                    copy.wait_send()

        class Parts:
            def __init__(self, name):
                self.src, self.dst = getattr(r, name + "_src"), getattr(r, name + "_dst")
                self.send, self.recv = getattr(r, name + "_s"), getattr(r, name + "_r")

            def copy(self, i):
                at = rows(i, 2 * CHUNK)
                return rc(self.src.at[at], self.dst.at[at], self.send.at[i], self.recv.at[i], sib)

            def fill(self, make):
                def body(i):
                    self.src[rows(i, 2 * CHUNK), :] = make(i).astype(BF16)
                    self.copy(i).start()

                each(2, body)

            def get(self, i):
                copy = self.copy(i)
                copy.wait_recv()
                copy.wait_send()
                return self.dst[rows(i, 2 * CHUNK), :].astype(F32)

        class Gather:
            def __init__(self, name, split):
                self.g, self.split = getattr(r, name), split
                self.zs, self.zr = getattr(r, name + "z_s"), getattr(r, name + "z_r")
                self.vs, self.vr = getattr(r, name + "v_s"), getattr(r, name + "v_r")
                self.ws, self.wr = getattr(r, name + "w_s"), getattr(r, name + "w_r")

            def at(self, i, far_w, far_v):
                o = order(self.split, i)
                vv, ww = x + o * (y - x), y + o * (x - y)
                return (ww + far_w * (1 - 2 * ww)) * 2 + vv + far_v * (1 - 2 * vv)

            def zcopy(self, k):
                peer = (lax.rem(z + k, 4) * 2 + y, h)
                src, dst = self.g.at[self.at(0, 0, 0), 0], self.g.at[self.at(4 - k, 0, 0), 4 - k]
                return rc(src, dst, self.zs.at[k], self.zr.at[4 - k], peer)

            def vcopy(self, far_v, i):
                o = order(self.split, i)
                ref = self.g.at[self.at(i, 0, far_v), i]
                dev = (d + o * (1 - 2 * y), h + (1 - o) * (2 - 4 * x))
                return rc(ref, ref, self.vs.at[i], self.vr.at[i], dev)

            def wcopy(self, far_w, far_v, i):
                o = order(self.split, i)
                ref = self.g.at[self.at(i, far_w, far_v), i]
                dev = (d + (1 - o) * (1 - 2 * y), h + o * (2 - 4 * x))
                return rc(ref, ref, self.ws.at[2 * i + far_v], self.wr.at[2 * i + far_v], dev)

            def own(self):
                for k in range(1, 4):
                    self.zcopy(k).start()
                self.vcopy(0, 0).start()
                self.wcopy(0, 0, 0).start()

            def pass_own(self):
                self.vcopy(1, 0).wait_recv()
                self.wcopy(0, 1, 0).start()

            def pass_z(self, *ks):
                for k in ks:
                    self.zcopy(k).wait_recv()
                    self.vcopy(0, 4 - k).start()
                    self.wcopy(0, 0, 4 - k).start()

            def pass_v(self, *ks):
                for k in ks:
                    self.vcopy(1, 4 - k).wait_recv()
                    self.wcopy(0, 1, 4 - k).start()

            def take(self, blocks):
                for i, far_v in ((0, 0), (0, 1), (3, 0), (1, 0), (2, 0), (3, 1), (1, 1), (2, 1)):
                    self.wcopy(1, far_v, i).wait_recv()
                    blocks.unpack([(self.at(i, 1, far_v), i)])

            def finish(self):
                for k in range(1, 4):
                    self.zcopy(k).wait_send()
                for i in range(4):
                    self.vcopy(0, i).wait_send()
                    for far_v in range(2):
                        self.wcopy(0, far_v, i).wait_send()

            def blocks(self, far_w):
                return [(self.at(i, far_w, far_v), i) for i in range(4) for far_v in range(2)]

        class Reduce:
            def __init__(self, name, count):
                get = lambda tail: getattr(r, name + tail)
                self.acc, self.count = get("_acc"), count
                self.wdst, self.ws, self.wr, self.own = get("w_dst"), get("w_s"), get("w_r"), get("_own")
                self.vsrc, self.vdst, self.vs, self.vr = get("v_src"), get("v_dst"), get("v_s"), get("v_r")
                self.zsrc, self.zdst, self.zs, self.zr = get("z_src"), get("z_dst"), get("z_s"), get("z_r")

            def wcopy(self, a):
                ref = self.acc.at[a, pl.ds((1 - w) * 2, 2)]
                return rc(ref, self.wdst.at[a], self.ws.at[a], self.wr.at[a], wdev)

            def vcopy(self, a, size):
                at = pl.ds(a, size)
                return rc(self.vsrc.at[at], self.vdst.at[at], self.vs.at[a], self.vr.at[a], vdev)

            def zcopy(self, a, size, k):
                at = pl.ds(a, size)
                return rc(
                    self.zsrc.at[k, at],
                    self.zdst.at[4 - k, at],
                    self.zs.at[a * 4 + k],
                    self.zr.at[a * 4 + 4 - k],
                    (lax.rem(z + k, 4) * 2 + y, h),
                )

            def start(self, a):
                self.wcopy(a).start()

            def second(self, first, size):
                for a in range(first, first + size):
                    self.wcopy(a).wait_recv()

                    def step(zz, carry):
                        self.vsrc[a, zz] = (
                            self.acc[a, w * 2 + 1 - v, zz].astype(F32) + self.wdst[a, 1 - v, zz].astype(F32)
                        ).astype(BF16)
                        return carry

                    lax.fori_loop(0, 4, step, 0)
                self.vcopy(first, size).start()

            def third(self, first, size):
                self.vcopy(first, size).wait_recv()
                for a in range(first, first + size):

                    for k in range(4):
                        zz = lax.rem(z + k, 4)
                        total = (
                            self.acc[a, w * 2 + v, zz].astype(F32)
                            + self.wdst[a, v, zz].astype(F32)
                            + self.vdst[a, zz].astype(F32)
                        )
                        if k == 0:
                            self.own[a] = total
                        else:
                            self.zsrc[k, a] = total.astype(BF16)
                for k in range(1, 4):
                    self.zcopy(first, size, k).start()

            def finish(self, groups):
                for first, size in groups:
                    self.vcopy(first, size).wait_send()
                    for k in range(1, 4):
                        copy = self.zcopy(first, size, k)
                        copy.wait_recv()
                        copy.wait_send()
                for a in range(self.count):
                    self.wcopy(a).wait_send()

            def last(self, a):
                total = self.own[a]
                for k in range(1, 4):
                    total = total + self.zdst[k, a].astype(F32)
                return total

        def rel(zc):
            return lax.rem(zc - z + 4, 4) if inside else zc

        def where_is(split, xx, yy, zc):
            i = rel(zc)
            return slot(xx, yy, order(split, i)), i

        class Taps:
            def __init__(self, packed, last, split):
                self.packed, self.last, self.split = packed, last, split

            def block(self, tap, zc, xx, yy):
                a, b = tap // 3, tap % 3
                q, i = where_is(self.split, xx, yy, zc)
                if b < 2:
                    return self.packed[q, i, pl.ds(a * 112 + b * 48, 48), :]
                return self.last[q, i, pl.ds(a * 48, 48), :]

            def unpack(self, places):
                for q, i in places:
                    for a in range(3):
                        self.last[q, i, pl.ds(a * 48, 48), :] = last_tap(self.packed[q, i, pl.ds(a * 112, 112), :])

        class Plain:
            def __init__(self, blocks, split):
                self.blocks, self.split = blocks, split

            def block(self, tap, zc, xx, yy):
                q, i = where_is(self.split, xx, yy, zc)
                return self.blocks[q, i, pl.ds(tap * 48, 48), :]

            def unpack(self, places):
                for q, i in places:
                    self.blocks[q, i] = jnp.concatenate(unpack_four(r.p3[q, i]), axis=0)

        k1, k2, k3 = Taps(r.g1, r.t1, True), Taps(r.g2, r.t2, False), Plain(r.g3, True)

        def wtile(g, tap, zc, xx):
            return jnp.concatenate(
                [g.block(tap, zc, xx, 0), g.block(tap, zc, xx, 1), jnp.zeros((32, 128), BF16)], axis=0
            )

        def wtap(g, tap, zcs):
            return jnp.concatenate(
                [jnp.concatenate([wtile(g, tap, zc, xx) for xx in range(2)], axis=1) for zc in zcs], axis=0
            )

        ALL = (0, 2, 1, 3)

        def half_of(core):
            return (core, core + 2)

        def wproj(zcs):
            return jnp.concatenate(
                [
                    jnp.concatenate([wtile(k3, j, zc, xx) for xx in range(2) for j in range(3)], axis=1)
                    for zc in zcs
                ],
                axis=0,
            )

        def flat(buf, base, i, size):
            return jnp.concatenate([buf[0, rows(i, size, base), :], buf[1, rows(i, size, base), :]], axis=1)

        barrier = pltpu.get_barrier_semaphore()

        def greet(k, carry):
            pl.semaphore_signal(barrier, inc=1, device_id=(lax.rem(d + k, n), h), device_id_type=MESH)
            return carry

        lax.fori_loop(1, n, greet, 0)
        for k in range(1, 4):
            pl.semaphore_signal(barrier, inc=1, device_id=(d, lax.rem(h + k, 4)), device_id_type=MESH)
        def fetch(name):
            return pltpu.make_async_copy(getattr(r, name + "_far"), getattr(r, name), r.far_s.at[FAR.index(name)])

        for name in FAR:
            fetch(name).start()
        if inside:
            ga, gb, gc = Gather("g1", True), Gather("g2", False), Gather("p3", True)
            for a in range(3):
                r.g1[ga.at(0, 0, 0), 0, pl.ds(a * 112, 112), :] = pack_taps(*[r.k1[3 * a + b] for b in range(3)])
        pl.semaphore_wait(barrier, n - 1 + 3)
        if inside:
            ga.own()

        for name in FAR:
            fetch(name).wait()
        def head_copy(src, dst, send, recv, k):
            peer = lax.rem(h + k, 4)
            return rc(src.at[peer], dst.at[h], send.at[k], recv.at[h], (d, peer))

        for step in range(2):
            m = x + (1 - step) * (1 - 2 * x)
            keep, spread = plan(r.steps[m], 384)
            low = (keep * r.images[m].astype(F32) + spread * r.noise[m].astype(F32)).astype(BF16)
            for core in range(2):
                r.mx_src[m * 2 + core] = pack_pixels(dot(low, r.sel[core])).astype(BF16)
            for k in (2, 3 - 2 * c) if step == 0 else (1 + 2 * c,):
                head_copy(r.mx_src, r.mx_dst, r.mx_s, r.mx_r, k).start()
        r.mx_dst[h] = r.mx_src[h]
        if inside:
            ga.pass_own()

        r.el[d] = silu(r.emb[...].astype(F32)).astype(BF16).astype(F32)
        dp_start(lambda p: r.el.at[d], r.el, r.el_s, r.el_r)

        if inside:
            blocks = dot(r.wa[...], r.selp[: 3 * BLK, : 3 * 128]).astype(BF16)
            r.sw_src[...] = blocks[:, 128:256]
            swap = rc(r.sw_src, r.sw_dst, r.sw_s.at[0], r.sw_r.at[0], sib)
            swap.start()
            for a in range(3):
                r.g2[gb.at(0, 0, 0), 0, pl.ds(a * 112, 112), :] = pack_taps(*[r.k2[3 * a + b] for b in range(3)])
        r.par[0:3, :] = r.gains[...]
        r.par[3:13, :] = r.biases[...]
        r.par[13:16, :] = jnp.zeros((3, 384), F32)
        r.parown[...] = exact_dot(r.par[...], r.sel[c])

        def prow(i):
            return r.parown[pl.ds(i, 1), :]

        for buf in (r.act1, r.act2):
            for core in range(2):
                buf[core, pl.ds(0, ROW), :] = jnp.zeros((ROW, HALF), BF16)
                buf[core, pl.ds(PX + ROW, ROW), :] = jnp.zeros((ROW, HALF), BF16)
        for buf in (r.gr1, r.gr2):
            for b in range(3):
                buf[b, pl.ds(0, ROW), :] = jnp.zeros((ROW, HALF), BF16)
                buf[b, pl.ds(PX + ROW, ROW), :] = jnp.zeros((ROW, HALF), BF16)
        r.wfp[...] = jnp.zeros((128, HALF), BF16)
        r.wfp[pl.ds(0, film_rows), :] = dot(r.wf[...], r.selp[: 2 * BLK, :HALF]).astype(BF16)
        if inside:
            ga.pass_z(1, 3, 2)
            gb.own()

        count = float(PX * 12)

        def fold(vals):
            return jnp.sum(vals.reshape(CHUNK // 8, 8, HALF), axis=0)

        def sums_of(fn, k):
            def step(i, carry):
                return tuple(a + fold(b) for a, b in zip(carry, fn(i)))

            zero = jnp.zeros((8, HALF), F32)
            return lax.fori_loop(0, 4, step, (zero,) * k)

        def group_mean(part):
            return jnp.sum(exact_dot(part, r.gmask[...]), axis=0, keepdims=True) / count

        def norm(load, which, total):
            mean = group_mean(total)
            (square,) = sums_of(lambda i: (jnp.square(load(i) - mean),), 1)
            inv = lax.rsqrt(group_mean(square) + EPS)
            r.stat[pl.ds(2 * which, 1), :] = mean
            r.stat[pl.ds(2 * which + 1, 1), :] = inv
            return mean, inv

        zero8 = jnp.zeros((8, HALF), F32)

        def norm_back(sums, load_grad, load_hat, coef, inv):
            plain, cross = sums
            means = exact_dot(jnp.concatenate([coef * plain, coef * cross], axis=0), r.gmask[...])
            plain_mean = jnp.sum(means[:8], axis=0, keepdims=True) / count
            cross_mean = jnp.sum(means[8:], axis=0, keepdims=True) / count
            outer, base, slope = inv * coef, inv * plain_mean, inv * cross_mean

            def chunk(i):
                return outer * load_grad(i) - base - load_hat(i) * slope

            return (
                jnp.sum(plain, axis=0, keepdims=True),
                jnp.sum(cross, axis=0, keepdims=True),
                chunk,
            )

        def transposed(name, core):
            ref = getattr(r, name).at[core]
            return rc(ref, ref, getattr(r, name + "_s").at[0], getattr(r, name + "_r").at[0], sib)

        def transpose_act(buf, base, name):
            out = getattr(r, name)
            for q in range(4):
                out[c, :, pl.ds(q * CHUNK, CHUNK)] = jnp.transpose(buf[c, pl.ds(base + q * CHUNK, CHUNK), :])
            transposed(name, c).start()

        def transposed_wait(name):
            copy = transposed(name, 1 - c)
            copy.wait_recv()
            copy.wait_send()

        head_wait(lambda p: r.mx_src.at[p], r.mx_dst, r.mx_s, r.mx_r)

        def unpack_mixed(i, carry):
            vals = unpack_pixels(r.mx_dst[i])
            r.mx[i] = vals
            return carry + fold(vals.astype(F32))

        mixed_sum = lax.fori_loop(0, 4, unpack_mixed, zero8)

        def mixed(i):
            return r.mx[i].astype(F32)

        if inside:
            ga.pass_v(1, 3)
        mean1, inv1 = norm(mixed, 0, mixed_sum)
        if inside:
            ga.pass_v(2)
        gain1, shift1 = prow(0), prow(3)
        act1 = Halves("act1", ROW)

        def affine(mean, inv, gain, shift):
            return inv * gain, shift - mean * (inv * gain)

        mul1, add1 = affine(mean1, inv1, gain1, shift1)

        def pre1(i):
            return mixed(i) * mul1 + add1

        act1.fill(lambda i: silu(pre1(i)).astype(BF16))
        dp_wait(lambda p: r.el.at[d], r.el, r.el_s, r.el_r)
        for j in range(n):
            r.em[pl.ds(2 * j, 2), :] = r.el[j]
        place = lax.broadcasted_iota(jnp.int32, (768, 128), 0) - film_rows * d
        lane = lax.broadcasted_iota(jnp.int32, (768, 128), 1)
        pick = jnp.where((place == lane) & (lane < film_rows), 1.0, 0.0).astype(BF16)
        r.esel[...] = dot(r.em[...].astype(BF16), pick)
        film_part = dot(r.esel[...].astype(BF16), r.wfp[...])
        for j in range(n):
            r.fp[j] = film_part[2 * j : 2 * j + 2]
        dp_start(lambda p: r.fp.at[p], r.fr, r.fr_s, r.fr_r)
        r.fr[d] = r.fp[d]
        if inside:
            swap.wait()
            got = r.sw_dst[...]
            keep0, keep2 = blocks[:, :128], blocks[:, 256:]
            r.p3[gc.at(0, 0, 0), 0] = pack_four(
                jnp.where(c == 0, keep0, got),
                jnp.where(c == 0, keep2, keep0),
                jnp.where(c == 0, got, keep2),
                r.wo[...],
            )
        act1.wait()
        transpose_act(r.act1, ROW, "act1_t")
        if inside:
            gb.pass_own()
            gb.pass_z(1, 3, 2)
            gc.own()
        def split_cot(m, carry):
            for core in range(2):
                r.cx_src[m * 2 + core] = pack_pixels(dot(r.cot[m], r.sel[core])).astype(BF16)
            return carry

        lax.fori_loop(0, 2, split_cot, 0)
        column = lax.broadcasted_iota(jnp.int32, (1, ROW, HALF), 1)
        not_first = jnp.where(column > 0, 1.0, 0.0)
        not_last = jnp.where(column < ROW - 1, 1.0, 0.0)

        def in_rows(vals, mask):
            return (vals.reshape(CHUNK // ROW, ROW, HALF) * mask).reshape(CHUNK, HALF)

        def from_left(vals):
            return in_rows(pltpu.roll(vals, 1, 0), not_first)

        def from_right(vals):
            return in_rows(pltpu.roll(vals, CHUNK - 1, 0), not_last)

        def conv(buf, g, store, between):
            weights = lambda: jnp.concatenate(
                [jnp.concatenate([wtap(g, 3 * a + b, ALL) for b in range(3)], axis=1) for a in range(3)], axis=0
            )

            total = zero8
            for i in range(2):
                left = jnp.concatenate([flat(buf, ROW * a, i, 2 * CHUNK) for a in range(3)], axis=1)
                out = dot(left, weights())
                for j in range(2):
                    part = out[j * CHUNK : j * CHUNK + CHUNK]
                    part = part[:, HALF : 2 * HALF] + from_left(part[:, :HALF]) + from_right(part[:, 2 * HALF :])
                    total = total + fold(store(2 * i + j, part))
                if i == 0:
                    between()
            return total

        if inside:
            k1.unpack(ga.blocks(0))
            ga.take(k1)

        dp_wait(lambda p: r.fp.at[p], r.fr, r.fr_s, r.fr_r)
        film_sum = r.fr[0]
        for j in range(1, n):
            film_sum = film_sum + r.fr[j]
        for m in range(2):
            for core in range(2):
                r.fx[m * 2 + core] = film_sum[m : m + 1, core * 128 : core * 128 + 128]
        head_start(lambda p: r.fx.at[p], r.fh, r.fh_s, r.fh_r)
        r.fh[h] = r.fx[h]

        def store_v2(i, vals):
            vals = vals + prow(6)
            r.v2[rows(i), :] = vals
            return vals

        v2_sum = conv(r.act1, k1, store_v2, (lambda: gb.pass_v(1, 3, 2)) if inside else lambda: None)
        head_wait(lambda p: r.fx.at[p], r.fh, r.fh_s, r.fh_r)
        scale = 1.0 + (jnp.concatenate([r.fh[0], r.fh[1]], axis=1) + prow(8))
        shift = jnp.concatenate([r.fh[2], r.fh[3]], axis=1) + prow(9)
        mean2, inv2 = norm(lambda i: r.v2[rows(i), :], 1, v2_sum)
        gain2, shift2 = prow(1), prow(4)
        act2 = Halves("act2", ROW)

        def hat2(i):
            return (r.v2[rows(i), :] - mean2) * inv2

        mul2, add2 = affine(mean2, inv2, gain2 * scale, shift2 * scale + shift)

        def pre2(i):
            return r.v2[rows(i), :] * mul2 + add2

        act2.fill(lambda i: silu(pre2(i)).astype(BF16))
        if inside:
            gc.pass_own()
            gc.pass_z(1, 3, 2)

        transpose_act(r.act2, ROW, "act2_t")
        act2.wait()
        if inside:
            k2.unpack(gb.blocks(0))
            gb.take(k2)

        head_start(lambda p: r.cx_src.at[p], r.cx_dst, r.cx_s, r.cx_r)
        r.cx_dst[h] = r.cx_src[h]

        def store_v3(i, vals):
            vals = mixed(i) + (vals + prow(7))
            r.v3[rows(i), :] = vals
            return vals

        v3_sum = conv(r.act2, k2, store_v3, (lambda: gc.pass_v(1, 3, 2)) if inside else lambda: None)
        mean3, inv3 = norm(lambda i: r.v3[rows(i), :], 2, v3_sum)
        gain3, shift3 = prow(2), prow(5)
        ai = Halves("ai", 0)

        def hat3(i):
            return (r.v3[rows(i), :] - mean3) * inv3

        mul3, add3 = affine(mean3, inv3, gain3, shift3)
        ai.fill(lambda i: (r.v3[rows(i), :] * mul3 + add3).astype(BF16))
        transpose_act(r.ai, 0, "ai_t")

        if inside:
            k3.unpack(gc.blocks(0))
            gc.take(k3)
        head_wait(lambda p: r.cx_src.at[p], r.cx_dst, r.cx_s, r.cx_r)

        def unpack_cot(i):
            r.cx[i] = unpack_pixels(r.cx_dst[i])

        loop(4, unpack_cot)
        dop = Parts("do")

        def cot_rows(i):
            return jnp.concatenate([r.cx[2 * i], r.cx[2 * i + 1]], axis=0)

        dop.fill(lambda i: dot_nt(cot_rows(i), wtap(k3, 3, half_of(1 - c))))

        ai.wait()
        bias_proj = [prow(10)[:, :128], prow(10)[:, 128:], None, None, prow(11)[:, :128], prow(11)[:, 128:]]

        def project(i):
            out = dot(flat(r.ai, 0, i, 2 * CHUNK), wproj(ALL))
            for k in range(6):
                part = out[:, k * 128 : k * 128 + 128]
                if bias_proj[k] is not None:
                    part = part + bias_proj[k]
                r.qkv[k, rows(i, 2 * CHUNK), :] = part.astype(BF16)

        each(2, project)

        def do_own(i):
            full = (dot_nt(cot_rows(i), wtap(k3, 3, half_of(c))) + dop.get(i)).astype(BF16)
            for k in range(2):
                r.dout[k, rows(i, 2 * CHUNK), :] = full[:, k * 128 : k * 128 + 128]

        each(2, do_own)

        factor = 1.0 / math.sqrt(HEAD_DIM)
        factor2 = factor * math.log2(math.e)
        att = []

        def transposes(k):
            r.kvt[k] = jnp.transpose(r.qkv[k + 2])

        loop(4, transposes)

        def att_copy(core, k):
            ref = r.att.at[core * 2 + k]
            return rc(ref, ref, r.att_s.at[k], r.att_r.at[k], sib)

        def att_t_copy(core, k):
            ref = r.att_t.at[core, pl.ds(pl.multiple_of(k * 128, 128), 128)]
            return rc(ref, ref, r.att_s.at[2 + k], r.att_r.at[2 + k], sib)

        def one_head(k):
            lows, grads = [], []
            for b in range(2):
                at = pl.ds(b * 2 * CHUNK, 2 * CHUNK)
                query = r.qkv[k, at, :]
                grad = r.dout[k, at, :]
                scores = dot_nt(r.qkv[2 + k], query)
                peak = jnp.max(scores, axis=0, keepdims=True)
                expo = jnp.exp2((scores - peak) * factor2)
                inverse = 1.0 / jnp.sum(expo, axis=0, keepdims=True)
                low = (expo * inverse).astype(BF16)
                got = dot(r.kvt[2 + k], low)
                got_low = got.astype(BF16)
                r.att_t[c, pl.ds(pl.multiple_of(k * 128, 128), 128), at] = got_low
                r.att[2 * c + k, at, :] = jnp.transpose(got_low)
                spread = jnp.sum(got * jnp.transpose(grad).astype(F32), axis=0, keepdims=True)
                probs_grad = dot_nt(r.qkv[4 + k], grad)
                scores_grad = ((probs_grad - spread) * inverse * expo).astype(BF16)
                back = dot(r.kvt[k], scores_grad)
                r.dproj[k, at, :] = (jnp.transpose(back) * factor).astype(BF16)
                lows.append(low)
                grads.append(scores_grad)
            att_copy(c, k).start()
            att_t_copy(c, k).start()
            r.dproj[4 + k] = dot(jnp.concatenate(lows, axis=1), r.dout[k]).astype(BF16)
            r.dproj[2 + k] = (dot(jnp.concatenate(grads, axis=1), r.qkv[k]) * factor).astype(BF16)

        loop(2, one_head)

        n3 = Parts("n3")

        def proj_rows(i):
            return jnp.concatenate([r.dproj[k, rows(i, 2 * CHUNK), :] for k in range(6)], axis=1)

        n3.fill(lambda i: dot_nt(proj_rows(i), wproj(half_of(1 - c))))

        def rows_of(act_t):
            return jnp.concatenate([act_t[p // 2, pl.ds(p % 2 * 128, BLK), :] for p in range(4)], axis=0)

        for k in range(2):
            copy = att_copy(1 - c, k)
            copy.wait_recv()
            copy.wait_send()

        def result(i):
            left = jnp.concatenate([r.att[p, rows(i), :] for p in range(4)], axis=1)
            branch = dot(left, wtap(k3, 3, ALL)) + prow(12)
            r.ro_src[i] = pack_pixels(r.v3[rows(i), :] + branch).astype(BF16)

        loop(4, result)
        head_start(lambda p: r.ro_src.at[p], r.ro_dst, r.ro_s, r.ro_r)
        r.ro_dst[h] = r.ro_src[h]

        if inside:
            red1, red2, red3 = Reduce("r1", 3), Reduce("r2", 3), Reduce("r3", 1)
            acc1, acc2, acc3 = r.r1_acc, r.r2_acc, r.r3_acc
        else:
            acc1, acc2, acc3 = r.first, r.second, r.attend

        transposed_wait("ai_t")
        for k in range(2):
            copy = att_t_copy(1 - c, k)
            copy.wait_recv()
            copy.wait_send()
        right = jnp.concatenate([r.dproj[k] for k in range(6)], axis=1)
        cot_all = jnp.concatenate([r.cx[i] for i in range(4)], axis=0)
        attend_out = dot(rows_of(r.ai_t), right)
        output_out = dot(rows_of(r.att_t), cot_all)
        for p, zc in enumerate(ALL):
            for yy in range(2):
                for xx in range(2):
                    row = p * BLK + yy * 48
                    tiles = [
                        attend_out[row : row + 48, (xx * 3 + j) * 128 : (xx * 3 + j) * 128 + 128] for j in range(3)
                    ]
                    acc3[0, slot(xx, yy), zc] = pack_four(
                        *tiles, output_out[row : row + 48, xx * 128 : xx * 128 + 128]
                    ).astype(acc3.dtype)
        if inside:
            red3.start(0)

        def proj_sums(i, carry):
            q = jnp.concatenate([r.dproj[0, rows(i), :], r.dproj[1, rows(i), :]], axis=1).astype(F32)
            val = jnp.concatenate([r.dproj[4, rows(i), :], r.dproj[5, rows(i), :]], axis=1).astype(F32)
            return (carry[0] + fold(q), carry[1] + fold(val), carry[2] + fold(r.cx[i].astype(F32)))

        qsum, vsum, csum = lax.fori_loop(0, 4, proj_sums, (zero8, zero8, zero8))
        r.sums[pl.ds(3 + 7, 1), :] = jnp.sum(qsum, axis=0, keepdims=True)
        r.sums[pl.ds(3 + 8, 1), :] = jnp.sum(vsum, axis=0, keepdims=True)
        r.sums[pl.ds(3 + 9, 1), :] = jnp.sum(csum, axis=0, keepdims=True)
        r.sums[pl.ds(13, 3), :] = jnp.zeros((3, HALF), F32)

        def n3_own(i, carry):
            both = dot_nt(proj_rows(i), wproj(half_of(c))) + n3.get(i)
            for j in range(2):
                vals = both[j * CHUNK : j * CHUNK + CHUNK]
                r.gtmp[rows(2 * i + j), :] = vals
                carry = carry[0] + fold(vals), carry[1] + fold(vals * hat3(2 * i + j))
            return carry

        sums3 = n3_own(1, n3_own(0, (zero8, zero8)))
        plain3, cross3, back3 = norm_back(sums3, lambda i: r.gtmp[rows(i), :], hat3, gain3, inv3)
        r.sums[pl.ds(2, 1), :] = cross3
        r.sums[pl.ds(3 + 2, 1), :] = plain3

        def shifted(buf, i, vals):
            buf[0, rows(i, CHUNK, ROW), :] = from_right(vals).astype(BF16)
            buf[1, rows(i, CHUNK, ROW), :] = vals.astype(BF16)
            buf[2, rows(i, CHUNK, ROW), :] = from_left(vals).astype(BF16)

        def residual_back(i, carry):
            vals = r.cx[i].astype(F32) + back3(i)
            r.gres[rows(i), :] = vals
            shifted(r.gr2, i, vals)
            return carry + fold(vals.astype(BF16).astype(F32))

        bias_two = lax.fori_loop(0, 4, residual_back, jnp.zeros((8, HALF), F32))
        r.sums[pl.ds(3 + 4, 1), :] = jnp.sum(bias_two, axis=0, keepdims=True)

        def act_back(buf, g, core, i, size):
            left = jnp.concatenate(
                [buf[b, rows(i, size, 2 * ROW - ROW * a), :] for a in range(3) for b in range(3)], axis=1
            )
            right = jnp.concatenate(
                [wtap(g, 3 * a + b, half_of(core)) for a in range(3) for b in range(3)], axis=1
            )
            return dot_nt(left, right)

        def conv_back(parts, buf, g):
            parts.fill(lambda i: act_back(buf, g, 1 - c, i, 2 * CHUNK))

        def conv_back_own(parts, buf, g, outer, hat):
            def own(i, carry):
                vals = act_back(buf, g, c, i, 2 * CHUNK) + parts.get(i)
                for j in range(2):
                    at = 2 * i + j
                    grad = vals[j * CHUNK : j * CHUNK + CHUNK] * outer(at)
                    r.gtmp[rows(at), :] = grad
                    carry = carry[0] + fold(grad), carry[1] + fold(grad * hat(at))
                return carry

            return own(1, own(0, (zero8, zero8)))

        def kernel_grad(act_t, buf, acc, after):
            def step(a):
                right = jnp.concatenate([buf[b, pl.ds(2 * ROW - ROW * a, PX), :] for b in range(3)], axis=1)
                out = dot(rows_of(act_t), right)
                for p, zc in enumerate(ALL):
                    for yy in range(2):
                        for xx in range(2):
                            row = p * BLK + yy * 48
                            tiles = [
                                out[row : row + 48, b * HALF + xx * 128 : b * HALF + xx * 128 + 128].astype(acc.dtype)
                                for b in range(3)
                            ]
                            acc[a, slot(xx, yy), zc] = pack_taps(*tiles)
                after(a)

            each(3, step)

        serve = inside
        d2 = Parts("d2")
        transposed_wait("act2_t")
        kernel_grad(r.act2_t, r.gr2, acc2, red2.start if inside else lambda a: None)
        if serve:
            red3.second(0, 1)
        conv_back(d2, r.gr2, k2)
        if serve:
            red2.second(0, 1)
        sums2 = conv_back_own(d2, r.gr2, k2, lambda i: silu_slope(pre2(i)), hat2)
        if serve:
            red2.second(1, 1)
            red3.third(0, 1)

        plain2, cross2, back2 = norm_back(sums2, lambda i: r.gtmp[rows(i), :], hat2, gain2 * scale, inv2)
        r.sums[pl.ds(1, 1), :] = scale * cross2
        r.sums[pl.ds(3 + 1, 1), :] = scale * plain2
        film_scale_term = gain2 * cross2 + shift2 * plain2
        r.sums[pl.ds(3 + 5, 1), :] = film_scale_term
        r.sums[pl.ds(3 + 6, 1), :] = plain2
        for j in range(2):
            r.ft[j] = film_scale_term[:, j * 128 : j * 128 + 128]
            r.ft[2 + j] = plain2[:, j * 128 : j * 128 + 128]
        head_start(lambda p: r.ft.at[p], r.th, r.th_s, r.th_r)
        r.th[h] = r.ft[h]

        def first_back(i, carry):
            vals = back2(i)
            shifted(r.gr1, i, vals)
            return carry + fold(vals.astype(BF16).astype(F32))

        bias_one = lax.fori_loop(0, 4, first_back, jnp.zeros((8, HALF), F32))
        r.sums[pl.ds(3 + 3, 1), :] = jnp.sum(bias_one, axis=0, keepdims=True)

        if serve:
            red2.second(2, 1)
            red2.third(0, 1)
            red2.third(1, 1)

        head_wait(lambda p: r.ft.at[p], r.th, r.th_s, r.th_r)
        for m in range(2):
            r.fa[d, pl.ds(m, 1), :] = jnp.concatenate([r.th[2 * m], r.th[2 * m + 1]], axis=1)
        dp_start(lambda p: r.fa.at[d], r.fa, r.fa_s, r.fa_r)

        d1 = Parts("d1")

        def after_chunk(a):
            if serve:
                red1.start(a)
                if a == 1:
                    red2.third(2, 1)

        transposed_wait("act1_t")
        kernel_grad(r.act1_t, r.gr1, acc1, after_chunk)
        conv_back(d1, r.gr1, k1)
        if serve:
            red1.second(0, 1)

        dp_wait(lambda p: r.fa.at[d], r.fa, r.fa_s, r.fa_r)
        for j in range(n):
            r.fta[pl.ds(2 * j, 2), :] = r.fa[j]
        film_block = dot_tn_high(r.esel[...], r.fta[...])
        r.film[...] = jnp.concatenate([film_block[:film_rows, :BLK], film_block[:film_rows, 128 : 128 + BLK]], axis=1)
        embed_part = dot_nt_high(r.fta[...], r.wfp[...].astype(F32))
        for j in range(n):
            r.ep[j] = embed_part[2 * j : 2 * j + 2]
        dp_start(lambda p: r.ep.at[p], r.er, r.er_s, r.er_r)
        r.er[d] = r.ep[d]

        def hat1(i):
            return (mixed(i) - mean1) * inv1

        sums1 = conv_back_own(d1, r.gr1, k1, lambda i: silu_slope(pre1(i)), hat1)
        if serve:
            red1.second(1, 1)

        plain1, cross1, back1 = norm_back(sums1, lambda i: r.gtmp[rows(i), :], hat1, gain1, inv1)
        r.sums[pl.ds(0, 1), :] = cross1
        r.sums[pl.ds(3, 1), :] = plain1
        r.ad[d] = r.sums[...]
        dp_start(lambda p: r.ad.at[d], r.ad, r.ad_s, r.ad_r)

        if serve:
            red1.second(2, 1)
            red1.third(0, 1)
        keep, _ = plan(r.steps[x], HALF)

        def image_back(i):
            return pack_pixels(keep * (r.gres[rows(i), :] + back1(i))).astype(BF16)

        for k in (2, 1, 3):
            peer = lax.rem(h + k, 4)
            r.io_src[peer] = image_back(peer)
            rc(r.io_src.at[peer], r.io_dst.at[h], r.io_s.at[k], r.io_r.at[h], (d, peer)).start()
        r.io_dst[h] = image_back(h)
        if serve:
            red1.third(1, 1)
            red1.third(2, 1)

        dp_wait(lambda p: r.ep.at[p], r.er, r.er_s, r.er_r)
        r.eh[h] = r.er[...]
        head_start(lambda p: r.eh.at[h], r.eh, r.eh_s, r.eh_r)
        dp_wait(lambda p: r.ad.at[d], r.ad, r.ad_s, r.ad_r)
        total = r.ad[0]
        for j in range(1, n):
            total = total + r.ad[j]
        r.hb[h] = total
        head_start(lambda p: r.hb.at[h], r.hb, r.hb_s, r.hb_r)
        head_wait(lambda p: r.ro_src.at[p], r.ro_dst, r.ro_s, r.ro_r)

        if inside:
            red2.finish(((0, 1), (1, 1), (2, 1)))
            for a in range(3):
                r.second[a] = red2.last(a)

        head_wait(lambda p: r.hb.at[h], r.hb, r.hb_s, r.hb_r)
        even = r.hb[0] + r.hb[2]
        odd = r.hb[1] + r.hb[3]
        wide = jnp.concatenate(
            [even[:, :BLK], odd[:, :BLK], even[:, 128 : 128 + BLK], odd[:, 128 : 128 + BLK]], axis=1
        )
        r.gains_out[...] = wide[0:3]
        r.biases_out[...] = wide[3:13]

        head_wait(lambda p: r.eh.at[h], r.eh, r.eh_s, r.eh_r)
        pieces = []
        for j in range(n):
            piece = (r.eh[0, j] + r.eh[1, j]) + (r.eh[2, j] + r.eh[3, j])
            pieces.append(piece[:, :film_rows])
        r.embed_grad[...] = jnp.concatenate(pieces, axis=1) * silu_slope(r.emb[...].astype(F32))

        head_wait(lambda p: r.io_src.at[p], r.io_dst, r.io_s, r.io_r)

        if inside:
            red3.finish(((0, 1),))
            tiles = unpack_four(red3.last(0))
            r.sb_src[...] = jnp.where(c == 0, tiles[2], tiles[0])
            back = rc(r.sb_src, r.sb_dst, r.sb_s.at[0], r.sb_r.at[0], sib)
            back.start()
            r.output[...] = tiles[3]
            for part in (ga, gb, gc):
                part.finish()
            red1.finish(((0, 1), (1, 1), (2, 1)))
            for a in range(3):
                r.first[a] = red1.last(a)
            back.wait()
            r.attend[:, 0:128] = jnp.where(c == 0, tiles[0], tiles[1])
            r.attend[:, 128:256] = r.sb_dst[...]
            r.attend[:, 256:384] = jnp.where(c == 0, tiles[1], tiles[2])

    return kernel


def make_writer(names_in, names_out):
    def kernel(*refs):
        count, wide = len(names_in), len(names_out)
        far_in, far_out = refs[:count], refs[count : count + wide]
        near_in, near_out = refs[count + wide : 2 * count + wide], refs[2 * count + wide : 2 * count + 2 * wide]
        sem_in, sem_out = refs[-2:]
        src, dst = Names(names_in, near_in), Names(names_out, near_out)
        loads = {
            name: pltpu.make_async_copy(far_in[i], near_in[i], sem_in.at[i]) for i, name in enumerate(names_in)
        }
        stores = {
            name: pltpu.make_async_copy(near_out[i], far_out[i], sem_out.at[i]) for i, name in enumerate(names_out)
        }
        for name in ("sel", "ro_dst", "io_dst"):
            loads[name].start()
        for name in names_in:
            if name not in ("sel", "ro_dst", "io_dst"):
                loads[name].start()
        loads["sel"].wait()
        for name, packed in (("result", "ro_dst"), ("image_grad", "io_dst")):
            loads[packed].wait()
            ref = getattr(src, packed)
            for m in range(2):
                getattr(dst, name)[m] = dot_nt(unpack_pixels(ref[2 * m]), src.sel[0]) + dot_nt(
                    unpack_pixels(ref[2 * m + 1]), src.sel[1]
                )
            stores[name].start()
        for name in ("first", "second"):
            if name in names_out:
                loads[name].wait()
                for a in range(3):
                    block = getattr(src, name)[a]
                    getattr(dst, name)[3 * a] = block[:48, :BLK]
                    getattr(dst, name)[3 * a + 1] = block[48:96, :BLK]
                    getattr(dst, name)[3 * a + 2] = last_tap(block)[:, :BLK]
                stores[name].start()
        if "attend" in names_out:
            loads["attend"].wait()
            dst.attend[...] = jnp.concatenate([src.attend[:, j * 128 : j * 128 + BLK] for j in range(3)], axis=1)
            stores["attend"].start()
            loads["output"].wait()
            dst.output[...] = src.output[:, :BLK]
            stores["output"].start()
        for name in ("embed_grad", "film", "gains_out", "biases_out"):
            loads[name].wait()
            getattr(dst, name)[...] = getattr(src, name)[...]
            stores[name].start()
        for name in names_out:
            stores[name].wait()

    return kernel


def per_device(n, *args):
    (
        images,
        noise_field,
        time_steps,
        embedding,
        first_kernel,
        second_kernel,
        film_weight,
        attend_weight,
        output_weight,
        norm_gains,
        biases,
        cotangent,
    ) = args
    inside = n == 8
    maps, height, width, channels = images.shape
    flat_shape = (maps, height * width, channels)
    film_rows = film_weight.shape[0]
    inputs = dict(
        steps=time_steps,
        images=images.reshape(flat_shape),
        noise=noise_field.reshape(flat_shape),
        cot=cotangent.reshape(flat_shape),
        emb=embedding,
        k1=first_kernel.reshape((9,) + first_kernel.shape[2:]),
        k2=second_kernel.reshape((9,) + second_kernel.shape[2:]),
        wf=film_weight,
        wa=attend_weight,
        wo=output_weight,
        gains=norm_gains,
        biases=biases,
        sel=jnp.asarray(channel_lanes(), BF16),
        gmask=jnp.asarray(group_mask(), BF16),
        selp=jnp.asarray(block_lanes(3), BF16),
    )
    shapes = dict(
        ro_dst=(4, 384, 128),
        io_dst=(4, 384, 128),
        embed_grad=embedding.shape,
        first=(3, 112, 128),
        second=(3, 112, 128),
        film=film_weight.shape,
        attend=(48, 384),
        output=(48, 128),
        gains_out=norm_gains.shape,
        biases_out=biases.shape,
    )
    names_in, names_out = list(INPUTS), list(OUTPUTS)
    core = lax.axis_index("head") % 2
    if not inside:
        def whole(array, row_axis):
            array = lax.all_gather(array, "dp", axis=row_axis, tiled=True)
            return lax.all_gather(array, "head", axis=array.ndim - 1, tiled=True)

        def spread(array, count):
            taps = array.shape[0]
            array = array.reshape(taps, 4, 2, 48, 2, 2, BLK)
            array = lax.dynamic_index_in_dim(array, core, 5, keepdims=False)
            array = jnp.transpose(array, (2, 4, 1, 0, 3, 5))
            array = jnp.pad(array, ((0, 0),) * 5 + ((0, 32),))
            return array.reshape(4, 4, taps * 48, 128)

        full_a = whole(attend_weight, 0).reshape(384, 2, 3, 2, BLK)
        full_a = jnp.transpose(full_a, (2, 0, 1, 3, 4)).reshape(3, 384, 384)
        full_o = whole(output_weight, 0)[None]
        for name, last, array in (("g1", "t1", first_kernel), ("g2", "t2", second_kernel)):
            blocks = spread(whole(array, 2).reshape(9, 384, 384), 9).reshape(4, 4, 3, 3, 48, 128)
            two = blocks[:, :, :, :2].reshape(4, 4, 3, 96, 128)
            inputs[name] = jnp.pad(two, ((0, 0),) * 3 + ((0, 16), (0, 0))).reshape(4, 4, 336, 128)
            inputs[last] = blocks[:, :, :, 2].reshape(4, 4, 144, 128)
        inputs["g3"] = spread(jnp.concatenate([full_a, full_o], axis=0), 4)
        names_in += ["g1", "g2", "t1", "t2", "g3"]
        shapes["first"] = shapes["second"] = (3, 4, 4, 112, 128)
        shapes["attend"] = (1, 4, 4, 144, 128)
        del shapes["output"]
        names_out.remove("output")
    items = scratch_list(n, inside, inputs)
    smem = pl.BlockSpec(memory_space=pltpu.SMEM)
    vmem = pl.BlockSpec(memory_space=pltpu.VMEM)
    outs = pl.pallas_call(
        make_kernel(
            n,
            inside,
            [name + "_far" if name in FAR else name for name in names_in] + names_out + [name for name, _ in items],
        ),
        out_shape=[
            jax.ShapeDtypeStruct(shapes[name], BF16 if name in ("ro_dst", "io_dst") else F32) for name in names_out
        ],
        in_specs=[
            smem if name == "steps" else pl.BlockSpec(memory_space=pl.ANY) if name in FAR else vmem
            for name in names_in
        ],
        out_specs=[vmem] * len(names_out),
        scratch_shapes=[item for _, item in items],
        compiler_params=pltpu.CompilerParams(
            collective_id=0, has_side_effects=True, vmem_limit_bytes=63 * 1024 * 1024
        ),
        name="blocks",
    )(*[inputs[name] for name in names_in])
    raw = dict(zip(names_out, outs))
    final = dict(
        result=flat_shape,
        image_grad=flat_shape,
        embed_grad=embedding.shape,
        film=film_weight.shape,
        gains_out=norm_gains.shape,
        biases_out=biases.shape,
    )
    if inside:
        final.update(first=(9, 48, BLK), second=(9, 48, BLK), attend=attend_weight.shape, output=output_weight.shape)
    names_last = [name for name in names_out if inside or name not in ("first", "second", "attend")] + ["sel"]
    names_final = list(final)
    given = [inputs["sel"] if name == "sel" else raw[name] for name in names_last]
    far = pl.BlockSpec(memory_space=pl.ANY)
    outs = pl.pallas_call(
        make_writer(names_last, names_final),
        out_shape=[jax.ShapeDtypeStruct(final[name], F32) for name in names_final],
        in_specs=[far] * len(names_last),
        out_specs=[far] * len(names_final),
        scratch_shapes=[pltpu.VMEM(array.shape, array.dtype) for array in given]
        + [pltpu.VMEM(final[name], F32) for name in names_final]
        + [pltpu.SemaphoreType.DMA((len(names_last),)), pltpu.SemaphoreType.DMA((len(names_final),))],
        compiler_params=pltpu.CompilerParams(vmem_limit_bytes=63 * 1024 * 1024),
        name="outputs",
    )(*given)
    out = dict(zip(names_final, outs))
    if not inside:

        def blocks_of(array, size):
            parts = [array[..., k * 48 : k * 48 + 48, :BLK] for k in range(size)]
            if size == 2:
                lanes = [array[..., k * 32 : k * 32 + 32, BLK:] for k in range(3)]
                lanes = jnp.concatenate(lanes, axis=-1)
                parts.append(jnp.concatenate([lanes, array[..., 96:112, :BLK]], axis=-2))
            else:
                lanes = [array[..., k * 48 : k * 48 + 48, BLK:] for k in range(3)]
                parts.append(jnp.concatenate(lanes, axis=-1))
            array = jnp.stack(parts, axis=1)
            array = array.reshape(array.shape[:2] + (2, 2, 4, 48, BLK))
            taps = array.shape[0] * array.shape[1]
            array = jnp.transpose(array, (0, 1, 4, 2, 5, 3, 6)).reshape(taps, 384, 2, 1, BLK)
            both = jnp.concatenate([array, jnp.zeros_like(array)], axis=3)
            return jnp.where(core == 0, both, both[:, :, :, ::-1]).reshape(taps, 384, 384)

        def shared(array, axis):
            array = lax.psum_scatter(array, "head", scatter_dimension=array.ndim - 1, tiled=True)
            return lax.psum_scatter(array, "dp", scatter_dimension=axis, tiled=True)

        out["first"] = shared(blocks_of(raw["first"], 2), 1)
        out["second"] = shared(blocks_of(raw["second"], 2), 1)
        both = blocks_of(raw["attend"], 3)
        joined = both[:3].reshape(3, 384, 2, 2, BLK)
        joined = jnp.transpose(joined, (1, 2, 0, 3, 4)).reshape(384, 1152)
        out["attend"] = shared(joined, 0)
        out["output"] = shared(both[3], 0)
    return (
        out["result"].reshape(images.shape),
        out["image_grad"].reshape(images.shape),
        out["embed_grad"],
        out["first"].reshape(first_kernel.shape),
        out["second"].reshape(second_kernel.shape),
        out["film"],
        out["attend"],
        out["output"],
        out["gains_out"],
        out["biases_out"],
    )


def solution(mesh):
    n = mesh.shape["dp"]
    field = P("dp", "head", None, None)
    taps = P(None, None, "dp", "head")
    both = P("dp", "head")
    return jax.shard_map(
        lambda *args: per_device(n, *args),
        mesh=mesh,
        in_specs=(field, field, P("dp"), P("dp", None), taps, taps, both, both, both, P(), P(), field),
        out_specs=(field, field, P("dp", None), taps, taps, both, both, both, P(), P()),
        check_vma=False,
    )
```

```python
import math

import jax
import jax.numpy as jnp
import numpy as np
from jax import lax
from jax.experimental import pallas as pl
from jax.experimental.pallas import tpu as pltpu
from jax.sharding import PartitionSpec as P

HEAD_DIM = 96
GROUPS = 32
STEPS = 4000
EPS = 1e-05
OFFSET = 0.008
MESH = pl.DeviceIdType.MESH
F32 = jnp.float32
BF16 = jnp.bfloat16

PX = 1024
ROW = 32
CHUNK = 256
BLK = 96
HALF = 256
NHEAD = 4


def plan(time_step, lanes):
    fraction = (jnp.full((1, lanes), time_step, jnp.int32).astype(F32) + 1.0) / STEPS
    start = math.cos(OFFSET / (1.0 + OFFSET) * (math.pi / 2)) ** 2
    curve = jnp.square(jnp.cos((fraction + OFFSET) / (1.0 + OFFSET) * (math.pi / 2))) / start
    return (jnp.sqrt(curve), jnp.sqrt(jnp.maximum(1.0 - curve, 0.0)))


def channel_lanes():
    sel = np.zeros((2, 384, HALF), np.float32)
    for block in range(4):
        for j in range(BLK):
            sel[block % 2, block * BLK + j, (block // 2) * 128 + j] = 1.0
    return sel


def block_lanes(count):
    sel = np.zeros((count * BLK, count * 128), np.float32)
    for block in range(count):
        for j in range(BLK):
            sel[block * BLK + j, block * 128 + j] = 1.0
    return sel


def group_mask():
    lane = np.arange(HALF)
    ok = lane % 128 < BLK
    group = (lane // 128) * 100 + (lane % 128) // 12
    return ((group[:, None] == group[None, :]) & ok[:, None] & ok[None, :]).astype(np.float32)


def dot(a, b):
    return lax.dot_general(a, b, (((1,), (0,)), ((), ())), preferred_element_type=F32)


def dot_nt(a, b):
    return lax.dot_general(a, b, (((1,), (1,)), ((), ())), preferred_element_type=F32)


def dot_nt_high(a, b):
    return lax.dot_general(
        a, b, (((1,), (1,)), ((), ())), preferred_element_type=F32, precision=lax.Precision.HIGHEST
    )


def dot_tn_high(a, b):
    return lax.dot_general(
        a, b, (((0,), (0,)), ((), ())), preferred_element_type=F32, precision=lax.Precision.HIGHEST
    )


def exact_dot(values, ones):
    high = values.astype(BF16).astype(F32)
    rest = values - high
    middle = rest.astype(BF16).astype(F32)
    low = rest - middle
    rows = values.shape[0]
    out = dot(jnp.concatenate([high, middle, low], axis=0).astype(BF16), ones)
    return out[:rows] + out[rows : 2 * rows] + out[2 * rows :]


def sigmoid(v):
    return 0.5 + 0.5 * jnp.tanh(0.5 * v)


def silu(v):
    return v * sigmoid(v)


def silu_slope(v):
    s = sigmoid(v)
    return s * (1.0 + v * (1.0 - s))


def pack_taps(t0, t1, t2):
    t0, t1, t2 = t0[:, :BLK], t1[:, :BLK], t2[:, :BLK]
    join = lambda a, b: jnp.concatenate([a, b], axis=1)
    return jnp.concatenate(
        [
            join(t0[:32], t2[:32, :32]),
            join(t0[32:], t2[:16, 32:64]),
            join(t1[:16], t2[16:32, 32:64]),
            join(t1[16:], t2[:32, 64:]),
            join(t2[32:], jnp.zeros((16, 32), t2.dtype)),
        ],
        axis=0,
    )


def last_tap(packed):
    lanes = [packed[:32, BLK:], packed[32:64, BLK:], packed[64:96, BLK:], jnp.zeros((32, 32), packed.dtype)]
    return jnp.concatenate([jnp.concatenate(lanes, axis=1), packed[96:112]], axis=0)


def pack_four(b0, b1, b2, b3):
    return jnp.concatenate(
        [jnp.concatenate([b[:, :BLK], b3[:, 32 * k : 32 * k + 32]], axis=1) for k, b in enumerate((b0, b1, b2))],
        axis=0,
    )


def unpack_four(packed):
    size = packed.shape[0] // 3
    parts = [packed[k * size : k * size + size] for k in range(3)]
    zero = jnp.zeros((size, 32), packed.dtype)
    fourth = jnp.concatenate([p[:, BLK:] for p in parts] + [zero], axis=1)
    return [jnp.concatenate([p[:, :BLK], zero], axis=1) for p in parts] + [fourth]


def pack_pixels(full):
    half = CHUNK // 2
    return pack_four(full[:half, :128], full[half:, :128], full[:half, 128:], full[half:, 128:])


def unpack_pixels(packed):
    b0, b1, b2, b3 = unpack_four(packed)
    return jnp.concatenate([jnp.concatenate([b0, b2], axis=1), jnp.concatenate([b1, b3], axis=1)], axis=0)


INPUTS = (
    "steps",
    "images",
    "noise",
    "cot",
    "emb",
    "k1",
    "k2",
    "wf",
    "wa",
    "wo",
    "gains",
    "biases",
    "sel",
    "gmask",
    "selp",
)
OUTPUTS = (
    "ro_dst",
    "io_dst",
    "embed_grad",
    "first",
    "second",
    "film",
    "attend",
    "output",
    "gains_out",
    "biases_out",
)


FAR = (
    "images",
    "noise",
    "cot",
    "sel",
    "selp",
    "k2",
    "wa",
    "wf",
    "gmask",
)


class Names:
    def __init__(self, names, refs):
        for name, ref in zip(names, refs):
            setattr(self, name, ref)


def scratch_list(n, inside, inputs):
    dma = pltpu.SemaphoreType.DMA
    items = []

    def vm(name, shape, dtype):
        items.append((name, pltpu.VMEM(shape, dtype)))

    def sem(name, count):
        items.append((name + "_s", dma((count,))))
        items.append((name + "_r", dma((count,))))

    for name in FAR:
        vm(name, inputs[name].shape, inputs[name].dtype)
    items.append(("far_s", dma((len(FAR),))))
    for name in ("mx", "cx", "ro", "io"):
        vm(name + "_src", (4, 384, 128), BF16)
        if name in ("mx", "cx"):
            vm(name + "_dst", (4, 384, 128), BF16)
            vm(name, (4, CHUNK, HALF), BF16)
        sem(name, 4)
    for name in ("act1", "act2"):
        vm(name, (2, PX + 2 * ROW, HALF), BF16)
        vm(name + "_t", (2, HALF, PX), BF16)
        sem(name, 4)
        sem(name + "_t", 1)
    vm("ai", (2, PX, HALF), BF16)
    vm("ai_t", (2, HALF, PX), BF16)
    sem("ai_t", 1)
    sem("ai", 4)
    vm("att", (4, PX, 128), BF16)
    vm("att_t", (2, HALF, PX), BF16)
    sem("att", 4)
    for name in ("do", "n3", "d2", "d1"):
        vm(name + "_src", (PX, HALF), BF16)
        vm(name + "_dst", (PX, HALF), BF16)
        sem(name, 2)
    vm("v2", (PX, HALF), F32)
    vm("v3", (PX, HALF), F32)
    vm("gres", (PX, HALF), F32)
    vm("gtmp", (PX, HALF), F32)
    vm("qkv", (6, PX, 128), BF16)
    vm("kvt", (4, 128, PX), BF16)
    vm("dout", (2, PX, 128), BF16)
    vm("dproj", (6, PX, 128), BF16)
    vm("gr2", (3, PX + 2 * ROW, HALF), BF16)
    vm("gr1", (3, PX + 2 * ROW, HALF), BF16)
    vm("par", (16, 384), F32)
    vm("parown", (16, HALF), F32)
    vm("stat", (16, HALF), F32)
    vm("sums", (16, HALF), F32)
    if inside:
        vm("g1", (4, 4, 336, 128), BF16)
        vm("g2", (4, 4, 336, 128), BF16)
        vm("t1", (4, 4, 144, 128), BF16)
        vm("t2", (4, 4, 144, 128), BF16)
        vm("p3", (4, 4, 144, 128), BF16)
        vm("g3", (4, 4, 192, 128), BF16)
        for name in ("g1", "g2", "p3"):
            sem(name + "z", 4)
            sem(name + "v", 4)
            sem(name + "w", 8)
        vm("sw_src", (48, 128), BF16)
        vm("sw_dst", (48, 128), BF16)
        sem("sw", 1)
        vm("sb_src", (48, 128), F32)
        vm("sb_dst", (48, 128), F32)
        sem("sb", 1)
        for name, nc, rows in (("r1", 3, 112), ("r2", 3, 112), ("r3", 1, 144)):
            vm(name + "_acc", (nc, 4, 4, rows, 128), BF16)
            vm(name + "_own", (nc, rows, 128), F32)
            vm(name + "w_dst", (nc, 2, 4, rows, 128), BF16)
            vm(name + "v_src", (nc, 4, rows, 128), BF16)
            vm(name + "v_dst", (nc, 4, rows, 128), BF16)
            vm(name + "z_src", (4, nc, rows, 128), BF16)
            vm(name + "z_dst", (4, nc, rows, 128), BF16)
            sem(name + "w", nc)
            sem(name + "v", nc)
            sem(name + "z", nc * 4)
    vm("el", (n, 2, 768), F32)
    sem("el", n)
    vm("em", (2 * n, 768), F32)
    vm("wfp", (128, HALF), BF16)
    vm("esel", (2 * n, 128), F32)
    vm("fp", (n, 2, HALF), F32)
    vm("fr", (n, 2, HALF), F32)
    sem("fr", n)
    vm("fx", (4, 1, 128), F32)
    vm("fh", (4, 1, 128), F32)
    sem("fh", 4)
    vm("ft", (4, 1, 128), F32)
    vm("th", (4, 1, 128), F32)
    sem("th", 4)
    vm("fa", (n, 2, HALF), F32)
    sem("fa", n)
    vm("fta", (2 * n, HALF), F32)
    vm("ep", (n, 2, 128), F32)
    vm("er", (n, 2, 128), F32)
    sem("er", n)
    vm("eh", (4, n, 2, 128), F32)
    sem("eh", 4)
    vm("ad", (n, 16, HALF), F32)
    sem("ad", n)
    vm("hb", (4, 16, HALF), F32)
    sem("hb", 4)
    return items


def make_kernel(n, inside, names):
    film_rows = 768 // n

    def kernel(*refs):
        r = Names(names, refs)
        d = lax.axis_index("dp")
        h = lax.axis_index("head")
        x = h // 2
        c = h - 2 * x
        z = d // 2
        y = d - 2 * z
        sib = (d, h + 1 - 2 * c)
        xdev = (d, h + 2 - 4 * x)
        v = x + c * (y - x)
        w = y + c * (x - y)
        vdev = (d + c * (1 - 2 * y), h + (1 - c) * (2 - 4 * x))
        wdev = (d + (1 - c) * (1 - 2 * y), h + c * (2 - 4 * x))

        def slot(xx, yy, o=c):
            if inside:
                return (yy + o * (xx - yy)) * 2 + xx + o * (yy - xx)
            return yy * 2 + xx

        def order(split, i):
            return c * (i // 2) if split else c

        def rc(src, dst, send, recv, dev):
            return pltpu.make_async_remote_copy(
                src_ref=src, dst_ref=dst, send_sem=send, recv_sem=recv, device_id=dev, device_id_type=MESH
            )

        def loop(count, body):
            def step(i, carry):
                body(i)
                return carry

            lax.fori_loop(0, count, step, 0)

        def each(count, body):
            for i in range(count):
                body(i)

        def rows(i, size=CHUNK, base=0):
            return pl.ds(pl.multiple_of(base + i * size, 32), size)

        def dp_start(src_of, dst, send, recv):
            def step(k, carry):
                peer = lax.rem(d + k, n)
                rc(src_of(peer), dst.at[d], send.at[k], recv.at[d], (peer, h)).start()
                return carry

            lax.fori_loop(1, n, step, 0)

        def dp_wait(src_of, dst, send, recv):
            def step(k, carry):
                peer = lax.rem(d + k, n)
                copy = rc(src_of(peer), dst.at[peer], send.at[k], recv.at[peer], (peer, h))
                copy.wait_recv()
                copy.wait_send()
                return carry

            lax.fori_loop(1, n, step, 0)

        def head_start(src_of, dst, send, recv):
            for k in range(1, 4):
                peer = lax.rem(h + k, 4)
                rc(src_of(peer), dst.at[h], send.at[k], recv.at[h], (d, peer)).start()

        def head_wait(src_of, dst, send, recv):
            for k in range(1, 4):
                peer = lax.rem(h + k, 4)
                copy = rc(src_of(peer), dst.at[peer], send.at[k], recv.at[peer], (d, peer))
                copy.wait_recv()
                copy.wait_send()

        class Halves:
            def __init__(self, name, base):
                self.buf, self.base = getattr(r, name), base
                self.send, self.recv = getattr(r, name + "_s"), getattr(r, name + "_r")

            def at(self, core, i):
                return self.buf.at[core, rows(i, CHUNK, self.base)]

            def fill(self, make):
                def body(i):
                    self.buf[c, rows(i, CHUNK, self.base), :] = make(i)
                    ref = self.at(c, i)
                    rc(ref, ref, self.send.at[i], self.recv.at[i], sib).start()

                loop(4, body)

            def wait(self):
                for i in range(4):
                    ref = self.at(1 - c, i)
                    copy = rc(ref, ref, self.send.at[i], self.recv.at[i], sib)
                    copy.wait_recv()
                    copy.wait_send()

        class Parts:
            def __init__(self, name):
                self.src, self.dst = getattr(r, name + "_src"), getattr(r, name + "_dst")
                self.send, self.recv = getattr(r, name + "_s"), getattr(r, name + "_r")

            def copy(self, i):
                at = rows(i, 2 * CHUNK)
                return rc(self.src.at[at], self.dst.at[at], self.send.at[i], self.recv.at[i], sib)

            def fill(self, make):
                def body(i):
                    self.src[rows(i, 2 * CHUNK), :] = make(i).astype(BF16)
                    self.copy(i).start()

                each(2, body)

            def get(self, i):
                copy = self.copy(i)
                copy.wait_recv()
                copy.wait_send()
                return self.dst[rows(i, 2 * CHUNK), :].astype(F32)

        class Gather:
            def __init__(self, name, split):
                self.g, self.split = getattr(r, name), split
                self.zs, self.zr = getattr(r, name + "z_s"), getattr(r, name + "z_r")
                self.vs, self.vr = getattr(r, name + "v_s"), getattr(r, name + "v_r")
                self.ws, self.wr = getattr(r, name + "w_s"), getattr(r, name + "w_r")

            def at(self, i, far_w, far_v):
                o = order(self.split, i)
                vv, ww = x + o * (y - x), y + o * (x - y)
                return (ww + far_w * (1 - 2 * ww)) * 2 + vv + far_v * (1 - 2 * vv)

            def zcopy(self, k):
                peer = (lax.rem(z + k, 4) * 2 + y, h)
                src, dst = self.g.at[self.at(0, 0, 0), 0], self.g.at[self.at(4 - k, 0, 0), 4 - k]
                return rc(src, dst, self.zs.at[k], self.zr.at[4 - k], peer)

            def vcopy(self, far_v, i):
                o = order(self.split, i)
                ref = self.g.at[self.at(i, 0, far_v), i]
                dev = (d + o * (1 - 2 * y), h + (1 - o) * (2 - 4 * x))
                return rc(ref, ref, self.vs.at[i], self.vr.at[i], dev)

            def wcopy(self, far_w, far_v, i):
                o = order(self.split, i)
                ref = self.g.at[self.at(i, far_w, far_v), i]
                dev = (d + (1 - o) * (1 - 2 * y), h + o * (2 - 4 * x))
                return rc(ref, ref, self.ws.at[2 * i + far_v], self.wr.at[2 * i + far_v], dev)

            def own_z(self):
                for k in range(1, 4):
                    self.zcopy(k).start()

            def own(self):
                self.vcopy(0, 0).start()
                self.wcopy(0, 0, 0).start()

            def pass_own(self):
                self.vcopy(1, 0).wait_recv()
                self.wcopy(0, 1, 0).start()

            def pass_z(self, *ks):
                for k in ks:
                    self.zcopy(k).wait_recv()
                    self.vcopy(0, 4 - k).start()
                    self.wcopy(0, 0, 4 - k).start()

            def pass_v(self, *ks):
                for k in ks:
                    self.vcopy(1, 4 - k).wait_recv()
                    self.wcopy(0, 1, 4 - k).start()

            def take(self, blocks):
                for i, far_v in ((0, 0), (0, 1), (3, 0), (1, 0), (2, 0), (3, 1), (1, 1), (2, 1)):
                    self.wcopy(1, far_v, i).wait_recv()
                    blocks.unpack([(self.at(i, 1, far_v), i)])

            def finish(self):
                for k in range(1, 4):
                    self.zcopy(k).wait_send()
                for i in range(4):
                    self.vcopy(0, i).wait_send()
                    for far_v in range(2):
                        self.wcopy(0, far_v, i).wait_send()

            def blocks(self, far_w):
                return [(self.at(i, far_w, far_v), i) for i in range(4) for far_v in range(2)]

        class Reduce:
            def __init__(self, name, count):
                get = lambda tail: getattr(r, name + tail)
                self.acc, self.count = get("_acc"), count
                self.wdst, self.ws, self.wr, self.own = get("w_dst"), get("w_s"), get("w_r"), get("_own")
                self.vsrc, self.vdst, self.vs, self.vr = get("v_src"), get("v_dst"), get("v_s"), get("v_r")
                self.zsrc, self.zdst, self.zs, self.zr = get("z_src"), get("z_dst"), get("z_s"), get("z_r")

            def wcopy(self, a):
                ref = self.acc.at[a, pl.ds((1 - w) * 2, 2)]
                return rc(ref, self.wdst.at[a], self.ws.at[a], self.wr.at[a], wdev)

            def vcopy(self, a, size):
                at = pl.ds(a, size)
                return rc(self.vsrc.at[at], self.vdst.at[at], self.vs.at[a], self.vr.at[a], vdev)

            def zcopy(self, a, size, k):
                at = pl.ds(a, size)
                return rc(
                    self.zsrc.at[k, at],
                    self.zdst.at[4 - k, at],
                    self.zs.at[a * 4 + k],
                    self.zr.at[a * 4 + 4 - k],
                    (lax.rem(z + k, 4) * 2 + y, h),
                )

            def start(self, a):
                self.wcopy(a).start()

            def second(self, first, size):
                for a in range(first, first + size):
                    self.wcopy(a).wait_recv()

                    def step(zz, carry):
                        self.vsrc[a, zz] = (
                            self.acc[a, w * 2 + 1 - v, zz].astype(F32) + self.wdst[a, 1 - v, zz].astype(F32)
                        ).astype(BF16)
                        return carry

                    lax.fori_loop(0, 4, step, 0)
                self.vcopy(first, size).start()

            def third(self, first, size):
                self.vcopy(first, size).wait_recv()
                for a in range(first, first + size):

                    for k in range(4):
                        zz = lax.rem(z + k, 4)
                        total = (
                            self.acc[a, w * 2 + v, zz].astype(F32)
                            + self.wdst[a, v, zz].astype(F32)
                            + self.vdst[a, zz].astype(F32)
                        )
                        if k == 0:
                            self.own[a] = total
                        else:
                            self.zsrc[k, a] = total.astype(BF16)
                for k in range(1, 4):
                    self.zcopy(first, size, k).start()

            def finish(self, groups):
                for first, size in groups:
                    self.vcopy(first, size).wait_send()
                    for k in range(1, 4):
                        copy = self.zcopy(first, size, k)
                        copy.wait_recv()
                        copy.wait_send()
                for a in range(self.count):
                    self.wcopy(a).wait_send()

            def last(self, a):
                total = self.own[a]
                for k in range(1, 4):
                    total = total + self.zdst[k, a].astype(F32)
                return total

        def rel(zc):
            return lax.rem(zc - z + 4, 4) if inside else zc

        def where_is(split, xx, yy, zc):
            i = rel(zc)
            return slot(xx, yy, order(split, i)), i

        class Taps:
            def __init__(self, packed, last, split):
                self.packed, self.last, self.split = packed, last, split

            def block(self, tap, zc, xx, yy):
                a, b = tap // 3, tap % 3
                q, i = where_is(self.split, xx, yy, zc)
                if b < 2:
                    return self.packed[q, i, pl.ds(a * 112 + b * 48, 48), :]
                return self.last[q, i, pl.ds(a * 48, 48), :]

            def unpack(self, places):
                for q, i in places:
                    for a in range(3):
                        self.last[q, i, pl.ds(a * 48, 48), :] = last_tap(self.packed[q, i, pl.ds(a * 112, 112), :])

        class Plain:
            def __init__(self, blocks, split):
                self.blocks, self.split = blocks, split

            def block(self, tap, zc, xx, yy):
                q, i = where_is(self.split, xx, yy, zc)
                return self.blocks[q, i, pl.ds(tap * 48, 48), :]

            def unpack(self, places):
                for q, i in places:
                    self.blocks[q, i] = jnp.concatenate(unpack_four(r.p3[q, i]), axis=0)

        k1, k2, k3 = Taps(r.g1, r.t1, True), Taps(r.g2, r.t2, False), Plain(r.g3, True)

        def wtile(g, tap, zc, xx):
            return jnp.concatenate(
                [g.block(tap, zc, xx, 0), g.block(tap, zc, xx, 1), jnp.zeros((32, 128), BF16)], axis=0
            )

        def wtap(g, tap, zcs):
            return jnp.concatenate(
                [jnp.concatenate([wtile(g, tap, zc, xx) for xx in range(2)], axis=1) for zc in zcs], axis=0
            )

        ALL = (0, 2, 1, 3)

        def half_of(core):
            return (core, core + 2)

        def wproj(zcs):
            return jnp.concatenate(
                [
                    jnp.concatenate([wtile(k3, j, zc, xx) for xx in range(2) for j in range(3)], axis=1)
                    for zc in zcs
                ],
                axis=0,
            )

        def flat(buf, base, i, size):
            return jnp.concatenate([buf[0, rows(i, size, base), :], buf[1, rows(i, size, base), :]], axis=1)

        barrier = pltpu.get_barrier_semaphore()

        def greet(k, carry):
            pl.semaphore_signal(barrier, inc=1, device_id=(lax.rem(d + k, n), h), device_id_type=MESH)
            return carry

        lax.fori_loop(1, n, greet, 0)
        for k in range(1, 4):
            pl.semaphore_signal(barrier, inc=1, device_id=(d, lax.rem(h + k, 4)), device_id_type=MESH)
        def fetch(name):
            return pltpu.make_async_copy(getattr(r, name + "_far"), getattr(r, name), r.far_s.at[FAR.index(name)])

        for name in FAR:
            fetch(name).start()
        if inside:
            ga, gb, gc = Gather("g1", True), Gather("g2", False), Gather("p3", True)
            for a in range(3):
                r.g1[ga.at(0, 0, 0), 0, pl.ds(a * 112, 112), :] = pack_taps(*[r.k1[3 * a + b] for b in range(3)])
        pl.semaphore_wait(barrier, n - 1 + 3)
        if inside:
            ga.own_z()
            ga.own()

        for name in FAR:
            fetch(name).wait()
        def head_copy(src, dst, send, recv, k):
            peer = lax.rem(h + k, 4)
            return rc(src.at[peer], dst.at[h], send.at[k], recv.at[h], (d, peer))

        for step in range(2):
            m = x + (1 - step) * (1 - 2 * x)
            keep, spread = plan(r.steps[m], 384)
            low = (keep * r.images[m].astype(F32) + spread * r.noise[m].astype(F32)).astype(BF16)
            for core in range(2):
                r.mx_src[m * 2 + core] = pack_pixels(dot(low, r.sel[core])).astype(BF16)
            for k in (2, 3 - 2 * c) if step == 0 else (1 + 2 * c,):
                head_copy(r.mx_src, r.mx_dst, r.mx_s, r.mx_r, k).start()
        r.mx_dst[h] = r.mx_src[h]
        if inside:
            ga.pass_own()

        r.el[d] = silu(r.emb[...].astype(F32)).astype(BF16).astype(F32)
        dp_start(lambda p: r.el.at[d], r.el, r.el_s, r.el_r)

        if inside:
            blocks = dot(r.wa[...], r.selp[: 3 * BLK, : 3 * 128]).astype(BF16)
            r.sw_src[...] = blocks[:, 128:256]
            swap = rc(r.sw_src, r.sw_dst, r.sw_s.at[0], r.sw_r.at[0], sib)
            swap.start()
            for a in range(3):
                r.g2[gb.at(0, 0, 0), 0, pl.ds(a * 112, 112), :] = pack_taps(*[r.k2[3 * a + b] for b in range(3)])
        r.par[0:3, :] = r.gains[...]
        r.par[3:13, :] = r.biases[...]
        r.par[13:16, :] = jnp.zeros((3, 384), F32)
        r.parown[...] = exact_dot(r.par[...], r.sel[c])

        def prow(i):
            return r.parown[pl.ds(i, 1), :]

        for buf in (r.act1, r.act2):
            for core in range(2):
                buf[core, pl.ds(0, ROW), :] = jnp.zeros((ROW, HALF), BF16)
                buf[core, pl.ds(PX + ROW, ROW), :] = jnp.zeros((ROW, HALF), BF16)
        for buf in (r.gr1, r.gr2):
            for b in range(3):
                buf[b, pl.ds(0, ROW), :] = jnp.zeros((ROW, HALF), BF16)
                buf[b, pl.ds(PX + ROW, ROW), :] = jnp.zeros((ROW, HALF), BF16)
        r.wfp[...] = jnp.zeros((128, HALF), BF16)
        r.wfp[pl.ds(0, film_rows), :] = dot(r.wf[...], r.selp[: 2 * BLK, :HALF]).astype(BF16)
        if inside:
            ga.pass_z(1, 3, 2)
            gb.own_z()

        count = float(PX * 12)

        def fold(vals):
            return jnp.sum(vals.reshape(CHUNK // 8, 8, HALF), axis=0)

        def sums_of(fn, k):
            def step(i, carry):
                return tuple(a + fold(b) for a, b in zip(carry, fn(i)))

            zero = jnp.zeros((8, HALF), F32)
            return lax.fori_loop(0, 4, step, (zero,) * k)

        def group_mean(part):
            return jnp.sum(exact_dot(part, r.gmask[...]), axis=0, keepdims=True) / count

        def norm(load, which, total):
            mean = group_mean(total)
            (square,) = sums_of(lambda i: (jnp.square(load(i) - mean),), 1)
            inv = lax.rsqrt(group_mean(square) + EPS)
            r.stat[pl.ds(2 * which, 1), :] = mean
            r.stat[pl.ds(2 * which + 1, 1), :] = inv
            return mean, inv

        zero8 = jnp.zeros((8, HALF), F32)

        def norm_back(sums, load_grad, load_hat, coef, inv):
            plain, cross = sums
            means = exact_dot(jnp.concatenate([coef * plain, coef * cross], axis=0), r.gmask[...])
            plain_mean = jnp.sum(means[:8], axis=0, keepdims=True) / count
            cross_mean = jnp.sum(means[8:], axis=0, keepdims=True) / count
            outer, base, slope = inv * coef, inv * plain_mean, inv * cross_mean

            def chunk(i):
                return outer * load_grad(i) - base - load_hat(i) * slope

            return (
                jnp.sum(plain, axis=0, keepdims=True),
                jnp.sum(cross, axis=0, keepdims=True),
                chunk,
            )

        def transposed(name, core):
            ref = getattr(r, name).at[core]
            return rc(ref, ref, getattr(r, name + "_s").at[0], getattr(r, name + "_r").at[0], sib)

        def transpose_act(buf, base, name):
            out = getattr(r, name)
            for q in range(4):
                out[c, :, pl.ds(q * CHUNK, CHUNK)] = jnp.transpose(buf[c, pl.ds(base + q * CHUNK, CHUNK), :])
            transposed(name, c).start()

        def transposed_wait(name):
            copy = transposed(name, 1 - c)
            copy.wait_recv()
            copy.wait_send()

        head_wait(lambda p: r.mx_src.at[p], r.mx_dst, r.mx_s, r.mx_r)

        def unpack_mixed(i, carry):
            vals = unpack_pixels(r.mx_dst[i])
            r.mx[i] = vals
            return carry + fold(vals.astype(F32))

        mixed_sum = lax.fori_loop(0, 4, unpack_mixed, zero8)

        def mixed(i):
            return r.mx[i].astype(F32)

        if inside:
            ga.pass_v(1, 3)
        mean1, inv1 = norm(mixed, 0, mixed_sum)
        if inside:
            ga.pass_v(2)
            gb.own()
        gain1, shift1 = prow(0), prow(3)
        act1 = Halves("act1", ROW)

        def affine(mean, inv, gain, shift):
            return inv * gain, shift - mean * (inv * gain)

        mul1, add1 = affine(mean1, inv1, gain1, shift1)

        def pre1(i):
            return mixed(i) * mul1 + add1

        act1.fill(lambda i: silu(pre1(i)).astype(BF16))
        dp_wait(lambda p: r.el.at[d], r.el, r.el_s, r.el_r)
        for j in range(n):
            r.em[pl.ds(2 * j, 2), :] = r.el[j]
        place = lax.broadcasted_iota(jnp.int32, (768, 128), 0) - film_rows * d
        lane = lax.broadcasted_iota(jnp.int32, (768, 128), 1)
        pick = jnp.where((place == lane) & (lane < film_rows), 1.0, 0.0).astype(BF16)
        r.esel[...] = dot(r.em[...].astype(BF16), pick)
        film_part = dot(r.esel[...].astype(BF16), r.wfp[...])
        for j in range(n):
            r.fp[j] = film_part[2 * j : 2 * j + 2]
        dp_start(lambda p: r.fp.at[p], r.fr, r.fr_s, r.fr_r)
        r.fr[d] = r.fp[d]
        if inside:
            swap.wait()
            got = r.sw_dst[...]
            keep0, keep2 = blocks[:, :128], blocks[:, 256:]
            r.p3[gc.at(0, 0, 0), 0] = pack_four(
                jnp.where(c == 0, keep0, got),
                jnp.where(c == 0, keep2, keep0),
                jnp.where(c == 0, got, keep2),
                r.wo[...],
            )
        act1.wait()
        transpose_act(r.act1, ROW, "act1_t")
        if inside:
            gb.pass_own()
            gb.pass_z(1, 3, 2)
            gc.own_z()
        def split_cot(m, carry):
            for core in range(2):
                r.cx_src[m * 2 + core] = pack_pixels(dot(r.cot[m], r.sel[core])).astype(BF16)
            return carry

        lax.fori_loop(0, 2, split_cot, 0)
        column = lax.broadcasted_iota(jnp.int32, (1, ROW, HALF), 1)
        not_first = jnp.where(column > 0, 1.0, 0.0)
        not_last = jnp.where(column < ROW - 1, 1.0, 0.0)

        def in_rows(vals, mask):
            return (vals.reshape(CHUNK // ROW, ROW, HALF) * mask).reshape(CHUNK, HALF)

        def from_left(vals):
            return in_rows(pltpu.roll(vals, 1, 0), not_first)

        def from_right(vals):
            return in_rows(pltpu.roll(vals, CHUNK - 1, 0), not_last)

        def conv(buf, g, store, between):
            weights = lambda: jnp.concatenate(
                [jnp.concatenate([wtap(g, 3 * a + b, ALL) for b in range(3)], axis=1) for a in range(3)], axis=0
            )

            total = zero8
            for i in range(2):
                left = jnp.concatenate([flat(buf, ROW * a, i, 2 * CHUNK) for a in range(3)], axis=1)
                out = dot(left, weights())
                for j in range(2):
                    part = out[j * CHUNK : j * CHUNK + CHUNK]
                    part = part[:, HALF : 2 * HALF] + from_left(part[:, :HALF]) + from_right(part[:, 2 * HALF :])
                    total = total + fold(store(2 * i + j, part))
                if i == 0:
                    between()
            return total

        if inside:
            k1.unpack(ga.blocks(0))
            ga.take(k1)

        dp_wait(lambda p: r.fp.at[p], r.fr, r.fr_s, r.fr_r)
        film_sum = r.fr[0]
        for j in range(1, n):
            film_sum = film_sum + r.fr[j]
        for m in range(2):
            for core in range(2):
                r.fx[m * 2 + core] = film_sum[m : m + 1, core * 128 : core * 128 + 128]
        head_start(lambda p: r.fx.at[p], r.fh, r.fh_s, r.fh_r)
        r.fh[h] = r.fx[h]

        def store_v2(i, vals):
            vals = vals + prow(6)
            r.v2[rows(i), :] = vals
            return vals

        v2_sum = conv(r.act1, k1, store_v2, (lambda: (gb.pass_v(1, 3, 2), gc.own())) if inside else lambda: None)
        head_wait(lambda p: r.fx.at[p], r.fh, r.fh_s, r.fh_r)
        scale = 1.0 + (jnp.concatenate([r.fh[0], r.fh[1]], axis=1) + prow(8))
        shift = jnp.concatenate([r.fh[2], r.fh[3]], axis=1) + prow(9)
        mean2, inv2 = norm(lambda i: r.v2[rows(i), :], 1, v2_sum)
        gain2, shift2 = prow(1), prow(4)
        act2 = Halves("act2", ROW)

        def hat2(i):
            return (r.v2[rows(i), :] - mean2) * inv2

        mul2, add2 = affine(mean2, inv2, gain2 * scale, shift2 * scale + shift)

        def pre2(i):
            return r.v2[rows(i), :] * mul2 + add2

        act2.fill(lambda i: silu(pre2(i)).astype(BF16))
        if inside:
            gc.pass_own()
            gc.pass_z(1, 3, 2)

        transpose_act(r.act2, ROW, "act2_t")
        act2.wait()
        if inside:
            k2.unpack(gb.blocks(0))
            gb.take(k2)

        head_start(lambda p: r.cx_src.at[p], r.cx_dst, r.cx_s, r.cx_r)
        r.cx_dst[h] = r.cx_src[h]

        def store_v3(i, vals):
            vals = mixed(i) + (vals + prow(7))
            r.v3[rows(i), :] = vals
            return vals

        v3_sum = conv(r.act2, k2, store_v3, (lambda: gc.pass_v(1, 3, 2)) if inside else lambda: None)
        mean3, inv3 = norm(lambda i: r.v3[rows(i), :], 2, v3_sum)
        gain3, shift3 = prow(2), prow(5)
        ai = Halves("ai", 0)

        def hat3(i):
            return (r.v3[rows(i), :] - mean3) * inv3

        mul3, add3 = affine(mean3, inv3, gain3, shift3)
        ai.fill(lambda i: (r.v3[rows(i), :] * mul3 + add3).astype(BF16))
        transpose_act(r.ai, 0, "ai_t")

        if inside:
            k3.unpack(gc.blocks(0))
            gc.take(k3)
        head_wait(lambda p: r.cx_src.at[p], r.cx_dst, r.cx_s, r.cx_r)

        def unpack_cot(i):
            r.cx[i] = unpack_pixels(r.cx_dst[i])

        loop(4, unpack_cot)
        dop = Parts("do")

        def cot_rows(i):
            return jnp.concatenate([r.cx[2 * i], r.cx[2 * i + 1]], axis=0)

        dop.fill(lambda i: dot_nt(cot_rows(i), wtap(k3, 3, half_of(1 - c))))

        ai.wait()
        bias_proj = [prow(10)[:, :128], prow(10)[:, 128:], None, None, prow(11)[:, :128], prow(11)[:, 128:]]

        def project(i):
            out = dot(flat(r.ai, 0, i, 2 * CHUNK), wproj(ALL))
            for k in range(6):
                part = out[:, k * 128 : k * 128 + 128]
                if bias_proj[k] is not None:
                    part = part + bias_proj[k]
                r.qkv[k, rows(i, 2 * CHUNK), :] = part.astype(BF16)

        each(2, project)

        def do_own(i):
            full = (dot_nt(cot_rows(i), wtap(k3, 3, half_of(c))) + dop.get(i)).astype(BF16)
            for k in range(2):
                r.dout[k, rows(i, 2 * CHUNK), :] = full[:, k * 128 : k * 128 + 128]

        each(2, do_own)

        factor = 1.0 / math.sqrt(HEAD_DIM)
        factor2 = factor * math.log2(math.e)
        att = []

        def transposes(k):
            r.kvt[k] = jnp.transpose(r.qkv[k + 2])

        loop(4, transposes)

        def att_copy(core, k):
            ref = r.att.at[core * 2 + k]
            return rc(ref, ref, r.att_s.at[k], r.att_r.at[k], sib)

        def att_t_copy(core, k):
            ref = r.att_t.at[core, pl.ds(pl.multiple_of(k * 128, 128), 128)]
            return rc(ref, ref, r.att_s.at[2 + k], r.att_r.at[2 + k], sib)

        def one_head(k):
            lows, grads = [], []
            for b in range(2):
                at = pl.ds(b * 2 * CHUNK, 2 * CHUNK)
                query = r.qkv[k, at, :]
                grad = r.dout[k, at, :]
                scores = dot_nt(r.qkv[2 + k], query)
                peak = jnp.max(scores, axis=0, keepdims=True)
                expo = jnp.exp2((scores - peak) * factor2)
                inverse = 1.0 / jnp.sum(expo, axis=0, keepdims=True)
                low = (expo * inverse).astype(BF16)
                got = dot(r.kvt[2 + k], low)
                got_low = got.astype(BF16)
                r.att_t[c, pl.ds(pl.multiple_of(k * 128, 128), 128), at] = got_low
                r.att[2 * c + k, at, :] = jnp.transpose(got_low)
                spread = jnp.sum(got * jnp.transpose(grad).astype(F32), axis=0, keepdims=True)
                probs_grad = dot_nt(r.qkv[4 + k], grad)
                scores_grad = ((probs_grad - spread) * inverse * expo).astype(BF16)
                back = dot(r.kvt[k], scores_grad)
                r.dproj[k, at, :] = (jnp.transpose(back) * factor).astype(BF16)
                lows.append(low)
                grads.append(scores_grad)
            att_copy(c, k).start()
            att_t_copy(c, k).start()
            r.dproj[4 + k] = dot(jnp.concatenate(lows, axis=1), r.dout[k]).astype(BF16)
            r.dproj[2 + k] = (dot(jnp.concatenate(grads, axis=1), r.qkv[k]) * factor).astype(BF16)

        loop(2, one_head)

        n3 = Parts("n3")

        def proj_rows(i):
            return jnp.concatenate([r.dproj[k, rows(i, 2 * CHUNK), :] for k in range(6)], axis=1)

        n3.fill(lambda i: dot_nt(proj_rows(i), wproj(half_of(1 - c))))

        def rows_of(act_t):
            return jnp.concatenate([act_t[p // 2, pl.ds(p % 2 * 128, BLK), :] for p in range(4)], axis=0)

        for k in range(2):
            copy = att_copy(1 - c, k)
            copy.wait_recv()
            copy.wait_send()

        def result(i):
            left = jnp.concatenate([r.att[p, rows(i), :] for p in range(4)], axis=1)
            branch = dot(left, wtap(k3, 3, ALL)) + prow(12)
            r.ro_src[i] = pack_pixels(r.v3[rows(i), :] + branch).astype(BF16)

        loop(4, result)
        head_start(lambda p: r.ro_src.at[p], r.ro_dst, r.ro_s, r.ro_r)
        r.ro_dst[h] = r.ro_src[h]

        if inside:
            red1, red2, red3 = Reduce("r1", 3), Reduce("r2", 3), Reduce("r3", 1)
            acc1, acc2, acc3 = r.r1_acc, r.r2_acc, r.r3_acc
        else:
            acc1, acc2, acc3 = r.first, r.second, r.attend

        transposed_wait("ai_t")
        for k in range(2):
            copy = att_t_copy(1 - c, k)
            copy.wait_recv()
            copy.wait_send()
        right = jnp.concatenate([r.dproj[k] for k in range(6)], axis=1)
        cot_all = jnp.concatenate([r.cx[i] for i in range(4)], axis=0)
        attend_out = dot(rows_of(r.ai_t), right)
        output_out = dot(rows_of(r.att_t), cot_all)
        for p, zc in enumerate(ALL):
            for yy in range(2):
                for xx in range(2):
                    row = p * BLK + yy * 48
                    tiles = [
                        attend_out[row : row + 48, (xx * 3 + j) * 128 : (xx * 3 + j) * 128 + 128] for j in range(3)
                    ]
                    acc3[0, slot(xx, yy), zc] = pack_four(
                        *tiles, output_out[row : row + 48, xx * 128 : xx * 128 + 128]
                    ).astype(acc3.dtype)
        if inside:
            red3.start(0)

        def proj_sums(i, carry):
            q = jnp.concatenate([r.dproj[0, rows(i), :], r.dproj[1, rows(i), :]], axis=1).astype(F32)
            val = jnp.concatenate([r.dproj[4, rows(i), :], r.dproj[5, rows(i), :]], axis=1).astype(F32)
            return (carry[0] + fold(q), carry[1] + fold(val), carry[2] + fold(r.cx[i].astype(F32)))

        qsum, vsum, csum = lax.fori_loop(0, 4, proj_sums, (zero8, zero8, zero8))
        r.sums[pl.ds(3 + 7, 1), :] = jnp.sum(qsum, axis=0, keepdims=True)
        r.sums[pl.ds(3 + 8, 1), :] = jnp.sum(vsum, axis=0, keepdims=True)
        r.sums[pl.ds(3 + 9, 1), :] = jnp.sum(csum, axis=0, keepdims=True)
        r.sums[pl.ds(13, 3), :] = jnp.zeros((3, HALF), F32)

        def n3_own(i, carry):
            both = dot_nt(proj_rows(i), wproj(half_of(c))) + n3.get(i)
            for j in range(2):
                vals = both[j * CHUNK : j * CHUNK + CHUNK]
                r.gtmp[rows(2 * i + j), :] = vals
                carry = carry[0] + fold(vals), carry[1] + fold(vals * hat3(2 * i + j))
            return carry

        sums3 = n3_own(1, n3_own(0, (zero8, zero8)))
        plain3, cross3, back3 = norm_back(sums3, lambda i: r.gtmp[rows(i), :], hat3, gain3, inv3)
        r.sums[pl.ds(2, 1), :] = cross3
        r.sums[pl.ds(3 + 2, 1), :] = plain3

        def shifted(buf, i, vals):
            buf[0, rows(i, CHUNK, ROW), :] = from_right(vals).astype(BF16)
            buf[1, rows(i, CHUNK, ROW), :] = vals.astype(BF16)
            buf[2, rows(i, CHUNK, ROW), :] = from_left(vals).astype(BF16)

        def residual_back(i, carry):
            vals = r.cx[i].astype(F32) + back3(i)
            r.gres[rows(i), :] = vals
            shifted(r.gr2, i, vals)
            return carry + fold(vals.astype(BF16).astype(F32))

        bias_two = lax.fori_loop(0, 4, residual_back, jnp.zeros((8, HALF), F32))
        r.sums[pl.ds(3 + 4, 1), :] = jnp.sum(bias_two, axis=0, keepdims=True)

        def act_back(buf, g, core, i, size):
            left = jnp.concatenate(
                [buf[b, rows(i, size, 2 * ROW - ROW * a), :] for a in range(3) for b in range(3)], axis=1
            )
            right = jnp.concatenate(
                [wtap(g, 3 * a + b, half_of(core)) for a in range(3) for b in range(3)], axis=1
            )
            return dot_nt(left, right)

        def conv_back(parts, buf, g):
            parts.fill(lambda i: act_back(buf, g, 1 - c, i, 2 * CHUNK))

        def conv_back_own(parts, buf, g, outer, hat):
            def own(i, carry):
                vals = act_back(buf, g, c, i, 2 * CHUNK) + parts.get(i)
                for j in range(2):
                    at = 2 * i + j
                    grad = vals[j * CHUNK : j * CHUNK + CHUNK] * outer(at)
                    r.gtmp[rows(at), :] = grad
                    carry = carry[0] + fold(grad), carry[1] + fold(grad * hat(at))
                return carry

            return own(1, own(0, (zero8, zero8)))

        def kernel_grad(act_t, buf, acc, after):
            def step(a):
                right = jnp.concatenate([buf[b, pl.ds(2 * ROW - ROW * a, PX), :] for b in range(3)], axis=1)
                out = dot(rows_of(act_t), right)
                for p, zc in enumerate(ALL):
                    for yy in range(2):
                        for xx in range(2):
                            row = p * BLK + yy * 48
                            tiles = [
                                out[row : row + 48, b * HALF + xx * 128 : b * HALF + xx * 128 + 128].astype(acc.dtype)
                                for b in range(3)
                            ]
                            acc[a, slot(xx, yy), zc] = pack_taps(*tiles)
                after(a)

            each(3, step)

        serve = inside
        d2 = Parts("d2")
        transposed_wait("act2_t")
        kernel_grad(r.act2_t, r.gr2, acc2, red2.start if inside else lambda a: None)
        if serve:
            red3.second(0, 1)
        conv_back(d2, r.gr2, k2)
        if serve:
            red2.second(0, 1)
        sums2 = conv_back_own(d2, r.gr2, k2, lambda i: silu_slope(pre2(i)), hat2)
        if serve:
            red2.second(1, 1)
            red3.third(0, 1)

        plain2, cross2, back2 = norm_back(sums2, lambda i: r.gtmp[rows(i), :], hat2, gain2 * scale, inv2)
        r.sums[pl.ds(1, 1), :] = scale * cross2
        r.sums[pl.ds(3 + 1, 1), :] = scale * plain2
        film_scale_term = gain2 * cross2 + shift2 * plain2
        r.sums[pl.ds(3 + 5, 1), :] = film_scale_term
        r.sums[pl.ds(3 + 6, 1), :] = plain2
        for j in range(2):
            r.ft[j] = film_scale_term[:, j * 128 : j * 128 + 128]
            r.ft[2 + j] = plain2[:, j * 128 : j * 128 + 128]
        head_start(lambda p: r.ft.at[p], r.th, r.th_s, r.th_r)
        r.th[h] = r.ft[h]

        def first_back(i, carry):
            vals = back2(i)
            shifted(r.gr1, i, vals)
            return carry + fold(vals.astype(BF16).astype(F32))

        bias_one = lax.fori_loop(0, 4, first_back, jnp.zeros((8, HALF), F32))
        r.sums[pl.ds(3 + 3, 1), :] = jnp.sum(bias_one, axis=0, keepdims=True)

        if serve:
            red2.second(2, 1)
            red2.third(0, 1)
            red2.third(1, 1)

        head_wait(lambda p: r.ft.at[p], r.th, r.th_s, r.th_r)
        for m in range(2):
            r.fa[d, pl.ds(m, 1), :] = jnp.concatenate([r.th[2 * m], r.th[2 * m + 1]], axis=1)
        dp_start(lambda p: r.fa.at[d], r.fa, r.fa_s, r.fa_r)

        d1 = Parts("d1")

        def after_chunk(a):
            if serve:
                red1.start(a)
                if a == 1:
                    red2.third(2, 1)

        transposed_wait("act1_t")
        kernel_grad(r.act1_t, r.gr1, acc1, after_chunk)
        conv_back(d1, r.gr1, k1)
        if serve:
            red1.second(0, 1)

        dp_wait(lambda p: r.fa.at[d], r.fa, r.fa_s, r.fa_r)
        for j in range(n):
            r.fta[pl.ds(2 * j, 2), :] = r.fa[j]
        film_block = dot_tn_high(r.esel[...], r.fta[...])
        r.film[...] = jnp.concatenate([film_block[:film_rows, :BLK], film_block[:film_rows, 128 : 128 + BLK]], axis=1)
        embed_part = dot_nt_high(r.fta[...], r.wfp[...].astype(F32))
        for j in range(n):
            r.ep[j] = embed_part[2 * j : 2 * j + 2]
        dp_start(lambda p: r.ep.at[p], r.er, r.er_s, r.er_r)
        r.er[d] = r.ep[d]

        def hat1(i):
            return (mixed(i) - mean1) * inv1

        sums1 = conv_back_own(d1, r.gr1, k1, lambda i: silu_slope(pre1(i)), hat1)
        if serve:
            red1.second(1, 1)

        plain1, cross1, back1 = norm_back(sums1, lambda i: r.gtmp[rows(i), :], hat1, gain1, inv1)
        r.sums[pl.ds(0, 1), :] = cross1
        r.sums[pl.ds(3, 1), :] = plain1
        r.ad[d] = r.sums[...]
        dp_start(lambda p: r.ad.at[d], r.ad, r.ad_s, r.ad_r)

        if serve:
            red1.second(2, 1)
            red1.third(0, 1)
        keep, _ = plan(r.steps[x], HALF)

        def image_back(i):
            return pack_pixels(keep * (r.gres[rows(i), :] + back1(i))).astype(BF16)

        for k in (2, 1, 3):
            peer = lax.rem(h + k, 4)
            r.io_src[peer] = image_back(peer)
            rc(r.io_src.at[peer], r.io_dst.at[h], r.io_s.at[k], r.io_r.at[h], (d, peer)).start()
        r.io_dst[h] = image_back(h)
        if serve:
            red1.third(1, 1)
            red1.third(2, 1)

        dp_wait(lambda p: r.ep.at[p], r.er, r.er_s, r.er_r)
        r.eh[h] = r.er[...]
        head_start(lambda p: r.eh.at[h], r.eh, r.eh_s, r.eh_r)
        dp_wait(lambda p: r.ad.at[d], r.ad, r.ad_s, r.ad_r)
        total = r.ad[0]
        for j in range(1, n):
            total = total + r.ad[j]
        r.hb[h] = total
        head_start(lambda p: r.hb.at[h], r.hb, r.hb_s, r.hb_r)
        head_wait(lambda p: r.ro_src.at[p], r.ro_dst, r.ro_s, r.ro_r)

        if inside:
            red2.finish(((0, 1), (1, 1), (2, 1)))
            for a in range(3):
                r.second[a] = red2.last(a)

        head_wait(lambda p: r.hb.at[h], r.hb, r.hb_s, r.hb_r)
        even = r.hb[0] + r.hb[2]
        odd = r.hb[1] + r.hb[3]
        wide = jnp.concatenate(
            [even[:, :BLK], odd[:, :BLK], even[:, 128 : 128 + BLK], odd[:, 128 : 128 + BLK]], axis=1
        )
        r.gains_out[...] = wide[0:3]
        r.biases_out[...] = wide[3:13]

        head_wait(lambda p: r.eh.at[h], r.eh, r.eh_s, r.eh_r)
        pieces = []
        for j in range(n):
            piece = (r.eh[0, j] + r.eh[1, j]) + (r.eh[2, j] + r.eh[3, j])
            pieces.append(piece[:, :film_rows])
        r.embed_grad[...] = jnp.concatenate(pieces, axis=1) * silu_slope(r.emb[...].astype(F32))

        head_wait(lambda p: r.io_src.at[p], r.io_dst, r.io_s, r.io_r)

        if inside:
            red3.finish(((0, 1),))
            tiles = unpack_four(red3.last(0))
            r.sb_src[...] = jnp.where(c == 0, tiles[2], tiles[0])
            back = rc(r.sb_src, r.sb_dst, r.sb_s.at[0], r.sb_r.at[0], sib)
            back.start()
            r.output[...] = tiles[3]
            for part in (ga, gb, gc):
                part.finish()
            red1.finish(((0, 1), (1, 1), (2, 1)))
            for a in range(3):
                r.first[a] = red1.last(a)
            back.wait()
            r.attend[:, 0:128] = jnp.where(c == 0, tiles[0], tiles[1])
            r.attend[:, 128:256] = r.sb_dst[...]
            r.attend[:, 256:384] = jnp.where(c == 0, tiles[1], tiles[2])

    return kernel


def make_writer(names_in, names_out):
    def kernel(*refs):
        count, wide = len(names_in), len(names_out)
        far_in, far_out = refs[:count], refs[count : count + wide]
        near_in, near_out = refs[count + wide : 2 * count + wide], refs[2 * count + wide : 2 * count + 2 * wide]
        sem_in, sem_out = refs[-2:]
        src, dst = Names(names_in, near_in), Names(names_out, near_out)
        loads = {
            name: pltpu.make_async_copy(far_in[i], near_in[i], sem_in.at[i]) for i, name in enumerate(names_in)
        }
        stores = {
            name: pltpu.make_async_copy(near_out[i], far_out[i], sem_out.at[i]) for i, name in enumerate(names_out)
        }
        for name in ("sel", "ro_dst", "io_dst"):
            loads[name].start()
        for name in names_in:
            if name not in ("sel", "ro_dst", "io_dst"):
                loads[name].start()
        loads["sel"].wait()
        for name, packed in (("result", "ro_dst"), ("image_grad", "io_dst")):
            loads[packed].wait()
            ref = getattr(src, packed)
            for m in range(2):
                getattr(dst, name)[m] = dot_nt(unpack_pixels(ref[2 * m]), src.sel[0]) + dot_nt(
                    unpack_pixels(ref[2 * m + 1]), src.sel[1]
                )
            stores[name].start()
        for name in ("first", "second"):
            if name in names_out:
                loads[name].wait()
                for a in range(3):
                    block = getattr(src, name)[a]
                    getattr(dst, name)[3 * a] = block[:48, :BLK]
                    getattr(dst, name)[3 * a + 1] = block[48:96, :BLK]
                    getattr(dst, name)[3 * a + 2] = last_tap(block)[:, :BLK]
                stores[name].start()
        if "attend" in names_out:
            loads["attend"].wait()
            dst.attend[...] = jnp.concatenate([src.attend[:, j * 128 : j * 128 + BLK] for j in range(3)], axis=1)
            stores["attend"].start()
            loads["output"].wait()
            dst.output[...] = src.output[:, :BLK]
            stores["output"].start()
        for name in ("embed_grad", "film", "gains_out", "biases_out"):
            loads[name].wait()
            getattr(dst, name)[...] = getattr(src, name)[...]
            stores[name].start()
        for name in names_out:
            stores[name].wait()

    return kernel


def per_device(n, *args):
    (
        images,
        noise_field,
        time_steps,
        embedding,
        first_kernel,
        second_kernel,
        film_weight,
        attend_weight,
        output_weight,
        norm_gains,
        biases,
        cotangent,
    ) = args
    inside = n == 8
    maps, height, width, channels = images.shape
    flat_shape = (maps, height * width, channels)
    film_rows = film_weight.shape[0]
    inputs = dict(
        steps=time_steps,
        images=images.reshape(flat_shape),
        noise=noise_field.reshape(flat_shape),
        cot=cotangent.reshape(flat_shape),
        emb=embedding,
        k1=first_kernel.reshape((9,) + first_kernel.shape[2:]),
        k2=second_kernel.reshape((9,) + second_kernel.shape[2:]),
        wf=film_weight,
        wa=attend_weight,
        wo=output_weight,
        gains=norm_gains,
        biases=biases,
        sel=jnp.asarray(channel_lanes(), BF16),
        gmask=jnp.asarray(group_mask(), BF16),
        selp=jnp.asarray(block_lanes(3), BF16),
    )
    shapes = dict(
        ro_dst=(4, 384, 128),
        io_dst=(4, 384, 128),
        embed_grad=embedding.shape,
        first=(3, 112, 128),
        second=(3, 112, 128),
        film=film_weight.shape,
        attend=(48, 384),
        output=(48, 128),
        gains_out=norm_gains.shape,
        biases_out=biases.shape,
    )
    names_in, names_out = list(INPUTS), list(OUTPUTS)
    core = lax.axis_index("head") % 2
    if not inside:
        def whole(array, row_axis):
            array = lax.all_gather(array, "dp", axis=row_axis, tiled=True)
            return lax.all_gather(array, "head", axis=array.ndim - 1, tiled=True)

        def spread(array, count):
            taps = array.shape[0]
            array = array.reshape(taps, 4, 2, 48, 2, 2, BLK)
            array = lax.dynamic_index_in_dim(array, core, 5, keepdims=False)
            array = jnp.transpose(array, (2, 4, 1, 0, 3, 5))
            array = jnp.pad(array, ((0, 0),) * 5 + ((0, 32),))
            return array.reshape(4, 4, taps * 48, 128)

        full_a = whole(attend_weight, 0).reshape(384, 2, 3, 2, BLK)
        full_a = jnp.transpose(full_a, (2, 0, 1, 3, 4)).reshape(3, 384, 384)
        full_o = whole(output_weight, 0)[None]
        for name, last, array in (("g1", "t1", first_kernel), ("g2", "t2", second_kernel)):
            blocks = spread(whole(array, 2).reshape(9, 384, 384), 9).reshape(4, 4, 3, 3, 48, 128)
            two = blocks[:, :, :, :2].reshape(4, 4, 3, 96, 128)
            inputs[name] = jnp.pad(two, ((0, 0),) * 3 + ((0, 16), (0, 0))).reshape(4, 4, 336, 128)
            inputs[last] = blocks[:, :, :, 2].reshape(4, 4, 144, 128)
        inputs["g3"] = spread(jnp.concatenate([full_a, full_o], axis=0), 4)
        names_in += ["g1", "g2", "t1", "t2", "g3"]
        shapes["first"] = shapes["second"] = (3, 4, 4, 112, 128)
        shapes["attend"] = (1, 4, 4, 144, 128)
        del shapes["output"]
        names_out.remove("output")
    items = scratch_list(n, inside, inputs)
    smem = pl.BlockSpec(memory_space=pltpu.SMEM)
    vmem = pl.BlockSpec(memory_space=pltpu.VMEM)
    outs = pl.pallas_call(
        make_kernel(
            n,
            inside,
            [name + "_far" if name in FAR else name for name in names_in] + names_out + [name for name, _ in items],
        ),
        out_shape=[
            jax.ShapeDtypeStruct(shapes[name], BF16 if name in ("ro_dst", "io_dst") else F32) for name in names_out
        ],
        in_specs=[
            smem if name == "steps" else pl.BlockSpec(memory_space=pl.ANY) if name in FAR else vmem
            for name in names_in
        ],
        out_specs=[vmem] * len(names_out),
        scratch_shapes=[item for _, item in items],
        compiler_params=pltpu.CompilerParams(
            collective_id=0, has_side_effects=True, vmem_limit_bytes=63 * 1024 * 1024
        ),
        name="blocks",
    )(*[inputs[name] for name in names_in])
    raw = dict(zip(names_out, outs))
    final = dict(
        result=flat_shape,
        image_grad=flat_shape,
        embed_grad=embedding.shape,
        film=film_weight.shape,
        gains_out=norm_gains.shape,
        biases_out=biases.shape,
    )
    if inside:
        final.update(first=(9, 48, BLK), second=(9, 48, BLK), attend=attend_weight.shape, output=output_weight.shape)
    names_last = [name for name in names_out if inside or name not in ("first", "second", "attend")] + ["sel"]
    names_final = list(final)
    given = [inputs["sel"] if name == "sel" else raw[name] for name in names_last]
    far = pl.BlockSpec(memory_space=pl.ANY)
    outs = pl.pallas_call(
        make_writer(names_last, names_final),
        out_shape=[jax.ShapeDtypeStruct(final[name], F32) for name in names_final],
        in_specs=[far] * len(names_last),
        out_specs=[far] * len(names_final),
        scratch_shapes=[pltpu.VMEM(array.shape, array.dtype) for array in given]
        + [pltpu.VMEM(final[name], F32) for name in names_final]
        + [pltpu.SemaphoreType.DMA((len(names_last),)), pltpu.SemaphoreType.DMA((len(names_final),))],
        compiler_params=pltpu.CompilerParams(vmem_limit_bytes=63 * 1024 * 1024),
        name="outputs",
    )(*given)
    out = dict(zip(names_final, outs))
    if not inside:

        def blocks_of(array, size):
            parts = [array[..., k * 48 : k * 48 + 48, :BLK] for k in range(size)]
            if size == 2:
                lanes = [array[..., k * 32 : k * 32 + 32, BLK:] for k in range(3)]
                lanes = jnp.concatenate(lanes, axis=-1)
                parts.append(jnp.concatenate([lanes, array[..., 96:112, :BLK]], axis=-2))
            else:
                lanes = [array[..., k * 48 : k * 48 + 48, BLK:] for k in range(3)]
                parts.append(jnp.concatenate(lanes, axis=-1))
            array = jnp.stack(parts, axis=1)
            array = array.reshape(array.shape[:2] + (2, 2, 4, 48, BLK))
            taps = array.shape[0] * array.shape[1]
            array = jnp.transpose(array, (0, 1, 4, 2, 5, 3, 6)).reshape(taps, 384, 2, 1, BLK)
            both = jnp.concatenate([array, jnp.zeros_like(array)], axis=3)
            return jnp.where(core == 0, both, both[:, :, :, ::-1]).reshape(taps, 384, 384)

        def shared(array, axis):
            array = lax.psum_scatter(array, "head", scatter_dimension=array.ndim - 1, tiled=True)
            return lax.psum_scatter(array, "dp", scatter_dimension=axis, tiled=True)

        out["first"] = shared(blocks_of(raw["first"], 2), 1)
        out["second"] = shared(blocks_of(raw["second"], 2), 1)
        both = blocks_of(raw["attend"], 3)
        joined = both[:3].reshape(3, 384, 2, 2, BLK)
        joined = jnp.transpose(joined, (1, 2, 0, 3, 4)).reshape(384, 1152)
        out["attend"] = shared(joined, 0)
        out["output"] = shared(both[3], 0)
    return (
        out["result"].reshape(images.shape),
        out["image_grad"].reshape(images.shape),
        out["embed_grad"],
        out["first"].reshape(first_kernel.shape),
        out["second"].reshape(second_kernel.shape),
        out["film"],
        out["attend"],
        out["output"],
        out["gains_out"],
        out["biases_out"],
    )


def solution(mesh):
    n = mesh.shape["dp"]
    field = P("dp", "head", None, None)
    taps = P(None, None, "dp", "head")
    both = P("dp", "head")
    return jax.shard_map(
        lambda *args: per_device(n, *args),
        mesh=mesh,
        in_specs=(field, field, P("dp"), P("dp", None), taps, taps, both, both, both, P(), P(), field),
        out_specs=(field, field, P("dp", None), taps, taps, both, both, both, P(), P()),
        check_vma=False,
    )
```
